32 devices in a mesh: ctx: 8 (over y, x, core), fsdp: 4 (over z).
Axes of the slice: x: 2, y: 2, z: 4, core: 2. Of those that a mesh axis runs over, the one named last changes fastest.
Arguments:
- layer_input: bfloat16 [4, 1024, 1024], P('fsdp', 'ctx'), may hold values from -6 to 6
- token_positions: int32 [4, 1024], P('fsdp'), may hold values from 0 to 1023, as said below
- attention_gain: float32 [1024], replicated, may hold values from 0.5 to 1.5
- query_weight: bfloat16 [1024, 2048], P('fsdp'), may hold values from -0.1875 to 0.1875
- key_matrix: bfloat16 [1024, 1024], P('fsdp'), may hold values from -0.1875 to 0.1875
- value_matrix: bfloat16 [1024, 1024], P('fsdp'), may hold values from -0.1875 to 0.1875
- query_gain: float32 [128], replicated, may hold values from 0.5 to 1.5
- key_norm_gain: float32 [128], replicated, may hold values from 0.5 to 1.5
- output_weight: bfloat16 [2048, 1024], P('fsdp'), may hold values from -1 to 1
- feedforward_gain: float32 [1024], replicated, may hold values from 0.5 to 1.5
- gate_weight: bfloat16 [1024, 3072], P('fsdp'), may hold values from -0.1875 to 0.1875
- up_weight: bfloat16 [1024, 3072], P('fsdp'), may hold values from -0.1875 to 0.1875
- down_weight: bfloat16 [3072, 1024], P('fsdp'), may hold values from -0.15625 to 0.15625
- out_cotangent: bfloat16 [4, 1024, 1024], P('fsdp', 'ctx'), may hold values from -6 to 6
Outputs:
- layer_output: bfloat16 [4, 1024, 1024], P('fsdp', 'ctx')
- input_gradient: float32 [4, 1024, 1024], P('fsdp', 'ctx')
- attention_gain_gradient: float32 [1024], replicated
- query_gradient: float32 [1024, 2048], P(('ctx', 'fsdp'))
- key_gradient: float32 [1024, 1024], P(('ctx', 'fsdp'))
- value_gradient: float32 [1024, 1024], P(('ctx', 'fsdp'))
- query_gain_gradient: float32 [128], replicated
- key_gain_gradient: float32 [128], replicated
- output_gradient: float32 [2048, 1024], P(None, ('ctx', 'fsdp'))
- feedforward_gain_gradient: float32 [1024], replicated
- gate_gradient: float32 [1024, 3072], P(('ctx', 'fsdp'))
- up_gradient: float32 [1024, 3072], P(('ctx', 'fsdp'))
- down_gradient: float32 [3072, 1024], P(None, ('ctx', 'fsdp'))
The draws below stay inside these ranges and needn't reach their ends.
Inputs may be any that keep to these rules, and one draw needn't show every extreme that they name: `token_positions`: each row is a permutation of the positions of one sequence. Every aligned block of 128 stored rows holds two runs of 64 consecutive rising positions, run k and run 2 * 8 - 1 - k for some k.
All inputs are finite; a program needn't handle non-finite values.
Results may differ from the reference program's by a relative error of at most 0.02.
Values may be sent and summed in bfloat16 or wider, within the bound.
A program may use at most 256 MiB of HBM per device.

```python
import jax
import jax.numpy as jnp
from jax import lax

MODEL_WIDTH = 1024
QUERY_HEADS = 16
KEY_VALUE_HEADS = 8
HEAD_WIDTH = 128
FF = 3072
TOK_DEV = 128
SEQUENCE_LENGTH = 1024
SEQUENCE_COUNT = 4


def draw_token_positions(key, part):
    key = jax.random.fold_in(key, 7)
    blocks = SEQUENCE_LENGTH // TOK_DEV
    half = TOK_DEV // 2
    seeds = jax.random.split(key, SEQUENCE_COUNT)
    orders = jax.vmap(lambda single: jax.random.permutation(single, blocks))(seeds).astype(jnp.int32)
    within = jnp.arange(TOK_DEV, dtype=jnp.int32)[None, None, :]
    lower = orders[:, :, None] * half + within
    upper = (2 * blocks - 1 - orders[:, :, None]) * half + within - half
    result = jnp.where(within < half, lower, upper)
    return result.reshape(SEQUENCE_COUNT, SEQUENCE_LENGTH).astype(jnp.int32)


def block_scale(stream_key, dims, cuts, least, high):
    level = 1.0
    for dim, blocks in cuts:
        heights = jax.random.uniform(jax.random.fold_in(jax.random.fold_in(stream_key, 6), dim), (blocks,), jnp.float32, least / len(cuts), high / len(cuts))
        level = level * jnp.repeat(jnp.exp(heights), dims[dim] // blocks).reshape((-1,) + (1,) * (len(dims) - 1 - dim))
    return level


def scatter_about(rng, shape, spread, reach, shards=(), kind=jnp.bfloat16):
    factor_of = block_scale(rng, shape, shards, -0.22, 0.18) if shards else 1.0
    entries = jax.random.normal(rng, shape, jnp.float32) * spread * factor_of
    return jnp.minimum(jnp.maximum(entries, -reach), reach).astype(kind)


def setup_inputs(seed: int = 0) -> dict:
    streams_of = jax.random.split(jax.random.key(seed), 15)
    layer_input = scatter_about(streams_of[0], (SEQUENCE_COUNT, SEQUENCE_LENGTH, MODEL_WIDTH), 1.0, 6.0, ((0, 4), (1, 8)))
    token_positions = draw_token_positions(jax.random.fold_in(streams_of[14], 71), 0)
    attention_gain = jnp.clip(1.0 + 0.1 * jax.random.normal(streams_of[2], (MODEL_WIDTH,), jnp.float32), 0.5, 1.5)
    query_weight = scatter_about(streams_of[3], (MODEL_WIDTH, QUERY_HEADS * HEAD_WIDTH), MODEL_WIDTH ** -0.5, 0.1875, ((0, 4),))
    key_matrix = scatter_about(streams_of[4], (MODEL_WIDTH, KEY_VALUE_HEADS * HEAD_WIDTH), MODEL_WIDTH ** -0.5, 0.1875, ((0, 4),))
    value_matrix = scatter_about(streams_of[5], (MODEL_WIDTH, KEY_VALUE_HEADS * HEAD_WIDTH), MODEL_WIDTH ** -0.5, 0.1875, ((0, 4),))
    query_gain = jnp.clip(1.0 + 0.1 * jax.random.normal(streams_of[6], (HEAD_WIDTH,), jnp.float32), 0.5, 1.5)
    key_norm_gain = jnp.clip(1.0 + 0.1 * jax.random.normal(streams_of[7], (HEAD_WIDTH,), jnp.float32), 0.5, 1.5)
    output_weight = scatter_about(streams_of[8], (QUERY_HEADS * HEAD_WIDTH, MODEL_WIDTH), (QUERY_HEADS * HEAD_WIDTH // 64) ** -0.5, 1.0, ((0, 4),))
    feedforward_gain = jnp.clip(1.0 + 0.1 * jax.random.normal(streams_of[9], (MODEL_WIDTH,), jnp.float32), 0.5, 1.5)
    gate_weight = scatter_about(streams_of[10], (MODEL_WIDTH, FF), MODEL_WIDTH ** -0.5, 0.1875, ((0, 4),))
    up_weight = scatter_about(streams_of[11], (MODEL_WIDTH, FF), MODEL_WIDTH ** -0.5, 0.1875, ((0, 4),))
    down_weight = scatter_about(streams_of[12], (FF, MODEL_WIDTH), (FF // 2) ** -0.5, 0.15625, ((0, 4),))
    out_cotangent = scatter_about(streams_of[13], (SEQUENCE_COUNT, SEQUENCE_LENGTH, MODEL_WIDTH), 1.0, 6.0, ((0, 4), (1, 8)))
    return {"layer_input": layer_input, "token_positions": token_positions, "attention_gain": attention_gain, "query_weight": query_weight, "key_matrix": key_matrix, "value_matrix": value_matrix, "query_gain": query_gain, "key_norm_gain": key_norm_gain, "output_weight": output_weight, "feedforward_gain": feedforward_gain, "gate_weight": gate_weight, "up_weight": up_weight, "down_weight": down_weight, "out_cotangent": out_cotangent}


@jax.custom_vjp
def reduced_precision(v):
    return lax.optimization_barrier(v.astype(jnp.bfloat16)).astype(jnp.float32)

@jax.custom_vjp
def low_back(v):
    return v

def low_keep(v):
    return (reduced_precision(v), None)

def low_pass(kept, grad):
    return (grad,)

def back_keep(v):
    return (v, None)

def back_low(kept, grad):
    return (reduced_precision(grad),)
reduced_precision.defvjp(low_keep, low_pass)
low_back.defvjp(back_keep, back_low)
epsilon = 1e-06
rope_base = 1000000.0
masked_score = -1e+30
highest = lax.Precision.HIGHEST

def product(left, right):
    return jnp.dot(left, right, precision=highest, preferred_element_type=jnp.float32)

def normed_rows(value_rows, gain):
    return value_rows * lax.rsqrt(lax.optimization_barrier(jnp.mean(value_rows * value_rows, -1, keepdims=True)) + epsilon) * gain

def rotate(value_rows):
    half = value_rows.shape[-1] // 2
    return jnp.concatenate([-value_rows[..., half:], value_rows[..., :half]], -1)

def rope_tables(token_offsets):
    half = HEAD_WIDTH // 2
    inverse = rope_base ** (-(jnp.arange(half).astype(jnp.float32) * 2.0) / HEAD_WIDTH)
    angles = token_offsets.astype(jnp.float32)[:, None] * inverse[None, :]
    cosine = jnp.cos(angles)
    sine = jnp.sin(angles)
    return (jnp.concatenate([cosine, cosine], -1), jnp.concatenate([sine, sine], -1))

def attend_block(query_tile_block, query_pos, key_rows, value_rows, key_pos):
    input_rows = query_tile_block.shape[0]
    grouped_heads = query_tile_block.reshape(input_rows, KEY_VALUE_HEADS, QUERY_HEADS // KEY_VALUE_HEADS, HEAD_WIDTH)
    scores = jnp.einsum('bkgd,lkd->kgbl', grouped_heads, key_rows, precision=highest) * HEAD_WIDTH ** (-0.5)
    allowed = query_pos[:, None] >= key_pos[None, :]
    scores = low_back(jnp.where(allowed, scores, masked_score))
    probs = jax.nn.softmax(scores, axis=-1)
    mixed_heads = jnp.einsum('kgbl,lkd->bkgd', reduced_precision(probs), value_rows, precision=highest)
    return mixed_heads.reshape(input_rows, QUERY_HEADS * HEAD_WIDTH)

def attend_full_sequence(items):
    query_rows, key_rows, value_rows, token_offsets = items
    block = min(512, SEQUENCE_LENGTH)
    query_blocks = query_rows.reshape(SEQUENCE_LENGTH // block, block, QUERY_HEADS, HEAD_WIDTH)
    pos_blocks = token_offsets.reshape(SEQUENCE_LENGTH // block, block)
    checked = jax.checkpoint(attend_block)
    result = lax.map(lambda pair: checked(pair[0], pair[1], key_rows, value_rows, token_offsets), (query_blocks, pos_blocks))
    return result.reshape(SEQUENCE_LENGTH, QUERY_HEADS * HEAD_WIDTH)

def forward(hidden_in, attention_gain, query_weight, key_matrix, value_matrix, query_gain, key_norm_gain, output_weight, feedforward_gain, gate_weight, up_weight, down_weight, token_offsets):
    flat = hidden_in.reshape(SEQUENCE_COUNT * SEQUENCE_LENGTH, MODEL_WIDTH)
    first = reduced_precision(normed_rows(flat, attention_gain))
    query_raw = low_back(product(first, query_weight))
    key_unnormed = low_back(product(first, key_matrix))
    value_unnormed = low_back(product(first, value_matrix))
    cosine, sine = rope_tables(token_offsets.reshape(-1))
    query_rows = normed_rows(query_raw.reshape(-1, QUERY_HEADS, HEAD_WIDTH), query_gain)
    query_rows = reduced_precision(query_rows * cosine[:, None, :] + rotate(query_rows) * sine[:, None, :])
    key_rows = normed_rows(key_unnormed.reshape(-1, KEY_VALUE_HEADS, HEAD_WIDTH), key_norm_gain)
    key_rows = reduced_precision(key_rows * cosine[:, None, :] + rotate(key_rows) * sine[:, None, :])
    value_rows = reduced_precision(value_unnormed).reshape(-1, KEY_VALUE_HEADS, HEAD_WIDTH)
    mixed_heads = lax.map(attend_full_sequence, (query_rows.reshape(SEQUENCE_COUNT, SEQUENCE_LENGTH, QUERY_HEADS, HEAD_WIDTH), key_rows.reshape(SEQUENCE_COUNT, SEQUENCE_LENGTH, KEY_VALUE_HEADS, HEAD_WIDTH), value_rows.reshape(SEQUENCE_COUNT, SEQUENCE_LENGTH, KEY_VALUE_HEADS, HEAD_WIDTH), token_offsets))
    mixed_heads = reduced_precision(low_back(mixed_heads.reshape(-1, QUERY_HEADS * HEAD_WIDTH)))
    middle = flat + low_back(product(mixed_heads, output_weight))
    second = reduced_precision(normed_rows(middle, feedforward_gain))
    gate = low_back(product(second, gate_weight))
    up = low_back(product(second, up_weight))
    hidden = reduced_precision(jax.nn.silu(gate) * up)
    return (middle + product(hidden, down_weight)).reshape(SEQUENCE_COUNT, SEQUENCE_LENGTH, MODEL_WIDTH)

def reference(layer_input, token_positions, attention_gain, query_weight, key_matrix, value_matrix, query_gain, key_norm_gain, output_weight, feedforward_gain, gate_weight, up_weight, down_weight, out_cotangent):
    primals = (layer_input.astype(jnp.float32), attention_gain.astype(jnp.float32), query_weight.astype(jnp.float32), key_matrix.astype(jnp.float32), value_matrix.astype(jnp.float32), query_gain.astype(jnp.float32), key_norm_gain.astype(jnp.float32), output_weight.astype(jnp.float32), feedforward_gain.astype(jnp.float32), gate_weight.astype(jnp.float32), up_weight.astype(jnp.float32), down_weight.astype(jnp.float32))

    def run(*inputs):
        return forward(*inputs, token_positions)
    output, pullback = jax.vjp(run, *primals)
    gradients = pullback(out_cotangent.astype(jnp.float32))
    return (output.astype(jnp.bfloat16), gradients[0], gradients[1], gradients[2], gradients[3], gradients[4], gradients[5], gradients[6], gradients[7], gradients[8], gradients[9], gradients[10], gradients[11])
```

```python
import jax
import jax.numpy as jnp
from jax import lax
from jax.sharding import PartitionSpec as P

epsilon = 1e-06
rope_base = 1000000.0
masked_score = -1e30


def from_behind(block, axis, distance):
    devices = range(lax.axis_size(axis))
    route = [((i - distance) % len(devices), i) for i in devices]
    return lax.ppermute(block, axis, route)


def rotate(value_rows):
    half = value_rows.shape[-1] // 2
    return jnp.concatenate([-value_rows[..., half:], value_rows[..., :half]], -1)


def rotate_back(value_rows):
    half = value_rows.shape[-1] // 2
    return jnp.concatenate([value_rows[..., half:], -value_rows[..., :half]], -1)


def rope_tables(token_offsets, head_size):
    half = head_size // 2
    inverse = rope_base ** (-(jnp.arange(half).astype(jnp.float32) * 2.0) / head_size)
    angles = token_offsets.astype(jnp.float32)[:, None] * inverse[None, :]
    cosine = jnp.cos(angles)
    sine = jnp.sin(angles)
    return (jnp.concatenate([cosine, cosine], -1), jnp.concatenate([sine, sine], -1))


def norm_scale(value_rows):
    return lax.rsqrt(jnp.mean(value_rows * value_rows, -1, keepdims=True) + epsilon)


def norm_back(value_rows, scale, gain, grad):
    weighted = grad * gain
    inner = jnp.mean(weighted * value_rows, -1, keepdims=True)
    result = scale * weighted - value_rows * scale * scale * scale * inner
    gain_part = jnp.sum((grad * value_rows * scale).reshape(-1, gain.shape[0]), 0)
    return (result, gain_part)


def row_products(left, pieces):
    return tuple((jnp.dot(left, piece, preferred_element_type=jnp.float32) for piece in pieces))


def column_products(rights, pieces):
    total = jnp.einsum("tc,rc->tr", rights[0], pieces[0], preferred_element_type=jnp.float32)
    for right, piece in zip(rights[1:], pieces[1:]):
        total = total + jnp.einsum("tc,rc->tr", right, piece, preferred_element_type=jnp.float32)
    return total


def on_device(
    layer_input,
    token_positions,
    attention_gain,
    query_weight,
    key_matrix,
    value_matrix,
    query_gain,
    key_norm_gain,
    output_weight,
    feedforward_gain,
    gate_weight,
    up_weight,
    down_weight,
    out_cotangent,
):
    hidden_in = layer_input[0].astype(jnp.float32)
    count = hidden_in.shape[0]
    head_size = query_gain.shape[0]
    query_width = query_weight.shape[1]
    key_width = key_matrix.shape[1]
    inner_width = gate_weight.shape[1]
    heads = query_width // head_size
    key_heads = key_width // head_size
    group = heads // key_heads
    scale = head_size ** (-0.5)
    cycles = lax.axis_size("ctx")
    own_index = lax.axis_index("ctx")
    sequence_pos = token_positions[0]
    token_offsets = lax.dynamic_slice_in_dim(sequence_pos, own_index * count, count)
    cosine, sine = rope_tables(token_offsets, head_size)
    cosine = cosine[:, None, :]
    sine = sine[:, None, :]
    first_scale = norm_scale(hidden_in)
    first = (hidden_in * first_scale * attention_gain).astype(jnp.bfloat16)
    query_raw, key_unnormed, value_unnormed = row_products(
        first,
        (
            lax.all_gather(query_weight, "fsdp", axis=0, tiled=True),
            lax.all_gather(key_matrix, "fsdp", axis=0, tiled=True),
            lax.all_gather(value_matrix, "fsdp", axis=0, tiled=True),
        ),
    )
    query_heads = query_raw.reshape(count, heads, head_size)
    query_scale = norm_scale(query_heads)
    query_normed = query_heads * query_scale * query_gain
    query_rot = query_normed * cosine + rotate(query_normed) * sine
    query_grouped = (
        query_rot.reshape(count, key_heads, group, head_size)
        .transpose(1, 2, 0, 3)
        .astype(jnp.bfloat16)
    )
    key_heads_raw = key_unnormed.reshape(count, key_heads, head_size)
    key_scale = norm_scale(key_heads_raw)
    key_normed = key_heads_raw * key_scale * key_norm_gain
    key_low = (
        (key_normed * cosine + rotate(key_normed) * sine)
        .reshape(count, key_width)
        .astype(jnp.bfloat16)
    )
    value_low = value_unnormed.astype(jnp.bfloat16)
    rowmax = jnp.full((key_heads, group, count), masked_score, jnp.float32)
    keys_piece = lax.all_gather(key_low, "ctx", axis=0, tiled=True).reshape(
        -1, key_heads, head_size
    )
    values_piece = lax.all_gather(value_low, "ctx", axis=0, tiled=True).reshape(
        -1, key_heads, head_size
    )
    key_pos = sequence_pos
    allowed = token_offsets[:, None] >= key_pos[None, :]
    scores = (
        jnp.einsum("kgtd,skd->kgts", query_grouped, keys_piece, preferred_element_type=jnp.float32)
        * scale
    )
    scores = jnp.where(allowed, scores, masked_score)
    newmax = jnp.maximum(rowmax, jnp.max(scores, -1))
    weights = jnp.where(allowed, jnp.exp(scores - newmax[..., None]), 0.0)
    accum = jnp.einsum(
        "kgts,skd->kgtd",
        weights.astype(jnp.bfloat16),
        values_piece,
        preferred_element_type=jnp.float32,
    )
    rowsum = jnp.sum(weights, -1)
    accum, rowmax, rowsum = (accum, newmax, rowsum)
    normalized = accum / rowsum[..., None]
    logsum = rowmax + jnp.log(rowsum)
    attention_low = (
        normalized.transpose(2, 0, 1, 3).reshape(count, query_width).astype(jnp.bfloat16)
    )
    output_whole = lax.all_gather(output_weight, "fsdp", axis=0, tiled=True)
    branch_out = jnp.dot(attention_low, output_whole, preferred_element_type=jnp.float32)
    middle = hidden_in + branch_out
    second_scale = norm_scale(middle)
    second = (middle * second_scale * feedforward_gain).astype(jnp.bfloat16)
    gate, up = row_products(
        second,
        (
            lax.all_gather(gate_weight, "fsdp", axis=0, tiled=True),
            lax.all_gather(up_weight, "fsdp", axis=0, tiled=True),
        ),
    )
    sigmoid_gate = jax.nn.sigmoid(gate)
    silu_gate = gate * sigmoid_gate
    hidden_low = (silu_gate * up).astype(jnp.bfloat16)
    (down_out,) = row_products(
        hidden_low, (lax.all_gather(down_weight, "fsdp", axis=0, tiled=True),)
    )
    layer_output = (middle + down_out).astype(jnp.bfloat16)[None]
    cotangent = out_cotangent[0]
    hidden_grad = column_products(
        (cotangent,), lax.all_gather((down_weight,), "fsdp", axis=0, tiled=True)
    )
    up_low = (hidden_grad * silu_gate).astype(jnp.bfloat16)
    gate_low = (hidden_grad * up * sigmoid_gate * (1.0 + gate * (1.0 - sigmoid_gate))).astype(
        jnp.bfloat16
    )
    second_grad = column_products(
        (gate_low, up_low), lax.all_gather((gate_weight, up_weight), "fsdp", axis=0, tiled=True)
    )
    middle_part, feedforward_part = norm_back(middle, second_scale, feedforward_gain, second_grad)
    middle_grad = cotangent.astype(jnp.float32) + middle_part
    middle_low = middle_grad.astype(jnp.bfloat16)
    attention_grad = jnp.einsum(
        "tc,rc->tr", middle_low, output_whole, preferred_element_type=jnp.float32
    )
    attention_grad_low = attention_grad.astype(jnp.bfloat16)
    mixed_grad = attention_grad_low.reshape(count, key_heads, group, head_size).transpose(
        1, 2, 0, 3
    )
    delta = jnp.sum(mixed_grad.astype(jnp.float32) * normalized, -1)

    def cycle_step(index, carry):
        keys_held, values_held, key_acc, value_acc, query_acc = carry
        anchor = (own_index - index) % cycles
        key_pos = lax.dynamic_slice_in_dim(sequence_pos, anchor * count, count)
        keys_piece = keys_held.astype(jnp.bfloat16).reshape(count, key_heads, head_size)
        values_piece = values_held.astype(jnp.bfloat16).reshape(count, key_heads, head_size)
        allowed = token_offsets[:, None] >= key_pos[None, :]
        scores = (
            jnp.einsum(
                "kgtd,skd->kgts", query_grouped, keys_piece, preferred_element_type=jnp.float32
            )
            * scale
        )
        probs = jnp.where(allowed, jnp.exp(scores - logsum[..., None]), 0.0)
        value_acc = value_acc + jnp.einsum(
            "kgts,kgtd->skd",
            probs.astype(jnp.bfloat16),
            mixed_grad,
            preferred_element_type=jnp.float32,
        ).reshape(count, key_width)
        prob_grad = jnp.einsum(
            "kgtd,skd->kgts", mixed_grad, values_piece, preferred_element_type=jnp.float32
        )
        score_grad = (probs * (prob_grad - delta[..., None])).astype(jnp.bfloat16)
        query_acc = (
            query_acc
            + jnp.einsum(
                "kgts,skd->kgtd", score_grad, keys_piece, preferred_element_type=jnp.float32
            )
            * scale
        )
        key_acc = (
            key_acc
            + jnp.einsum(
                "kgts,kgtd->skd", score_grad, query_grouped, preferred_element_type=jnp.float32
            ).reshape(count, key_width)
            * scale
        )
        moved = (
            from_behind(keys_held.astype(jnp.bfloat16), "ctx", 1).astype(keys_held.dtype),
            from_behind(values_held.astype(jnp.bfloat16), "ctx", 1).astype(values_held.dtype),
            from_behind(key_acc.astype(jnp.bfloat16), "ctx", 1).astype(key_acc.dtype),
            from_behind(value_acc.astype(jnp.bfloat16), "ctx", 1).astype(value_acc.dtype),
        )
        return (moved[0], moved[1], moved[2], moved[3], query_acc)

    start_cycle = (
        key_low.astype(jnp.float32),
        value_low.astype(jnp.float32),
        jnp.zeros((count, key_width), jnp.float32),
        jnp.zeros((count, key_width), jnp.float32),
        jnp.zeros((key_heads, group, count, head_size), jnp.float32),
    )
    cycle_done = lax.fori_loop(0, cycles, cycle_step, start_cycle)
    key_acc = cycle_done[2]
    value_acc = cycle_done[3]
    query_acc = cycle_done[4]
    query_rot_grad = query_acc.transpose(2, 0, 1, 3).reshape(count, heads, head_size)
    query_normed_grad = query_rot_grad * cosine + rotate_back(query_rot_grad * sine)
    query_heads_grad, query_part = norm_back(
        query_heads, query_scale, query_gain, query_normed_grad
    )
    query_low_grad = query_heads_grad.reshape(count, query_width).astype(jnp.bfloat16)
    key_rot_grad = key_acc.reshape(count, key_heads, head_size)
    key_normed_grad = key_rot_grad * cosine + rotate_back(key_rot_grad * sine)
    key_heads_grad, key_part = norm_back(key_heads_raw, key_scale, key_norm_gain, key_normed_grad)
    key_low_grad = key_heads_grad.reshape(count, key_width).astype(jnp.bfloat16)
    value_low_grad = value_acc.astype(jnp.bfloat16)
    first_grad = column_products(
        (query_low_grad, key_low_grad, value_low_grad),
        lax.all_gather((query_weight, key_matrix, value_matrix), "fsdp", axis=0, tiled=True),
    )
    input_part, attention_part = norm_back(hidden_in, first_scale, attention_gain, first_grad)
    input_gradient = (middle_grad + input_part)[None]
    rights_first = jnp.concatenate([query_low_grad, key_low_grad, value_low_grad], 1)
    rights_second = jnp.concatenate([gate_low, up_low], 1)
    pairs = (
        (first, rights_first),
        (second, rights_second),
        (middle_low, attention_low),
        (cotangent, hidden_low),
    )
    parts = []
    for left, right in pairs:
        parts.append(jnp.einsum("tr,tc->rc", left, right, preferred_element_type=jnp.float32))
    sums = lax.psum_scatter(
        jnp.concatenate(parts, 1), ("ctx", "fsdp"), scatter_dimension=0, tiled=True
    )
    edges = [0, query_width, query_width + key_width, query_width + 2 * key_width]
    edges = edges + [edges[3] + inner_width, edges[3] + 2 * inner_width]
    edges = edges + [edges[5] + query_width, edges[5] + query_width + inner_width]
    query_gradient = sums[:, edges[0] : edges[1]]
    key_gradient = sums[:, edges[1] : edges[2]]
    value_gradient = sums[:, edges[2] : edges[3]]
    gate_gradient = sums[:, edges[3] : edges[4]]
    up_gradient = sums[:, edges[4] : edges[5]]
    output_gradient = sums[:, edges[5] : edges[6]].T
    down_gradient = sums[:, edges[6] : edges[7]].T
    attention_total, query_total, key_total, feedforward_total = lax.psum(
        (attention_part, query_part, key_part, feedforward_part), ("ctx", "fsdp")
    )
    return (
        layer_output,
        input_gradient,
        attention_total,
        query_gradient,
        key_gradient,
        value_gradient,
        query_total,
        key_total,
        output_gradient,
        feedforward_total,
        gate_gradient,
        up_gradient,
        down_gradient,
    )


def plane_device(
    layer_input,
    token_positions,
    attention_gain,
    query_weight,
    key_matrix,
    value_matrix,
    query_gain,
    key_norm_gain,
    output_weight,
    feedforward_gain,
    gate_weight,
    up_weight,
    down_weight,
    out_cotangent,
):
    n = lax.axis_size("ctx")
    planes = lax.axis_size("fsdp")
    me = lax.axis_index("ctx")
    plane = lax.axis_index("fsdp")
    head = query_gain.shape[0]
    qw = query_weight.shape[1] // n
    kw = key_matrix.shape[1] // n
    fw = gate_weight.shape[1] // n
    group = qw // head
    width = layer_input.shape[2]
    length = token_positions.shape[1]
    f32 = jnp.float32
    bf16 = jnp.bfloat16

    def columns(weight, size):
        return lax.dynamic_slice_in_dim(weight, me * size, size, 1)

    def rows_from_plane(weight, size):
        held = weight.shape[0]
        start = me * size
        piece = lax.dynamic_slice_in_dim(weight, start % held, size, 0)
        return lax.psum(jnp.where(start // held == plane, piece, jnp.zeros_like(piece)), "fsdp")

    def gather_rows(block):
        return lax.all_gather(block, "ctx", axis=0, tiled=True)

    def scatter_rows(partial):
        return lax.psum_scatter(partial.astype(bf16), "ctx", scatter_dimension=0, tiled=True).astype(f32)

    def dot(left, right):
        return jnp.dot(left, right, preferred_element_type=f32)

    def dot_nt(left, right):
        return jnp.einsum("tc,rc->tr", left, right, preferred_element_type=f32)

    w_qkv = lax.all_gather(
        jnp.concatenate([columns(query_weight, qw), columns(key_matrix, kw), columns(value_matrix, kw)], 1),
        "fsdp", axis=0, tiled=True)
    w_gu = lax.all_gather(
        jnp.concatenate([columns(gate_weight, fw), columns(up_weight, fw)], 1), "fsdp", axis=0, tiled=True)
    w_out = rows_from_plane(output_weight, qw)
    w_down = rows_from_plane(down_weight, fw)

    x = layer_input[0].astype(f32)
    first_scale = norm_scale(x)
    first = gather_rows((x * first_scale * attention_gain).astype(bf16))
    dy = gather_rows(out_cotangent[0])
    positions = token_positions[0]
    cosine, sine = rope_tables(positions, head)
    cosine, sine = cosine[:, None, :], sine[:, None, :]

    raw = dot(first, w_qkv)
    q_raw = raw[:, :qw].reshape(length, group, head)
    k_raw = raw[:, qw:qw + kw].reshape(length, 1, head)
    values = raw[:, qw + kw:].astype(bf16)
    q_scale, k_scale = norm_scale(q_raw), norm_scale(k_raw)
    q_n = q_raw * q_scale * query_gain
    k_n = k_raw * k_scale * key_norm_gain
    queries = (q_n * cosine + rotate(q_n) * sine).astype(bf16).transpose(1, 0, 2)
    keys = (k_n * cosine + rotate(k_n) * sine).astype(bf16)[:, 0]
    scale = head ** (-0.5)
    allowed = positions[:, None] >= positions[None, :]
    scores = jnp.einsum("gtd,sd->gts", queries, keys, preferred_element_type=f32) * scale
    scores = jnp.where(allowed, scores, masked_score)
    peak = jnp.max(scores, -1, keepdims=True)
    weights = jnp.exp(scores - peak)
    probs = weights / jnp.sum(weights, -1, keepdims=True)
    mixed = jnp.einsum("gts,sd->gtd", probs.astype(bf16), values, preferred_element_type=f32)
    mixed_low = mixed.transpose(1, 0, 2).reshape(length, qw).astype(bf16)
    middle = x + scatter_rows(dot(mixed_low, w_out))
    second_scale = norm_scale(middle)
    second = gather_rows((middle * second_scale * feedforward_gain).astype(bf16))
    gate_up = dot(second, w_gu)
    gate, up = gate_up[:, :fw], gate_up[:, fw:]
    sig = jax.nn.sigmoid(gate)
    silu = gate * sig
    hidden = (silu * up).astype(bf16)
    layer_output = (middle + scatter_rows(dot(hidden, w_down))).astype(bf16)[None]
    d_hidden = dot_nt(dy, w_down)
    d_up = (d_hidden * silu).astype(bf16)
    d_gate = (d_hidden * up * sig * (1.0 + gate * (1.0 - sig))).astype(bf16)
    d_gu = jnp.concatenate([d_gate, d_up], 1)
    d_second = scatter_rows(dot_nt(d_gu, w_gu))
    middle_part, ff_part = norm_back(middle, second_scale, feedforward_gain, d_second)
    d_middle = out_cotangent[0].astype(f32) + middle_part
    d_mid_all = gather_rows(d_middle.astype(bf16))
    d_mixed = dot_nt(d_mid_all, w_out).astype(bf16).reshape(length, group, head).transpose(1, 0, 2)
    delta = jnp.sum(d_mixed.astype(f32) * mixed, -1, keepdims=True)
    d_probs = jnp.einsum("gtd,sd->gts", d_mixed, values, preferred_element_type=f32)
    d_scores = (probs * (d_probs - delta)).astype(bf16)
    d_v = jnp.einsum("gts,gtd->sd", probs.astype(bf16), d_mixed, preferred_element_type=f32)
    d_q = jnp.einsum("gts,sd->gtd", d_scores, keys, preferred_element_type=f32) * scale
    d_k = jnp.einsum("gts,gtd->sd", d_scores, queries, preferred_element_type=f32) * scale
    d_q = d_q.transpose(1, 0, 2)
    d_k = d_k[:, None]
    d_qn = d_q * cosine + rotate_back(d_q * sine)
    d_kn = d_k * cosine + rotate_back(d_k * sine)
    d_qraw, q_part = norm_back(q_raw, q_scale, query_gain, d_qn)
    d_kraw, k_part = norm_back(k_raw, k_scale, key_norm_gain, d_kn)
    d_qkv = jnp.concatenate(
        [d_qraw.reshape(length, qw).astype(bf16), d_kraw.reshape(length, kw).astype(bf16), d_v.astype(bf16)], 1)
    d_first = scatter_rows(dot_nt(d_qkv, w_qkv))
    input_part, attention_part = norm_back(x, first_scale, attention_gain, d_first)
    input_gradient = (d_middle + input_part)[None]

    def to_owner(left, right):
        grad = jnp.einsum("tr,tc->rc", left, right, preferred_element_type=f32).astype(bf16)
        grad = grad.reshape(n, planes, width // (n * planes), right.shape[1])
        return lax.psum_scatter(grad.transpose(1, 0, 2, 3), "fsdp", scatter_dimension=0, tiled=False)

    def spread(owned):
        return lax.all_to_all(owned, "ctx", split_axis=0, concat_axis=0, tiled=True).astype(f32)

    own_down = to_owner(dy, hidden)
    own_gu = to_owner(second, d_gu)
    own_out = to_owner(d_mid_all, mixed_low)
    own_qkv = to_owner(first, d_qkv)
    got = spread(jnp.concatenate([own_qkv, own_gu, own_out, own_down], 2))

    def part(start, size):
        return got[:, :, start:start + size].transpose(1, 0, 2).reshape(got.shape[1], n * size)

    edge = [0, qw, qw + kw, qw + 2 * kw, qw + 2 * kw + fw, qw + 2 * kw + 2 * fw, 2 * qw + 2 * kw + 2 * fw]
    gains = lax.psum(jnp.concatenate([attention_part, ff_part, q_part, k_part]), ("ctx", "fsdp"))
    return (
        layer_output,
        input_gradient,
        gains[:width],
        part(edge[0], qw),
        part(edge[1], kw),
        part(edge[2], kw),
        gains[2 * width:2 * width + head],
        gains[2 * width + head:],
        part(edge[5], qw).T,
        gains[width:2 * width],
        part(edge[3], fw),
        part(edge[4], fw),
        part(edge[6], fw).T,
    )


def solution(mesh):
    in_specs = (
        P("fsdp", "ctx", None),
        P("fsdp", None),
        P(),
        P("fsdp", None),
        P("fsdp", None),
        P("fsdp", None),
        P(),
        P(),
        P("fsdp", None),
        P(),
        P("fsdp", None),
        P("fsdp", None),
        P("fsdp", None),
        P("fsdp", "ctx", None),
    )
    out_specs = (
        P("fsdp", "ctx", None),
        P("fsdp", "ctx", None),
        P(),
        P(("ctx", "fsdp"), None),
        P(("ctx", "fsdp"), None),
        P(("ctx", "fsdp"), None),
        P(),
        P(),
        P(None, ("ctx", "fsdp")),
        P(),
        P(("ctx", "fsdp"), None),
        P(("ctx", "fsdp"), None),
        P(None, ("ctx", "fsdp")),
    )
    def run(*arguments):
        split = arguments[4].shape[1] // arguments[6].shape[0] == mesh.shape["ctx"]
        return jax.shard_map(
            plane_device if split else on_device,
            mesh=mesh, in_specs=in_specs, out_specs=out_specs, check_vma=False,
        )(*arguments)

    return run
```

```python
import functools

import jax
import jax.numpy as jnp
from jax import lax
from jax.experimental import pallas as pl
from jax.experimental.pallas import tpu as pltpu
from jax.sharding import PartitionSpec as P

epsilon = 1e-06
rope_base = 1000000.0
masked_score = -1e30


def from_behind(block, axis, distance):
    devices = range(lax.axis_size(axis))
    route = [((i - distance) % len(devices), i) for i in devices]
    return lax.ppermute(block, axis, route)


def rotate(value_rows):
    half = value_rows.shape[-1] // 2
    return jnp.concatenate([-value_rows[..., half:], value_rows[..., :half]], -1)


def rotate_back(value_rows):
    half = value_rows.shape[-1] // 2
    return jnp.concatenate([value_rows[..., half:], -value_rows[..., :half]], -1)


def rope_tables(token_offsets, head_size):
    half = head_size // 2
    inverse = rope_base ** (-(jnp.arange(half).astype(jnp.float32) * 2.0) / head_size)
    angles = token_offsets.astype(jnp.float32)[:, None] * inverse[None, :]
    cosine = jnp.cos(angles)
    sine = jnp.sin(angles)
    return (jnp.concatenate([cosine, cosine], -1), jnp.concatenate([sine, sine], -1))


def norm_scale(value_rows):
    return lax.rsqrt(jnp.mean(value_rows * value_rows, -1, keepdims=True) + epsilon)


def norm_back(value_rows, scale, gain, grad):
    weighted = grad * gain
    inner = jnp.mean(weighted * value_rows, -1, keepdims=True)
    result = scale * weighted - value_rows * scale * scale * scale * inner
    gain_part = jnp.sum((grad * value_rows * scale).reshape(-1, gain.shape[0]), 0)
    return (result, gain_part)


def row_products(left, pieces):
    return tuple((jnp.dot(left, piece, preferred_element_type=jnp.float32) for piece in pieces))


def column_products(rights, pieces):
    total = jnp.einsum("tc,rc->tr", rights[0], pieces[0], preferred_element_type=jnp.float32)
    for right, piece in zip(rights[1:], pieces[1:]):
        total = total + jnp.einsum("tc,rc->tr", right, piece, preferred_element_type=jnp.float32)
    return total


def on_device(
    layer_input,
    token_positions,
    attention_gain,
    query_weight,
    key_matrix,
    value_matrix,
    query_gain,
    key_norm_gain,
    output_weight,
    feedforward_gain,
    gate_weight,
    up_weight,
    down_weight,
    out_cotangent,
):
    hidden_in = layer_input[0].astype(jnp.float32)
    count = hidden_in.shape[0]
    head_size = query_gain.shape[0]
    query_width = query_weight.shape[1]
    key_width = key_matrix.shape[1]
    inner_width = gate_weight.shape[1]
    heads = query_width // head_size
    key_heads = key_width // head_size
    group = heads // key_heads
    scale = head_size ** (-0.5)
    cycles = lax.axis_size("ctx")
    own_index = lax.axis_index("ctx")
    sequence_pos = token_positions[0]
    token_offsets = lax.dynamic_slice_in_dim(sequence_pos, own_index * count, count)
    cosine, sine = rope_tables(token_offsets, head_size)
    cosine = cosine[:, None, :]
    sine = sine[:, None, :]
    first_scale = norm_scale(hidden_in)
    first = (hidden_in * first_scale * attention_gain).astype(jnp.bfloat16)
    query_raw, key_unnormed, value_unnormed = row_products(
        first,
        (
            lax.all_gather(query_weight, "fsdp", axis=0, tiled=True),
            lax.all_gather(key_matrix, "fsdp", axis=0, tiled=True),
            lax.all_gather(value_matrix, "fsdp", axis=0, tiled=True),
        ),
    )
    query_heads = query_raw.reshape(count, heads, head_size)
    query_scale = norm_scale(query_heads)
    query_normed = query_heads * query_scale * query_gain
    query_rot = query_normed * cosine + rotate(query_normed) * sine
    query_grouped = (
        query_rot.reshape(count, key_heads, group, head_size)
        .transpose(1, 2, 0, 3)
        .astype(jnp.bfloat16)
    )
    key_heads_raw = key_unnormed.reshape(count, key_heads, head_size)
    key_scale = norm_scale(key_heads_raw)
    key_normed = key_heads_raw * key_scale * key_norm_gain
    key_low = (
        (key_normed * cosine + rotate(key_normed) * sine)
        .reshape(count, key_width)
        .astype(jnp.bfloat16)
    )
    value_low = value_unnormed.astype(jnp.bfloat16)
    rowmax = jnp.full((key_heads, group, count), masked_score, jnp.float32)
    keys_piece = lax.all_gather(key_low, "ctx", axis=0, tiled=True).reshape(
        -1, key_heads, head_size
    )
    values_piece = lax.all_gather(value_low, "ctx", axis=0, tiled=True).reshape(
        -1, key_heads, head_size
    )
    key_pos = sequence_pos
    allowed = token_offsets[:, None] >= key_pos[None, :]
    scores = (
        jnp.einsum("kgtd,skd->kgts", query_grouped, keys_piece, preferred_element_type=jnp.float32)
        * scale
    )
    scores = jnp.where(allowed, scores, masked_score)
    newmax = jnp.maximum(rowmax, jnp.max(scores, -1))
    weights = jnp.where(allowed, jnp.exp(scores - newmax[..., None]), 0.0)
    accum = jnp.einsum(
        "kgts,skd->kgtd",
        weights.astype(jnp.bfloat16),
        values_piece,
        preferred_element_type=jnp.float32,
    )
    rowsum = jnp.sum(weights, -1)
    accum, rowmax, rowsum = (accum, newmax, rowsum)
    normalized = accum / rowsum[..., None]
    logsum = rowmax + jnp.log(rowsum)
    attention_low = (
        normalized.transpose(2, 0, 1, 3).reshape(count, query_width).astype(jnp.bfloat16)
    )
    output_whole = lax.all_gather(output_weight, "fsdp", axis=0, tiled=True)
    branch_out = jnp.dot(attention_low, output_whole, preferred_element_type=jnp.float32)
    middle = hidden_in + branch_out
    second_scale = norm_scale(middle)
    second = (middle * second_scale * feedforward_gain).astype(jnp.bfloat16)
    gate, up = row_products(
        second,
        (
            lax.all_gather(gate_weight, "fsdp", axis=0, tiled=True),
            lax.all_gather(up_weight, "fsdp", axis=0, tiled=True),
        ),
    )
    sigmoid_gate = jax.nn.sigmoid(gate)
    silu_gate = gate * sigmoid_gate
    hidden_low = (silu_gate * up).astype(jnp.bfloat16)
    (down_out,) = row_products(
        hidden_low, (lax.all_gather(down_weight, "fsdp", axis=0, tiled=True),)
    )
    layer_output = (middle + down_out).astype(jnp.bfloat16)[None]
    cotangent = out_cotangent[0]
    hidden_grad = column_products(
        (cotangent,), lax.all_gather((down_weight,), "fsdp", axis=0, tiled=True)
    )
    up_low = (hidden_grad * silu_gate).astype(jnp.bfloat16)
    gate_low = (hidden_grad * up * sigmoid_gate * (1.0 + gate * (1.0 - sigmoid_gate))).astype(
        jnp.bfloat16
    )
    second_grad = column_products(
        (gate_low, up_low), lax.all_gather((gate_weight, up_weight), "fsdp", axis=0, tiled=True)
    )
    middle_part, feedforward_part = norm_back(middle, second_scale, feedforward_gain, second_grad)
    middle_grad = cotangent.astype(jnp.float32) + middle_part
    middle_low = middle_grad.astype(jnp.bfloat16)
    attention_grad = jnp.einsum(
        "tc,rc->tr", middle_low, output_whole, preferred_element_type=jnp.float32
    )
    attention_grad_low = attention_grad.astype(jnp.bfloat16)
    mixed_grad = attention_grad_low.reshape(count, key_heads, group, head_size).transpose(
        1, 2, 0, 3
    )
    delta = jnp.sum(mixed_grad.astype(jnp.float32) * normalized, -1)

    def cycle_step(index, carry):
        keys_held, values_held, key_acc, value_acc, query_acc = carry
        anchor = (own_index - index) % cycles
        key_pos = lax.dynamic_slice_in_dim(sequence_pos, anchor * count, count)
        keys_piece = keys_held.astype(jnp.bfloat16).reshape(count, key_heads, head_size)
        values_piece = values_held.astype(jnp.bfloat16).reshape(count, key_heads, head_size)
        allowed = token_offsets[:, None] >= key_pos[None, :]
        scores = (
            jnp.einsum(
                "kgtd,skd->kgts", query_grouped, keys_piece, preferred_element_type=jnp.float32
            )
            * scale
        )
        probs = jnp.where(allowed, jnp.exp(scores - logsum[..., None]), 0.0)
        value_acc = value_acc + jnp.einsum(
            "kgts,kgtd->skd",
            probs.astype(jnp.bfloat16),
            mixed_grad,
            preferred_element_type=jnp.float32,
        ).reshape(count, key_width)
        prob_grad = jnp.einsum(
            "kgtd,skd->kgts", mixed_grad, values_piece, preferred_element_type=jnp.float32
        )
        score_grad = (probs * (prob_grad - delta[..., None])).astype(jnp.bfloat16)
        query_acc = (
            query_acc
            + jnp.einsum(
                "kgts,skd->kgtd", score_grad, keys_piece, preferred_element_type=jnp.float32
            )
            * scale
        )
        key_acc = (
            key_acc
            + jnp.einsum(
                "kgts,kgtd->skd", score_grad, query_grouped, preferred_element_type=jnp.float32
            ).reshape(count, key_width)
            * scale
        )
        moved = (
            from_behind(keys_held.astype(jnp.bfloat16), "ctx", 1).astype(keys_held.dtype),
            from_behind(values_held.astype(jnp.bfloat16), "ctx", 1).astype(values_held.dtype),
            from_behind(key_acc.astype(jnp.bfloat16), "ctx", 1).astype(key_acc.dtype),
            from_behind(value_acc.astype(jnp.bfloat16), "ctx", 1).astype(value_acc.dtype),
        )
        return (moved[0], moved[1], moved[2], moved[3], query_acc)

    start_cycle = (
        key_low.astype(jnp.float32),
        value_low.astype(jnp.float32),
        jnp.zeros((count, key_width), jnp.float32),
        jnp.zeros((count, key_width), jnp.float32),
        jnp.zeros((key_heads, group, count, head_size), jnp.float32),
    )
    cycle_done = lax.fori_loop(0, cycles, cycle_step, start_cycle)
    key_acc = cycle_done[2]
    value_acc = cycle_done[3]
    query_acc = cycle_done[4]
    query_rot_grad = query_acc.transpose(2, 0, 1, 3).reshape(count, heads, head_size)
    query_normed_grad = query_rot_grad * cosine + rotate_back(query_rot_grad * sine)
    query_heads_grad, query_part = norm_back(
        query_heads, query_scale, query_gain, query_normed_grad
    )
    query_low_grad = query_heads_grad.reshape(count, query_width).astype(jnp.bfloat16)
    key_rot_grad = key_acc.reshape(count, key_heads, head_size)
    key_normed_grad = key_rot_grad * cosine + rotate_back(key_rot_grad * sine)
    key_heads_grad, key_part = norm_back(key_heads_raw, key_scale, key_norm_gain, key_normed_grad)
    key_low_grad = key_heads_grad.reshape(count, key_width).astype(jnp.bfloat16)
    value_low_grad = value_acc.astype(jnp.bfloat16)
    first_grad = column_products(
        (query_low_grad, key_low_grad, value_low_grad),
        lax.all_gather((query_weight, key_matrix, value_matrix), "fsdp", axis=0, tiled=True),
    )
    input_part, attention_part = norm_back(hidden_in, first_scale, attention_gain, first_grad)
    input_gradient = (middle_grad + input_part)[None]
    rights_first = jnp.concatenate([query_low_grad, key_low_grad, value_low_grad], 1)
    rights_second = jnp.concatenate([gate_low, up_low], 1)
    pairs = (
        (first, rights_first),
        (second, rights_second),
        (middle_low, attention_low),
        (cotangent, hidden_low),
    )
    parts = []
    for left, right in pairs:
        parts.append(jnp.einsum("tr,tc->rc", left, right, preferred_element_type=jnp.float32))
    sums = lax.psum_scatter(
        jnp.concatenate(parts, 1), ("ctx", "fsdp"), scatter_dimension=0, tiled=True
    )
    edges = [0, query_width, query_width + key_width, query_width + 2 * key_width]
    edges = edges + [edges[3] + inner_width, edges[3] + 2 * inner_width]
    edges = edges + [edges[5] + query_width, edges[5] + query_width + inner_width]
    query_gradient = sums[:, edges[0] : edges[1]]
    key_gradient = sums[:, edges[1] : edges[2]]
    value_gradient = sums[:, edges[2] : edges[3]]
    gate_gradient = sums[:, edges[3] : edges[4]]
    up_gradient = sums[:, edges[4] : edges[5]]
    output_gradient = sums[:, edges[5] : edges[6]].T
    down_gradient = sums[:, edges[6] : edges[7]].T
    attention_total, query_total, key_total, feedforward_total = lax.psum(
        (attention_part, query_part, key_part, feedforward_part), ("ctx", "fsdp")
    )
    return (
        layer_output,
        input_gradient,
        attention_total,
        query_gradient,
        key_gradient,
        value_gradient,
        query_total,
        key_total,
        output_gradient,
        feedforward_total,
        gate_gradient,
        up_gradient,
        down_gradient,
    )


MESH = pl.DeviceIdType.MESH
f32 = jnp.float32
bf16 = jnp.bfloat16


def dot(left, right):
    return jnp.dot(left, right, preferred_element_type=f32)


def dot_nt(left, right):
    return lax.dot_general(left, right, (((1,), (1,)), ((), ())), preferred_element_type=f32)


def dot_tn(left, right):
    return lax.dot_general(left, right, (((0,), (0,)), ((), ())), preferred_element_type=f32)


def layer_kernel(
    n, planes, block, head, group, fw,
    x_ref, dy_ref, pos_col, pos_row, cos_ref, sin_ref, ag_ref, fg_ref, qg_ref, kg_ref,
    wq, wk, wv, wo, wg, wu, wd,
    out_ref, dx_ref, gains_ref, got_qkv, got_gu, got_out, got_down,
    w_qkv, w_gu, w_out, w_down, t_out, t_down,
    first, dy_all, second, dmid,
    raw, queries, keys, values, probs, mixed, mixed_low,
    hidden, d_gu, d_mixed, d_qkv, dk_acc, dv_acc, dq_acc,
    stage_down, stage_gu, stage_out, stage_qkv,
    land_down, land_gu, land_out, land_qkv,
    own_down, own_gu, own_out, own_qkv,
    rs_sa, rs_ra, rs_sb, rs_rb, rs_acc,
    middle, d_middle, gain_own, gain_plane, gain_all,
    local_sem, wz_send, wz_recv, hand_send, hand_recv,
    ag_send, ag_recv, ra_send, ra_recv, rb_send, rb_recv,
    zr_send, zr_recv, aa_send, aa_recv, gp_send, gp_recv, gz_send, gz_recv,
):
    c = lax.axis_index("ctx")
    z = lax.axis_index("fsdp")
    cy, cx, ck = lax.div(c, 4), lax.rem(lax.div(c, 2), 2), lax.rem(c, 2)
    qw, kw = group * head, head
    width = x_ref.shape[1]
    scale = head ** (-0.5)
    log2e = 1.4426950408889634

    def partner(j):
        y = lax.rem(cy + j // 4, 2)
        x = lax.rem(cx + (j // 2) % 2, 2)
        k = lax.rem(ck + j % 2, 2)
        return y * 4 + x * 2 + k

    def rows(start, size):
        return pl.ds(pl.multiple_of(start * size, size), size)

    def remote(src, dst, send, recv, ctx, plane):
        return pltpu.make_async_remote_copy(
            src_ref=src, dst_ref=dst, send_sem=send, recv_sem=recv,
            device_id={"ctx": ctx, "fsdp": plane}, device_id_type=MESH,
        )

    in_plane, along = [], []

    def launch(started, copy, when=None):
        if when is None:
            copy().start()
        else:
            pl.when(when)(lambda: copy().start())
        started.append((copy, when))

    def drain(started):
        for copy, when in started:
            if when is None:
                copy().wait_send()
            else:
                pl.when(when)(lambda copy=copy: copy().wait_send())
        started.clear()

    own_rows = wq.shape[0]
    out_rows = wo.shape[0] // n
    down_rows = wd.shape[0] // n

    def own_slices():
        mine = rows(z, own_rows)
        return [
            (wq.at[:, rows(c, qw)], w_qkv.at[mine, 0:qw]),
            (wk.at[:, rows(c, kw)], w_qkv.at[mine, qw:qw + kw]),
            (wv.at[:, rows(c, kw)], w_qkv.at[mine, qw + kw:qw + 2 * kw]),
            (wo.at[rows(c, out_rows)], t_out.at[rows(z, out_rows)]),
            (wg.at[:, rows(c, fw)], w_gu.at[mine, 0:fw]),
            (wu.at[:, rows(c, fw)], w_gu.at[mine, fw:2 * fw]),
            (wd.at[rows(c, down_rows)], t_down.at[rows(z, down_rows)]),
        ]

    local = [pltpu.make_async_copy(src, dst, local_sem.at[i]) for i, (src, dst) in enumerate(own_slices())]
    for copy in local:
        copy.start()

    barrier = pltpu.get_barrier_semaphore()
    for j in range(1, n):
        pl.semaphore_signal(barrier, inc=1, device_id={"ctx": partner(j), "fsdp": z}, device_id_type=MESH)
    for d in range(1, planes):
        pl.semaphore_signal(
            barrier, inc=1, device_id={"ctx": c, "fsdp": lax.rem(z + d, planes)}, device_id_type=MESH)
    pl.semaphore_wait(barrier, n + planes - 2)

    def inside(t):
        return jnp.logical_and(t >= 0, t < planes)

    def weight_copy(buf, size, w, slot, origin, target):
        part = buf.at[rows(origin, size)]
        return remote(part, part, wz_send.at[w, slot], wz_recv.at[w, origin], c, target)

    def weight_start(buf, size, w):
        for slot, d in enumerate((1, -1, 2, -2)):
            launch(along, lambda slot=slot, d=d: weight_copy(buf, size, w, slot, z, z + d), inside(z + d))

    def weight_receive(buf, size, w):
        for d in range(1, planes):
            for side, sign in enumerate((1, -1)):
                origin = z - sign * d
                valid = inside(origin)
                pl.when(valid)(
                    lambda origin=origin: weight_copy(buf, size, w, 0, origin, z).wait_recv())
                if 2 <= d < planes - 1:
                    slot = 4 + 2 * (d - 2) + side
                    launch(
                        along, lambda slot=slot, origin=origin, sign=sign: weight_copy(
                            buf, size, w, slot, origin, z + sign),
                        jnp.logical_and(valid, inside(z + sign)))

    def gather_copy(buf, g, j, send, origin, target):
        part = buf.at[rows(origin, block)]
        return remote(part, part, ag_send.at[g, send], ag_recv.at[g, j], target, z)

    def gather_start(buf, g):
        for j in (6, 2, 4, 1):
            launch(in_plane, lambda j=j: gather_copy(buf, g, j, j, c, partner(j)))

    def gather_finish(buf, g):
        for j in (2, 4, 6):
            gather_copy(buf, g, j, j, partner(j), c).wait_recv()
            launch(in_plane, lambda j=j: gather_copy(buf, g, j + 1, j + 1, partner(j), partner(1)))
        for j in (1, 3, 5, 7):
            gather_copy(buf, g, j, j, partner(j), c).wait_recv()

    def sum_pair_copy(s, slot):
        return remote(rs_sa.at[s % 2, slot], rs_ra.at[s % 2, slot], ra_send.at[s, slot], ra_recv.at[s, slot], partner(1), z)

    def sum_chip_copy(s, slot):
        return remote(
            rs_sb.at[s % 2, slot], rs_rb.at[s % 2, slot], rb_send.at[s, slot], rb_recv.at[s, slot], partner(2 * slot), z)

    def sum_start(s, partial):
        for slot in (3, 2, 1, 0):
            rs_sa[s % 2, slot] = partial(partner(2 * slot + 1)).astype(bf16)
            launch(in_plane, lambda slot=slot: sum_pair_copy(s, slot))
        for slot in (3, 2, 1):
            value = partial(partner(2 * slot))
            sum_pair_copy(s, slot).wait_recv()
            rs_sb[s % 2, slot] = (value + rs_ra[s % 2, slot].astype(f32)).astype(bf16)
            launch(in_plane, lambda slot=slot: sum_chip_copy(s, slot))
        value = partial(c)
        sum_pair_copy(s, 0).wait_recv()
        rs_acc[s % 2] = value + rs_ra[s % 2, 0].astype(f32)

    def sum_finish(s):
        total = rs_acc[s % 2]
        for slot in (1, 2, 3):
            sum_chip_copy(s, slot).wait_recv()
            total = total + rs_rb[s % 2, slot].astype(f32)
        return total

    per = block // planes

    def weight_grad(m, left, right, stage, land):
        def body(i, carry):
            grad = dot_tn(left[:, rows(i, block)], right[...])
            for t in range(planes):
                stage[t, i] = grad[t * per:(t + 1) * per].astype(bf16)
            return carry

        lax.fori_loop(0, n, body, 0)
        for d in range(1, planes):
            launch(along, lambda d=d: grad_copy(m, stage, land, d))

    def grad_copy(m, stage, land, d):
        target = lax.rem(z + d, planes)
        return remote(stage.at[target], land.at[d], zr_send.at[m, d], zr_recv.at[m, d], c, target)

    def owner_copy(m, own, got, j):
        return remote(own.at[partner(j)], got.at[c], aa_send.at[m, j], aa_recv.at[m, j], partner(j), z)

    def hand_out(m, stage, land, own, got):
        for d in range(1, planes):
            grad_copy(m, stage, land, d).wait_recv()

        def body(i, carry):
            total = stage[z, i].astype(f32)
            for d in range(1, planes):
                total = total + land[d, i].astype(f32)
            own[i] = total.astype(bf16)
            return carry

        lax.fori_loop(0, n, body, 0)
        for j in (6, 7, 2, 3, 4, 5, 1):
            launch(in_plane, lambda j=j: owner_copy(m, own, got, j))
        got[c] = own[c]

    def hand_receive(m, own, got):
        for j in range(1, n):
            owner_copy(m, own, got, j).wait_recv()

    for copy in local[:3]:
        copy.wait()
    weight_start(w_qkv, own_rows, 0)
    x = x_ref[...].astype(f32)
    x_scale = lax.rsqrt(jnp.mean(x * x, -1, keepdims=True) + epsilon)
    first[rows(c, block)] = (x * x_scale * ag_ref[...]).astype(bf16)
    gather_start(first, 0)
    dy_all[rows(c, block)] = dy_ref[...]
    gather_finish(first, 0)
    gather_start(dy_all, 1)
    for copy in local[3:]:
        copy.wait()
    weight_receive(w_qkv, own_rows, 0)
    weight_start(t_out, out_rows, 1)
    gather_finish(dy_all, 1)

    def turn(value, at):
        return value * cos_ref[at] + pltpu.roll(value, head // 2, 1) * sin_ref[at]

    def turn_back(grad, at):
        return grad * cos_ref[at] - pltpu.roll(grad, head // 2, 1) * sin_ref[at]

    def project(i, carry):
        at = rows(i, block)
        result = dot(first[at], w_qkv[...])
        raw[at] = result[:, :qw + kw]
        values[at] = result[:, qw + kw:].astype(bf16)
        for h in range(group + 1):
            part = result[:, h * head:(h + 1) * head]
            inv = lax.rsqrt(jnp.mean(part * part, -1, keepdims=True) + epsilon)
            gain = qg_ref[...] if h < group else kg_ref[...]
            turned = turn(part * inv * gain, at).astype(bf16)
            if h < group:
                queries[at, h * head:(h + 1) * head] = turned
            else:
                keys[at] = turned
        return carry

    lax.fori_loop(0, n, project, 0)

    def hand_copy(buf, size, dst, w, j):
        return remote(
            buf.at[rows(j, size)], dst.at[rows(lax.rem(c, 4), size)],
            hand_send.at[w, j], hand_recv.at[w, lax.rem(c, 4)], 2 * j + cy, z)

    def hand_over(buf, size, dst, w):
        for j in range(planes):
            away = 2 * j + cy != c
            launch(in_plane, lambda j=j: hand_copy(buf, size, dst, w, j), away)

            @pl.when(jnp.logical_not(away))
            def _():
                dst[rows(lax.rem(c, 4), size)] = buf[rows(j, size)]

    def hand_arrive(buf, size, dst, w):
        for i in range(4):
            @pl.when(4 * ck + i != c)
            def _():
                remote(
                    buf.at[rows(0, size)], dst.at[rows(i, size)],
                    hand_send.at[w, 0], hand_recv.at[w, i], c, z).wait_recv()

    weight_receive(t_out, out_rows, 1)
    hand_over(t_out, out_rows, w_out, 0)
    weight_start(w_gu, own_rows, 2)
    weight_start(t_down, down_rows, 3)

    def stack(ref, at):
        return jnp.concatenate([ref[at, h * head:(h + 1) * head] for h in range(group)], 0)

    def attend(i, carry):
        at = rows(i, block)
        scores = dot_nt(stack(queries, at), keys[...])
        allowed = pos_col[at] >= pos_row[...]
        scores = jnp.concatenate(
            [jnp.where(allowed, scores[h * block:(h + 1) * block], masked_score) for h in range(group)], 0)
        peak = jnp.max(scores, -1, keepdims=True)
        weight = jnp.exp2((scores - peak) * (scale * log2e))
        prob = (weight * (1.0 / jnp.sum(weight, -1, keepdims=True))).astype(bf16)
        probs[i] = prob
        result = dot(prob, values[...])
        for h in range(group):
            part = result[h * block:(h + 1) * block]
            mixed[at, h * head:(h + 1) * head] = part
            mixed_low[at, h * head:(h + 1) * head] = part.astype(bf16)
        return carry

    lax.fori_loop(0, n, attend, 0)
    hand_arrive(t_out, out_rows, w_out, 0)

    sum_start(0, lambda d: dot(mixed_low[rows(d, block)], w_out[...]))
    weight_receive(w_gu, own_rows, 2)
    mid = x_ref[...].astype(f32) + sum_finish(0)
    middle[...] = mid
    mid_scale = lax.rsqrt(jnp.mean(mid * mid, -1, keepdims=True) + epsilon)
    second[rows(c, block)] = (mid * mid_scale * fg_ref[...]).astype(bf16)
    gather_start(second, 2)
    weight_receive(t_down, down_rows, 3)
    hand_over(t_down, down_rows, w_down, 1)
    gather_finish(second, 2)
    hand_arrive(t_down, down_rows, w_down, 1)

    def feed(i, carry):
        at = rows(i, block)
        both = dot(second[at], w_gu[...])
        back = dot_nt(dy_all[at], w_down[...])
        gate, up = both[:, :fw], both[:, fw:]
        sig = 1.0 / (1.0 + jnp.exp(-gate))
        silu = gate * sig
        hidden[at] = (silu * up).astype(bf16)
        d_gu[at, :fw] = (back * up * sig * (1.0 + gate * (1.0 - sig))).astype(bf16)
        d_gu[at, fw:] = (back * silu).astype(bf16)
        return carry

    lax.fori_loop(0, n, feed, 0)
    sum_start(1, lambda d: dot_nt(d_gu[rows(d, block)], w_gu[...]))
    weight_grad(0, dy_all, hidden, stage_down, land_down)
    weight_grad(1, second, d_gu, stage_gu, land_gu)
    d_second = sum_finish(1)

    def norm_back(value, gain, grad):
        inv = lax.rsqrt(jnp.mean(value * value, -1, keepdims=True) + epsilon)
        weighted = grad * gain
        inner = jnp.mean(weighted * value, -1, keepdims=True)
        result = inv * weighted - value * (inv * inv * inv * inner)
        return result, jnp.sum(grad * value * inv, 0, keepdims=True)

    gain_own[...] = jnp.zeros_like(gain_own)
    part, gain_own[1:2, :] = norm_back(middle[...], fg_ref[...], d_second)
    d_mid = dy_ref[...].astype(f32) + part
    d_middle[...] = d_mid
    dmid[rows(c, block)] = d_mid.astype(bf16)
    gather_start(dmid, 3)
    gather_finish(dmid, 3)
    drain(in_plane)
    sum_start(2, lambda d: dot(hidden[rows(d, block)], w_down[...]))
    weight_grad(2, dmid, mixed_low, stage_out, land_out)

    dk_acc[...] = jnp.zeros_like(dk_acc)
    dv_acc[...] = jnp.zeros_like(dv_acc)

    def attend_back(i, carry):
        at = rows(i, block)
        d_mix = dot_nt(dmid[at], w_out[...]).astype(bf16)
        d_mix = jnp.concatenate([d_mix[:, h * head:(h + 1) * head] for h in range(group)], 0)
        delta = jnp.sum(d_mix.astype(f32) * stack(mixed, at), -1, keepdims=True)
        prob = probs[i]
        d_prob = dot_nt(d_mix, values[...])
        d_score = (prob.astype(f32) * (d_prob - delta)).astype(bf16)
        dv_acc[...] += dot_tn(prob, d_mix)
        dk_acc[...] += dot_tn(d_score, stack(queries, at))
        d_query = dot(d_score, keys[...]) * scale
        for h in range(group):
            dq_acc[at, h * head:(h + 1) * head] = d_query[h * block:(h + 1) * block]
        return carry

    lax.fori_loop(0, n, attend_back, 0)

    def project_back(i, carry):
        at = rows(i, block)
        q_sum, k_sum = carry
        for h in range(group + 1):
            if h < group:
                grad, gain = dq_acc[at, h * head:(h + 1) * head], qg_ref[...]
            else:
                grad, gain = dk_acc[at] * scale, kg_ref[...]
            part, gain_part = norm_back(raw[at, h * head:(h + 1) * head], gain, turn_back(grad, at))
            d_qkv[at, h * head:(h + 1) * head] = part.astype(bf16)
            if h < group:
                q_sum = q_sum + gain_part
            else:
                k_sum = k_sum + gain_part
        d_qkv[at, qw + kw:] = dv_acc[at].astype(bf16)
        return q_sum, k_sum

    zero = jnp.zeros((1, head), f32)
    q_sum, k_sum = lax.fori_loop(0, n, project_back, (zero, zero))
    gain_own[2:3, 0:head] = q_sum
    gain_own[3:4, 0:head] = k_sum

    weight_grad(3, first, d_qkv, stage_qkv, land_qkv)
    sum_start(3, lambda d: dot_nt(d_qkv[rows(d, block)], w_qkv[...]))
    out_ref[...] = (middle[...] + sum_finish(2)).astype(bf16)
    hand_out(0, stage_down, land_down, own_down, got_down)
    hand_out(1, stage_gu, land_gu, own_gu, got_gu)
    hand_out(2, stage_out, land_out, own_out, got_out)
    x_part, gain_own[0:1, :] = norm_back(x_ref[...].astype(f32), ag_ref[...], sum_finish(3))
    dx_ref[...] = d_middle[...] + x_part

    def gain_plane_copy(j):
        return remote(gain_own, gain_plane.at[c], gp_send.at[j], gp_recv.at[j], partner(j), z)

    def gain_copy(d):
        return remote(gain_all.at[z], gain_all.at[z], gz_send.at[d], gz_recv.at[d], c, lax.rem(z + d, planes))

    for j in range(1, n):
        launch(in_plane, lambda j=j: gain_plane_copy(j))
    gain_plane[c] = gain_own[...]
    for j in range(1, n):
        gain_plane_copy(j).wait_recv()
    total = gain_plane[0]
    for i in range(1, n):
        total = total + gain_plane[i]
    gain_all[z] = total
    for d in range(1, planes):
        launch(along, lambda d=d: gain_copy(d))
    for d in range(1, planes):
        origin = gain_all.at[lax.rem(z + planes - d, planes)]
        remote(origin, origin, gz_send.at[d], gz_recv.at[d], c, z).wait_recv()
    total = gain_all[0]
    for i in range(1, planes):
        total = total + gain_all[i]
    gains_ref[...] = total

    hand_out(3, stage_qkv, land_qkv, own_qkv, got_qkv)
    hand_receive(0, own_down, got_down)
    hand_receive(1, own_gu, got_gu)
    hand_receive(2, own_out, got_out)
    hand_receive(3, own_qkv, got_qkv)
    drain(in_plane)
    drain(along)


def plane_device(
    layer_input,
    token_positions,
    attention_gain,
    query_weight,
    key_matrix,
    value_matrix,
    query_gain,
    key_norm_gain,
    output_weight,
    feedforward_gain,
    gate_weight,
    up_weight,
    down_weight,
    out_cotangent,
):
    n = lax.axis_size("ctx")
    planes = lax.axis_size("fsdp")
    block, width = layer_input.shape[1:]
    length = token_positions.shape[1]
    head = query_gain.shape[0]
    qw = query_weight.shape[1] // n
    kw = key_matrix.shape[1] // n
    fw = gate_weight.shape[1] // n
    group = qw // head
    per = block // planes
    positions = token_positions[0]
    cosine, sine = rope_tables(positions, head)
    half = head // 2
    sine = jnp.concatenate([-sine[:, :half], sine[:, half:]], -1)
    vmem = pl.BlockSpec(memory_space=pltpu.VMEM)
    hbm = pl.BlockSpec(memory_space=pl.ANY)
    dma = pltpu.SemaphoreType.DMA
    sizes = (fw, 2 * fw, qw, qw + 2 * kw)
    low = lambda *shape: pltpu.VMEM(shape, bf16)
    wide = lambda *shape: pltpu.VMEM(shape, f32)
    scratch = [
        low(width, qw + 2 * kw), low(width, 2 * fw), low(qw, width), low(fw, width),
        low(planes * (output_weight.shape[0] // n), width), low(planes * (down_weight.shape[0] // n), width),
        low(length, width), low(length, width), low(length, width), low(length, width),
        wide(length, qw + kw), low(length, qw), low(length, kw), low(length, kw),
        low(n, group * block, length), wide(length, qw), low(length, qw),
        low(length, fw), low(length, 2 * fw), low(length, qw), low(length, qw + 2 * kw),
        wide(length, kw), wide(length, kw), wide(length, qw),
    ]
    scratch += [low(planes, n, per, size) for size in sizes]
    scratch += [low(planes, n, per, size) for size in sizes]
    scratch += [low(n, per, size) for size in sizes]
    scratch += [low(2, 4, block, width) for _ in range(4)] + [wide(2, block, width)]
    scratch += [
        wide(block, width), wide(block, width), wide(8, width), wide(n, 8, width), wide(planes, 8, width),
        dma((7,)), dma((4, 4 + 2 * planes)), dma((4, planes)), dma((2, planes)), dma((2, 4)),
        dma((4, n)), dma((4, n)), dma((4, 4)), dma((4, 4)), dma((4, 4)), dma((4, 4)),
        dma((4, planes)), dma((4, planes)), dma((4, n)), dma((4, n)), dma((n,)), dma((n,)),
        dma((planes,)), dma((planes,)),
    ]
    shapes = [
        jax.ShapeDtypeStruct((block, width), bf16),
        jax.ShapeDtypeStruct((block, width), f32),
        jax.ShapeDtypeStruct((8, width), f32),
    ] + [jax.ShapeDtypeStruct((n, per, size), bf16) for size in (sizes[3], sizes[1], sizes[2], sizes[0])]
    layer_output, input_gradient, gains, got_qkv, got_gu, got_out, got_down = pl.pallas_call(
        functools.partial(layer_kernel, n, planes, block, head, group, fw),
        out_shape=shapes,
        in_specs=[vmem] * 10 + [hbm] * 7,
        out_specs=[vmem] * 7,
        scratch_shapes=scratch,
        compiler_params=pltpu.CompilerParams(
            collective_id=0, has_side_effects=True, vmem_limit_bytes=60 * 1024 * 1024),
    )(
        layer_input[0], out_cotangent[0], positions[:, None], positions[None, :], cosine, sine,
        attention_gain[None], feedforward_gain[None], query_gain[None], key_norm_gain[None],
        query_weight, key_matrix, value_matrix, output_weight, gate_weight, up_weight, down_weight,
    )

    def part(got, start, size):
        piece = got[:, :, start:start + size].astype(f32)
        return piece.transpose(1, 0, 2).reshape(per, n * size)

    return (
        layer_output[None],
        input_gradient[None],
        gains[0],
        part(got_qkv, 0, qw),
        part(got_qkv, qw, kw),
        part(got_qkv, qw + kw, kw),
        gains[2, :head],
        gains[3, :head],
        part(got_out, 0, qw).T,
        gains[1],
        part(got_gu, 0, fw),
        part(got_gu, fw, fw),
        part(got_down, 0, fw).T,
    )


def solution(mesh):
    in_specs = (
        P("fsdp", "ctx", None),
        P("fsdp", None),
        P(),
        P("fsdp", None),
        P("fsdp", None),
        P("fsdp", None),
        P(),
        P(),
        P("fsdp", None),
        P(),
        P("fsdp", None),
        P("fsdp", None),
        P("fsdp", None),
        P("fsdp", "ctx", None),
    )
    out_specs = (
        P("fsdp", "ctx", None),
        P("fsdp", "ctx", None),
        P(),
        P(("ctx", "fsdp"), None),
        P(("ctx", "fsdp"), None),
        P(("ctx", "fsdp"), None),
        P(),
        P(),
        P(None, ("ctx", "fsdp")),
        P(),
        P(("ctx", "fsdp"), None),
        P(("ctx", "fsdp"), None),
        P(None, ("ctx", "fsdp")),
    )

    def run(*arguments):
        n, planes = mesh.shape["ctx"], mesh.shape["fsdp"]
        key_heads = arguments[4].shape[1] // arguments[6].shape[0]
        whole_heads = n == 8 and planes == 4 and key_heads == n
        return jax.shard_map(
            plane_device if whole_heads else on_device,
            mesh=mesh, in_specs=in_specs, out_specs=out_specs, check_vma=False,
        )(*arguments)

    return run
```

```python
import functools

import jax
import jax.numpy as jnp
import numpy as np
from jax import lax
from jax.experimental import pallas as pl
from jax.experimental.pallas import tpu as pltpu
from jax.sharding import PartitionSpec as P

epsilon = 1e-06
rope_base = 1000000.0
masked_score = -1e30


def from_behind(block, axis, distance):
    devices = range(lax.axis_size(axis))
    route = [((i - distance) % len(devices), i) for i in devices]
    return lax.ppermute(block, axis, route)


def rotate(value_rows):
    half = value_rows.shape[-1] // 2
    return jnp.concatenate([-value_rows[..., half:], value_rows[..., :half]], -1)


def rotate_back(value_rows):
    half = value_rows.shape[-1] // 2
    return jnp.concatenate([value_rows[..., half:], -value_rows[..., :half]], -1)


def rope_tables(token_offsets, head_size):
    half = head_size // 2
    inverse = rope_base ** (-(jnp.arange(half).astype(jnp.float32) * 2.0) / head_size)
    angles = token_offsets.astype(jnp.float32)[:, None] * inverse[None, :]
    cosine = jnp.cos(angles)
    sine = jnp.sin(angles)
    return (jnp.concatenate([cosine, cosine], -1), jnp.concatenate([sine, sine], -1))


def norm_scale(value_rows):
    return lax.rsqrt(jnp.mean(value_rows * value_rows, -1, keepdims=True) + epsilon)


def norm_back(value_rows, scale, gain, grad):
    weighted = grad * gain
    inner = jnp.mean(weighted * value_rows, -1, keepdims=True)
    result = scale * weighted - value_rows * scale * scale * scale * inner
    gain_part = jnp.sum((grad * value_rows * scale).reshape(-1, gain.shape[0]), 0)
    return (result, gain_part)


def row_products(left, pieces):
    return tuple((jnp.dot(left, piece, preferred_element_type=jnp.float32) for piece in pieces))


def column_products(rights, pieces):
    total = jnp.einsum("tc,rc->tr", rights[0], pieces[0], preferred_element_type=jnp.float32)
    for right, piece in zip(rights[1:], pieces[1:]):
        total = total + jnp.einsum("tc,rc->tr", right, piece, preferred_element_type=jnp.float32)
    return total


def on_device(
    layer_input,
    token_positions,
    attention_gain,
    query_weight,
    key_matrix,
    value_matrix,
    query_gain,
    key_norm_gain,
    output_weight,
    feedforward_gain,
    gate_weight,
    up_weight,
    down_weight,
    out_cotangent,
):
    hidden_in = layer_input[0].astype(jnp.float32)
    count = hidden_in.shape[0]
    head_size = query_gain.shape[0]
    query_width = query_weight.shape[1]
    key_width = key_matrix.shape[1]
    inner_width = gate_weight.shape[1]
    heads = query_width // head_size
    key_heads = key_width // head_size
    group = heads // key_heads
    scale = head_size ** (-0.5)
    cycles = lax.axis_size("ctx")
    own_index = lax.axis_index("ctx")
    sequence_pos = token_positions[0]
    token_offsets = lax.dynamic_slice_in_dim(sequence_pos, own_index * count, count)
    cosine, sine = rope_tables(token_offsets, head_size)
    cosine = cosine[:, None, :]
    sine = sine[:, None, :]
    first_scale = norm_scale(hidden_in)
    first = (hidden_in * first_scale * attention_gain).astype(jnp.bfloat16)
    query_raw, key_unnormed, value_unnormed = row_products(
        first,
        (
            lax.all_gather(query_weight, "fsdp", axis=0, tiled=True),
            lax.all_gather(key_matrix, "fsdp", axis=0, tiled=True),
            lax.all_gather(value_matrix, "fsdp", axis=0, tiled=True),
        ),
    )
    query_heads = query_raw.reshape(count, heads, head_size)
    query_scale = norm_scale(query_heads)
    query_normed = query_heads * query_scale * query_gain
    query_rot = query_normed * cosine + rotate(query_normed) * sine
    query_grouped = (
        query_rot.reshape(count, key_heads, group, head_size)
        .transpose(1, 2, 0, 3)
        .astype(jnp.bfloat16)
    )
    key_heads_raw = key_unnormed.reshape(count, key_heads, head_size)
    key_scale = norm_scale(key_heads_raw)
    key_normed = key_heads_raw * key_scale * key_norm_gain
    key_low = (
        (key_normed * cosine + rotate(key_normed) * sine)
        .reshape(count, key_width)
        .astype(jnp.bfloat16)
    )
    value_low = value_unnormed.astype(jnp.bfloat16)
    rowmax = jnp.full((key_heads, group, count), masked_score, jnp.float32)
    keys_piece = lax.all_gather(key_low, "ctx", axis=0, tiled=True).reshape(
        -1, key_heads, head_size
    )
    values_piece = lax.all_gather(value_low, "ctx", axis=0, tiled=True).reshape(
        -1, key_heads, head_size
    )
    key_pos = sequence_pos
    allowed = token_offsets[:, None] >= key_pos[None, :]
    scores = (
        jnp.einsum("kgtd,skd->kgts", query_grouped, keys_piece, preferred_element_type=jnp.float32)
        * scale
    )
    scores = jnp.where(allowed, scores, masked_score)
    newmax = jnp.maximum(rowmax, jnp.max(scores, -1))
    weights = jnp.where(allowed, jnp.exp(scores - newmax[..., None]), 0.0)
    accum = jnp.einsum(
        "kgts,skd->kgtd",
        weights.astype(jnp.bfloat16),
        values_piece,
        preferred_element_type=jnp.float32,
    )
    rowsum = jnp.sum(weights, -1)
    accum, rowmax, rowsum = (accum, newmax, rowsum)
    normalized = accum / rowsum[..., None]
    logsum = rowmax + jnp.log(rowsum)
    attention_low = (
        normalized.transpose(2, 0, 1, 3).reshape(count, query_width).astype(jnp.bfloat16)
    )
    output_whole = lax.all_gather(output_weight, "fsdp", axis=0, tiled=True)
    branch_out = jnp.dot(attention_low, output_whole, preferred_element_type=jnp.float32)
    middle = hidden_in + branch_out
    second_scale = norm_scale(middle)
    second = (middle * second_scale * feedforward_gain).astype(jnp.bfloat16)
    gate, up = row_products(
        second,
        (
            lax.all_gather(gate_weight, "fsdp", axis=0, tiled=True),
            lax.all_gather(up_weight, "fsdp", axis=0, tiled=True),
        ),
    )
    sigmoid_gate = jax.nn.sigmoid(gate)
    silu_gate = gate * sigmoid_gate
    hidden_low = (silu_gate * up).astype(jnp.bfloat16)
    (down_out,) = row_products(
        hidden_low, (lax.all_gather(down_weight, "fsdp", axis=0, tiled=True),)
    )
    layer_output = (middle + down_out).astype(jnp.bfloat16)[None]
    cotangent = out_cotangent[0]
    hidden_grad = column_products(
        (cotangent,), lax.all_gather((down_weight,), "fsdp", axis=0, tiled=True)
    )
    up_low = (hidden_grad * silu_gate).astype(jnp.bfloat16)
    gate_low = (hidden_grad * up * sigmoid_gate * (1.0 + gate * (1.0 - sigmoid_gate))).astype(
        jnp.bfloat16
    )
    second_grad = column_products(
        (gate_low, up_low), lax.all_gather((gate_weight, up_weight), "fsdp", axis=0, tiled=True)
    )
    middle_part, feedforward_part = norm_back(middle, second_scale, feedforward_gain, second_grad)
    middle_grad = cotangent.astype(jnp.float32) + middle_part
    middle_low = middle_grad.astype(jnp.bfloat16)
    attention_grad = jnp.einsum(
        "tc,rc->tr", middle_low, output_whole, preferred_element_type=jnp.float32
    )
    attention_grad_low = attention_grad.astype(jnp.bfloat16)
    mixed_grad = attention_grad_low.reshape(count, key_heads, group, head_size).transpose(
        1, 2, 0, 3
    )
    delta = jnp.sum(mixed_grad.astype(jnp.float32) * normalized, -1)

    def cycle_step(index, carry):
        keys_held, values_held, key_acc, value_acc, query_acc = carry
        anchor = (own_index - index) % cycles
        key_pos = lax.dynamic_slice_in_dim(sequence_pos, anchor * count, count)
        keys_piece = keys_held.astype(jnp.bfloat16).reshape(count, key_heads, head_size)
        values_piece = values_held.astype(jnp.bfloat16).reshape(count, key_heads, head_size)
        allowed = token_offsets[:, None] >= key_pos[None, :]
        scores = (
            jnp.einsum(
                "kgtd,skd->kgts", query_grouped, keys_piece, preferred_element_type=jnp.float32
            )
            * scale
        )
        probs = jnp.where(allowed, jnp.exp(scores - logsum[..., None]), 0.0)
        value_acc = value_acc + jnp.einsum(
            "kgts,kgtd->skd",
            probs.astype(jnp.bfloat16),
            mixed_grad,
            preferred_element_type=jnp.float32,
        ).reshape(count, key_width)
        prob_grad = jnp.einsum(
            "kgtd,skd->kgts", mixed_grad, values_piece, preferred_element_type=jnp.float32
        )
        score_grad = (probs * (prob_grad - delta[..., None])).astype(jnp.bfloat16)
        query_acc = (
            query_acc
            + jnp.einsum(
                "kgts,skd->kgtd", score_grad, keys_piece, preferred_element_type=jnp.float32
            )
            * scale
        )
        key_acc = (
            key_acc
            + jnp.einsum(
                "kgts,kgtd->skd", score_grad, query_grouped, preferred_element_type=jnp.float32
            ).reshape(count, key_width)
            * scale
        )
        moved = (
            from_behind(keys_held.astype(jnp.bfloat16), "ctx", 1).astype(keys_held.dtype),
            from_behind(values_held.astype(jnp.bfloat16), "ctx", 1).astype(values_held.dtype),
            from_behind(key_acc.astype(jnp.bfloat16), "ctx", 1).astype(key_acc.dtype),
            from_behind(value_acc.astype(jnp.bfloat16), "ctx", 1).astype(value_acc.dtype),
        )
        return (moved[0], moved[1], moved[2], moved[3], query_acc)

    start_cycle = (
        key_low.astype(jnp.float32),
        value_low.astype(jnp.float32),
        jnp.zeros((count, key_width), jnp.float32),
        jnp.zeros((count, key_width), jnp.float32),
        jnp.zeros((key_heads, group, count, head_size), jnp.float32),
    )
    cycle_done = lax.fori_loop(0, cycles, cycle_step, start_cycle)
    key_acc = cycle_done[2]
    value_acc = cycle_done[3]
    query_acc = cycle_done[4]
    query_rot_grad = query_acc.transpose(2, 0, 1, 3).reshape(count, heads, head_size)
    query_normed_grad = query_rot_grad * cosine + rotate_back(query_rot_grad * sine)
    query_heads_grad, query_part = norm_back(
        query_heads, query_scale, query_gain, query_normed_grad
    )
    query_low_grad = query_heads_grad.reshape(count, query_width).astype(jnp.bfloat16)
    key_rot_grad = key_acc.reshape(count, key_heads, head_size)
    key_normed_grad = key_rot_grad * cosine + rotate_back(key_rot_grad * sine)
    key_heads_grad, key_part = norm_back(key_heads_raw, key_scale, key_norm_gain, key_normed_grad)
    key_low_grad = key_heads_grad.reshape(count, key_width).astype(jnp.bfloat16)
    value_low_grad = value_acc.astype(jnp.bfloat16)
    first_grad = column_products(
        (query_low_grad, key_low_grad, value_low_grad),
        lax.all_gather((query_weight, key_matrix, value_matrix), "fsdp", axis=0, tiled=True),
    )
    input_part, attention_part = norm_back(hidden_in, first_scale, attention_gain, first_grad)
    input_gradient = (middle_grad + input_part)[None]
    rights_first = jnp.concatenate([query_low_grad, key_low_grad, value_low_grad], 1)
    rights_second = jnp.concatenate([gate_low, up_low], 1)
    pairs = (
        (first, rights_first),
        (second, rights_second),
        (middle_low, attention_low),
        (cotangent, hidden_low),
    )
    parts = []
    for left, right in pairs:
        parts.append(jnp.einsum("tr,tc->rc", left, right, preferred_element_type=jnp.float32))
    sums = lax.psum_scatter(
        jnp.concatenate(parts, 1), ("ctx", "fsdp"), scatter_dimension=0, tiled=True
    )
    edges = [0, query_width, query_width + key_width, query_width + 2 * key_width]
    edges = edges + [edges[3] + inner_width, edges[3] + 2 * inner_width]
    edges = edges + [edges[5] + query_width, edges[5] + query_width + inner_width]
    query_gradient = sums[:, edges[0] : edges[1]]
    key_gradient = sums[:, edges[1] : edges[2]]
    value_gradient = sums[:, edges[2] : edges[3]]
    gate_gradient = sums[:, edges[3] : edges[4]]
    up_gradient = sums[:, edges[4] : edges[5]]
    output_gradient = sums[:, edges[5] : edges[6]].T
    down_gradient = sums[:, edges[6] : edges[7]].T
    attention_total, query_total, key_total, feedforward_total = lax.psum(
        (attention_part, query_part, key_part, feedforward_part), ("ctx", "fsdp")
    )
    return (
        layer_output,
        input_gradient,
        attention_total,
        query_gradient,
        key_gradient,
        value_gradient,
        query_total,
        key_total,
        output_gradient,
        feedforward_total,
        gate_gradient,
        up_gradient,
        down_gradient,
    )


MESH = pl.DeviceIdType.MESH
f32 = jnp.float32
bf16 = jnp.bfloat16


def dot(left, right):
    return jnp.dot(left, right, preferred_element_type=f32)


def dot_nt(left, right):
    return lax.dot_general(left, right, (((1,), (1,)), ((), ())), preferred_element_type=f32)


def dot_tn(left, right):
    return lax.dot_general(left, right, (((0,), (0,)), ((), ())), preferred_element_type=f32)


def layer_kernel(
    n, planes, block, head, group, fw,
    x_ref, dy_ref, pos_row, inverse_ref, ag_ref, fg_ref, qg_ref, kg_ref,
    wq, wk, wv, wo, wg, wu, wd,
    out_ref, dx_ref, gains_ref, got_a, got_b, got_c, got_out, got_qkv,
    w_qkv, w_gu, w_out, w_down, t_out, t_down,
    first, dy_all, second, dmid,
    positions, cosine, sine,
    raw, queries, keys, values, probs, mixed, mixed_low,
    hidden, d_gu, d_qkv, dk_acc, dv_acc, dq_acc,
    stage_a, stage_b, stage_c, stage_out, stage_qkv,
    land_a, land_b, land_c, land_out, land_qkv,
    join_a, join_b, join_c, join_out, join_qkv,
    own_a, own_b, own_c, own_out, own_qkv,
    rs_sa, rs_ra, rs_sb, rs_rb, rs_acc,
    middle, d_middle, gain_own, gain_plane, gain_all,
    local_sem, wz_send, wz_recv, hand_send, hand_recv,
    ag_send, ag_recv, ra_send, ra_recv, rb_send, rb_recv,
    zr_send, zr_recv, zj_recv, aa_send, aa_recv, gp_send, gp_recv, gz_send, gz_recv,
):
    c = lax.axis_index("ctx")
    z = lax.axis_index("fsdp")
    cy, cx, ck = lax.div(c, 4), lax.rem(lax.div(c, 2), 2), lax.rem(c, 2)
    ci = lax.rem(c, 4)
    qw, kw = group * head, head
    pw = 128
    thirds = fw // pw
    piece = pw // 4
    width = x_ref.shape[1]
    scale = head ** (-0.5)
    log2e = 1.4426950408889634
    gots = (got_a, got_b, got_c, got_out, got_qkv)
    stages = (stage_a, stage_b, stage_c, stage_out, stage_qkv)
    lands = (land_a, land_b, land_c, land_out, land_qkv)
    joins = (join_a, join_b, join_c, join_out, join_qkv)
    owns = (own_a, own_b, own_c, own_out, own_qkv)

    def partner(j):
        y = lax.rem(cy + lax.div(j, 4), 2)
        x = lax.rem(cx + lax.rem(lax.div(j, 2), 2), 2)
        k = lax.rem(ck + lax.rem(j, 2), 2)
        return y * 4 + x * 2 + k

    def rows(start, size):
        return pl.ds(pl.multiple_of(start * size, size), size)

    def remote(src, dst, send, recv, ctx, plane):
        return pltpu.make_async_remote_copy(
            src_ref=src, dst_ref=dst, send_sem=send, recv_sem=recv,
            device_id={"ctx": ctx, "fsdp": plane}, device_id_type=MESH,
        )

    in_plane, along = [], []

    def launch(started, copy, when=None):
        if when is None:
            copy().start()
        else:
            pl.when(when)(lambda: copy().start())
        started.append((copy, when))

    def drain(started):
        for copy, when in started:
            if when is None:
                copy().wait_send()
            else:
                pl.when(when)(lambda copy=copy: copy().wait_send())
        started.clear()

    own_rows = wq.shape[0]
    out_rows = wo.shape[0] // n

    def own_slices():
        mine = rows(z, own_rows)
        pairs = [
            (wq.at[:, rows(c, qw)], w_qkv.at[mine, 0:qw]),
            (wk.at[:, rows(c, kw)], w_qkv.at[mine, qw:qw + kw]),
            (wv.at[:, rows(c, kw)], w_qkv.at[mine, qw + kw:qw + 2 * kw]),
            (wo.at[rows(c, out_rows)], t_out.at[rows(z, out_rows)]),
        ]
        for t in range(thirds):
            at = 2 * pw * t
            pairs.append((wg.at[:, rows(c * thirds + t, pw)], w_gu.at[mine, at:at + pw]))
            pairs.append((wu.at[:, rows(c * thirds + t, pw)], w_gu.at[mine, at + pw:at + 2 * pw]))
            pairs.append((wd.at[rows((cy * thirds + t) * 4 + ci, piece)], t_down.at[t, rows(z, piece)]))
        return pairs

    local = [pltpu.make_async_copy(src, dst, local_sem.at[i]) for i, (src, dst) in enumerate(own_slices())]
    for copy in local:
        copy.start()

    edge = jnp.logical_or(z == 0, z == planes - 1)
    for land in lands:
        @pl.when(edge)
        def _(land=land):
            land[planes - 1 - z] = jnp.zeros(land.shape[1:], bf16)

    barrier = pltpu.get_barrier_semaphore()
    for j in range(1, n):
        pl.semaphore_signal(barrier, inc=1, device_id={"ctx": partner(j), "fsdp": z}, device_id_type=MESH)
    for d in range(1, planes):
        pl.semaphore_signal(
            barrier, inc=1, device_id={"ctx": c, "fsdp": lax.rem(z + d, planes)}, device_id_type=MESH)
    x = x_ref[...].astype(f32)
    x_scale = lax.rsqrt(jnp.mean(x * x, -1, keepdims=True) + epsilon)
    first[rows(c, block)] = (x * x_scale * ag_ref[...]).astype(bf16)
    dy_all[rows(c, block)] = dy_ref[...]
    for copy in local[:3]:
        copy.wait()
    pl.semaphore_wait(barrier, n + planes - 2)

    def inside(t):
        return jnp.logical_and(t >= 0, t < planes)

    weights = [
        (lambda o: w_qkv.at[rows(o, own_rows)], None),
        (lambda o: t_out.at[rows(o, out_rows)], 0),
    ]
    for t in range(thirds):
        weights.append((lambda o, t=t: w_gu.at[rows(o, own_rows), 2 * pw * t:2 * pw * (t + 1)], None))
        weights.append((lambda o, t=t: t_down.at[t, rows(o, piece)], 1 + t))

    def weight_copy(w, slot, origin, target):
        part = weights[w][0](origin)
        return remote(part, part, wz_send.at[w, slot], wz_recv.at[w, origin], c, target)

    def weight_start(w):
        for slot, d in enumerate((1, -1, 2, -2)):
            launch(along, lambda slot=slot, d=d: weight_copy(w, slot, z, z + d), inside(z + d))
        if weights[w][1] is not None:
            hand_over(w, z, 0, None)

    def hand_target(h):
        if h == 0:
            return lambda i: w_out.at[rows(i, out_rows)]
        return lambda i: w_down.at[rows((h - 1) * 4 + i, piece)]

    def hand_copy(w, origin, slot):
        h = weights[w][1]
        return remote(
            weights[w][0](origin), hand_target(h)(ci), hand_send.at[h, slot], hand_recv.at[h, ci], 2 * origin + cy, z)

    def hand_over(w, origin, slot, valid):
        away = 2 * origin + cy != c
        here = jnp.logical_not(away)
        if valid is not None:
            away, here = jnp.logical_and(valid, away), jnp.logical_and(valid, here)
        launch(in_plane, lambda: hand_copy(w, origin, slot), away)

        @pl.when(here)
        def _():
            hand_target(weights[w][1])(ci)[...] = weights[w][0](origin)[...]

    def hand_arrive(w):
        h = weights[w][1]
        for i in range(4):
            @pl.when(4 * ck + i != c)
            def _(i=i):
                part = hand_target(h)(i)
                remote(part, part, hand_send.at[h, 0], hand_recv.at[h, i], c, z).wait_recv()

    def weight_receive(w):
        for d in range(1, planes):
            for side, sign in enumerate((1, -1)):
                origin = z - sign * d
                valid = inside(origin)
                pl.when(valid)(lambda origin=origin: weight_copy(w, 0, origin, z).wait_recv())
                if 2 <= d < planes - 1:
                    slot = 4 + 2 * (d - 2) + side
                    launch(
                        along,
                        lambda slot=slot, origin=origin, sign=sign: weight_copy(w, slot, origin, z + sign),
                        jnp.logical_and(valid, inside(z + sign)))
                if weights[w][1] is not None:
                    hand_over(w, origin, 2 * d - 1 + side, valid)

    def gather_copy(buf, g, j, send, origin, target):
        part = buf.at[rows(origin, block)]
        return remote(part, part, ag_send.at[g, send], ag_recv.at[g, j], target, z)

    def gather_start(buf, g):
        for j in (1, 2, 4, 6):
            launch(in_plane, lambda j=j: gather_copy(buf, g, j, j, c, partner(j)))

    def gather_forward(buf, g, j):
        return gather_copy(buf, g, j + 1, j + 1, partner(j), partner(1))

    def gather_finish(buf, g):
        for j in (2, 4, 6):
            gather_copy(buf, g, j, j, partner(j), c).wait_recv()
            launch(in_plane, lambda j=j: gather_forward(buf, g, j))
        for j in (1, 3, 5, 7):
            gather_copy(buf, g, j, j, partner(j), c).wait_recv()

    def gather_step(buf, g, j):
        @pl.when(j > 0)
        def _():
            gather_copy(buf, g, j, j, partner(j), c).wait_recv()

        @pl.when(jnp.logical_and(j > 0, lax.rem(j, 2) == 0))
        def _():
            gather_forward(buf, g, j).start()

    def gather_stepped(buf, g):
        for j in (2, 4, 6):
            in_plane.append((lambda j=j: gather_forward(buf, g, j), None))

    def sum_pair_copy(s, slot):
        return remote(rs_sa.at[s % 2, slot], rs_ra.at[s % 2, slot], ra_send.at[s, slot], ra_recv.at[s, slot], partner(1), z)

    def sum_chip_copy(s, slot):
        return remote(
            rs_sb.at[s % 2, slot], rs_rb.at[s % 2, slot], rb_send.at[s, slot], rb_recv.at[s, slot], partner(2 * slot), z)

    def sum_start(s, partial):
        def pair(slot):
            rs_sa[s % 2, slot] = partial(partner(2 * slot + 1)).astype(bf16)
            launch(in_plane, lambda: sum_pair_copy(s, slot))

        def chip(slot):
            value = partial(partner(2 * slot))
            sum_pair_copy(s, slot).wait_recv()
            rs_sb[s % 2, slot] = (value + rs_ra[s % 2, slot].astype(f32)).astype(bf16)
            launch(in_plane, lambda: sum_chip_copy(s, slot))

        pair(3)
        pair(2)
        chip(3)
        pair(1)
        chip(2)
        pair(0)
        chip(1)
        value = partial(c)
        sum_pair_copy(s, 0).wait_recv()
        rs_acc[s % 2] = value + rs_ra[s % 2, 0].astype(f32)

    def sum_finish(s):
        total = rs_acc[s % 2]
        for slot in (1, 2, 3):
            sum_chip_copy(s, slot).wait_recv()
            total = total + rs_rb[s % 2, slot].astype(f32)
        return total

    per = block // planes

    def weight_grad(m, parts):
        def body(i, carry):
            at = 0
            for left, right in parts:
                value = right()
                grad = dot_tn(left[:, rows(i, block)], value)
                for t in range(planes):
                    stages[m][t, i, :, at:at + value.shape[1]] = grad[t * per:(t + 1) * per].astype(bf16)
                at += value.shape[1]
            return carry

        lax.fori_loop(0, n, body, 0)
        far = planes - 1 - z
        launch(along, lambda: grad_join_copy(m, far), edge)
        for d in (1, -1):
            launch(along, lambda d=d: grad_copy(m, z + d), inside(z + d))
        launch(along, lambda: grad_copy(m, near_edge()), edge)

    def near_edge():
        return jnp.where(z == 0, 2, planes - 3)

    def grad_slot(target):
        return lax.rem(target - z + planes, planes)

    def grad_copy(m, target):
        return remote(
            stages[m].at[target], lands[m].at[z], zr_send.at[m, grad_slot(target)], zr_recv.at[m, z], c, target)

    def grad_join_copy(m, far):
        return remote(
            stages[m].at[far], joins[m], zr_send.at[m, 0], zj_recv.at[m], c, jnp.where(z == 0, 1, planes - 2))

    def grad_join(m):
        inner = jnp.logical_not(edge)
        far = jnp.where(z == 1, planes - 1, 0)

        @pl.when(inner)
        def _():
            remote(joins[m], joins[m], zr_send.at[m, 0], zj_recv.at[m], c, z).wait_recv()

            def body(i, carry):
                stages[m][far, i] = (stages[m][far, i].astype(f32) + joins[m][i].astype(f32)).astype(bf16)
                return carry

            lax.fori_loop(0, n, body, 0)

        launch(along, lambda: grad_copy(m, far), inner)

    def owner_copy(m, j):
        return remote(owns[m].at[partner(j)], gots[m].at[c], aa_send.at[m, j], aa_recv.at[m, j], partner(j), z)

    def hand_out(m):
        for d in (1, -1, 2, -2):
            @pl.when(inside(z + d))
            def _(d=d):
                origin = z + d
                part = lands[m].at[origin]
                remote(part, part, zr_send.at[m, 0], zr_recv.at[m, origin], c, z).wait_recv()

        def body(i, carry):
            total = stages[m][z, i].astype(f32)
            for d in range(1, planes):
                total = total + lands[m][lax.rem(z + d, planes), i].astype(f32)
            owns[m][i] = total.astype(bf16)
            return carry

        lax.fori_loop(0, n, body, 0)
        for j in (6, 7, 2, 3, 4, 5, 1):
            launch(in_plane, lambda j=j: owner_copy(m, j))
        gots[m][c] = owns[m][c]

    def hand_receive(m):
        for j in range(1, n):
            owner_copy(m, j).wait_recv()

    weight_start(0)
    gather_start(first, 0)

    spread = jnp.broadcast_to(pos_row[...].astype(f32), (head, pos_row.shape[1]))
    positions[...] = spread.T
    side = jnp.where(lax.broadcasted_iota(jnp.int32, (1, head), 1) < head // 2, -1.0, 1.0)

    def table(i, carry):
        at = rows(i, block)
        angle = positions[at] * inverse_ref[...]
        cosine[at] = jnp.cos(angle)
        sine[at] = jnp.sin(angle) * side
        return carry

    gather_finish(first, 0)
    gather_start(dy_all, 1)
    lax.fori_loop(0, n, table, 0)
    for copy in local[3:]:
        copy.wait()
    weight_receive(0)
    weight_start(1)
    gather_finish(dy_all, 1)

    def turn(value, at):
        return value * cosine[at] + pltpu.roll(value, head // 2, 1) * sine[at]

    def turn_back(grad, at):
        return grad * cosine[at] - pltpu.roll(grad, head // 2, 1) * sine[at]

    def project(i, carry):
        at = rows(i, block)
        result = dot(first[at], w_qkv[...])
        raw[at] = result[:, :qw + kw]
        values[at] = result[:, qw + kw:].astype(bf16)
        for h in range(group + 1):
            part = result[:, h * head:(h + 1) * head]
            inv = lax.rsqrt(jnp.mean(part * part, -1, keepdims=True) + epsilon)
            gain = qg_ref[...] if h < group else kg_ref[...]
            turned = turn(part * inv * gain, at).astype(bf16)
            if h < group:
                queries[at, h * head:(h + 1) * head] = turned
            else:
                keys[at] = turned
        return carry

    lax.fori_loop(0, n, project, 0)

    def stack(ref, at):
        return jnp.concatenate([ref[at, h * head:(h + 1) * head] for h in range(group)], 0)

    key_positions = pos_row[...].astype(f32)

    def attend(i, carry):
        at = rows(i, block)
        scores = dot_nt(stack(queries, at), keys[...])
        allowed = positions[at, 0:1] >= pos_row[...].astype(f32)
        scores = jnp.concatenate(
            [jnp.where(allowed, scores[h * block:(h + 1) * block], masked_score) for h in range(group)], 0)
        peak = jnp.max(scores, -1, keepdims=True)
        weight = jnp.exp2((scores - peak) * (scale * log2e))
        prob = (weight * (1.0 / jnp.sum(weight, -1, keepdims=True))).astype(bf16)
        probs[i] = prob
        result = dot(prob, values[...])
        for h in range(group):
            part = result[h * block:(h + 1) * block]
            mixed[at, h * head:(h + 1) * head] = part
            mixed_low[at, h * head:(h + 1) * head] = part.astype(bf16)
        return carry

    lax.fori_loop(0, n // 2, attend, 0)
    weight_receive(1)
    weight_start(2)
    weight_start(3)
    lax.fori_loop(n // 2, n, attend, 0)
    hand_arrive(1)
    sum_start(0, lambda d: dot(mixed_low[rows(d, block)], w_out[...]))
    weight_start(4)
    weight_start(5)
    mid = x_ref[...].astype(f32) + sum_finish(0)
    middle[...] = mid
    mid_scale = lax.rsqrt(jnp.mean(mid * mid, -1, keepdims=True) + epsilon)
    second[rows(c, block)] = (mid * mid_scale * fg_ref[...]).astype(bf16)
    gather_start(second, 2)
    weight_receive(2)
    weight_receive(3)
    weight_start(6)
    weight_start(7)
    hand_arrive(3)

    def feed(t, at):
        units, pair = slice(t * pw, (t + 1) * pw), 2 * pw * t
        both = dot(second[at], w_gu[:, pair:pair + 2 * pw])
        back = dot_nt(dy_all[at], w_down[units])
        gate, up = both[:, :pw], both[:, pw:]
        sig = 1.0 / (1.0 + jnp.exp(-gate))
        silu = gate * sig
        hidden[at, units] = (silu * up).astype(bf16)
        d_gu[at, pair:pair + pw] = (back * up * sig * (1.0 + gate * (1.0 - sig))).astype(bf16)
        d_gu[at, pair + pw:pair + 2 * pw] = (back * silu).astype(bf16)

    def feed_arriving(j, carry):
        gather_step(second, 2, j)
        feed(0, rows(partner(j), block))
        return carry

    def third_grad(t):
        weight_grad(t, [
            (second, lambda: d_gu[:, 2 * pw * t:2 * pw * (t + 1)]),
            (dy_all, lambda: hidden[:, t * pw:(t + 1) * pw]),
        ])

    def feed_third(t):
        def body(i, carry):
            feed(t, rows(i, 2 * block))
            return carry

        lax.fori_loop(0, n // 2, body, 0)

    lax.fori_loop(0, n, feed_arriving, 0)
    gather_stepped(second, 2)
    third_grad(0)
    for t in range(1, thirds):
        weight_receive(2 + 2 * t)
        weight_receive(3 + 2 * t)
        hand_arrive(3 + 2 * t)
        feed_third(t)
        if t < thirds - 1:
            third_grad(t)
    sum_start(1, lambda d: dot_nt(d_gu[rows(d, block)], w_gu[...]))
    third_grad(thirds - 1)
    grad_join(0)
    d_second = sum_finish(1)

    def norm_back(value, gain, grad):
        inv = lax.rsqrt(jnp.mean(value * value, -1, keepdims=True) + epsilon)
        weighted = grad * gain
        inner = jnp.mean(weighted * value, -1, keepdims=True)
        result = inv * weighted - value * (inv * inv * inv * inner)
        return result, jnp.sum(grad * value * inv, 0, keepdims=True)

    gain_own[...] = jnp.zeros_like(gain_own)
    part, gain_own[1:2, :] = norm_back(middle[...], fg_ref[...], d_second)
    d_mid = dy_ref[...].astype(f32) + part
    d_middle[...] = d_mid
    dmid[rows(c, block)] = d_mid.astype(bf16)
    gather_start(dmid, 3)

    dk_acc[...] = jnp.zeros_like(dk_acc)
    dv_acc[...] = jnp.zeros_like(dv_acc)

    def attend_back(j, carry):
        gather_step(dmid, 3, j)
        i = partner(j)
        at = rows(i, block)
        d_mix = dot_nt(dmid[at], w_out[...]).astype(bf16)
        d_mix = jnp.concatenate([d_mix[:, h * head:(h + 1) * head] for h in range(group)], 0)
        delta = jnp.sum(d_mix.astype(f32) * stack(mixed, at), -1, keepdims=True)
        prob = probs[i]
        d_prob = dot_nt(d_mix, values[...])
        d_score = (prob.astype(f32) * (d_prob - delta)).astype(bf16)
        dv_acc[...] += dot_tn(prob, d_mix)
        dk_acc[...] += dot_tn(d_score, stack(queries, at))
        d_query = dot(d_score, keys[...]) * scale
        for h in range(group):
            dq_acc[at, h * head:(h + 1) * head] = d_query[h * block:(h + 1) * block]
        return carry

    lax.fori_loop(0, n, attend_back, 0)
    gather_stepped(dmid, 3)
    weight_grad(3, [(dmid, lambda: mixed_low[...])])
    grad_join(1)
    grad_join(2)

    def project_back(i, carry):
        at = rows(i, block)
        q_sum, k_sum = carry
        for h in range(group + 1):
            if h < group:
                grad, gain = dq_acc[at, h * head:(h + 1) * head], qg_ref[...]
            else:
                grad, gain = dk_acc[at] * scale, kg_ref[...]
            part, gain_part = norm_back(raw[at, h * head:(h + 1) * head], gain, turn_back(grad, at))
            d_qkv[at, h * head:(h + 1) * head] = part.astype(bf16)
            if h < group:
                q_sum = q_sum + gain_part
            else:
                k_sum = k_sum + gain_part
        d_qkv[at, qw + kw:] = dv_acc[at].astype(bf16)
        return q_sum, k_sum

    zero = jnp.zeros((1, head), f32)
    q_sum, k_sum = lax.fori_loop(0, n, project_back, (zero, zero))
    gain_own[2:3, 0:head] = q_sum
    gain_own[3:4, 0:head] = k_sum

    weight_grad(4, [(first, lambda: d_qkv[...])])
    grad_join(3)
    drain(in_plane)
    sum_start(3, lambda d: dot_nt(d_qkv[rows(d, block)], w_qkv[...]))
    sum_start(2, lambda d: dot(hidden[rows(d, block)], w_down[...]))
    grad_join(4)
    for m in range(4):
        hand_out(m)
    x_part, gain_own[0:1, :] = norm_back(x_ref[...].astype(f32), ag_ref[...], sum_finish(3))
    dx_ref[...] = d_middle[...] + x_part

    def gain_plane_copy(j):
        return remote(gain_own, gain_plane.at[c], gp_send.at[j], gp_recv.at[j], partner(j), z)

    def gain_copy(d):
        return remote(gain_all.at[z], gain_all.at[z], gz_send.at[d], gz_recv.at[d], c, lax.rem(z + d, planes))

    for j in range(1, n):
        launch(in_plane, lambda j=j: gain_plane_copy(j))
    gain_plane[c] = gain_own[...]
    out_ref[...] = (middle[...] + sum_finish(2)).astype(bf16)
    for j in range(1, n):
        gain_plane_copy(j).wait_recv()
    total = gain_plane[0]
    for i in range(1, n):
        total = total + gain_plane[i]
    gain_all[z] = total
    for d in range(1, planes):
        launch(along, lambda d=d: gain_copy(d))
    for d in range(1, planes):
        origin = gain_all.at[lax.rem(z + planes - d, planes)]
        remote(origin, origin, gz_send.at[d], gz_recv.at[d], c, z).wait_recv()
    total = gain_all[0]
    for i in range(1, planes):
        total = total + gain_all[i]
    gains_ref[...] = total

    hand_out(4)
    for m in range(5):
        hand_receive(m)
    drain(in_plane)
    drain(along)


def finish_kernel(
    n, head, out_in, dx_in, gains_in, got_a, got_b, got_c, got_out, got_qkv,
    out_ref, dx_ref, ag_ref, q_ref, k_ref, v_ref, qg_ref, kg_ref, o_ref, fg_ref, g_ref, u_ref, d_ref,
):
    out_ref[...] = out_in[...]
    dx_ref[...] = dx_in[...]
    ag_ref[...] = gains_in[0:1, :]
    fg_ref[...] = gains_in[1:2, :]
    qg_ref[...] = gains_in[2:3, 0:head]
    kg_ref[...] = gains_in[3:4, 0:head]
    qw, kw = q_ref.shape[1] // n, k_ref.shape[1] // n
    pw = got_a.shape[2] // 3
    thirds = (got_a, got_b, got_c)
    for i in range(n):
        q_ref[:, i * qw:(i + 1) * qw] = got_qkv[i, :, 0:qw].astype(f32)
        k_ref[:, i * kw:(i + 1) * kw] = got_qkv[i, :, qw:qw + kw].astype(f32)
        v_ref[:, i * kw:(i + 1) * kw] = got_qkv[i, :, qw + kw:].astype(f32)
        o_ref[:, i * qw:(i + 1) * qw] = got_out[i].astype(f32)
        for t, got in enumerate(thirds):
            at = (i * len(thirds) + t) * pw
            g_ref[:, at:at + pw] = got[i, :, 0:pw].astype(f32)
            u_ref[:, at:at + pw] = got[i, :, pw:2 * pw].astype(f32)
            d_ref[:, at:at + pw] = got[i, :, 2 * pw:].astype(f32)


def plane_device(
    layer_input,
    token_positions,
    attention_gain,
    query_weight,
    key_matrix,
    value_matrix,
    query_gain,
    key_norm_gain,
    output_weight,
    feedforward_gain,
    gate_weight,
    up_weight,
    down_weight,
    out_cotangent,
):
    n = lax.axis_size("ctx")
    planes = lax.axis_size("fsdp")
    block, width = layer_input.shape[1:]
    length = token_positions.shape[1]
    head = query_gain.shape[0]
    qw = query_weight.shape[1] // n
    kw = key_matrix.shape[1] // n
    fw = gate_weight.shape[1] // n
    group = qw // head
    per = block // planes
    half = head // 2
    inverse = np.power(rope_base, -np.arange(half) * 2.0 / head).astype(np.float32)
    inverse = jnp.asarray(np.concatenate([inverse, inverse])[None])
    vmem = pl.BlockSpec(memory_space=pltpu.VMEM)
    hbm = pl.BlockSpec(memory_space=pl.ANY)
    dma = pltpu.SemaphoreType.DMA
    sizes = (fw, fw, fw, qw, qw + 2 * kw)
    low = lambda *shape: pltpu.VMEM(shape, bf16)
    wide = lambda *shape: pltpu.VMEM(shape, f32)
    scratch = [
        low(width, qw + 2 * kw), low(width, 2 * fw), low(qw, width), low(fw, width),
        low(planes * (output_weight.shape[0] // n), width), low(3, planes * 32, width),
        low(length, width), low(length, width), low(length, width), low(length, width),
        wide(length, head), wide(length, head), wide(length, head),
        wide(length, qw + kw), low(length, qw), low(length, kw), low(length, kw),
        low(n, group * block, length), wide(length, qw), low(length, qw),
        low(length, fw), low(length, 2 * fw), low(length, qw + 2 * kw),
        wide(length, kw), wide(length, kw), wide(length, qw),
    ]
    scratch += [low(planes, n, per, size) for size in sizes]
    scratch += [low(planes, n, per, size) for size in sizes]
    scratch += [low(n, per, size) for size in sizes]
    scratch += [low(n, per, size) for size in sizes]
    scratch += [low(2, 4, block, width) for _ in range(4)] + [wide(2, block, width)]
    scratch += [
        wide(block, width), wide(block, width), wide(8, width), wide(n, 8, width), wide(planes, 8, width),
        dma((13,)), dma((8, 6)), dma((8, planes)), dma((4, 7)), dma((4, 4)),
        dma((4, n)), dma((4, n)), dma((4, 4)), dma((4, 4)), dma((4, 4)), dma((4, 4)),
        dma((5, planes)), dma((5, planes)), dma((5,)), dma((5, n)), dma((5, n)), dma((n,)), dma((n,)),
        dma((planes,)), dma((planes,)),
    ]
    shapes = [
        jax.ShapeDtypeStruct((block, width), bf16),
        jax.ShapeDtypeStruct((block, width), f32),
        jax.ShapeDtypeStruct((8, width), f32),
    ] + [jax.ShapeDtypeStruct((n, per, size), bf16) for size in sizes]
    results = pl.pallas_call(
        functools.partial(layer_kernel, n, planes, block, head, group, fw),
        out_shape=shapes,
        in_specs=[vmem] * 8 + [hbm] * 7,
        out_specs=[vmem] * len(shapes),
        scratch_shapes=scratch,
        compiler_params=pltpu.CompilerParams(
            collective_id=0, has_side_effects=True, vmem_limit_bytes=60 * 1024 * 1024),
    )(
        layer_input[0], out_cotangent[0], token_positions, inverse,
        attention_gain[None], feedforward_gain[None], query_gain[None], key_norm_gain[None],
        query_weight, key_matrix, value_matrix, output_weight, gate_weight, up_weight, down_weight,
    )
    plain = lambda rows, columns, kind=f32: jax.ShapeDtypeStruct((rows, columns), kind)
    finals = [
        plain(block, width, bf16), plain(block, width), plain(1, width),
        plain(per, n * qw), plain(per, n * kw), plain(per, n * kw), plain(1, head), plain(1, head),
        plain(per, n * qw), plain(1, width), plain(per, n * fw), plain(per, n * fw), plain(per, n * fw),
    ]
    done = pl.pallas_call(
        functools.partial(finish_kernel, n, head),
        out_shape=finals,
        in_specs=[vmem] * len(shapes),
        out_specs=[vmem] * len(finals),
    )(*results)
    out, dx, ag, q, k, v, qg, kg, o, fg, g, u, d = done
    return out[None], dx[None], ag[0], q, k, v, qg[0], kg[0], o.T, fg[0], g, u, d.T


def solution(mesh):
    in_specs = (
        P("fsdp", "ctx", None),
        P("fsdp", None),
        P(),
        P("fsdp", None),
        P("fsdp", None),
        P("fsdp", None),
        P(),
        P(),
        P("fsdp", None),
        P(),
        P("fsdp", None),
        P("fsdp", None),
        P("fsdp", None),
        P("fsdp", "ctx", None),
    )
    out_specs = (
        P("fsdp", "ctx", None),
        P("fsdp", "ctx", None),
        P(),
        P(("ctx", "fsdp"), None),
        P(("ctx", "fsdp"), None),
        P(("ctx", "fsdp"), None),
        P(),
        P(),
        P(None, ("ctx", "fsdp")),
        P(),
        P(("ctx", "fsdp"), None),
        P(("ctx", "fsdp"), None),
        P(None, ("ctx", "fsdp")),
    )

    def run(*arguments):
        n, planes = mesh.shape["ctx"], mesh.shape["fsdp"]
        key_heads = arguments[4].shape[1] // arguments[6].shape[0]
        whole_heads = n == 8 and planes == 4 and key_heads == n
        return jax.shard_map(
            plane_device if whole_heads else on_device,
            mesh=mesh, in_specs=in_specs, out_specs=out_specs, check_vma=False,
        )(*arguments)

    return run
```

```python
import functools

import jax
import jax.numpy as jnp
import numpy as np
from jax import lax
from jax.experimental import pallas as pl
from jax.experimental.pallas import tpu as pltpu
from jax.sharding import PartitionSpec as P

epsilon = 1e-06
rope_base = 1000000.0
masked_score = -1e30


def from_behind(block, axis, distance):
    devices = range(lax.axis_size(axis))
    route = [((i - distance) % len(devices), i) for i in devices]
    return lax.ppermute(block, axis, route)


def rotate(value_rows):
    half = value_rows.shape[-1] // 2
    return jnp.concatenate([-value_rows[..., half:], value_rows[..., :half]], -1)


def rotate_back(value_rows):
    half = value_rows.shape[-1] // 2
    return jnp.concatenate([value_rows[..., half:], -value_rows[..., :half]], -1)


def rope_tables(token_offsets, head_size):
    half = head_size // 2
    inverse = rope_base ** (-(jnp.arange(half).astype(jnp.float32) * 2.0) / head_size)
    angles = token_offsets.astype(jnp.float32)[:, None] * inverse[None, :]
    cosine = jnp.cos(angles)
    sine = jnp.sin(angles)
    return (jnp.concatenate([cosine, cosine], -1), jnp.concatenate([sine, sine], -1))


def norm_scale(value_rows):
    return lax.rsqrt(jnp.mean(value_rows * value_rows, -1, keepdims=True) + epsilon)


def norm_back(value_rows, scale, gain, grad):
    weighted = grad * gain
    inner = jnp.mean(weighted * value_rows, -1, keepdims=True)
    result = scale * weighted - value_rows * scale * scale * scale * inner
    gain_part = jnp.sum((grad * value_rows * scale).reshape(-1, gain.shape[0]), 0)
    return (result, gain_part)


def row_products(left, pieces):
    return tuple((jnp.dot(left, piece, preferred_element_type=jnp.float32) for piece in pieces))


def column_products(rights, pieces):
    total = jnp.einsum("tc,rc->tr", rights[0], pieces[0], preferred_element_type=jnp.float32)
    for right, piece in zip(rights[1:], pieces[1:]):
        total = total + jnp.einsum("tc,rc->tr", right, piece, preferred_element_type=jnp.float32)
    return total


def on_device(
    layer_input,
    token_positions,
    attention_gain,
    query_weight,
    key_matrix,
    value_matrix,
    query_gain,
    key_norm_gain,
    output_weight,
    feedforward_gain,
    gate_weight,
    up_weight,
    down_weight,
    out_cotangent,
):
    hidden_in = layer_input[0].astype(jnp.float32)
    count = hidden_in.shape[0]
    head_size = query_gain.shape[0]
    query_width = query_weight.shape[1]
    key_width = key_matrix.shape[1]
    inner_width = gate_weight.shape[1]
    heads = query_width // head_size
    key_heads = key_width // head_size
    group = heads // key_heads
    scale = head_size ** (-0.5)
    cycles = lax.axis_size("ctx")
    own_index = lax.axis_index("ctx")
    sequence_pos = token_positions[0]
    token_offsets = lax.dynamic_slice_in_dim(sequence_pos, own_index * count, count)
    cosine, sine = rope_tables(token_offsets, head_size)
    cosine = cosine[:, None, :]
    sine = sine[:, None, :]
    first_scale = norm_scale(hidden_in)
    first = (hidden_in * first_scale * attention_gain).astype(jnp.bfloat16)
    query_raw, key_unnormed, value_unnormed = row_products(
        first,
        (
            lax.all_gather(query_weight, "fsdp", axis=0, tiled=True),
            lax.all_gather(key_matrix, "fsdp", axis=0, tiled=True),
            lax.all_gather(value_matrix, "fsdp", axis=0, tiled=True),
        ),
    )
    query_heads = query_raw.reshape(count, heads, head_size)
    query_scale = norm_scale(query_heads)
    query_normed = query_heads * query_scale * query_gain
    query_rot = query_normed * cosine + rotate(query_normed) * sine
    query_grouped = (
        query_rot.reshape(count, key_heads, group, head_size)
        .transpose(1, 2, 0, 3)
        .astype(jnp.bfloat16)
    )
    key_heads_raw = key_unnormed.reshape(count, key_heads, head_size)
    key_scale = norm_scale(key_heads_raw)
    key_normed = key_heads_raw * key_scale * key_norm_gain
    key_low = (
        (key_normed * cosine + rotate(key_normed) * sine)
        .reshape(count, key_width)
        .astype(jnp.bfloat16)
    )
    value_low = value_unnormed.astype(jnp.bfloat16)
    rowmax = jnp.full((key_heads, group, count), masked_score, jnp.float32)
    keys_piece = lax.all_gather(key_low, "ctx", axis=0, tiled=True).reshape(
        -1, key_heads, head_size
    )
    values_piece = lax.all_gather(value_low, "ctx", axis=0, tiled=True).reshape(
        -1, key_heads, head_size
    )
    key_pos = sequence_pos
    allowed = token_offsets[:, None] >= key_pos[None, :]
    scores = (
        jnp.einsum("kgtd,skd->kgts", query_grouped, keys_piece, preferred_element_type=jnp.float32)
        * scale
    )
    scores = jnp.where(allowed, scores, masked_score)
    newmax = jnp.maximum(rowmax, jnp.max(scores, -1))
    weights = jnp.where(allowed, jnp.exp(scores - newmax[..., None]), 0.0)
    accum = jnp.einsum(
        "kgts,skd->kgtd",
        weights.astype(jnp.bfloat16),
        values_piece,
        preferred_element_type=jnp.float32,
    )
    rowsum = jnp.sum(weights, -1)
    accum, rowmax, rowsum = (accum, newmax, rowsum)
    normalized = accum / rowsum[..., None]
    logsum = rowmax + jnp.log(rowsum)
    attention_low = (
        normalized.transpose(2, 0, 1, 3).reshape(count, query_width).astype(jnp.bfloat16)
    )
    output_whole = lax.all_gather(output_weight, "fsdp", axis=0, tiled=True)
    branch_out = jnp.dot(attention_low, output_whole, preferred_element_type=jnp.float32)
    middle = hidden_in + branch_out
    second_scale = norm_scale(middle)
    second = (middle * second_scale * feedforward_gain).astype(jnp.bfloat16)
    gate, up = row_products(
        second,
        (
            lax.all_gather(gate_weight, "fsdp", axis=0, tiled=True),
            lax.all_gather(up_weight, "fsdp", axis=0, tiled=True),
        ),
    )
    sigmoid_gate = jax.nn.sigmoid(gate)
    silu_gate = gate * sigmoid_gate
    hidden_low = (silu_gate * up).astype(jnp.bfloat16)
    (down_out,) = row_products(
        hidden_low, (lax.all_gather(down_weight, "fsdp", axis=0, tiled=True),)
    )
    layer_output = (middle + down_out).astype(jnp.bfloat16)[None]
    cotangent = out_cotangent[0]
    hidden_grad = column_products(
        (cotangent,), lax.all_gather((down_weight,), "fsdp", axis=0, tiled=True)
    )
    up_low = (hidden_grad * silu_gate).astype(jnp.bfloat16)
    gate_low = (hidden_grad * up * sigmoid_gate * (1.0 + gate * (1.0 - sigmoid_gate))).astype(
        jnp.bfloat16
    )
    second_grad = column_products(
        (gate_low, up_low), lax.all_gather((gate_weight, up_weight), "fsdp", axis=0, tiled=True)
    )
    middle_part, feedforward_part = norm_back(middle, second_scale, feedforward_gain, second_grad)
    middle_grad = cotangent.astype(jnp.float32) + middle_part
    middle_low = middle_grad.astype(jnp.bfloat16)
    attention_grad = jnp.einsum(
        "tc,rc->tr", middle_low, output_whole, preferred_element_type=jnp.float32
    )
    attention_grad_low = attention_grad.astype(jnp.bfloat16)
    mixed_grad = attention_grad_low.reshape(count, key_heads, group, head_size).transpose(
        1, 2, 0, 3
    )
    delta = jnp.sum(mixed_grad.astype(jnp.float32) * normalized, -1)

    def cycle_step(index, carry):
        keys_held, values_held, key_acc, value_acc, query_acc = carry
        anchor = (own_index - index) % cycles
        key_pos = lax.dynamic_slice_in_dim(sequence_pos, anchor * count, count)
        keys_piece = keys_held.astype(jnp.bfloat16).reshape(count, key_heads, head_size)
        values_piece = values_held.astype(jnp.bfloat16).reshape(count, key_heads, head_size)
        allowed = token_offsets[:, None] >= key_pos[None, :]
        scores = (
            jnp.einsum(
                "kgtd,skd->kgts", query_grouped, keys_piece, preferred_element_type=jnp.float32
            )
            * scale
        )
        probs = jnp.where(allowed, jnp.exp(scores - logsum[..., None]), 0.0)
        value_acc = value_acc + jnp.einsum(
            "kgts,kgtd->skd",
            probs.astype(jnp.bfloat16),
            mixed_grad,
            preferred_element_type=jnp.float32,
        ).reshape(count, key_width)
        prob_grad = jnp.einsum(
            "kgtd,skd->kgts", mixed_grad, values_piece, preferred_element_type=jnp.float32
        )
        score_grad = (probs * (prob_grad - delta[..., None])).astype(jnp.bfloat16)
        query_acc = (
            query_acc
            + jnp.einsum(
                "kgts,skd->kgtd", score_grad, keys_piece, preferred_element_type=jnp.float32
            )
            * scale
        )
        key_acc = (
            key_acc
            + jnp.einsum(
                "kgts,kgtd->skd", score_grad, query_grouped, preferred_element_type=jnp.float32
            ).reshape(count, key_width)
            * scale
        )
        moved = (
            from_behind(keys_held.astype(jnp.bfloat16), "ctx", 1).astype(keys_held.dtype),
            from_behind(values_held.astype(jnp.bfloat16), "ctx", 1).astype(values_held.dtype),
            from_behind(key_acc.astype(jnp.bfloat16), "ctx", 1).astype(key_acc.dtype),
            from_behind(value_acc.astype(jnp.bfloat16), "ctx", 1).astype(value_acc.dtype),
        )
        return (moved[0], moved[1], moved[2], moved[3], query_acc)

    start_cycle = (
        key_low.astype(jnp.float32),
        value_low.astype(jnp.float32),
        jnp.zeros((count, key_width), jnp.float32),
        jnp.zeros((count, key_width), jnp.float32),
        jnp.zeros((key_heads, group, count, head_size), jnp.float32),
    )
    cycle_done = lax.fori_loop(0, cycles, cycle_step, start_cycle)
    key_acc = cycle_done[2]
    value_acc = cycle_done[3]
    query_acc = cycle_done[4]
    query_rot_grad = query_acc.transpose(2, 0, 1, 3).reshape(count, heads, head_size)
    query_normed_grad = query_rot_grad * cosine + rotate_back(query_rot_grad * sine)
    query_heads_grad, query_part = norm_back(
        query_heads, query_scale, query_gain, query_normed_grad
    )
    query_low_grad = query_heads_grad.reshape(count, query_width).astype(jnp.bfloat16)
    key_rot_grad = key_acc.reshape(count, key_heads, head_size)
    key_normed_grad = key_rot_grad * cosine + rotate_back(key_rot_grad * sine)
    key_heads_grad, key_part = norm_back(key_heads_raw, key_scale, key_norm_gain, key_normed_grad)
    key_low_grad = key_heads_grad.reshape(count, key_width).astype(jnp.bfloat16)
    value_low_grad = value_acc.astype(jnp.bfloat16)
    first_grad = column_products(
        (query_low_grad, key_low_grad, value_low_grad),
        lax.all_gather((query_weight, key_matrix, value_matrix), "fsdp", axis=0, tiled=True),
    )
    input_part, attention_part = norm_back(hidden_in, first_scale, attention_gain, first_grad)
    input_gradient = (middle_grad + input_part)[None]
    rights_first = jnp.concatenate([query_low_grad, key_low_grad, value_low_grad], 1)
    rights_second = jnp.concatenate([gate_low, up_low], 1)
    pairs = (
        (first, rights_first),
        (second, rights_second),
        (middle_low, attention_low),
        (cotangent, hidden_low),
    )
    parts = []
    for left, right in pairs:
        parts.append(jnp.einsum("tr,tc->rc", left, right, preferred_element_type=jnp.float32))
    sums = lax.psum_scatter(
        jnp.concatenate(parts, 1), ("ctx", "fsdp"), scatter_dimension=0, tiled=True
    )
    edges = [0, query_width, query_width + key_width, query_width + 2 * key_width]
    edges = edges + [edges[3] + inner_width, edges[3] + 2 * inner_width]
    edges = edges + [edges[5] + query_width, edges[5] + query_width + inner_width]
    query_gradient = sums[:, edges[0] : edges[1]]
    key_gradient = sums[:, edges[1] : edges[2]]
    value_gradient = sums[:, edges[2] : edges[3]]
    gate_gradient = sums[:, edges[3] : edges[4]]
    up_gradient = sums[:, edges[4] : edges[5]]
    output_gradient = sums[:, edges[5] : edges[6]].T
    down_gradient = sums[:, edges[6] : edges[7]].T
    attention_total, query_total, key_total, feedforward_total = lax.psum(
        (attention_part, query_part, key_part, feedforward_part), ("ctx", "fsdp")
    )
    return (
        layer_output,
        input_gradient,
        attention_total,
        query_gradient,
        key_gradient,
        value_gradient,
        query_total,
        key_total,
        output_gradient,
        feedforward_total,
        gate_gradient,
        up_gradient,
        down_gradient,
    )


MESH = pl.DeviceIdType.MESH
f32 = jnp.float32
bf16 = jnp.bfloat16


def dot(left, right):
    return jnp.dot(left, right, preferred_element_type=f32)


def dot_nt(left, right):
    return lax.dot_general(left, right, (((1,), (1,)), ((), ())), preferred_element_type=f32)


def dot_tn(left, right):
    return lax.dot_general(left, right, (((0,), (0,)), ((), ())), preferred_element_type=f32)


def layer_kernel(
    n, planes, block, head, group, fw,
    x_ref, dy_ref, pos_row, inverse_ref, ag_ref, fg_ref, qg_ref, kg_ref,
    wq, wk, wv, wo, wg, wu, wd,
    out_ref, dx_ref, gains_ref, got_a, got_b, got_c, got_out, got_qkv,
    w_qkv, w_gu, w_out, w_down, t_out, t_down,
    first, dy_all, second, first_t, dy_t, second_t, dmid_t,
    positions, cosine, sine,
    raw, queries, keys, values, keys_t, values_t, probs, mixed_t, mixed_low,
    hidden, d_gu, d_qkv, dk_acc, dv_acc, dq_acc,
    stage_a, stage_b, stage_c, stage_out, stage_qkv,
    land_a, land_b, land_c, land_out, land_qkv,
    join_a, join_b, join_c, join_out, join_qkv,
    own_a, own_b, own_c, own_out, own_qkv,
    rs_sa, rs_ra, rs_sb, rs_rb, rs_acc,
    middle, d_middle, gain_own, gain_plane, gain_all,
    local_sem, wz_send, wz_recv, hand_send, hand_recv,
    ag_send, ag_recv, ra_send, ra_recv, rb_send, rb_recv,
    zr_send, zr_recv, zj_recv, aa_send, aa_recv, gp_send, gp_recv, gz_send, gz_recv,
):
    c = lax.axis_index("ctx")
    z = lax.axis_index("fsdp")
    dmid = first
    cy, cx, ck = lax.div(c, 4), lax.rem(lax.div(c, 2), 2), lax.rem(c, 2)
    ci = lax.rem(c, 4)
    qw, kw = group * head, head
    pw = 128
    thirds = fw // pw
    piece = pw // 4
    width = x_ref.shape[1]
    scale = head ** (-0.5)
    log2e = 1.4426950408889634
    gots = (got_a, got_b, got_c, got_out, got_qkv)
    stages = (stage_a, stage_b, stage_c, stage_out, stage_qkv)
    lands = (land_a, land_b, land_c, land_out, land_qkv)
    joins = (join_a, join_b, join_c, join_out, join_qkv)
    owns = (own_a, own_b, own_c, own_out, own_qkv)

    def partner(j):
        y = lax.rem(cy + lax.div(j, 4), 2)
        x = lax.rem(cx + lax.rem(lax.div(j, 2), 2), 2)
        k = lax.rem(ck + lax.rem(j, 2), 2)
        return y * 4 + x * 2 + k

    def chip(slot):
        return lax.rem(cy + lax.div(slot, 2), 2) * 2 + lax.rem(cx + lax.rem(slot, 2), 2)

    def rows(start, size):
        return pl.ds(pl.multiple_of(start * size, size), size)

    def remote(src, dst, send, recv, ctx, plane):
        return pltpu.make_async_remote_copy(
            src_ref=src, dst_ref=dst, send_sem=send, recv_sem=recv,
            device_id={"ctx": ctx, "fsdp": plane}, device_id_type=MESH,
        )

    in_plane, along = [], []

    def launch(started, copy, when=None):
        if when is None:
            copy().start()
        else:
            pl.when(when)(lambda: copy().start())
        started.append((copy, when))

    def drain(started):
        for copy, when in started:
            if when is None:
                copy().wait_send()
            else:
                pl.when(when)(lambda copy=copy: copy().wait_send())
        started.clear()

    own_rows = wq.shape[0]
    out_rows = wo.shape[0] // n

    def own_slices():
        mine = rows(z, own_rows)
        pairs = [
            (wq.at[:, rows(c, qw)], w_qkv.at[mine, 0:qw]),
            (wk.at[:, rows(c, kw)], w_qkv.at[mine, qw:qw + kw]),
            (wv.at[:, rows(c, kw)], w_qkv.at[mine, qw + kw:qw + 2 * kw]),
            (wo.at[rows(c, out_rows)], t_out.at[rows(z, out_rows)]),
        ]
        for t in range(thirds):
            at = 2 * pw * t
            pairs.append((wg.at[:, rows(c * thirds + t, pw)], w_gu.at[mine, at:at + pw]))
            pairs.append((wu.at[:, rows(c * thirds + t, pw)], w_gu.at[mine, at + pw:at + 2 * pw]))
            pairs.append((wd.at[rows((cy * thirds + t) * 4 + ci, piece)], t_down.at[t, rows(z, piece)]))
        return pairs

    local = [pltpu.make_async_copy(src, dst, local_sem.at[i]) for i, (src, dst) in enumerate(own_slices())]
    for copy in local:
        copy.start()

    edge = jnp.logical_or(z == 0, z == planes - 1)
    for land in lands:
        @pl.when(edge)
        def _(land=land):
            land[planes - 1 - z] = jnp.zeros(land.shape[1:], bf16)

    barrier = pltpu.get_barrier_semaphore()
    for j in range(1, n):
        pl.semaphore_signal(barrier, inc=1, device_id={"ctx": partner(j), "fsdp": z}, device_id_type=MESH)
    for d in range(1, planes):
        pl.semaphore_signal(
            barrier, inc=1, device_id={"ctx": c, "fsdp": lax.rem(z + d, planes)}, device_id_type=MESH)
    x = x_ref[...].astype(f32)
    x_scale = lax.rsqrt(jnp.mean(x * x, -1, keepdims=True) + epsilon)
    first[rows(c, block)] = (x * x_scale * ag_ref[...]).astype(bf16)
    dy_all[rows(c, block)] = dy_ref[...]
    for copy in local[:3]:
        copy.wait()
    pl.semaphore_wait(barrier, n + planes - 2)

    def inside(t):
        return jnp.logical_and(t >= 0, t < planes)

    weights = [
        (lambda o: w_qkv.at[rows(o, own_rows)], None),
        (lambda o: t_out.at[rows(o, out_rows)], 0),
    ]
    for t in range(thirds):
        weights.append((lambda o, t=t: w_gu.at[rows(o, own_rows), 2 * pw * t:2 * pw * (t + 1)], None))
        weights.append((lambda o, t=t: t_down.at[t, rows(o, piece)], 1 + t))

    def weight_copy(w, slot, origin, target):
        part = weights[w][0](origin)
        return remote(part, part, wz_send.at[w, slot], wz_recv.at[w, origin], c, target)

    def weight_start(w):
        for slot, d in enumerate((1, -1, 2, -2)):
            launch(along, lambda slot=slot, d=d: weight_copy(w, slot, z, z + d), inside(z + d))
        if weights[w][1] is not None:
            hand_over(w, z, 0, None)

    def hand_target(h):
        if h == 0:
            return lambda i: w_out.at[rows(i, out_rows)]
        return lambda i: w_down.at[rows((h - 1) * 4 + i, piece)]

    def hand_copy(w, origin, slot):
        h = weights[w][1]
        return remote(
            weights[w][0](origin), hand_target(h)(ci), hand_send.at[h, slot], hand_recv.at[h, ci], 2 * origin + cy, z)

    def hand_over(w, origin, slot, valid):
        away = 2 * origin + cy != c
        here = jnp.logical_not(away)
        if valid is not None:
            away, here = jnp.logical_and(valid, away), jnp.logical_and(valid, here)
        launch(in_plane, lambda: hand_copy(w, origin, slot), away)

        @pl.when(here)
        def _():
            hand_target(weights[w][1])(ci)[...] = weights[w][0](origin)[...]

    def hand_arrive(w):
        h = weights[w][1]
        for i in range(4):
            @pl.when(4 * ck + i != c)
            def _(i=i):
                part = hand_target(h)(i)
                remote(part, part, hand_send.at[h, 0], hand_recv.at[h, i], c, z).wait_recv()

    def weight_receive(w):
        for d in range(1, planes):
            for side, sign in enumerate((1, -1)):
                origin = z - sign * d
                valid = inside(origin)
                pl.when(valid)(lambda origin=origin: weight_copy(w, 0, origin, z).wait_recv())
                if 2 <= d < planes - 1:
                    slot = 4 + 2 * (d - 2) + side
                    launch(
                        along,
                        lambda slot=slot, origin=origin, sign=sign: weight_copy(w, slot, origin, z + sign),
                        jnp.logical_and(valid, inside(z + sign)))
                if weights[w][1] is not None:
                    hand_over(w, origin, 2 * d - 1 + side, valid)

    def gather_copy(buf, g, j, send, origin, target):
        part = buf.at[rows(origin, block)]
        return remote(part, part, ag_send.at[g, send], ag_recv.at[g, j], target, z)

    def gather_start(buf, g):
        for j in (1, 2, 4, 6):
            launch(in_plane, lambda j=j: gather_copy(buf, g, j, j, c, partner(j)))

    def gather_forward(buf, g, j):
        return gather_copy(buf, g, j + 1, j + 1, partner(j), partner(1))

    def gather_finish(buf, g):
        for j in (2, 4, 6):
            gather_copy(buf, g, j, j, partner(j), c).wait_recv()
            launch(in_plane, lambda j=j: gather_forward(buf, g, j))
        for j in (1, 3, 5, 7):
            gather_copy(buf, g, j, j, partner(j), c).wait_recv()

    def gather_step(buf, g, slot):
        def arrive(j):
            gather_copy(buf, g, j, j, partner(j), c).wait_recv()
            gather_forward(buf, g, j).start()

        @pl.when(slot == 1)
        def _():
            arrive(2)
            arrive(4)

        @pl.when(slot == 3)
        def _():
            arrive(6)

        gather_copy(buf, g, 2 * slot + 1, 0, partner(2 * slot + 1), c).wait_recv()

    def gather_stepped(buf, g):
        for j in (2, 4, 6):
            in_plane.append((lambda j=j: gather_forward(buf, g, j), None))

    def sum_pair_copy(s, slot):
        return remote(rs_sa.at[s % 2, slot], rs_ra.at[s % 2, slot], ra_send.at[s, slot], ra_recv.at[s, slot], partner(1), z)

    def sum_chip_copy(s, slot):
        return remote(
            rs_sb.at[s % 2, slot], rs_rb.at[s % 2, slot], rb_send.at[s, slot], rb_recv.at[s, slot], partner(2 * slot), z)

    def sum_start(s, left, partial):
        kept = [None] * 4

        def pair(slot):
            at = [rows(partner(2 * slot + 1), block), rows(partner(2 * slot), block)]
            both = partial(jnp.concatenate([left[i] for i in at], 0))
            rs_sa[s % 2, slot] = both[:block].astype(bf16)
            launch(in_plane, lambda: sum_pair_copy(s, slot))
            kept[slot] = both[block:]

        def chips(slot):
            sum_pair_copy(s, slot).wait_recv()
            rs_sb[s % 2, slot] = (kept[slot] + rs_ra[s % 2, slot].astype(f32)).astype(bf16)
            launch(in_plane, lambda: sum_chip_copy(s, slot))

        pair(3)
        pair(2)
        chips(3)
        pair(1)
        chips(2)
        pair(0)
        chips(1)
        sum_pair_copy(s, 0).wait_recv()
        rs_acc[s % 2] = kept[0] + rs_ra[s % 2, 0].astype(f32)

    def sum_finish(s):
        total = rs_acc[s % 2]
        for slot in (1, 2, 3):
            sum_chip_copy(s, slot).wait_recv()
            total = total + rs_rb[s % 2, slot].astype(f32)
        return total

    per = block // planes

    def weight_grad(m, parts):
        def body(i, carry):
            at = 0
            for left, right in parts:
                value = right()
                grad = dot(left[rows(i, 2 * block)], value)
                for k in range(2):
                    for t in range(planes):
                        start = k * block + t * per
                        stages[m][t, 2 * i + k, :, at:at + value.shape[1]] = grad[start:start + per].astype(bf16)
                at += value.shape[1]
            return carry

        lax.fori_loop(0, n // 2, body, 0)
        far = planes - 1 - z
        launch(along, lambda: grad_join_copy(m, far), edge)
        for d in (1, -1):
            launch(along, lambda d=d: grad_copy(m, z + d), inside(z + d))
        launch(along, lambda: grad_copy(m, near_edge()), edge)

    def near_edge():
        return jnp.where(z == 0, 2, planes - 3)

    def grad_slot(target):
        return lax.rem(target - z + planes, planes)

    def grad_copy(m, target):
        return remote(
            stages[m].at[target], lands[m].at[z], zr_send.at[m, grad_slot(target)], zr_recv.at[m, z], c, target)

    def grad_join_copy(m, far):
        return remote(
            stages[m].at[far], joins[m], zr_send.at[m, 0], zj_recv.at[m], c, jnp.where(z == 0, 1, planes - 2))

    def grad_join(m):
        inner = jnp.logical_not(edge)
        far = jnp.where(z == 1, planes - 1, 0)

        @pl.when(inner)
        def _():
            remote(joins[m], joins[m], zr_send.at[m, 0], zj_recv.at[m], c, z).wait_recv()

            def body(i, carry):
                stages[m][far, i] = (stages[m][far, i].astype(f32) + joins[m][i].astype(f32)).astype(bf16)
                return carry

            lax.fori_loop(0, n, body, 0)

        launch(along, lambda: grad_copy(m, far), inner)

    def owner_copy(m, j):
        return remote(owns[m].at[partner(j)], gots[m].at[c], aa_send.at[m, j], aa_recv.at[m, j], partner(j), z)

    def hand_out(m):
        for d in (1, -1, 2, -2):
            @pl.when(inside(z + d))
            def _(d=d):
                origin = z + d
                part = lands[m].at[origin]
                remote(part, part, zr_send.at[m, 0], zr_recv.at[m, origin], c, z).wait_recv()

        def body(i, carry):
            total = stages[m][z, i].astype(f32)
            for d in range(1, planes):
                total = total + lands[m][lax.rem(z + d, planes), i].astype(f32)
            owns[m][i] = total.astype(bf16)
            return carry

        lax.fori_loop(0, n, body, 0)
        for j in (6, 7, 2, 3, 4, 5, 1):
            launch(in_plane, lambda j=j: owner_copy(m, j))
        gots[m][c] = owns[m][c]

    def hand_receive(m):
        for j in range(1, n):
            owner_copy(m, j).wait_recv()

    weight_start(0)
    gather_start(first, 0)

    spread = jnp.broadcast_to(pos_row[...].astype(f32), (head, pos_row.shape[1]))
    positions[...] = spread.T
    side = jnp.where(lax.broadcasted_iota(jnp.int32, (1, head), 1) < head // 2, -1.0, 1.0)

    def table(i, carry):
        at = rows(i, block)
        angle = positions[at] * inverse_ref[...]
        cosine[at] = jnp.cos(angle)
        sine[at] = jnp.sin(angle) * side
        return carry

    gather_finish(first, 0)
    gather_start(dy_all, 1)
    lax.fori_loop(0, n, table, 0)

    def turn_over(src, dst):
        def body(i, carry):
            at = rows(i, block)
            dst[:, at] = src[at].T
            return carry

        lax.fori_loop(0, n, body, 0)

    turn_over(first, first_t)
    for copy in local[3:]:
        copy.wait()
    weight_receive(0)
    weight_start(1)
    gather_finish(dy_all, 1)

    def turn(value, at):
        return value * cosine[at] + pltpu.roll(value, head // 2, 1) * sine[at]

    def turn_back(grad, at):
        return grad * cosine[at] - pltpu.roll(grad, head // 2, 1) * sine[at]

    def project(i, carry):
        at = rows(i, 2 * block)
        result = dot(first[at], w_qkv[...])
        raw[at] = result[:, :qw + kw]
        low_values = result[:, qw + kw:].astype(bf16)
        values[at] = low_values
        values_t[:, at] = low_values.T
        for h in range(group + 1):
            part = result[:, h * head:(h + 1) * head]
            inv = lax.rsqrt(jnp.mean(part * part, -1, keepdims=True) + epsilon)
            gain = qg_ref[...] if h < group else kg_ref[...]
            turned = turn(part * inv * gain, at).astype(bf16)
            if h < group:
                queries[at, h * head:(h + 1) * head] = turned
            else:
                keys[at] = turned
                keys_t[:, at] = turned.T
        return carry

    lax.fori_loop(0, n // 2, project, 0)
    turn_over(dy_all, dy_t)

    def stack(ref, at):
        return jnp.concatenate([ref[at, h * head:(h + 1) * head] for h in range(group)], 0)

    def attend_block(i):
        at = rows(i, block)
        scores = dot_nt(keys[...], stack(queries, at))
        allowed = positions[...] <= pos_row[:, at].astype(f32)
        scores = jnp.concatenate(
            [jnp.where(allowed, scores[:, h * block:(h + 1) * block], masked_score) for h in range(group)], 1)
        peak = jnp.max(scores, 0, keepdims=True)
        weight = jnp.exp2((scores - peak) * (scale * log2e))
        prob = (weight * (1.0 / jnp.sum(weight, 0, keepdims=True))).astype(bf16)
        probs[i] = prob
        result = dot(values_t[...], prob)
        mixed_t[i] = result
        for h in range(group):
            mixed_low[at, h * head:(h + 1) * head] = result[:, h * block:(h + 1) * block].T.astype(bf16)

    def attend(i, carry):
        attend_block(2 * i)
        attend_block(2 * i + 1)
        return carry

    lax.fori_loop(0, n // 4, attend, 0)
    weight_receive(1)
    weight_start(2)
    weight_start(3)
    lax.fori_loop(n // 4, n // 2, attend, 0)
    hand_arrive(1)
    drain(in_plane)
    sum_start(0, mixed_low, lambda left: dot(left, w_out[...]))
    weight_start(4)
    weight_start(5)
    mid = x_ref[...].astype(f32) + sum_finish(0)
    middle[...] = mid
    mid_scale = lax.rsqrt(jnp.mean(mid * mid, -1, keepdims=True) + epsilon)
    second[rows(c, block)] = (mid * mid_scale * fg_ref[...]).astype(bf16)
    gather_start(second, 2)
    weight_receive(2)
    weight_receive(3)
    weight_start(6)
    weight_start(7)
    hand_arrive(3)

    def feed(t, at):
        units, pair = slice(t * pw, (t + 1) * pw), 2 * pw * t
        both = dot(second[at], w_gu[:, pair:pair + 2 * pw])
        back = dot_nt(dy_all[at], w_down[units])
        gate, up = both[:, :pw], both[:, pw:]
        sig = 1.0 / (1.0 + jnp.exp(-gate))
        silu = gate * sig
        hidden[at, units] = (silu * up).astype(bf16)
        d_gu[at, pair:pair + pw] = (back * up * sig * (1.0 + gate * (1.0 - sig))).astype(bf16)
        d_gu[at, pair + pw:pair + 2 * pw] = (back * silu).astype(bf16)

    def feed_arriving(slot, carry):
        gather_step(second, 2, slot)
        at = rows(chip(slot), 2 * block)
        feed(0, at)
        second_t[:, at] = second[at].T
        return carry

    def third_grad(t):
        weight_grad(t, [
            (second_t, lambda: d_gu[:, 2 * pw * t:2 * pw * (t + 1)]),
            (dy_t, lambda: hidden[:, t * pw:(t + 1) * pw]),
        ])

    def feed_third(t):
        def body(i, carry):
            feed(t, rows(i, 2 * block))
            return carry

        lax.fori_loop(0, n // 2, body, 0)

    lax.fori_loop(0, n // 2, feed_arriving, 0)
    gather_stepped(second, 2)
    third_grad(0)
    for t in range(1, thirds):
        weight_receive(2 + 2 * t)
        weight_receive(3 + 2 * t)
        hand_arrive(3 + 2 * t)
        feed_third(t)
        if t < thirds - 1:
            third_grad(t)
    sum_start(1, d_gu, lambda left: dot_nt(left, w_gu[...]))
    third_grad(thirds - 1)
    grad_join(0)
    d_second = sum_finish(1)

    def norm_back(value, gain, grad):
        inv = lax.rsqrt(jnp.mean(value * value, -1, keepdims=True) + epsilon)
        weighted = grad * gain
        inner = jnp.mean(weighted * value, -1, keepdims=True)
        result = inv * weighted - value * (inv * inv * inv * inner)
        return result, jnp.sum(grad * value * inv, 0, keepdims=True)

    gain_own[...] = jnp.zeros_like(gain_own)
    part, gain_own[1:2, :] = norm_back(middle[...], fg_ref[...], d_second)
    d_mid = dy_ref[...].astype(f32) + part
    d_middle[...] = d_mid
    dmid[rows(c, block)] = d_mid.astype(bf16)
    gather_start(dmid, 3)

    dk_acc[...] = jnp.zeros_like(dk_acc)
    dv_acc[...] = jnp.zeros_like(dv_acc)

    def attend_back_block(i):
        at = rows(i, block)
        d_mix = dot_nt(dmid[at], w_out[...]).astype(bf16)
        d_mix = jnp.concatenate([d_mix[:, h * head:(h + 1) * head] for h in range(group)], 0)
        delta = jnp.sum(d_mix.T.astype(f32) * mixed_t[i], 0, keepdims=True)
        prob = probs[i]
        d_prob = dot_nt(values[...], d_mix)
        d_score = (prob.astype(f32) * (d_prob - delta)).astype(bf16)
        d_query = dot(keys_t[...], d_score) * scale
        for h in range(group):
            dq_acc[at, h * head:(h + 1) * head] = d_query[:, h * block:(h + 1) * block].T
        return dot(prob, d_mix), dot(d_score, stack(queries, at))

    def attend_back(slot, carry):
        gather_step(dmid, 3, slot)
        at = rows(chip(slot), 2 * block)
        dmid_t[:, at] = dmid[at].T
        dv_one, dk_one = attend_back_block(2 * chip(slot))
        dv_two, dk_two = attend_back_block(2 * chip(slot) + 1)
        dv_acc[...] += dv_one + dv_two
        dk_acc[...] += dk_one + dk_two
        return carry

    lax.fori_loop(0, n // 2, attend_back, 0)
    gather_stepped(dmid, 3)
    weight_grad(3, [(dmid_t, lambda: mixed_low[...])])
    grad_join(1)
    grad_join(2)

    def project_back(i, carry):
        at = rows(i, block)
        q_sum, k_sum = carry
        for h in range(group + 1):
            if h < group:
                grad, gain = dq_acc[at, h * head:(h + 1) * head], qg_ref[...]
            else:
                grad, gain = dk_acc[at] * scale, kg_ref[...]
            part, gain_part = norm_back(raw[at, h * head:(h + 1) * head], gain, turn_back(grad, at))
            d_qkv[at, h * head:(h + 1) * head] = part.astype(bf16)
            if h < group:
                q_sum = q_sum + gain_part
            else:
                k_sum = k_sum + gain_part
        d_qkv[at, qw + kw:] = dv_acc[at].astype(bf16)
        return q_sum, k_sum

    zero = jnp.zeros((1, head), f32)
    q_sum, k_sum = lax.fori_loop(0, n, project_back, (zero, zero))
    gain_own[2:3, 0:head] = q_sum
    gain_own[3:4, 0:head] = k_sum

    weight_grad(4, [(first_t, lambda: d_qkv[...])])
    grad_join(3)
    drain(in_plane)
    sum_start(3, d_qkv, lambda left: dot_nt(left, w_qkv[...]))
    sum_start(2, hidden, lambda left: dot(left, w_down[...]))
    grad_join(4)
    for m in range(4):
        hand_out(m)
    x_part, gain_own[0:1, :] = norm_back(x_ref[...].astype(f32), ag_ref[...], sum_finish(3))
    dx_ref[...] = d_middle[...] + x_part

    def gain_plane_copy(j):
        return remote(gain_own, gain_plane.at[c], gp_send.at[j], gp_recv.at[j], partner(j), z)

    def gain_copy(d):
        return remote(gain_all.at[z], gain_all.at[z], gz_send.at[d], gz_recv.at[d], c, lax.rem(z + d, planes))

    for j in range(1, n):
        launch(in_plane, lambda j=j: gain_plane_copy(j))
    gain_plane[c] = gain_own[...]
    out_ref[...] = (middle[...] + sum_finish(2)).astype(bf16)
    for j in range(1, n):
        gain_plane_copy(j).wait_recv()
    total = gain_plane[0]
    for i in range(1, n):
        total = total + gain_plane[i]
    gain_all[z] = total
    for d in range(1, planes):
        launch(along, lambda d=d: gain_copy(d))
    for d in range(1, planes):
        origin = gain_all.at[lax.rem(z + planes - d, planes)]
        remote(origin, origin, gz_send.at[d], gz_recv.at[d], c, z).wait_recv()
    total = gain_all[0]
    for i in range(1, planes):
        total = total + gain_all[i]
    gains_ref[...] = total

    hand_out(4)
    for m in range(5):
        hand_receive(m)
    drain(in_plane)
    drain(along)


def finish_kernel(
    n, head, out_in, dx_in, gains_in, got_a, got_b, got_c, got_out, got_qkv,
    out_ref, dx_ref, ag_ref, q_ref, k_ref, v_ref, qg_ref, kg_ref, o_ref, fg_ref, g_ref, u_ref, d_ref,
):
    out_ref[...] = out_in[...]
    dx_ref[...] = dx_in[...]
    ag_ref[...] = gains_in[0:1, :]
    fg_ref[...] = gains_in[1:2, :]
    qg_ref[...] = gains_in[2:3, 0:head]
    kg_ref[...] = gains_in[3:4, 0:head]
    qw, kw = q_ref.shape[1] // n, k_ref.shape[1] // n
    pw = got_a.shape[2] // 3
    thirds = (got_a, got_b, got_c)
    for i in range(n):
        q_ref[:, i * qw:(i + 1) * qw] = got_qkv[i, :, 0:qw].astype(f32)
        k_ref[:, i * kw:(i + 1) * kw] = got_qkv[i, :, qw:qw + kw].astype(f32)
        v_ref[:, i * kw:(i + 1) * kw] = got_qkv[i, :, qw + kw:].astype(f32)
        o_ref[:, i * qw:(i + 1) * qw] = got_out[i].astype(f32)
        for t, got in enumerate(thirds):
            at = (i * len(thirds) + t) * pw
            g_ref[:, at:at + pw] = got[i, :, 0:pw].astype(f32)
            u_ref[:, at:at + pw] = got[i, :, pw:2 * pw].astype(f32)
            d_ref[:, at:at + pw] = got[i, :, 2 * pw:].astype(f32)


def plane_device(
    layer_input,
    token_positions,
    attention_gain,
    query_weight,
    key_matrix,
    value_matrix,
    query_gain,
    key_norm_gain,
    output_weight,
    feedforward_gain,
    gate_weight,
    up_weight,
    down_weight,
    out_cotangent,
):
    n = lax.axis_size("ctx")
    planes = lax.axis_size("fsdp")
    block, width = layer_input.shape[1:]
    length = token_positions.shape[1]
    head = query_gain.shape[0]
    qw = query_weight.shape[1] // n
    kw = key_matrix.shape[1] // n
    fw = gate_weight.shape[1] // n
    group = qw // head
    per = block // planes
    half = head // 2
    inverse = np.power(rope_base, -np.arange(half) * 2.0 / head).astype(np.float32)
    inverse = jnp.asarray(np.concatenate([inverse, inverse])[None])
    vmem = pl.BlockSpec(memory_space=pltpu.VMEM)
    hbm = pl.BlockSpec(memory_space=pl.ANY)
    dma = pltpu.SemaphoreType.DMA
    sizes = (fw, fw, fw, qw, qw + 2 * kw)
    low = lambda *shape: pltpu.VMEM(shape, bf16)
    wide = lambda *shape: pltpu.VMEM(shape, f32)
    scratch = [
        low(width, qw + 2 * kw), low(width, 2 * fw), low(qw, width), low(fw, width),
        low(planes * (output_weight.shape[0] // n), width), low(3, planes * 32, width),
        low(length, width), low(length, width), low(length, width),
        low(width, length), low(width, length), low(width, length), low(width, length),
        wide(length, head), wide(length, head), wide(length, head),
        wide(length, qw + kw), low(length, qw), low(length, kw), low(length, kw),
        low(kw, length), low(kw, length), low(n, length, group * block), wide(n, head, group * block), low(length, qw),
        low(length, fw), low(length, 2 * fw), low(length, qw + 2 * kw),
        wide(length, kw), wide(length, kw), wide(length, qw),
    ]
    scratch += [low(planes, n, per, size) for size in sizes]
    scratch += [low(planes, n, per, size) for size in sizes]
    scratch += [low(n, per, size) for size in sizes]
    scratch += [low(n, per, size) for size in sizes]
    scratch += [low(2, 4, block, width) for _ in range(4)] + [wide(2, block, width)]
    scratch += [
        wide(block, width), wide(block, width), wide(8, width), wide(n, 8, width), wide(planes, 8, width),
        dma((13,)), dma((8, 6)), dma((8, planes)), dma((4, 7)), dma((4, 4)),
        dma((4, n)), dma((4, n)), dma((4, 4)), dma((4, 4)), dma((4, 4)), dma((4, 4)),
        dma((5, planes)), dma((5, planes)), dma((5,)), dma((5, n)), dma((5, n)), dma((n,)), dma((n,)),
        dma((planes,)), dma((planes,)),
    ]
    shapes = [
        jax.ShapeDtypeStruct((block, width), bf16),
        jax.ShapeDtypeStruct((block, width), f32),
        jax.ShapeDtypeStruct((8, width), f32),
    ] + [jax.ShapeDtypeStruct((n, per, size), bf16) for size in sizes]
    results = pl.pallas_call(
        functools.partial(layer_kernel, n, planes, block, head, group, fw),
        out_shape=shapes,
        in_specs=[vmem] * 8 + [hbm] * 7,
        out_specs=[vmem] * len(shapes),
        scratch_shapes=scratch,
        compiler_params=pltpu.CompilerParams(
            collective_id=0, has_side_effects=True, vmem_limit_bytes=60 * 1024 * 1024),
    )(
        layer_input[0], out_cotangent[0], token_positions, inverse,
        attention_gain[None], feedforward_gain[None], query_gain[None], key_norm_gain[None],
        query_weight, key_matrix, value_matrix, output_weight, gate_weight, up_weight, down_weight,
    )
    plain = lambda rows, columns, kind=f32: jax.ShapeDtypeStruct((rows, columns), kind)
    finals = [
        plain(block, width, bf16), plain(block, width), plain(1, width),
        plain(per, n * qw), plain(per, n * kw), plain(per, n * kw), plain(1, head), plain(1, head),
        plain(per, n * qw), plain(1, width), plain(per, n * fw), plain(per, n * fw), plain(per, n * fw),
    ]
    done = pl.pallas_call(
        functools.partial(finish_kernel, n, head),
        out_shape=finals,
        in_specs=[vmem] * len(shapes),
        out_specs=[vmem] * len(finals),
    )(*results)
    out, dx, ag, q, k, v, qg, kg, o, fg, g, u, d = done
    return out[None], dx[None], ag[0], q, k, v, qg[0], kg[0], o.T, fg[0], g, u, d.T


def solution(mesh):
    in_specs = (
        P("fsdp", "ctx", None),
        P("fsdp", None),
        P(),
        P("fsdp", None),
        P("fsdp", None),
        P("fsdp", None),
        P(),
        P(),
        P("fsdp", None),
        P(),
        P("fsdp", None),
        P("fsdp", None),
        P("fsdp", None),
        P("fsdp", "ctx", None),
    )
    out_specs = (
        P("fsdp", "ctx", None),
        P("fsdp", "ctx", None),
        P(),
        P(("ctx", "fsdp"), None),
        P(("ctx", "fsdp"), None),
        P(("ctx", "fsdp"), None),
        P(),
        P(),
        P(None, ("ctx", "fsdp")),
        P(),
        P(("ctx", "fsdp"), None),
        P(("ctx", "fsdp"), None),
        P(None, ("ctx", "fsdp")),
    )

    def run(*arguments):
        n, planes = mesh.shape["ctx"], mesh.shape["fsdp"]
        key_heads = arguments[4].shape[1] // arguments[6].shape[0]
        whole_heads = n == 8 and planes == 4 and key_heads == n
        return jax.shard_map(
            plane_device if whole_heads else on_device,
            mesh=mesh, in_specs=in_specs, out_specs=out_specs, check_vma=False,
        )(*arguments)

    return run
```

```python
import functools

import jax
import jax.numpy as jnp
import numpy as np
from jax import lax
from jax.experimental import pallas as pl
from jax.experimental.pallas import tpu as pltpu
from jax.sharding import PartitionSpec as P

epsilon = 1e-06
rope_base = 1000000.0
masked_score = -1e30


def from_behind(block, axis, distance):
    devices = range(lax.axis_size(axis))
    route = [((i - distance) % len(devices), i) for i in devices]
    return lax.ppermute(block, axis, route)


def rotate(value_rows):
    half = value_rows.shape[-1] // 2
    return jnp.concatenate([-value_rows[..., half:], value_rows[..., :half]], -1)


def rotate_back(value_rows):
    half = value_rows.shape[-1] // 2
    return jnp.concatenate([value_rows[..., half:], -value_rows[..., :half]], -1)


def rope_tables(token_offsets, head_size):
    half = head_size // 2
    inverse = rope_base ** (-(jnp.arange(half).astype(jnp.float32) * 2.0) / head_size)
    angles = token_offsets.astype(jnp.float32)[:, None] * inverse[None, :]
    cosine = jnp.cos(angles)
    sine = jnp.sin(angles)
    return (jnp.concatenate([cosine, cosine], -1), jnp.concatenate([sine, sine], -1))


def norm_scale(value_rows):
    return lax.rsqrt(jnp.mean(value_rows * value_rows, -1, keepdims=True) + epsilon)


def norm_back(value_rows, scale, gain, grad):
    weighted = grad * gain
    inner = jnp.mean(weighted * value_rows, -1, keepdims=True)
    result = scale * weighted - value_rows * scale * scale * scale * inner
    gain_part = jnp.sum((grad * value_rows * scale).reshape(-1, gain.shape[0]), 0)
    return (result, gain_part)


def row_products(left, pieces):
    return tuple((jnp.dot(left, piece, preferred_element_type=jnp.float32) for piece in pieces))


def column_products(rights, pieces):
    total = jnp.einsum("tc,rc->tr", rights[0], pieces[0], preferred_element_type=jnp.float32)
    for right, piece in zip(rights[1:], pieces[1:]):
        total = total + jnp.einsum("tc,rc->tr", right, piece, preferred_element_type=jnp.float32)
    return total


def on_device(
    layer_input,
    token_positions,
    attention_gain,
    query_weight,
    key_matrix,
    value_matrix,
    query_gain,
    key_norm_gain,
    output_weight,
    feedforward_gain,
    gate_weight,
    up_weight,
    down_weight,
    out_cotangent,
):
    hidden_in = layer_input[0].astype(jnp.float32)
    count = hidden_in.shape[0]
    head_size = query_gain.shape[0]
    query_width = query_weight.shape[1]
    key_width = key_matrix.shape[1]
    inner_width = gate_weight.shape[1]
    heads = query_width // head_size
    key_heads = key_width // head_size
    group = heads // key_heads
    scale = head_size ** (-0.5)
    cycles = lax.axis_size("ctx")
    own_index = lax.axis_index("ctx")
    sequence_pos = token_positions[0]
    token_offsets = lax.dynamic_slice_in_dim(sequence_pos, own_index * count, count)
    cosine, sine = rope_tables(token_offsets, head_size)
    cosine = cosine[:, None, :]
    sine = sine[:, None, :]
    first_scale = norm_scale(hidden_in)
    first = (hidden_in * first_scale * attention_gain).astype(jnp.bfloat16)
    query_raw, key_unnormed, value_unnormed = row_products(
        first,
        (
            lax.all_gather(query_weight, "fsdp", axis=0, tiled=True),
            lax.all_gather(key_matrix, "fsdp", axis=0, tiled=True),
            lax.all_gather(value_matrix, "fsdp", axis=0, tiled=True),
        ),
    )
    query_heads = query_raw.reshape(count, heads, head_size)
    query_scale = norm_scale(query_heads)
    query_normed = query_heads * query_scale * query_gain
    query_rot = query_normed * cosine + rotate(query_normed) * sine
    query_grouped = (
        query_rot.reshape(count, key_heads, group, head_size)
        .transpose(1, 2, 0, 3)
        .astype(jnp.bfloat16)
    )
    key_heads_raw = key_unnormed.reshape(count, key_heads, head_size)
    key_scale = norm_scale(key_heads_raw)
    key_normed = key_heads_raw * key_scale * key_norm_gain
    key_low = (
        (key_normed * cosine + rotate(key_normed) * sine)
        .reshape(count, key_width)
        .astype(jnp.bfloat16)
    )
    value_low = value_unnormed.astype(jnp.bfloat16)
    rowmax = jnp.full((key_heads, group, count), masked_score, jnp.float32)
    keys_piece = lax.all_gather(key_low, "ctx", axis=0, tiled=True).reshape(
        -1, key_heads, head_size
    )
    values_piece = lax.all_gather(value_low, "ctx", axis=0, tiled=True).reshape(
        -1, key_heads, head_size
    )
    key_pos = sequence_pos
    allowed = token_offsets[:, None] >= key_pos[None, :]
    scores = (
        jnp.einsum("kgtd,skd->kgts", query_grouped, keys_piece, preferred_element_type=jnp.float32)
        * scale
    )
    scores = jnp.where(allowed, scores, masked_score)
    newmax = jnp.maximum(rowmax, jnp.max(scores, -1))
    weights = jnp.where(allowed, jnp.exp(scores - newmax[..., None]), 0.0)
    accum = jnp.einsum(
        "kgts,skd->kgtd",
        weights.astype(jnp.bfloat16),
        values_piece,
        preferred_element_type=jnp.float32,
    )
    rowsum = jnp.sum(weights, -1)
    accum, rowmax, rowsum = (accum, newmax, rowsum)
    normalized = accum / rowsum[..., None]
    logsum = rowmax + jnp.log(rowsum)
    attention_low = (
        normalized.transpose(2, 0, 1, 3).reshape(count, query_width).astype(jnp.bfloat16)
    )
    output_whole = lax.all_gather(output_weight, "fsdp", axis=0, tiled=True)
    branch_out = jnp.dot(attention_low, output_whole, preferred_element_type=jnp.float32)
    middle = hidden_in + branch_out
    second_scale = norm_scale(middle)
    second = (middle * second_scale * feedforward_gain).astype(jnp.bfloat16)
    gate, up = row_products(
        second,
        (
            lax.all_gather(gate_weight, "fsdp", axis=0, tiled=True),
            lax.all_gather(up_weight, "fsdp", axis=0, tiled=True),
        ),
    )
    sigmoid_gate = jax.nn.sigmoid(gate)
    silu_gate = gate * sigmoid_gate
    hidden_low = (silu_gate * up).astype(jnp.bfloat16)
    (down_out,) = row_products(
        hidden_low, (lax.all_gather(down_weight, "fsdp", axis=0, tiled=True),)
    )
    layer_output = (middle + down_out).astype(jnp.bfloat16)[None]
    cotangent = out_cotangent[0]
    hidden_grad = column_products(
        (cotangent,), lax.all_gather((down_weight,), "fsdp", axis=0, tiled=True)
    )
    up_low = (hidden_grad * silu_gate).astype(jnp.bfloat16)
    gate_low = (hidden_grad * up * sigmoid_gate * (1.0 + gate * (1.0 - sigmoid_gate))).astype(
        jnp.bfloat16
    )
    second_grad = column_products(
        (gate_low, up_low), lax.all_gather((gate_weight, up_weight), "fsdp", axis=0, tiled=True)
    )
    middle_part, feedforward_part = norm_back(middle, second_scale, feedforward_gain, second_grad)
    middle_grad = cotangent.astype(jnp.float32) + middle_part
    middle_low = middle_grad.astype(jnp.bfloat16)
    attention_grad = jnp.einsum(
        "tc,rc->tr", middle_low, output_whole, preferred_element_type=jnp.float32
    )
    attention_grad_low = attention_grad.astype(jnp.bfloat16)
    mixed_grad = attention_grad_low.reshape(count, key_heads, group, head_size).transpose(
        1, 2, 0, 3
    )
    delta = jnp.sum(mixed_grad.astype(jnp.float32) * normalized, -1)

    def cycle_step(index, carry):
        keys_held, values_held, key_acc, value_acc, query_acc = carry
        anchor = (own_index - index) % cycles
        key_pos = lax.dynamic_slice_in_dim(sequence_pos, anchor * count, count)
        keys_piece = keys_held.astype(jnp.bfloat16).reshape(count, key_heads, head_size)
        values_piece = values_held.astype(jnp.bfloat16).reshape(count, key_heads, head_size)
        allowed = token_offsets[:, None] >= key_pos[None, :]
        scores = (
            jnp.einsum(
                "kgtd,skd->kgts", query_grouped, keys_piece, preferred_element_type=jnp.float32
            )
            * scale
        )
        probs = jnp.where(allowed, jnp.exp(scores - logsum[..., None]), 0.0)
        value_acc = value_acc + jnp.einsum(
            "kgts,kgtd->skd",
            probs.astype(jnp.bfloat16),
            mixed_grad,
            preferred_element_type=jnp.float32,
        ).reshape(count, key_width)
        prob_grad = jnp.einsum(
            "kgtd,skd->kgts", mixed_grad, values_piece, preferred_element_type=jnp.float32
        )
        score_grad = (probs * (prob_grad - delta[..., None])).astype(jnp.bfloat16)
        query_acc = (
            query_acc
            + jnp.einsum(
                "kgts,skd->kgtd", score_grad, keys_piece, preferred_element_type=jnp.float32
            )
            * scale
        )
        key_acc = (
            key_acc
            + jnp.einsum(
                "kgts,kgtd->skd", score_grad, query_grouped, preferred_element_type=jnp.float32
            ).reshape(count, key_width)
            * scale
        )
        moved = (
            from_behind(keys_held.astype(jnp.bfloat16), "ctx", 1).astype(keys_held.dtype),
            from_behind(values_held.astype(jnp.bfloat16), "ctx", 1).astype(values_held.dtype),
            from_behind(key_acc.astype(jnp.bfloat16), "ctx", 1).astype(key_acc.dtype),
            from_behind(value_acc.astype(jnp.bfloat16), "ctx", 1).astype(value_acc.dtype),
        )
        return (moved[0], moved[1], moved[2], moved[3], query_acc)

    start_cycle = (
        key_low.astype(jnp.float32),
        value_low.astype(jnp.float32),
        jnp.zeros((count, key_width), jnp.float32),
        jnp.zeros((count, key_width), jnp.float32),
        jnp.zeros((key_heads, group, count, head_size), jnp.float32),
    )
    cycle_done = lax.fori_loop(0, cycles, cycle_step, start_cycle)
    key_acc = cycle_done[2]
    value_acc = cycle_done[3]
    query_acc = cycle_done[4]
    query_rot_grad = query_acc.transpose(2, 0, 1, 3).reshape(count, heads, head_size)
    query_normed_grad = query_rot_grad * cosine + rotate_back(query_rot_grad * sine)
    query_heads_grad, query_part = norm_back(
        query_heads, query_scale, query_gain, query_normed_grad
    )
    query_low_grad = query_heads_grad.reshape(count, query_width).astype(jnp.bfloat16)
    key_rot_grad = key_acc.reshape(count, key_heads, head_size)
    key_normed_grad = key_rot_grad * cosine + rotate_back(key_rot_grad * sine)
    key_heads_grad, key_part = norm_back(key_heads_raw, key_scale, key_norm_gain, key_normed_grad)
    key_low_grad = key_heads_grad.reshape(count, key_width).astype(jnp.bfloat16)
    value_low_grad = value_acc.astype(jnp.bfloat16)
    first_grad = column_products(
        (query_low_grad, key_low_grad, value_low_grad),
        lax.all_gather((query_weight, key_matrix, value_matrix), "fsdp", axis=0, tiled=True),
    )
    input_part, attention_part = norm_back(hidden_in, first_scale, attention_gain, first_grad)
    input_gradient = (middle_grad + input_part)[None]
    rights_first = jnp.concatenate([query_low_grad, key_low_grad, value_low_grad], 1)
    rights_second = jnp.concatenate([gate_low, up_low], 1)
    pairs = (
        (first, rights_first),
        (second, rights_second),
        (middle_low, attention_low),
        (cotangent, hidden_low),
    )
    parts = []
    for left, right in pairs:
        parts.append(jnp.einsum("tr,tc->rc", left, right, preferred_element_type=jnp.float32))
    sums = lax.psum_scatter(
        jnp.concatenate(parts, 1), ("ctx", "fsdp"), scatter_dimension=0, tiled=True
    )
    edges = [0, query_width, query_width + key_width, query_width + 2 * key_width]
    edges = edges + [edges[3] + inner_width, edges[3] + 2 * inner_width]
    edges = edges + [edges[5] + query_width, edges[5] + query_width + inner_width]
    query_gradient = sums[:, edges[0] : edges[1]]
    key_gradient = sums[:, edges[1] : edges[2]]
    value_gradient = sums[:, edges[2] : edges[3]]
    gate_gradient = sums[:, edges[3] : edges[4]]
    up_gradient = sums[:, edges[4] : edges[5]]
    output_gradient = sums[:, edges[5] : edges[6]].T
    down_gradient = sums[:, edges[6] : edges[7]].T
    attention_total, query_total, key_total, feedforward_total = lax.psum(
        (attention_part, query_part, key_part, feedforward_part), ("ctx", "fsdp")
    )
    return (
        layer_output,
        input_gradient,
        attention_total,
        query_gradient,
        key_gradient,
        value_gradient,
        query_total,
        key_total,
        output_gradient,
        feedforward_total,
        gate_gradient,
        up_gradient,
        down_gradient,
    )


MESH = pl.DeviceIdType.MESH
f32 = jnp.float32
bf16 = jnp.bfloat16


def dot(left, right):
    return jnp.dot(left, right, preferred_element_type=f32)


def dot_nt(left, right):
    return lax.dot_general(left, right, (((1,), (1,)), ((), ())), preferred_element_type=f32)


def dot_tn(left, right):
    return lax.dot_general(left, right, (((0,), (0,)), ((), ())), preferred_element_type=f32)


def layer_kernel(
    n, planes, block, head, group, fw,
    x_ref, dy_ref, pos_row, inverse_ref, ag_ref, fg_ref, qg_ref, kg_ref,
    wq, wk, wv, wo, wg, wu, wd,
    out_ref, dx_ref, gains_ref, got_a, got_b, got_c, got_out, got_qkv,
    w_qkv, w_gu, w_out, w_down, t_out, t_down,
    first, dy_all, second, first_t, dy_t, second_t, dmid_t,
    positions, cosine, sine,
    raw, queries, keys, values, keys_t, values_t, probs, mixed_t, mixed_low,
    hidden, d_gu, d_qkv, dk_acc, dv_acc, dq_acc,
    stage_a, stage_b, stage_c, stage_out, stage_qkv,
    land_a, land_b, land_c, land_out, land_qkv,
    join_a, join_b, join_c, join_out, join_qkv,
    own_a, own_b, own_c, own_out, own_qkv,
    rs_sa, rs_ra, rs_sb, rs_rb, rs_acc,
    middle, d_middle, gain_own, gain_plane, gain_all,
    local_sem, wz_send, wz_recv, hand_send, hand_recv,
    ag_send, ag_recv, ra_send, ra_recv, rb_send, rb_recv,
    zr_send, zr_recv, zj_recv, aa_send, aa_recv, gp_send, gp_recv, gz_send, gz_recv,
):
    c = lax.axis_index("ctx")
    z = lax.axis_index("fsdp")
    dmid = first
    cy, cx, ck = lax.div(c, 4), lax.rem(lax.div(c, 2), 2), lax.rem(c, 2)
    ci = lax.rem(c, 4)
    sign = 1 - 2 * ck
    qw, kw = group * head, head
    pw = 128
    thirds = fw // pw
    piece = pw // 4
    width = x_ref.shape[1]
    scale = head ** (-0.5)
    log2e = 1.4426950408889634
    gots = (got_a, got_b, got_c, got_out, got_qkv)
    stages = (stage_a, stage_b, stage_c, stage_out, stage_qkv)
    lands = (land_a, land_b, land_c, land_out, land_qkv)
    joins = (join_a, join_b, join_c, join_out, join_qkv)
    owns = (own_a, own_b, own_c, own_out, own_qkv)

    def partner(j):
        y = lax.rem(cy + lax.div(j, 4), 2)
        x = lax.rem(cx + lax.rem(lax.div(j, 2), 2), 2)
        k = lax.rem(ck + lax.rem(j, 2), 2)
        return y * 4 + x * 2 + k

    def chip(slot):
        return lax.rem(cy + lax.div(slot, 2), 2) * 2 + lax.rem(cx + lax.rem(slot, 2), 2)

    def rows(start, size):
        return pl.ds(pl.multiple_of(start * size, size), size)

    def remote(src, dst, send, recv, ctx, plane):
        return pltpu.make_async_remote_copy(
            src_ref=src, dst_ref=dst, send_sem=send, recv_sem=recv,
            device_id={"ctx": ctx, "fsdp": plane}, device_id_type=MESH,
        )

    in_plane, along = [], []

    def launch(started, copy, when=None):
        if when is None:
            copy().start()
        else:
            pl.when(when)(lambda: copy().start())
        started.append((copy, when))

    def drain(started):
        for copy, when in started:
            if when is None:
                copy().wait_send()
            else:
                pl.when(when)(lambda copy=copy: copy().wait_send())
        started.clear()

    own_rows = wq.shape[0]
    out_rows = wo.shape[0] // n

    def own_slices():
        mine = rows(z, own_rows)
        pairs = [
            (wq.at[:, rows(c, qw)], w_qkv.at[mine, 0:qw]),
            (wk.at[:, rows(c, kw)], w_qkv.at[mine, qw:qw + kw]),
            (wv.at[:, rows(c, kw)], w_qkv.at[mine, qw + kw:qw + 2 * kw]),
            (wo.at[rows(c, out_rows)], t_out.at[rows(z, out_rows)]),
        ]
        for t in range(thirds):
            at = 2 * pw * t
            pairs.append((wg.at[:, rows(c * thirds + t, pw)], w_gu.at[mine, at:at + pw]))
            pairs.append((wu.at[:, rows(c * thirds + t, pw)], w_gu.at[mine, at + pw:at + 2 * pw]))
            pairs.append((wd.at[rows((cy * thirds + t) * 4 + ci, piece)], t_down.at[t, rows(z, piece)]))
        return pairs

    local = [pltpu.make_async_copy(src, dst, local_sem.at[i]) for i, (src, dst) in enumerate(own_slices())]
    for copy in local:
        copy.start()

    edge = jnp.logical_or(z == 0, z == planes - 1)
    for land in lands:
        @pl.when(edge)
        def _(land=land):
            land[planes - 1 - z] = jnp.zeros(land.shape[1:], bf16)

    barrier = pltpu.get_barrier_semaphore()
    for j in range(1, n):
        pl.semaphore_signal(barrier, inc=1, device_id={"ctx": partner(j), "fsdp": z}, device_id_type=MESH)
    for d in range(1, planes):
        pl.semaphore_signal(
            barrier, inc=1, device_id={"ctx": c, "fsdp": lax.rem(z + d, planes)}, device_id_type=MESH)
    x = x_ref[...].astype(f32)
    x_scale = lax.rsqrt(jnp.mean(x * x, -1, keepdims=True) + epsilon)
    first[rows(c, block)] = (x * x_scale * ag_ref[...]).astype(bf16)
    dy_all[rows(c, block)] = dy_ref[...]
    for copy in local[:3]:
        copy.wait()
    pl.semaphore_wait(barrier, n + planes - 2)

    def inside(t):
        return jnp.logical_and(t >= 0, t < planes)

    weights = [
        (lambda o: w_qkv.at[rows(o, own_rows)], None),
        (lambda o: t_out.at[rows(o, out_rows)], 0),
    ]
    for t in range(thirds):
        weights.append((lambda o, t=t: w_gu.at[rows(o, own_rows), 2 * pw * t:2 * pw * (t + 1)], None))
        weights.append((lambda o, t=t: t_down.at[t, rows(o, piece)], 1 + t))

    def weight_copy(w, slot, origin, target):
        part = weights[w][0](origin)
        return remote(part, part, wz_send.at[w, slot], wz_recv.at[w, origin], c, target)

    def weight_start(w):
        for slot, k in enumerate((1, -1, 2, -2)):
            d = sign * k
            launch(along, lambda slot=slot, d=d: weight_copy(w, slot, z, z + d), inside(z + d))
        if weights[w][1] is not None:
            hand_over(w, z, 0, None)

    def hand_target(h):
        if h == 0:
            return lambda i: w_out.at[rows(i, out_rows)]
        return lambda i: w_down.at[rows((h - 1) * 4 + i, piece)]

    def hand_copy(w, origin, slot):
        h = weights[w][1]
        return remote(
            weights[w][0](origin), hand_target(h)(ci), hand_send.at[h, slot], hand_recv.at[h, ci], 2 * origin + cy, z)

    def hand_over(w, origin, slot, valid):
        away = 2 * origin + cy != c
        here = jnp.logical_not(away)
        if valid is not None:
            away, here = jnp.logical_and(valid, away), jnp.logical_and(valid, here)
        launch(in_plane, lambda: hand_copy(w, origin, slot), away)

        @pl.when(here)
        def _():
            hand_target(weights[w][1])(ci)[...] = weights[w][0](origin)[...]

    def hand_arrive(w):
        h = weights[w][1]
        for i in range(4):
            @pl.when(4 * ck + i != c)
            def _(i=i):
                part = hand_target(h)(i)
                remote(part, part, hand_send.at[h, 0], hand_recv.at[h, i], c, z).wait_recv()

    def weight_receive(w):
        for d in range(1, planes):
            for side, way in enumerate((1, -1)):
                origin = z - way * d
                valid = inside(origin)
                pl.when(valid)(lambda origin=origin: weight_copy(w, 0, origin, z).wait_recv())
                if 2 <= d < planes - 1:
                    slot = 4 + 2 * (d - 2) + side
                    launch(
                        along,
                        lambda slot=slot, origin=origin, way=way: weight_copy(w, slot, origin, z + way),
                        jnp.logical_and(valid, inside(z + way)))
                if weights[w][1] is not None:
                    hand_over(w, origin, 2 * d - 1 + side, valid)

    def gather_copy(buf, g, j, send, origin, target):
        part = buf.at[rows(origin, block)]
        return remote(part, part, ag_send.at[g, send], ag_recv.at[g, j], target, z)

    def gather_start(buf, g):
        for j in (1, 2 + 2 * ck, 4 - 2 * ck, 6):
            launch(in_plane, lambda j=j: gather_copy(buf, g, j, j, c, partner(j)))

    def gather_forward(buf, g, j):
        return gather_copy(buf, g, j + 1, j + 1, partner(j), partner(1))

    def gather_finish(buf, g):
        for j in (2, 4, 6):
            gather_copy(buf, g, j, j, partner(j), c).wait_recv()
            launch(in_plane, lambda j=j: gather_forward(buf, g, j))
        for j in (1, 3, 5, 7):
            gather_copy(buf, g, j, j, partner(j), c).wait_recv()

    def gather_step(buf, g, slot):
        def arrive(j):
            gather_copy(buf, g, j, j, partner(j), c).wait_recv()
            gather_forward(buf, g, j).start()

        @pl.when(slot == 1)
        def _():
            arrive(2)
            arrive(4)

        @pl.when(slot == 3)
        def _():
            arrive(6)

        gather_copy(buf, g, 2 * slot + 1, 0, partner(2 * slot + 1), c).wait_recv()

    def gather_stepped(buf, g):
        for j in (2, 4, 6):
            in_plane.append((lambda j=j: gather_forward(buf, g, j), None))

    def sum_pair_copy(s, slot):
        return remote(rs_sa.at[s % 2, slot], rs_ra.at[s % 2, slot], ra_send.at[s, slot], ra_recv.at[s, slot], partner(1), z)

    def sum_chip_copy(s, slot):
        return remote(
            rs_sb.at[s % 2, slot], rs_rb.at[s % 2, slot], rb_send.at[s, slot], rb_recv.at[s, slot], partner(2 * slot), z)

    def sum_start(s, left, partial):
        slots, kept = (3, 2 - ck, 1 + ck, 0), [None] * 4

        def pair(p):
            slot = slots[p]
            at = [rows(partner(2 * slot + 1), block), rows(partner(2 * slot), block)]
            both = partial(jnp.concatenate([left[i] for i in at], 0))
            rs_sa[s % 2, slot] = both[:block].astype(bf16)
            launch(in_plane, lambda: sum_pair_copy(s, slot))
            kept[p] = both[block:]

        def chips(p):
            slot = slots[p]
            sum_pair_copy(s, slot).wait_recv()
            rs_sb[s % 2, slot] = (kept[p] + rs_ra[s % 2, slot].astype(f32)).astype(bf16)
            launch(in_plane, lambda: sum_chip_copy(s, slot))

        pair(0)
        pair(1)
        chips(0)
        pair(2)
        chips(1)
        pair(3)
        chips(2)
        sum_pair_copy(s, 0).wait_recv()
        rs_acc[s % 2] = kept[3] + rs_ra[s % 2, 0].astype(f32)

    def sum_finish(s):
        total = rs_acc[s % 2]
        for slot in (1, 2, 3):
            sum_chip_copy(s, slot).wait_recv()
            total = total + rs_rb[s % 2, slot].astype(f32)
        return total

    per = block // planes

    def weight_grad(m, parts):
        def body(i, carry):
            at = 0
            for left, right in parts:
                value = right()
                grad = dot(left[rows(i, 2 * block)], value)
                for k in range(2):
                    for t in range(planes):
                        start = k * block + t * per
                        stages[m][t, 2 * i + k, :, at:at + value.shape[1]] = grad[start:start + per].astype(bf16)
                at += value.shape[1]
            return carry

        lax.fori_loop(0, n // 2, body, 0)
        far = planes - 1 - z
        launch(along, lambda: grad_join_copy(m, far), edge)
        for d in (sign, -sign):
            launch(along, lambda d=d: grad_copy(m, z + d), inside(z + d))
        launch(along, lambda: grad_copy(m, near_edge()), edge)

    def near_edge():
        return jnp.where(z == 0, 2, planes - 3)

    def grad_slot(target):
        return lax.rem(target - z + planes, planes)

    def grad_copy(m, target):
        return remote(
            stages[m].at[target], lands[m].at[z], zr_send.at[m, grad_slot(target)], zr_recv.at[m, z], c, target)

    def grad_join_copy(m, far):
        return remote(
            stages[m].at[far], joins[m], zr_send.at[m, 0], zj_recv.at[m], c, jnp.where(z == 0, 1, planes - 2))

    def grad_join(m):
        inner = jnp.logical_not(edge)
        far = jnp.where(z == 1, planes - 1, 0)

        @pl.when(inner)
        def _():
            remote(joins[m], joins[m], zr_send.at[m, 0], zj_recv.at[m], c, z).wait_recv()

            def body(i, carry):
                stages[m][far, i] = (stages[m][far, i].astype(f32) + joins[m][i].astype(f32)).astype(bf16)
                return carry

            lax.fori_loop(0, n, body, 0)

        launch(along, lambda: grad_copy(m, far), inner)

    def owner_copy(m, j):
        return remote(owns[m].at[partner(j)], gots[m].at[c], aa_send.at[m, j], aa_recv.at[m, j], partner(j), z)

    def hand_out(m):
        for d in (1, -1, 2, -2):
            @pl.when(inside(z + d))
            def _(d=d):
                origin = z + d
                part = lands[m].at[origin]
                remote(part, part, zr_send.at[m, 0], zr_recv.at[m, origin], c, z).wait_recv()

        def body(i, carry):
            total = stages[m][z, i].astype(f32)
            for d in range(1, planes):
                total = total + lands[m][lax.rem(z + d, planes), i].astype(f32)
            owns[m][i] = total.astype(bf16)
            return carry

        lax.fori_loop(0, n, body, 0)
        for j in (2 + 2 * ck, 3 + 2 * ck, 4 - 2 * ck, 5 - 2 * ck, 6, 7, 1):
            launch(in_plane, lambda j=j: owner_copy(m, j))
        gots[m][c] = owns[m][c]

    def hand_receive(m):
        for j in range(1, n):
            owner_copy(m, j).wait_recv()

    weight_start(0)
    gather_start(first, 0)

    spread = jnp.broadcast_to(pos_row[...].astype(f32), (head, pos_row.shape[1]))
    positions[...] = spread.T
    side = jnp.where(lax.broadcasted_iota(jnp.int32, (1, head), 1) < head // 2, -1.0, 1.0)

    def table(i, carry):
        at = rows(i, block)
        angle = positions[at] * inverse_ref[...]
        cosine[at] = jnp.cos(angle)
        sine[at] = jnp.sin(angle) * side
        return carry

    gather_finish(first, 0)
    gather_start(dy_all, 1)
    lax.fori_loop(0, n, table, 0)

    def turn_over(src, dst):
        def body(i, carry):
            at = rows(i, block)
            dst[:, at] = src[at].T
            return carry

        lax.fori_loop(0, n, body, 0)

    turn_over(first, first_t)
    for copy in local[3:]:
        copy.wait()
    weight_receive(0)
    weight_start(1)
    gather_finish(dy_all, 1)

    def turn(value, at):
        return value * cosine[at] + pltpu.roll(value, head // 2, 1) * sine[at]

    def turn_back(grad, at):
        return grad * cosine[at] - pltpu.roll(grad, head // 2, 1) * sine[at]

    def project(i, carry):
        at = rows(i, 2 * block)
        result = dot(first[at], w_qkv[...])
        raw[at] = result[:, :qw + kw]
        low_values = result[:, qw + kw:].astype(bf16)
        values[at] = low_values
        values_t[:, at] = low_values.T
        for h in range(group + 1):
            part = result[:, h * head:(h + 1) * head]
            inv = lax.rsqrt(jnp.mean(part * part, -1, keepdims=True) + epsilon)
            gain = qg_ref[...] if h < group else kg_ref[...]
            turned = turn(part * inv * gain, at).astype(bf16)
            if h < group:
                queries[at, h * head:(h + 1) * head] = turned
            else:
                keys[at] = turned
                keys_t[:, at] = turned.T
        return carry

    lax.fori_loop(0, n // 2, project, 0)
    turn_over(dy_all, dy_t)

    def stack(ref, at):
        return jnp.concatenate([ref[at, h * head:(h + 1) * head] for h in range(group)], 0)

    def attend_block(i):
        at = rows(i, block)
        scores = dot_nt(keys[...], stack(queries, at))
        allowed = positions[...] <= pos_row[:, at].astype(f32)
        scores = jnp.concatenate(
            [jnp.where(allowed, scores[:, h * block:(h + 1) * block], masked_score) for h in range(group)], 1)
        peak = jnp.max(scores, 0, keepdims=True)
        weight = jnp.exp2((scores - peak) * (scale * log2e))
        prob = (weight * (1.0 / jnp.sum(weight, 0, keepdims=True))).astype(bf16)
        probs[i] = prob
        result = dot(values_t[...], prob)
        mixed_t[i] = result
        for h in range(group):
            mixed_low[at, h * head:(h + 1) * head] = result[:, h * block:(h + 1) * block].T.astype(bf16)

    def attend(i, carry):
        attend_block(2 * i)
        attend_block(2 * i + 1)
        return carry

    lax.fori_loop(0, n // 4, attend, 0)
    weight_receive(1)
    weight_start(2)
    weight_start(3)
    lax.fori_loop(n // 4, n // 2, attend, 0)
    hand_arrive(1)
    drain(in_plane)
    sum_start(0, mixed_low, lambda left: dot(left, w_out[...]))
    for w in range(4, 2 + 2 * thirds):
        weight_start(w)
    mid = x_ref[...].astype(f32) + sum_finish(0)
    middle[...] = mid
    mid_scale = lax.rsqrt(jnp.mean(mid * mid, -1, keepdims=True) + epsilon)
    second[rows(c, block)] = (mid * mid_scale * fg_ref[...]).astype(bf16)
    gather_start(second, 2)
    for w in range(2, 2 * thirds):
        weight_receive(w)
    hand_arrive(3)

    def feed(t, at):
        units, pair = slice(t * pw, (t + 1) * pw), 2 * pw * t
        both = dot(second[at], w_gu[:, pair:pair + 2 * pw])
        back = dot_nt(dy_all[at], w_down[units])
        gate, up = both[:, :pw], both[:, pw:]
        sig = 1.0 / (1.0 + jnp.exp(-gate))
        silu = gate * sig
        hidden[at, units] = (silu * up).astype(bf16)
        d_gu[at, pair:pair + pw] = (back * up * sig * (1.0 + gate * (1.0 - sig))).astype(bf16)
        d_gu[at, pair + pw:pair + 2 * pw] = (back * silu).astype(bf16)

    def feed_arriving(slot, carry):
        gather_step(second, 2, slot)
        at = rows(chip(slot), 2 * block)
        feed(0, at)
        second_t[:, at] = second[at].T
        return carry

    def third_grad(t):
        weight_grad(t, [
            (second_t, lambda: d_gu[:, 2 * pw * t:2 * pw * (t + 1)]),
            (dy_t, lambda: hidden[:, t * pw:(t + 1) * pw]),
        ])

    def feed_third(t):
        def body(i, carry):
            feed(t, rows(i, 2 * block))
            return carry

        lax.fori_loop(0, n // 2, body, 0)

    lax.fori_loop(0, n // 2, feed_arriving, 0)
    gather_stepped(second, 2)
    weight_receive(2 * thirds)
    weight_receive(2 * thirds + 1)
    third_grad(0)
    for t in range(1, thirds):
        hand_arrive(3 + 2 * t)
        feed_third(t)
        if t < thirds - 1:
            third_grad(t)
    sum_start(1, d_gu, lambda left: dot_nt(left, w_gu[...]))
    third_grad(thirds - 1)
    grad_join(0)
    d_second = sum_finish(1)

    def norm_back(value, gain, grad):
        inv = lax.rsqrt(jnp.mean(value * value, -1, keepdims=True) + epsilon)
        weighted = grad * gain
        inner = jnp.mean(weighted * value, -1, keepdims=True)
        result = inv * weighted - value * (inv * inv * inv * inner)
        return result, jnp.sum(grad * value * inv, 0, keepdims=True)

    gain_own[...] = jnp.zeros_like(gain_own)
    part, gain_own[1:2, :] = norm_back(middle[...], fg_ref[...], d_second)
    d_mid = dy_ref[...].astype(f32) + part
    d_middle[...] = d_mid
    dmid[rows(c, block)] = d_mid.astype(bf16)
    gather_start(dmid, 3)

    dk_acc[...] = jnp.zeros_like(dk_acc)
    dv_acc[...] = jnp.zeros_like(dv_acc)

    def attend_back_block(i):
        at = rows(i, block)
        d_mix = dot_nt(dmid[at], w_out[...]).astype(bf16)
        d_mix = jnp.concatenate([d_mix[:, h * head:(h + 1) * head] for h in range(group)], 0)
        delta = jnp.sum(d_mix.T.astype(f32) * mixed_t[i], 0, keepdims=True)
        prob = probs[i]
        d_prob = dot_nt(values[...], d_mix)
        d_score = (prob.astype(f32) * (d_prob - delta)).astype(bf16)
        d_query = dot(keys_t[...], d_score) * scale
        for h in range(group):
            dq_acc[at, h * head:(h + 1) * head] = d_query[:, h * block:(h + 1) * block].T
        return dot(prob, d_mix), dot(d_score, stack(queries, at))

    def attend_back(slot, carry):
        gather_step(dmid, 3, slot)
        at = rows(chip(slot), 2 * block)
        dmid_t[:, at] = dmid[at].T
        dv_one, dk_one = attend_back_block(2 * chip(slot))
        dv_two, dk_two = attend_back_block(2 * chip(slot) + 1)
        dv_acc[...] += dv_one + dv_two
        dk_acc[...] += dk_one + dk_two
        return carry

    lax.fori_loop(0, n // 2, attend_back, 0)
    gather_stepped(dmid, 3)
    weight_grad(3, [(dmid_t, lambda: mixed_low[...])])
    grad_join(1)
    grad_join(2)

    def project_back(i, carry):
        at = rows(i, block)
        q_sum, k_sum = carry
        for h in range(group + 1):
            if h < group:
                grad, gain = dq_acc[at, h * head:(h + 1) * head], qg_ref[...]
            else:
                grad, gain = dk_acc[at] * scale, kg_ref[...]
            part, gain_part = norm_back(raw[at, h * head:(h + 1) * head], gain, turn_back(grad, at))
            d_qkv[at, h * head:(h + 1) * head] = part.astype(bf16)
            if h < group:
                q_sum = q_sum + gain_part
            else:
                k_sum = k_sum + gain_part
        d_qkv[at, qw + kw:] = dv_acc[at].astype(bf16)
        return q_sum, k_sum

    zero = jnp.zeros((1, head), f32)
    q_sum, k_sum = lax.fori_loop(0, n, project_back, (zero, zero))
    gain_own[2:3, 0:head] = q_sum
    gain_own[3:4, 0:head] = k_sum

    weight_grad(4, [(first_t, lambda: d_qkv[...])])
    grad_join(3)
    drain(in_plane)
    sum_start(3, d_qkv, lambda left: dot_nt(left, w_qkv[...]))
    sum_start(2, hidden, lambda left: dot(left, w_down[...]))
    grad_join(4)
    for m in range(4):
        hand_out(m)
    x_part, gain_own[0:1, :] = norm_back(x_ref[...].astype(f32), ag_ref[...], sum_finish(3))
    dx_ref[...] = d_middle[...] + x_part

    def gain_plane_copy(j):
        return remote(gain_own, gain_plane.at[c], gp_send.at[j], gp_recv.at[j], partner(j), z)

    def gain_copy(d):
        return remote(gain_all.at[z], gain_all.at[z], gz_send.at[d], gz_recv.at[d], c, lax.rem(z + d, planes))

    for j in range(1, n):
        launch(in_plane, lambda j=j: gain_plane_copy(j))
    gain_plane[c] = gain_own[...]
    out_ref[...] = (middle[...] + sum_finish(2)).astype(bf16)
    for j in range(1, n):
        gain_plane_copy(j).wait_recv()
    total = gain_plane[0]
    for i in range(1, n):
        total = total + gain_plane[i]
    gain_all[z] = total
    for d in range(1, planes):
        launch(along, lambda d=d: gain_copy(d))
    for d in range(1, planes):
        origin = gain_all.at[lax.rem(z + planes - d, planes)]
        remote(origin, origin, gz_send.at[d], gz_recv.at[d], c, z).wait_recv()
    total = gain_all[0]
    for i in range(1, planes):
        total = total + gain_all[i]
    gains_ref[...] = total

    hand_out(4)
    for m in range(5):
        hand_receive(m)
    drain(in_plane)
    drain(along)


def finish_kernel(
    n, head, out_in, dx_in, gains_in, got_a, got_b, got_c, got_out, got_qkv,
    out_ref, dx_ref, ag_ref, q_ref, k_ref, v_ref, qg_ref, kg_ref, o_ref, fg_ref, g_ref, u_ref, d_ref,
):
    out_ref[...] = out_in[...]
    dx_ref[...] = dx_in[...]
    ag_ref[...] = gains_in[0:1, :]
    fg_ref[...] = gains_in[1:2, :]
    qg_ref[...] = gains_in[2:3, 0:head]
    kg_ref[...] = gains_in[3:4, 0:head]
    qw, kw = q_ref.shape[1] // n, k_ref.shape[1] // n
    pw = got_a.shape[2] // 3
    thirds = (got_a, got_b, got_c)
    for i in range(n):
        q_ref[:, i * qw:(i + 1) * qw] = got_qkv[i, :, 0:qw].astype(f32)
        k_ref[:, i * kw:(i + 1) * kw] = got_qkv[i, :, qw:qw + kw].astype(f32)
        v_ref[:, i * kw:(i + 1) * kw] = got_qkv[i, :, qw + kw:].astype(f32)
        o_ref[:, i * qw:(i + 1) * qw] = got_out[i].astype(f32)
        for t, got in enumerate(thirds):
            at = (i * len(thirds) + t) * pw
            g_ref[:, at:at + pw] = got[i, :, 0:pw].astype(f32)
            u_ref[:, at:at + pw] = got[i, :, pw:2 * pw].astype(f32)
            d_ref[:, at:at + pw] = got[i, :, 2 * pw:].astype(f32)


def plane_device(
    layer_input,
    token_positions,
    attention_gain,
    query_weight,
    key_matrix,
    value_matrix,
    query_gain,
    key_norm_gain,
    output_weight,
    feedforward_gain,
    gate_weight,
    up_weight,
    down_weight,
    out_cotangent,
):
    n = lax.axis_size("ctx")
    planes = lax.axis_size("fsdp")
    block, width = layer_input.shape[1:]
    length = token_positions.shape[1]
    head = query_gain.shape[0]
    qw = query_weight.shape[1] // n
    kw = key_matrix.shape[1] // n
    fw = gate_weight.shape[1] // n
    group = qw // head
    per = block // planes
    half = head // 2
    inverse = np.power(rope_base, -np.arange(half) * 2.0 / head).astype(np.float32)
    inverse = jnp.asarray(np.concatenate([inverse, inverse])[None])
    vmem = pl.BlockSpec(memory_space=pltpu.VMEM)
    hbm = pl.BlockSpec(memory_space=pl.ANY)
    dma = pltpu.SemaphoreType.DMA
    sizes = (fw, fw, fw, qw, qw + 2 * kw)
    low = lambda *shape: pltpu.VMEM(shape, bf16)
    wide = lambda *shape: pltpu.VMEM(shape, f32)
    scratch = [
        low(width, qw + 2 * kw), low(width, 2 * fw), low(qw, width), low(fw, width),
        low(planes * (output_weight.shape[0] // n), width), low(3, planes * 32, width),
        low(length, width), low(length, width), low(length, width),
        low(width, length), low(width, length), low(width, length), low(width, length),
        wide(length, head), wide(length, head), wide(length, head),
        wide(length, qw + kw), low(length, qw), low(length, kw), low(length, kw),
        low(kw, length), low(kw, length), low(n, length, group * block), wide(n, head, group * block), low(length, qw),
        low(length, fw), low(length, 2 * fw), low(length, qw + 2 * kw),
        wide(length, kw), wide(length, kw), wide(length, qw),
    ]
    scratch += [low(planes, n, per, size) for size in sizes]
    scratch += [low(planes, n, per, size) for size in sizes]
    scratch += [low(n, per, size) for size in sizes]
    scratch += [low(n, per, size) for size in sizes]
    scratch += [low(2, 4, block, width) for _ in range(4)] + [wide(2, block, width)]
    scratch += [
        wide(block, width), wide(block, width), wide(8, width), wide(n, 8, width), wide(planes, 8, width),
        dma((13,)), dma((8, 6)), dma((8, planes)), dma((4, 7)), dma((4, 4)),
        dma((4, n)), dma((4, n)), dma((4, 4)), dma((4, 4)), dma((4, 4)), dma((4, 4)),
        dma((5, planes)), dma((5, planes)), dma((5,)), dma((5, n)), dma((5, n)), dma((n,)), dma((n,)),
        dma((planes,)), dma((planes,)),
    ]
    shapes = [
        jax.ShapeDtypeStruct((block, width), bf16),
        jax.ShapeDtypeStruct((block, width), f32),
        jax.ShapeDtypeStruct((8, width), f32),
    ] + [jax.ShapeDtypeStruct((n, per, size), bf16) for size in sizes]
    results = pl.pallas_call(
        functools.partial(layer_kernel, n, planes, block, head, group, fw),
        out_shape=shapes,
        in_specs=[vmem] * 8 + [hbm] * 7,
        out_specs=[vmem] * len(shapes),
        scratch_shapes=scratch,
        compiler_params=pltpu.CompilerParams(
            collective_id=0, has_side_effects=True, vmem_limit_bytes=60 * 1024 * 1024),
    )(
        layer_input[0], out_cotangent[0], token_positions, inverse,
        attention_gain[None], feedforward_gain[None], query_gain[None], key_norm_gain[None],
        query_weight, key_matrix, value_matrix, output_weight, gate_weight, up_weight, down_weight,
    )
    plain = lambda rows, columns, kind=f32: jax.ShapeDtypeStruct((rows, columns), kind)
    finals = [
        plain(block, width, bf16), plain(block, width), plain(1, width),
        plain(per, n * qw), plain(per, n * kw), plain(per, n * kw), plain(1, head), plain(1, head),
        plain(per, n * qw), plain(1, width), plain(per, n * fw), plain(per, n * fw), plain(per, n * fw),
    ]
    done = pl.pallas_call(
        functools.partial(finish_kernel, n, head),
        out_shape=finals,
        in_specs=[vmem] * len(shapes),
        out_specs=[vmem] * len(finals),
    )(*results)
    out, dx, ag, q, k, v, qg, kg, o, fg, g, u, d = done
    return out[None], dx[None], ag[0], q, k, v, qg[0], kg[0], o.T, fg[0], g, u, d.T


def solution(mesh):
    in_specs = (
        P("fsdp", "ctx", None),
        P("fsdp", None),
        P(),
        P("fsdp", None),
        P("fsdp", None),
        P("fsdp", None),
        P(),
        P(),
        P("fsdp", None),
        P(),
        P("fsdp", None),
        P("fsdp", None),
        P("fsdp", None),
        P("fsdp", "ctx", None),
    )
    out_specs = (
        P("fsdp", "ctx", None),
        P("fsdp", "ctx", None),
        P(),
        P(("ctx", "fsdp"), None),
        P(("ctx", "fsdp"), None),
        P(("ctx", "fsdp"), None),
        P(),
        P(),
        P(None, ("ctx", "fsdp")),
        P(),
        P(("ctx", "fsdp"), None),
        P(("ctx", "fsdp"), None),
        P(None, ("ctx", "fsdp")),
    )

    def run(*arguments):
        n, planes = mesh.shape["ctx"], mesh.shape["fsdp"]
        key_heads = arguments[4].shape[1] // arguments[6].shape[0]
        whole_heads = n == 8 and planes == 4 and key_heads == n
        return jax.shard_map(
            plane_device if whole_heads else on_device,
            mesh=mesh, in_specs=in_specs, out_specs=out_specs, check_vma=False,
        )(*arguments)

    return run
```

```python
import functools

import jax
import jax.numpy as jnp
import numpy as np
from jax import lax
from jax.experimental import pallas as pl
from jax.experimental.pallas import tpu as pltpu
from jax.sharding import PartitionSpec as P

epsilon = 1e-06
rope_base = 1000000.0
masked_score = -1e30


def from_behind(block, axis, distance):
    devices = range(lax.axis_size(axis))
    route = [((i - distance) % len(devices), i) for i in devices]
    return lax.ppermute(block, axis, route)


def rotate(value_rows):
    half = value_rows.shape[-1] // 2
    return jnp.concatenate([-value_rows[..., half:], value_rows[..., :half]], -1)


def rotate_back(value_rows):
    half = value_rows.shape[-1] // 2
    return jnp.concatenate([value_rows[..., half:], -value_rows[..., :half]], -1)


def rope_tables(token_offsets, head_size):
    half = head_size // 2
    inverse = rope_base ** (-(jnp.arange(half).astype(jnp.float32) * 2.0) / head_size)
    angles = token_offsets.astype(jnp.float32)[:, None] * inverse[None, :]
    cosine = jnp.cos(angles)
    sine = jnp.sin(angles)
    return (jnp.concatenate([cosine, cosine], -1), jnp.concatenate([sine, sine], -1))


def norm_scale(value_rows):
    return lax.rsqrt(jnp.mean(value_rows * value_rows, -1, keepdims=True) + epsilon)


def norm_back(value_rows, scale, gain, grad):
    weighted = grad * gain
    inner = jnp.mean(weighted * value_rows, -1, keepdims=True)
    result = scale * weighted - value_rows * scale * scale * scale * inner
    gain_part = jnp.sum((grad * value_rows * scale).reshape(-1, gain.shape[0]), 0)
    return (result, gain_part)


def row_products(left, pieces):
    return tuple((jnp.dot(left, piece, preferred_element_type=jnp.float32) for piece in pieces))


def column_products(rights, pieces):
    total = jnp.einsum("tc,rc->tr", rights[0], pieces[0], preferred_element_type=jnp.float32)
    for right, piece in zip(rights[1:], pieces[1:]):
        total = total + jnp.einsum("tc,rc->tr", right, piece, preferred_element_type=jnp.float32)
    return total


def on_device(
    layer_input,
    token_positions,
    attention_gain,
    query_weight,
    key_matrix,
    value_matrix,
    query_gain,
    key_norm_gain,
    output_weight,
    feedforward_gain,
    gate_weight,
    up_weight,
    down_weight,
    out_cotangent,
):
    hidden_in = layer_input[0].astype(jnp.float32)
    count = hidden_in.shape[0]
    head_size = query_gain.shape[0]
    query_width = query_weight.shape[1]
    key_width = key_matrix.shape[1]
    inner_width = gate_weight.shape[1]
    heads = query_width // head_size
    key_heads = key_width // head_size
    group = heads // key_heads
    scale = head_size ** (-0.5)
    cycles = lax.axis_size("ctx")
    own_index = lax.axis_index("ctx")
    sequence_pos = token_positions[0]
    token_offsets = lax.dynamic_slice_in_dim(sequence_pos, own_index * count, count)
    cosine, sine = rope_tables(token_offsets, head_size)
    cosine = cosine[:, None, :]
    sine = sine[:, None, :]
    first_scale = norm_scale(hidden_in)
    first = (hidden_in * first_scale * attention_gain).astype(jnp.bfloat16)
    query_raw, key_unnormed, value_unnormed = row_products(
        first,
        (
            lax.all_gather(query_weight, "fsdp", axis=0, tiled=True),
            lax.all_gather(key_matrix, "fsdp", axis=0, tiled=True),
            lax.all_gather(value_matrix, "fsdp", axis=0, tiled=True),
        ),
    )
    query_heads = query_raw.reshape(count, heads, head_size)
    query_scale = norm_scale(query_heads)
    query_normed = query_heads * query_scale * query_gain
    query_rot = query_normed * cosine + rotate(query_normed) * sine
    query_grouped = (
        query_rot.reshape(count, key_heads, group, head_size)
        .transpose(1, 2, 0, 3)
        .astype(jnp.bfloat16)
    )
    key_heads_raw = key_unnormed.reshape(count, key_heads, head_size)
    key_scale = norm_scale(key_heads_raw)
    key_normed = key_heads_raw * key_scale * key_norm_gain
    key_low = (
        (key_normed * cosine + rotate(key_normed) * sine)
        .reshape(count, key_width)
        .astype(jnp.bfloat16)
    )
    value_low = value_unnormed.astype(jnp.bfloat16)
    rowmax = jnp.full((key_heads, group, count), masked_score, jnp.float32)
    keys_piece = lax.all_gather(key_low, "ctx", axis=0, tiled=True).reshape(
        -1, key_heads, head_size
    )
    values_piece = lax.all_gather(value_low, "ctx", axis=0, tiled=True).reshape(
        -1, key_heads, head_size
    )
    key_pos = sequence_pos
    allowed = token_offsets[:, None] >= key_pos[None, :]
    scores = (
        jnp.einsum("kgtd,skd->kgts", query_grouped, keys_piece, preferred_element_type=jnp.float32)
        * scale
    )
    scores = jnp.where(allowed, scores, masked_score)
    newmax = jnp.maximum(rowmax, jnp.max(scores, -1))
    weights = jnp.where(allowed, jnp.exp(scores - newmax[..., None]), 0.0)
    accum = jnp.einsum(
        "kgts,skd->kgtd",
        weights.astype(jnp.bfloat16),
        values_piece,
        preferred_element_type=jnp.float32,
    )
    rowsum = jnp.sum(weights, -1)
    accum, rowmax, rowsum = (accum, newmax, rowsum)
    normalized = accum / rowsum[..., None]
    logsum = rowmax + jnp.log(rowsum)
    attention_low = (
        normalized.transpose(2, 0, 1, 3).reshape(count, query_width).astype(jnp.bfloat16)
    )
    output_whole = lax.all_gather(output_weight, "fsdp", axis=0, tiled=True)
    branch_out = jnp.dot(attention_low, output_whole, preferred_element_type=jnp.float32)
    middle = hidden_in + branch_out
    second_scale = norm_scale(middle)
    second = (middle * second_scale * feedforward_gain).astype(jnp.bfloat16)
    gate, up = row_products(
        second,
        (
            lax.all_gather(gate_weight, "fsdp", axis=0, tiled=True),
            lax.all_gather(up_weight, "fsdp", axis=0, tiled=True),
        ),
    )
    sigmoid_gate = jax.nn.sigmoid(gate)
    silu_gate = gate * sigmoid_gate
    hidden_low = (silu_gate * up).astype(jnp.bfloat16)
    (down_out,) = row_products(
        hidden_low, (lax.all_gather(down_weight, "fsdp", axis=0, tiled=True),)
    )
    layer_output = (middle + down_out).astype(jnp.bfloat16)[None]
    cotangent = out_cotangent[0]
    hidden_grad = column_products(
        (cotangent,), lax.all_gather((down_weight,), "fsdp", axis=0, tiled=True)
    )
    up_low = (hidden_grad * silu_gate).astype(jnp.bfloat16)
    gate_low = (hidden_grad * up * sigmoid_gate * (1.0 + gate * (1.0 - sigmoid_gate))).astype(
        jnp.bfloat16
    )
    second_grad = column_products(
        (gate_low, up_low), lax.all_gather((gate_weight, up_weight), "fsdp", axis=0, tiled=True)
    )
    middle_part, feedforward_part = norm_back(middle, second_scale, feedforward_gain, second_grad)
    middle_grad = cotangent.astype(jnp.float32) + middle_part
    middle_low = middle_grad.astype(jnp.bfloat16)
    attention_grad = jnp.einsum(
        "tc,rc->tr", middle_low, output_whole, preferred_element_type=jnp.float32
    )
    attention_grad_low = attention_grad.astype(jnp.bfloat16)
    mixed_grad = attention_grad_low.reshape(count, key_heads, group, head_size).transpose(
        1, 2, 0, 3
    )
    delta = jnp.sum(mixed_grad.astype(jnp.float32) * normalized, -1)

    def cycle_step(index, carry):
        keys_held, values_held, key_acc, value_acc, query_acc = carry
        anchor = (own_index - index) % cycles
        key_pos = lax.dynamic_slice_in_dim(sequence_pos, anchor * count, count)
        keys_piece = keys_held.astype(jnp.bfloat16).reshape(count, key_heads, head_size)
        values_piece = values_held.astype(jnp.bfloat16).reshape(count, key_heads, head_size)
        allowed = token_offsets[:, None] >= key_pos[None, :]
        scores = (
            jnp.einsum(
                "kgtd,skd->kgts", query_grouped, keys_piece, preferred_element_type=jnp.float32
            )
            * scale
        )
        probs = jnp.where(allowed, jnp.exp(scores - logsum[..., None]), 0.0)
        value_acc = value_acc + jnp.einsum(
            "kgts,kgtd->skd",
            probs.astype(jnp.bfloat16),
            mixed_grad,
            preferred_element_type=jnp.float32,
        ).reshape(count, key_width)
        prob_grad = jnp.einsum(
            "kgtd,skd->kgts", mixed_grad, values_piece, preferred_element_type=jnp.float32
        )
        score_grad = (probs * (prob_grad - delta[..., None])).astype(jnp.bfloat16)
        query_acc = (
            query_acc
            + jnp.einsum(
                "kgts,skd->kgtd", score_grad, keys_piece, preferred_element_type=jnp.float32
            )
            * scale
        )
        key_acc = (
            key_acc
            + jnp.einsum(
                "kgts,kgtd->skd", score_grad, query_grouped, preferred_element_type=jnp.float32
            ).reshape(count, key_width)
            * scale
        )
        moved = (
            from_behind(keys_held.astype(jnp.bfloat16), "ctx", 1).astype(keys_held.dtype),
            from_behind(values_held.astype(jnp.bfloat16), "ctx", 1).astype(values_held.dtype),
            from_behind(key_acc.astype(jnp.bfloat16), "ctx", 1).astype(key_acc.dtype),
            from_behind(value_acc.astype(jnp.bfloat16), "ctx", 1).astype(value_acc.dtype),
        )
        return (moved[0], moved[1], moved[2], moved[3], query_acc)

    start_cycle = (
        key_low.astype(jnp.float32),
        value_low.astype(jnp.float32),
        jnp.zeros((count, key_width), jnp.float32),
        jnp.zeros((count, key_width), jnp.float32),
        jnp.zeros((key_heads, group, count, head_size), jnp.float32),
    )
    cycle_done = lax.fori_loop(0, cycles, cycle_step, start_cycle)
    key_acc = cycle_done[2]
    value_acc = cycle_done[3]
    query_acc = cycle_done[4]
    query_rot_grad = query_acc.transpose(2, 0, 1, 3).reshape(count, heads, head_size)
    query_normed_grad = query_rot_grad * cosine + rotate_back(query_rot_grad * sine)
    query_heads_grad, query_part = norm_back(
        query_heads, query_scale, query_gain, query_normed_grad
    )
    query_low_grad = query_heads_grad.reshape(count, query_width).astype(jnp.bfloat16)
    key_rot_grad = key_acc.reshape(count, key_heads, head_size)
    key_normed_grad = key_rot_grad * cosine + rotate_back(key_rot_grad * sine)
    key_heads_grad, key_part = norm_back(key_heads_raw, key_scale, key_norm_gain, key_normed_grad)
    key_low_grad = key_heads_grad.reshape(count, key_width).astype(jnp.bfloat16)
    value_low_grad = value_acc.astype(jnp.bfloat16)
    first_grad = column_products(
        (query_low_grad, key_low_grad, value_low_grad),
        lax.all_gather((query_weight, key_matrix, value_matrix), "fsdp", axis=0, tiled=True),
    )
    input_part, attention_part = norm_back(hidden_in, first_scale, attention_gain, first_grad)
    input_gradient = (middle_grad + input_part)[None]
    rights_first = jnp.concatenate([query_low_grad, key_low_grad, value_low_grad], 1)
    rights_second = jnp.concatenate([gate_low, up_low], 1)
    pairs = (
        (first, rights_first),
        (second, rights_second),
        (middle_low, attention_low),
        (cotangent, hidden_low),
    )
    parts = []
    for left, right in pairs:
        parts.append(jnp.einsum("tr,tc->rc", left, right, preferred_element_type=jnp.float32))
    sums = lax.psum_scatter(
        jnp.concatenate(parts, 1), ("ctx", "fsdp"), scatter_dimension=0, tiled=True
    )
    edges = [0, query_width, query_width + key_width, query_width + 2 * key_width]
    edges = edges + [edges[3] + inner_width, edges[3] + 2 * inner_width]
    edges = edges + [edges[5] + query_width, edges[5] + query_width + inner_width]
    query_gradient = sums[:, edges[0] : edges[1]]
    key_gradient = sums[:, edges[1] : edges[2]]
    value_gradient = sums[:, edges[2] : edges[3]]
    gate_gradient = sums[:, edges[3] : edges[4]]
    up_gradient = sums[:, edges[4] : edges[5]]
    output_gradient = sums[:, edges[5] : edges[6]].T
    down_gradient = sums[:, edges[6] : edges[7]].T
    attention_total, query_total, key_total, feedforward_total = lax.psum(
        (attention_part, query_part, key_part, feedforward_part), ("ctx", "fsdp")
    )
    return (
        layer_output,
        input_gradient,
        attention_total,
        query_gradient,
        key_gradient,
        value_gradient,
        query_total,
        key_total,
        output_gradient,
        feedforward_total,
        gate_gradient,
        up_gradient,
        down_gradient,
    )


MESH = pl.DeviceIdType.MESH
f32 = jnp.float32
bf16 = jnp.bfloat16


def dot(left, right):
    return jnp.dot(left, right, preferred_element_type=f32)


def dot_nt(left, right):
    return lax.dot_general(left, right, (((1,), (1,)), ((), ())), preferred_element_type=f32)


def dot_tn(left, right):
    return lax.dot_general(left, right, (((0,), (0,)), ((), ())), preferred_element_type=f32)


def layer_kernel(
    n, planes, block, head, group, fw,
    x_ref, dy_ref, pos_row, inverse_ref, ag_ref, fg_ref, qg_ref, kg_ref,
    wq, wk, wv, wo, wg, wu, wd,
    out_ref, dx_ref, gains_ref, got_a, got_b, got_c, got_out, got_qkv,
    w_qkv, w_gu, w_out, w_down, t_out, t_down,
    first, dy_all, second, first_t, dy_t, second_t, dmid_t,
    positions, cosine, sine,
    raw, queries, keys, values, keys_t, values_t, probs, sums, mixed_t, mixed_low,
    hidden, d_gu, d_qkv, dk_acc, dv_acc,
    stage_a, stage_b, stage_c, stage_out, stage_qkv,
    land_a, land_b, land_c, land_out, land_qkv,
    join_a, join_b, join_c, join_out, join_qkv,
    rs_sa, rs_ra, rs_sb, rs_rb, rs_kept, rs_acc,
    middle, d_middle, gain_own, gain_plane, gain_all,
    local_sem, wz_send, wz_recv, hand_send, hand_recv,
    ag_send, ag_recv, ra_send, ra_recv, rb_send, rb_recv,
    zr_send, zr_recv, zj_recv, aa_send, aa_recv, gp_send, gp_recv, gz_send, gz_recv,
):
    c = lax.axis_index("ctx")
    z = lax.axis_index("fsdp")
    dmid = first
    cy, cx, ck = lax.div(c, 4), lax.rem(lax.div(c, 2), 2), lax.rem(c, 2)
    ci = lax.rem(c, 4)
    sign = 1 - 2 * ck
    qw, kw = group * head, head
    pw = 128
    thirds = fw // pw
    piece = pw // 4
    width = x_ref.shape[1]
    scale = head ** (-0.5)
    log2e = 1.4426950408889634
    gots = (got_a, got_b, got_c, got_out, got_qkv)
    stages = (stage_a, stage_b, stage_c, stage_out, stage_qkv)
    lands = (land_a, land_b, land_c, land_out, land_qkv)
    joins = (join_a, join_b, join_c, join_out, join_qkv)
    owns = joins

    def partner(j):
        y = lax.rem(cy + lax.div(j, 4), 2)
        x = lax.rem(cx + lax.rem(lax.div(j, 2), 2), 2)
        k = lax.rem(ck + lax.rem(j, 2), 2)
        return y * 4 + x * 2 + k

    def chip(slot):
        return lax.rem(cy + lax.div(slot, 2), 2) * 2 + lax.rem(cx + lax.rem(slot, 2), 2)

    def rows(start, size):
        return pl.ds(pl.multiple_of(start * size, size), size)

    def remote(src, dst, send, recv, ctx, plane):
        return pltpu.make_async_remote_copy(
            src_ref=src, dst_ref=dst, send_sem=send, recv_sem=recv,
            device_id={"ctx": ctx, "fsdp": plane}, device_id_type=MESH,
        )

    in_plane, along = [], []

    def launch(started, copy, when=None):
        if when is None:
            copy().start()
        else:
            pl.when(when)(lambda: copy().start())
        started.append((copy, when))

    def drain(started):
        for copy, when in started:
            if when is None:
                copy().wait_send()
            else:
                pl.when(when)(lambda copy=copy: copy().wait_send())
        started.clear()

    own_rows = wq.shape[0]
    out_rows = wo.shape[0] // n

    def own_slices():
        mine = rows(z, own_rows)
        pairs = [
            (wq.at[:, rows(c, qw)], w_qkv.at[mine, 0:qw]),
            (wk.at[:, rows(c, kw)], w_qkv.at[mine, qw:qw + kw]),
            (wv.at[:, rows(c, kw)], w_qkv.at[mine, qw + kw:qw + 2 * kw]),
            (wo.at[rows(c, out_rows)], t_out.at[rows(z, out_rows)]),
        ]
        for t in range(thirds):
            at = 2 * pw * t
            pairs.append((wg.at[:, rows(c * thirds + t, pw)], w_gu.at[mine, at:at + pw]))
            pairs.append((wu.at[:, rows(c * thirds + t, pw)], w_gu.at[mine, at + pw:at + 2 * pw]))
            pairs.append((wd.at[rows((cy * thirds + t) * 4 + ci, piece)], t_down.at[t, rows(z, piece)]))
        return pairs

    local = [pltpu.make_async_copy(src, dst, local_sem.at[i]) for i, (src, dst) in enumerate(own_slices())]
    for copy in local:
        copy.start()

    edge = jnp.logical_or(z == 0, z == planes - 1)
    for land in lands:
        @pl.when(edge)
        def _(land=land):
            land[planes - 1 - z] = jnp.zeros(land.shape[1:], bf16)

    barrier = pltpu.get_barrier_semaphore()
    for j in range(1, n):
        pl.semaphore_signal(barrier, inc=1, device_id={"ctx": partner(j), "fsdp": z}, device_id_type=MESH)
    for d in range(1, planes):
        pl.semaphore_signal(
            barrier, inc=1, device_id={"ctx": c, "fsdp": lax.rem(z + d, planes)}, device_id_type=MESH)
    x = x_ref[...].astype(f32)
    x_scale = lax.rsqrt(jnp.mean(x * x, -1, keepdims=True) + epsilon)
    first[rows(c, block)] = (x * x_scale * ag_ref[...]).astype(bf16)
    dy_all[rows(c, block)] = dy_ref[...]
    for copy in local[:3]:
        copy.wait()
    pl.semaphore_wait(barrier, n + planes - 2)

    def inside(t):
        return jnp.logical_and(t >= 0, t < planes)

    weights = [
        (lambda o: w_qkv.at[rows(o, own_rows)], None),
        (lambda o: t_out.at[rows(o, out_rows)], 0),
    ]
    for t in range(thirds):
        weights.append((lambda o, t=t: w_gu.at[rows(o, own_rows), 2 * pw * t:2 * pw * (t + 1)], None))
        weights.append((lambda o, t=t: t_down.at[t, rows(o, piece)], 1 + t))

    def weight_copy(w, slot, origin, target):
        part = weights[w][0](origin)
        return remote(part, part, wz_send.at[w, slot], wz_recv.at[w, origin], c, target)

    def weight_start(w):
        for slot, k in enumerate((1, -1, 2, -2)):
            d = sign * k
            launch(along, lambda slot=slot, d=d: weight_copy(w, slot, z, z + d), inside(z + d))
        if weights[w][1] is not None:
            hand_over(w, z, 0, None)

    def hand_target(h):
        if h == 0:
            return lambda i: w_out.at[rows(i, out_rows)]
        return lambda i: w_down.at[rows((h - 1) * 4 + i, piece)]

    def hand_copy(w, origin, slot):
        h = weights[w][1]
        return remote(
            weights[w][0](origin), hand_target(h)(ci), hand_send.at[h, slot], hand_recv.at[h, ci], 2 * origin + cy, z)

    def hand_over(w, origin, slot, valid):
        away = 2 * origin + cy != c
        here = jnp.logical_not(away)
        if valid is not None:
            away, here = jnp.logical_and(valid, away), jnp.logical_and(valid, here)
        launch(in_plane, lambda: hand_copy(w, origin, slot), away)

        @pl.when(here)
        def _():
            hand_target(weights[w][1])(ci)[...] = weights[w][0](origin)[...]

    def hand_arrive(w):
        h = weights[w][1]
        for i in range(4):
            @pl.when(4 * ck + i != c)
            def _(i=i):
                part = hand_target(h)(i)
                remote(part, part, hand_send.at[h, 0], hand_recv.at[h, i], c, z).wait_recv()

    def weight_arrivals():
        for d in range(1, planes):
            for side, way in enumerate((1, -1)):
                origin = z - way * d
                passed = jnp.logical_and(inside(origin), inside(z + way)) if 1 < d < planes - 1 else None
                yield d, side, way, origin, passed

    def weight_forward(w):
        for d, side, way, origin, passed in weight_arrivals():
            if passed is not None:
                pl.when(passed)(lambda origin=origin: weight_copy(w, 0, origin, z).wait_recv())
                launch(
                    along,
                    lambda d=d, side=side, way=way, origin=origin: weight_copy(
                        w, 2 * d + side, origin, z + way),
                    passed)

    def weight_receive(w, forward=True):
        if forward:
            weight_forward(w)
        for d, side, way, origin, passed in weight_arrivals():
            valid = inside(origin)
            here = valid if passed is None else jnp.logical_and(valid, jnp.logical_not(passed))
            pl.when(here)(lambda origin=origin: weight_copy(w, 0, origin, z).wait_recv())
            if weights[w][1] is not None:
                hand_over(w, origin, 2 * d - 1 + side, valid)

    def gather_copy(buf, g, j, send, origin, target):
        part = buf.at[rows(origin, block)]
        return remote(part, part, ag_send.at[g, send], ag_recv.at[g, j], target, z)

    def gather_start(buf, g):
        for j in (1, 2 + 2 * ck, 4 - 2 * ck, 6):
            launch(in_plane, lambda j=j: gather_copy(buf, g, j, j, c, partner(j)))

    def gather_forward(buf, g, j):
        return gather_copy(buf, g, j + 1, j + 1, partner(j), partner(1))

    def gather_finish(buf, g):
        for j in (2, 4, 6):
            gather_copy(buf, g, j, j, partner(j), c).wait_recv()
            launch(in_plane, lambda j=j: gather_forward(buf, g, j))
        for j in (1, 3, 5, 7):
            gather_copy(buf, g, j, j, partner(j), c).wait_recv()

    def gather_step(buf, g, slot):
        def arrive(j):
            gather_copy(buf, g, j, j, partner(j), c).wait_recv()
            gather_forward(buf, g, j).start()

        @pl.when(slot == 1)
        def _():
            arrive(2)
            arrive(4)

        @pl.when(slot == 3)
        def _():
            arrive(6)

        gather_copy(buf, g, 2 * slot + 1, 0, partner(2 * slot + 1), c).wait_recv()

    def gather_stepped(buf, g):
        for j in (2, 4, 6):
            in_plane.append((lambda j=j: gather_forward(buf, g, j), None))

    def sum_pair_copy(s, slot):
        return remote(rs_sa.at[s % 2, slot], rs_ra.at[s % 2, slot], ra_send.at[s, slot], ra_recv.at[s, slot], partner(1), z)

    def sum_chip_copy(s, slot):
        return remote(
            rs_sb.at[s % 2, slot], rs_rb.at[s % 2, slot], rb_send.at[s, slot], rb_recv.at[s, slot], partner(2 * slot), z)

    def sum_slot(p):
        return jnp.where(p == 0, 3, jnp.where(p == 1, 2 - ck, jnp.where(p == 2, 1 + ck, 0)))

    def sum_start(s, left, partial, prepare=None, ready=None):
        if prepare is not None:
            prepare(chip(sum_slot(0)))
        if ready is not None:
            ready()

        def body(p, carry):
            slot = sum_slot(p)
            at = [rows(partner(2 * slot + 1), block), rows(partner(2 * slot), block)]
            both = partial(jnp.concatenate([left[i] for i in at], 0))
            rs_sa[s % 2, slot] = both[:block].astype(bf16)
            sum_pair_copy(s, slot).start()
            rs_kept[lax.rem(p, 2)] = both[block:]
            if prepare is not None:
                @pl.when(p < 3)
                def _():
                    prepare(chip(sum_slot(p + 1)))

            @pl.when(p > 0)
            def _():
                before = sum_slot(p - 1)
                sum_pair_copy(s, before).wait_recv()
                rs_sb[s % 2, before] = (
                    rs_kept[lax.rem(p + 1, 2)] + rs_ra[s % 2, before].astype(f32)).astype(bf16)
                sum_chip_copy(s, before).start()

            return carry

        lax.fori_loop(0, 4, body, 0)
        for slot in range(4):
            in_plane.append((lambda slot=slot: sum_pair_copy(s, slot), None))
            if slot > 0:
                in_plane.append((lambda slot=slot: sum_chip_copy(s, slot), None))
        sum_pair_copy(s, 0).wait_recv()
        rs_acc[s % 2] = rs_kept[1] + rs_ra[s % 2, 0].astype(f32)

    def sum_finish(s):
        total = rs_acc[s % 2]
        for slot in (1, 2, 3):
            sum_chip_copy(s, slot).wait_recv()
            total = total + rs_rb[s % 2, slot].astype(f32)
        return total

    per = block // planes

    def weight_grad(m, parts):
        def body(i, carry):
            at = 0
            for left, right in parts:
                value = right()
                grad = dot(left[rows(i, 2 * block)], value)
                for k in range(2):
                    for t in range(planes):
                        start = k * block + t * per
                        stages[m][t, 2 * i + k, :, at:at + value.shape[1]] = grad[start:start + per].astype(bf16)
                at += value.shape[1]
            return carry

        lax.fori_loop(0, n // 2, body, 0)
        far = planes - 1 - z
        launch(along, lambda: grad_join_copy(m, far), edge)
        for d in (sign, -sign):
            launch(along, lambda d=d: grad_copy(m, z + d), inside(z + d))
        launch(along, lambda: grad_copy(m, near_edge()), edge)

    def near_edge():
        return jnp.where(z == 0, 2, planes - 3)

    def grad_slot(target):
        return lax.rem(target - z + planes, planes)

    def grad_copy(m, target):
        return remote(
            stages[m].at[target], lands[m].at[z], zr_send.at[m, grad_slot(target)], zr_recv.at[m, z], c, target)

    def grad_join_copy(m, far):
        return remote(
            stages[m].at[far], joins[m], zr_send.at[m, 0], zj_recv.at[m], c, jnp.where(z == 0, 1, planes - 2))

    def grad_join(m):
        inner = jnp.logical_not(edge)
        far = jnp.where(z == 1, planes - 1, 0)

        @pl.when(inner)
        def _():
            remote(joins[m], joins[m], zr_send.at[m, 0], zj_recv.at[m], c, z).wait_recv()

            def body(i, carry):
                stages[m][far, i] = (stages[m][far, i].astype(f32) + joins[m][i].astype(f32)).astype(bf16)
                return carry

            lax.fori_loop(0, n, body, 0)

        launch(along, lambda: grad_copy(m, far), inner)

    def owner_copy(m, j):
        return remote(owns[m].at[partner(j)], gots[m].at[c], aa_send.at[m, j], aa_recv.at[m, j], partner(j), z)

    def hand_out(m):
        for d in (1, -1, 2, -2):
            @pl.when(inside(z + d))
            def _(d=d):
                origin = z + d
                part = lands[m].at[origin]
                remote(part, part, zr_send.at[m, 0], zr_recv.at[m, origin], c, z).wait_recv()

        def body(i, carry):
            total = stages[m][z, i].astype(f32)
            for d in range(1, planes):
                total = total + lands[m][lax.rem(z + d, planes), i].astype(f32)
            owns[m][i] = total.astype(bf16)
            return carry

        lax.fori_loop(0, n, body, 0)
        for j in (2 + 2 * ck, 3 + 2 * ck, 4 - 2 * ck, 5 - 2 * ck, 6, 7, 1):
            launch(in_plane, lambda j=j: owner_copy(m, j))
        gots[m][c] = owns[m][c]

    def hand_receive(m):
        for j in range(1, n):
            owner_copy(m, j).wait_recv()

    weight_start(0)
    gather_start(first, 0)
    local[3].wait()
    weight_start(1)

    spread = jnp.broadcast_to(pos_row[...].astype(f32), (head, pos_row.shape[1]))
    positions[...] = spread.T
    side = jnp.where(lax.broadcasted_iota(jnp.int32, (1, head), 1) < head // 2, -1.0, 1.0)

    def table(i, carry):
        at = rows(i, block)
        angle = positions[at] * inverse_ref[...]
        cosine[at] = jnp.cos(angle)
        sine[at] = jnp.sin(angle) * side
        return carry

    gather_finish(first, 0)
    gather_start(dy_all, 1)
    lax.fori_loop(0, n, table, 0)

    def turn_over(src, dst):
        def body(i, carry):
            at = rows(i, block)
            dst[:, at] = src[at].T
            return carry

        lax.fori_loop(0, n, body, 0)

    turn_over(first, first_t)
    for copy in local[4:]:
        copy.wait()
    weight_receive(0)
    weight_start(2)
    weight_start(3)
    gather_finish(dy_all, 1)

    def turn(value, at):
        return value * cosine[at] + pltpu.roll(value, head // 2, 1) * sine[at]

    def turn_back(grad, at):
        return grad * cosine[at] - pltpu.roll(grad, head // 2, 1) * sine[at]

    def project(i, carry):
        at = rows(i, 2 * block)
        result = dot(first[at], w_qkv[...])
        raw[at] = result[:, :qw + kw]
        low_values = result[:, qw + kw:].astype(bf16)
        values[at] = low_values
        values_t[:, at] = low_values.T
        for h in range(group + 1):
            part = result[:, h * head:(h + 1) * head]
            inv = lax.rsqrt(jnp.mean(part * part, -1, keepdims=True) + epsilon)
            gain = qg_ref[...] if h < group else kg_ref[...]
            turned = turn(part * inv * gain, at)
            if h < group:
                queries[at, h * head:(h + 1) * head] = (turned * (scale * log2e)).astype(bf16)
            else:
                low_keys = turned.astype(bf16)
                keys[at] = low_keys
                keys_t[:, at] = low_keys.T
        return carry

    lax.fori_loop(0, n // 2, project, 0)
    turn_over(dy_all, dy_t)

    def stack(ref, at):
        return jnp.concatenate([ref[at, h * head:(h + 1) * head] for h in range(group)], 0)

    def attend_block(i):
        at = rows(i, block)
        scores = dot_nt(keys[...], stack(queries, at))
        allowed = positions[...] <= pos_row[:, at].astype(f32)
        weight = jnp.concatenate(
            [jnp.exp2(jnp.where(allowed, scores[:, h * block:(h + 1) * block], masked_score)) for h in range(group)], 1)
        inv = 1.0 / jnp.sum(weight, 0, keepdims=True)
        low_weight = weight.astype(bf16)
        probs[i] = low_weight
        sums[i] = inv
        result = dot(values_t[...], low_weight) * inv
        mixed_t[i] = result
        for h in range(group):
            mixed_low[at, h * head:(h + 1) * head] = result[:, h * block:(h + 1) * block].T.astype(bf16)

    def attend(place):
        attend_block(2 * place)
        attend_block(2 * place + 1)

    def output_ready():
        weight_receive(1)
        weight_start(4)
        weight_start(5)
        hand_arrive(1)
        drain(in_plane)

    sum_start(0, mixed_low, lambda left: dot(left, w_out[...]), attend, output_ready)
    weight_start(6)
    weight_start(7)
    mid = x_ref[...].astype(f32) + sum_finish(0)
    middle[...] = mid
    mid_scale = lax.rsqrt(jnp.mean(mid * mid, -1, keepdims=True) + epsilon)
    second[rows(c, block)] = (mid * mid_scale * fg_ref[...]).astype(bf16)
    gather_start(second, 2)
    weight_receive(2)
    weight_receive(3)
    hand_arrive(3)

    def feed(t, at):
        units, pair = slice(t * pw, (t + 1) * pw), 2 * pw * t
        both = dot(second[at], w_gu[:, pair:pair + 2 * pw])
        back = dot_nt(dy_all[at], w_down[units])
        gate, up = both[:, :pw], both[:, pw:]
        sig = 1.0 / (1.0 + jnp.exp(-gate))
        silu = gate * sig
        hidden[at, units] = (silu * up).astype(bf16)
        d_gu[at, pair:pair + pw] = (back * up * sig * (1.0 + gate * (1.0 - sig))).astype(bf16)
        d_gu[at, pair + pw:pair + 2 * pw] = (back * silu).astype(bf16)

    def feed_arriving(slot, carry):
        gather_step(second, 2, slot)
        at = rows(chip(slot), 2 * block)
        feed(0, at)
        second_t[:, at] = second[at].T
        return carry

    def third_grad(t):
        weight_grad(t, [
            (second_t, lambda: d_gu[:, 2 * pw * t:2 * pw * (t + 1)]),
            (dy_t, lambda: hidden[:, t * pw:(t + 1) * pw]),
        ])

    def feed_third(t):
        def body(i, carry):
            feed(t, rows(i, 2 * block))
            return carry

        lax.fori_loop(0, n // 2, body, 0)

    lax.fori_loop(0, n // 2, feed_arriving, 0)
    gather_stepped(second, 2)
    for t in range(1, thirds):
        weight_forward(2 + 2 * t)
        weight_forward(3 + 2 * t)
        third_grad(t - 1)
        weight_receive(2 + 2 * t, False)
        weight_receive(3 + 2 * t, False)
        hand_arrive(3 + 2 * t)
        if t < thirds - 1:
            feed_third(t)
    sum_start(
        1, d_gu, lambda left: dot_nt(left, w_gu[...]),
        lambda place: feed(thirds - 1, rows(place, 2 * block)))
    third_grad(thirds - 1)
    grad_join(0)
    grad_join(1)
    d_second = sum_finish(1)

    def norm_back(value, gain, grad):
        inv = lax.rsqrt(jnp.mean(value * value, -1, keepdims=True) + epsilon)
        weighted = grad * gain
        inner = jnp.mean(weighted * value, -1, keepdims=True)
        result = inv * weighted - value * (inv * inv * inv * inner)
        return result, jnp.sum(grad * value * inv, 0, keepdims=True)

    gain_own[...] = jnp.zeros_like(gain_own)
    part, gain_own[1:2, :] = norm_back(middle[...], fg_ref[...], d_second)
    d_mid = dy_ref[...].astype(f32) + part
    d_middle[...] = d_mid
    dmid[rows(c, block)] = d_mid.astype(bf16)
    gather_start(dmid, 3)

    dk_acc[...] = jnp.zeros_like(dk_acc)
    dv_acc[...] = jnp.zeros_like(dv_acc)

    def attend_back_block(i, d_mix):
        at = rows(i, block)
        d_mix_t = jnp.concatenate([d_mix[h * head:(h + 1) * head] for h in range(group)], 1)
        d_mix_t = (d_mix_t.astype(bf16).astype(f32) * sums[i]).astype(bf16)
        delta = jnp.sum(d_mix_t.astype(f32) * mixed_t[i], 0, keepdims=True)
        weight = probs[i]
        d_prob = dot(values[...], d_mix_t)
        d_score = (weight.astype(f32) * (d_prob - delta)).astype(bf16)
        d_query = dot(keys_t[...], d_score) * scale
        gained = jnp.zeros((1, head), f32)
        for h in range(group):
            grad = turn_back(d_query[:, h * block:(h + 1) * block].T, at)
            part, gain_part = norm_back(raw[at, h * head:(h + 1) * head], qg_ref[...], grad)
            d_qkv[at, h * head:(h + 1) * head] = part.astype(bf16)
            gained = gained + gain_part
        return dot(weight, d_mix_t.T), dot(d_score, stack(queries, at)), gained

    def attend_back(slot, q_sum):
        gather_step(dmid, 3, slot)
        at = rows(chip(slot), 2 * block)
        d_mix = dot_nt(w_out[...], dmid[at])
        dmid_t[:, at] = dmid[at].T
        dv_one, dk_one, gain_one = attend_back_block(2 * chip(slot), d_mix[:, :block])
        dv_two, dk_two, gain_two = attend_back_block(2 * chip(slot) + 1, d_mix[:, block:])
        dv_acc[...] += dv_one + dv_two
        dk_acc[...] += dk_one + dk_two
        return q_sum + gain_one + gain_two

    zero = jnp.zeros((1, head), f32)
    gain_own[2:3, 0:head] = lax.fori_loop(0, n // 2, attend_back, zero)
    gather_stepped(dmid, 3)
    weight_grad(3, [(dmid_t, lambda: mixed_low[...])])
    grad_join(2)

    def project_back(i, k_sum):
        at = rows(i, 2 * block)
        grad = turn_back(dk_acc[at] * (1.0 / log2e), at)
        part, gain_part = norm_back(raw[at, qw:qw + kw], kg_ref[...], grad)
        d_qkv[at, qw:qw + kw] = part.astype(bf16)
        d_qkv[at, qw + kw:] = dv_acc[at].astype(bf16)
        return k_sum + gain_part

    gain_own[3:4, 0:head] = lax.fori_loop(0, n // 2, project_back, zero)

    weight_grad(4, [(first_t, lambda: d_qkv[...])])
    grad_join(3)
    drain(in_plane)
    sum_start(3, d_qkv, lambda left: dot_nt(left, w_qkv[...]))
    grad_join(4)
    sum_start(2, hidden, lambda left: dot(left, w_down[...]))
    for m in range(4):
        hand_out(m)
    x_part, gain_own[0:1, :] = norm_back(x_ref[...].astype(f32), ag_ref[...], sum_finish(3))
    dx_ref[...] = d_middle[...] + x_part

    def gain_plane_copy(j):
        return remote(gain_own, gain_plane.at[c], gp_send.at[j], gp_recv.at[j], partner(j), z)

    def gain_copy(d):
        return remote(gain_all.at[z], gain_all.at[z], gz_send.at[d], gz_recv.at[d], c, lax.rem(z + d, planes))

    for j in range(1, n):
        launch(in_plane, lambda j=j: gain_plane_copy(j))
    gain_plane[c] = gain_own[...]
    out_ref[...] = (middle[...] + sum_finish(2)).astype(bf16)
    for j in range(1, n):
        gain_plane_copy(j).wait_recv()
    total = gain_plane[0]
    for i in range(1, n):
        total = total + gain_plane[i]
    gain_all[z] = total
    for d in range(1, planes):
        launch(along, lambda d=d: gain_copy(d))
    for d in range(1, planes):
        origin = gain_all.at[lax.rem(z + planes - d, planes)]
        remote(origin, origin, gz_send.at[d], gz_recv.at[d], c, z).wait_recv()
    total = gain_all[0]
    for i in range(1, planes):
        total = total + gain_all[i]
    gains_ref[...] = total

    hand_out(4)
    for m in range(5):
        hand_receive(m)
    drain(in_plane)
    drain(along)


def finish_kernel(
    n, head, out_in, dx_in, gains_in, got_a, got_b, got_c, got_out, got_qkv,
    out_ref, dx_ref, ag_ref, q_ref, k_ref, v_ref, qg_ref, kg_ref, o_ref, fg_ref, g_ref, u_ref, d_ref,
):
    out_ref[...] = out_in[...]
    dx_ref[...] = dx_in[...]
    ag_ref[...] = gains_in[0:1, :]
    fg_ref[...] = gains_in[1:2, :]
    qg_ref[...] = gains_in[2:3, 0:head]
    kg_ref[...] = gains_in[3:4, 0:head]
    qw, kw = q_ref.shape[1] // n, k_ref.shape[1] // n
    pw = got_a.shape[2] // 3
    thirds = (got_a, got_b, got_c)
    for i in range(n):
        q_ref[:, i * qw:(i + 1) * qw] = got_qkv[i, :, 0:qw].astype(f32)
        k_ref[:, i * kw:(i + 1) * kw] = got_qkv[i, :, qw:qw + kw].astype(f32)
        v_ref[:, i * kw:(i + 1) * kw] = got_qkv[i, :, qw + kw:].astype(f32)
        o_ref[:, i * qw:(i + 1) * qw] = got_out[i].astype(f32)
        for t, got in enumerate(thirds):
            at = (i * len(thirds) + t) * pw
            g_ref[:, at:at + pw] = got[i, :, 0:pw].astype(f32)
            u_ref[:, at:at + pw] = got[i, :, pw:2 * pw].astype(f32)
            d_ref[:, at:at + pw] = got[i, :, 2 * pw:].astype(f32)


def plane_device(
    layer_input,
    token_positions,
    attention_gain,
    query_weight,
    key_matrix,
    value_matrix,
    query_gain,
    key_norm_gain,
    output_weight,
    feedforward_gain,
    gate_weight,
    up_weight,
    down_weight,
    out_cotangent,
):
    n = lax.axis_size("ctx")
    planes = lax.axis_size("fsdp")
    block, width = layer_input.shape[1:]
    length = token_positions.shape[1]
    head = query_gain.shape[0]
    qw = query_weight.shape[1] // n
    kw = key_matrix.shape[1] // n
    fw = gate_weight.shape[1] // n
    group = qw // head
    per = block // planes
    half = head // 2
    inverse = np.power(rope_base, -np.arange(half) * 2.0 / head).astype(np.float32)
    inverse = jnp.asarray(np.concatenate([inverse, inverse])[None])
    vmem = pl.BlockSpec(memory_space=pltpu.VMEM)
    hbm = pl.BlockSpec(memory_space=pl.ANY)
    dma = pltpu.SemaphoreType.DMA
    sizes = (fw, fw, fw, qw, qw + 2 * kw)
    low = lambda *shape: pltpu.VMEM(shape, bf16)
    wide = lambda *shape: pltpu.VMEM(shape, f32)
    scratch = [
        low(width, qw + 2 * kw), low(width, 2 * fw), low(qw, width), low(fw, width),
        low(planes * (output_weight.shape[0] // n), width), low(3, planes * 32, width),
        low(length, width), low(length, width), low(length, width),
        low(width, length), low(width, length), low(width, length), low(width, length),
        wide(length, head), wide(length, head), wide(length, head),
        wide(length, qw + kw), low(length, qw), low(length, kw), low(length, kw),
        low(kw, length), low(kw, length), low(n, length, group * block), wide(n, 1, group * block), wide(n, head, group * block), low(length, qw),
        low(length, fw), low(length, 2 * fw), low(length, qw + 2 * kw),
        wide(length, kw), wide(length, kw),
    ]
    scratch += [low(planes, n, per, size) for size in sizes]
    scratch += [low(planes, n, per, size) for size in sizes]
    scratch += [low(n, per, size) for size in sizes]
    scratch += [low(2, 4, block, width) for _ in range(4)] + [wide(2, block, width), wide(2, block, width)]
    scratch += [
        wide(block, width), wide(block, width), wide(8, width), wide(n, 8, width), wide(planes, 8, width),
        dma((13,)), dma((8, 6)), dma((8, planes)), dma((4, 7)), dma((4, 4)),
        dma((4, n)), dma((4, n)), dma((4, 4)), dma((4, 4)), dma((4, 4)), dma((4, 4)),
        dma((5, planes)), dma((5, planes)), dma((5,)), dma((5, n)), dma((5, n)), dma((n,)), dma((n,)),
        dma((planes,)), dma((planes,)),
    ]
    shapes = [
        jax.ShapeDtypeStruct((block, width), bf16),
        jax.ShapeDtypeStruct((block, width), f32),
        jax.ShapeDtypeStruct((8, width), f32),
    ] + [jax.ShapeDtypeStruct((n, per, size), bf16) for size in sizes]
    results = pl.pallas_call(
        functools.partial(layer_kernel, n, planes, block, head, group, fw),
        out_shape=shapes,
        in_specs=[vmem] * 8 + [hbm] * 7,
        out_specs=[vmem] * len(shapes),
        scratch_shapes=scratch,
        compiler_params=pltpu.CompilerParams(
            collective_id=0, has_side_effects=True, vmem_limit_bytes=60 * 1024 * 1024),
    )(
        layer_input[0], out_cotangent[0], token_positions, inverse,
        attention_gain[None], feedforward_gain[None], query_gain[None], key_norm_gain[None],
        query_weight, key_matrix, value_matrix, output_weight, gate_weight, up_weight, down_weight,
    )
    plain = lambda rows, columns, kind=f32: jax.ShapeDtypeStruct((rows, columns), kind)
    finals = [
        plain(block, width, bf16), plain(block, width), plain(1, width),
        plain(per, n * qw), plain(per, n * kw), plain(per, n * kw), plain(1, head), plain(1, head),
        plain(per, n * qw), plain(1, width), plain(per, n * fw), plain(per, n * fw), plain(per, n * fw),
    ]
    done = pl.pallas_call(
        functools.partial(finish_kernel, n, head),
        out_shape=finals,
        in_specs=[vmem] * len(shapes),
        out_specs=[vmem] * len(finals),
    )(*results)
    out, dx, ag, q, k, v, qg, kg, o, fg, g, u, d = done
    return out[None], dx[None], ag[0], q, k, v, qg[0], kg[0], o.T, fg[0], g, u, d.T


def solution(mesh):
    in_specs = (
        P("fsdp", "ctx", None),
        P("fsdp", None),
        P(),
        P("fsdp", None),
        P("fsdp", None),
        P("fsdp", None),
        P(),
        P(),
        P("fsdp", None),
        P(),
        P("fsdp", None),
        P("fsdp", None),
        P("fsdp", None),
        P("fsdp", "ctx", None),
    )
    out_specs = (
        P("fsdp", "ctx", None),
        P("fsdp", "ctx", None),
        P(),
        P(("ctx", "fsdp"), None),
        P(("ctx", "fsdp"), None),
        P(("ctx", "fsdp"), None),
        P(),
        P(),
        P(None, ("ctx", "fsdp")),
        P(),
        P(("ctx", "fsdp"), None),
        P(("ctx", "fsdp"), None),
        P(None, ("ctx", "fsdp")),
    )

    def run(*arguments):
        n, planes = mesh.shape["ctx"], mesh.shape["fsdp"]
        key_heads = arguments[4].shape[1] // arguments[6].shape[0]
        whole_heads = n == 8 and planes == 4 and key_heads == n
        return jax.shard_map(
            plane_device if whole_heads else on_device,
            mesh=mesh, in_specs=in_specs, out_specs=out_specs, check_vma=False,
        )(*arguments)

    return run
```

```python
import functools

import jax
import jax.numpy as jnp
import numpy as np
from jax import lax
from jax.experimental import pallas as pl
from jax.experimental.pallas import tpu as pltpu
from jax.sharding import PartitionSpec as P

epsilon = 1e-06
rope_base = 1000000.0
masked_score = -1e30


def from_behind(block, axis, distance):
    devices = range(lax.axis_size(axis))
    route = [((i - distance) % len(devices), i) for i in devices]
    return lax.ppermute(block, axis, route)


def rotate(value_rows):
    half = value_rows.shape[-1] // 2
    return jnp.concatenate([-value_rows[..., half:], value_rows[..., :half]], -1)


def rotate_back(value_rows):
    half = value_rows.shape[-1] // 2
    return jnp.concatenate([value_rows[..., half:], -value_rows[..., :half]], -1)


def rope_tables(token_offsets, head_size):
    half = head_size // 2
    inverse = rope_base ** (-(jnp.arange(half).astype(jnp.float32) * 2.0) / head_size)
    angles = token_offsets.astype(jnp.float32)[:, None] * inverse[None, :]
    cosine = jnp.cos(angles)
    sine = jnp.sin(angles)
    return (jnp.concatenate([cosine, cosine], -1), jnp.concatenate([sine, sine], -1))


def norm_scale(value_rows):
    return lax.rsqrt(jnp.mean(value_rows * value_rows, -1, keepdims=True) + epsilon)


def norm_back(value_rows, scale, gain, grad):
    weighted = grad * gain
    inner = jnp.mean(weighted * value_rows, -1, keepdims=True)
    result = scale * weighted - value_rows * scale * scale * scale * inner
    gain_part = jnp.sum((grad * value_rows * scale).reshape(-1, gain.shape[0]), 0)
    return (result, gain_part)


def row_products(left, pieces):
    return tuple((jnp.dot(left, piece, preferred_element_type=jnp.float32) for piece in pieces))


def column_products(rights, pieces):
    total = jnp.einsum("tc,rc->tr", rights[0], pieces[0], preferred_element_type=jnp.float32)
    for right, piece in zip(rights[1:], pieces[1:]):
        total = total + jnp.einsum("tc,rc->tr", right, piece, preferred_element_type=jnp.float32)
    return total


def on_device(
    layer_input,
    token_positions,
    attention_gain,
    query_weight,
    key_matrix,
    value_matrix,
    query_gain,
    key_norm_gain,
    output_weight,
    feedforward_gain,
    gate_weight,
    up_weight,
    down_weight,
    out_cotangent,
):
    hidden_in = layer_input[0].astype(jnp.float32)
    count = hidden_in.shape[0]
    head_size = query_gain.shape[0]
    query_width = query_weight.shape[1]
    key_width = key_matrix.shape[1]
    inner_width = gate_weight.shape[1]
    heads = query_width // head_size
    key_heads = key_width // head_size
    group = heads // key_heads
    scale = head_size ** (-0.5)
    cycles = lax.axis_size("ctx")
    own_index = lax.axis_index("ctx")
    sequence_pos = token_positions[0]
    token_offsets = lax.dynamic_slice_in_dim(sequence_pos, own_index * count, count)
    cosine, sine = rope_tables(token_offsets, head_size)
    cosine = cosine[:, None, :]
    sine = sine[:, None, :]
    first_scale = norm_scale(hidden_in)
    first = (hidden_in * first_scale * attention_gain).astype(jnp.bfloat16)
    query_raw, key_unnormed, value_unnormed = row_products(
        first,
        (
            lax.all_gather(query_weight, "fsdp", axis=0, tiled=True),
            lax.all_gather(key_matrix, "fsdp", axis=0, tiled=True),
            lax.all_gather(value_matrix, "fsdp", axis=0, tiled=True),
        ),
    )
    query_heads = query_raw.reshape(count, heads, head_size)
    query_scale = norm_scale(query_heads)
    query_normed = query_heads * query_scale * query_gain
    query_rot = query_normed * cosine + rotate(query_normed) * sine
    query_grouped = (
        query_rot.reshape(count, key_heads, group, head_size)
        .transpose(1, 2, 0, 3)
        .astype(jnp.bfloat16)
    )
    key_heads_raw = key_unnormed.reshape(count, key_heads, head_size)
    key_scale = norm_scale(key_heads_raw)
    key_normed = key_heads_raw * key_scale * key_norm_gain
    key_low = (
        (key_normed * cosine + rotate(key_normed) * sine)
        .reshape(count, key_width)
        .astype(jnp.bfloat16)
    )
    value_low = value_unnormed.astype(jnp.bfloat16)
    rowmax = jnp.full((key_heads, group, count), masked_score, jnp.float32)
    keys_piece = lax.all_gather(key_low, "ctx", axis=0, tiled=True).reshape(
        -1, key_heads, head_size
    )
    values_piece = lax.all_gather(value_low, "ctx", axis=0, tiled=True).reshape(
        -1, key_heads, head_size
    )
    key_pos = sequence_pos
    allowed = token_offsets[:, None] >= key_pos[None, :]
    scores = (
        jnp.einsum("kgtd,skd->kgts", query_grouped, keys_piece, preferred_element_type=jnp.float32)
        * scale
    )
    scores = jnp.where(allowed, scores, masked_score)
    newmax = jnp.maximum(rowmax, jnp.max(scores, -1))
    weights = jnp.where(allowed, jnp.exp(scores - newmax[..., None]), 0.0)
    accum = jnp.einsum(
        "kgts,skd->kgtd",
        weights.astype(jnp.bfloat16),
        values_piece,
        preferred_element_type=jnp.float32,
    )
    rowsum = jnp.sum(weights, -1)
    accum, rowmax, rowsum = (accum, newmax, rowsum)
    normalized = accum / rowsum[..., None]
    logsum = rowmax + jnp.log(rowsum)
    attention_low = (
        normalized.transpose(2, 0, 1, 3).reshape(count, query_width).astype(jnp.bfloat16)
    )
    output_whole = lax.all_gather(output_weight, "fsdp", axis=0, tiled=True)
    branch_out = jnp.dot(attention_low, output_whole, preferred_element_type=jnp.float32)
    middle = hidden_in + branch_out
    second_scale = norm_scale(middle)
    second = (middle * second_scale * feedforward_gain).astype(jnp.bfloat16)
    gate, up = row_products(
        second,
        (
            lax.all_gather(gate_weight, "fsdp", axis=0, tiled=True),
            lax.all_gather(up_weight, "fsdp", axis=0, tiled=True),
        ),
    )
    sigmoid_gate = jax.nn.sigmoid(gate)
    silu_gate = gate * sigmoid_gate
    hidden_low = (silu_gate * up).astype(jnp.bfloat16)
    (down_out,) = row_products(
        hidden_low, (lax.all_gather(down_weight, "fsdp", axis=0, tiled=True),)
    )
    layer_output = (middle + down_out).astype(jnp.bfloat16)[None]
    cotangent = out_cotangent[0]
    hidden_grad = column_products(
        (cotangent,), lax.all_gather((down_weight,), "fsdp", axis=0, tiled=True)
    )
    up_low = (hidden_grad * silu_gate).astype(jnp.bfloat16)
    gate_low = (hidden_grad * up * sigmoid_gate * (1.0 + gate * (1.0 - sigmoid_gate))).astype(
        jnp.bfloat16
    )
    second_grad = column_products(
        (gate_low, up_low), lax.all_gather((gate_weight, up_weight), "fsdp", axis=0, tiled=True)
    )
    middle_part, feedforward_part = norm_back(middle, second_scale, feedforward_gain, second_grad)
    middle_grad = cotangent.astype(jnp.float32) + middle_part
    middle_low = middle_grad.astype(jnp.bfloat16)
    attention_grad = jnp.einsum(
        "tc,rc->tr", middle_low, output_whole, preferred_element_type=jnp.float32
    )
    attention_grad_low = attention_grad.astype(jnp.bfloat16)
    mixed_grad = attention_grad_low.reshape(count, key_heads, group, head_size).transpose(
        1, 2, 0, 3
    )
    delta = jnp.sum(mixed_grad.astype(jnp.float32) * normalized, -1)

    def cycle_step(index, carry):
        keys_held, values_held, key_acc, value_acc, query_acc = carry
        anchor = (own_index - index) % cycles
        key_pos = lax.dynamic_slice_in_dim(sequence_pos, anchor * count, count)
        keys_piece = keys_held.astype(jnp.bfloat16).reshape(count, key_heads, head_size)
        values_piece = values_held.astype(jnp.bfloat16).reshape(count, key_heads, head_size)
        allowed = token_offsets[:, None] >= key_pos[None, :]
        scores = (
            jnp.einsum(
                "kgtd,skd->kgts", query_grouped, keys_piece, preferred_element_type=jnp.float32
            )
            * scale
        )
        probs = jnp.where(allowed, jnp.exp(scores - logsum[..., None]), 0.0)
        value_acc = value_acc + jnp.einsum(
            "kgts,kgtd->skd",
            probs.astype(jnp.bfloat16),
            mixed_grad,
            preferred_element_type=jnp.float32,
        ).reshape(count, key_width)
        prob_grad = jnp.einsum(
            "kgtd,skd->kgts", mixed_grad, values_piece, preferred_element_type=jnp.float32
        )
        score_grad = (probs * (prob_grad - delta[..., None])).astype(jnp.bfloat16)
        query_acc = (
            query_acc
            + jnp.einsum(
                "kgts,skd->kgtd", score_grad, keys_piece, preferred_element_type=jnp.float32
            )
            * scale
        )
        key_acc = (
            key_acc
            + jnp.einsum(
                "kgts,kgtd->skd", score_grad, query_grouped, preferred_element_type=jnp.float32
            ).reshape(count, key_width)
            * scale
        )
        moved = (
            from_behind(keys_held.astype(jnp.bfloat16), "ctx", 1).astype(keys_held.dtype),
            from_behind(values_held.astype(jnp.bfloat16), "ctx", 1).astype(values_held.dtype),
            from_behind(key_acc.astype(jnp.bfloat16), "ctx", 1).astype(key_acc.dtype),
            from_behind(value_acc.astype(jnp.bfloat16), "ctx", 1).astype(value_acc.dtype),
        )
        return (moved[0], moved[1], moved[2], moved[3], query_acc)

    start_cycle = (
        key_low.astype(jnp.float32),
        value_low.astype(jnp.float32),
        jnp.zeros((count, key_width), jnp.float32),
        jnp.zeros((count, key_width), jnp.float32),
        jnp.zeros((key_heads, group, count, head_size), jnp.float32),
    )
    cycle_done = lax.fori_loop(0, cycles, cycle_step, start_cycle)
    key_acc = cycle_done[2]
    value_acc = cycle_done[3]
    query_acc = cycle_done[4]
    query_rot_grad = query_acc.transpose(2, 0, 1, 3).reshape(count, heads, head_size)
    query_normed_grad = query_rot_grad * cosine + rotate_back(query_rot_grad * sine)
    query_heads_grad, query_part = norm_back(
        query_heads, query_scale, query_gain, query_normed_grad
    )
    query_low_grad = query_heads_grad.reshape(count, query_width).astype(jnp.bfloat16)
    key_rot_grad = key_acc.reshape(count, key_heads, head_size)
    key_normed_grad = key_rot_grad * cosine + rotate_back(key_rot_grad * sine)
    key_heads_grad, key_part = norm_back(key_heads_raw, key_scale, key_norm_gain, key_normed_grad)
    key_low_grad = key_heads_grad.reshape(count, key_width).astype(jnp.bfloat16)
    value_low_grad = value_acc.astype(jnp.bfloat16)
    first_grad = column_products(
        (query_low_grad, key_low_grad, value_low_grad),
        lax.all_gather((query_weight, key_matrix, value_matrix), "fsdp", axis=0, tiled=True),
    )
    input_part, attention_part = norm_back(hidden_in, first_scale, attention_gain, first_grad)
    input_gradient = (middle_grad + input_part)[None]
    rights_first = jnp.concatenate([query_low_grad, key_low_grad, value_low_grad], 1)
    rights_second = jnp.concatenate([gate_low, up_low], 1)
    pairs = (
        (first, rights_first),
        (second, rights_second),
        (middle_low, attention_low),
        (cotangent, hidden_low),
    )
    parts = []
    for left, right in pairs:
        parts.append(jnp.einsum("tr,tc->rc", left, right, preferred_element_type=jnp.float32))
    sums = lax.psum_scatter(
        jnp.concatenate(parts, 1), ("ctx", "fsdp"), scatter_dimension=0, tiled=True
    )
    edges = [0, query_width, query_width + key_width, query_width + 2 * key_width]
    edges = edges + [edges[3] + inner_width, edges[3] + 2 * inner_width]
    edges = edges + [edges[5] + query_width, edges[5] + query_width + inner_width]
    query_gradient = sums[:, edges[0] : edges[1]]
    key_gradient = sums[:, edges[1] : edges[2]]
    value_gradient = sums[:, edges[2] : edges[3]]
    gate_gradient = sums[:, edges[3] : edges[4]]
    up_gradient = sums[:, edges[4] : edges[5]]
    output_gradient = sums[:, edges[5] : edges[6]].T
    down_gradient = sums[:, edges[6] : edges[7]].T
    attention_total, query_total, key_total, feedforward_total = lax.psum(
        (attention_part, query_part, key_part, feedforward_part), ("ctx", "fsdp")
    )
    return (
        layer_output,
        input_gradient,
        attention_total,
        query_gradient,
        key_gradient,
        value_gradient,
        query_total,
        key_total,
        output_gradient,
        feedforward_total,
        gate_gradient,
        up_gradient,
        down_gradient,
    )


MESH = pl.DeviceIdType.MESH
f32 = jnp.float32
bf16 = jnp.bfloat16


def dot(left, right):
    return jnp.dot(left, right, preferred_element_type=f32)


def dot_nt(left, right):
    return lax.dot_general(left, right, (((1,), (1,)), ((), ())), preferred_element_type=f32)


def dot_tn(left, right):
    return lax.dot_general(left, right, (((0,), (0,)), ((), ())), preferred_element_type=f32)


def layer_kernel(
    n, planes, block, head, group, fw,
    x_ref, dy_ref, pos_row, inverse_ref, ag_ref, fg_ref, qg_ref, kg_ref,
    wq, wk, wv, wo, wg, wu, wd,
    out_ref, dx_ref, gains_ref, got_a, got_b, got_c, got_out, got_qkv,
    w_qkv, w_gu, w_out, w_down, t_out, t_down,
    first, dy_all, second, first_t, dy_t, second_t, dmid_t,
    positions, cosine, sine,
    raw, queries, keys, values, keys_t, values_t, probs, sums, mixed_t, mixed_low,
    hidden, d_gu, d_qkv, dk_acc, dv_acc,
    stage_a, stage_b, stage_c, stage_out, stage_qkv,
    land_a, land_b, land_c, land_out, land_qkv,
    own_a, own_b, own_c, own_out, own_qkv,
    rs_sa, rs_ra, rs_sb, rs_rb, rs_kept, rs_acc,
    middle, d_middle, gain_own, gain_plane, gain_all,
    local_sem, wz_send, wz_recv, hand_send, hand_recv,
    ag_send, ag_recv, ra_send, ra_recv, rb_send, rb_recv,
    zr_send, zr_recv, aa_send, aa_recv, gp_send, gp_recv, gz_send, gz_recv,
):
    c = lax.axis_index("ctx")
    z = lax.axis_index("fsdp")
    dmid = first
    cy, cx, ck = lax.div(c, 4), lax.rem(lax.div(c, 2), 2), lax.rem(c, 2)
    ci = lax.rem(c, 4)
    sign = 1 - 2 * ck
    qw, kw = group * head, head
    pw = 128
    thirds = fw // pw
    piece = pw // 4
    width = x_ref.shape[1]
    scale = head ** (-0.5)
    log2e = 1.4426950408889634
    gots = (got_a, got_b, got_c, got_out, got_qkv)
    stages = (stage_a, stage_b, stage_c, stage_out, stage_qkv)
    lands = (land_a, land_b, land_c, land_out, land_qkv)
    owns = (own_a, own_b, own_c, own_out, own_qkv)

    def partner(j):
        y = lax.rem(cy + lax.div(j, 4), 2)
        x = lax.rem(cx + lax.rem(lax.div(j, 2), 2), 2)
        k = lax.rem(ck + lax.rem(j, 2), 2)
        return y * 4 + x * 2 + k

    def chip(slot):
        return lax.rem(cy + lax.div(slot, 2), 2) * 2 + lax.rem(cx + lax.rem(slot, 2), 2)

    def rows(start, size):
        return pl.ds(pl.multiple_of(start * size, size), size)

    def remote(src, dst, send, recv, ctx, plane):
        return pltpu.make_async_remote_copy(
            src_ref=src, dst_ref=dst, send_sem=send, recv_sem=recv,
            device_id={"ctx": ctx, "fsdp": plane}, device_id_type=MESH,
        )

    in_plane, along = [], []

    def launch(started, copy, when=None):
        if when is None:
            copy().start()
        else:
            pl.when(when)(lambda: copy().start())
        started.append((copy, when))

    def drain(started):
        for copy, when in started:
            if when is None:
                copy().wait_send()
            else:
                pl.when(when)(lambda copy=copy: copy().wait_send())
        started.clear()

    own_rows = wq.shape[0]
    out_rows = wo.shape[0] // n

    def own_slices():
        mine = rows(z, own_rows)
        pairs = [
            (wq.at[:, rows(c, qw)], w_qkv.at[mine, 0:qw]),
            (wk.at[:, rows(c, kw)], w_qkv.at[mine, qw:qw + kw]),
            (wv.at[:, rows(c, kw)], w_qkv.at[mine, qw + kw:qw + 2 * kw]),
            (wo.at[rows(c, out_rows)], t_out.at[rows(z, out_rows)]),
        ]
        for t in range(thirds):
            at = 2 * pw * t
            pairs.append((wg.at[:, rows(c * thirds + t, pw)], w_gu.at[mine, at:at + pw]))
            pairs.append((wu.at[:, rows(c * thirds + t, pw)], w_gu.at[mine, at + pw:at + 2 * pw]))
            pairs.append((wd.at[rows((cy * thirds + t) * 4 + ci, piece)], t_down.at[t, rows(z, piece)]))
        return pairs

    local = [pltpu.make_async_copy(src, dst, local_sem.at[i]) for i, (src, dst) in enumerate(own_slices())]
    for copy in local:
        copy.start()

    barrier = pltpu.get_barrier_semaphore()
    for j in range(1, n):
        pl.semaphore_signal(barrier, inc=1, device_id={"ctx": partner(j), "fsdp": z}, device_id_type=MESH)
    for d in range(1, planes):
        pl.semaphore_signal(
            barrier, inc=1, device_id={"ctx": c, "fsdp": lax.rem(z + d, planes)}, device_id_type=MESH)
    x = x_ref[...].astype(f32)
    x_scale = lax.rsqrt(jnp.mean(x * x, -1, keepdims=True) + epsilon)
    first[rows(c, block)] = (x * x_scale * ag_ref[...]).astype(bf16)
    dy_all[rows(c, block)] = dy_ref[...]
    for copy in local[:3]:
        copy.wait()
    pl.semaphore_wait(barrier, n + planes - 2)

    def inside(t):
        return jnp.logical_and(t >= 0, t < planes)

    weights = [
        (lambda o: w_qkv.at[rows(o, own_rows)], None),
        (lambda o: t_out.at[rows(o, out_rows)], 0),
    ]
    for t in range(thirds):
        weights.append((lambda o, t=t: w_gu.at[rows(o, own_rows), 2 * pw * t:2 * pw * (t + 1)], None))
        weights.append((lambda o, t=t: t_down.at[t, rows(o, piece)], 1 + t))

    def weight_copy(w, slot, origin, target):
        part = weights[w][0](origin)
        return remote(part, part, wz_send.at[w, slot], wz_recv.at[w, origin], c, target)

    def weight_start(w):
        for slot, k in enumerate((1, -1, 2, -2)):
            d = sign * k
            launch(along, lambda slot=slot, d=d: weight_copy(w, slot, z, z + d), inside(z + d))
        if weights[w][1] is not None:
            hand_over(w, z, 0, None)

    def hand_target(h):
        if h == 0:
            return lambda i: w_out.at[rows(i, out_rows)]
        return lambda i: w_down.at[rows((h - 1) * 4 + i, piece)]

    def hand_copy(w, origin, slot):
        h = weights[w][1]
        return remote(
            weights[w][0](origin), hand_target(h)(ci), hand_send.at[h, slot], hand_recv.at[h, ci], 2 * origin + cy, z)

    def hand_over(w, origin, slot, valid):
        away = 2 * origin + cy != c
        here = jnp.logical_not(away)
        if valid is not None:
            away, here = jnp.logical_and(valid, away), jnp.logical_and(valid, here)
        launch(in_plane, lambda: hand_copy(w, origin, slot), away)

        @pl.when(here)
        def _():
            hand_target(weights[w][1])(ci)[...] = weights[w][0](origin)[...]

    def hand_arrive(w):
        h = weights[w][1]
        for i in range(4):
            @pl.when(4 * ck + i != c)
            def _(i=i):
                part = hand_target(h)(i)
                remote(part, part, hand_send.at[h, 0], hand_recv.at[h, i], c, z).wait_recv()

    def weight_arrivals():
        for d in range(1, planes):
            for side, way in enumerate((1, -1)):
                origin = z - way * d
                passed = jnp.logical_and(inside(origin), inside(z + way)) if 1 < d < planes - 1 else None
                yield d, side, way, origin, passed

    def weight_forward(w):
        for d, side, way, origin, passed in weight_arrivals():
            if passed is not None:
                pl.when(passed)(lambda origin=origin: weight_copy(w, 0, origin, z).wait_recv())
                launch(
                    along,
                    lambda d=d, side=side, way=way, origin=origin: weight_copy(
                        w, 2 * d + side, origin, z + way),
                    passed)

    def weight_receive(w, forward=True):
        if forward:
            weight_forward(w)
        for d, side, way, origin, passed in weight_arrivals():
            valid = inside(origin)
            here = valid if passed is None else jnp.logical_and(valid, jnp.logical_not(passed))
            pl.when(here)(lambda origin=origin: weight_copy(w, 0, origin, z).wait_recv())
            if weights[w][1] is not None:
                hand_over(w, origin, 2 * d - 1 + side, valid)

    def gather_copy(buf, g, j, send, origin, target):
        part = buf.at[rows(origin, block)]
        return remote(part, part, ag_send.at[g, send], ag_recv.at[g, j], target, z)

    def gather_start(buf, g):
        for j in (1, 2 + 2 * ck, 4 - 2 * ck, 6):
            launch(in_plane, lambda j=j: gather_copy(buf, g, j, j, c, partner(j)))

    def gather_forward(buf, g, j):
        return gather_copy(buf, g, j + 1, j + 1, partner(j), partner(1))

    def gather_finish(buf, g):
        for j in (2, 4, 6):
            gather_copy(buf, g, j, j, partner(j), c).wait_recv()
            launch(in_plane, lambda j=j: gather_forward(buf, g, j))
        for j in (1, 3, 5, 7):
            gather_copy(buf, g, j, j, partner(j), c).wait_recv()

    def gather_step(buf, g, slot):
        def arrive(j):
            gather_copy(buf, g, j, j, partner(j), c).wait_recv()
            gather_forward(buf, g, j).start()

        @pl.when(slot == 1)
        def _():
            arrive(2)
            arrive(4)

        @pl.when(slot == 3)
        def _():
            arrive(6)

        gather_copy(buf, g, 2 * slot + 1, 0, partner(2 * slot + 1), c).wait_recv()

    def gather_stepped(buf, g):
        for j in (2, 4, 6):
            in_plane.append((lambda j=j: gather_forward(buf, g, j), None))

    def sum_pair_copy(s, slot):
        return remote(rs_sa.at[s % 2, slot], rs_ra.at[s % 2, slot], ra_send.at[s, slot], ra_recv.at[s, slot], partner(1), z)

    def sum_chip_copy(s, slot):
        return remote(
            rs_sb.at[s % 2, slot], rs_rb.at[s % 2, slot], rb_send.at[s, slot], rb_recv.at[s, slot], partner(2 * slot), z)

    def sum_slot(p):
        return jnp.where(p == 0, 3, jnp.where(p == 1, 2 - ck, jnp.where(p == 2, 1 + ck, 0)))

    def sum_start(s, left, partial, prepare=None, ready=None):
        if prepare is not None:
            prepare(chip(sum_slot(0)))
        if ready is not None:
            ready()

        def body(p, carry):
            slot = sum_slot(p)
            at = [rows(partner(2 * slot + 1), block), rows(partner(2 * slot), block)]
            both = partial(jnp.concatenate([left[i] for i in at], 0))
            rs_sa[s % 2, slot] = both[:block].astype(bf16)
            sum_pair_copy(s, slot).start()
            rs_kept[lax.rem(p, 2)] = both[block:]
            if prepare is not None:
                @pl.when(p < 3)
                def _():
                    prepare(chip(sum_slot(p + 1)))

            @pl.when(p > 0)
            def _():
                before = sum_slot(p - 1)
                sum_pair_copy(s, before).wait_recv()
                rs_sb[s % 2, before] = (
                    rs_kept[lax.rem(p + 1, 2)] + rs_ra[s % 2, before].astype(f32)).astype(bf16)
                sum_chip_copy(s, before).start()

            return carry

        lax.fori_loop(0, 4, body, 0)
        for slot in range(4):
            in_plane.append((lambda slot=slot: sum_pair_copy(s, slot), None))
            if slot > 0:
                in_plane.append((lambda slot=slot: sum_chip_copy(s, slot), None))
        sum_pair_copy(s, 0).wait_recv()
        rs_acc[s % 2] = rs_kept[1] + rs_ra[s % 2, 0].astype(f32)

    def sum_finish(s):
        total = rs_acc[s % 2]
        for slot in (1, 2, 3):
            sum_chip_copy(s, slot).wait_recv()
            total = total + rs_rb[s % 2, slot].astype(f32)
        return total

    per = block // planes

    def weight_grad(m, parts):
        def body(i, carry):
            at = 0
            for left, right in parts:
                value = right()
                grad = dot(left[rows(i, 2 * block)], value)
                for k in range(2):
                    for t in range(planes):
                        start = k * block + t * per
                        stages[m][t, 2 * i + k, :, at:at + value.shape[1]] = grad[start:start + per].astype(bf16)
                at += value.shape[1]
            return carry

        lax.fori_loop(0, n // 2, body, 0)
        for d in (sign, -sign, 2):
            launch(along, lambda d=d: grad_copy(m, lax.rem(z + d + planes, planes)))

    def grad_slot(target):
        return lax.rem(target - z + planes, planes)

    def grad_copy(m, target):
        return remote(
            stages[m].at[target], lands[m].at[z], zr_send.at[m, grad_slot(target)], zr_recv.at[m, z], c, target)

    def owner_copy(m, j):
        return remote(owns[m].at[partner(j)], gots[m].at[c], aa_send.at[m, j], aa_recv.at[m, j], partner(j), z)

    def hand_out(m):
        for d in range(1, planes):
            origin = lax.rem(z + d, planes)
            part = lands[m].at[origin]
            remote(part, part, zr_send.at[m, 0], zr_recv.at[m, origin], c, z).wait_recv()

        def body(i, carry):
            total = stages[m][z, i].astype(f32)
            for d in range(1, planes):
                total = total + lands[m][lax.rem(z + d, planes), i].astype(f32)
            owns[m][i] = total.astype(bf16)
            return carry

        lax.fori_loop(0, n, body, 0)
        for j in (2 + 2 * ck, 3 + 2 * ck, 4 - 2 * ck, 5 - 2 * ck, 6, 7, 1):
            launch(in_plane, lambda j=j: owner_copy(m, j))
        gots[m][c] = owns[m][c]

    def hand_receive(m):
        for j in range(1, n):
            owner_copy(m, j).wait_recv()

    weight_start(0)
    gather_start(first, 0)
    local[3].wait()
    weight_start(1)

    spread = jnp.broadcast_to(pos_row[...].astype(f32), (head, pos_row.shape[1]))
    positions[...] = spread.T
    side = jnp.where(lax.broadcasted_iota(jnp.int32, (1, head), 1) < head // 2, -1.0, 1.0)

    def table(i, carry):
        at = rows(i, block)
        angle = positions[at] * inverse_ref[...]
        cosine[at] = jnp.cos(angle)
        sine[at] = jnp.sin(angle) * side
        return carry

    gather_finish(first, 0)
    gather_start(dy_all, 1)
    lax.fori_loop(0, n, table, 0)

    def turn_over(src, dst):
        def body(i, carry):
            at = rows(i, block)
            dst[:, at] = src[at].T
            return carry

        lax.fori_loop(0, n, body, 0)

    turn_over(first, first_t)
    for copy in local[4:]:
        copy.wait()
    weight_receive(0)
    weight_start(2)
    weight_start(3)
    gather_finish(dy_all, 1)

    def turn(value, at):
        return value * cosine[at] + pltpu.roll(value, head // 2, 1) * sine[at]

    def turn_back(grad, at):
        return grad * cosine[at] - pltpu.roll(grad, head // 2, 1) * sine[at]

    def project(i, carry):
        at = rows(i, 2 * block)
        result = dot(first[at], w_qkv[...])
        raw[at] = result[:, :qw + kw]
        low_values = result[:, qw + kw:].astype(bf16)
        values[at] = low_values
        values_t[:, at] = low_values.T
        for h in range(group + 1):
            part = result[:, h * head:(h + 1) * head]
            inv = lax.rsqrt(jnp.mean(part * part, -1, keepdims=True) + epsilon)
            gain = qg_ref[...] if h < group else kg_ref[...]
            turned = turn(part * inv * gain, at)
            if h < group:
                queries[at, h * head:(h + 1) * head] = (turned * (scale * log2e)).astype(bf16)
            else:
                low_keys = turned.astype(bf16)
                keys[at] = low_keys
                keys_t[:, at] = low_keys.T
        return carry

    lax.fori_loop(0, n // 2, project, 0)
    turn_over(dy_all, dy_t)

    def stack(ref, at):
        return jnp.concatenate([ref[at, h * head:(h + 1) * head] for h in range(group)], 0)

    def attend_block(i):
        at = rows(i, block)
        scores = dot_nt(keys[...], stack(queries, at))
        allowed = positions[...] <= pos_row[:, at].astype(f32)
        weight = jnp.concatenate(
            [jnp.exp2(jnp.where(allowed, scores[:, h * block:(h + 1) * block], masked_score)) for h in range(group)], 1)
        inv = 1.0 / jnp.sum(weight, 0, keepdims=True)
        low_weight = weight.astype(bf16)
        probs[i] = low_weight
        sums[i] = inv
        result = dot(values_t[...], low_weight) * inv
        mixed_t[i] = result
        for h in range(group):
            mixed_low[at, h * head:(h + 1) * head] = result[:, h * block:(h + 1) * block].T.astype(bf16)

    def attend(place):
        attend_block(2 * place)
        attend_block(2 * place + 1)

    def output_ready():
        weight_receive(1)
        weight_start(4)
        weight_start(5)
        hand_arrive(1)
        drain(in_plane)

    sum_start(0, mixed_low, lambda left: dot(left, w_out[...]), attend, output_ready)
    weight_start(6)
    weight_start(7)
    mid = x_ref[...].astype(f32) + sum_finish(0)
    middle[...] = mid
    mid_scale = lax.rsqrt(jnp.mean(mid * mid, -1, keepdims=True) + epsilon)
    second[rows(c, block)] = (mid * mid_scale * fg_ref[...]).astype(bf16)
    gather_start(second, 2)
    weight_receive(2)
    weight_receive(3)
    hand_arrive(3)

    def feed(t, at):
        units, pair = slice(t * pw, (t + 1) * pw), 2 * pw * t
        both = dot(second[at], w_gu[:, pair:pair + 2 * pw])
        back = dot_nt(dy_all[at], w_down[units])
        gate, up = both[:, :pw], both[:, pw:]
        sig = 1.0 / (1.0 + jnp.exp(-gate))
        silu = gate * sig
        hidden[at, units] = (silu * up).astype(bf16)
        d_gu[at, pair:pair + pw] = (back * up * sig * (1.0 + gate * (1.0 - sig))).astype(bf16)
        d_gu[at, pair + pw:pair + 2 * pw] = (back * silu).astype(bf16)

    def feed_arriving(slot, carry):
        gather_step(second, 2, slot)
        at = rows(chip(slot), 2 * block)
        feed(0, at)
        second_t[:, at] = second[at].T
        return carry

    def third_grad(t):
        weight_grad(t, [
            (second_t, lambda: d_gu[:, 2 * pw * t:2 * pw * (t + 1)]),
            (dy_t, lambda: hidden[:, t * pw:(t + 1) * pw]),
        ])

    def feed_third(t):
        def body(i, carry):
            feed(t, rows(i, 2 * block))
            return carry

        lax.fori_loop(0, n // 2, body, 0)

    lax.fori_loop(0, n // 2, feed_arriving, 0)
    gather_stepped(second, 2)
    for t in range(1, thirds):
        weight_forward(2 + 2 * t)
        weight_forward(3 + 2 * t)
        third_grad(t - 1)
        weight_receive(2 + 2 * t, False)
        weight_receive(3 + 2 * t, False)
        hand_arrive(3 + 2 * t)
        if t < thirds - 1:
            feed_third(t)
    sum_start(
        1, d_gu, lambda left: dot_nt(left, w_gu[...]),
        lambda place: feed(thirds - 1, rows(place, 2 * block)))
    third_grad(thirds - 1)
    d_second = sum_finish(1)

    def norm_back(value, gain, grad):
        inv = lax.rsqrt(jnp.mean(value * value, -1, keepdims=True) + epsilon)
        weighted = grad * gain
        inner = jnp.mean(weighted * value, -1, keepdims=True)
        result = inv * weighted - value * (inv * inv * inv * inner)
        return result, jnp.sum(grad * value * inv, 0, keepdims=True)

    gain_own[...] = jnp.zeros_like(gain_own)
    part, gain_own[1:2, :] = norm_back(middle[...], fg_ref[...], d_second)
    d_mid = dy_ref[...].astype(f32) + part
    d_middle[...] = d_mid
    dmid[rows(c, block)] = d_mid.astype(bf16)
    gather_start(dmid, 3)

    dk_acc[...] = jnp.zeros_like(dk_acc)
    dv_acc[...] = jnp.zeros_like(dv_acc)

    def attend_back_block(i, d_mix):
        at = rows(i, block)
        d_mix_t = jnp.concatenate([d_mix[h * head:(h + 1) * head] for h in range(group)], 1)
        d_mix_t = (d_mix_t.astype(bf16).astype(f32) * sums[i]).astype(bf16)
        delta = jnp.sum(d_mix_t.astype(f32) * mixed_t[i], 0, keepdims=True)
        weight = probs[i]
        d_prob = dot(values[...], d_mix_t)
        d_score = (weight.astype(f32) * (d_prob - delta)).astype(bf16)
        d_query = dot(keys_t[...], d_score) * scale
        gained = jnp.zeros((1, head), f32)
        for h in range(group):
            grad = turn_back(d_query[:, h * block:(h + 1) * block].T, at)
            part, gain_part = norm_back(raw[at, h * head:(h + 1) * head], qg_ref[...], grad)
            d_qkv[at, h * head:(h + 1) * head] = part.astype(bf16)
            gained = gained + gain_part
        return dot(weight, d_mix_t.T), dot(d_score, stack(queries, at)), gained

    def attend_back(slot, q_sum):
        gather_step(dmid, 3, slot)
        at = rows(chip(slot), 2 * block)
        d_mix = dot_nt(w_out[...], dmid[at])
        dmid_t[:, at] = dmid[at].T
        dv_one, dk_one, gain_one = attend_back_block(2 * chip(slot), d_mix[:, :block])
        dv_two, dk_two, gain_two = attend_back_block(2 * chip(slot) + 1, d_mix[:, block:])
        dv_acc[...] += dv_one + dv_two
        dk_acc[...] += dk_one + dk_two
        return q_sum + gain_one + gain_two

    zero = jnp.zeros((1, head), f32)
    gain_own[2:3, 0:head] = lax.fori_loop(0, n // 2, attend_back, zero)
    gather_stepped(dmid, 3)
    weight_grad(3, [(dmid_t, lambda: mixed_low[...])])

    def project_back(i, k_sum):
        at = rows(i, 2 * block)
        grad = turn_back(dk_acc[at] * (1.0 / log2e), at)
        part, gain_part = norm_back(raw[at, qw:qw + kw], kg_ref[...], grad)
        d_qkv[at, qw:qw + kw] = part.astype(bf16)
        d_qkv[at, qw + kw:] = dv_acc[at].astype(bf16)
        return k_sum + gain_part

    gain_own[3:4, 0:head] = lax.fori_loop(0, n // 2, project_back, zero)

    weight_grad(4, [(first_t, lambda: d_qkv[...])])
    drain(in_plane)
    sum_start(3, d_qkv, lambda left: dot_nt(left, w_qkv[...]))
    sum_start(2, hidden, lambda left: dot(left, w_down[...]))
    for m in range(4):
        hand_out(m)
    x_part, gain_own[0:1, :] = norm_back(x_ref[...].astype(f32), ag_ref[...], sum_finish(3))
    dx_ref[...] = d_middle[...] + x_part

    def gain_plane_copy(j):
        return remote(gain_own, gain_plane.at[c], gp_send.at[j], gp_recv.at[j], partner(j), z)

    def gain_copy(d):
        return remote(gain_all.at[z], gain_all.at[z], gz_send.at[d], gz_recv.at[d], c, lax.rem(z + d, planes))

    for j in range(1, n):
        launch(in_plane, lambda j=j: gain_plane_copy(j))
    gain_plane[c] = gain_own[...]
    out_ref[...] = (middle[...] + sum_finish(2)).astype(bf16)
    for j in range(1, n):
        gain_plane_copy(j).wait_recv()
    total = gain_plane[0]
    for i in range(1, n):
        total = total + gain_plane[i]
    gain_all[z] = total
    for d in range(1, planes):
        launch(along, lambda d=d: gain_copy(d))
    for d in range(1, planes):
        origin = gain_all.at[lax.rem(z + planes - d, planes)]
        remote(origin, origin, gz_send.at[d], gz_recv.at[d], c, z).wait_recv()
    total = gain_all[0]
    for i in range(1, planes):
        total = total + gain_all[i]
    gains_ref[...] = total

    hand_out(4)
    for m in range(5):
        hand_receive(m)
    drain(in_plane)
    drain(along)


def finish_kernel(
    n, head, out_in, dx_in, gains_in, got_a, got_b, got_c, got_out, got_qkv,
    out_ref, dx_ref, ag_ref, q_ref, k_ref, v_ref, qg_ref, kg_ref, o_ref, fg_ref, g_ref, u_ref, d_ref,
):
    out_ref[...] = out_in[...]
    dx_ref[...] = dx_in[...]
    ag_ref[...] = gains_in[0:1, :]
    fg_ref[...] = gains_in[1:2, :]
    qg_ref[...] = gains_in[2:3, 0:head]
    kg_ref[...] = gains_in[3:4, 0:head]
    qw, kw = q_ref.shape[1] // n, k_ref.shape[1] // n
    pw = got_a.shape[2] // 3
    thirds = (got_a, got_b, got_c)
    for i in range(n):
        q_ref[:, i * qw:(i + 1) * qw] = got_qkv[i, :, 0:qw].astype(f32)
        k_ref[:, i * kw:(i + 1) * kw] = got_qkv[i, :, qw:qw + kw].astype(f32)
        v_ref[:, i * kw:(i + 1) * kw] = got_qkv[i, :, qw + kw:].astype(f32)
        o_ref[:, i * qw:(i + 1) * qw] = got_out[i].astype(f32)
        for t, got in enumerate(thirds):
            at = (i * len(thirds) + t) * pw
            g_ref[:, at:at + pw] = got[i, :, 0:pw].astype(f32)
            u_ref[:, at:at + pw] = got[i, :, pw:2 * pw].astype(f32)
            d_ref[:, at:at + pw] = got[i, :, 2 * pw:].astype(f32)


def plane_device(
    layer_input,
    token_positions,
    attention_gain,
    query_weight,
    key_matrix,
    value_matrix,
    query_gain,
    key_norm_gain,
    output_weight,
    feedforward_gain,
    gate_weight,
    up_weight,
    down_weight,
    out_cotangent,
):
    n = lax.axis_size("ctx")
    planes = lax.axis_size("fsdp")
    block, width = layer_input.shape[1:]
    length = token_positions.shape[1]
    head = query_gain.shape[0]
    qw = query_weight.shape[1] // n
    kw = key_matrix.shape[1] // n
    fw = gate_weight.shape[1] // n
    group = qw // head
    per = block // planes
    half = head // 2
    inverse = np.power(rope_base, -np.arange(half) * 2.0 / head).astype(np.float32)
    inverse = jnp.asarray(np.concatenate([inverse, inverse])[None])
    vmem = pl.BlockSpec(memory_space=pltpu.VMEM)
    hbm = pl.BlockSpec(memory_space=pl.ANY)
    dma = pltpu.SemaphoreType.DMA
    sizes = (fw, fw, fw, qw, qw + 2 * kw)
    low = lambda *shape: pltpu.VMEM(shape, bf16)
    wide = lambda *shape: pltpu.VMEM(shape, f32)
    scratch = [
        low(width, qw + 2 * kw), low(width, 2 * fw), low(qw, width), low(fw, width),
        low(planes * (output_weight.shape[0] // n), width), low(3, planes * 32, width),
        low(length, width), low(length, width), low(length, width),
        low(width, length), low(width, length), low(width, length), low(width, length),
        wide(length, head), wide(length, head), wide(length, head),
        wide(length, qw + kw), low(length, qw), low(length, kw), low(length, kw),
        low(kw, length), low(kw, length), low(n, length, group * block), wide(n, 1, group * block), wide(n, head, group * block), low(length, qw),
        low(length, fw), low(length, 2 * fw), low(length, qw + 2 * kw),
        wide(length, kw), wide(length, kw),
    ]
    scratch += [low(planes, n, per, size) for size in sizes]
    scratch += [low(planes, n, per, size) for size in sizes]
    scratch += [low(n, per, size) for size in sizes]
    scratch += [low(2, 4, block, width) for _ in range(4)] + [wide(2, block, width), wide(2, block, width)]
    scratch += [
        wide(block, width), wide(block, width), wide(8, width), wide(n, 8, width), wide(planes, 8, width),
        dma((13,)), dma((8, 6)), dma((8, planes)), dma((4, 7)), dma((4, 4)),
        dma((4, n)), dma((4, n)), dma((4, 4)), dma((4, 4)), dma((4, 4)), dma((4, 4)),
        dma((5, planes)), dma((5, planes)), dma((5, n)), dma((5, n)), dma((n,)), dma((n,)),
        dma((planes,)), dma((planes,)),
    ]
    shapes = [
        jax.ShapeDtypeStruct((block, width), bf16),
        jax.ShapeDtypeStruct((block, width), f32),
        jax.ShapeDtypeStruct((8, width), f32),
    ] + [jax.ShapeDtypeStruct((n, per, size), bf16) for size in sizes]
    results = pl.pallas_call(
        functools.partial(layer_kernel, n, planes, block, head, group, fw),
        out_shape=shapes,
        in_specs=[vmem] * 8 + [hbm] * 7,
        out_specs=[vmem] * len(shapes),
        scratch_shapes=scratch,
        compiler_params=pltpu.CompilerParams(
            collective_id=0, has_side_effects=True, vmem_limit_bytes=60 * 1024 * 1024),
    )(
        layer_input[0], out_cotangent[0], token_positions, inverse,
        attention_gain[None], feedforward_gain[None], query_gain[None], key_norm_gain[None],
        query_weight, key_matrix, value_matrix, output_weight, gate_weight, up_weight, down_weight,
    )
    plain = lambda rows, columns, kind=f32: jax.ShapeDtypeStruct((rows, columns), kind)
    finals = [
        plain(block, width, bf16), plain(block, width), plain(1, width),
        plain(per, n * qw), plain(per, n * kw), plain(per, n * kw), plain(1, head), plain(1, head),
        plain(per, n * qw), plain(1, width), plain(per, n * fw), plain(per, n * fw), plain(per, n * fw),
    ]
    done = pl.pallas_call(
        functools.partial(finish_kernel, n, head),
        out_shape=finals,
        in_specs=[vmem] * len(shapes),
        out_specs=[vmem] * len(finals),
    )(*results)
    out, dx, ag, q, k, v, qg, kg, o, fg, g, u, d = done
    return out[None], dx[None], ag[0], q, k, v, qg[0], kg[0], o.T, fg[0], g, u, d.T


def solution(mesh):
    in_specs = (
        P("fsdp", "ctx", None),
        P("fsdp", None),
        P(),
        P("fsdp", None),
        P("fsdp", None),
        P("fsdp", None),
        P(),
        P(),
        P("fsdp", None),
        P(),
        P("fsdp", None),
        P("fsdp", None),
        P("fsdp", None),
        P("fsdp", "ctx", None),
    )
    out_specs = (
        P("fsdp", "ctx", None),
        P("fsdp", "ctx", None),
        P(),
        P(("ctx", "fsdp"), None),
        P(("ctx", "fsdp"), None),
        P(("ctx", "fsdp"), None),
        P(),
        P(),
        P(None, ("ctx", "fsdp")),
        P(),
        P(("ctx", "fsdp"), None),
        P(("ctx", "fsdp"), None),
        P(None, ("ctx", "fsdp")),
    )

    def run(*arguments):
        n, planes = mesh.shape["ctx"], mesh.shape["fsdp"]
        key_heads = arguments[4].shape[1] // arguments[6].shape[0]
        whole_heads = n == 8 and planes == 4 and key_heads == n
        return jax.shard_map(
            plane_device if whole_heads else on_device,
            mesh=mesh, in_specs=in_specs, out_specs=out_specs, check_vma=False,
        )(*arguments)

    return run
```

```python
import functools

import jax
import jax.numpy as jnp
import numpy as np
from jax import lax
from jax.experimental import pallas as pl
from jax.experimental.pallas import tpu as pltpu
from jax.sharding import PartitionSpec as P

epsilon = 1e-06
rope_base = 1000000.0
masked_score = -1e30


def from_behind(block, axis, distance):
    devices = range(lax.axis_size(axis))
    route = [((i - distance) % len(devices), i) for i in devices]
    return lax.ppermute(block, axis, route)


def rotate(value_rows):
    half = value_rows.shape[-1] // 2
    return jnp.concatenate([-value_rows[..., half:], value_rows[..., :half]], -1)


def rotate_back(value_rows):
    half = value_rows.shape[-1] // 2
    return jnp.concatenate([value_rows[..., half:], -value_rows[..., :half]], -1)


def rope_tables(token_offsets, head_size):
    half = head_size // 2
    inverse = rope_base ** (-(jnp.arange(half).astype(jnp.float32) * 2.0) / head_size)
    angles = token_offsets.astype(jnp.float32)[:, None] * inverse[None, :]
    cosine = jnp.cos(angles)
    sine = jnp.sin(angles)
    return (jnp.concatenate([cosine, cosine], -1), jnp.concatenate([sine, sine], -1))


def norm_scale(value_rows):
    return lax.rsqrt(jnp.mean(value_rows * value_rows, -1, keepdims=True) + epsilon)


def norm_back(value_rows, scale, gain, grad):
    weighted = grad * gain
    inner = jnp.mean(weighted * value_rows, -1, keepdims=True)
    result = scale * weighted - value_rows * scale * scale * scale * inner
    gain_part = jnp.sum((grad * value_rows * scale).reshape(-1, gain.shape[0]), 0)
    return (result, gain_part)


def row_products(left, pieces):
    return tuple((jnp.dot(left, piece, preferred_element_type=jnp.float32) for piece in pieces))


def column_products(rights, pieces):
    total = jnp.einsum("tc,rc->tr", rights[0], pieces[0], preferred_element_type=jnp.float32)
    for right, piece in zip(rights[1:], pieces[1:]):
        total = total + jnp.einsum("tc,rc->tr", right, piece, preferred_element_type=jnp.float32)
    return total


def on_device(
    layer_input,
    token_positions,
    attention_gain,
    query_weight,
    key_matrix,
    value_matrix,
    query_gain,
    key_norm_gain,
    output_weight,
    feedforward_gain,
    gate_weight,
    up_weight,
    down_weight,
    out_cotangent,
):
    hidden_in = layer_input[0].astype(jnp.float32)
    count = hidden_in.shape[0]
    head_size = query_gain.shape[0]
    query_width = query_weight.shape[1]
    key_width = key_matrix.shape[1]
    inner_width = gate_weight.shape[1]
    heads = query_width // head_size
    key_heads = key_width // head_size
    group = heads // key_heads
    scale = head_size ** (-0.5)
    cycles = lax.axis_size("ctx")
    own_index = lax.axis_index("ctx")
    sequence_pos = token_positions[0]
    token_offsets = lax.dynamic_slice_in_dim(sequence_pos, own_index * count, count)
    cosine, sine = rope_tables(token_offsets, head_size)
    cosine = cosine[:, None, :]
    sine = sine[:, None, :]
    first_scale = norm_scale(hidden_in)
    first = (hidden_in * first_scale * attention_gain).astype(jnp.bfloat16)
    query_raw, key_unnormed, value_unnormed = row_products(
        first,
        (
            lax.all_gather(query_weight, "fsdp", axis=0, tiled=True),
            lax.all_gather(key_matrix, "fsdp", axis=0, tiled=True),
            lax.all_gather(value_matrix, "fsdp", axis=0, tiled=True),
        ),
    )
    query_heads = query_raw.reshape(count, heads, head_size)
    query_scale = norm_scale(query_heads)
    query_normed = query_heads * query_scale * query_gain
    query_rot = query_normed * cosine + rotate(query_normed) * sine
    query_grouped = (
        query_rot.reshape(count, key_heads, group, head_size)
        .transpose(1, 2, 0, 3)
        .astype(jnp.bfloat16)
    )
    key_heads_raw = key_unnormed.reshape(count, key_heads, head_size)
    key_scale = norm_scale(key_heads_raw)
    key_normed = key_heads_raw * key_scale * key_norm_gain
    key_low = (
        (key_normed * cosine + rotate(key_normed) * sine)
        .reshape(count, key_width)
        .astype(jnp.bfloat16)
    )
    value_low = value_unnormed.astype(jnp.bfloat16)
    rowmax = jnp.full((key_heads, group, count), masked_score, jnp.float32)
    keys_piece = lax.all_gather(key_low, "ctx", axis=0, tiled=True).reshape(
        -1, key_heads, head_size
    )
    values_piece = lax.all_gather(value_low, "ctx", axis=0, tiled=True).reshape(
        -1, key_heads, head_size
    )
    key_pos = sequence_pos
    allowed = token_offsets[:, None] >= key_pos[None, :]
    scores = (
        jnp.einsum("kgtd,skd->kgts", query_grouped, keys_piece, preferred_element_type=jnp.float32)
        * scale
    )
    scores = jnp.where(allowed, scores, masked_score)
    newmax = jnp.maximum(rowmax, jnp.max(scores, -1))
    weights = jnp.where(allowed, jnp.exp(scores - newmax[..., None]), 0.0)
    accum = jnp.einsum(
        "kgts,skd->kgtd",
        weights.astype(jnp.bfloat16),
        values_piece,
        preferred_element_type=jnp.float32,
    )
    rowsum = jnp.sum(weights, -1)
    accum, rowmax, rowsum = (accum, newmax, rowsum)
    normalized = accum / rowsum[..., None]
    logsum = rowmax + jnp.log(rowsum)
    attention_low = (
        normalized.transpose(2, 0, 1, 3).reshape(count, query_width).astype(jnp.bfloat16)
    )
    output_whole = lax.all_gather(output_weight, "fsdp", axis=0, tiled=True)
    branch_out = jnp.dot(attention_low, output_whole, preferred_element_type=jnp.float32)
    middle = hidden_in + branch_out
    second_scale = norm_scale(middle)
    second = (middle * second_scale * feedforward_gain).astype(jnp.bfloat16)
    gate, up = row_products(
        second,
        (
            lax.all_gather(gate_weight, "fsdp", axis=0, tiled=True),
            lax.all_gather(up_weight, "fsdp", axis=0, tiled=True),
        ),
    )
    sigmoid_gate = jax.nn.sigmoid(gate)
    silu_gate = gate * sigmoid_gate
    hidden_low = (silu_gate * up).astype(jnp.bfloat16)
    (down_out,) = row_products(
        hidden_low, (lax.all_gather(down_weight, "fsdp", axis=0, tiled=True),)
    )
    layer_output = (middle + down_out).astype(jnp.bfloat16)[None]
    cotangent = out_cotangent[0]
    hidden_grad = column_products(
        (cotangent,), lax.all_gather((down_weight,), "fsdp", axis=0, tiled=True)
    )
    up_low = (hidden_grad * silu_gate).astype(jnp.bfloat16)
    gate_low = (hidden_grad * up * sigmoid_gate * (1.0 + gate * (1.0 - sigmoid_gate))).astype(
        jnp.bfloat16
    )
    second_grad = column_products(
        (gate_low, up_low), lax.all_gather((gate_weight, up_weight), "fsdp", axis=0, tiled=True)
    )
    middle_part, feedforward_part = norm_back(middle, second_scale, feedforward_gain, second_grad)
    middle_grad = cotangent.astype(jnp.float32) + middle_part
    middle_low = middle_grad.astype(jnp.bfloat16)
    attention_grad = jnp.einsum(
        "tc,rc->tr", middle_low, output_whole, preferred_element_type=jnp.float32
    )
    attention_grad_low = attention_grad.astype(jnp.bfloat16)
    mixed_grad = attention_grad_low.reshape(count, key_heads, group, head_size).transpose(
        1, 2, 0, 3
    )
    delta = jnp.sum(mixed_grad.astype(jnp.float32) * normalized, -1)

    def cycle_step(index, carry):
        keys_held, values_held, key_acc, value_acc, query_acc = carry
        anchor = (own_index - index) % cycles
        key_pos = lax.dynamic_slice_in_dim(sequence_pos, anchor * count, count)
        keys_piece = keys_held.astype(jnp.bfloat16).reshape(count, key_heads, head_size)
        values_piece = values_held.astype(jnp.bfloat16).reshape(count, key_heads, head_size)
        allowed = token_offsets[:, None] >= key_pos[None, :]
        scores = (
            jnp.einsum(
                "kgtd,skd->kgts", query_grouped, keys_piece, preferred_element_type=jnp.float32
            )
            * scale
        )
        probs = jnp.where(allowed, jnp.exp(scores - logsum[..., None]), 0.0)
        value_acc = value_acc + jnp.einsum(
            "kgts,kgtd->skd",
            probs.astype(jnp.bfloat16),
            mixed_grad,
            preferred_element_type=jnp.float32,
        ).reshape(count, key_width)
        prob_grad = jnp.einsum(
            "kgtd,skd->kgts", mixed_grad, values_piece, preferred_element_type=jnp.float32
        )
        score_grad = (probs * (prob_grad - delta[..., None])).astype(jnp.bfloat16)
        query_acc = (
            query_acc
            + jnp.einsum(
                "kgts,skd->kgtd", score_grad, keys_piece, preferred_element_type=jnp.float32
            )
            * scale
        )
        key_acc = (
            key_acc
            + jnp.einsum(
                "kgts,kgtd->skd", score_grad, query_grouped, preferred_element_type=jnp.float32
            ).reshape(count, key_width)
            * scale
        )
        moved = (
            from_behind(keys_held.astype(jnp.bfloat16), "ctx", 1).astype(keys_held.dtype),
            from_behind(values_held.astype(jnp.bfloat16), "ctx", 1).astype(values_held.dtype),
            from_behind(key_acc.astype(jnp.bfloat16), "ctx", 1).astype(key_acc.dtype),
            from_behind(value_acc.astype(jnp.bfloat16), "ctx", 1).astype(value_acc.dtype),
        )
        return (moved[0], moved[1], moved[2], moved[3], query_acc)

    start_cycle = (
        key_low.astype(jnp.float32),
        value_low.astype(jnp.float32),
        jnp.zeros((count, key_width), jnp.float32),
        jnp.zeros((count, key_width), jnp.float32),
        jnp.zeros((key_heads, group, count, head_size), jnp.float32),
    )
    cycle_done = lax.fori_loop(0, cycles, cycle_step, start_cycle)
    key_acc = cycle_done[2]
    value_acc = cycle_done[3]
    query_acc = cycle_done[4]
    query_rot_grad = query_acc.transpose(2, 0, 1, 3).reshape(count, heads, head_size)
    query_normed_grad = query_rot_grad * cosine + rotate_back(query_rot_grad * sine)
    query_heads_grad, query_part = norm_back(
        query_heads, query_scale, query_gain, query_normed_grad
    )
    query_low_grad = query_heads_grad.reshape(count, query_width).astype(jnp.bfloat16)
    key_rot_grad = key_acc.reshape(count, key_heads, head_size)
    key_normed_grad = key_rot_grad * cosine + rotate_back(key_rot_grad * sine)
    key_heads_grad, key_part = norm_back(key_heads_raw, key_scale, key_norm_gain, key_normed_grad)
    key_low_grad = key_heads_grad.reshape(count, key_width).astype(jnp.bfloat16)
    value_low_grad = value_acc.astype(jnp.bfloat16)
    first_grad = column_products(
        (query_low_grad, key_low_grad, value_low_grad),
        lax.all_gather((query_weight, key_matrix, value_matrix), "fsdp", axis=0, tiled=True),
    )
    input_part, attention_part = norm_back(hidden_in, first_scale, attention_gain, first_grad)
    input_gradient = (middle_grad + input_part)[None]
    rights_first = jnp.concatenate([query_low_grad, key_low_grad, value_low_grad], 1)
    rights_second = jnp.concatenate([gate_low, up_low], 1)
    pairs = (
        (first, rights_first),
        (second, rights_second),
        (middle_low, attention_low),
        (cotangent, hidden_low),
    )
    parts = []
    for left, right in pairs:
        parts.append(jnp.einsum("tr,tc->rc", left, right, preferred_element_type=jnp.float32))
    sums = lax.psum_scatter(
        jnp.concatenate(parts, 1), ("ctx", "fsdp"), scatter_dimension=0, tiled=True
    )
    edges = [0, query_width, query_width + key_width, query_width + 2 * key_width]
    edges = edges + [edges[3] + inner_width, edges[3] + 2 * inner_width]
    edges = edges + [edges[5] + query_width, edges[5] + query_width + inner_width]
    query_gradient = sums[:, edges[0] : edges[1]]
    key_gradient = sums[:, edges[1] : edges[2]]
    value_gradient = sums[:, edges[2] : edges[3]]
    gate_gradient = sums[:, edges[3] : edges[4]]
    up_gradient = sums[:, edges[4] : edges[5]]
    output_gradient = sums[:, edges[5] : edges[6]].T
    down_gradient = sums[:, edges[6] : edges[7]].T
    attention_total, query_total, key_total, feedforward_total = lax.psum(
        (attention_part, query_part, key_part, feedforward_part), ("ctx", "fsdp")
    )
    return (
        layer_output,
        input_gradient,
        attention_total,
        query_gradient,
        key_gradient,
        value_gradient,
        query_total,
        key_total,
        output_gradient,
        feedforward_total,
        gate_gradient,
        up_gradient,
        down_gradient,
    )


MESH = pl.DeviceIdType.MESH
f32 = jnp.float32
bf16 = jnp.bfloat16


def dot(left, right):
    return jnp.dot(left, right, preferred_element_type=f32)


def dot_nt(left, right):
    return lax.dot_general(left, right, (((1,), (1,)), ((), ())), preferred_element_type=f32)


def dot_tn(left, right):
    return lax.dot_general(left, right, (((0,), (0,)), ((), ())), preferred_element_type=f32)


def layer_kernel(
    n, planes, block, head, group, fw,
    x_ref, dy_ref, pos_row, inverse_ref, ag_ref, fg_ref, qg_ref, kg_ref,
    wq, wk, wv, wo, wg, wu, wd,
    out_ref, dx_ref, gains_ref, got_a, got_b, got_c, got_out, got_qkv,
    w_qkv, w_gu, w_out, w_down, t_out, t_down,
    first, dy_all, second, first_t, dy_t, second_t, dmid_t,
    positions, cosine, sine,
    raw, queries, keys, values, keys_t, values_t, probs, sums, mixed_t, mixed_low,
    hidden, d_gu, d_qkv, dk_acc, dv_acc,
    stage_a, stage_b, stage_c, stage_out, stage_qkv,
    land_a, land_b, land_c, land_out, land_qkv,
    rs_sa, rs_ra, rs_sb, rs_rb, rs_kept, rs_acc,
    middle, d_middle, gain_own, gain_plane, gain_all,
    local_sem, wz_send, wz_recv, hand_send, hand_recv,
    ag_send, ag_recv, ra_send, ra_recv, rb_send, rb_recv,
    zr_send, zr_recv, aa_send, aa_recv, gp_send, gp_recv, gz_send, gz_recv,
):
    c = lax.axis_index("ctx")
    z = lax.axis_index("fsdp")
    dmid = first
    cy, cx, ck = lax.div(c, 4), lax.rem(lax.div(c, 2), 2), lax.rem(c, 2)
    ci = lax.rem(c, 4)
    sign = 1 - 2 * ck
    qw, kw = group * head, head
    pw = 128
    thirds = fw // pw
    piece = pw // 4
    width = x_ref.shape[1]
    scale = head ** (-0.5)
    log2e = 1.4426950408889634
    gots = (got_a, got_b, got_c, got_out, got_qkv)
    stages = (stage_a, stage_b, stage_c, stage_out, stage_qkv)
    lands = (land_a, land_b, land_c, land_out, land_qkv)

    def partner(j):
        y = lax.rem(cy + lax.div(j, 4), 2)
        x = lax.rem(cx + lax.rem(lax.div(j, 2), 2), 2)
        k = lax.rem(ck + lax.rem(j, 2), 2)
        return y * 4 + x * 2 + k

    def chip(slot):
        return lax.rem(cy + lax.div(slot, 2), 2) * 2 + lax.rem(cx + lax.rem(slot, 2), 2)

    def rows(start, size):
        return pl.ds(pl.multiple_of(start * size, size), size)

    def remote(src, dst, send, recv, ctx, plane):
        return pltpu.make_async_remote_copy(
            src_ref=src, dst_ref=dst, send_sem=send, recv_sem=recv,
            device_id={"ctx": ctx, "fsdp": plane}, device_id_type=MESH,
        )

    in_plane, along = [], []

    def launch(started, copy, when=None):
        if when is None:
            copy().start()
        else:
            pl.when(when)(lambda: copy().start())
        started.append((copy, when))

    def drain(started):
        for copy, when in started:
            if when is None:
                copy().wait_send()
            else:
                pl.when(when)(lambda copy=copy: copy().wait_send())
        started.clear()

    own_rows = wq.shape[0]
    out_rows = wo.shape[0] // n

    def own_slices():
        mine = rows(z, own_rows)
        pairs = [
            (wq.at[:, rows(c, qw)], w_qkv.at[mine, 0:qw]),
            (wk.at[:, rows(c, kw)], w_qkv.at[mine, qw:qw + kw]),
            (wv.at[:, rows(c, kw)], w_qkv.at[mine, qw + kw:qw + 2 * kw]),
            (wo.at[rows(c, out_rows)], t_out.at[rows(z, out_rows)]),
        ]
        for t in range(thirds):
            at = 2 * pw * t
            pairs.append((wg.at[:, rows(c * thirds + t, pw)], w_gu.at[mine, at:at + pw]))
            pairs.append((wu.at[:, rows(c * thirds + t, pw)], w_gu.at[mine, at + pw:at + 2 * pw]))
            pairs.append((wd.at[rows((cy * thirds + t) * 4 + ci, piece)], t_down.at[t, rows(z, piece)]))
        return pairs

    local = [pltpu.make_async_copy(src, dst, local_sem.at[i]) for i, (src, dst) in enumerate(own_slices())]
    for copy in local:
        copy.start()

    for land in lands:
        @pl.when(z == 0)
        def _(land=land):
            land[0] = jnp.zeros(land.shape[1:], bf16)

        @pl.when(z == planes - 1)
        def _(land=land):
            land[planes] = jnp.zeros(land.shape[1:], bf16)

    barrier = pltpu.get_barrier_semaphore()
    for j in range(1, n):
        pl.semaphore_signal(barrier, inc=1, device_id={"ctx": partner(j), "fsdp": z}, device_id_type=MESH)
    for d in range(1, planes):
        pl.semaphore_signal(
            barrier, inc=1, device_id={"ctx": c, "fsdp": lax.rem(z + d, planes)}, device_id_type=MESH)
    x = x_ref[...].astype(f32)
    x_scale = lax.rsqrt(jnp.mean(x * x, -1, keepdims=True) + epsilon)
    first[rows(c, block)] = (x * x_scale * ag_ref[...]).astype(bf16)
    dy_all[rows(c, block)] = dy_ref[...]
    for copy in local[:3]:
        copy.wait()
    pl.semaphore_wait(barrier, n + planes - 2)

    def inside(t):
        return jnp.logical_and(t >= 0, t < planes)

    weights = [
        (lambda o: w_qkv.at[rows(o, own_rows)], None),
        (lambda o: t_out.at[rows(o, out_rows)], 0),
    ]
    for t in range(thirds):
        weights.append((lambda o, t=t: w_gu.at[rows(o, own_rows), 2 * pw * t:2 * pw * (t + 1)], None))
        weights.append((lambda o, t=t: t_down.at[t, rows(o, piece)], 1 + t))

    def weight_copy(w, slot, origin, target):
        part = weights[w][0](origin)
        return remote(part, part, wz_send.at[w, slot], wz_recv.at[w, origin], c, target)

    def weight_start(w):
        for side in range(2):
            d = sign * (1 - 2 * side)
            launch(along, lambda side=side, d=d: weight_copy(w, side, z, z + d), inside(z + d))
        if weights[w][1] is not None:
            hand_over(w, z, 0, None)

    def hand_target(h):
        if h == 0:
            return lambda i: w_out.at[rows(i, out_rows)]
        return lambda i: w_down.at[rows((h - 1) * 4 + i, piece)]

    def hand_copy(w, origin, slot):
        h = weights[w][1]
        return remote(
            weights[w][0](origin), hand_target(h)(ci), hand_send.at[h, slot], hand_recv.at[h, ci], 2 * origin + cy, z)

    def hand_over(w, origin, slot, valid):
        away = 2 * origin + cy != c
        here = jnp.logical_not(away)
        if valid is not None:
            away, here = jnp.logical_and(valid, away), jnp.logical_and(valid, here)
        launch(in_plane, lambda: hand_copy(w, origin, slot), away)

        @pl.when(here)
        def _():
            hand_target(weights[w][1])(ci)[...] = weights[w][0](origin)[...]

    def hand_arrive(w):
        h = weights[w][1]
        for i in range(4):
            @pl.when(4 * ck + i != c)
            def _(i=i):
                part = hand_target(h)(i)
                remote(part, part, hand_send.at[h, 0], hand_recv.at[h, i], c, z).wait_recv()

    def weight_hop(w, d):
        for side, way in enumerate((1, -1)):
            origin = z - way * d
            valid = inside(origin)
            pl.when(valid)(lambda origin=origin: weight_copy(w, 0, origin, z).wait_recv())
            if d < planes - 1:
                launch(
                    along,
                    lambda side=side, way=way, origin=origin: weight_copy(w, 2 * d + side, origin, z + way),
                    jnp.logical_and(valid, inside(z + way)))
            if weights[w][1] is not None:
                hand_over(w, origin, 2 * d - 1 + side, valid)

    def gather_copy(buf, g, j, send, origin, target):
        part = buf.at[rows(origin, block)]
        return remote(part, part, ag_send.at[g, send], ag_recv.at[g, j], target, z)

    def gather_start(buf, g):
        for j in (1, 2 + 2 * ck, 4 - 2 * ck, 6):
            launch(in_plane, lambda j=j: gather_copy(buf, g, j, j, c, partner(j)))

    def gather_forward(buf, g, j):
        return gather_copy(buf, g, j + 1, j + 1, partner(j), partner(1))

    def gather_finish(buf, g):
        for j in (2, 4, 6):
            gather_copy(buf, g, j, j, partner(j), c).wait_recv()
            launch(in_plane, lambda j=j: gather_forward(buf, g, j))
        for j in (1, 3, 5, 7):
            gather_copy(buf, g, j, j, partner(j), c).wait_recv()

    def gather_step(buf, g, slot):
        def arrive(j):
            gather_copy(buf, g, j, j, partner(j), c).wait_recv()
            gather_forward(buf, g, j).start()

        @pl.when(slot == 1)
        def _():
            arrive(2)
            arrive(4)

        @pl.when(slot == 3)
        def _():
            arrive(6)

        gather_copy(buf, g, 2 * slot + 1, 0, partner(2 * slot + 1), c).wait_recv()

    def gather_stepped(buf, g):
        for j in (2, 4, 6):
            in_plane.append((lambda j=j: gather_forward(buf, g, j), None))

    def sum_pair_copy(s, slot):
        return remote(rs_sa.at[s % 2, slot], rs_ra.at[s % 2, slot], ra_send.at[s, slot], ra_recv.at[s, slot], partner(1), z)

    def sum_chip_copy(s, slot):
        return remote(
            rs_sb.at[s % 2, slot], rs_rb.at[s % 2, slot], rb_send.at[s, slot], rb_recv.at[s, slot], partner(2 * slot), z)

    def sum_slot(p):
        return jnp.where(p == 0, 3, jnp.where(p == 1, 2 - ck, jnp.where(p == 2, 1 + ck, 0)))

    def sum_start(s, left, partial, prepare=None, ready=None):
        if prepare is not None:
            prepare(chip(sum_slot(0)))
        if ready is not None:
            ready()

        def body(p, carry):
            slot = sum_slot(p)
            at = [rows(partner(2 * slot + 1), block), rows(partner(2 * slot), block)]
            both = partial(jnp.concatenate([left[i] for i in at], 0))
            rs_sa[s % 2, slot] = both[:block].astype(bf16)
            sum_pair_copy(s, slot).start()
            rs_kept[lax.rem(p, 2)] = both[block:]
            if prepare is not None:
                @pl.when(p < 3)
                def _():
                    prepare(chip(sum_slot(p + 1)))

            @pl.when(p > 0)
            def _():
                before = sum_slot(p - 1)
                sum_pair_copy(s, before).wait_recv()
                rs_sb[s % 2, before] = (
                    rs_kept[lax.rem(p + 1, 2)] + rs_ra[s % 2, before].astype(f32)).astype(bf16)
                sum_chip_copy(s, before).start()

            return carry

        lax.fori_loop(0, 4, body, 0)
        for slot in range(4):
            in_plane.append((lambda slot=slot: sum_pair_copy(s, slot), None))
            if slot > 0:
                in_plane.append((lambda slot=slot: sum_chip_copy(s, slot), None))
        sum_pair_copy(s, 0).wait_recv()
        rs_acc[s % 2] = rs_kept[1] + rs_ra[s % 2, 0].astype(f32)

    def sum_finish(s):
        total = rs_acc[s % 2]
        for slot in (1, 2, 3):
            sum_chip_copy(s, slot).wait_recv()
            total = total + rs_rb[s % 2, slot].astype(f32)
        return total

    per = block // planes

    def weight_grad(m, parts):
        def body(i, carry):
            at = 0
            for left, right in parts:
                value = right()
                grad = dot(left[rows(i, 2 * block)], value)
                for k in range(2):
                    for t in range(planes):
                        start = k * block + t * per
                        stages[m][t, 2 * i + k, :, at:at + value.shape[1]] = grad[start:start + per].astype(bf16)
                at += value.shape[1]
            return carry

        lax.fori_loop(0, n // 2, body, 0)
        at_edge = jnp.logical_or(z == 0, z == planes - 1)
        for k in range(planes - 1):
            t = jnp.where(z == 0, planes - 1 - k, k)
            launch(along, lambda t=t: grad_copy(m, t), at_edge)

    def grad_copy(m, t):
        way = jnp.where(z < t, 1, -1)
        last = z + way == t
        slot = jnp.where(jnp.logical_and(last, way < 0), planes, t)
        return remote(
            stages[m].at[t], lands[m].at[slot], zr_send.at[m, t], zr_recv.at[m, slot], c, z + way)

    def grad_arrive(m, slot):
        part = lands[m].at[slot]
        remote(part, part, zr_send.at[m, 0], zr_recv.at[m, slot], c, z).wait_recv()

    def grad_pass(m, t, valid):
        @pl.when(valid)
        def _():
            grad_arrive(m, t)

            def body(i, carry):
                stages[m][t, i] = (stages[m][t, i].astype(f32) + lands[m][t, i].astype(f32)).astype(bf16)
                return carry

            lax.fori_loop(0, n, body, 0)

        launch(along, lambda: grad_copy(m, t), valid)

    def grad_near(m):
        for t in (3, 2):
            grad_pass(m, t, z == 1)
        for t in (0, 1):
            grad_pass(m, t, z == 2)

    def grad_far(m):
        grad_pass(m, 3, z == 2)
        grad_pass(m, 0, z == 1)

    def owner_copy(m, j):
        return remote(lands[m].at[z, partner(j)], gots[m].at[c], aa_send.at[m, j], aa_recv.at[m, j], partner(j), z)

    def hand_out(m):
        pl.when(z > 0)(lambda: grad_arrive(m, z))
        pl.when(z < planes - 1)(lambda: grad_arrive(m, planes))

        def body(i, carry):
            total = stages[m][z, i].astype(f32) + lands[m][z, i].astype(f32) + lands[m][planes, i].astype(f32)
            lands[m][z, i] = total.astype(bf16)
            return carry

        lax.fori_loop(0, n, body, 0)
        for j in (2 + 2 * ck, 3 + 2 * ck, 4 - 2 * ck, 5 - 2 * ck, 6, 7, 1):
            launch(in_plane, lambda j=j: owner_copy(m, j))
        gots[m][c] = lands[m][z, c]

    def hand_receive(m):
        for j in range(1, n):
            owner_copy(m, j).wait_recv()

    weight_start(0)
    gather_start(first, 0)
    for copy in local[3:]:
        copy.wait()

    spread = jnp.broadcast_to(pos_row[...].astype(f32), (head, pos_row.shape[1]))
    positions[...] = spread.T
    side = jnp.where(lax.broadcasted_iota(jnp.int32, (1, head), 1) < head // 2, -1.0, 1.0)

    def table(i, carry):
        at = rows(i, block)
        angle = positions[at] * inverse_ref[...]
        cosine[at] = jnp.cos(angle)
        sine[at] = jnp.sin(angle) * side
        return carry

    def turn_over(src, dst):
        def body(i, carry):
            at = rows(i, block)
            dst[:, at] = src[at].T
            return carry

        lax.fori_loop(0, n, body, 0)

    lax.fori_loop(0, n, table, 0)
    weight_hop(0, 1)
    gather_finish(first, 0)
    gather_start(dy_all, 1)
    turn_over(first, first_t)
    weight_hop(0, 2)
    weight_start(1)
    weight_hop(0, 3)
    gather_finish(dy_all, 1)
    weight_start(2)
    weight_start(3)

    def turn(value, at):
        return value * cosine[at] + pltpu.roll(value, head // 2, 1) * sine[at]

    def turn_back(grad, at):
        return grad * cosine[at] - pltpu.roll(grad, head // 2, 1) * sine[at]

    def project(i, carry):
        at = rows(i, 2 * block)
        result = dot(first[at], w_qkv[...])
        raw[at] = result[:, :qw + kw]
        low_values = result[:, qw + kw:].astype(bf16)
        values[at] = low_values
        values_t[:, at] = low_values.T
        for h in range(group + 1):
            part = result[:, h * head:(h + 1) * head]
            inv = lax.rsqrt(jnp.mean(part * part, -1, keepdims=True) + epsilon)
            gain = qg_ref[...] if h < group else kg_ref[...]
            turned = turn(part * inv * gain, at)
            if h < group:
                queries[at, h * head:(h + 1) * head] = (turned * (scale * log2e)).astype(bf16)
            else:
                low_keys = turned.astype(bf16)
                keys[at] = low_keys
                keys_t[:, at] = low_keys.T
        return carry

    lax.fori_loop(0, n // 2, project, 0)
    weight_hop(1, 1)
    turn_over(dy_all, dy_t)
    weight_hop(1, 2)

    def stack(ref, at):
        return jnp.concatenate([ref[at, h * head:(h + 1) * head] for h in range(group)], 0)

    def attend_block(i):
        at = rows(i, block)
        scores = dot_nt(keys[...], stack(queries, at))
        allowed = positions[...] <= pos_row[:, at].astype(f32)
        weight = jnp.concatenate(
            [jnp.exp2(jnp.where(allowed, scores[:, h * block:(h + 1) * block], masked_score)) for h in range(group)], 1)
        inv = 1.0 / jnp.sum(weight, 0, keepdims=True)
        low_weight = weight.astype(bf16)
        probs[i] = low_weight
        sums[i] = inv
        result = dot(values_t[...], low_weight) * inv
        mixed_t[i] = result
        for h in range(group):
            mixed_low[at, h * head:(h + 1) * head] = result[:, h * block:(h + 1) * block].T.astype(bf16)

    def attend(place):
        attend_block(2 * place)
        attend_block(2 * place + 1)

    def output_ready():
        weight_hop(1, 3)
        weight_hop(2, 1)
        weight_hop(3, 1)
        weight_start(4)
        weight_start(5)
        hand_arrive(1)
        drain(in_plane)

    sum_start(0, mixed_low, lambda left: dot(left, w_out[...]), attend, output_ready)
    weight_hop(2, 2)
    weight_hop(3, 2)
    weight_start(6)
    weight_start(7)
    mid = x_ref[...].astype(f32) + sum_finish(0)
    middle[...] = mid
    mid_scale = lax.rsqrt(jnp.mean(mid * mid, -1, keepdims=True) + epsilon)
    second[rows(c, block)] = (mid * mid_scale * fg_ref[...]).astype(bf16)
    gather_start(second, 2)
    weight_hop(2, 3)
    weight_hop(3, 3)
    hand_arrive(3)
    weight_hop(4, 1)
    weight_hop(5, 1)

    def feed(t, at):
        units, pair = slice(t * pw, (t + 1) * pw), 2 * pw * t
        both = dot(second[at], w_gu[:, pair:pair + 2 * pw])
        back = dot_nt(dy_all[at], w_down[units])
        gate, up = both[:, :pw], both[:, pw:]
        sig = 1.0 / (1.0 + jnp.exp(-gate))
        silu = gate * sig
        hidden[at, units] = (silu * up).astype(bf16)
        d_gu[at, pair:pair + pw] = (back * up * sig * (1.0 + gate * (1.0 - sig))).astype(bf16)
        d_gu[at, pair + pw:pair + 2 * pw] = (back * silu).astype(bf16)

    def feed_arriving(slot, carry):
        gather_step(second, 2, slot)
        at = rows(chip(slot), 2 * block)
        feed(0, at)
        second_t[:, at] = second[at].T
        return carry

    def third_grad(t):
        weight_grad(t, [
            (second_t, lambda: d_gu[:, 2 * pw * t:2 * pw * (t + 1)]),
            (dy_t, lambda: hidden[:, t * pw:(t + 1) * pw]),
        ])

    def feed_third(t):
        def body(i, carry):
            feed(t, rows(i, 2 * block))
            return carry

        lax.fori_loop(0, n // 2, body, 0)

    lax.fori_loop(0, n // 2, feed_arriving, 0)
    gather_stepped(second, 2)
    weight_hop(4, 2)
    weight_hop(5, 2)
    weight_hop(6, 1)
    weight_hop(7, 1)
    third_grad(0)
    weight_hop(4, 3)
    weight_hop(5, 3)
    hand_arrive(5)
    feed_third(1)
    weight_hop(6, 2)
    weight_hop(7, 2)
    third_grad(1)
    grad_near(0)
    weight_hop(6, 3)
    weight_hop(7, 3)
    hand_arrive(7)
    sum_start(
        1, d_gu, lambda left: dot_nt(left, w_gu[...]),
        lambda place: feed(thirds - 1, rows(place, 2 * block)))
    third_grad(2)
    grad_far(0)
    grad_near(1)
    d_second = sum_finish(1)

    def norm_back(value, gain, grad):
        inv = lax.rsqrt(jnp.mean(value * value, -1, keepdims=True) + epsilon)
        weighted = grad * gain
        inner = jnp.mean(weighted * value, -1, keepdims=True)
        result = inv * weighted - value * (inv * inv * inv * inner)
        return result, jnp.sum(grad * value * inv, 0, keepdims=True)

    gain_own[...] = jnp.zeros_like(gain_own)
    part, gain_own[1:2, :] = norm_back(middle[...], fg_ref[...], d_second)
    d_mid = dy_ref[...].astype(f32) + part
    d_middle[...] = d_mid
    dmid[rows(c, block)] = d_mid.astype(bf16)
    gather_start(dmid, 3)
    grad_far(1)
    grad_near(2)

    dk_acc[...] = jnp.zeros_like(dk_acc)
    dv_acc[...] = jnp.zeros_like(dv_acc)

    def attend_back_block(i, d_mix):
        at = rows(i, block)
        d_mix_t = jnp.concatenate([d_mix[h * head:(h + 1) * head] for h in range(group)], 1)
        d_mix_t = (d_mix_t.astype(bf16).astype(f32) * sums[i]).astype(bf16)
        delta = jnp.sum(d_mix_t.astype(f32) * mixed_t[i], 0, keepdims=True)
        weight = probs[i]
        d_prob = dot(values[...], d_mix_t)
        d_score = (weight.astype(f32) * (d_prob - delta)).astype(bf16)
        d_query = dot(keys_t[...], d_score) * scale
        gained = jnp.zeros((1, head), f32)
        for h in range(group):
            grad = turn_back(d_query[:, h * block:(h + 1) * block].T, at)
            part, gain_part = norm_back(raw[at, h * head:(h + 1) * head], qg_ref[...], grad)
            d_qkv[at, h * head:(h + 1) * head] = part.astype(bf16)
            gained = gained + gain_part
        return dot(weight, d_mix_t.T), dot(d_score, stack(queries, at)), gained

    def attend_back(slot, q_sum):
        gather_step(dmid, 3, slot)
        at = rows(chip(slot), 2 * block)
        d_mix = dot_nt(w_out[...], dmid[at])
        dmid_t[:, at] = dmid[at].T
        dv_one, dk_one, gain_one = attend_back_block(2 * chip(slot), d_mix[:, :block])
        dv_two, dk_two, gain_two = attend_back_block(2 * chip(slot) + 1, d_mix[:, block:])
        dv_acc[...] += dv_one + dv_two
        dk_acc[...] += dk_one + dk_two
        return q_sum + gain_one + gain_two

    zero = jnp.zeros((1, head), f32)
    gain_own[2:3, 0:head] = lax.fori_loop(0, n // 2, attend_back, zero)
    gather_stepped(dmid, 3)
    weight_grad(3, [(dmid_t, lambda: mixed_low[...])])
    grad_far(2)

    def project_back(i, k_sum):
        at = rows(i, 2 * block)
        grad = turn_back(dk_acc[at] * (1.0 / log2e), at)
        part, gain_part = norm_back(raw[at, qw:qw + kw], kg_ref[...], grad)
        d_qkv[at, qw:qw + kw] = part.astype(bf16)
        d_qkv[at, qw + kw:] = dv_acc[at].astype(bf16)
        return k_sum + gain_part

    gain_own[3:4, 0:head] = lax.fori_loop(0, n // 2, project_back, zero)

    weight_grad(4, [(first_t, lambda: d_qkv[...])])
    grad_near(3)
    drain(in_plane)
    sum_start(3, d_qkv, lambda left: dot_nt(left, w_qkv[...]))
    grad_far(3)
    grad_near(4)
    sum_start(2, hidden, lambda left: dot(left, w_down[...]))
    grad_far(4)
    for m in range(4):
        hand_out(m)
    x_part, gain_own[0:1, :] = norm_back(x_ref[...].astype(f32), ag_ref[...], sum_finish(3))
    dx_ref[...] = d_middle[...] + x_part

    def gain_plane_copy(j):
        return remote(gain_own, gain_plane.at[c], gp_send.at[j], gp_recv.at[j], partner(j), z)

    def gain_copy(d):
        return remote(gain_all.at[z], gain_all.at[z], gz_send.at[d], gz_recv.at[d], c, lax.rem(z + d, planes))

    for j in range(1, n):
        launch(in_plane, lambda j=j: gain_plane_copy(j))
    gain_plane[c] = gain_own[...]
    out_ref[...] = (middle[...] + sum_finish(2)).astype(bf16)
    for j in range(1, n):
        gain_plane_copy(j).wait_recv()
    total = gain_plane[0]
    for i in range(1, n):
        total = total + gain_plane[i]
    gain_all[z] = total
    for d in range(1, planes):
        launch(along, lambda d=d: gain_copy(d))
    for d in range(1, planes):
        origin = gain_all.at[lax.rem(z + planes - d, planes)]
        remote(origin, origin, gz_send.at[d], gz_recv.at[d], c, z).wait_recv()
    total = gain_all[0]
    for i in range(1, planes):
        total = total + gain_all[i]
    gains_ref[...] = total

    hand_out(4)
    for m in range(5):
        hand_receive(m)
    drain(in_plane)
    drain(along)


def finish_kernel(
    n, head, out_in, dx_in, gains_in, got_a, got_b, got_c, got_out, got_qkv,
    out_ref, dx_ref, ag_ref, q_ref, k_ref, v_ref, qg_ref, kg_ref, o_ref, fg_ref, g_ref, u_ref, d_ref,
):
    out_ref[...] = out_in[...]
    dx_ref[...] = dx_in[...]
    ag_ref[...] = gains_in[0:1, :]
    fg_ref[...] = gains_in[1:2, :]
    qg_ref[...] = gains_in[2:3, 0:head]
    kg_ref[...] = gains_in[3:4, 0:head]
    qw, kw = q_ref.shape[1] // n, k_ref.shape[1] // n
    pw = got_a.shape[2] // 3
    thirds = (got_a, got_b, got_c)
    for i in range(n):
        q_ref[:, i * qw:(i + 1) * qw] = got_qkv[i, :, 0:qw].astype(f32)
        k_ref[:, i * kw:(i + 1) * kw] = got_qkv[i, :, qw:qw + kw].astype(f32)
        v_ref[:, i * kw:(i + 1) * kw] = got_qkv[i, :, qw + kw:].astype(f32)
        o_ref[:, i * qw:(i + 1) * qw] = got_out[i].astype(f32)
        for t, got in enumerate(thirds):
            at = (i * len(thirds) + t) * pw
            g_ref[:, at:at + pw] = got[i, :, 0:pw].astype(f32)
            u_ref[:, at:at + pw] = got[i, :, pw:2 * pw].astype(f32)
            d_ref[:, at:at + pw] = got[i, :, 2 * pw:].astype(f32)


def plane_device(
    layer_input,
    token_positions,
    attention_gain,
    query_weight,
    key_matrix,
    value_matrix,
    query_gain,
    key_norm_gain,
    output_weight,
    feedforward_gain,
    gate_weight,
    up_weight,
    down_weight,
    out_cotangent,
):
    n = lax.axis_size("ctx")
    planes = lax.axis_size("fsdp")
    block, width = layer_input.shape[1:]
    length = token_positions.shape[1]
    head = query_gain.shape[0]
    qw = query_weight.shape[1] // n
    kw = key_matrix.shape[1] // n
    fw = gate_weight.shape[1] // n
    group = qw // head
    per = block // planes
    half = head // 2
    inverse = np.power(rope_base, -np.arange(half) * 2.0 / head).astype(np.float32)
    inverse = jnp.asarray(np.concatenate([inverse, inverse])[None])
    vmem = pl.BlockSpec(memory_space=pltpu.VMEM)
    hbm = pl.BlockSpec(memory_space=pl.ANY)
    dma = pltpu.SemaphoreType.DMA
    sizes = (fw, fw, fw, qw, qw + 2 * kw)
    low = lambda *shape: pltpu.VMEM(shape, bf16)
    wide = lambda *shape: pltpu.VMEM(shape, f32)
    scratch = [
        low(width, qw + 2 * kw), low(width, 2 * fw), low(qw, width), low(fw, width),
        low(planes * (output_weight.shape[0] // n), width), low(3, planes * 32, width),
        low(length, width), low(length, width), low(length, width),
        low(width, length), low(width, length), low(width, length), low(width, length),
        wide(length, head), wide(length, head), wide(length, head),
        wide(length, qw + kw), low(length, qw), low(length, kw), low(length, kw),
        low(kw, length), low(kw, length), low(n, length, group * block), wide(n, 1, group * block), wide(n, head, group * block), low(length, qw),
        low(length, fw), low(length, 2 * fw), low(length, qw + 2 * kw),
        wide(length, kw), wide(length, kw),
    ]
    scratch += [low(planes, n, per, size) for size in sizes]
    scratch += [low(planes + 1, n, per, size) for size in sizes]
    scratch += [low(2, 4, block, width) for _ in range(4)] + [wide(2, block, width), wide(2, block, width)]
    scratch += [
        wide(block, width), wide(block, width), wide(8, width), wide(n, 8, width), wide(planes, 8, width),
        dma((13,)), dma((8, 6)), dma((8, planes)), dma((4, 7)), dma((4, 4)),
        dma((4, n)), dma((4, n)), dma((4, 4)), dma((4, 4)), dma((4, 4)), dma((4, 4)),
        dma((5, planes)), dma((5, planes + 1)), dma((5, n)), dma((5, n)), dma((n,)), dma((n,)),
        dma((planes,)), dma((planes,)),
    ]
    shapes = [
        jax.ShapeDtypeStruct((block, width), bf16),
        jax.ShapeDtypeStruct((block, width), f32),
        jax.ShapeDtypeStruct((8, width), f32),
    ] + [jax.ShapeDtypeStruct((n, per, size), bf16) for size in sizes]
    results = pl.pallas_call(
        functools.partial(layer_kernel, n, planes, block, head, group, fw),
        out_shape=shapes,
        in_specs=[vmem] * 8 + [hbm] * 7,
        out_specs=[vmem] * len(shapes),
        scratch_shapes=scratch,
        compiler_params=pltpu.CompilerParams(
            collective_id=0, has_side_effects=True, vmem_limit_bytes=60 * 1024 * 1024),
    )(
        layer_input[0], out_cotangent[0], token_positions, inverse,
        attention_gain[None], feedforward_gain[None], query_gain[None], key_norm_gain[None],
        query_weight, key_matrix, value_matrix, output_weight, gate_weight, up_weight, down_weight,
    )
    plain = lambda rows, columns, kind=f32: jax.ShapeDtypeStruct((rows, columns), kind)
    finals = [
        plain(block, width, bf16), plain(block, width), plain(1, width),
        plain(per, n * qw), plain(per, n * kw), plain(per, n * kw), plain(1, head), plain(1, head),
        plain(per, n * qw), plain(1, width), plain(per, n * fw), plain(per, n * fw), plain(per, n * fw),
    ]
    done = pl.pallas_call(
        functools.partial(finish_kernel, n, head),
        out_shape=finals,
        in_specs=[vmem] * len(shapes),
        out_specs=[vmem] * len(finals),
    )(*results)
    out, dx, ag, q, k, v, qg, kg, o, fg, g, u, d = done
    return out[None], dx[None], ag[0], q, k, v, qg[0], kg[0], o.T, fg[0], g, u, d.T


def solution(mesh):
    in_specs = (
        P("fsdp", "ctx", None),
        P("fsdp", None),
        P(),
        P("fsdp", None),
        P("fsdp", None),
        P("fsdp", None),
        P(),
        P(),
        P("fsdp", None),
        P(),
        P("fsdp", None),
        P("fsdp", None),
        P("fsdp", None),
        P("fsdp", "ctx", None),
    )
    out_specs = (
        P("fsdp", "ctx", None),
        P("fsdp", "ctx", None),
        P(),
        P(("ctx", "fsdp"), None),
        P(("ctx", "fsdp"), None),
        P(("ctx", "fsdp"), None),
        P(),
        P(),
        P(None, ("ctx", "fsdp")),
        P(),
        P(("ctx", "fsdp"), None),
        P(("ctx", "fsdp"), None),
        P(None, ("ctx", "fsdp")),
    )

    def run(*arguments):
        n, planes = mesh.shape["ctx"], mesh.shape["fsdp"]
        key_heads = arguments[4].shape[1] // arguments[6].shape[0]
        whole_heads = n == 8 and planes == 4 and key_heads == n
        return jax.shard_map(
            plane_device if whole_heads else on_device,
            mesh=mesh, in_specs=in_specs, out_specs=out_specs, check_vma=False,
        )(*arguments)

    return run
```

```python
import functools

import jax
import jax.numpy as jnp
import numpy as np
from jax import lax
from jax.experimental import pallas as pl
from jax.experimental.pallas import tpu as pltpu
from jax.sharding import PartitionSpec as P

epsilon = 1e-06
rope_base = 1000000.0
masked_score = -1e30


def from_behind(block, axis, distance):
    devices = range(lax.axis_size(axis))
    route = [((i - distance) % len(devices), i) for i in devices]
    return lax.ppermute(block, axis, route)


def rotate(value_rows):
    half = value_rows.shape[-1] // 2
    return jnp.concatenate([-value_rows[..., half:], value_rows[..., :half]], -1)


def rotate_back(value_rows):
    half = value_rows.shape[-1] // 2
    return jnp.concatenate([value_rows[..., half:], -value_rows[..., :half]], -1)


def rope_tables(token_offsets, head_size):
    half = head_size // 2
    inverse = rope_base ** (-(jnp.arange(half).astype(jnp.float32) * 2.0) / head_size)
    angles = token_offsets.astype(jnp.float32)[:, None] * inverse[None, :]
    cosine = jnp.cos(angles)
    sine = jnp.sin(angles)
    return (jnp.concatenate([cosine, cosine], -1), jnp.concatenate([sine, sine], -1))


def norm_scale(value_rows):
    return lax.rsqrt(jnp.mean(value_rows * value_rows, -1, keepdims=True) + epsilon)


def norm_back(value_rows, scale, gain, grad):
    weighted = grad * gain
    inner = jnp.mean(weighted * value_rows, -1, keepdims=True)
    result = scale * weighted - value_rows * scale * scale * scale * inner
    gain_part = jnp.sum((grad * value_rows * scale).reshape(-1, gain.shape[0]), 0)
    return (result, gain_part)


def row_products(left, pieces):
    return tuple((jnp.dot(left, piece, preferred_element_type=jnp.float32) for piece in pieces))


def column_products(rights, pieces):
    total = jnp.einsum("tc,rc->tr", rights[0], pieces[0], preferred_element_type=jnp.float32)
    for right, piece in zip(rights[1:], pieces[1:]):
        total = total + jnp.einsum("tc,rc->tr", right, piece, preferred_element_type=jnp.float32)
    return total


def on_device(
    layer_input,
    token_positions,
    attention_gain,
    query_weight,
    key_matrix,
    value_matrix,
    query_gain,
    key_norm_gain,
    output_weight,
    feedforward_gain,
    gate_weight,
    up_weight,
    down_weight,
    out_cotangent,
):
    hidden_in = layer_input[0].astype(jnp.float32)
    count = hidden_in.shape[0]
    head_size = query_gain.shape[0]
    query_width = query_weight.shape[1]
    key_width = key_matrix.shape[1]
    inner_width = gate_weight.shape[1]
    heads = query_width // head_size
    key_heads = key_width // head_size
    group = heads // key_heads
    scale = head_size ** (-0.5)
    cycles = lax.axis_size("ctx")
    own_index = lax.axis_index("ctx")
    sequence_pos = token_positions[0]
    token_offsets = lax.dynamic_slice_in_dim(sequence_pos, own_index * count, count)
    cosine, sine = rope_tables(token_offsets, head_size)
    cosine = cosine[:, None, :]
    sine = sine[:, None, :]
    first_scale = norm_scale(hidden_in)
    first = (hidden_in * first_scale * attention_gain).astype(jnp.bfloat16)
    query_raw, key_unnormed, value_unnormed = row_products(
        first,
        (
            lax.all_gather(query_weight, "fsdp", axis=0, tiled=True),
            lax.all_gather(key_matrix, "fsdp", axis=0, tiled=True),
            lax.all_gather(value_matrix, "fsdp", axis=0, tiled=True),
        ),
    )
    query_heads = query_raw.reshape(count, heads, head_size)
    query_scale = norm_scale(query_heads)
    query_normed = query_heads * query_scale * query_gain
    query_rot = query_normed * cosine + rotate(query_normed) * sine
    query_grouped = (
        query_rot.reshape(count, key_heads, group, head_size)
        .transpose(1, 2, 0, 3)
        .astype(jnp.bfloat16)
    )
    key_heads_raw = key_unnormed.reshape(count, key_heads, head_size)
    key_scale = norm_scale(key_heads_raw)
    key_normed = key_heads_raw * key_scale * key_norm_gain
    key_low = (
        (key_normed * cosine + rotate(key_normed) * sine)
        .reshape(count, key_width)
        .astype(jnp.bfloat16)
    )
    value_low = value_unnormed.astype(jnp.bfloat16)
    rowmax = jnp.full((key_heads, group, count), masked_score, jnp.float32)
    keys_piece = lax.all_gather(key_low, "ctx", axis=0, tiled=True).reshape(
        -1, key_heads, head_size
    )
    values_piece = lax.all_gather(value_low, "ctx", axis=0, tiled=True).reshape(
        -1, key_heads, head_size
    )
    key_pos = sequence_pos
    allowed = token_offsets[:, None] >= key_pos[None, :]
    scores = (
        jnp.einsum("kgtd,skd->kgts", query_grouped, keys_piece, preferred_element_type=jnp.float32)
        * scale
    )
    scores = jnp.where(allowed, scores, masked_score)
    newmax = jnp.maximum(rowmax, jnp.max(scores, -1))
    weights = jnp.where(allowed, jnp.exp(scores - newmax[..., None]), 0.0)
    accum = jnp.einsum(
        "kgts,skd->kgtd",
        weights.astype(jnp.bfloat16),
        values_piece,
        preferred_element_type=jnp.float32,
    )
    rowsum = jnp.sum(weights, -1)
    accum, rowmax, rowsum = (accum, newmax, rowsum)
    normalized = accum / rowsum[..., None]
    logsum = rowmax + jnp.log(rowsum)
    attention_low = (
        normalized.transpose(2, 0, 1, 3).reshape(count, query_width).astype(jnp.bfloat16)
    )
    output_whole = lax.all_gather(output_weight, "fsdp", axis=0, tiled=True)
    branch_out = jnp.dot(attention_low, output_whole, preferred_element_type=jnp.float32)
    middle = hidden_in + branch_out
    second_scale = norm_scale(middle)
    second = (middle * second_scale * feedforward_gain).astype(jnp.bfloat16)
    gate, up = row_products(
        second,
        (
            lax.all_gather(gate_weight, "fsdp", axis=0, tiled=True),
            lax.all_gather(up_weight, "fsdp", axis=0, tiled=True),
        ),
    )
    sigmoid_gate = jax.nn.sigmoid(gate)
    silu_gate = gate * sigmoid_gate
    hidden_low = (silu_gate * up).astype(jnp.bfloat16)
    (down_out,) = row_products(
        hidden_low, (lax.all_gather(down_weight, "fsdp", axis=0, tiled=True),)
    )
    layer_output = (middle + down_out).astype(jnp.bfloat16)[None]
    cotangent = out_cotangent[0]
    hidden_grad = column_products(
        (cotangent,), lax.all_gather((down_weight,), "fsdp", axis=0, tiled=True)
    )
    up_low = (hidden_grad * silu_gate).astype(jnp.bfloat16)
    gate_low = (hidden_grad * up * sigmoid_gate * (1.0 + gate * (1.0 - sigmoid_gate))).astype(
        jnp.bfloat16
    )
    second_grad = column_products(
        (gate_low, up_low), lax.all_gather((gate_weight, up_weight), "fsdp", axis=0, tiled=True)
    )
    middle_part, feedforward_part = norm_back(middle, second_scale, feedforward_gain, second_grad)
    middle_grad = cotangent.astype(jnp.float32) + middle_part
    middle_low = middle_grad.astype(jnp.bfloat16)
    attention_grad = jnp.einsum(
        "tc,rc->tr", middle_low, output_whole, preferred_element_type=jnp.float32
    )
    attention_grad_low = attention_grad.astype(jnp.bfloat16)
    mixed_grad = attention_grad_low.reshape(count, key_heads, group, head_size).transpose(
        1, 2, 0, 3
    )
    delta = jnp.sum(mixed_grad.astype(jnp.float32) * normalized, -1)

    def cycle_step(index, carry):
        keys_held, values_held, key_acc, value_acc, query_acc = carry
        anchor = (own_index - index) % cycles
        key_pos = lax.dynamic_slice_in_dim(sequence_pos, anchor * count, count)
        keys_piece = keys_held.astype(jnp.bfloat16).reshape(count, key_heads, head_size)
        values_piece = values_held.astype(jnp.bfloat16).reshape(count, key_heads, head_size)
        allowed = token_offsets[:, None] >= key_pos[None, :]
        scores = (
            jnp.einsum(
                "kgtd,skd->kgts", query_grouped, keys_piece, preferred_element_type=jnp.float32
            )
            * scale
        )
        probs = jnp.where(allowed, jnp.exp(scores - logsum[..., None]), 0.0)
        value_acc = value_acc + jnp.einsum(
            "kgts,kgtd->skd",
            probs.astype(jnp.bfloat16),
            mixed_grad,
            preferred_element_type=jnp.float32,
        ).reshape(count, key_width)
        prob_grad = jnp.einsum(
            "kgtd,skd->kgts", mixed_grad, values_piece, preferred_element_type=jnp.float32
        )
        score_grad = (probs * (prob_grad - delta[..., None])).astype(jnp.bfloat16)
        query_acc = (
            query_acc
            + jnp.einsum(
                "kgts,skd->kgtd", score_grad, keys_piece, preferred_element_type=jnp.float32
            )
            * scale
        )
        key_acc = (
            key_acc
            + jnp.einsum(
                "kgts,kgtd->skd", score_grad, query_grouped, preferred_element_type=jnp.float32
            ).reshape(count, key_width)
            * scale
        )
        moved = (
            from_behind(keys_held.astype(jnp.bfloat16), "ctx", 1).astype(keys_held.dtype),
            from_behind(values_held.astype(jnp.bfloat16), "ctx", 1).astype(values_held.dtype),
            from_behind(key_acc.astype(jnp.bfloat16), "ctx", 1).astype(key_acc.dtype),
            from_behind(value_acc.astype(jnp.bfloat16), "ctx", 1).astype(value_acc.dtype),
        )
        return (moved[0], moved[1], moved[2], moved[3], query_acc)

    start_cycle = (
        key_low.astype(jnp.float32),
        value_low.astype(jnp.float32),
        jnp.zeros((count, key_width), jnp.float32),
        jnp.zeros((count, key_width), jnp.float32),
        jnp.zeros((key_heads, group, count, head_size), jnp.float32),
    )
    cycle_done = lax.fori_loop(0, cycles, cycle_step, start_cycle)
    key_acc = cycle_done[2]
    value_acc = cycle_done[3]
    query_acc = cycle_done[4]
    query_rot_grad = query_acc.transpose(2, 0, 1, 3).reshape(count, heads, head_size)
    query_normed_grad = query_rot_grad * cosine + rotate_back(query_rot_grad * sine)
    query_heads_grad, query_part = norm_back(
        query_heads, query_scale, query_gain, query_normed_grad
    )
    query_low_grad = query_heads_grad.reshape(count, query_width).astype(jnp.bfloat16)
    key_rot_grad = key_acc.reshape(count, key_heads, head_size)
    key_normed_grad = key_rot_grad * cosine + rotate_back(key_rot_grad * sine)
    key_heads_grad, key_part = norm_back(key_heads_raw, key_scale, key_norm_gain, key_normed_grad)
    key_low_grad = key_heads_grad.reshape(count, key_width).astype(jnp.bfloat16)
    value_low_grad = value_acc.astype(jnp.bfloat16)
    first_grad = column_products(
        (query_low_grad, key_low_grad, value_low_grad),
        lax.all_gather((query_weight, key_matrix, value_matrix), "fsdp", axis=0, tiled=True),
    )
    input_part, attention_part = norm_back(hidden_in, first_scale, attention_gain, first_grad)
    input_gradient = (middle_grad + input_part)[None]
    rights_first = jnp.concatenate([query_low_grad, key_low_grad, value_low_grad], 1)
    rights_second = jnp.concatenate([gate_low, up_low], 1)
    pairs = (
        (first, rights_first),
        (second, rights_second),
        (middle_low, attention_low),
        (cotangent, hidden_low),
    )
    parts = []
    for left, right in pairs:
        parts.append(jnp.einsum("tr,tc->rc", left, right, preferred_element_type=jnp.float32))
    sums = lax.psum_scatter(
        jnp.concatenate(parts, 1), ("ctx", "fsdp"), scatter_dimension=0, tiled=True
    )
    edges = [0, query_width, query_width + key_width, query_width + 2 * key_width]
    edges = edges + [edges[3] + inner_width, edges[3] + 2 * inner_width]
    edges = edges + [edges[5] + query_width, edges[5] + query_width + inner_width]
    query_gradient = sums[:, edges[0] : edges[1]]
    key_gradient = sums[:, edges[1] : edges[2]]
    value_gradient = sums[:, edges[2] : edges[3]]
    gate_gradient = sums[:, edges[3] : edges[4]]
    up_gradient = sums[:, edges[4] : edges[5]]
    output_gradient = sums[:, edges[5] : edges[6]].T
    down_gradient = sums[:, edges[6] : edges[7]].T
    attention_total, query_total, key_total, feedforward_total = lax.psum(
        (attention_part, query_part, key_part, feedforward_part), ("ctx", "fsdp")
    )
    return (
        layer_output,
        input_gradient,
        attention_total,
        query_gradient,
        key_gradient,
        value_gradient,
        query_total,
        key_total,
        output_gradient,
        feedforward_total,
        gate_gradient,
        up_gradient,
        down_gradient,
    )


MESH = pl.DeviceIdType.MESH
f32 = jnp.float32
bf16 = jnp.bfloat16


def dot(left, right):
    return jnp.dot(left, right, preferred_element_type=f32)


def dot_nt(left, right):
    return lax.dot_general(left, right, (((1,), (1,)), ((), ())), preferred_element_type=f32)


def dot_tn(left, right):
    return lax.dot_general(left, right, (((0,), (0,)), ((), ())), preferred_element_type=f32)


def layer_kernel(
    n, planes, block, head, group, fw,
    x_ref, dy_ref, pos_row, inverse_ref, step_cos, step_sin, ag_ref, fg_ref, qg_ref, kg_ref,
    wq, wk, wv, wo, wg, wu, wd,
    out_ref, dx_ref, gains_ref, got_a, got_b, got_c, got_out, got_qkv,
    w_qkv, w_gu, w_out, w_down, t_out, t_down,
    first, dy_all, second, first_t, dy_t, second_t, dmid_t,
    positions, cosine, sine,
    raw, queries, keys, values, keys_t, values_t, probs, sums, mixed_t, mixed_low,
    hidden, d_gu, d_qkv, dk_acc, dv_acc,
    stage_a, stage_b, stage_c, stage_out, stage_qkv,
    land_a, land_b, land_c, land_out, land_qkv,
    rs_sa, rs_ra, rs_sb, rs_rb, rs_kept, rs_acc,
    middle, d_middle, gain_own, gain_plane, gain_all,
    local_sem, wz_send, wz_recv, hand_send, hand_recv,
    ag_send, ag_recv, ra_send, ra_recv, rb_send, rb_recv,
    zr_send, zr_recv, aa_send, aa_recv, gp_send, gp_recv, gz_send, gz_recv,
):
    c = lax.axis_index("ctx")
    z = lax.axis_index("fsdp")
    dmid = first
    cy, cx, ck = lax.div(c, 4), lax.rem(lax.div(c, 2), 2), lax.rem(c, 2)
    ci = lax.rem(c, 4)
    sign = 1 - 2 * ck
    qw, kw = group * head, head
    pw = 128
    thirds = fw // pw
    piece = pw // 4
    width = x_ref.shape[1]
    scale = head ** (-0.5)
    log2e = 1.4426950408889634
    gots = (got_a, got_b, got_c, got_out, got_qkv)
    stages = (stage_a, stage_b, stage_c, stage_out, stage_qkv)
    lands = (land_a, land_b, land_c, land_out, land_qkv)

    def partner(j):
        y = lax.rem(cy + lax.div(j, 4), 2)
        x = lax.rem(cx + lax.rem(lax.div(j, 2), 2), 2)
        k = lax.rem(ck + lax.rem(j, 2), 2)
        return y * 4 + x * 2 + k

    def chip(slot):
        return lax.rem(cy + lax.div(slot, 2), 2) * 2 + lax.rem(cx + lax.rem(slot, 2), 2)

    def rows(start, size):
        return pl.ds(pl.multiple_of(start * size, size), size)

    def remote(src, dst, send, recv, ctx, plane):
        return pltpu.make_async_remote_copy(
            src_ref=src, dst_ref=dst, send_sem=send, recv_sem=recv,
            device_id={"ctx": ctx, "fsdp": plane}, device_id_type=MESH,
        )

    in_plane, along = [], []

    def launch(started, copy, when=None):
        if when is None:
            copy().start()
        else:
            pl.when(when)(lambda: copy().start())
        started.append((copy, when))

    def drain(started):
        for copy, when in started:
            if when is None:
                copy().wait_send()
            else:
                pl.when(when)(lambda copy=copy: copy().wait_send())
        started.clear()

    own_rows = wq.shape[0]
    out_rows = wo.shape[0] // n

    def own_slices():
        mine = rows(z, own_rows)
        pairs = [
            (wq.at[:, rows(c, qw)], w_qkv.at[mine, 0:qw]),
            (wk.at[:, rows(c, kw)], w_qkv.at[mine, qw:qw + kw]),
            (wv.at[:, rows(c, kw)], w_qkv.at[mine, qw + kw:qw + 2 * kw]),
            (wo.at[rows(c, out_rows)], t_out.at[rows(z, out_rows)]),
        ]
        for t in range(thirds):
            at = 2 * pw * t
            pairs.append((wg.at[:, rows(c * thirds + t, pw)], w_gu.at[mine, at:at + pw]))
            pairs.append((wu.at[:, rows(c * thirds + t, pw)], w_gu.at[mine, at + pw:at + 2 * pw]))
            pairs.append((wd.at[rows((cy * thirds + t) * 4 + ci, piece)], t_down.at[t, rows(z, piece)]))
        return pairs

    local = [pltpu.make_async_copy(src, dst, local_sem.at[i]) for i, (src, dst) in enumerate(own_slices())]
    for copy in local:
        copy.start()

    for land in lands:
        @pl.when(z == 0)
        def _(land=land):
            land[0] = jnp.zeros(land.shape[1:], bf16)

        @pl.when(z == planes - 1)
        def _(land=land):
            land[planes] = jnp.zeros(land.shape[1:], bf16)

    barrier = pltpu.get_barrier_semaphore()
    for j in range(1, n):
        pl.semaphore_signal(barrier, inc=1, device_id={"ctx": partner(j), "fsdp": z}, device_id_type=MESH)
    for d in range(1, planes):
        pl.semaphore_signal(
            barrier, inc=1, device_id={"ctx": c, "fsdp": lax.rem(z + d, planes)}, device_id_type=MESH)
    x = x_ref[...].astype(f32)
    x_scale = lax.rsqrt(jnp.mean(x * x, -1, keepdims=True) + epsilon)
    first[rows(c, block)] = (x * x_scale * ag_ref[...]).astype(bf16)
    dy_all[rows(c, block)] = dy_ref[...]
    for copy in local[:3]:
        copy.wait()
    pl.semaphore_wait(barrier, n + planes - 2)

    def inside(t):
        return jnp.logical_and(t >= 0, t < planes)

    weights = [
        (lambda o: w_qkv.at[rows(o, own_rows)], None),
        (lambda o: t_out.at[rows(o, out_rows)], 0),
    ]
    for t in range(thirds):
        weights.append((lambda o, t=t: w_gu.at[rows(o, own_rows), 2 * pw * t:2 * pw * (t + 1)], None))
        weights.append((lambda o, t=t: t_down.at[t, rows(o, piece)], 1 + t))

    def weight_copy(w, slot, origin, target):
        part = weights[w][0](origin)
        return remote(part, part, wz_send.at[w, slot], wz_recv.at[w, origin], c, target)

    def weight_start(w):
        for side in range(2):
            d = sign * (1 - 2 * side)
            launch(along, lambda side=side, d=d: weight_copy(w, side, z, z + d), inside(z + d))
        if weights[w][1] is not None:
            hand_over(w, z, 0, None)

    def hand_target(h):
        if h == 0:
            return lambda i: w_out.at[rows(i, out_rows)]
        return lambda i: w_down.at[rows((h - 1) * 4 + i, piece)]

    def hand_copy(w, origin, slot):
        h = weights[w][1]
        return remote(
            weights[w][0](origin), hand_target(h)(ci), hand_send.at[h, slot], hand_recv.at[h, ci], 2 * origin + cy, z)

    def hand_over(w, origin, slot, valid):
        away = 2 * origin + cy != c
        here = jnp.logical_not(away)
        if valid is not None:
            away, here = jnp.logical_and(valid, away), jnp.logical_and(valid, here)
        launch(in_plane, lambda: hand_copy(w, origin, slot), away)

        @pl.when(here)
        def _():
            hand_target(weights[w][1])(ci)[...] = weights[w][0](origin)[...]

    def hand_arrive(w):
        h = weights[w][1]
        for i in range(4):
            @pl.when(4 * ck + i != c)
            def _(i=i):
                part = hand_target(h)(i)
                remote(part, part, hand_send.at[h, 0], hand_recv.at[h, i], c, z).wait_recv()

    def weight_hop(w, d):
        for side, way in enumerate((1, -1)):
            origin = z - way * d
            valid = inside(origin)
            pl.when(valid)(lambda origin=origin: weight_copy(w, 0, origin, z).wait_recv())
            if d < planes - 1:
                launch(
                    along,
                    lambda side=side, way=way, origin=origin: weight_copy(w, 2 * d + side, origin, z + way),
                    jnp.logical_and(valid, inside(z + way)))
            if weights[w][1] is not None:
                hand_over(w, origin, 2 * d - 1 + side, valid)

    def gather_copy(buf, g, j, send, origin, target):
        part = buf.at[rows(origin, block)]
        return remote(part, part, ag_send.at[g, send], ag_recv.at[g, j], target, z)

    def gather_start(buf, g):
        for j in (1, 2 + 2 * ck, 4 - 2 * ck, 6):
            launch(in_plane, lambda j=j: gather_copy(buf, g, j, j, c, partner(j)))

    def gather_forward(buf, g, j):
        return gather_copy(buf, g, j + 1, j + 1, partner(j), partner(1))

    def gather_finish(buf, g):
        for j in (2, 4, 6):
            gather_copy(buf, g, j, j, partner(j), c).wait_recv()
            launch(in_plane, lambda j=j: gather_forward(buf, g, j))
        for j in (1, 3, 5, 7):
            gather_copy(buf, g, j, j, partner(j), c).wait_recv()

    def gather_step(buf, g, slot):
        def arrive(j):
            gather_copy(buf, g, j, j, partner(j), c).wait_recv()
            gather_forward(buf, g, j).start()

        @pl.when(slot == 1)
        def _():
            arrive(2)
            arrive(4)

        @pl.when(slot == 3)
        def _():
            arrive(6)

        gather_copy(buf, g, 2 * slot + 1, 0, partner(2 * slot + 1), c).wait_recv()

    def gather_stepped(buf, g):
        for j in (2, 4, 6):
            in_plane.append((lambda j=j: gather_forward(buf, g, j), None))

    def sum_pair_copy(s, slot):
        return remote(rs_sa.at[s % 2, slot], rs_ra.at[s % 2, slot], ra_send.at[s, slot], ra_recv.at[s, slot], partner(1), z)

    def sum_chip_copy(s, slot):
        return remote(
            rs_sb.at[s % 2, slot], rs_rb.at[s % 2, slot], rb_send.at[s, slot], rb_recv.at[s, slot], partner(2 * slot), z)

    def sum_slot(p):
        return jnp.where(p == 0, 3, jnp.where(p == 1, 2 - ck, jnp.where(p == 2, 1 + ck, 0)))

    def sum_start(s, left, partial, prepare=None, ready=None):
        if prepare is not None:
            prepare(chip(sum_slot(0)))
        if ready is not None:
            ready()

        def body(p, carry):
            slot = sum_slot(p)
            at = [rows(partner(2 * slot + 1), block), rows(partner(2 * slot), block)]
            both = partial(jnp.concatenate([left[i] for i in at], 0))
            rs_sa[s % 2, slot] = both[:block].astype(bf16)
            sum_pair_copy(s, slot).start()
            rs_kept[lax.rem(p, 2)] = both[block:]
            if prepare is not None:
                @pl.when(p < 3)
                def _():
                    prepare(chip(sum_slot(p + 1)))

            @pl.when(p > 0)
            def _():
                before = sum_slot(p - 1)
                sum_pair_copy(s, before).wait_recv()
                rs_sb[s % 2, before] = (
                    rs_kept[lax.rem(p + 1, 2)] + rs_ra[s % 2, before].astype(f32)).astype(bf16)
                sum_chip_copy(s, before).start()

            return carry

        lax.fori_loop(0, 4, body, 0)
        for slot in range(4):
            in_plane.append((lambda slot=slot: sum_pair_copy(s, slot), None))
            if slot > 0:
                in_plane.append((lambda slot=slot: sum_chip_copy(s, slot), None))
        sum_pair_copy(s, 0).wait_recv()
        rs_acc[s % 2] = rs_kept[1] + rs_ra[s % 2, 0].astype(f32)

    def sum_finish(s):
        total = rs_acc[s % 2]
        for slot in (1, 2, 3):
            sum_chip_copy(s, slot).wait_recv()
            total = total + rs_rb[s % 2, slot].astype(f32)
        return total

    per = block // planes

    def weight_grad(m, parts):
        def body(i, carry):
            at = 0
            for left, right in parts:
                value = right()
                grad = dot(left[rows(i, 2 * block)], value)
                for k in range(2):
                    for t in range(planes):
                        start = k * block + t * per
                        stages[m][t, 2 * i + k, :, at:at + value.shape[1]] = grad[start:start + per].astype(bf16)
                at += value.shape[1]
            return carry

        lax.fori_loop(0, n // 2, body, 0)
        at_edge = jnp.logical_or(z == 0, z == planes - 1)
        for k in range(planes - 1):
            t = jnp.where(z == 0, planes - 1 - k, k)
            launch(along, lambda t=t: grad_copy(m, t), at_edge)

    def grad_copy(m, t):
        way = jnp.where(z < t, 1, -1)
        last = z + way == t
        slot = jnp.where(jnp.logical_and(last, way < 0), planes, t)
        return remote(
            stages[m].at[t], lands[m].at[slot], zr_send.at[m, t], zr_recv.at[m, slot], c, z + way)

    def grad_arrive(m, slot):
        part = lands[m].at[slot]
        remote(part, part, zr_send.at[m, 0], zr_recv.at[m, slot], c, z).wait_recv()

    def grad_pass(m, t, valid):
        @pl.when(valid)
        def _():
            grad_arrive(m, t)

            def body(i, carry):
                stages[m][t, i] = (stages[m][t, i].astype(f32) + lands[m][t, i].astype(f32)).astype(bf16)
                return carry

            lax.fori_loop(0, n, body, 0)

        launch(along, lambda: grad_copy(m, t), valid)

    def grad_near(m):
        for t in (3, 2):
            grad_pass(m, t, z == 1)
        for t in (0, 1):
            grad_pass(m, t, z == 2)

    def grad_far(m):
        grad_pass(m, 3, z == 2)
        grad_pass(m, 0, z == 1)

    def owner_copy(m, j):
        return remote(lands[m].at[z, partner(j)], gots[m].at[c], aa_send.at[m, j], aa_recv.at[m, j], partner(j), z)

    def hand_out(m):
        pl.when(z > 0)(lambda: grad_arrive(m, z))
        pl.when(z < planes - 1)(lambda: grad_arrive(m, planes))

        def body(i, carry):
            total = stages[m][z, i].astype(f32) + lands[m][z, i].astype(f32) + lands[m][planes, i].astype(f32)
            lands[m][z, i] = total.astype(bf16)
            return carry

        lax.fori_loop(0, n, body, 0)
        for j in (2 + 2 * ck, 3 + 2 * ck, 4 - 2 * ck, 5 - 2 * ck, 6, 7, 1):
            launch(in_plane, lambda j=j: owner_copy(m, j))
        gots[m][c] = lands[m][z, c]

    def hand_receive(m):
        for j in range(1, n):
            owner_copy(m, j).wait_recv()

    weight_start(0)
    gather_start(first, 0)
    for copy in local[3:]:
        copy.wait()

    spread = jnp.broadcast_to(pos_row[...].astype(f32), (head, pos_row.shape[1]))
    positions[...] = spread.T
    side = jnp.where(lax.broadcasted_iota(jnp.int32, (1, head), 1) < head // 2, -1.0, 1.0)

    def table(i, carry):
        run = step_cos.shape[0]
        at = rows(i, run)
        start = positions[pl.ds(pl.multiple_of(i * run, run), 1)] * inverse_ref[...]
        start_cos, start_sin = jnp.cos(start), jnp.sin(start)
        cosine[at] = start_cos * step_cos[...] - start_sin * step_sin[...]
        sine[at] = (start_sin * step_cos[...] + start_cos * step_sin[...]) * side
        return carry

    def turn_over(src, dst):
        def body(i, carry):
            at = rows(i, block)
            dst[:, at] = src[at].T
            return carry

        lax.fori_loop(0, n, body, 0)

    lax.fori_loop(0, 2 * n, table, 0)
    weight_hop(0, 1)
    gather_finish(first, 0)
    weight_hop(0, 2)
    weight_start(1)
    gather_start(dy_all, 1)
    turn_over(first, first_t)
    weight_hop(0, 3)
    weight_start(2)
    weight_start(3)

    def turn(value, at):
        return value * cosine[at] + pltpu.roll(value, head // 2, 1) * sine[at]

    def turn_back(grad, at):
        return grad * cosine[at] - pltpu.roll(grad, head // 2, 1) * sine[at]

    def project(i, carry):
        at = rows(i, 2 * block)
        result = dot(first[at], w_qkv[...])
        raw[at] = result[:, :qw + kw]
        low_values = result[:, qw + kw:].astype(bf16)
        values[at] = low_values
        values_t[:, at] = low_values.T
        for h in range(group + 1):
            part = result[:, h * head:(h + 1) * head]
            inv = lax.rsqrt(jnp.mean(part * part, -1, keepdims=True) + epsilon)
            gain = qg_ref[...] if h < group else kg_ref[...]
            turned = turn(part * inv * gain, at)
            if h < group:
                queries[at, h * head:(h + 1) * head] = (turned * (scale * log2e)).astype(bf16)
            else:
                low_keys = turned.astype(bf16)
                keys[at] = low_keys
                keys_t[:, at] = low_keys.T
        return carry

    lax.fori_loop(0, n // 2, project, 0)
    weight_hop(1, 1)
    gather_finish(dy_all, 1)
    turn_over(dy_all, dy_t)
    weight_hop(1, 2)

    def stack(ref, at):
        return jnp.concatenate([ref[at, h * head:(h + 1) * head] for h in range(group)], 0)

    def attend_block(i):
        at = rows(i, block)
        scores = dot_nt(keys[...], stack(queries, at))
        allowed = positions[...] <= pos_row[:, at].astype(f32)
        weight = jnp.concatenate(
            [jnp.exp2(jnp.where(allowed, scores[:, h * block:(h + 1) * block], masked_score)) for h in range(group)], 1)
        inv = 1.0 / jnp.sum(weight, 0, keepdims=True)
        low_weight = weight.astype(bf16)
        probs[i] = low_weight
        sums[i] = inv
        result = dot(values_t[...], low_weight) * inv
        mixed_t[i] = result
        for h in range(group):
            mixed_low[at, h * head:(h + 1) * head] = result[:, h * block:(h + 1) * block].T.astype(bf16)

    def attend(place):
        attend_block(2 * place)
        attend_block(2 * place + 1)

    def output_ready():
        weight_hop(1, 3)
        weight_hop(2, 1)
        weight_hop(3, 1)
        weight_start(4)
        weight_start(5)
        hand_arrive(1)
        drain(in_plane)

    sum_start(0, mixed_low, lambda left: dot(left, w_out[...]), attend, output_ready)
    weight_hop(2, 2)
    weight_hop(3, 2)
    weight_start(6)
    weight_start(7)
    mid = x_ref[...].astype(f32) + sum_finish(0)
    middle[...] = mid
    mid_scale = lax.rsqrt(jnp.mean(mid * mid, -1, keepdims=True) + epsilon)
    second[rows(c, block)] = (mid * mid_scale * fg_ref[...]).astype(bf16)
    gather_start(second, 2)
    weight_hop(2, 3)
    weight_hop(3, 3)
    hand_arrive(3)
    weight_hop(4, 1)
    weight_hop(5, 1)

    def feed(t, at):
        units, pair = slice(t * pw, (t + 1) * pw), 2 * pw * t
        both = dot(second[at], w_gu[:, pair:pair + 2 * pw])
        back = dot_nt(dy_all[at], w_down[units])
        gate, up = both[:, :pw], both[:, pw:]
        sig = 1.0 / (1.0 + jnp.exp(-gate))
        silu = gate * sig
        hidden[at, units] = (silu * up).astype(bf16)
        d_gu[at, pair:pair + pw] = (back * up * sig * (1.0 + gate * (1.0 - sig))).astype(bf16)
        d_gu[at, pair + pw:pair + 2 * pw] = (back * silu).astype(bf16)

    def feed_arriving(slot, carry):
        gather_step(second, 2, slot)
        at = rows(chip(slot), 2 * block)
        feed(0, at)
        second_t[:, at] = second[at].T
        return carry

    def third_grad(t):
        weight_grad(t, [
            (second_t, lambda: d_gu[:, 2 * pw * t:2 * pw * (t + 1)]),
            (dy_t, lambda: hidden[:, t * pw:(t + 1) * pw]),
        ])

    def feed_third(t):
        def body(i, carry):
            feed(t, rows(i, 2 * block))
            return carry

        lax.fori_loop(0, n // 2, body, 0)

    lax.fori_loop(0, n // 2, feed_arriving, 0)
    gather_stepped(second, 2)
    weight_hop(4, 2)
    weight_hop(5, 2)
    weight_hop(6, 1)
    weight_hop(7, 1)
    third_grad(0)
    weight_hop(4, 3)
    weight_hop(5, 3)
    hand_arrive(5)
    feed_third(1)
    weight_hop(6, 2)
    weight_hop(7, 2)
    third_grad(1)
    grad_near(0)
    weight_hop(6, 3)
    weight_hop(7, 3)
    hand_arrive(7)
    sum_start(
        1, d_gu, lambda left: dot_nt(left, w_gu[...]),
        lambda place: feed(thirds - 1, rows(place, 2 * block)))
    third_grad(2)
    grad_far(0)
    grad_near(1)
    d_second = sum_finish(1)

    def norm_back(value, gain, grad):
        inv = lax.rsqrt(jnp.mean(value * value, -1, keepdims=True) + epsilon)
        weighted = grad * gain
        inner = jnp.mean(weighted * value, -1, keepdims=True)
        result = inv * weighted - value * (inv * inv * inv * inner)
        return result, jnp.sum(grad * value * inv, 0, keepdims=True)

    gain_own[...] = jnp.zeros_like(gain_own)
    part, gain_own[1:2, :] = norm_back(middle[...], fg_ref[...], d_second)
    d_mid = dy_ref[...].astype(f32) + part
    d_middle[...] = d_mid
    dmid[rows(c, block)] = d_mid.astype(bf16)
    gather_start(dmid, 3)
    grad_far(1)
    grad_near(2)

    dk_acc[...] = jnp.zeros_like(dk_acc)
    dv_acc[...] = jnp.zeros_like(dv_acc)

    def attend_back_block(i, d_mix):
        at = rows(i, block)
        d_mix_t = jnp.concatenate([d_mix[h * head:(h + 1) * head] for h in range(group)], 1)
        d_mix_t = (d_mix_t.astype(bf16).astype(f32) * sums[i]).astype(bf16)
        delta = jnp.sum(d_mix_t.astype(f32) * mixed_t[i], 0, keepdims=True)
        weight = probs[i]
        d_prob = dot(values[...], d_mix_t)
        d_score = (weight.astype(f32) * (d_prob - delta)).astype(bf16)
        d_query = dot(keys_t[...], d_score) * scale
        gained = jnp.zeros((1, head), f32)
        for h in range(group):
            grad = turn_back(d_query[:, h * block:(h + 1) * block].T, at)
            part, gain_part = norm_back(raw[at, h * head:(h + 1) * head], qg_ref[...], grad)
            d_qkv[at, h * head:(h + 1) * head] = part.astype(bf16)
            gained = gained + gain_part
        return dot(weight, d_mix_t.T), dot(d_score, stack(queries, at)), gained

    def attend_back(slot, q_sum):
        gather_step(dmid, 3, slot)
        at = rows(chip(slot), 2 * block)
        d_mix = dot_nt(w_out[...], dmid[at])
        dmid_t[:, at] = dmid[at].T
        dv_one, dk_one, gain_one = attend_back_block(2 * chip(slot), d_mix[:, :block])
        dv_two, dk_two, gain_two = attend_back_block(2 * chip(slot) + 1, d_mix[:, block:])
        dv_acc[...] += dv_one + dv_two
        dk_acc[...] += dk_one + dk_two
        return q_sum + gain_one + gain_two

    zero = jnp.zeros((1, head), f32)
    gain_own[2:3, 0:head] = lax.fori_loop(0, n // 2, attend_back, zero)
    gather_stepped(dmid, 3)
    weight_grad(3, [(dmid_t, lambda: mixed_low[...])])
    grad_far(2)

    def project_back(i, k_sum):
        at = rows(i, 2 * block)
        grad = turn_back(dk_acc[at] * (1.0 / log2e), at)
        part, gain_part = norm_back(raw[at, qw:qw + kw], kg_ref[...], grad)
        d_qkv[at, qw:qw + kw] = part.astype(bf16)
        d_qkv[at, qw + kw:] = dv_acc[at].astype(bf16)
        return k_sum + gain_part

    gain_own[3:4, 0:head] = lax.fori_loop(0, n // 2, project_back, zero)

    weight_grad(4, [(first_t, lambda: d_qkv[...])])
    grad_near(3)
    drain(in_plane)
    sum_start(3, d_qkv, lambda left: dot_nt(left, w_qkv[...]))
    grad_far(3)
    grad_near(4)
    sum_start(2, hidden, lambda left: dot(left, w_down[...]))
    grad_far(4)
    for m in range(4):
        hand_out(m)
    x_part, gain_own[0:1, :] = norm_back(x_ref[...].astype(f32), ag_ref[...], sum_finish(3))
    dx_ref[...] = d_middle[...] + x_part

    def gain_plane_copy(j):
        return remote(gain_own, gain_plane.at[c], gp_send.at[j], gp_recv.at[j], partner(j), z)

    def gain_copy(d):
        return remote(gain_all.at[z], gain_all.at[z], gz_send.at[d], gz_recv.at[d], c, lax.rem(z + d, planes))

    for j in range(1, n):
        launch(in_plane, lambda j=j: gain_plane_copy(j))
    gain_plane[c] = gain_own[...]
    out_ref[...] = (middle[...] + sum_finish(2)).astype(bf16)
    for j in range(1, n):
        gain_plane_copy(j).wait_recv()
    total = gain_plane[0]
    for i in range(1, n):
        total = total + gain_plane[i]
    gain_all[z] = total
    for d in range(1, planes):
        launch(along, lambda d=d: gain_copy(d))
    for d in range(1, planes):
        origin = gain_all.at[lax.rem(z + planes - d, planes)]
        remote(origin, origin, gz_send.at[d], gz_recv.at[d], c, z).wait_recv()
    total = gain_all[0]
    for i in range(1, planes):
        total = total + gain_all[i]
    gains_ref[...] = total

    hand_out(4)
    for m in range(5):
        hand_receive(m)
    drain(in_plane)
    drain(along)


def finish_kernel(
    n, head, out_in, dx_in, gains_in, got_a, got_b, got_c, got_out, got_qkv,
    out_ref, dx_ref, ag_ref, q_ref, k_ref, v_ref, qg_ref, kg_ref, o_ref, fg_ref, g_ref, u_ref, d_ref,
):
    out_ref[...] = out_in[...]
    dx_ref[...] = dx_in[...]
    ag_ref[...] = gains_in[0:1, :]
    fg_ref[...] = gains_in[1:2, :]
    qg_ref[...] = gains_in[2:3, 0:head]
    kg_ref[...] = gains_in[3:4, 0:head]
    qw, kw = q_ref.shape[1] // n, k_ref.shape[1] // n
    pw = got_a.shape[2] // 3
    thirds = (got_a, got_b, got_c)
    for i in range(n):
        q_ref[:, i * qw:(i + 1) * qw] = got_qkv[i, :, 0:qw].astype(f32)
        k_ref[:, i * kw:(i + 1) * kw] = got_qkv[i, :, qw:qw + kw].astype(f32)
        v_ref[:, i * kw:(i + 1) * kw] = got_qkv[i, :, qw + kw:].astype(f32)
        o_ref[:, i * qw:(i + 1) * qw] = got_out[i].astype(f32)
        for t, got in enumerate(thirds):
            at = (i * len(thirds) + t) * pw
            g_ref[:, at:at + pw] = got[i, :, 0:pw].astype(f32)
            u_ref[:, at:at + pw] = got[i, :, pw:2 * pw].astype(f32)
            d_ref[:, at:at + pw] = got[i, :, 2 * pw:].astype(f32)


def plane_device(
    layer_input,
    token_positions,
    attention_gain,
    query_weight,
    key_matrix,
    value_matrix,
    query_gain,
    key_norm_gain,
    output_weight,
    feedforward_gain,
    gate_weight,
    up_weight,
    down_weight,
    out_cotangent,
):
    n = lax.axis_size("ctx")
    planes = lax.axis_size("fsdp")
    block, width = layer_input.shape[1:]
    length = token_positions.shape[1]
    head = query_gain.shape[0]
    qw = query_weight.shape[1] // n
    kw = key_matrix.shape[1] // n
    fw = gate_weight.shape[1] // n
    group = qw // head
    per = block // planes
    half = head // 2
    inverse = np.power(rope_base, -np.arange(half) * 2.0 / head).astype(np.float32)
    inverse = np.concatenate([inverse, inverse])[None]
    steps = np.arange(block // 2)[:, None] * inverse.astype(np.float64)
    step_cos, step_sin = (jnp.asarray(f(steps).astype(np.float32)) for f in (np.cos, np.sin))
    inverse = jnp.asarray(inverse)
    vmem = pl.BlockSpec(memory_space=pltpu.VMEM)
    hbm = pl.BlockSpec(memory_space=pl.ANY)
    dma = pltpu.SemaphoreType.DMA
    sizes = (fw, fw, fw, qw, qw + 2 * kw)
    low = lambda *shape: pltpu.VMEM(shape, bf16)
    wide = lambda *shape: pltpu.VMEM(shape, f32)
    scratch = [
        low(width, qw + 2 * kw), low(width, 2 * fw), low(qw, width), low(fw, width),
        low(planes * (output_weight.shape[0] // n), width), low(3, planes * 32, width),
        low(length, width), low(length, width), low(length, width),
        low(width, length), low(width, length), low(width, length), low(width, length),
        wide(length, head), wide(length, head), wide(length, head),
        wide(length, qw + kw), low(length, qw), low(length, kw), low(length, kw),
        low(kw, length), low(kw, length), low(n, length, group * block), wide(n, 1, group * block), wide(n, head, group * block), low(length, qw),
        low(length, fw), low(length, 2 * fw), low(length, qw + 2 * kw),
        wide(length, kw), wide(length, kw),
    ]
    scratch += [low(planes, n, per, size) for size in sizes]
    scratch += [low(planes + 1, n, per, size) for size in sizes]
    scratch += [low(2, 4, block, width) for _ in range(4)] + [wide(2, block, width), wide(2, block, width)]
    scratch += [
        wide(block, width), wide(block, width), wide(8, width), wide(n, 8, width), wide(planes, 8, width),
        dma((13,)), dma((8, 6)), dma((8, planes)), dma((4, 7)), dma((4, 4)),
        dma((4, n)), dma((4, n)), dma((4, 4)), dma((4, 4)), dma((4, 4)), dma((4, 4)),
        dma((5, planes)), dma((5, planes + 1)), dma((5, n)), dma((5, n)), dma((n,)), dma((n,)),
        dma((planes,)), dma((planes,)),
    ]
    shapes = [
        jax.ShapeDtypeStruct((block, width), bf16),
        jax.ShapeDtypeStruct((block, width), f32),
        jax.ShapeDtypeStruct((8, width), f32),
    ] + [jax.ShapeDtypeStruct((n, per, size), bf16) for size in sizes]
    results = pl.pallas_call(
        functools.partial(layer_kernel, n, planes, block, head, group, fw),
        out_shape=shapes,
        in_specs=[vmem] * 10 + [hbm] * 7,
        out_specs=[vmem] * len(shapes),
        scratch_shapes=scratch,
        compiler_params=pltpu.CompilerParams(
            collective_id=0, has_side_effects=True, vmem_limit_bytes=60 * 1024 * 1024),
    )(
        layer_input[0], out_cotangent[0], token_positions, inverse, step_cos, step_sin,
        attention_gain[None], feedforward_gain[None], query_gain[None], key_norm_gain[None],
        query_weight, key_matrix, value_matrix, output_weight, gate_weight, up_weight, down_weight,
    )
    plain = lambda rows, columns, kind=f32: jax.ShapeDtypeStruct((rows, columns), kind)
    finals = [
        plain(block, width, bf16), plain(block, width), plain(1, width),
        plain(per, n * qw), plain(per, n * kw), plain(per, n * kw), plain(1, head), plain(1, head),
        plain(per, n * qw), plain(1, width), plain(per, n * fw), plain(per, n * fw), plain(per, n * fw),
    ]
    done = pl.pallas_call(
        functools.partial(finish_kernel, n, head),
        out_shape=finals,
        in_specs=[vmem] * len(shapes),
        out_specs=[vmem] * len(finals),
    )(*results)
    out, dx, ag, q, k, v, qg, kg, o, fg, g, u, d = done
    return out[None], dx[None], ag[0], q, k, v, qg[0], kg[0], o.T, fg[0], g, u, d.T


def solution(mesh):
    in_specs = (
        P("fsdp", "ctx", None),
        P("fsdp", None),
        P(),
        P("fsdp", None),
        P("fsdp", None),
        P("fsdp", None),
        P(),
        P(),
        P("fsdp", None),
        P(),
        P("fsdp", None),
        P("fsdp", None),
        P("fsdp", None),
        P("fsdp", "ctx", None),
    )
    out_specs = (
        P("fsdp", "ctx", None),
        P("fsdp", "ctx", None),
        P(),
        P(("ctx", "fsdp"), None),
        P(("ctx", "fsdp"), None),
        P(("ctx", "fsdp"), None),
        P(),
        P(),
        P(None, ("ctx", "fsdp")),
        P(),
        P(("ctx", "fsdp"), None),
        P(("ctx", "fsdp"), None),
        P(None, ("ctx", "fsdp")),
    )

    def run(*arguments):
        n, planes = mesh.shape["ctx"], mesh.shape["fsdp"]
        key_heads = arguments[4].shape[1] // arguments[6].shape[0]
        whole_heads = n == 8 and planes == 4 and key_heads == n
        return jax.shard_map(
            plane_device if whole_heads else on_device,
            mesh=mesh, in_specs=in_specs, out_specs=out_specs, check_vma=False,
        )(*arguments)

    return run
```

```python
import functools

import jax
import jax.numpy as jnp
import numpy as np
from jax import lax
from jax.experimental import pallas as pl
from jax.experimental.pallas import tpu as pltpu
from jax.sharding import PartitionSpec as P

epsilon = 1e-06
rope_base = 1000000.0
masked_score = -1e30


def from_behind(block, axis, distance):
    devices = range(lax.axis_size(axis))
    route = [((i - distance) % len(devices), i) for i in devices]
    return lax.ppermute(block, axis, route)


def rotate(value_rows):
    half = value_rows.shape[-1] // 2
    return jnp.concatenate([-value_rows[..., half:], value_rows[..., :half]], -1)


def rotate_back(value_rows):
    half = value_rows.shape[-1] // 2
    return jnp.concatenate([value_rows[..., half:], -value_rows[..., :half]], -1)


def rope_tables(token_offsets, head_size):
    half = head_size // 2
    inverse = rope_base ** (-(jnp.arange(half).astype(jnp.float32) * 2.0) / head_size)
    angles = token_offsets.astype(jnp.float32)[:, None] * inverse[None, :]
    cosine = jnp.cos(angles)
    sine = jnp.sin(angles)
    return (jnp.concatenate([cosine, cosine], -1), jnp.concatenate([sine, sine], -1))


def norm_scale(value_rows):
    return lax.rsqrt(jnp.mean(value_rows * value_rows, -1, keepdims=True) + epsilon)


def norm_back(value_rows, scale, gain, grad):
    weighted = grad * gain
    inner = jnp.mean(weighted * value_rows, -1, keepdims=True)
    result = scale * weighted - value_rows * scale * scale * scale * inner
    gain_part = jnp.sum((grad * value_rows * scale).reshape(-1, gain.shape[0]), 0)
    return (result, gain_part)


def row_products(left, pieces):
    return tuple((jnp.dot(left, piece, preferred_element_type=jnp.float32) for piece in pieces))


def column_products(rights, pieces):
    total = jnp.einsum("tc,rc->tr", rights[0], pieces[0], preferred_element_type=jnp.float32)
    for right, piece in zip(rights[1:], pieces[1:]):
        total = total + jnp.einsum("tc,rc->tr", right, piece, preferred_element_type=jnp.float32)
    return total


def on_device(
    layer_input,
    token_positions,
    attention_gain,
    query_weight,
    key_matrix,
    value_matrix,
    query_gain,
    key_norm_gain,
    output_weight,
    feedforward_gain,
    gate_weight,
    up_weight,
    down_weight,
    out_cotangent,
):
    hidden_in = layer_input[0].astype(jnp.float32)
    count = hidden_in.shape[0]
    head_size = query_gain.shape[0]
    query_width = query_weight.shape[1]
    key_width = key_matrix.shape[1]
    inner_width = gate_weight.shape[1]
    heads = query_width // head_size
    key_heads = key_width // head_size
    group = heads // key_heads
    scale = head_size ** (-0.5)
    cycles = lax.axis_size("ctx")
    own_index = lax.axis_index("ctx")
    sequence_pos = token_positions[0]
    token_offsets = lax.dynamic_slice_in_dim(sequence_pos, own_index * count, count)
    cosine, sine = rope_tables(token_offsets, head_size)
    cosine = cosine[:, None, :]
    sine = sine[:, None, :]
    first_scale = norm_scale(hidden_in)
    first = (hidden_in * first_scale * attention_gain).astype(jnp.bfloat16)
    query_raw, key_unnormed, value_unnormed = row_products(
        first,
        (
            lax.all_gather(query_weight, "fsdp", axis=0, tiled=True),
            lax.all_gather(key_matrix, "fsdp", axis=0, tiled=True),
            lax.all_gather(value_matrix, "fsdp", axis=0, tiled=True),
        ),
    )
    query_heads = query_raw.reshape(count, heads, head_size)
    query_scale = norm_scale(query_heads)
    query_normed = query_heads * query_scale * query_gain
    query_rot = query_normed * cosine + rotate(query_normed) * sine
    query_grouped = (
        query_rot.reshape(count, key_heads, group, head_size)
        .transpose(1, 2, 0, 3)
        .astype(jnp.bfloat16)
    )
    key_heads_raw = key_unnormed.reshape(count, key_heads, head_size)
    key_scale = norm_scale(key_heads_raw)
    key_normed = key_heads_raw * key_scale * key_norm_gain
    key_low = (
        (key_normed * cosine + rotate(key_normed) * sine)
        .reshape(count, key_width)
        .astype(jnp.bfloat16)
    )
    value_low = value_unnormed.astype(jnp.bfloat16)
    rowmax = jnp.full((key_heads, group, count), masked_score, jnp.float32)
    keys_piece = lax.all_gather(key_low, "ctx", axis=0, tiled=True).reshape(
        -1, key_heads, head_size
    )
    values_piece = lax.all_gather(value_low, "ctx", axis=0, tiled=True).reshape(
        -1, key_heads, head_size
    )
    key_pos = sequence_pos
    allowed = token_offsets[:, None] >= key_pos[None, :]
    scores = (
        jnp.einsum("kgtd,skd->kgts", query_grouped, keys_piece, preferred_element_type=jnp.float32)
        * scale
    )
    scores = jnp.where(allowed, scores, masked_score)
    newmax = jnp.maximum(rowmax, jnp.max(scores, -1))
    weights = jnp.where(allowed, jnp.exp(scores - newmax[..., None]), 0.0)
    accum = jnp.einsum(
        "kgts,skd->kgtd",
        weights.astype(jnp.bfloat16),
        values_piece,
        preferred_element_type=jnp.float32,
    )
    rowsum = jnp.sum(weights, -1)
    accum, rowmax, rowsum = (accum, newmax, rowsum)
    normalized = accum / rowsum[..., None]
    logsum = rowmax + jnp.log(rowsum)
    attention_low = (
        normalized.transpose(2, 0, 1, 3).reshape(count, query_width).astype(jnp.bfloat16)
    )
    output_whole = lax.all_gather(output_weight, "fsdp", axis=0, tiled=True)
    branch_out = jnp.dot(attention_low, output_whole, preferred_element_type=jnp.float32)
    middle = hidden_in + branch_out
    second_scale = norm_scale(middle)
    second = (middle * second_scale * feedforward_gain).astype(jnp.bfloat16)
    gate, up = row_products(
        second,
        (
            lax.all_gather(gate_weight, "fsdp", axis=0, tiled=True),
            lax.all_gather(up_weight, "fsdp", axis=0, tiled=True),
        ),
    )
    sigmoid_gate = jax.nn.sigmoid(gate)
    silu_gate = gate * sigmoid_gate
    hidden_low = (silu_gate * up).astype(jnp.bfloat16)
    (down_out,) = row_products(
        hidden_low, (lax.all_gather(down_weight, "fsdp", axis=0, tiled=True),)
    )
    layer_output = (middle + down_out).astype(jnp.bfloat16)[None]
    cotangent = out_cotangent[0]
    hidden_grad = column_products(
        (cotangent,), lax.all_gather((down_weight,), "fsdp", axis=0, tiled=True)
    )
    up_low = (hidden_grad * silu_gate).astype(jnp.bfloat16)
    gate_low = (hidden_grad * up * sigmoid_gate * (1.0 + gate * (1.0 - sigmoid_gate))).astype(
        jnp.bfloat16
    )
    second_grad = column_products(
        (gate_low, up_low), lax.all_gather((gate_weight, up_weight), "fsdp", axis=0, tiled=True)
    )
    middle_part, feedforward_part = norm_back(middle, second_scale, feedforward_gain, second_grad)
    middle_grad = cotangent.astype(jnp.float32) + middle_part
    middle_low = middle_grad.astype(jnp.bfloat16)
    attention_grad = jnp.einsum(
        "tc,rc->tr", middle_low, output_whole, preferred_element_type=jnp.float32
    )
    attention_grad_low = attention_grad.astype(jnp.bfloat16)
    mixed_grad = attention_grad_low.reshape(count, key_heads, group, head_size).transpose(
        1, 2, 0, 3
    )
    delta = jnp.sum(mixed_grad.astype(jnp.float32) * normalized, -1)

    def cycle_step(index, carry):
        keys_held, values_held, key_acc, value_acc, query_acc = carry
        anchor = (own_index - index) % cycles
        key_pos = lax.dynamic_slice_in_dim(sequence_pos, anchor * count, count)
        keys_piece = keys_held.astype(jnp.bfloat16).reshape(count, key_heads, head_size)
        values_piece = values_held.astype(jnp.bfloat16).reshape(count, key_heads, head_size)
        allowed = token_offsets[:, None] >= key_pos[None, :]
        scores = (
            jnp.einsum(
                "kgtd,skd->kgts", query_grouped, keys_piece, preferred_element_type=jnp.float32
            )
            * scale
        )
        probs = jnp.where(allowed, jnp.exp(scores - logsum[..., None]), 0.0)
        value_acc = value_acc + jnp.einsum(
            "kgts,kgtd->skd",
            probs.astype(jnp.bfloat16),
            mixed_grad,
            preferred_element_type=jnp.float32,
        ).reshape(count, key_width)
        prob_grad = jnp.einsum(
            "kgtd,skd->kgts", mixed_grad, values_piece, preferred_element_type=jnp.float32
        )
        score_grad = (probs * (prob_grad - delta[..., None])).astype(jnp.bfloat16)
        query_acc = (
            query_acc
            + jnp.einsum(
                "kgts,skd->kgtd", score_grad, keys_piece, preferred_element_type=jnp.float32
            )
            * scale
        )
        key_acc = (
            key_acc
            + jnp.einsum(
                "kgts,kgtd->skd", score_grad, query_grouped, preferred_element_type=jnp.float32
            ).reshape(count, key_width)
            * scale
        )
        moved = (
            from_behind(keys_held.astype(jnp.bfloat16), "ctx", 1).astype(keys_held.dtype),
            from_behind(values_held.astype(jnp.bfloat16), "ctx", 1).astype(values_held.dtype),
            from_behind(key_acc.astype(jnp.bfloat16), "ctx", 1).astype(key_acc.dtype),
            from_behind(value_acc.astype(jnp.bfloat16), "ctx", 1).astype(value_acc.dtype),
        )
        return (moved[0], moved[1], moved[2], moved[3], query_acc)

    start_cycle = (
        key_low.astype(jnp.float32),
        value_low.astype(jnp.float32),
        jnp.zeros((count, key_width), jnp.float32),
        jnp.zeros((count, key_width), jnp.float32),
        jnp.zeros((key_heads, group, count, head_size), jnp.float32),
    )
    cycle_done = lax.fori_loop(0, cycles, cycle_step, start_cycle)
    key_acc = cycle_done[2]
    value_acc = cycle_done[3]
    query_acc = cycle_done[4]
    query_rot_grad = query_acc.transpose(2, 0, 1, 3).reshape(count, heads, head_size)
    query_normed_grad = query_rot_grad * cosine + rotate_back(query_rot_grad * sine)
    query_heads_grad, query_part = norm_back(
        query_heads, query_scale, query_gain, query_normed_grad
    )
    query_low_grad = query_heads_grad.reshape(count, query_width).astype(jnp.bfloat16)
    key_rot_grad = key_acc.reshape(count, key_heads, head_size)
    key_normed_grad = key_rot_grad * cosine + rotate_back(key_rot_grad * sine)
    key_heads_grad, key_part = norm_back(key_heads_raw, key_scale, key_norm_gain, key_normed_grad)
    key_low_grad = key_heads_grad.reshape(count, key_width).astype(jnp.bfloat16)
    value_low_grad = value_acc.astype(jnp.bfloat16)
    first_grad = column_products(
        (query_low_grad, key_low_grad, value_low_grad),
        lax.all_gather((query_weight, key_matrix, value_matrix), "fsdp", axis=0, tiled=True),
    )
    input_part, attention_part = norm_back(hidden_in, first_scale, attention_gain, first_grad)
    input_gradient = (middle_grad + input_part)[None]
    rights_first = jnp.concatenate([query_low_grad, key_low_grad, value_low_grad], 1)
    rights_second = jnp.concatenate([gate_low, up_low], 1)
    pairs = (
        (first, rights_first),
        (second, rights_second),
        (middle_low, attention_low),
        (cotangent, hidden_low),
    )
    parts = []
    for left, right in pairs:
        parts.append(jnp.einsum("tr,tc->rc", left, right, preferred_element_type=jnp.float32))
    sums = lax.psum_scatter(
        jnp.concatenate(parts, 1), ("ctx", "fsdp"), scatter_dimension=0, tiled=True
    )
    edges = [0, query_width, query_width + key_width, query_width + 2 * key_width]
    edges = edges + [edges[3] + inner_width, edges[3] + 2 * inner_width]
    edges = edges + [edges[5] + query_width, edges[5] + query_width + inner_width]
    query_gradient = sums[:, edges[0] : edges[1]]
    key_gradient = sums[:, edges[1] : edges[2]]
    value_gradient = sums[:, edges[2] : edges[3]]
    gate_gradient = sums[:, edges[3] : edges[4]]
    up_gradient = sums[:, edges[4] : edges[5]]
    output_gradient = sums[:, edges[5] : edges[6]].T
    down_gradient = sums[:, edges[6] : edges[7]].T
    attention_total, query_total, key_total, feedforward_total = lax.psum(
        (attention_part, query_part, key_part, feedforward_part), ("ctx", "fsdp")
    )
    return (
        layer_output,
        input_gradient,
        attention_total,
        query_gradient,
        key_gradient,
        value_gradient,
        query_total,
        key_total,
        output_gradient,
        feedforward_total,
        gate_gradient,
        up_gradient,
        down_gradient,
    )


MESH = pl.DeviceIdType.MESH
f32 = jnp.float32
bf16 = jnp.bfloat16


def dot(left, right):
    return jnp.dot(left, right, preferred_element_type=f32)


def dot_nt(left, right):
    return lax.dot_general(left, right, (((1,), (1,)), ((), ())), preferred_element_type=f32)


def dot_tn(left, right):
    return lax.dot_general(left, right, (((0,), (0,)), ((), ())), preferred_element_type=f32)


def layer_kernel(
    n, planes, block, head, group, fw,
    x_ref, dy_ref, pos_row, inverse_ref, step_cos, step_sin, ag_ref, fg_ref, qg_ref, kg_ref,
    wq, wk, wv, wo, wg, wu, wd,
    out_ref, dx_ref, gains_ref, got_a, got_b, got_c, got_out, got_qkv,
    w_qkv, w_gu, w_out, w_down, t_out, t_down,
    first, dy_all, second, first_t, dy_t, second_t, dmid_t,
    positions, cosine, sine,
    raw, queries, keys, values, keys_t, values_t, probs, sums, mixed_t, mixed_low,
    hidden, d_gu, d_qkv, dk_acc, dv_acc,
    stage_a, stage_b, stage_c, stage_out, stage_qkv,
    land_a, land_b, land_c, land_out, land_qkv,
    rs_sa, rs_ra, rs_sb, rs_rb, rs_kept, rs_acc,
    middle, d_middle, gain_own, gain_plane, gain_all,
    local_sem, wz_send, wz_recv, hand_send, hand_recv,
    ag_send, ag_recv, ra_send, ra_recv, rb_send, rb_recv,
    zr_send, zr_recv, aa_send, aa_recv, gp_send, gp_recv, gz_send, gz_recv,
):
    c = lax.axis_index("ctx")
    z = lax.axis_index("fsdp")
    dmid = first
    cy, cx, ck = lax.div(c, 4), lax.rem(lax.div(c, 2), 2), lax.rem(c, 2)
    ci = lax.rem(c, 4)
    sign = 1 - 2 * ck
    qw, kw = group * head, head
    pw = 128
    thirds = fw // pw
    piece = pw // 4
    width = x_ref.shape[1]
    scale = head ** (-0.5)
    log2e = 1.4426950408889634
    gots = (got_a, got_b, got_c, got_out, got_qkv)
    stages = (stage_a, stage_b, stage_c, stage_out, stage_qkv)
    lands = (land_a, land_b, land_c, land_out, land_qkv)

    def partner(j):
        y = lax.rem(cy + lax.div(j, 4), 2)
        x = lax.rem(cx + lax.rem(lax.div(j, 2), 2), 2)
        k = lax.rem(ck + lax.rem(j, 2), 2)
        return y * 4 + x * 2 + k

    def chip(slot):
        return lax.rem(cy + lax.div(slot, 2), 2) * 2 + lax.rem(cx + lax.rem(slot, 2), 2)

    def rows(start, size):
        return pl.ds(pl.multiple_of(start * size, size), size)

    def remote(src, dst, send, recv, ctx, plane):
        return pltpu.make_async_remote_copy(
            src_ref=src, dst_ref=dst, send_sem=send, recv_sem=recv,
            device_id={"ctx": ctx, "fsdp": plane}, device_id_type=MESH,
        )

    in_plane, along = [], []

    def launch(started, copy, when=None):
        if when is None:
            copy().start()
        else:
            pl.when(when)(lambda: copy().start())
        started.append((copy, when))

    def drain(started):
        for copy, when in started:
            if when is None:
                copy().wait_send()
            else:
                pl.when(when)(lambda copy=copy: copy().wait_send())
        started.clear()

    own_rows = wq.shape[0]
    out_rows = wo.shape[0] // n

    def own_slices():
        mine = rows(z, own_rows)
        pairs = [
            (wq.at[:, rows(c, qw)], w_qkv.at[mine, 0:qw]),
            (wk.at[:, rows(c, kw)], w_qkv.at[mine, qw:qw + kw]),
            (wv.at[:, rows(c, kw)], w_qkv.at[mine, qw + kw:qw + 2 * kw]),
            (wo.at[rows(c, out_rows)], t_out.at[rows(z, out_rows)]),
        ]
        for t in range(thirds):
            at = 2 * pw * t
            pairs.append((wg.at[:, rows(c * thirds + t, pw)], w_gu.at[mine, at:at + pw]))
            pairs.append((wu.at[:, rows(c * thirds + t, pw)], w_gu.at[mine, at + pw:at + 2 * pw]))
            pairs.append((wd.at[rows((cy * thirds + t) * 4 + ci, piece)], t_down.at[t, rows(z, piece)]))
        return pairs

    local = [pltpu.make_async_copy(src, dst, local_sem.at[i]) for i, (src, dst) in enumerate(own_slices())]
    for copy in local:
        copy.start()

    for land in lands:
        @pl.when(z == 0)
        def _(land=land):
            land[0] = jnp.zeros(land.shape[1:], bf16)

        @pl.when(z == planes - 1)
        def _(land=land):
            land[planes] = jnp.zeros(land.shape[1:], bf16)

    barrier = pltpu.get_barrier_semaphore()
    for j in range(1, n):
        pl.semaphore_signal(barrier, inc=1, device_id={"ctx": partner(j), "fsdp": z}, device_id_type=MESH)
    for d in range(1, planes):
        pl.semaphore_signal(
            barrier, inc=1, device_id={"ctx": c, "fsdp": lax.rem(z + d, planes)}, device_id_type=MESH)
    x = x_ref[...].astype(f32)
    x_scale = lax.rsqrt(jnp.mean(x * x, -1, keepdims=True) + epsilon)
    first[rows(c, block)] = (x * x_scale * ag_ref[...]).astype(bf16)
    dy_all[rows(c, block)] = dy_ref[...]
    for copy in local[:3]:
        copy.wait()
    pl.semaphore_wait(barrier, n + planes - 2)

    def inside(t):
        return jnp.logical_and(t >= 0, t < planes)

    weights = [
        (lambda o: w_qkv.at[rows(o, own_rows)], None),
        (lambda o: t_out.at[rows(o, out_rows)], 0),
    ]
    for t in range(thirds):
        weights.append((lambda o, t=t: w_gu.at[rows(o, own_rows), 2 * pw * t:2 * pw * (t + 1)], None))
        weights.append((lambda o, t=t: t_down.at[t, rows(o, piece)], 1 + t))

    def weight_copy(w, slot, origin, target):
        part = weights[w][0](origin)
        return remote(part, part, wz_send.at[w, slot], wz_recv.at[w, origin], c, target)

    def hand_split(origin, valid):
        mine = 2 * origin + cy == c
        return jnp.logical_and(valid, jnp.logical_not(mine)), jnp.logical_and(valid, mine)

    def weight_start(w):
        for side in range(2):
            d = sign * (1 - 2 * side)
            launch(along, lambda side=side, d=d: weight_copy(w, side, z, z + d), inside(z + d))
        if weights[w][1] is not None:
            hand_over(w, z, 0, *hand_split(z, True))

    def hand_target(h):
        if h == 0:
            return lambda i: w_out.at[rows(i, out_rows)]
        return lambda i: w_down.at[rows((h - 1) * 4 + i, piece)]

    def hand_copy(w, origin, slot):
        h = weights[w][1]
        return remote(
            weights[w][0](origin), hand_target(h)(ci), hand_send.at[h, slot], hand_recv.at[h, ci], 2 * origin + cy, z)

    def hand_over(w, origin, slot, away, here):
        launch(in_plane, lambda: hand_copy(w, origin, slot), away)

        @pl.when(here)
        def _():
            hand_target(weights[w][1])(ci)[...] = weights[w][0](origin)[...]

    def hand_arrive(w):
        h = weights[w][1]
        for i in range(4):
            @pl.when(4 * ck + i != c)
            def _(i=i):
                part = hand_target(h)(i)
                remote(part, part, hand_send.at[h, 0], hand_recv.at[h, i], c, z).wait_recv()

    hops = {}
    for d in range(1, planes):
        for side, way in enumerate((1, -1)):
            origin = z - way * d
            valid = inside(origin)
            passed = jnp.logical_and(valid, inside(z + way))
            hops[d, side] = origin, z + way, valid, passed, hand_split(origin, valid)

    def weight_hop(w, d):
        for side in range(2):
            origin, following, valid, passed, split = hops[d, side]
            pl.when(valid)(lambda: weight_copy(w, 0, origin, z).wait_recv())
            if d < planes - 1:
                launch(
                    along,
                    lambda side=side, origin=origin, following=following: weight_copy(
                        w, 2 * d + side, origin, following),
                    passed)
            if weights[w][1] is not None:
                hand_over(w, origin, 2 * d - 1 + side, *split)

    def gather_copy(buf, g, j, send, origin, target):
        part = buf.at[rows(origin, block)]
        return remote(part, part, ag_send.at[g, send], ag_recv.at[g, j], target, z)

    def gather_start(buf, g):
        for j in (1, 2 + 2 * ck, 4 - 2 * ck, 6):
            launch(in_plane, lambda j=j: gather_copy(buf, g, j, j, c, partner(j)))

    def gather_forward(buf, g, j):
        return gather_copy(buf, g, j + 1, j + 1, partner(j), partner(1))

    def gather_finish(buf, g):
        for j in (2, 4, 6):
            gather_copy(buf, g, j, j, partner(j), c).wait_recv()
            launch(in_plane, lambda j=j: gather_forward(buf, g, j))
        for j in (1, 3, 5, 7):
            gather_copy(buf, g, j, j, partner(j), c).wait_recv()

    def gather_step(buf, g, slot):
        def arrive(j):
            gather_copy(buf, g, j, j, partner(j), c).wait_recv()
            gather_forward(buf, g, j).start()

        @pl.when(slot == 1)
        def _():
            arrive(2)
            arrive(4)

        @pl.when(slot == 3)
        def _():
            arrive(6)

        gather_copy(buf, g, 2 * slot + 1, 0, partner(2 * slot + 1), c).wait_recv()

    def gather_stepped(buf, g):
        for j in (2, 4, 6):
            in_plane.append((lambda j=j: gather_forward(buf, g, j), None))

    def sum_pair_copy(s, slot):
        return remote(rs_sa.at[s % 2, slot], rs_ra.at[s % 2, slot], ra_send.at[s, slot], ra_recv.at[s, slot], partner(1), z)

    def sum_chip_copy(s, slot):
        return remote(
            rs_sb.at[s % 2, slot], rs_rb.at[s % 2, slot], rb_send.at[s, slot], rb_recv.at[s, slot], partner(2 * slot), z)

    def sum_slot(p):
        return jnp.where(p == 0, 3, jnp.where(p == 1, 2 - ck, jnp.where(p == 2, 1 + ck, 0)))

    def sum_start(s, left, partial, prepare=None, ready=None, during=()):
        if prepare is not None:
            prepare(chip(sum_slot(0)))
        if ready is not None:
            ready()

        def body(p, carry):
            slot = sum_slot(p)
            at = [rows(partner(2 * slot + 1), block), rows(partner(2 * slot), block)]
            both = partial(jnp.concatenate([left[i] for i in at], 0))
            rs_sa[s % 2, slot] = both[:block].astype(bf16)
            sum_pair_copy(s, slot).start()
            rs_kept[lax.rem(p, 2)] = both[block:]
            if prepare is not None:
                @pl.when(p < 3)
                def _():
                    prepare(chip(sum_slot(p + 1)))

            @pl.when(p > 0)
            def _():
                before = sum_slot(p - 1)
                sum_pair_copy(s, before).wait_recv()
                rs_sb[s % 2, before] = (
                    rs_kept[lax.rem(p + 1, 2)] + rs_ra[s % 2, before].astype(f32)).astype(bf16)
                sum_chip_copy(s, before).start()

            for k, poll in enumerate(during):
                pl.when(p == k)(poll)
            return carry

        lax.fori_loop(0, 4, body, 0)
        for slot in range(4):
            in_plane.append((lambda slot=slot: sum_pair_copy(s, slot), None))
            if slot > 0:
                in_plane.append((lambda slot=slot: sum_chip_copy(s, slot), None))
        sum_pair_copy(s, 0).wait_recv()
        rs_acc[s % 2] = rs_kept[1] + rs_ra[s % 2, 0].astype(f32)

    def sum_finish(s):
        total = rs_acc[s % 2]
        for slot in (1, 2, 3):
            sum_chip_copy(s, slot).wait_recv()
            total = total + rs_rb[s % 2, slot].astype(f32)
        return total

    per = block // planes

    def weight_grad(m, parts):
        def body(i, carry):
            at = 0
            for left, right in parts:
                value = right()
                grad = dot(left[rows(i, 2 * block)], value)
                for k in range(2):
                    for t in range(planes):
                        start = k * block + t * per
                        stages[m][t, 2 * i + k, :, at:at + value.shape[1]] = grad[start:start + per].astype(bf16)
                at += value.shape[1]
            return carry

        lax.fori_loop(0, n // 2, body, 0)
        at_edge = jnp.logical_or(z == 0, z == planes - 1)
        for k in range(planes - 1):
            t = jnp.where(z == 0, planes - 1 - k, k)
            launch(along, lambda t=t: grad_copy(m, t), at_edge)

    def grad_copy(m, t):
        way = jnp.where(z < t, 1, -1)
        last = z + way == t
        slot = jnp.where(jnp.logical_and(last, way < 0), planes, t)
        return remote(
            stages[m].at[t], lands[m].at[slot], zr_send.at[m, t], zr_recv.at[m, slot], c, z + way)

    def grad_arrive(m, slot):
        part = lands[m].at[slot]
        remote(part, part, zr_send.at[m, 0], zr_recv.at[m, slot], c, z).wait_recv()

    def grad_pass(m, t, valid):
        @pl.when(valid)
        def _():
            grad_arrive(m, t)

            def body(i, carry):
                stages[m][t, i] = (stages[m][t, i].astype(f32) + lands[m][t, i].astype(f32)).astype(bf16)
                return carry

            lax.fori_loop(0, n, body, 0)

        launch(along, lambda: grad_copy(m, t), valid)

    def grad_near(m):
        for t in (3, 2):
            grad_pass(m, t, z == 1)
        for t in (0, 1):
            grad_pass(m, t, z == 2)

    def grad_far(m):
        grad_pass(m, 3, z == 2)
        grad_pass(m, 0, z == 1)

    def owner_copy(m, j):
        return remote(lands[m].at[z, partner(j)], gots[m].at[c], aa_send.at[m, j], aa_recv.at[m, j], partner(j), z)

    def hand_out(m):
        pl.when(z > 0)(lambda: grad_arrive(m, z))
        pl.when(z < planes - 1)(lambda: grad_arrive(m, planes))

        def body(i, carry):
            total = stages[m][z, i].astype(f32) + lands[m][z, i].astype(f32) + lands[m][planes, i].astype(f32)
            lands[m][z, i] = total.astype(bf16)
            return carry

        lax.fori_loop(0, n, body, 0)
        for j in (2 + 2 * ck, 3 + 2 * ck, 4 - 2 * ck, 5 - 2 * ck, 6, 7, 1):
            launch(in_plane, lambda j=j: owner_copy(m, j))
        gots[m][c] = lands[m][z, c]

    def hand_receive(m):
        for j in range(1, n):
            owner_copy(m, j).wait_recv()

    weight_start(0)
    gather_start(first, 0)
    for copy in local[3:]:
        copy.wait()

    spread = jnp.broadcast_to(pos_row[...].astype(f32), (head, pos_row.shape[1]))
    positions[...] = spread.T
    side = jnp.where(lax.broadcasted_iota(jnp.int32, (1, head), 1) < head // 2, -1.0, 1.0)

    def table(i, carry):
        run = step_cos.shape[0]
        at = rows(i, run)
        start = positions[pl.ds(pl.multiple_of(i * run, run), 1)] * inverse_ref[...]
        start_cos, start_sin = jnp.cos(start), jnp.sin(start)
        cosine[at] = start_cos * step_cos[...] - start_sin * step_sin[...]
        sine[at] = (start_sin * step_cos[...] + start_cos * step_sin[...]) * side
        return carry

    def turn_over(src, dst):
        def body(i, carry):
            at = rows(i, block)
            dst[:, at] = src[at].T
            return carry

        lax.fori_loop(0, n, body, 0)

    lax.fori_loop(0, 2 * n, table, 0)
    weight_hop(0, 1)
    gather_finish(first, 0)
    weight_hop(0, 2)
    weight_start(1)
    gather_start(dy_all, 1)
    turn_over(first, first_t)
    weight_hop(0, 3)
    weight_start(2)
    weight_start(3)

    def turn(value, at):
        return value * cosine[at] + pltpu.roll(value, head // 2, 1) * sine[at]

    def turn_back(grad, at):
        return grad * cosine[at] - pltpu.roll(grad, head // 2, 1) * sine[at]

    def project(i, carry):
        at = rows(i, 2 * block)
        result = dot(first[at], w_qkv[...])
        raw[at] = result[:, :qw + kw]
        low_values = result[:, qw + kw:].astype(bf16)
        values[at] = low_values
        values_t[:, at] = low_values.T
        for h in range(group + 1):
            part = result[:, h * head:(h + 1) * head]
            inv = lax.rsqrt(jnp.mean(part * part, -1, keepdims=True) + epsilon)
            gain = qg_ref[...] if h < group else kg_ref[...]
            turned = turn(part * inv * gain, at)
            if h < group:
                queries[at, h * head:(h + 1) * head] = (turned * (scale * log2e)).astype(bf16)
            else:
                low_keys = turned.astype(bf16)
                keys[at] = low_keys
                keys_t[:, at] = low_keys.T
        return carry

    lax.fori_loop(0, n // 4, project, 0)
    weight_hop(1, 1)
    lax.fori_loop(n // 4, n // 2, project, 0)
    weight_hop(1, 2)
    gather_finish(dy_all, 1)

    def stack(ref, at):
        return jnp.concatenate([ref[at, h * head:(h + 1) * head] for h in range(group)], 0)

    def attend_block(i):
        at = rows(i, block)
        scores = dot_nt(keys[...], stack(queries, at))
        allowed = positions[...] <= pos_row[:, at].astype(f32)
        weight = jnp.concatenate(
            [jnp.exp2(jnp.where(allowed, scores[:, h * block:(h + 1) * block], masked_score)) for h in range(group)], 1)
        inv = 1.0 / jnp.sum(weight, 0, keepdims=True)
        low_weight = weight.astype(bf16)
        probs[i] = low_weight
        sums[i] = inv
        result = dot(values_t[...], low_weight) * inv
        mixed_t[i] = result
        for h in range(group):
            mixed_low[at, h * head:(h + 1) * head] = result[:, h * block:(h + 1) * block].T.astype(bf16)

    def attend(place):
        attend_block(2 * place)
        attend_block(2 * place + 1)

    def output_ready():
        weight_hop(1, 3)
        weight_start(4)
        weight_start(5)
        hand_arrive(1)
        drain(in_plane)

    def hop_third(t, d):
        weight_hop(2 + 2 * t, d)
        weight_hop(3 + 2 * t, d)

    sum_start(
        0, mixed_low, lambda left: dot(left, w_out[...]), attend, output_ready,
        (lambda: hop_third(0, 1), lambda: hop_third(0, 2)))
    weight_start(6)
    weight_start(7)
    turn_over(dy_all, dy_t)
    hop_third(0, 3)
    mid = x_ref[...].astype(f32) + sum_finish(0)
    middle[...] = mid
    mid_scale = lax.rsqrt(jnp.mean(mid * mid, -1, keepdims=True) + epsilon)
    second[rows(c, block)] = (mid * mid_scale * fg_ref[...]).astype(bf16)
    gather_start(second, 2)
    hop_third(1, 1)
    hand_arrive(3)

    def feed(t, at):
        units, pair = slice(t * pw, (t + 1) * pw), 2 * pw * t
        both = dot(second[at], w_gu[:, pair:pair + 2 * pw])
        back = dot_nt(dy_all[at], w_down[units])
        gate, up = both[:, :pw], both[:, pw:]
        sig = 1.0 / (1.0 + jnp.exp(-gate))
        silu = gate * sig
        hidden[at, units] = (silu * up).astype(bf16)
        d_gu[at, pair:pair + pw] = (back * up * sig * (1.0 + gate * (1.0 - sig))).astype(bf16)
        d_gu[at, pair + pw:pair + 2 * pw] = (back * silu).astype(bf16)

    def feed_arriving(slot, carry):
        gather_step(second, 2, slot)
        at = rows(chip(slot), 2 * block)
        feed(0, at)
        second_t[:, at] = second[at].T
        pl.when(slot == 2)(lambda: hop_third(1, 2))
        return carry

    def third_grad(t):
        weight_grad(t, [
            (second_t, lambda: d_gu[:, 2 * pw * t:2 * pw * (t + 1)]),
            (dy_t, lambda: hidden[:, t * pw:(t + 1) * pw]),
        ])

    def feed_third(t):
        def body(i, carry):
            feed(t, rows(i, 2 * block))
            return carry

        lax.fori_loop(0, n // 2, body, 0)

    lax.fori_loop(0, n // 2, feed_arriving, 0)
    gather_stepped(second, 2)
    hop_third(2, 1)
    third_grad(0)
    hop_third(1, 3)
    hand_arrive(5)
    feed_third(1)
    hop_third(2, 2)
    third_grad(1)
    hop_third(2, 3)
    hand_arrive(7)
    sum_start(
        1, d_gu, lambda left: dot_nt(left, w_gu[...]),
        lambda place: feed(thirds - 1, rows(place, 2 * block)))
    third_grad(2)
    d_second = sum_finish(1)

    def norm_back(value, gain, grad):
        inv = lax.rsqrt(jnp.mean(value * value, -1, keepdims=True) + epsilon)
        weighted = grad * gain
        inner = jnp.mean(weighted * value, -1, keepdims=True)
        result = inv * weighted - value * (inv * inv * inv * inner)
        return result, jnp.sum(grad * value * inv, 0, keepdims=True)

    gain_own[...] = jnp.zeros_like(gain_own)
    part, gain_own[1:2, :] = norm_back(middle[...], fg_ref[...], d_second)
    d_mid = dy_ref[...].astype(f32) + part
    d_middle[...] = d_mid
    dmid[rows(c, block)] = d_mid.astype(bf16)
    gather_start(dmid, 3)
    grad_near(0)

    dk_acc[...] = jnp.zeros_like(dk_acc)
    dv_acc[...] = jnp.zeros_like(dv_acc)

    def attend_back_block(i, d_mix):
        at = rows(i, block)
        d_mix_t = jnp.concatenate([d_mix[h * head:(h + 1) * head] for h in range(group)], 1)
        d_mix_t = (d_mix_t.astype(bf16).astype(f32) * sums[i]).astype(bf16)
        delta = jnp.sum(d_mix_t.astype(f32) * mixed_t[i], 0, keepdims=True)
        weight = probs[i]
        d_prob = dot(values[...], d_mix_t)
        d_score = (weight.astype(f32) * (d_prob - delta)).astype(bf16)
        d_query = dot(keys_t[...], d_score) * scale
        gained = jnp.zeros((1, head), f32)
        for h in range(group):
            grad = turn_back(d_query[:, h * block:(h + 1) * block].T, at)
            part, gain_part = norm_back(raw[at, h * head:(h + 1) * head], qg_ref[...], grad)
            d_qkv[at, h * head:(h + 1) * head] = part.astype(bf16)
            gained = gained + gain_part
        return dot(weight, d_mix_t.T), dot(d_score, stack(queries, at)), gained

    def attend_back(slot, q_sum):
        gather_step(dmid, 3, slot)
        at = rows(chip(slot), 2 * block)
        d_mix = dot_nt(w_out[...], dmid[at])
        dmid_t[:, at] = dmid[at].T
        dv_one, dk_one, gain_one = attend_back_block(2 * chip(slot), d_mix[:, :block])
        dv_two, dk_two, gain_two = attend_back_block(2 * chip(slot) + 1, d_mix[:, block:])
        dv_acc[...] += dv_one + dv_two
        dk_acc[...] += dk_one + dk_two
        return q_sum + gain_one + gain_two

    zero = jnp.zeros((1, head), f32)
    gain_own[2:3, 0:head] = lax.fori_loop(0, n // 2, attend_back, zero)
    gather_stepped(dmid, 3)
    weight_grad(3, [(dmid_t, lambda: mixed_low[...])])
    grad_far(0)
    grad_near(1)
    drain(in_plane)
    sum_start(2, hidden, lambda left: dot(left, w_down[...]))

    def project_back(i, k_sum):
        at = rows(i, 2 * block)
        grad = turn_back(dk_acc[at] * (1.0 / log2e), at)
        part, gain_part = norm_back(raw[at, qw:qw + kw], kg_ref[...], grad)
        d_qkv[at, qw:qw + kw] = part.astype(bf16)
        d_qkv[at, qw + kw:] = dv_acc[at].astype(bf16)
        return k_sum + gain_part

    gain_own[3:4, 0:head] = lax.fori_loop(0, n // 2, project_back, zero)

    weight_grad(4, [(first_t, lambda: d_qkv[...])])
    sum_start(3, d_qkv, lambda left: dot_nt(left, w_qkv[...]))
    grad_far(1)
    grad_near(2)
    out_ref[...] = (middle[...] + sum_finish(2)).astype(bf16)
    hand_out(0)
    grad_far(2)
    grad_near(3)
    hand_out(1)
    x_part, gain_own[0:1, :] = norm_back(x_ref[...].astype(f32), ag_ref[...], sum_finish(3))
    dx_ref[...] = d_middle[...] + x_part

    def gain_plane_copy(j):
        return remote(gain_own, gain_plane.at[c], gp_send.at[j], gp_recv.at[j], partner(j), z)

    def gain_copy(d):
        return remote(gain_all.at[z], gain_all.at[z], gz_send.at[d], gz_recv.at[d], c, lax.rem(z + d, planes))

    for j in range(1, n):
        launch(in_plane, lambda j=j: gain_plane_copy(j))
    gain_plane[c] = gain_own[...]
    grad_far(3)
    hand_out(2)
    for j in range(1, n):
        gain_plane_copy(j).wait_recv()
    total = gain_plane[0]
    for i in range(1, n):
        total = total + gain_plane[i]
    gain_all[z] = total
    for d in range(1, planes):
        launch(along, lambda d=d: gain_copy(d))
    grad_near(4)
    hand_out(3)
    grad_far(4)
    for d in range(1, planes):
        origin = gain_all.at[lax.rem(z + planes - d, planes)]
        remote(origin, origin, gz_send.at[d], gz_recv.at[d], c, z).wait_recv()
    total = gain_all[0]
    for i in range(1, planes):
        total = total + gain_all[i]
    gains_ref[...] = total

    hand_out(4)
    for m in range(5):
        hand_receive(m)
    drain(in_plane)
    drain(along)


def finish_kernel(
    n, head, out_in, dx_in, gains_in, got_a, got_b, got_c, got_out, got_qkv,
    out_ref, dx_ref, ag_ref, q_ref, k_ref, v_ref, qg_ref, kg_ref, o_ref, fg_ref, g_ref, u_ref, d_ref,
):
    out_ref[...] = out_in[...]
    dx_ref[...] = dx_in[...]
    ag_ref[...] = gains_in[0:1, :]
    fg_ref[...] = gains_in[1:2, :]
    qg_ref[...] = gains_in[2:3, 0:head]
    kg_ref[...] = gains_in[3:4, 0:head]
    qw, kw = q_ref.shape[1] // n, k_ref.shape[1] // n
    pw = got_a.shape[2] // 3
    thirds = (got_a, got_b, got_c)
    for i in range(n):
        q_ref[:, i * qw:(i + 1) * qw] = got_qkv[i, :, 0:qw].astype(f32)
        k_ref[:, i * kw:(i + 1) * kw] = got_qkv[i, :, qw:qw + kw].astype(f32)
        v_ref[:, i * kw:(i + 1) * kw] = got_qkv[i, :, qw + kw:].astype(f32)
        o_ref[:, i * qw:(i + 1) * qw] = got_out[i].astype(f32)
        for t, got in enumerate(thirds):
            at = (i * len(thirds) + t) * pw
            g_ref[:, at:at + pw] = got[i, :, 0:pw].astype(f32)
            u_ref[:, at:at + pw] = got[i, :, pw:2 * pw].astype(f32)
            d_ref[:, at:at + pw] = got[i, :, 2 * pw:].astype(f32)


def plane_device(
    layer_input,
    token_positions,
    attention_gain,
    query_weight,
    key_matrix,
    value_matrix,
    query_gain,
    key_norm_gain,
    output_weight,
    feedforward_gain,
    gate_weight,
    up_weight,
    down_weight,
    out_cotangent,
):
    n = lax.axis_size("ctx")
    planes = lax.axis_size("fsdp")
    block, width = layer_input.shape[1:]
    length = token_positions.shape[1]
    head = query_gain.shape[0]
    qw = query_weight.shape[1] // n
    kw = key_matrix.shape[1] // n
    fw = gate_weight.shape[1] // n
    group = qw // head
    per = block // planes
    half = head // 2
    inverse = np.power(rope_base, -np.arange(half) * 2.0 / head).astype(np.float32)
    inverse = np.concatenate([inverse, inverse])[None]
    steps = np.arange(block // 2)[:, None] * inverse.astype(np.float64)
    step_cos, step_sin = (jnp.asarray(f(steps).astype(np.float32)) for f in (np.cos, np.sin))
    inverse = jnp.asarray(inverse)
    vmem = pl.BlockSpec(memory_space=pltpu.VMEM)
    hbm = pl.BlockSpec(memory_space=pl.ANY)
    dma = pltpu.SemaphoreType.DMA
    sizes = (fw, fw, fw, qw, qw + 2 * kw)
    low = lambda *shape: pltpu.VMEM(shape, bf16)
    wide = lambda *shape: pltpu.VMEM(shape, f32)
    scratch = [
        low(width, qw + 2 * kw), low(width, 2 * fw), low(qw, width), low(fw, width),
        low(planes * (output_weight.shape[0] // n), width), low(3, planes * 32, width),
        low(length, width), low(length, width), low(length, width),
        low(width, length), low(width, length), low(width, length), low(width, length),
        wide(length, head), wide(length, head), wide(length, head),
        wide(length, qw + kw), low(length, qw), low(length, kw), low(length, kw),
        low(kw, length), low(kw, length), low(n, length, group * block), wide(n, 1, group * block), wide(n, head, group * block), low(length, qw),
        low(length, fw), low(length, 2 * fw), low(length, qw + 2 * kw),
        wide(length, kw), wide(length, kw),
    ]
    scratch += [low(planes, n, per, size) for size in sizes]
    scratch += [low(planes + 1, n, per, size) for size in sizes]
    scratch += [low(2, 4, block, width) for _ in range(4)] + [wide(2, block, width), wide(2, block, width)]
    scratch += [
        wide(block, width), wide(block, width), wide(8, width), wide(n, 8, width), wide(planes, 8, width),
        dma((13,)), dma((8, 6)), dma((8, planes)), dma((4, 7)), dma((4, 4)),
        dma((4, n)), dma((4, n)), dma((4, 4)), dma((4, 4)), dma((4, 4)), dma((4, 4)),
        dma((5, planes)), dma((5, planes + 1)), dma((5, n)), dma((5, n)), dma((n,)), dma((n,)),
        dma((planes,)), dma((planes,)),
    ]
    shapes = [
        jax.ShapeDtypeStruct((block, width), bf16),
        jax.ShapeDtypeStruct((block, width), f32),
        jax.ShapeDtypeStruct((8, width), f32),
    ] + [jax.ShapeDtypeStruct((n, per, size), bf16) for size in sizes]
    results = pl.pallas_call(
        functools.partial(layer_kernel, n, planes, block, head, group, fw),
        out_shape=shapes,
        in_specs=[vmem] * 10 + [hbm] * 7,
        out_specs=[vmem] * len(shapes),
        scratch_shapes=scratch,
        compiler_params=pltpu.CompilerParams(
            collective_id=0, has_side_effects=True, vmem_limit_bytes=60 * 1024 * 1024),
    )(
        layer_input[0], out_cotangent[0], token_positions, inverse, step_cos, step_sin,
        attention_gain[None], feedforward_gain[None], query_gain[None], key_norm_gain[None],
        query_weight, key_matrix, value_matrix, output_weight, gate_weight, up_weight, down_weight,
    )
    plain = lambda rows, columns, kind=f32: jax.ShapeDtypeStruct((rows, columns), kind)
    finals = [
        plain(block, width, bf16), plain(block, width), plain(1, width),
        plain(per, n * qw), plain(per, n * kw), plain(per, n * kw), plain(1, head), plain(1, head),
        plain(per, n * qw), plain(1, width), plain(per, n * fw), plain(per, n * fw), plain(per, n * fw),
    ]
    done = pl.pallas_call(
        functools.partial(finish_kernel, n, head),
        out_shape=finals,
        in_specs=[vmem] * len(shapes),
        out_specs=[vmem] * len(finals),
    )(*results)
    out, dx, ag, q, k, v, qg, kg, o, fg, g, u, d = done
    return out[None], dx[None], ag[0], q, k, v, qg[0], kg[0], o.T, fg[0], g, u, d.T


def solution(mesh):
    in_specs = (
        P("fsdp", "ctx", None),
        P("fsdp", None),
        P(),
        P("fsdp", None),
        P("fsdp", None),
        P("fsdp", None),
        P(),
        P(),
        P("fsdp", None),
        P(),
        P("fsdp", None),
        P("fsdp", None),
        P("fsdp", None),
        P("fsdp", "ctx", None),
    )
    out_specs = (
        P("fsdp", "ctx", None),
        P("fsdp", "ctx", None),
        P(),
        P(("ctx", "fsdp"), None),
        P(("ctx", "fsdp"), None),
        P(("ctx", "fsdp"), None),
        P(),
        P(),
        P(None, ("ctx", "fsdp")),
        P(),
        P(("ctx", "fsdp"), None),
        P(("ctx", "fsdp"), None),
        P(None, ("ctx", "fsdp")),
    )

    def run(*arguments):
        n, planes = mesh.shape["ctx"], mesh.shape["fsdp"]
        key_heads = arguments[4].shape[1] // arguments[6].shape[0]
        whole_heads = n == 8 and planes == 4 and key_heads == n
        return jax.shard_map(
            plane_device if whole_heads else on_device,
            mesh=mesh, in_specs=in_specs, out_specs=out_specs, check_vma=False,
        )(*arguments)

    return run
```

```python
import functools

import jax
import jax.numpy as jnp
import numpy as np
from jax import lax
from jax.experimental import pallas as pl
from jax.experimental.pallas import tpu as pltpu
from jax.sharding import PartitionSpec as P

epsilon = 1e-06
rope_base = 1000000.0
masked_score = -1e30


def from_behind(block, axis, distance):
    devices = range(lax.axis_size(axis))
    route = [((i - distance) % len(devices), i) for i in devices]
    return lax.ppermute(block, axis, route)


def rotate(value_rows):
    half = value_rows.shape[-1] // 2
    return jnp.concatenate([-value_rows[..., half:], value_rows[..., :half]], -1)


def rotate_back(value_rows):
    half = value_rows.shape[-1] // 2
    return jnp.concatenate([value_rows[..., half:], -value_rows[..., :half]], -1)


def rope_tables(token_offsets, head_size):
    half = head_size // 2
    inverse = rope_base ** (-(jnp.arange(half).astype(jnp.float32) * 2.0) / head_size)
    angles = token_offsets.astype(jnp.float32)[:, None] * inverse[None, :]
    cosine = jnp.cos(angles)
    sine = jnp.sin(angles)
    return (jnp.concatenate([cosine, cosine], -1), jnp.concatenate([sine, sine], -1))


def norm_scale(value_rows):
    return lax.rsqrt(jnp.mean(value_rows * value_rows, -1, keepdims=True) + epsilon)


def norm_back(value_rows, scale, gain, grad):
    weighted = grad * gain
    inner = jnp.mean(weighted * value_rows, -1, keepdims=True)
    result = scale * weighted - value_rows * scale * scale * scale * inner
    gain_part = jnp.sum((grad * value_rows * scale).reshape(-1, gain.shape[0]), 0)
    return (result, gain_part)


def row_products(left, pieces):
    return tuple((jnp.dot(left, piece, preferred_element_type=jnp.float32) for piece in pieces))


def column_products(rights, pieces):
    total = jnp.einsum("tc,rc->tr", rights[0], pieces[0], preferred_element_type=jnp.float32)
    for right, piece in zip(rights[1:], pieces[1:]):
        total = total + jnp.einsum("tc,rc->tr", right, piece, preferred_element_type=jnp.float32)
    return total


def on_device(
    layer_input,
    token_positions,
    attention_gain,
    query_weight,
    key_matrix,
    value_matrix,
    query_gain,
    key_norm_gain,
    output_weight,
    feedforward_gain,
    gate_weight,
    up_weight,
    down_weight,
    out_cotangent,
):
    hidden_in = layer_input[0].astype(jnp.float32)
    count = hidden_in.shape[0]
    head_size = query_gain.shape[0]
    query_width = query_weight.shape[1]
    key_width = key_matrix.shape[1]
    inner_width = gate_weight.shape[1]
    heads = query_width // head_size
    key_heads = key_width // head_size
    group = heads // key_heads
    scale = head_size ** (-0.5)
    cycles = lax.axis_size("ctx")
    own_index = lax.axis_index("ctx")
    sequence_pos = token_positions[0]
    token_offsets = lax.dynamic_slice_in_dim(sequence_pos, own_index * count, count)
    cosine, sine = rope_tables(token_offsets, head_size)
    cosine = cosine[:, None, :]
    sine = sine[:, None, :]
    first_scale = norm_scale(hidden_in)
    first = (hidden_in * first_scale * attention_gain).astype(jnp.bfloat16)
    query_raw, key_unnormed, value_unnormed = row_products(
        first,
        (
            lax.all_gather(query_weight, "fsdp", axis=0, tiled=True),
            lax.all_gather(key_matrix, "fsdp", axis=0, tiled=True),
            lax.all_gather(value_matrix, "fsdp", axis=0, tiled=True),
        ),
    )
    query_heads = query_raw.reshape(count, heads, head_size)
    query_scale = norm_scale(query_heads)
    query_normed = query_heads * query_scale * query_gain
    query_rot = query_normed * cosine + rotate(query_normed) * sine
    query_grouped = (
        query_rot.reshape(count, key_heads, group, head_size)
        .transpose(1, 2, 0, 3)
        .astype(jnp.bfloat16)
    )
    key_heads_raw = key_unnormed.reshape(count, key_heads, head_size)
    key_scale = norm_scale(key_heads_raw)
    key_normed = key_heads_raw * key_scale * key_norm_gain
    key_low = (
        (key_normed * cosine + rotate(key_normed) * sine)
        .reshape(count, key_width)
        .astype(jnp.bfloat16)
    )
    value_low = value_unnormed.astype(jnp.bfloat16)
    rowmax = jnp.full((key_heads, group, count), masked_score, jnp.float32)
    keys_piece = lax.all_gather(key_low, "ctx", axis=0, tiled=True).reshape(
        -1, key_heads, head_size
    )
    values_piece = lax.all_gather(value_low, "ctx", axis=0, tiled=True).reshape(
        -1, key_heads, head_size
    )
    key_pos = sequence_pos
    allowed = token_offsets[:, None] >= key_pos[None, :]
    scores = (
        jnp.einsum("kgtd,skd->kgts", query_grouped, keys_piece, preferred_element_type=jnp.float32)
        * scale
    )
    scores = jnp.where(allowed, scores, masked_score)
    newmax = jnp.maximum(rowmax, jnp.max(scores, -1))
    weights = jnp.where(allowed, jnp.exp(scores - newmax[..., None]), 0.0)
    accum = jnp.einsum(
        "kgts,skd->kgtd",
        weights.astype(jnp.bfloat16),
        values_piece,
        preferred_element_type=jnp.float32,
    )
    rowsum = jnp.sum(weights, -1)
    accum, rowmax, rowsum = (accum, newmax, rowsum)
    normalized = accum / rowsum[..., None]
    logsum = rowmax + jnp.log(rowsum)
    attention_low = (
        normalized.transpose(2, 0, 1, 3).reshape(count, query_width).astype(jnp.bfloat16)
    )
    output_whole = lax.all_gather(output_weight, "fsdp", axis=0, tiled=True)
    branch_out = jnp.dot(attention_low, output_whole, preferred_element_type=jnp.float32)
    middle = hidden_in + branch_out
    second_scale = norm_scale(middle)
    second = (middle * second_scale * feedforward_gain).astype(jnp.bfloat16)
    gate, up = row_products(
        second,
        (
            lax.all_gather(gate_weight, "fsdp", axis=0, tiled=True),
            lax.all_gather(up_weight, "fsdp", axis=0, tiled=True),
        ),
    )
    sigmoid_gate = jax.nn.sigmoid(gate)
    silu_gate = gate * sigmoid_gate
    hidden_low = (silu_gate * up).astype(jnp.bfloat16)
    (down_out,) = row_products(
        hidden_low, (lax.all_gather(down_weight, "fsdp", axis=0, tiled=True),)
    )
    layer_output = (middle + down_out).astype(jnp.bfloat16)[None]
    cotangent = out_cotangent[0]
    hidden_grad = column_products(
        (cotangent,), lax.all_gather((down_weight,), "fsdp", axis=0, tiled=True)
    )
    up_low = (hidden_grad * silu_gate).astype(jnp.bfloat16)
    gate_low = (hidden_grad * up * sigmoid_gate * (1.0 + gate * (1.0 - sigmoid_gate))).astype(
        jnp.bfloat16
    )
    second_grad = column_products(
        (gate_low, up_low), lax.all_gather((gate_weight, up_weight), "fsdp", axis=0, tiled=True)
    )
    middle_part, feedforward_part = norm_back(middle, second_scale, feedforward_gain, second_grad)
    middle_grad = cotangent.astype(jnp.float32) + middle_part
    middle_low = middle_grad.astype(jnp.bfloat16)
    attention_grad = jnp.einsum(
        "tc,rc->tr", middle_low, output_whole, preferred_element_type=jnp.float32
    )
    attention_grad_low = attention_grad.astype(jnp.bfloat16)
    mixed_grad = attention_grad_low.reshape(count, key_heads, group, head_size).transpose(
        1, 2, 0, 3
    )
    delta = jnp.sum(mixed_grad.astype(jnp.float32) * normalized, -1)

    def cycle_step(index, carry):
        keys_held, values_held, key_acc, value_acc, query_acc = carry
        anchor = (own_index - index) % cycles
        key_pos = lax.dynamic_slice_in_dim(sequence_pos, anchor * count, count)
        keys_piece = keys_held.astype(jnp.bfloat16).reshape(count, key_heads, head_size)
        values_piece = values_held.astype(jnp.bfloat16).reshape(count, key_heads, head_size)
        allowed = token_offsets[:, None] >= key_pos[None, :]
        scores = (
            jnp.einsum(
                "kgtd,skd->kgts", query_grouped, keys_piece, preferred_element_type=jnp.float32
            )
            * scale
        )
        probs = jnp.where(allowed, jnp.exp(scores - logsum[..., None]), 0.0)
        value_acc = value_acc + jnp.einsum(
            "kgts,kgtd->skd",
            probs.astype(jnp.bfloat16),
            mixed_grad,
            preferred_element_type=jnp.float32,
        ).reshape(count, key_width)
        prob_grad = jnp.einsum(
            "kgtd,skd->kgts", mixed_grad, values_piece, preferred_element_type=jnp.float32
        )
        score_grad = (probs * (prob_grad - delta[..., None])).astype(jnp.bfloat16)
        query_acc = (
            query_acc
            + jnp.einsum(
                "kgts,skd->kgtd", score_grad, keys_piece, preferred_element_type=jnp.float32
            )
            * scale
        )
        key_acc = (
            key_acc
            + jnp.einsum(
                "kgts,kgtd->skd", score_grad, query_grouped, preferred_element_type=jnp.float32
            ).reshape(count, key_width)
            * scale
        )
        moved = (
            from_behind(keys_held.astype(jnp.bfloat16), "ctx", 1).astype(keys_held.dtype),
            from_behind(values_held.astype(jnp.bfloat16), "ctx", 1).astype(values_held.dtype),
            from_behind(key_acc.astype(jnp.bfloat16), "ctx", 1).astype(key_acc.dtype),
            from_behind(value_acc.astype(jnp.bfloat16), "ctx", 1).astype(value_acc.dtype),
        )
        return (moved[0], moved[1], moved[2], moved[3], query_acc)

    start_cycle = (
        key_low.astype(jnp.float32),
        value_low.astype(jnp.float32),
        jnp.zeros((count, key_width), jnp.float32),
        jnp.zeros((count, key_width), jnp.float32),
        jnp.zeros((key_heads, group, count, head_size), jnp.float32),
    )
    cycle_done = lax.fori_loop(0, cycles, cycle_step, start_cycle)
    key_acc = cycle_done[2]
    value_acc = cycle_done[3]
    query_acc = cycle_done[4]
    query_rot_grad = query_acc.transpose(2, 0, 1, 3).reshape(count, heads, head_size)
    query_normed_grad = query_rot_grad * cosine + rotate_back(query_rot_grad * sine)
    query_heads_grad, query_part = norm_back(
        query_heads, query_scale, query_gain, query_normed_grad
    )
    query_low_grad = query_heads_grad.reshape(count, query_width).astype(jnp.bfloat16)
    key_rot_grad = key_acc.reshape(count, key_heads, head_size)
    key_normed_grad = key_rot_grad * cosine + rotate_back(key_rot_grad * sine)
    key_heads_grad, key_part = norm_back(key_heads_raw, key_scale, key_norm_gain, key_normed_grad)
    key_low_grad = key_heads_grad.reshape(count, key_width).astype(jnp.bfloat16)
    value_low_grad = value_acc.astype(jnp.bfloat16)
    first_grad = column_products(
        (query_low_grad, key_low_grad, value_low_grad),
        lax.all_gather((query_weight, key_matrix, value_matrix), "fsdp", axis=0, tiled=True),
    )
    input_part, attention_part = norm_back(hidden_in, first_scale, attention_gain, first_grad)
    input_gradient = (middle_grad + input_part)[None]
    rights_first = jnp.concatenate([query_low_grad, key_low_grad, value_low_grad], 1)
    rights_second = jnp.concatenate([gate_low, up_low], 1)
    pairs = (
        (first, rights_first),
        (second, rights_second),
        (middle_low, attention_low),
        (cotangent, hidden_low),
    )
    parts = []
    for left, right in pairs:
        parts.append(jnp.einsum("tr,tc->rc", left, right, preferred_element_type=jnp.float32))
    sums = lax.psum_scatter(
        jnp.concatenate(parts, 1), ("ctx", "fsdp"), scatter_dimension=0, tiled=True
    )
    edges = [0, query_width, query_width + key_width, query_width + 2 * key_width]
    edges = edges + [edges[3] + inner_width, edges[3] + 2 * inner_width]
    edges = edges + [edges[5] + query_width, edges[5] + query_width + inner_width]
    query_gradient = sums[:, edges[0] : edges[1]]
    key_gradient = sums[:, edges[1] : edges[2]]
    value_gradient = sums[:, edges[2] : edges[3]]
    gate_gradient = sums[:, edges[3] : edges[4]]
    up_gradient = sums[:, edges[4] : edges[5]]
    output_gradient = sums[:, edges[5] : edges[6]].T
    down_gradient = sums[:, edges[6] : edges[7]].T
    attention_total, query_total, key_total, feedforward_total = lax.psum(
        (attention_part, query_part, key_part, feedforward_part), ("ctx", "fsdp")
    )
    return (
        layer_output,
        input_gradient,
        attention_total,
        query_gradient,
        key_gradient,
        value_gradient,
        query_total,
        key_total,
        output_gradient,
        feedforward_total,
        gate_gradient,
        up_gradient,
        down_gradient,
    )


MESH = pl.DeviceIdType.MESH
f32 = jnp.float32
bf16 = jnp.bfloat16


def dot(left, right):
    return jnp.dot(left, right, preferred_element_type=f32)


def dot_nt(left, right):
    return lax.dot_general(left, right, (((1,), (1,)), ((), ())), preferred_element_type=f32)


def dot_tn(left, right):
    return lax.dot_general(left, right, (((0,), (0,)), ((), ())), preferred_element_type=f32)


def layer_kernel(
    n, planes, block, head, group, fw,
    x_ref, dy_ref, pos_row, inverse_ref, step_cos, step_sin, ag_ref, fg_ref, qg_ref, kg_ref,
    wq, wk, wv, wo, wg, wu, wd,
    out_ref, dx_ref, gains_ref, got_a, got_b, got_c, got_out, got_qkv,
    w_qkv, w_gu, w_out, w_down, t_out, t_down,
    first, dy_all, second, first_t, dy_t, second_t, dmid_t,
    positions, cosine, sine,
    raw, queries, keys, values, keys_t, values_t, probs, sums, mixed_t, mixed_low,
    hidden, d_gu, d_qkv, dk_acc, dv_acc,
    stage_a, stage_b, stage_c, stage_out, stage_qkv,
    land_a, land_b, land_c, land_out, land_qkv,
    rs_sa, rs_ra, rs_sb, rs_rb, rs_kept, rs_acc,
    middle, d_middle, gain_own, gain_plane, gain_all,
    local_sem, wz_send, wz_recv, hand_send, hand_recv,
    ag_send, ag_recv, ra_send, ra_recv, rb_send, rb_recv,
    zr_send, zr_recv, aa_send, aa_recv, gp_send, gp_recv, gz_send, gz_recv,
):
    c = lax.axis_index("ctx")
    z = lax.axis_index("fsdp")
    dmid = first
    cy, cx, ck = lax.div(c, 4), lax.rem(lax.div(c, 2), 2), lax.rem(c, 2)
    ci = lax.rem(c, 4)
    sign = 1 - 2 * ck
    qw, kw = group * head, head
    pw = 128
    thirds = fw // pw
    piece = pw // 4
    width = x_ref.shape[1]
    scale = head ** (-0.5)
    log2e = 1.4426950408889634
    gots = (got_a, got_b, got_c, got_out, got_qkv)
    stages = (stage_a, stage_b, stage_c, stage_out, stage_qkv)
    lands = (land_a, land_b, land_c, land_out, land_qkv)

    def partner(j):
        y = lax.rem(cy + lax.div(j, 4), 2)
        x = lax.rem(cx + lax.rem(lax.div(j, 2), 2), 2)
        k = lax.rem(ck + lax.rem(j, 2), 2)
        return y * 4 + x * 2 + k

    def chip(slot):
        return lax.rem(cy + lax.div(slot, 2), 2) * 2 + lax.rem(cx + lax.rem(slot, 2), 2)

    def rows(start, size):
        return pl.ds(pl.multiple_of(start * size, size), size)

    def remote(src, dst, send, recv, ctx, plane):
        return pltpu.make_async_remote_copy(
            src_ref=src, dst_ref=dst, send_sem=send, recv_sem=recv,
            device_id={"ctx": ctx, "fsdp": plane}, device_id_type=MESH,
        )

    in_plane, along = [], []

    def launch(started, copy, when=None):
        if when is None:
            copy().start()
        else:
            pl.when(when)(lambda: copy().start())
        started.append((copy, when))

    def drain(started):
        for copy, when in started:
            if when is None:
                copy().wait_send()
            else:
                pl.when(when)(lambda copy=copy: copy().wait_send())
        started.clear()

    own_rows = wq.shape[0]
    out_rows = wo.shape[0] // n

    def own_slices():
        mine = rows(z, own_rows)
        pairs = [
            (wq.at[:, rows(c, qw)], w_qkv.at[mine, 0:qw]),
            (wk.at[:, rows(c, kw)], w_qkv.at[mine, qw:qw + kw]),
            (wv.at[:, rows(c, kw)], w_qkv.at[mine, qw + kw:qw + 2 * kw]),
            (wo.at[rows(c, out_rows)], t_out.at[rows(z, out_rows)]),
        ]
        for t in range(thirds):
            at = 2 * pw * t
            pairs.append((wg.at[:, rows(c * thirds + t, pw)], w_gu.at[mine, at:at + pw]))
            pairs.append((wu.at[:, rows(c * thirds + t, pw)], w_gu.at[mine, at + pw:at + 2 * pw]))
            pairs.append((wd.at[rows((cy * thirds + t) * 4 + ci, piece)], t_down.at[t, rows(z, piece)]))
        return pairs

    local = [pltpu.make_async_copy(src, dst, local_sem.at[i]) for i, (src, dst) in enumerate(own_slices())]
    for copy in local:
        copy.start()

    for land in lands:
        @pl.when(z == 0)
        def _(land=land):
            land[0] = jnp.zeros(land.shape[1:], bf16)

        @pl.when(z == planes - 1)
        def _(land=land):
            land[planes] = jnp.zeros(land.shape[1:], bf16)

    barrier = pltpu.get_barrier_semaphore()
    for j in range(1, n):
        pl.semaphore_signal(barrier, inc=1, device_id={"ctx": partner(j), "fsdp": z}, device_id_type=MESH)
    for d in range(1, planes):
        pl.semaphore_signal(
            barrier, inc=1, device_id={"ctx": c, "fsdp": lax.rem(z + d, planes)}, device_id_type=MESH)
    x = x_ref[...].astype(f32)
    x_scale = lax.rsqrt(jnp.mean(x * x, -1, keepdims=True) + epsilon)
    first[rows(c, block)] = (x * x_scale * ag_ref[...]).astype(bf16)
    dy_all[rows(c, block)] = dy_ref[...]
    for copy in local[:3]:
        copy.wait()
    pl.semaphore_wait(barrier, n + planes - 2)

    def inside(t):
        return jnp.logical_and(t >= 0, t < planes)

    weights = [
        (lambda o: w_qkv.at[rows(o, own_rows)], None),
        (lambda o: t_out.at[rows(o, out_rows)], 0),
    ]
    for t in range(thirds):
        weights.append((lambda o, t=t: w_gu.at[rows(o, own_rows), 2 * pw * t:2 * pw * (t + 1)], None))
        weights.append((lambda o, t=t: t_down.at[t, rows(o, piece)], 1 + t))

    def weight_copy(w, slot, origin, target):
        part = weights[w][0](origin)
        return remote(part, part, wz_send.at[w, slot], wz_recv.at[w, origin], c, target)

    def hand_split(origin, valid):
        mine = 2 * origin + cy == c
        return jnp.logical_and(valid, jnp.logical_not(mine)), jnp.logical_and(valid, mine)

    def weight_start(w):
        for side in range(2):
            d = sign * (1 - 2 * side)
            launch(along, lambda side=side, d=d: weight_copy(w, side, z, z + d), inside(z + d))
        if weights[w][1] is not None:
            hand_over(w, z, 0, *hand_split(z, True))

    def hand_target(h):
        if h == 0:
            return lambda i: w_out.at[rows(i, out_rows)]
        return lambda i: w_down.at[rows((h - 1) * 4 + i, piece)]

    def hand_copy(w, origin, slot):
        h = weights[w][1]
        return remote(
            weights[w][0](origin), hand_target(h)(ci), hand_send.at[h, slot], hand_recv.at[h, ci], 2 * origin + cy, z)

    def hand_over(w, origin, slot, away, here):
        launch(in_plane, lambda: hand_copy(w, origin, slot), away)

        @pl.when(here)
        def _():
            hand_target(weights[w][1])(ci)[...] = weights[w][0](origin)[...]

    def hand_arrive(w):
        h = weights[w][1]
        for i in range(4):
            @pl.when(4 * ck + i != c)
            def _(i=i):
                part = hand_target(h)(i)
                remote(part, part, hand_send.at[h, 0], hand_recv.at[h, i], c, z).wait_recv()

    hops = {}
    for d in range(1, planes):
        for side, way in enumerate((1, -1)):
            origin = z - way * d
            valid = inside(origin)
            passed = jnp.logical_and(valid, inside(z + way))
            hops[d, side] = origin, z + way, valid, passed, hand_split(origin, valid)

    def weight_hop(w, d):
        for side in range(2):
            origin, following, valid, passed, split = hops[d, side]
            pl.when(valid)(lambda: weight_copy(w, 0, origin, z).wait_recv())
            if d < planes - 1:
                launch(
                    along,
                    lambda side=side, origin=origin, following=following: weight_copy(
                        w, 2 * d + side, origin, following),
                    passed)
            if weights[w][1] is not None:
                hand_over(w, origin, 2 * d - 1 + side, *split)

    def gather_copy(buf, g, j, send, origin, target):
        part = buf.at[rows(origin, block)]
        return remote(part, part, ag_send.at[g, send], ag_recv.at[g, j], target, z)

    def gather_start(buf, g):
        for j in (1, 2 + 2 * ck, 4 - 2 * ck, 6):
            launch(in_plane, lambda j=j: gather_copy(buf, g, j, j, c, partner(j)))

    def gather_forward(buf, g, j):
        return gather_copy(buf, g, j + 1, j + 1, partner(j), partner(1))

    def gather_finish(buf, g):
        for j in (2, 4, 6):
            gather_copy(buf, g, j, j, partner(j), c).wait_recv()
            launch(in_plane, lambda j=j: gather_forward(buf, g, j))
        for j in (1, 3, 5, 7):
            gather_copy(buf, g, j, j, partner(j), c).wait_recv()

    def gather_step(buf, g, slot):
        def arrive(j):
            gather_copy(buf, g, j, j, partner(j), c).wait_recv()
            gather_forward(buf, g, j).start()

        @pl.when(slot == 1)
        def _():
            arrive(2)
            arrive(4)

        @pl.when(slot == 3)
        def _():
            arrive(6)

        gather_copy(buf, g, 2 * slot + 1, 0, partner(2 * slot + 1), c).wait_recv()

    def gather_stepped(buf, g):
        for j in (2, 4, 6):
            in_plane.append((lambda j=j: gather_forward(buf, g, j), None))

    def sum_pair_copy(s, slot):
        return remote(rs_sa.at[s % 2, slot], rs_ra.at[s % 2, slot], ra_send.at[s, slot], ra_recv.at[s, slot], partner(1), z)

    def sum_chip_copy(s, slot):
        return remote(
            rs_sb.at[s % 2, slot], rs_rb.at[s % 2, slot], rb_send.at[s, slot], rb_recv.at[s, slot], partner(2 * slot), z)

    def sum_slot(p):
        return jnp.where(p == 0, 3, jnp.where(p == 1, 2 - ck, jnp.where(p == 2, 1 + ck, 0)))

    def sum_start(s, left, partial, prepare=None, ready=None, during=()):
        if prepare is not None:
            prepare(chip(sum_slot(0)))
        if ready is not None:
            ready()

        def body(p, carry):
            slot = sum_slot(p)
            at = [rows(partner(2 * slot + 1), block), rows(partner(2 * slot), block)]
            both = partial(jnp.concatenate([left[i] for i in at], 0))
            rs_sa[s % 2, slot] = both[:block].astype(bf16)
            sum_pair_copy(s, slot).start()
            rs_kept[lax.rem(p, 2)] = both[block:]
            if prepare is not None:
                @pl.when(p < 3)
                def _():
                    prepare(chip(sum_slot(p + 1)))

            @pl.when(p > 0)
            def _():
                before = sum_slot(p - 1)
                sum_pair_copy(s, before).wait_recv()
                rs_sb[s % 2, before] = (
                    rs_kept[lax.rem(p + 1, 2)] + rs_ra[s % 2, before].astype(f32)).astype(bf16)
                sum_chip_copy(s, before).start()

            for k, poll in enumerate(during):
                pl.when(p == k)(poll)
            return carry

        lax.fori_loop(0, 4, body, 0)
        for slot in range(4):
            in_plane.append((lambda slot=slot: sum_pair_copy(s, slot), None))
            if slot > 0:
                in_plane.append((lambda slot=slot: sum_chip_copy(s, slot), None))
        sum_pair_copy(s, 0).wait_recv()
        rs_acc[s % 2] = rs_kept[1] + rs_ra[s % 2, 0].astype(f32)

    def sum_finish(s):
        total = rs_acc[s % 2]
        for slot in (1, 2, 3):
            sum_chip_copy(s, slot).wait_recv()
            total = total + rs_rb[s % 2, slot].astype(f32)
        return total

    per = block // planes

    def weight_grad(m, parts):
        def body(i, carry):
            at = 0
            for left, right in parts:
                value = right()
                grad = dot(left[rows(i, 2 * block)], value)
                for k in range(2):
                    for t in range(planes):
                        start = k * block + t * per
                        stages[m][t, 2 * i + k, :, at:at + value.shape[1]] = grad[start:start + per].astype(bf16)
                at += value.shape[1]
            return carry

        lax.fori_loop(0, n // 2, body, 0)
        at_edge = jnp.logical_or(z == 0, z == planes - 1)
        for k in range(planes - 1):
            t = jnp.where(z == 0, planes - 1 - k, k)
            launch(along, lambda t=t: grad_copy(m, t), at_edge)

    def grad_copy(m, t):
        way = jnp.where(z < t, 1, -1)
        last = z + way == t
        slot = jnp.where(jnp.logical_and(last, way < 0), planes, t)
        return remote(
            stages[m].at[t], lands[m].at[slot], zr_send.at[m, t], zr_recv.at[m, slot], c, z + way)

    def grad_arrive(m, slot):
        part = lands[m].at[slot]
        remote(part, part, zr_send.at[m, 0], zr_recv.at[m, slot], c, z).wait_recv()

    def grad_pass(m, t, valid):
        @pl.when(valid)
        def _():
            grad_arrive(m, t)

            def body(i, carry):
                stages[m][t, i] = (stages[m][t, i].astype(f32) + lands[m][t, i].astype(f32)).astype(bf16)
                return carry

            lax.fori_loop(0, n, body, 0)

        launch(along, lambda: grad_copy(m, t), valid)

    def grad_near(m):
        for t in (3, 2):
            grad_pass(m, t, z == 1)
        for t in (0, 1):
            grad_pass(m, t, z == 2)

    def grad_far(m):
        grad_pass(m, 3, z == 2)
        grad_pass(m, 0, z == 1)

    def owner_copy(m, j):
        return remote(lands[m].at[z, partner(j)], gots[m].at[c], aa_send.at[m, j], aa_recv.at[m, j], partner(j), z)

    def hand_out(m):
        pl.when(z > 0)(lambda: grad_arrive(m, z))
        pl.when(z < planes - 1)(lambda: grad_arrive(m, planes))

        def body(i, carry):
            total = stages[m][z, i].astype(f32) + lands[m][z, i].astype(f32) + lands[m][planes, i].astype(f32)
            lands[m][z, i] = total.astype(bf16)
            return carry

        lax.fori_loop(0, n, body, 0)
        for j in (2 + 2 * ck, 3 + 2 * ck, 4 - 2 * ck, 5 - 2 * ck, 6, 7, 1):
            launch(in_plane, lambda j=j: owner_copy(m, j))
        gots[m][c] = lands[m][z, c]

    def hand_receive(m):
        for j in range(1, n):
            owner_copy(m, j).wait_recv()

    weight_start(0)
    gather_start(first, 0)
    for copy in local[3:]:
        copy.wait()

    spread = jnp.broadcast_to(pos_row[...].astype(f32), (head, pos_row.shape[1]))
    positions[...] = spread.T
    side = jnp.where(lax.broadcasted_iota(jnp.int32, (1, head), 1) < head // 2, -1.0, 1.0)

    def table(i, carry):
        run = step_cos.shape[0]
        at = rows(i, run)
        start = positions[pl.ds(pl.multiple_of(i * run, run), 1)] * inverse_ref[...]
        start_cos, start_sin = jnp.cos(start), jnp.sin(start)
        cosine[at] = start_cos * step_cos[...] - start_sin * step_sin[...]
        sine[at] = (start_sin * step_cos[...] + start_cos * step_sin[...]) * side
        return carry

    def turn_over(src, dst):
        def body(i, carry):
            at = rows(i, block)
            dst[:, at] = src[at].T
            return carry

        lax.fori_loop(0, n, body, 0)

    lax.fori_loop(0, 2 * n, table, 0)
    weight_hop(0, 1)
    gather_finish(first, 0)
    weight_hop(0, 2)
    weight_start(1)
    gather_start(dy_all, 1)
    turn_over(first, first_t)
    weight_hop(0, 3)
    weight_start(2)
    weight_start(3)

    def turn(value, at):
        return value * cosine[at] + pltpu.roll(value, head // 2, 1) * sine[at]

    def turn_back(grad, at):
        return grad * cosine[at] - pltpu.roll(grad, head // 2, 1) * sine[at]

    def project(i, carry):
        at = rows(i, 2 * block)
        result = dot(first[at], w_qkv[...])
        raw[at] = result[:, :qw + kw]
        low_values = result[:, qw + kw:].astype(bf16)
        values[at] = low_values
        values_t[:, at] = low_values.T
        for h in range(group + 1):
            part = result[:, h * head:(h + 1) * head]
            inv = lax.rsqrt(jnp.mean(part * part, -1, keepdims=True) + epsilon)
            gain = qg_ref[...] if h < group else kg_ref[...]
            turned = turn(part * inv * gain, at)
            if h < group:
                queries[at, h * head:(h + 1) * head] = (turned * (scale * log2e)).astype(bf16)
            else:
                low_keys = turned.astype(bf16)
                keys[at] = low_keys
                keys_t[:, at] = low_keys.T
        return carry

    lax.fori_loop(0, n // 4, project, 0)
    weight_hop(1, 1)
    lax.fori_loop(n // 4, n // 2, project, 0)
    weight_hop(1, 2)
    gather_finish(dy_all, 1)

    def stack(ref, at):
        return jnp.concatenate([ref[at, h * head:(h + 1) * head] for h in range(group)], 0)

    def attend_block(i):
        at = rows(i, block)
        scores = dot_nt(keys[...], stack(queries, at))
        allowed = positions[...] <= pos_row[:, at].astype(f32)
        weight = jnp.concatenate(
            [jnp.exp2(jnp.where(allowed, scores[:, h * block:(h + 1) * block], masked_score)) for h in range(group)], 1)
        inv = 1.0 / jnp.sum(weight, 0, keepdims=True)
        low_weight = weight.astype(bf16)
        probs[i] = low_weight
        sums[i] = inv
        result = dot(values_t[...], low_weight) * inv
        mixed_t[i] = result
        for h in range(group):
            mixed_low[at, h * head:(h + 1) * head] = result[:, h * block:(h + 1) * block].T.astype(bf16)

    def attend(place):
        attend_block(2 * place)
        attend_block(2 * place + 1)

    def output_ready():
        weight_hop(1, 3)
        weight_start(4)
        weight_start(5)
        hand_arrive(1)
        drain(in_plane)

    def hop_third(t, d):
        weight_hop(2 + 2 * t, d)
        weight_hop(3 + 2 * t, d)

    sum_start(
        0, mixed_low, lambda left: dot(left, w_out[...]), attend, output_ready,
        (lambda: hop_third(0, 1), lambda: hop_third(0, 2)))
    weight_start(6)
    weight_start(7)
    turn_over(dy_all, dy_t)
    hop_third(0, 3)
    mid = x_ref[...].astype(f32) + sum_finish(0)
    middle[...] = mid
    mid_scale = lax.rsqrt(jnp.mean(mid * mid, -1, keepdims=True) + epsilon)
    second[rows(c, block)] = (mid * mid_scale * fg_ref[...]).astype(bf16)
    gather_start(second, 2)
    hop_third(1, 1)
    hand_arrive(3)

    def feed(t, at):
        units, pair = slice(t * pw, (t + 1) * pw), 2 * pw * t
        both = dot(second[at], w_gu[:, pair:pair + 2 * pw])
        back = dot_nt(dy_all[at], w_down[units])
        gate, up = both[:, :pw], both[:, pw:]
        sig = 1.0 / (1.0 + jnp.exp(-gate))
        silu = gate * sig
        hidden[at, units] = (silu * up).astype(bf16)
        d_gu[at, pair:pair + pw] = (back * up * sig * (1.0 + gate * (1.0 - sig))).astype(bf16)
        d_gu[at, pair + pw:pair + 2 * pw] = (back * silu).astype(bf16)

    def feed_arriving(slot, carry):
        gather_step(second, 2, slot)
        at = rows(chip(slot), 2 * block)
        feed(0, at)
        second_t[:, at] = second[at].T
        pl.when(slot == 2)(lambda: hop_third(1, 2))
        return carry

    def third_grad(t):
        weight_grad(t, [
            (second_t, lambda: d_gu[:, 2 * pw * t:2 * pw * (t + 1)]),
            (dy_t, lambda: hidden[:, t * pw:(t + 1) * pw]),
        ])

    def feed_third(t):
        def body(i, carry):
            feed(t, rows(i, 2 * block))
            return carry

        lax.fori_loop(0, n // 2, body, 0)

    lax.fori_loop(0, n // 2, feed_arriving, 0)
    gather_stepped(second, 2)
    hop_third(2, 1)
    third_grad(0)
    hop_third(1, 3)
    hand_arrive(5)
    feed_third(1)
    hop_third(2, 2)
    hop_third(2, 3)
    hand_arrive(7)
    sum_start(
        1, d_gu, lambda left: dot_nt(left, w_gu[...]),
        lambda place: feed(thirds - 1, rows(place, 2 * block)))
    third_grad(1)
    third_grad(2)
    d_second = sum_finish(1)

    def norm_back(value, gain, grad):
        inv = lax.rsqrt(jnp.mean(value * value, -1, keepdims=True) + epsilon)
        weighted = grad * gain
        inner = jnp.mean(weighted * value, -1, keepdims=True)
        result = inv * weighted - value * (inv * inv * inv * inner)
        return result, jnp.sum(grad * value * inv, 0, keepdims=True)

    gain_own[...] = jnp.zeros_like(gain_own)
    part, gain_own[1:2, :] = norm_back(middle[...], fg_ref[...], d_second)
    d_mid = dy_ref[...].astype(f32) + part
    d_middle[...] = d_mid
    dmid[rows(c, block)] = d_mid.astype(bf16)
    gather_start(dmid, 3)
    grad_near(0)

    dk_acc[...] = jnp.zeros_like(dk_acc)
    dv_acc[...] = jnp.zeros_like(dv_acc)

    def attend_back_block(i, d_mix):
        at = rows(i, block)
        d_mix_t = jnp.concatenate([d_mix[h * head:(h + 1) * head] for h in range(group)], 1)
        d_mix_t = (d_mix_t.astype(bf16).astype(f32) * sums[i]).astype(bf16)
        delta = jnp.sum(d_mix_t.astype(f32) * mixed_t[i], 0, keepdims=True)
        weight = probs[i]
        d_prob = dot(values[...], d_mix_t)
        d_score = (weight.astype(f32) * (d_prob - delta)).astype(bf16)
        d_query = dot(keys_t[...], d_score) * scale
        gained = jnp.zeros((1, head), f32)
        for h in range(group):
            grad = turn_back(d_query[:, h * block:(h + 1) * block].T, at)
            part, gain_part = norm_back(raw[at, h * head:(h + 1) * head], qg_ref[...], grad)
            d_qkv[at, h * head:(h + 1) * head] = part.astype(bf16)
            gained = gained + gain_part
        return dot(weight, d_mix_t.T), dot(d_score, stack(queries, at)), gained

    def attend_back(slot, q_sum):
        gather_step(dmid, 3, slot)
        at = rows(chip(slot), 2 * block)
        d_mix = dot_nt(w_out[...], dmid[at])
        dmid_t[:, at] = dmid[at].T
        dv_one, dk_one, gain_one = attend_back_block(2 * chip(slot), d_mix[:, :block])
        dv_two, dk_two, gain_two = attend_back_block(2 * chip(slot) + 1, d_mix[:, block:])
        dv_acc[...] += dv_one + dv_two
        dk_acc[...] += dk_one + dk_two
        return q_sum + gain_one + gain_two

    zero = jnp.zeros((1, head), f32)
    gain_own[2:3, 0:head] = lax.fori_loop(0, n // 2, attend_back, zero)
    gather_stepped(dmid, 3)
    weight_grad(3, [(dmid_t, lambda: mixed_low[...])])
    grad_far(0)
    grad_near(1)
    drain(in_plane)
    sum_start(2, hidden, lambda left: dot(left, w_down[...]))

    def project_back(i, k_sum):
        at = rows(i, 2 * block)
        grad = turn_back(dk_acc[at] * (1.0 / log2e), at)
        part, gain_part = norm_back(raw[at, qw:qw + kw], kg_ref[...], grad)
        d_qkv[at, qw:qw + kw] = part.astype(bf16)
        d_qkv[at, qw + kw:] = dv_acc[at].astype(bf16)
        return k_sum + gain_part

    gain_own[3:4, 0:head] = lax.fori_loop(0, n // 2, project_back, zero)

    weight_grad(4, [(first_t, lambda: d_qkv[...])])
    sum_start(3, d_qkv, lambda left: dot_nt(left, w_qkv[...]))
    grad_far(1)
    grad_near(2)
    out_ref[...] = (middle[...] + sum_finish(2)).astype(bf16)
    hand_out(0)
    grad_far(2)
    grad_near(3)
    hand_out(1)
    x_part, gain_own[0:1, :] = norm_back(x_ref[...].astype(f32), ag_ref[...], sum_finish(3))
    dx_ref[...] = d_middle[...] + x_part

    def gain_plane_copy(j):
        return remote(gain_own, gain_plane.at[c], gp_send.at[j], gp_recv.at[j], partner(j), z)

    def gain_copy(d):
        return remote(gain_all.at[z], gain_all.at[z], gz_send.at[d], gz_recv.at[d], c, lax.rem(z + d, planes))

    for j in range(1, n):
        launch(in_plane, lambda j=j: gain_plane_copy(j))
    gain_plane[c] = gain_own[...]
    grad_far(3)
    hand_out(2)
    for j in range(1, n):
        gain_plane_copy(j).wait_recv()
    total = gain_plane[0]
    for i in range(1, n):
        total = total + gain_plane[i]
    gain_all[z] = total
    for d in range(1, planes):
        launch(along, lambda d=d: gain_copy(d))
    grad_near(4)
    hand_out(3)
    grad_far(4)
    for d in range(1, planes):
        origin = gain_all.at[lax.rem(z + planes - d, planes)]
        remote(origin, origin, gz_send.at[d], gz_recv.at[d], c, z).wait_recv()
    total = gain_all[0]
    for i in range(1, planes):
        total = total + gain_all[i]
    gains_ref[...] = total

    hand_out(4)
    for m in range(5):
        hand_receive(m)
    drain(in_plane)
    drain(along)


def finish_kernel(
    n, head, out_in, dx_in, gains_in, got_a, got_b, got_c, got_out, got_qkv,
    out_ref, dx_ref, ag_ref, q_ref, k_ref, v_ref, qg_ref, kg_ref, o_ref, fg_ref, g_ref, u_ref, d_ref,
):
    out_ref[...] = out_in[...]
    dx_ref[...] = dx_in[...]
    ag_ref[...] = gains_in[0:1, :]
    fg_ref[...] = gains_in[1:2, :]
    qg_ref[...] = gains_in[2:3, 0:head]
    kg_ref[...] = gains_in[3:4, 0:head]
    qw, kw = q_ref.shape[1] // n, k_ref.shape[1] // n
    pw = got_a.shape[2] // 3
    thirds = (got_a, got_b, got_c)
    for i in range(n):
        q_ref[:, i * qw:(i + 1) * qw] = got_qkv[i, :, 0:qw].astype(f32)
        k_ref[:, i * kw:(i + 1) * kw] = got_qkv[i, :, qw:qw + kw].astype(f32)
        v_ref[:, i * kw:(i + 1) * kw] = got_qkv[i, :, qw + kw:].astype(f32)
        o_ref[:, i * qw:(i + 1) * qw] = got_out[i].astype(f32)
        for t, got in enumerate(thirds):
            at = (i * len(thirds) + t) * pw
            g_ref[:, at:at + pw] = got[i, :, 0:pw].astype(f32)
            u_ref[:, at:at + pw] = got[i, :, pw:2 * pw].astype(f32)
            d_ref[:, at:at + pw] = got[i, :, 2 * pw:].astype(f32)


def plane_device(
    layer_input,
    token_positions,
    attention_gain,
    query_weight,
    key_matrix,
    value_matrix,
    query_gain,
    key_norm_gain,
    output_weight,
    feedforward_gain,
    gate_weight,
    up_weight,
    down_weight,
    out_cotangent,
):
    n = lax.axis_size("ctx")
    planes = lax.axis_size("fsdp")
    block, width = layer_input.shape[1:]
    length = token_positions.shape[1]
    head = query_gain.shape[0]
    qw = query_weight.shape[1] // n
    kw = key_matrix.shape[1] // n
    fw = gate_weight.shape[1] // n
    group = qw // head
    per = block // planes
    half = head // 2
    inverse = np.power(rope_base, -np.arange(half) * 2.0 / head).astype(np.float32)
    inverse = np.concatenate([inverse, inverse])[None]
    steps = np.arange(block // 2)[:, None] * inverse.astype(np.float64)
    step_cos, step_sin = (jnp.asarray(f(steps).astype(np.float32)) for f in (np.cos, np.sin))
    inverse = jnp.asarray(inverse)
    vmem = pl.BlockSpec(memory_space=pltpu.VMEM)
    hbm = pl.BlockSpec(memory_space=pl.ANY)
    dma = pltpu.SemaphoreType.DMA
    sizes = (fw, fw, fw, qw, qw + 2 * kw)
    low = lambda *shape: pltpu.VMEM(shape, bf16)
    wide = lambda *shape: pltpu.VMEM(shape, f32)
    scratch = [
        low(width, qw + 2 * kw), low(width, 2 * fw), low(qw, width), low(fw, width),
        low(planes * (output_weight.shape[0] // n), width), low(3, planes * 32, width),
        low(length, width), low(length, width), low(length, width),
        low(width, length), low(width, length), low(width, length), low(width, length),
        wide(length, head), wide(length, head), wide(length, head),
        wide(length, qw + kw), low(length, qw), low(length, kw), low(length, kw),
        low(kw, length), low(kw, length), low(n, length, group * block), wide(n, 1, group * block), wide(n, head, group * block), low(length, qw),
        low(length, fw), low(length, 2 * fw), low(length, qw + 2 * kw),
        wide(length, kw), wide(length, kw),
    ]
    scratch += [low(planes, n, per, size) for size in sizes]
    scratch += [low(planes + 1, n, per, size) for size in sizes]
    scratch += [low(2, 4, block, width) for _ in range(4)] + [wide(2, block, width), wide(2, block, width)]
    scratch += [
        wide(block, width), wide(block, width), wide(8, width), wide(n, 8, width), wide(planes, 8, width),
        dma((13,)), dma((8, 6)), dma((8, planes)), dma((4, 7)), dma((4, 4)),
        dma((4, n)), dma((4, n)), dma((4, 4)), dma((4, 4)), dma((4, 4)), dma((4, 4)),
        dma((5, planes)), dma((5, planes + 1)), dma((5, n)), dma((5, n)), dma((n,)), dma((n,)),
        dma((planes,)), dma((planes,)),
    ]
    shapes = [
        jax.ShapeDtypeStruct((block, width), bf16),
        jax.ShapeDtypeStruct((block, width), f32),
        jax.ShapeDtypeStruct((8, width), f32),
    ] + [jax.ShapeDtypeStruct((n, per, size), bf16) for size in sizes]
    results = pl.pallas_call(
        functools.partial(layer_kernel, n, planes, block, head, group, fw),
        out_shape=shapes,
        in_specs=[vmem] * 10 + [hbm] * 7,
        out_specs=[vmem] * len(shapes),
        scratch_shapes=scratch,
        compiler_params=pltpu.CompilerParams(
            collective_id=0, has_side_effects=True, vmem_limit_bytes=60 * 1024 * 1024),
    )(
        layer_input[0], out_cotangent[0], token_positions, inverse, step_cos, step_sin,
        attention_gain[None], feedforward_gain[None], query_gain[None], key_norm_gain[None],
        query_weight, key_matrix, value_matrix, output_weight, gate_weight, up_weight, down_weight,
    )
    plain = lambda rows, columns, kind=f32: jax.ShapeDtypeStruct((rows, columns), kind)
    finals = [
        plain(block, width, bf16), plain(block, width), plain(1, width),
        plain(per, n * qw), plain(per, n * kw), plain(per, n * kw), plain(1, head), plain(1, head),
        plain(per, n * qw), plain(1, width), plain(per, n * fw), plain(per, n * fw), plain(per, n * fw),
    ]
    done = pl.pallas_call(
        functools.partial(finish_kernel, n, head),
        out_shape=finals,
        in_specs=[vmem] * len(shapes),
        out_specs=[vmem] * len(finals),
    )(*results)
    out, dx, ag, q, k, v, qg, kg, o, fg, g, u, d = done
    return out[None], dx[None], ag[0], q, k, v, qg[0], kg[0], o.T, fg[0], g, u, d.T


def solution(mesh):
    in_specs = (
        P("fsdp", "ctx", None),
        P("fsdp", None),
        P(),
        P("fsdp", None),
        P("fsdp", None),
        P("fsdp", None),
        P(),
        P(),
        P("fsdp", None),
        P(),
        P("fsdp", None),
        P("fsdp", None),
        P("fsdp", None),
        P("fsdp", "ctx", None),
    )
    out_specs = (
        P("fsdp", "ctx", None),
        P("fsdp", "ctx", None),
        P(),
        P(("ctx", "fsdp"), None),
        P(("ctx", "fsdp"), None),
        P(("ctx", "fsdp"), None),
        P(),
        P(),
        P(None, ("ctx", "fsdp")),
        P(),
        P(("ctx", "fsdp"), None),
        P(("ctx", "fsdp"), None),
        P(None, ("ctx", "fsdp")),
    )

    def run(*arguments):
        n, planes = mesh.shape["ctx"], mesh.shape["fsdp"]
        key_heads = arguments[4].shape[1] // arguments[6].shape[0]
        whole_heads = n == 8 and planes == 4 and key_heads == n
        return jax.shard_map(
            plane_device if whole_heads else on_device,
            mesh=mesh, in_specs=in_specs, out_specs=out_specs, check_vma=False,
        )(*arguments)

    return run
```

```python
import functools

import jax
import jax.numpy as jnp
import numpy as np
from jax import lax
from jax.experimental import pallas as pl
from jax.experimental.pallas import tpu as pltpu
from jax.sharding import PartitionSpec as P

epsilon = 1e-06
rope_base = 1000000.0
masked_score = -1e30


def from_behind(block, axis, distance):
    devices = range(lax.axis_size(axis))
    route = [((i - distance) % len(devices), i) for i in devices]
    return lax.ppermute(block, axis, route)


def rotate(value_rows):
    half = value_rows.shape[-1] // 2
    return jnp.concatenate([-value_rows[..., half:], value_rows[..., :half]], -1)


def rotate_back(value_rows):
    half = value_rows.shape[-1] // 2
    return jnp.concatenate([value_rows[..., half:], -value_rows[..., :half]], -1)


def rope_tables(token_offsets, head_size):
    half = head_size // 2
    inverse = rope_base ** (-(jnp.arange(half).astype(jnp.float32) * 2.0) / head_size)
    angles = token_offsets.astype(jnp.float32)[:, None] * inverse[None, :]
    cosine = jnp.cos(angles)
    sine = jnp.sin(angles)
    return (jnp.concatenate([cosine, cosine], -1), jnp.concatenate([sine, sine], -1))


def norm_scale(value_rows):
    return lax.rsqrt(jnp.mean(value_rows * value_rows, -1, keepdims=True) + epsilon)


def norm_back(value_rows, scale, gain, grad):
    weighted = grad * gain
    inner = jnp.mean(weighted * value_rows, -1, keepdims=True)
    result = scale * weighted - value_rows * scale * scale * scale * inner
    gain_part = jnp.sum((grad * value_rows * scale).reshape(-1, gain.shape[0]), 0)
    return (result, gain_part)


def row_products(left, pieces):
    return tuple((jnp.dot(left, piece, preferred_element_type=jnp.float32) for piece in pieces))


def column_products(rights, pieces):
    total = jnp.einsum("tc,rc->tr", rights[0], pieces[0], preferred_element_type=jnp.float32)
    for right, piece in zip(rights[1:], pieces[1:]):
        total = total + jnp.einsum("tc,rc->tr", right, piece, preferred_element_type=jnp.float32)
    return total


def on_device(
    layer_input,
    token_positions,
    attention_gain,
    query_weight,
    key_matrix,
    value_matrix,
    query_gain,
    key_norm_gain,
    output_weight,
    feedforward_gain,
    gate_weight,
    up_weight,
    down_weight,
    out_cotangent,
):
    hidden_in = layer_input[0].astype(jnp.float32)
    count = hidden_in.shape[0]
    head_size = query_gain.shape[0]
    query_width = query_weight.shape[1]
    key_width = key_matrix.shape[1]
    inner_width = gate_weight.shape[1]
    heads = query_width // head_size
    key_heads = key_width // head_size
    group = heads // key_heads
    scale = head_size ** (-0.5)
    cycles = lax.axis_size("ctx")
    own_index = lax.axis_index("ctx")
    sequence_pos = token_positions[0]
    token_offsets = lax.dynamic_slice_in_dim(sequence_pos, own_index * count, count)
    cosine, sine = rope_tables(token_offsets, head_size)
    cosine = cosine[:, None, :]
    sine = sine[:, None, :]
    first_scale = norm_scale(hidden_in)
    first = (hidden_in * first_scale * attention_gain).astype(jnp.bfloat16)
    query_raw, key_unnormed, value_unnormed = row_products(
        first,
        (
            lax.all_gather(query_weight, "fsdp", axis=0, tiled=True),
            lax.all_gather(key_matrix, "fsdp", axis=0, tiled=True),
            lax.all_gather(value_matrix, "fsdp", axis=0, tiled=True),
        ),
    )
    query_heads = query_raw.reshape(count, heads, head_size)
    query_scale = norm_scale(query_heads)
    query_normed = query_heads * query_scale * query_gain
    query_rot = query_normed * cosine + rotate(query_normed) * sine
    query_grouped = (
        query_rot.reshape(count, key_heads, group, head_size)
        .transpose(1, 2, 0, 3)
        .astype(jnp.bfloat16)
    )
    key_heads_raw = key_unnormed.reshape(count, key_heads, head_size)
    key_scale = norm_scale(key_heads_raw)
    key_normed = key_heads_raw * key_scale * key_norm_gain
    key_low = (
        (key_normed * cosine + rotate(key_normed) * sine)
        .reshape(count, key_width)
        .astype(jnp.bfloat16)
    )
    value_low = value_unnormed.astype(jnp.bfloat16)
    rowmax = jnp.full((key_heads, group, count), masked_score, jnp.float32)
    keys_piece = lax.all_gather(key_low, "ctx", axis=0, tiled=True).reshape(
        -1, key_heads, head_size
    )
    values_piece = lax.all_gather(value_low, "ctx", axis=0, tiled=True).reshape(
        -1, key_heads, head_size
    )
    key_pos = sequence_pos
    allowed = token_offsets[:, None] >= key_pos[None, :]
    scores = (
        jnp.einsum("kgtd,skd->kgts", query_grouped, keys_piece, preferred_element_type=jnp.float32)
        * scale
    )
    scores = jnp.where(allowed, scores, masked_score)
    newmax = jnp.maximum(rowmax, jnp.max(scores, -1))
    weights = jnp.where(allowed, jnp.exp(scores - newmax[..., None]), 0.0)
    accum = jnp.einsum(
        "kgts,skd->kgtd",
        weights.astype(jnp.bfloat16),
        values_piece,
        preferred_element_type=jnp.float32,
    )
    rowsum = jnp.sum(weights, -1)
    accum, rowmax, rowsum = (accum, newmax, rowsum)
    normalized = accum / rowsum[..., None]
    logsum = rowmax + jnp.log(rowsum)
    attention_low = (
        normalized.transpose(2, 0, 1, 3).reshape(count, query_width).astype(jnp.bfloat16)
    )
    output_whole = lax.all_gather(output_weight, "fsdp", axis=0, tiled=True)
    branch_out = jnp.dot(attention_low, output_whole, preferred_element_type=jnp.float32)
    middle = hidden_in + branch_out
    second_scale = norm_scale(middle)
    second = (middle * second_scale * feedforward_gain).astype(jnp.bfloat16)
    gate, up = row_products(
        second,
        (
            lax.all_gather(gate_weight, "fsdp", axis=0, tiled=True),
            lax.all_gather(up_weight, "fsdp", axis=0, tiled=True),
        ),
    )
    sigmoid_gate = jax.nn.sigmoid(gate)
    silu_gate = gate * sigmoid_gate
    hidden_low = (silu_gate * up).astype(jnp.bfloat16)
    (down_out,) = row_products(
        hidden_low, (lax.all_gather(down_weight, "fsdp", axis=0, tiled=True),)
    )
    layer_output = (middle + down_out).astype(jnp.bfloat16)[None]
    cotangent = out_cotangent[0]
    hidden_grad = column_products(
        (cotangent,), lax.all_gather((down_weight,), "fsdp", axis=0, tiled=True)
    )
    up_low = (hidden_grad * silu_gate).astype(jnp.bfloat16)
    gate_low = (hidden_grad * up * sigmoid_gate * (1.0 + gate * (1.0 - sigmoid_gate))).astype(
        jnp.bfloat16
    )
    second_grad = column_products(
        (gate_low, up_low), lax.all_gather((gate_weight, up_weight), "fsdp", axis=0, tiled=True)
    )
    middle_part, feedforward_part = norm_back(middle, second_scale, feedforward_gain, second_grad)
    middle_grad = cotangent.astype(jnp.float32) + middle_part
    middle_low = middle_grad.astype(jnp.bfloat16)
    attention_grad = jnp.einsum(
        "tc,rc->tr", middle_low, output_whole, preferred_element_type=jnp.float32
    )
    attention_grad_low = attention_grad.astype(jnp.bfloat16)
    mixed_grad = attention_grad_low.reshape(count, key_heads, group, head_size).transpose(
        1, 2, 0, 3
    )
    delta = jnp.sum(mixed_grad.astype(jnp.float32) * normalized, -1)

    def cycle_step(index, carry):
        keys_held, values_held, key_acc, value_acc, query_acc = carry
        anchor = (own_index - index) % cycles
        key_pos = lax.dynamic_slice_in_dim(sequence_pos, anchor * count, count)
        keys_piece = keys_held.astype(jnp.bfloat16).reshape(count, key_heads, head_size)
        values_piece = values_held.astype(jnp.bfloat16).reshape(count, key_heads, head_size)
        allowed = token_offsets[:, None] >= key_pos[None, :]
        scores = (
            jnp.einsum(
                "kgtd,skd->kgts", query_grouped, keys_piece, preferred_element_type=jnp.float32
            )
            * scale
        )
        probs = jnp.where(allowed, jnp.exp(scores - logsum[..., None]), 0.0)
        value_acc = value_acc + jnp.einsum(
            "kgts,kgtd->skd",
            probs.astype(jnp.bfloat16),
            mixed_grad,
            preferred_element_type=jnp.float32,
        ).reshape(count, key_width)
        prob_grad = jnp.einsum(
            "kgtd,skd->kgts", mixed_grad, values_piece, preferred_element_type=jnp.float32
        )
        score_grad = (probs * (prob_grad - delta[..., None])).astype(jnp.bfloat16)
        query_acc = (
            query_acc
            + jnp.einsum(
                "kgts,skd->kgtd", score_grad, keys_piece, preferred_element_type=jnp.float32
            )
            * scale
        )
        key_acc = (
            key_acc
            + jnp.einsum(
                "kgts,kgtd->skd", score_grad, query_grouped, preferred_element_type=jnp.float32
            ).reshape(count, key_width)
            * scale
        )
        moved = (
            from_behind(keys_held.astype(jnp.bfloat16), "ctx", 1).astype(keys_held.dtype),
            from_behind(values_held.astype(jnp.bfloat16), "ctx", 1).astype(values_held.dtype),
            from_behind(key_acc.astype(jnp.bfloat16), "ctx", 1).astype(key_acc.dtype),
            from_behind(value_acc.astype(jnp.bfloat16), "ctx", 1).astype(value_acc.dtype),
        )
        return (moved[0], moved[1], moved[2], moved[3], query_acc)

    start_cycle = (
        key_low.astype(jnp.float32),
        value_low.astype(jnp.float32),
        jnp.zeros((count, key_width), jnp.float32),
        jnp.zeros((count, key_width), jnp.float32),
        jnp.zeros((key_heads, group, count, head_size), jnp.float32),
    )
    cycle_done = lax.fori_loop(0, cycles, cycle_step, start_cycle)
    key_acc = cycle_done[2]
    value_acc = cycle_done[3]
    query_acc = cycle_done[4]
    query_rot_grad = query_acc.transpose(2, 0, 1, 3).reshape(count, heads, head_size)
    query_normed_grad = query_rot_grad * cosine + rotate_back(query_rot_grad * sine)
    query_heads_grad, query_part = norm_back(
        query_heads, query_scale, query_gain, query_normed_grad
    )
    query_low_grad = query_heads_grad.reshape(count, query_width).astype(jnp.bfloat16)
    key_rot_grad = key_acc.reshape(count, key_heads, head_size)
    key_normed_grad = key_rot_grad * cosine + rotate_back(key_rot_grad * sine)
    key_heads_grad, key_part = norm_back(key_heads_raw, key_scale, key_norm_gain, key_normed_grad)
    key_low_grad = key_heads_grad.reshape(count, key_width).astype(jnp.bfloat16)
    value_low_grad = value_acc.astype(jnp.bfloat16)
    first_grad = column_products(
        (query_low_grad, key_low_grad, value_low_grad),
        lax.all_gather((query_weight, key_matrix, value_matrix), "fsdp", axis=0, tiled=True),
    )
    input_part, attention_part = norm_back(hidden_in, first_scale, attention_gain, first_grad)
    input_gradient = (middle_grad + input_part)[None]
    rights_first = jnp.concatenate([query_low_grad, key_low_grad, value_low_grad], 1)
    rights_second = jnp.concatenate([gate_low, up_low], 1)
    pairs = (
        (first, rights_first),
        (second, rights_second),
        (middle_low, attention_low),
        (cotangent, hidden_low),
    )
    parts = []
    for left, right in pairs:
        parts.append(jnp.einsum("tr,tc->rc", left, right, preferred_element_type=jnp.float32))
    sums = lax.psum_scatter(
        jnp.concatenate(parts, 1), ("ctx", "fsdp"), scatter_dimension=0, tiled=True
    )
    edges = [0, query_width, query_width + key_width, query_width + 2 * key_width]
    edges = edges + [edges[3] + inner_width, edges[3] + 2 * inner_width]
    edges = edges + [edges[5] + query_width, edges[5] + query_width + inner_width]
    query_gradient = sums[:, edges[0] : edges[1]]
    key_gradient = sums[:, edges[1] : edges[2]]
    value_gradient = sums[:, edges[2] : edges[3]]
    gate_gradient = sums[:, edges[3] : edges[4]]
    up_gradient = sums[:, edges[4] : edges[5]]
    output_gradient = sums[:, edges[5] : edges[6]].T
    down_gradient = sums[:, edges[6] : edges[7]].T
    attention_total, query_total, key_total, feedforward_total = lax.psum(
        (attention_part, query_part, key_part, feedforward_part), ("ctx", "fsdp")
    )
    return (
        layer_output,
        input_gradient,
        attention_total,
        query_gradient,
        key_gradient,
        value_gradient,
        query_total,
        key_total,
        output_gradient,
        feedforward_total,
        gate_gradient,
        up_gradient,
        down_gradient,
    )


MESH = pl.DeviceIdType.MESH
f32 = jnp.float32
bf16 = jnp.bfloat16


def dot(left, right):
    return jnp.dot(left, right, preferred_element_type=f32)


def dot_nt(left, right):
    return lax.dot_general(left, right, (((1,), (1,)), ((), ())), preferred_element_type=f32)


def dot_tn(left, right):
    return lax.dot_general(left, right, (((0,), (0,)), ((), ())), preferred_element_type=f32)


def layer_kernel(
    n, planes, block, head, group, fw,
    x_ref, dy_ref, pos_row, inverse_ref, step_cos, step_sin, ag_ref, fg_ref, qg_ref, kg_ref,
    wq, wk, wv, wo, wg, wu, wd,
    out_ref, dx_ref, gains_ref, got_a, got_b, got_c, got_out, got_qkv,
    w_qkv, w_gu, w_out, w_down, t_out, t_down,
    first, dy_all, second, first_t, dy_t, second_t,
    positions, cosine, sine,
    raw, queries, keys, values, keys_t, values_t, probs, sums, mixed_t, mixed_low,
    hidden, d_gu, d_qkv, dk_acc, dv_acc,
    stage_a, stage_b, stage_c, stage_out, stage_qkv,
    land_a, land_b, land_c, land_out, land_qkv,
    rs_sa, rs_ra, rs_sb, rs_rb, rs_kept, rs_acc,
    middle, d_middle, gain_own, gain_plane, gain_all,
    local_sem, wz_send, wz_recv, hand_send, hand_recv,
    ag_send, ag_recv, ra_send, ra_recv, rb_send, rb_recv,
    zr_send, zr_recv, aa_send, aa_recv, gp_send, gp_recv, gz_send, gz_recv,
):
    c = lax.axis_index("ctx")
    z = lax.axis_index("fsdp")
    dmid = first
    dmid_t = second
    cy, cx, ck = lax.div(c, 4), lax.rem(lax.div(c, 2), 2), lax.rem(c, 2)
    ci = lax.rem(c, 4)
    sign = 1 - 2 * ck
    qw, kw = group * head, head
    pw = 128
    thirds = fw // pw
    piece = pw // 4
    width = x_ref.shape[1]
    scale = head ** (-0.5)
    log2e = 1.4426950408889634
    gots = (got_a, got_b, got_c, got_out, got_qkv)
    stages = (stage_a, stage_b, stage_c, stage_out, stage_qkv)
    lands = (land_a, land_b, land_c, land_out, land_qkv)

    def partner(j):
        y = lax.rem(cy + lax.div(j, 4), 2)
        x = lax.rem(cx + lax.rem(lax.div(j, 2), 2), 2)
        k = lax.rem(ck + lax.rem(j, 2), 2)
        return y * 4 + x * 2 + k

    def chip(slot):
        return lax.rem(cy + lax.div(slot, 2), 2) * 2 + lax.rem(cx + lax.rem(slot, 2), 2)

    def rows(start, size):
        return pl.ds(pl.multiple_of(start * size, size), size)

    def remote(src, dst, send, recv, ctx, plane):
        return pltpu.make_async_remote_copy(
            src_ref=src, dst_ref=dst, send_sem=send, recv_sem=recv,
            device_id={"ctx": ctx, "fsdp": plane}, device_id_type=MESH,
        )

    in_plane, along = [], []

    def launch(started, copy, when=None):
        if when is None:
            copy().start()
        else:
            pl.when(when)(lambda: copy().start())
        started.append((copy, when))

    def drain(started):
        for copy, when in started:
            if when is None:
                copy().wait_send()
            else:
                pl.when(when)(lambda copy=copy: copy().wait_send())
        started.clear()

    own_rows = wq.shape[0]
    out_rows = wo.shape[0] // n

    def own_slices():
        mine = rows(z, own_rows)
        pairs = [
            (wq.at[:, rows(c, qw)], w_qkv.at[mine, 0:qw]),
            (wk.at[:, rows(c, kw)], w_qkv.at[mine, qw:qw + kw]),
            (wv.at[:, rows(c, kw)], w_qkv.at[mine, qw + kw:qw + 2 * kw]),
            (wo.at[rows(c, out_rows)], t_out.at[rows(z, out_rows)]),
        ]
        for t in range(thirds):
            at = 2 * pw * t
            pairs.append((wg.at[:, rows(c * thirds + t, pw)], w_gu.at[mine, at:at + pw]))
            pairs.append((wu.at[:, rows(c * thirds + t, pw)], w_gu.at[mine, at + pw:at + 2 * pw]))
            pairs.append((wd.at[rows((cy * thirds + t) * 4 + ci, piece)], t_down.at[t, rows(z, piece)]))
        return pairs

    local = [pltpu.make_async_copy(src, dst, local_sem.at[i]) for i, (src, dst) in enumerate(own_slices())]
    for copy in local:
        copy.start()

    for land in lands:
        @pl.when(z == 0)
        def _(land=land):
            land[0] = jnp.zeros(land.shape[1:], bf16)

        @pl.when(z == planes - 1)
        def _(land=land):
            land[planes] = jnp.zeros(land.shape[1:], bf16)

    barrier = pltpu.get_barrier_semaphore()
    for j in range(1, n):
        pl.semaphore_signal(barrier, inc=1, device_id={"ctx": partner(j), "fsdp": z}, device_id_type=MESH)
    for d in range(1, planes):
        pl.semaphore_signal(
            barrier, inc=1, device_id={"ctx": c, "fsdp": lax.rem(z + d, planes)}, device_id_type=MESH)
    x = x_ref[...].astype(f32)
    x_scale = lax.rsqrt(jnp.mean(x * x, -1, keepdims=True) + epsilon)
    first[rows(c, block)] = (x * x_scale * ag_ref[...]).astype(bf16)
    dy_all[rows(c, block)] = dy_ref[...]
    for copy in local[:3]:
        copy.wait()
    pl.semaphore_wait(barrier, n + planes - 2)

    def inside(t):
        return jnp.logical_and(t >= 0, t < planes)

    weights = [
        (lambda o: w_qkv.at[rows(o, own_rows)], None),
        (lambda o: t_out.at[rows(o, out_rows)], 0),
    ]
    for t in range(thirds):
        weights.append((lambda o, t=t: w_gu.at[rows(o, own_rows), 2 * pw * t:2 * pw * (t + 1)], None))
        weights.append((lambda o, t=t: t_down.at[t, rows(o, piece)], 1 + t))

    def weight_copy(w, slot, origin, target):
        part = weights[w][0](origin)
        return remote(part, part, wz_send.at[w, slot], wz_recv.at[w, origin], c, target)

    def hand_split(origin, valid):
        mine = 2 * origin + cy == c
        return jnp.logical_and(valid, jnp.logical_not(mine)), jnp.logical_and(valid, mine)

    def weight_start(w):
        for side in range(2):
            d = sign * (1 - 2 * side)
            launch(along, lambda side=side, d=d: weight_copy(w, side, z, z + d), inside(z + d))
        if weights[w][1] is not None:
            hand_over(w, z, 0, *hand_split(z, True))

    def hand_target(h):
        if h == 0:
            return lambda i: w_out.at[rows(i, out_rows)]
        return lambda i: w_down.at[rows((h - 1) * 4 + i, piece)]

    def hand_copy(w, origin, slot):
        h = weights[w][1]
        return remote(
            weights[w][0](origin), hand_target(h)(ci), hand_send.at[h, slot], hand_recv.at[h, ci], 2 * origin + cy, z)

    def hand_over(w, origin, slot, away, here):
        launch(in_plane, lambda: hand_copy(w, origin, slot), away)

        @pl.when(here)
        def _():
            hand_target(weights[w][1])(ci)[...] = weights[w][0](origin)[...]

    def hand_arrive(w):
        h = weights[w][1]
        for i in range(4):
            @pl.when(4 * ck + i != c)
            def _(i=i):
                part = hand_target(h)(i)
                remote(part, part, hand_send.at[h, 0], hand_recv.at[h, i], c, z).wait_recv()

    hops = {}
    for d in range(1, planes):
        for side, way in enumerate((1, -1)):
            origin = z - way * d
            valid = inside(origin)
            passed = jnp.logical_and(valid, inside(z + way))
            hops[d, side] = origin, z + way, valid, passed, hand_split(origin, valid)

    def weight_hop(w, d):
        for side in range(2):
            origin, following, valid, passed, split = hops[d, side]
            pl.when(valid)(lambda: weight_copy(w, 0, origin, z).wait_recv())
            if d < planes - 1:
                launch(
                    along,
                    lambda side=side, origin=origin, following=following: weight_copy(
                        w, 2 * d + side, origin, following),
                    passed)
            if weights[w][1] is not None:
                hand_over(w, origin, 2 * d - 1 + side, *split)

    def gather_copy(buf, g, j, send, origin, target):
        part = buf.at[rows(origin, block)]
        return remote(part, part, ag_send.at[g, send], ag_recv.at[g, j], target, z)

    def gather_start(buf, g):
        for j in (1, 2 + 2 * ck, 4 - 2 * ck, 6):
            launch(in_plane, lambda j=j: gather_copy(buf, g, j, j, c, partner(j)))

    def gather_forward(buf, g, j):
        return gather_copy(buf, g, j + 1, j + 1, partner(j), partner(1))

    def gather_finish(buf, g):
        for j in (2, 4, 6):
            gather_copy(buf, g, j, j, partner(j), c).wait_recv()
            launch(in_plane, lambda j=j: gather_forward(buf, g, j))
        for j in (1, 3, 5, 7):
            gather_copy(buf, g, j, j, partner(j), c).wait_recv()

    def gather_step(buf, g, slot):
        def arrive(j):
            gather_copy(buf, g, j, j, partner(j), c).wait_recv()
            gather_forward(buf, g, j).start()

        @pl.when(slot == 1)
        def _():
            arrive(2)
            arrive(4)

        @pl.when(slot == 3)
        def _():
            arrive(6)

        gather_copy(buf, g, 2 * slot + 1, 0, partner(2 * slot + 1), c).wait_recv()

    def gather_stepped(buf, g):
        for j in (2, 4, 6):
            in_plane.append((lambda j=j: gather_forward(buf, g, j), None))

    def sum_pair_copy(s, slot):
        return remote(rs_sa.at[s % 2, slot], rs_ra.at[s % 2, slot], ra_send.at[s, slot], ra_recv.at[s, slot], partner(1), z)

    def sum_chip_copy(s, slot):
        return remote(
            rs_sb.at[s % 2, slot], rs_rb.at[s % 2, slot], rb_send.at[s, slot], rb_recv.at[s, slot], partner(2 * slot), z)

    def sum_slot(p):
        return jnp.where(p == 0, 3, jnp.where(p == 1, 2 - ck, jnp.where(p == 2, 1 + ck, 0)))

    def sum_start(s, left, partial, prepare=None, ready=None, during=()):
        if prepare is not None:
            prepare(chip(sum_slot(0)))
        if ready is not None:
            ready()

        def body(p, carry):
            slot = sum_slot(p)
            at = [rows(partner(2 * slot + 1), block), rows(partner(2 * slot), block)]
            both = partial(jnp.concatenate([left[i] for i in at], 0))
            rs_sa[s % 2, slot] = both[:block].astype(bf16)
            sum_pair_copy(s, slot).start()
            rs_kept[lax.rem(p, 2)] = both[block:]
            if prepare is not None:
                @pl.when(p < 3)
                def _():
                    prepare(chip(sum_slot(p + 1)))

            @pl.when(p > 0)
            def _():
                before = sum_slot(p - 1)
                sum_pair_copy(s, before).wait_recv()
                rs_sb[s % 2, before] = (
                    rs_kept[lax.rem(p + 1, 2)] + rs_ra[s % 2, before].astype(f32)).astype(bf16)
                sum_chip_copy(s, before).start()

            for k, poll in enumerate(during):
                pl.when(p == k)(poll)
            return carry

        lax.fori_loop(0, 4, body, 0)
        for slot in range(4):
            in_plane.append((lambda slot=slot: sum_pair_copy(s, slot), None))
            if slot > 0:
                in_plane.append((lambda slot=slot: sum_chip_copy(s, slot), None))
        sum_pair_copy(s, 0).wait_recv()
        rs_acc[s % 2] = rs_kept[1] + rs_ra[s % 2, 0].astype(f32)

    def sum_finish(s):
        total = rs_acc[s % 2]
        for slot in (1, 2, 3):
            sum_chip_copy(s, slot).wait_recv()
            total = total + rs_rb[s % 2, slot].astype(f32)
        return total

    per = block // planes

    def weight_grad(m, parts):
        def body(i, carry):
            at = 0
            for left, right in parts:
                value = right()
                grad = dot(left[rows(i, 4 * block)], value)
                for k in range(4):
                    for t in range(planes):
                        start = k * block + t * per
                        stages[m][t, 4 * i + k, :, at:at + value.shape[1]] = grad[start:start + per].astype(bf16)
                at += value.shape[1]
            return carry

        lax.fori_loop(0, n // 4, body, 0)
        at_edge = jnp.logical_or(z == 0, z == planes - 1)
        for k in range(planes - 1):
            t = jnp.where(z == 0, planes - 1 - k, k)
            launch(along, lambda t=t: grad_copy(m, t), at_edge)

    def grad_copy(m, t):
        way = jnp.where(z < t, 1, -1)
        last = z + way == t
        slot = jnp.where(jnp.logical_and(last, way < 0), planes, t)
        return remote(
            stages[m].at[t], lands[m].at[slot], zr_send.at[m, t], zr_recv.at[m, slot], c, z + way)

    def grad_arrive(m, slot):
        part = lands[m].at[slot]
        remote(part, part, zr_send.at[m, 0], zr_recv.at[m, slot], c, z).wait_recv()

    def grad_pass(m, t, valid):
        @pl.when(valid)
        def _():
            grad_arrive(m, t)

            def body(i, carry):
                stages[m][t, i] = (stages[m][t, i].astype(f32) + lands[m][t, i].astype(f32)).astype(bf16)
                return carry

            lax.fori_loop(0, n, body, 0)

        launch(along, lambda: grad_copy(m, t), valid)

    def grad_near(m):
        for t in (3, 2):
            grad_pass(m, t, z == 1)
        for t in (0, 1):
            grad_pass(m, t, z == 2)

    def grad_far(m):
        grad_pass(m, 3, z == 2)
        grad_pass(m, 0, z == 1)

    def owner_copy(m, j):
        return remote(lands[m].at[z, partner(j)], gots[m].at[c], aa_send.at[m, j], aa_recv.at[m, j], partner(j), z)

    def hand_out(m):
        pl.when(z > 0)(lambda: grad_arrive(m, z))
        pl.when(z < planes - 1)(lambda: grad_arrive(m, planes))

        def body(i, carry):
            total = stages[m][z, i].astype(f32) + lands[m][z, i].astype(f32) + lands[m][planes, i].astype(f32)
            lands[m][z, i] = total.astype(bf16)
            return carry

        lax.fori_loop(0, n, body, 0)
        for j in (2 + 2 * ck, 3 + 2 * ck, 4 - 2 * ck, 5 - 2 * ck, 6, 7, 1):
            launch(in_plane, lambda j=j: owner_copy(m, j))
        gots[m][c] = lands[m][z, c]

    def hand_receive(m):
        for j in range(1, n):
            owner_copy(m, j).wait_recv()

    weight_start(0)
    gather_start(first, 0)
    for copy in local[3:]:
        copy.wait()

    spread = jnp.broadcast_to(pos_row[...].astype(f32), (head, pos_row.shape[1]))
    positions[...] = spread.T
    side = jnp.where(lax.broadcasted_iota(jnp.int32, (1, head), 1) < head // 2, -1.0, 1.0)

    def table(i, carry):
        run = step_cos.shape[0]
        at = rows(i, run)
        start = positions[pl.ds(pl.multiple_of(i * run, run), 1)] * inverse_ref[...]
        start_cos, start_sin = jnp.cos(start), jnp.sin(start)
        cosine[at] = start_cos * step_cos[...] - start_sin * step_sin[...]
        sine[at] = (start_sin * step_cos[...] + start_cos * step_sin[...]) * side
        return carry

    def turn_over(src, dst):
        def body(i, carry):
            at = rows(i, block)
            dst[:, at] = src[at].T
            return carry

        lax.fori_loop(0, n, body, 0)

    lax.fori_loop(0, 2 * n, table, 0)
    weight_hop(0, 1)
    gather_finish(first, 0)
    weight_hop(0, 2)
    weight_start(1)
    gather_start(dy_all, 1)
    turn_over(first, first_t)
    weight_hop(0, 3)
    weight_start(2)
    weight_start(3)

    def turn(value, at):
        return value * cosine[at] + pltpu.roll(value, head // 2, 1) * sine[at]

    def turn_back(grad, at):
        return grad * cosine[at] - pltpu.roll(grad, head // 2, 1) * sine[at]

    def project(i, carry):
        at = rows(i, 2 * block)
        result = dot(first[at], w_qkv[...])
        raw[at] = result[:, :qw + kw]
        low_values = result[:, qw + kw:].astype(bf16)
        values[at] = low_values
        values_t[:, at] = low_values.T
        for h in range(group + 1):
            part = result[:, h * head:(h + 1) * head]
            inv = lax.rsqrt(jnp.mean(part * part, -1, keepdims=True) + epsilon)
            gain = qg_ref[...] if h < group else kg_ref[...]
            turned = turn(part * inv * gain, at)
            if h < group:
                queries[at, h * head:(h + 1) * head] = (turned * (scale * log2e)).astype(bf16)
            else:
                low_keys = turned.astype(bf16)
                keys[at] = low_keys
                keys_t[:, at] = low_keys.T
        return carry

    lax.fori_loop(0, n // 4, project, 0)
    weight_hop(1, 1)
    lax.fori_loop(n // 4, n // 2, project, 0)
    weight_hop(1, 2)
    gather_finish(dy_all, 1)

    def stack(ref, at):
        return jnp.concatenate([ref[at, h * head:(h + 1) * head] for h in range(group)], 0)

    def attend(place):
        at = rows(place, 2 * block)
        scores = dot_nt(keys[...], stack(queries, at))
        allowed = positions[...] <= pos_row[:, rows(2 * place, block)].astype(f32)
        later = positions[...] <= pos_row[:, rows(2 * place + 1, block)].astype(f32)
        weight = jnp.concatenate(
            [jnp.exp2(jnp.where(later if k % 2 else allowed, scores[:, k * block:(k + 1) * block], masked_score))
             for k in range(2 * group)], 1)
        inv = 1.0 / jnp.sum(weight, 0, keepdims=True)
        low_weight = weight.astype(bf16)
        probs[place] = low_weight
        sums[place] = inv
        result = dot(values_t[...], low_weight) * inv
        mixed_t[place] = result
        for h in range(group):
            mixed_low[at, h * head:(h + 1) * head] = result[:, 2 * h * block:2 * (h + 1) * block].T.astype(bf16)

    def output_ready():
        weight_hop(1, 3)
        weight_start(4)
        weight_start(5)
        hand_arrive(1)
        drain(in_plane)

    def hop_third(t, d):
        weight_hop(2 + 2 * t, d)
        weight_hop(3 + 2 * t, d)

    sum_start(
        0, mixed_low, lambda left: dot(left, w_out[...]), attend, output_ready,
        (lambda: hop_third(0, 1), lambda: hop_third(0, 2)))
    weight_start(6)
    weight_start(7)
    turn_over(dy_all, dy_t)
    hop_third(0, 3)
    mid = x_ref[...].astype(f32) + sum_finish(0)
    middle[...] = mid
    mid_scale = lax.rsqrt(jnp.mean(mid * mid, -1, keepdims=True) + epsilon)
    second[rows(c, block)] = (mid * mid_scale * fg_ref[...]).astype(bf16)
    gather_start(second, 2)
    hop_third(1, 1)
    hand_arrive(3)

    def feed(t, at):
        units, pair = slice(t * pw, (t + 1) * pw), 2 * pw * t
        both = dot(second[at], w_gu[:, pair:pair + 2 * pw])
        back = dot_nt(dy_all[at], w_down[units])
        gate, up = both[:, :pw], both[:, pw:]
        sig = 1.0 / (1.0 + jnp.exp(-gate))
        silu = gate * sig
        hidden[at, units] = (silu * up).astype(bf16)
        d_gu[at, pair:pair + pw] = (back * up * sig * (1.0 + gate * (1.0 - sig))).astype(bf16)
        d_gu[at, pair + pw:pair + 2 * pw] = (back * silu).astype(bf16)

    def feed_arriving(slot, carry):
        gather_step(second, 2, slot)
        at = rows(chip(slot), 2 * block)
        feed(0, at)
        second_t[:, at] = second[at].T
        pl.when(slot == 2)(lambda: hop_third(1, 2))
        return carry

    def third_grad(t):
        weight_grad(t, [
            (second_t, lambda: d_gu[:, 2 * pw * t:2 * pw * (t + 1)]),
            (dy_t, lambda: hidden[:, t * pw:(t + 1) * pw]),
        ])

    def feed_third(t):
        def body(i, carry):
            feed(t, rows(i, 2 * block))
            return carry

        lax.fori_loop(0, n // 2, body, 0)

    lax.fori_loop(0, n // 2, feed_arriving, 0)
    gather_stepped(second, 2)
    hop_third(2, 1)
    third_grad(0)
    hop_third(1, 3)
    hand_arrive(5)
    feed_third(1)
    hop_third(2, 2)
    hop_third(2, 3)
    hand_arrive(7)
    sum_start(
        1, d_gu, lambda left: dot_nt(left, w_gu[...]),
        lambda place: feed(thirds - 1, rows(place, 2 * block)))
    third_grad(1)
    third_grad(2)
    d_second = sum_finish(1)

    def norm_back(value, gain, grad):
        inv = lax.rsqrt(jnp.mean(value * value, -1, keepdims=True) + epsilon)
        weighted = grad * gain
        inner = jnp.mean(weighted * value, -1, keepdims=True)
        result = inv * weighted - value * (inv * inv * inv * inner)
        return result, jnp.sum(grad * value * inv, 0, keepdims=True)

    gain_own[...] = jnp.zeros_like(gain_own)
    part, gain_own[1:2, :] = norm_back(middle[...], fg_ref[...], d_second)
    d_mid = dy_ref[...].astype(f32) + part
    d_middle[...] = d_mid
    drain(in_plane)
    dmid[rows(c, block)] = d_mid.astype(bf16)
    gather_start(dmid, 3)
    grad_near(0)

    dk_acc[...] = jnp.zeros_like(dk_acc)
    dv_acc[...] = jnp.zeros_like(dv_acc)

    def attend_back(slot, q_sum):
        gather_step(dmid, 3, slot)
        place = chip(slot)
        at = rows(place, 2 * block)
        d_mix = dot_nt(w_out[...], dmid[at])
        dmid_t[:, at] = dmid[at].T
        d_mix_t = jnp.concatenate([d_mix[h * head:(h + 1) * head] for h in range(group)], 1)
        d_mix_t = (d_mix_t.astype(bf16).astype(f32) * sums[place]).astype(bf16)
        delta = jnp.sum(d_mix_t.astype(f32) * mixed_t[place], 0, keepdims=True)
        weight = probs[place]
        d_prob = dot(values[...], d_mix_t)
        d_score = (weight.astype(f32) * (d_prob - delta)).astype(bf16)
        d_query = dot(keys_t[...], d_score) * scale
        for h in range(group):
            grad = turn_back(d_query[:, 2 * h * block:2 * (h + 1) * block].T, at)
            part, gain_part = norm_back(raw[at, h * head:(h + 1) * head], qg_ref[...], grad)
            d_qkv[at, h * head:(h + 1) * head] = part.astype(bf16)
            q_sum = q_sum + gain_part
        dv_acc[...] += dot(weight, d_mix_t.T)
        dk_acc[...] += dot(d_score, stack(queries, at))
        return q_sum

    zero = jnp.zeros((1, head), f32)
    gain_own[2:3, 0:head] = lax.fori_loop(0, n // 2, attend_back, zero)
    gather_stepped(dmid, 3)
    weight_grad(3, [(dmid_t, lambda: mixed_low[...])])
    grad_far(0)
    grad_near(1)
    drain(in_plane)
    sum_start(2, hidden, lambda left: dot(left, w_down[...]))

    def project_back(i, k_sum):
        at = rows(i, 2 * block)
        grad = turn_back(dk_acc[at] * (1.0 / log2e), at)
        part, gain_part = norm_back(raw[at, qw:qw + kw], kg_ref[...], grad)
        d_qkv[at, qw:qw + kw] = part.astype(bf16)
        d_qkv[at, qw + kw:] = dv_acc[at].astype(bf16)
        return k_sum + gain_part

    gain_own[3:4, 0:head] = lax.fori_loop(0, n // 2, project_back, zero)

    weight_grad(4, [(first_t, lambda: d_qkv[...])])
    sum_start(3, d_qkv, lambda left: dot_nt(left, w_qkv[...]))
    grad_far(1)
    grad_near(2)
    out_ref[...] = (middle[...] + sum_finish(2)).astype(bf16)
    hand_out(0)
    grad_far(2)
    grad_near(3)
    hand_out(1)
    x_part, gain_own[0:1, :] = norm_back(x_ref[...].astype(f32), ag_ref[...], sum_finish(3))
    dx_ref[...] = d_middle[...] + x_part

    def gain_plane_copy(j):
        return remote(gain_own, gain_plane.at[c], gp_send.at[j], gp_recv.at[j], partner(j), z)

    def gain_copy(d):
        return remote(gain_all.at[z], gain_all.at[z], gz_send.at[d], gz_recv.at[d], c, lax.rem(z + d, planes))

    for j in range(1, n):
        launch(in_plane, lambda j=j: gain_plane_copy(j))
    gain_plane[c] = gain_own[...]
    grad_far(3)
    hand_out(2)
    for j in range(1, n):
        gain_plane_copy(j).wait_recv()
    total = gain_plane[0]
    for i in range(1, n):
        total = total + gain_plane[i]
    gain_all[z] = total
    for d in range(1, planes):
        launch(along, lambda d=d: gain_copy(d))
    grad_near(4)
    hand_out(3)
    grad_far(4)
    for d in range(1, planes):
        origin = gain_all.at[lax.rem(z + planes - d, planes)]
        remote(origin, origin, gz_send.at[d], gz_recv.at[d], c, z).wait_recv()
    total = gain_all[0]
    for i in range(1, planes):
        total = total + gain_all[i]
    gains_ref[...] = total

    hand_out(4)
    for m in range(5):
        hand_receive(m)
    drain(in_plane)
    drain(along)


def finish_kernel(
    n, head, out_in, dx_in, gains_in, got_a, got_b, got_c, got_out, got_qkv,
    out_ref, dx_ref, ag_ref, q_ref, k_ref, v_ref, qg_ref, kg_ref, o_ref, fg_ref, g_ref, u_ref, d_ref,
):
    out_ref[...] = out_in[...]
    dx_ref[...] = dx_in[...]
    ag_ref[...] = gains_in[0:1, :]
    fg_ref[...] = gains_in[1:2, :]
    qg_ref[...] = gains_in[2:3, 0:head]
    kg_ref[...] = gains_in[3:4, 0:head]
    qw, kw = q_ref.shape[1] // n, k_ref.shape[1] // n
    pw = got_a.shape[2] // 3
    thirds = (got_a, got_b, got_c)
    for i in range(n):
        q_ref[:, i * qw:(i + 1) * qw] = got_qkv[i, :, 0:qw].astype(f32)
        k_ref[:, i * kw:(i + 1) * kw] = got_qkv[i, :, qw:qw + kw].astype(f32)
        v_ref[:, i * kw:(i + 1) * kw] = got_qkv[i, :, qw + kw:].astype(f32)
        o_ref[:, i * qw:(i + 1) * qw] = got_out[i].astype(f32)
        for t, got in enumerate(thirds):
            at = (i * len(thirds) + t) * pw
            g_ref[:, at:at + pw] = got[i, :, 0:pw].astype(f32)
            u_ref[:, at:at + pw] = got[i, :, pw:2 * pw].astype(f32)
            d_ref[:, at:at + pw] = got[i, :, 2 * pw:].astype(f32)


def plane_device(
    layer_input,
    token_positions,
    attention_gain,
    query_weight,
    key_matrix,
    value_matrix,
    query_gain,
    key_norm_gain,
    output_weight,
    feedforward_gain,
    gate_weight,
    up_weight,
    down_weight,
    out_cotangent,
):
    n = lax.axis_size("ctx")
    planes = lax.axis_size("fsdp")
    block, width = layer_input.shape[1:]
    length = token_positions.shape[1]
    head = query_gain.shape[0]
    qw = query_weight.shape[1] // n
    kw = key_matrix.shape[1] // n
    fw = gate_weight.shape[1] // n
    group = qw // head
    per = block // planes
    half = head // 2
    inverse = np.power(rope_base, -np.arange(half) * 2.0 / head).astype(np.float32)
    inverse = np.concatenate([inverse, inverse])[None]
    steps = np.arange(block // 2)[:, None] * inverse.astype(np.float64)
    step_cos, step_sin = (jnp.asarray(f(steps).astype(np.float32)) for f in (np.cos, np.sin))
    inverse = jnp.asarray(inverse)
    vmem = pl.BlockSpec(memory_space=pltpu.VMEM)
    hbm = pl.BlockSpec(memory_space=pl.ANY)
    dma = pltpu.SemaphoreType.DMA
    sizes = (fw, fw, fw, qw, qw + 2 * kw)
    low = lambda *shape: pltpu.VMEM(shape, bf16)
    wide = lambda *shape: pltpu.VMEM(shape, f32)
    scratch = [
        low(width, qw + 2 * kw), low(width, 2 * fw), low(qw, width), low(fw, width),
        low(planes * (output_weight.shape[0] // n), width), low(3, planes * 32, width),
        low(length, width), low(length, width), low(length, width),
        low(width, length), low(width, length), low(width, length),
        wide(length, head), wide(length, head), wide(length, head),
        wide(length, qw + kw), low(length, qw), low(length, kw), low(length, kw),
        low(kw, length), low(kw, length), low(n // 2, length, 2 * group * block), wide(n // 2, 1, 2 * group * block),
        wide(n // 2, head, 2 * group * block), low(length, qw),
        low(length, fw), low(length, 2 * fw), low(length, qw + 2 * kw),
        wide(length, kw), wide(length, kw),
    ]
    scratch += [low(planes, n, per, size) for size in sizes]
    scratch += [low(planes + 1, n, per, size) for size in sizes]
    scratch += [low(2, 4, block, width) for _ in range(4)] + [wide(2, block, width), wide(2, block, width)]
    scratch += [
        wide(block, width), wide(block, width), wide(8, width), wide(n, 8, width), wide(planes, 8, width),
        dma((13,)), dma((8, 6)), dma((8, planes)), dma((4, 7)), dma((4, 4)),
        dma((4, n)), dma((4, n)), dma((4, 4)), dma((4, 4)), dma((4, 4)), dma((4, 4)),
        dma((5, planes)), dma((5, planes + 1)), dma((5, n)), dma((5, n)), dma((n,)), dma((n,)),
        dma((planes,)), dma((planes,)),
    ]
    shapes = [
        jax.ShapeDtypeStruct((block, width), bf16),
        jax.ShapeDtypeStruct((block, width), f32),
        jax.ShapeDtypeStruct((8, width), f32),
    ] + [jax.ShapeDtypeStruct((n, per, size), bf16) for size in sizes]
    results = pl.pallas_call(
        functools.partial(layer_kernel, n, planes, block, head, group, fw),
        out_shape=shapes,
        in_specs=[vmem] * 10 + [hbm] * 7,
        out_specs=[vmem] * len(shapes),
        scratch_shapes=scratch,
        compiler_params=pltpu.CompilerParams(
            collective_id=0, has_side_effects=True, vmem_limit_bytes=60 * 1024 * 1024),
    )(
        layer_input[0], out_cotangent[0], token_positions, inverse, step_cos, step_sin,
        attention_gain[None], feedforward_gain[None], query_gain[None], key_norm_gain[None],
        query_weight, key_matrix, value_matrix, output_weight, gate_weight, up_weight, down_weight,
    )
    plain = lambda rows, columns, kind=f32: jax.ShapeDtypeStruct((rows, columns), kind)
    finals = [
        plain(block, width, bf16), plain(block, width), plain(1, width),
        plain(per, n * qw), plain(per, n * kw), plain(per, n * kw), plain(1, head), plain(1, head),
        plain(per, n * qw), plain(1, width), plain(per, n * fw), plain(per, n * fw), plain(per, n * fw),
    ]
    done = pl.pallas_call(
        functools.partial(finish_kernel, n, head),
        out_shape=finals,
        in_specs=[vmem] * len(shapes),
        out_specs=[vmem] * len(finals),
    )(*results)
    out, dx, ag, q, k, v, qg, kg, o, fg, g, u, d = done
    return out[None], dx[None], ag[0], q, k, v, qg[0], kg[0], o.T, fg[0], g, u, d.T


def solution(mesh):
    in_specs = (
        P("fsdp", "ctx", None),
        P("fsdp", None),
        P(),
        P("fsdp", None),
        P("fsdp", None),
        P("fsdp", None),
        P(),
        P(),
        P("fsdp", None),
        P(),
        P("fsdp", None),
        P("fsdp", None),
        P("fsdp", None),
        P("fsdp", "ctx", None),
    )
    out_specs = (
        P("fsdp", "ctx", None),
        P("fsdp", "ctx", None),
        P(),
        P(("ctx", "fsdp"), None),
        P(("ctx", "fsdp"), None),
        P(("ctx", "fsdp"), None),
        P(),
        P(),
        P(None, ("ctx", "fsdp")),
        P(),
        P(("ctx", "fsdp"), None),
        P(("ctx", "fsdp"), None),
        P(None, ("ctx", "fsdp")),
    )

    def run(*arguments):
        n, planes = mesh.shape["ctx"], mesh.shape["fsdp"]
        key_heads = arguments[4].shape[1] // arguments[6].shape[0]
        whole_heads = n == 8 and planes == 4 and key_heads == n
        return jax.shard_map(
            plane_device if whole_heads else on_device,
            mesh=mesh, in_specs=in_specs, out_specs=out_specs, check_vma=False,
        )(*arguments)

    return run
```

```python
import functools

import jax
import jax.numpy as jnp
import numpy as np
from jax import lax
from jax.experimental import pallas as pl
from jax.experimental.pallas import tpu as pltpu
from jax.sharding import PartitionSpec as P

epsilon = 1e-06
rope_base = 1000000.0
masked_score = -1e30


def from_behind(block, axis, distance):
    devices = range(lax.axis_size(axis))
    route = [((i - distance) % len(devices), i) for i in devices]
    return lax.ppermute(block, axis, route)


def rotate(value_rows):
    half = value_rows.shape[-1] // 2
    return jnp.concatenate([-value_rows[..., half:], value_rows[..., :half]], -1)


def rotate_back(value_rows):
    half = value_rows.shape[-1] // 2
    return jnp.concatenate([value_rows[..., half:], -value_rows[..., :half]], -1)


def rope_tables(token_offsets, head_size):
    half = head_size // 2
    inverse = rope_base ** (-(jnp.arange(half).astype(jnp.float32) * 2.0) / head_size)
    angles = token_offsets.astype(jnp.float32)[:, None] * inverse[None, :]
    cosine = jnp.cos(angles)
    sine = jnp.sin(angles)
    return (jnp.concatenate([cosine, cosine], -1), jnp.concatenate([sine, sine], -1))


def norm_scale(value_rows):
    return lax.rsqrt(jnp.mean(value_rows * value_rows, -1, keepdims=True) + epsilon)


def norm_back(value_rows, scale, gain, grad):
    weighted = grad * gain
    inner = jnp.mean(weighted * value_rows, -1, keepdims=True)
    result = scale * weighted - value_rows * scale * scale * scale * inner
    gain_part = jnp.sum((grad * value_rows * scale).reshape(-1, gain.shape[0]), 0)
    return (result, gain_part)


def row_products(left, pieces):
    return tuple((jnp.dot(left, piece, preferred_element_type=jnp.float32) for piece in pieces))


def column_products(rights, pieces):
    total = jnp.einsum("tc,rc->tr", rights[0], pieces[0], preferred_element_type=jnp.float32)
    for right, piece in zip(rights[1:], pieces[1:]):
        total = total + jnp.einsum("tc,rc->tr", right, piece, preferred_element_type=jnp.float32)
    return total


def on_device(
    layer_input,
    token_positions,
    attention_gain,
    query_weight,
    key_matrix,
    value_matrix,
    query_gain,
    key_norm_gain,
    output_weight,
    feedforward_gain,
    gate_weight,
    up_weight,
    down_weight,
    out_cotangent,
):
    hidden_in = layer_input[0].astype(jnp.float32)
    count = hidden_in.shape[0]
    head_size = query_gain.shape[0]
    query_width = query_weight.shape[1]
    key_width = key_matrix.shape[1]
    inner_width = gate_weight.shape[1]
    heads = query_width // head_size
    key_heads = key_width // head_size
    group = heads // key_heads
    scale = head_size ** (-0.5)
    cycles = lax.axis_size("ctx")
    own_index = lax.axis_index("ctx")
    sequence_pos = token_positions[0]
    token_offsets = lax.dynamic_slice_in_dim(sequence_pos, own_index * count, count)
    cosine, sine = rope_tables(token_offsets, head_size)
    cosine = cosine[:, None, :]
    sine = sine[:, None, :]
    first_scale = norm_scale(hidden_in)
    first = (hidden_in * first_scale * attention_gain).astype(jnp.bfloat16)
    query_raw, key_unnormed, value_unnormed = row_products(
        first,
        (
            lax.all_gather(query_weight, "fsdp", axis=0, tiled=True),
            lax.all_gather(key_matrix, "fsdp", axis=0, tiled=True),
            lax.all_gather(value_matrix, "fsdp", axis=0, tiled=True),
        ),
    )
    query_heads = query_raw.reshape(count, heads, head_size)
    query_scale = norm_scale(query_heads)
    query_normed = query_heads * query_scale * query_gain
    query_rot = query_normed * cosine + rotate(query_normed) * sine
    query_grouped = (
        query_rot.reshape(count, key_heads, group, head_size)
        .transpose(1, 2, 0, 3)
        .astype(jnp.bfloat16)
    )
    key_heads_raw = key_unnormed.reshape(count, key_heads, head_size)
    key_scale = norm_scale(key_heads_raw)
    key_normed = key_heads_raw * key_scale * key_norm_gain
    key_low = (
        (key_normed * cosine + rotate(key_normed) * sine)
        .reshape(count, key_width)
        .astype(jnp.bfloat16)
    )
    value_low = value_unnormed.astype(jnp.bfloat16)
    rowmax = jnp.full((key_heads, group, count), masked_score, jnp.float32)
    keys_piece = lax.all_gather(key_low, "ctx", axis=0, tiled=True).reshape(
        -1, key_heads, head_size
    )
    values_piece = lax.all_gather(value_low, "ctx", axis=0, tiled=True).reshape(
        -1, key_heads, head_size
    )
    key_pos = sequence_pos
    allowed = token_offsets[:, None] >= key_pos[None, :]
    scores = (
        jnp.einsum("kgtd,skd->kgts", query_grouped, keys_piece, preferred_element_type=jnp.float32)
        * scale
    )
    scores = jnp.where(allowed, scores, masked_score)
    newmax = jnp.maximum(rowmax, jnp.max(scores, -1))
    weights = jnp.where(allowed, jnp.exp(scores - newmax[..., None]), 0.0)
    accum = jnp.einsum(
        "kgts,skd->kgtd",
        weights.astype(jnp.bfloat16),
        values_piece,
        preferred_element_type=jnp.float32,
    )
    rowsum = jnp.sum(weights, -1)
    accum, rowmax, rowsum = (accum, newmax, rowsum)
    normalized = accum / rowsum[..., None]
    logsum = rowmax + jnp.log(rowsum)
    attention_low = (
        normalized.transpose(2, 0, 1, 3).reshape(count, query_width).astype(jnp.bfloat16)
    )
    output_whole = lax.all_gather(output_weight, "fsdp", axis=0, tiled=True)
    branch_out = jnp.dot(attention_low, output_whole, preferred_element_type=jnp.float32)
    middle = hidden_in + branch_out
    second_scale = norm_scale(middle)
    second = (middle * second_scale * feedforward_gain).astype(jnp.bfloat16)
    gate, up = row_products(
        second,
        (
            lax.all_gather(gate_weight, "fsdp", axis=0, tiled=True),
            lax.all_gather(up_weight, "fsdp", axis=0, tiled=True),
        ),
    )
    sigmoid_gate = jax.nn.sigmoid(gate)
    silu_gate = gate * sigmoid_gate
    hidden_low = (silu_gate * up).astype(jnp.bfloat16)
    (down_out,) = row_products(
        hidden_low, (lax.all_gather(down_weight, "fsdp", axis=0, tiled=True),)
    )
    layer_output = (middle + down_out).astype(jnp.bfloat16)[None]
    cotangent = out_cotangent[0]
    hidden_grad = column_products(
        (cotangent,), lax.all_gather((down_weight,), "fsdp", axis=0, tiled=True)
    )
    up_low = (hidden_grad * silu_gate).astype(jnp.bfloat16)
    gate_low = (hidden_grad * up * sigmoid_gate * (1.0 + gate * (1.0 - sigmoid_gate))).astype(
        jnp.bfloat16
    )
    second_grad = column_products(
        (gate_low, up_low), lax.all_gather((gate_weight, up_weight), "fsdp", axis=0, tiled=True)
    )
    middle_part, feedforward_part = norm_back(middle, second_scale, feedforward_gain, second_grad)
    middle_grad = cotangent.astype(jnp.float32) + middle_part
    middle_low = middle_grad.astype(jnp.bfloat16)
    attention_grad = jnp.einsum(
        "tc,rc->tr", middle_low, output_whole, preferred_element_type=jnp.float32
    )
    attention_grad_low = attention_grad.astype(jnp.bfloat16)
    mixed_grad = attention_grad_low.reshape(count, key_heads, group, head_size).transpose(
        1, 2, 0, 3
    )
    delta = jnp.sum(mixed_grad.astype(jnp.float32) * normalized, -1)

    def cycle_step(index, carry):
        keys_held, values_held, key_acc, value_acc, query_acc = carry
        anchor = (own_index - index) % cycles
        key_pos = lax.dynamic_slice_in_dim(sequence_pos, anchor * count, count)
        keys_piece = keys_held.astype(jnp.bfloat16).reshape(count, key_heads, head_size)
        values_piece = values_held.astype(jnp.bfloat16).reshape(count, key_heads, head_size)
        allowed = token_offsets[:, None] >= key_pos[None, :]
        scores = (
            jnp.einsum(
                "kgtd,skd->kgts", query_grouped, keys_piece, preferred_element_type=jnp.float32
            )
            * scale
        )
        probs = jnp.where(allowed, jnp.exp(scores - logsum[..., None]), 0.0)
        value_acc = value_acc + jnp.einsum(
            "kgts,kgtd->skd",
            probs.astype(jnp.bfloat16),
            mixed_grad,
            preferred_element_type=jnp.float32,
        ).reshape(count, key_width)
        prob_grad = jnp.einsum(
            "kgtd,skd->kgts", mixed_grad, values_piece, preferred_element_type=jnp.float32
        )
        score_grad = (probs * (prob_grad - delta[..., None])).astype(jnp.bfloat16)
        query_acc = (
            query_acc
            + jnp.einsum(
                "kgts,skd->kgtd", score_grad, keys_piece, preferred_element_type=jnp.float32
            )
            * scale
        )
        key_acc = (
            key_acc
            + jnp.einsum(
                "kgts,kgtd->skd", score_grad, query_grouped, preferred_element_type=jnp.float32
            ).reshape(count, key_width)
            * scale
        )
        moved = (
            from_behind(keys_held.astype(jnp.bfloat16), "ctx", 1).astype(keys_held.dtype),
            from_behind(values_held.astype(jnp.bfloat16), "ctx", 1).astype(values_held.dtype),
            from_behind(key_acc.astype(jnp.bfloat16), "ctx", 1).astype(key_acc.dtype),
            from_behind(value_acc.astype(jnp.bfloat16), "ctx", 1).astype(value_acc.dtype),
        )
        return (moved[0], moved[1], moved[2], moved[3], query_acc)

    start_cycle = (
        key_low.astype(jnp.float32),
        value_low.astype(jnp.float32),
        jnp.zeros((count, key_width), jnp.float32),
        jnp.zeros((count, key_width), jnp.float32),
        jnp.zeros((key_heads, group, count, head_size), jnp.float32),
    )
    cycle_done = lax.fori_loop(0, cycles, cycle_step, start_cycle)
    key_acc = cycle_done[2]
    value_acc = cycle_done[3]
    query_acc = cycle_done[4]
    query_rot_grad = query_acc.transpose(2, 0, 1, 3).reshape(count, heads, head_size)
    query_normed_grad = query_rot_grad * cosine + rotate_back(query_rot_grad * sine)
    query_heads_grad, query_part = norm_back(
        query_heads, query_scale, query_gain, query_normed_grad
    )
    query_low_grad = query_heads_grad.reshape(count, query_width).astype(jnp.bfloat16)
    key_rot_grad = key_acc.reshape(count, key_heads, head_size)
    key_normed_grad = key_rot_grad * cosine + rotate_back(key_rot_grad * sine)
    key_heads_grad, key_part = norm_back(key_heads_raw, key_scale, key_norm_gain, key_normed_grad)
    key_low_grad = key_heads_grad.reshape(count, key_width).astype(jnp.bfloat16)
    value_low_grad = value_acc.astype(jnp.bfloat16)
    first_grad = column_products(
        (query_low_grad, key_low_grad, value_low_grad),
        lax.all_gather((query_weight, key_matrix, value_matrix), "fsdp", axis=0, tiled=True),
    )
    input_part, attention_part = norm_back(hidden_in, first_scale, attention_gain, first_grad)
    input_gradient = (middle_grad + input_part)[None]
    rights_first = jnp.concatenate([query_low_grad, key_low_grad, value_low_grad], 1)
    rights_second = jnp.concatenate([gate_low, up_low], 1)
    pairs = (
        (first, rights_first),
        (second, rights_second),
        (middle_low, attention_low),
        (cotangent, hidden_low),
    )
    parts = []
    for left, right in pairs:
        parts.append(jnp.einsum("tr,tc->rc", left, right, preferred_element_type=jnp.float32))
    sums = lax.psum_scatter(
        jnp.concatenate(parts, 1), ("ctx", "fsdp"), scatter_dimension=0, tiled=True
    )
    edges = [0, query_width, query_width + key_width, query_width + 2 * key_width]
    edges = edges + [edges[3] + inner_width, edges[3] + 2 * inner_width]
    edges = edges + [edges[5] + query_width, edges[5] + query_width + inner_width]
    query_gradient = sums[:, edges[0] : edges[1]]
    key_gradient = sums[:, edges[1] : edges[2]]
    value_gradient = sums[:, edges[2] : edges[3]]
    gate_gradient = sums[:, edges[3] : edges[4]]
    up_gradient = sums[:, edges[4] : edges[5]]
    output_gradient = sums[:, edges[5] : edges[6]].T
    down_gradient = sums[:, edges[6] : edges[7]].T
    attention_total, query_total, key_total, feedforward_total = lax.psum(
        (attention_part, query_part, key_part, feedforward_part), ("ctx", "fsdp")
    )
    return (
        layer_output,
        input_gradient,
        attention_total,
        query_gradient,
        key_gradient,
        value_gradient,
        query_total,
        key_total,
        output_gradient,
        feedforward_total,
        gate_gradient,
        up_gradient,
        down_gradient,
    )


MESH = pl.DeviceIdType.MESH
f32 = jnp.float32
bf16 = jnp.bfloat16


def dot(left, right):
    return jnp.dot(left, right, preferred_element_type=f32)


def dot_nt(left, right):
    return lax.dot_general(left, right, (((1,), (1,)), ((), ())), preferred_element_type=f32)


def dot_tn(left, right):
    return lax.dot_general(left, right, (((0,), (0,)), ((), ())), preferred_element_type=f32)


def layer_kernel(
    n, planes, block, head, group, fw,
    x_ref, dy_ref, pos_row, inverse_ref, step_cos, step_sin, ag_ref, fg_ref, qg_ref, kg_ref,
    wq, wk, wv, wo, wg, wu, wd,
    out_ref, dx_ref, gains_ref, got_a, got_b, got_c, got_out, got_qkv,
    w_qkv, w_gu, w_out, w_down, t_out, t_down,
    first, dy_all, second, first_t, dy_t, second_t,
    positions, cosine, sine,
    raw, queries, keys, values, keys_t, values_t, probs, sums, mixed_t, mixed_low,
    hidden, d_gu, d_qkv, dk_acc, dv_acc,
    stage_a, stage_b, stage_c, stage_out, stage_qkv,
    land_a, land_b, land_c, land_out, land_qkv,
    rs_sa, rs_ra, rs_sb, rs_rb, rs_kept, rs_acc,
    middle, d_middle, gain_own, gain_plane, gain_all,
    local_sem, wz_send, wz_recv, hand_send, hand_recv,
    ag_send, ag_recv, ra_send, ra_recv, rb_send, rb_recv,
    zr_send, zr_recv, aa_send, aa_recv, gp_send, gp_recv, gz_send, gz_recv,
):
    c = lax.axis_index("ctx")
    z = lax.axis_index("fsdp")
    dmid = first
    dmid_t = second
    cy, cx, ck = lax.div(c, 4), lax.rem(lax.div(c, 2), 2), lax.rem(c, 2)
    ci = lax.rem(c, 4)
    sign = 1 - 2 * ck
    qw, kw = group * head, head
    pw = 128
    thirds = fw // pw
    piece = pw // 4
    width = x_ref.shape[1]
    scale = head ** (-0.5)
    log2e = 1.4426950408889634
    gots = (got_a, got_b, got_c, got_out, got_qkv)
    stages = (stage_a, stage_b, stage_c, stage_out, stage_qkv)
    lands = (land_a, land_b, land_c, land_out, land_qkv)

    def partner(j):
        y = lax.rem(cy + lax.div(j, 4), 2)
        x = lax.rem(cx + lax.rem(lax.div(j, 2), 2), 2)
        k = lax.rem(ck + lax.rem(j, 2), 2)
        return y * 4 + x * 2 + k

    def chip(slot):
        return lax.rem(cy + lax.div(slot, 2), 2) * 2 + lax.rem(cx + lax.rem(slot, 2), 2)

    def rows(start, size):
        return pl.ds(pl.multiple_of(start * size, size), size)

    def remote(src, dst, send, recv, ctx, plane):
        return pltpu.make_async_remote_copy(
            src_ref=src, dst_ref=dst, send_sem=send, recv_sem=recv,
            device_id={"ctx": ctx, "fsdp": plane}, device_id_type=MESH,
        )

    in_plane, along = [], []

    def launch(started, copy, when=None):
        if when is None:
            copy().start()
        else:
            pl.when(when)(lambda: copy().start())
        started.append((copy, when))

    def drain(started):
        for copy, when in started:
            if when is None:
                copy().wait_send()
            else:
                pl.when(when)(lambda copy=copy: copy().wait_send())
        started.clear()

    own_rows = wq.shape[0]
    out_rows = wo.shape[0] // n

    def own_slices():
        mine = rows(z, own_rows)
        pairs = [
            (wq.at[:, rows(c, qw)], w_qkv.at[mine, 0:qw]),
            (wk.at[:, rows(c, kw)], w_qkv.at[mine, qw:qw + kw]),
            (wv.at[:, rows(c, kw)], w_qkv.at[mine, qw + kw:qw + 2 * kw]),
            (wo.at[rows(c, out_rows)], t_out.at[rows(z, out_rows)]),
        ]
        for t in range(thirds):
            at = 2 * pw * t
            pairs.append((wg.at[:, rows(c * thirds + t, pw)], w_gu.at[mine, at:at + pw]))
            pairs.append((wu.at[:, rows(c * thirds + t, pw)], w_gu.at[mine, at + pw:at + 2 * pw]))
            pairs.append((wd.at[rows((cy * thirds + t) * 4 + ci, piece)], t_down.at[t, rows(z, piece)]))
        return pairs

    local = [pltpu.make_async_copy(src, dst, local_sem.at[i]) for i, (src, dst) in enumerate(own_slices())]
    for copy in local:
        copy.start()

    for land in lands:
        @pl.when(z == 0)
        def _(land=land):
            land[0] = jnp.zeros(land.shape[1:], bf16)

        @pl.when(z == planes - 1)
        def _(land=land):
            land[planes] = jnp.zeros(land.shape[1:], bf16)

    barrier = pltpu.get_barrier_semaphore()
    for j in range(1, n):
        pl.semaphore_signal(barrier, inc=1, device_id={"ctx": partner(j), "fsdp": z}, device_id_type=MESH)
    for d in range(1, planes):
        pl.semaphore_signal(
            barrier, inc=1, device_id={"ctx": c, "fsdp": lax.rem(z + d, planes)}, device_id_type=MESH)
    x = x_ref[...].astype(f32)
    x_scale = lax.rsqrt(jnp.mean(x * x, -1, keepdims=True) + epsilon)
    first[rows(c, block)] = (x * x_scale * ag_ref[...]).astype(bf16)
    dy_all[rows(c, block)] = dy_ref[...]
    for copy in local[:3]:
        copy.wait()
    pl.semaphore_wait(barrier, n + planes - 2)

    def inside(t):
        return jnp.logical_and(t >= 0, t < planes)

    weights = [
        (lambda o: w_qkv.at[rows(o, own_rows)], None),
        (lambda o: t_out.at[rows(o, out_rows)], 0),
    ]
    for t in range(thirds):
        weights.append((lambda o, t=t: w_gu.at[rows(o, own_rows), 2 * pw * t:2 * pw * (t + 1)], None))
        weights.append((lambda o, t=t: t_down.at[t, rows(o, piece)], 1 + t))

    def weight_copy(w, slot, origin, target):
        part = weights[w][0](origin)
        return remote(part, part, wz_send.at[w, slot], wz_recv.at[w, origin], c, target)

    def hand_split(origin, valid):
        mine = 2 * origin + cy == c
        return jnp.logical_and(valid, jnp.logical_not(mine)), jnp.logical_and(valid, mine)

    def weight_start(w):
        for side in range(2):
            d = sign * (1 - 2 * side)
            launch(along, lambda side=side, d=d: weight_copy(w, side, z, z + d), inside(z + d))
        if weights[w][1] is not None:
            hand_over(w, z, 0, *hand_split(z, True))

    def hand_target(h):
        if h == 0:
            return lambda i: w_out.at[rows(i, out_rows)]
        return lambda i: w_down.at[rows((h - 1) * 4 + i, piece)]

    def hand_copy(w, origin, slot):
        h = weights[w][1]
        return remote(
            weights[w][0](origin), hand_target(h)(ci), hand_send.at[h, slot], hand_recv.at[h, ci], 2 * origin + cy, z)

    def hand_over(w, origin, slot, away, here):
        launch(in_plane, lambda: hand_copy(w, origin, slot), away)

        @pl.when(here)
        def _():
            hand_target(weights[w][1])(ci)[...] = weights[w][0](origin)[...]

    def hand_arrive(w):
        h = weights[w][1]
        for i in range(4):
            @pl.when(4 * ck + i != c)
            def _(i=i):
                part = hand_target(h)(i)
                remote(part, part, hand_send.at[h, 0], hand_recv.at[h, i], c, z).wait_recv()

    hops = {}
    for d in range(1, planes):
        for side, way in enumerate((1, -1)):
            origin = z - way * d
            valid = inside(origin)
            passed = jnp.logical_and(valid, inside(z + way))
            hops[d, side] = origin, z + way, valid, passed, hand_split(origin, valid)

    def weight_hop(w, d):
        for side in range(2):
            origin, following, valid, passed, split = hops[d, side]
            pl.when(valid)(lambda: weight_copy(w, 0, origin, z).wait_recv())
            if d < planes - 1:
                launch(
                    along,
                    lambda side=side, origin=origin, following=following: weight_copy(
                        w, 2 * d + side, origin, following),
                    passed)
            if weights[w][1] is not None:
                hand_over(w, origin, 2 * d - 1 + side, *split)

    def gather_copy(buf, g, j, send, origin, target):
        part = buf.at[rows(origin, block)]
        return remote(part, part, ag_send.at[g, send], ag_recv.at[g, j], target, z)

    def gather_start(buf, g):
        for j in (1, 2 + 2 * ck, 4 - 2 * ck):
            launch(in_plane, lambda j=j: gather_copy(buf, g, j, j, c, partner(j)))

    def gather_half(buf, g, j):
        half = block // 2
        part = buf.at[pl.ds(pl.multiple_of(partner(j) * block + (half if j == 2 else 0), half), half)]
        at = 0 if j == 2 else 6
        return remote(part, part, ag_send.at[g, at], ag_recv.at[g, at], partner(6 - j), z)

    def gather_diagonal(buf, g):
        half = block // 2
        for at in (6, 0):
            part = buf.at[pl.ds(pl.multiple_of(partner(6) * block + (0 if at == 6 else half), half), half)]
            remote(part, part, ag_send.at[g, at], ag_recv.at[g, at], c, z).wait_recv()

    def gather_forward(buf, g, j):
        return gather_copy(buf, g, j + 1, j + 1, partner(j), partner(1))

    def gather_take(buf, g, j):
        if j == 6:
            gather_diagonal(buf, g)
        else:
            gather_copy(buf, g, j, j, partner(j), c).wait_recv()
            gather_half(buf, g, j).start()
        gather_forward(buf, g, j).start()

    def gather_sent(buf, g):
        for j in (2, 4, 6):
            in_plane.append((lambda j=j: gather_forward(buf, g, j), None))
            if j < 6:
                in_plane.append((lambda j=j: gather_half(buf, g, j), None))

    def gather_finish(buf, g):
        for j in (2, 4, 6):
            gather_take(buf, g, j)
        gather_sent(buf, g)
        for j in (1, 3, 5, 7):
            gather_copy(buf, g, j, j, partner(j), c).wait_recv()

    def gather_step(buf, g, slot):
        @pl.when(slot == 1)
        def _():
            gather_take(buf, g, 2)
            gather_take(buf, g, 4)

        pl.when(slot == 3)(lambda: gather_take(buf, g, 6))
        gather_copy(buf, g, 2 * slot + 1, 0, partner(2 * slot + 1), c).wait_recv()

    def sum_pair_copy(s, slot):
        return remote(rs_sa.at[s % 2, slot], rs_ra.at[s % 2, slot], ra_send.at[s, slot], ra_recv.at[s, slot], partner(1), z)

    def sum_chip_copy(s, slot):
        return remote(
            rs_sb.at[s % 2, slot], rs_rb.at[s % 2, slot], rb_send.at[s, slot], rb_recv.at[s, slot], partner(2 * slot), z)

    def sum_half_copy(s, slot):
        half = block // 2
        at = pl.ds(pl.multiple_of((slot - 1) * half, half), half)
        return remote(
            rs_sb.at[s % 2, 3, at], rs_rb.at[s % 2, 3, at], rb_send.at[s, 6 - 3 * slot], rb_recv.at[s, 6 - 3 * slot],
            partner(6 - 2 * slot), z)

    def sum_slot(p):
        return jnp.where(p == 0, 3, jnp.where(p == 1, 2 - ck, jnp.where(p == 2, 1 + ck, 0)))

    def sum_start(s, left, partial, prepare=None, ready=None, during=()):
        if prepare is not None:
            prepare(chip(sum_slot(0)))
        if ready is not None:
            ready()

        def body(p, carry):
            slot = sum_slot(p)
            at = [rows(partner(2 * slot + 1), block), rows(partner(2 * slot), block)]
            both = partial(jnp.concatenate([left[i] for i in at], 0))
            rs_sa[s % 2, slot] = both[:block].astype(bf16)
            sum_pair_copy(s, slot).start()
            rs_kept[lax.rem(p, 2)] = both[block:]

            @pl.when(p > 0)
            def _():
                before = sum_slot(p - 1)
                sum_pair_copy(s, before).wait_recv()
                rs_sb[s % 2, before] = (
                    rs_kept[lax.rem(p + 1, 2)] + rs_ra[s % 2, before].astype(f32)).astype(bf16)

            @pl.when(p == 1)
            def _():
                sum_half_copy(s, 1).start()
                sum_half_copy(s, 2).start()

            @pl.when(p > 1)
            def _():
                before = sum_slot(p - 1)
                half = block // 2
                at = pl.ds(pl.multiple_of((before - 1) * half, half), half)
                sum_half_copy(s, before).wait_recv()
                rs_sb[s % 2, before, at] = (
                    rs_sb[s % 2, before, at].astype(f32) + rs_rb[s % 2, 3, at].astype(f32)).astype(bf16)
                sum_chip_copy(s, before).start()

            if prepare is not None:
                @pl.when(p < 3)
                def _():
                    prepare(chip(sum_slot(p + 1)))

            for k, poll in enumerate(during):
                pl.when(p == k)(poll)
            return carry

        lax.fori_loop(0, 4, body, 0)
        for slot in range(4):
            in_plane.append((lambda slot=slot: sum_pair_copy(s, slot), None))
        for slot in (1, 2):
            in_plane.append((lambda slot=slot: sum_half_copy(s, slot), None))
            in_plane.append((lambda slot=slot: sum_chip_copy(s, slot), None))
        sum_pair_copy(s, 0).wait_recv()
        rs_acc[s % 2] = rs_kept[1] + rs_ra[s % 2, 0].astype(f32)

    def sum_finish(s):
        total = rs_acc[s % 2]
        for slot in (1, 2):
            sum_chip_copy(s, slot).wait_recv()
            total = total + rs_rb[s % 2, slot].astype(f32)
        return total

    per = block // planes

    def weight_grad(m, parts):
        def body(i, carry):
            at = 0
            for left, right in parts:
                value = right()
                grad = dot(left[rows(i, 4 * block)], value)
                for k in range(4):
                    for t in range(planes):
                        start = k * block + t * per
                        stages[m][t, 4 * i + k, :, at:at + value.shape[1]] = grad[start:start + per].astype(bf16)
                at += value.shape[1]
            return carry

        lax.fori_loop(0, n // 4, body, 0)
        at_edge = jnp.logical_or(z == 0, z == planes - 1)
        for k in range(planes - 1):
            t = jnp.where(z == 0, planes - 1 - k, k)
            launch(along, lambda t=t: grad_copy(m, t), at_edge)

    def grad_copy(m, t):
        way = jnp.where(z < t, 1, -1)
        last = z + way == t
        slot = jnp.where(jnp.logical_and(last, way < 0), planes, t)
        return remote(
            stages[m].at[t], lands[m].at[slot], zr_send.at[m, t], zr_recv.at[m, slot], c, z + way)

    def grad_arrive(m, slot):
        part = lands[m].at[slot]
        remote(part, part, zr_send.at[m, 0], zr_recv.at[m, slot], c, z).wait_recv()

    def grad_pass(m, t, valid):
        @pl.when(valid)
        def _():
            grad_arrive(m, t)

            def body(i, carry):
                stages[m][t, i] = (stages[m][t, i].astype(f32) + lands[m][t, i].astype(f32)).astype(bf16)
                return carry

            lax.fori_loop(0, n, body, 0)

        launch(along, lambda: grad_copy(m, t), valid)

    def grad_near(m):
        for t in (3, 2):
            grad_pass(m, t, z == 1)
        for t in (0, 1):
            grad_pass(m, t, z == 2)

    def grad_far(m):
        grad_pass(m, 3, z == 2)
        grad_pass(m, 0, z == 1)

    def owner_copy(m, j):
        return remote(lands[m].at[z, partner(j)], gots[m].at[c], aa_send.at[m, j], aa_recv.at[m, j], partner(j), z)

    def hand_out(m):
        pl.when(z > 0)(lambda: grad_arrive(m, z))
        pl.when(z < planes - 1)(lambda: grad_arrive(m, planes))

        def body(i, carry):
            total = stages[m][z, i].astype(f32) + lands[m][z, i].astype(f32) + lands[m][planes, i].astype(f32)
            lands[m][z, i] = total.astype(bf16)
            return carry

        lax.fori_loop(0, n, body, 0)
        for j in (2 + 2 * ck, 3 + 2 * ck, 4 - 2 * ck, 5 - 2 * ck, 6, 7, 1):
            launch(in_plane, lambda j=j: owner_copy(m, j))
        gots[m][c] = lands[m][z, c]

    def hand_receive(m):
        for j in range(1, n):
            owner_copy(m, j).wait_recv()

    weight_start(0)
    gather_start(first, 0)
    for copy in local[3:]:
        copy.wait()

    spread = jnp.broadcast_to(pos_row[...].astype(f32), (head, pos_row.shape[1]))
    positions[...] = spread.T
    side = jnp.where(lax.broadcasted_iota(jnp.int32, (1, head), 1) < head // 2, -1.0, 1.0)

    def table(i, carry):
        run = step_cos.shape[0]
        at = rows(i, run)
        start = positions[pl.ds(pl.multiple_of(i * run, run), 1)] * inverse_ref[...]
        start_cos, start_sin = jnp.cos(start), jnp.sin(start)
        cosine[at] = start_cos * step_cos[...] - start_sin * step_sin[...]
        sine[at] = (start_sin * step_cos[...] + start_cos * step_sin[...]) * side
        return carry

    def turn_over(src, dst):
        def body(i, carry):
            at = rows(i, block)
            dst[:, at] = src[at].T
            return carry

        lax.fori_loop(0, n, body, 0)

    lax.fori_loop(0, 2 * n, table, 0)
    weight_hop(0, 1)
    gather_finish(first, 0)
    weight_hop(0, 2)
    weight_start(1)
    gather_start(dy_all, 1)
    turn_over(first, first_t)
    weight_hop(0, 3)
    weight_start(2)
    weight_start(3)

    def turn(value, at):
        return value * cosine[at] + pltpu.roll(value, head // 2, 1) * sine[at]

    def turn_back(grad, at):
        return grad * cosine[at] - pltpu.roll(grad, head // 2, 1) * sine[at]

    def project(i, carry):
        at = rows(i, 2 * block)
        result = dot(first[at], w_qkv[...])
        raw[at] = result[:, :qw + kw]
        low_values = result[:, qw + kw:].astype(bf16)
        values[at] = low_values
        values_t[:, at] = low_values.T
        for h in range(group + 1):
            part = result[:, h * head:(h + 1) * head]
            inv = lax.rsqrt(jnp.mean(part * part, -1, keepdims=True) + epsilon)
            gain = qg_ref[...] if h < group else kg_ref[...]
            turned = turn(part * inv * gain, at)
            if h < group:
                queries[at, h * head:(h + 1) * head] = (turned * (scale * log2e)).astype(bf16)
            else:
                low_keys = turned.astype(bf16)
                keys[at] = low_keys
                keys_t[:, at] = low_keys.T
        return carry

    lax.fori_loop(0, n // 4, project, 0)
    weight_hop(1, 1)
    lax.fori_loop(n // 4, n // 2, project, 0)
    weight_hop(1, 2)
    gather_finish(dy_all, 1)

    def stack(ref, at):
        return jnp.concatenate([ref[at, h * head:(h + 1) * head] for h in range(group)], 0)

    def attend(place):
        at = rows(place, 2 * block)
        scores = dot_nt(keys[...], stack(queries, at))
        allowed = positions[...] <= pos_row[:, rows(2 * place, block)].astype(f32)
        later = positions[...] <= pos_row[:, rows(2 * place + 1, block)].astype(f32)
        weight = jnp.concatenate(
            [jnp.exp2(jnp.where(later if k % 2 else allowed, scores[:, k * block:(k + 1) * block], masked_score))
             for k in range(2 * group)], 1)
        inv = 1.0 / jnp.sum(weight, 0, keepdims=True)
        low_weight = weight.astype(bf16)
        probs[place] = low_weight
        sums[place] = inv
        result = dot(values_t[...], low_weight) * inv
        mixed_t[place] = result
        for h in range(group):
            mixed_low[at, h * head:(h + 1) * head] = result[:, 2 * h * block:2 * (h + 1) * block].T.astype(bf16)

    def output_ready():
        weight_hop(1, 3)
        weight_start(4)
        weight_start(5)
        hand_arrive(1)
        drain(in_plane)

    def hop_third(t, d):
        weight_hop(2 + 2 * t, d)
        weight_hop(3 + 2 * t, d)

    sum_start(
        0, mixed_low, lambda left: dot(left, w_out[...]), attend, output_ready,
        (lambda: hop_third(0, 1), lambda: hop_third(0, 2)))
    weight_start(6)
    weight_start(7)
    turn_over(dy_all, dy_t)
    hop_third(0, 3)
    mid = x_ref[...].astype(f32) + sum_finish(0)
    middle[...] = mid
    mid_scale = lax.rsqrt(jnp.mean(mid * mid, -1, keepdims=True) + epsilon)
    second[rows(c, block)] = (mid * mid_scale * fg_ref[...]).astype(bf16)
    gather_start(second, 2)
    hop_third(1, 1)
    hand_arrive(3)

    def feed(t, at):
        units, pair = slice(t * pw, (t + 1) * pw), 2 * pw * t
        both = dot(second[at], w_gu[:, pair:pair + 2 * pw])
        back = dot_nt(dy_all[at], w_down[units])
        gate, up = both[:, :pw], both[:, pw:]
        sig = 1.0 / (1.0 + jnp.exp(-gate))
        silu = gate * sig
        hidden[at, units] = (silu * up).astype(bf16)
        d_gu[at, pair:pair + pw] = (back * up * sig * (1.0 + gate * (1.0 - sig))).astype(bf16)
        d_gu[at, pair + pw:pair + 2 * pw] = (back * silu).astype(bf16)

    def feed_arriving(slot, carry):
        gather_step(second, 2, slot)
        at = rows(chip(slot), 2 * block)
        feed(0, at)
        second_t[:, at] = second[at].T
        pl.when(slot == 2)(lambda: hop_third(1, 2))
        return carry

    def third_grad(t):
        weight_grad(t, [
            (second_t, lambda: d_gu[:, 2 * pw * t:2 * pw * (t + 1)]),
            (dy_t, lambda: hidden[:, t * pw:(t + 1) * pw]),
        ])

    def feed_third(t):
        def body(i, carry):
            feed(t, rows(i, 2 * block))
            return carry

        lax.fori_loop(0, n // 2, body, 0)

    lax.fori_loop(0, n // 2, feed_arriving, 0)
    gather_sent(second, 2)
    hop_third(2, 1)
    third_grad(0)
    hop_third(1, 3)
    hand_arrive(5)
    feed_third(1)
    hop_third(2, 2)
    hop_third(2, 3)
    hand_arrive(7)
    sum_start(
        1, d_gu, lambda left: dot_nt(left, w_gu[...]),
        lambda place: feed(thirds - 1, rows(place, 2 * block)))
    third_grad(1)
    third_grad(2)
    d_second = sum_finish(1)

    def norm_back(value, gain, grad):
        inv = lax.rsqrt(jnp.mean(value * value, -1, keepdims=True) + epsilon)
        weighted = grad * gain
        inner = jnp.mean(weighted * value, -1, keepdims=True)
        result = inv * weighted - value * (inv * inv * inv * inner)
        return result, jnp.sum(grad * value * inv, 0, keepdims=True)

    gain_own[...] = jnp.zeros_like(gain_own)
    part, gain_own[1:2, :] = norm_back(middle[...], fg_ref[...], d_second)
    d_mid = dy_ref[...].astype(f32) + part
    d_middle[...] = d_mid
    drain(in_plane)
    dmid[rows(c, block)] = d_mid.astype(bf16)
    gather_start(dmid, 3)
    grad_near(0)

    dk_acc[...] = jnp.zeros_like(dk_acc)
    dv_acc[...] = jnp.zeros_like(dv_acc)

    def attend_back(slot, q_sum):
        gather_step(dmid, 3, slot)
        place = chip(slot)
        at = rows(place, 2 * block)
        d_mix = dot_nt(w_out[...], dmid[at])
        dmid_t[:, at] = dmid[at].T
        d_mix_t = jnp.concatenate([d_mix[h * head:(h + 1) * head] for h in range(group)], 1)
        d_mix_t = (d_mix_t.astype(bf16).astype(f32) * sums[place]).astype(bf16)
        delta = jnp.sum(d_mix_t.astype(f32) * mixed_t[place], 0, keepdims=True)
        weight = probs[place]
        d_prob = dot(values[...], d_mix_t)
        d_score = (weight.astype(f32) * (d_prob - delta)).astype(bf16)
        d_query = dot(keys_t[...], d_score) * scale
        for h in range(group):
            grad = turn_back(d_query[:, 2 * h * block:2 * (h + 1) * block].T, at)
            part, gain_part = norm_back(raw[at, h * head:(h + 1) * head], qg_ref[...], grad)
            d_qkv[at, h * head:(h + 1) * head] = part.astype(bf16)
            q_sum = q_sum + gain_part
        dv_acc[...] += dot(weight, d_mix_t.T)
        dk_acc[...] += dot(d_score, stack(queries, at))
        return q_sum

    zero = jnp.zeros((1, head), f32)
    gain_own[2:3, 0:head] = lax.fori_loop(0, n // 2, attend_back, zero)
    gather_sent(dmid, 3)
    weight_grad(3, [(dmid_t, lambda: mixed_low[...])])
    grad_far(0)
    grad_near(1)
    drain(in_plane)
    sum_start(2, hidden, lambda left: dot(left, w_down[...]))

    def project_back(i, k_sum):
        at = rows(i, 2 * block)
        grad = turn_back(dk_acc[at] * (1.0 / log2e), at)
        part, gain_part = norm_back(raw[at, qw:qw + kw], kg_ref[...], grad)
        d_qkv[at, qw:qw + kw] = part.astype(bf16)
        d_qkv[at, qw + kw:] = dv_acc[at].astype(bf16)
        return k_sum + gain_part

    gain_own[3:4, 0:head] = lax.fori_loop(0, n // 2, project_back, zero)

    weight_grad(4, [(first_t, lambda: d_qkv[...])])
    sum_start(3, d_qkv, lambda left: dot_nt(left, w_qkv[...]))
    grad_far(1)
    grad_near(2)
    out_ref[...] = (middle[...] + sum_finish(2)).astype(bf16)
    hand_out(0)
    grad_far(2)
    grad_near(3)
    hand_out(1)
    x_part, gain_own[0:1, :] = norm_back(x_ref[...].astype(f32), ag_ref[...], sum_finish(3))
    dx_ref[...] = d_middle[...] + x_part

    def gain_plane_copy(j):
        return remote(gain_own, gain_plane.at[c], gp_send.at[j], gp_recv.at[j], partner(j), z)

    def gain_copy(d):
        return remote(gain_all.at[z], gain_all.at[z], gz_send.at[d], gz_recv.at[d], c, lax.rem(z + d, planes))

    for j in range(1, n):
        launch(in_plane, lambda j=j: gain_plane_copy(j))
    gain_plane[c] = gain_own[...]
    grad_far(3)
    hand_out(2)
    for j in range(1, n):
        gain_plane_copy(j).wait_recv()
    total = gain_plane[0]
    for i in range(1, n):
        total = total + gain_plane[i]
    gain_all[z] = total
    for d in range(1, planes):
        launch(along, lambda d=d: gain_copy(d))
    grad_near(4)
    hand_out(3)
    grad_far(4)
    for d in range(1, planes):
        origin = gain_all.at[lax.rem(z + planes - d, planes)]
        remote(origin, origin, gz_send.at[d], gz_recv.at[d], c, z).wait_recv()
    total = gain_all[0]
    for i in range(1, planes):
        total = total + gain_all[i]
    gains_ref[...] = total

    hand_out(4)
    for m in range(5):
        hand_receive(m)
    drain(in_plane)
    drain(along)


def finish_kernel(
    n, head, out_in, dx_in, gains_in, got_a, got_b, got_c, got_out, got_qkv,
    out_ref, dx_ref, ag_ref, q_ref, k_ref, v_ref, qg_ref, kg_ref, o_ref, fg_ref, g_ref, u_ref, d_ref,
):
    out_ref[...] = out_in[...]
    dx_ref[...] = dx_in[...]
    ag_ref[...] = gains_in[0:1, :]
    fg_ref[...] = gains_in[1:2, :]
    qg_ref[...] = gains_in[2:3, 0:head]
    kg_ref[...] = gains_in[3:4, 0:head]
    qw, kw = q_ref.shape[1] // n, k_ref.shape[1] // n
    pw = got_a.shape[2] // 3
    thirds = (got_a, got_b, got_c)
    for i in range(n):
        q_ref[:, i * qw:(i + 1) * qw] = got_qkv[i, :, 0:qw].astype(f32)
        k_ref[:, i * kw:(i + 1) * kw] = got_qkv[i, :, qw:qw + kw].astype(f32)
        v_ref[:, i * kw:(i + 1) * kw] = got_qkv[i, :, qw + kw:].astype(f32)
        o_ref[:, i * qw:(i + 1) * qw] = got_out[i].astype(f32)
        for t, got in enumerate(thirds):
            at = (i * len(thirds) + t) * pw
            g_ref[:, at:at + pw] = got[i, :, 0:pw].astype(f32)
            u_ref[:, at:at + pw] = got[i, :, pw:2 * pw].astype(f32)
            d_ref[:, at:at + pw] = got[i, :, 2 * pw:].astype(f32)


def plane_device(
    layer_input,
    token_positions,
    attention_gain,
    query_weight,
    key_matrix,
    value_matrix,
    query_gain,
    key_norm_gain,
    output_weight,
    feedforward_gain,
    gate_weight,
    up_weight,
    down_weight,
    out_cotangent,
):
    n = lax.axis_size("ctx")
    planes = lax.axis_size("fsdp")
    block, width = layer_input.shape[1:]
    length = token_positions.shape[1]
    head = query_gain.shape[0]
    qw = query_weight.shape[1] // n
    kw = key_matrix.shape[1] // n
    fw = gate_weight.shape[1] // n
    group = qw // head
    per = block // planes
    half = head // 2
    inverse = np.power(rope_base, -np.arange(half) * 2.0 / head).astype(np.float32)
    inverse = np.concatenate([inverse, inverse])[None]
    steps = np.arange(block // 2)[:, None] * inverse.astype(np.float64)
    step_cos, step_sin = (jnp.asarray(f(steps).astype(np.float32)) for f in (np.cos, np.sin))
    inverse = jnp.asarray(inverse)
    vmem = pl.BlockSpec(memory_space=pltpu.VMEM)
    hbm = pl.BlockSpec(memory_space=pl.ANY)
    dma = pltpu.SemaphoreType.DMA
    sizes = (fw, fw, fw, qw, qw + 2 * kw)
    low = lambda *shape: pltpu.VMEM(shape, bf16)
    wide = lambda *shape: pltpu.VMEM(shape, f32)
    scratch = [
        low(width, qw + 2 * kw), low(width, 2 * fw), low(qw, width), low(fw, width),
        low(planes * (output_weight.shape[0] // n), width), low(3, planes * 32, width),
        low(length, width), low(length, width), low(length, width),
        low(width, length), low(width, length), low(width, length),
        wide(length, head), wide(length, head), wide(length, head),
        wide(length, qw + kw), low(length, qw), low(length, kw), low(length, kw),
        low(kw, length), low(kw, length), low(n // 2, length, 2 * group * block), wide(n // 2, 1, 2 * group * block),
        wide(n // 2, head, 2 * group * block), low(length, qw),
        low(length, fw), low(length, 2 * fw), low(length, qw + 2 * kw),
        wide(length, kw), wide(length, kw),
    ]
    scratch += [low(planes, n, per, size) for size in sizes]
    scratch += [low(planes + 1, n, per, size) for size in sizes]
    scratch += [low(2, 4, block, width) for _ in range(4)] + [wide(2, block, width), wide(2, block, width)]
    scratch += [
        wide(block, width), wide(block, width), wide(8, width), wide(n, 8, width), wide(planes, 8, width),
        dma((13,)), dma((8, 6)), dma((8, planes)), dma((4, 7)), dma((4, 4)),
        dma((4, n)), dma((4, n)), dma((4, 4)), dma((4, 4)), dma((4, 4)), dma((4, 4)),
        dma((5, planes)), dma((5, planes + 1)), dma((5, n)), dma((5, n)), dma((n,)), dma((n,)),
        dma((planes,)), dma((planes,)),
    ]
    shapes = [
        jax.ShapeDtypeStruct((block, width), bf16),
        jax.ShapeDtypeStruct((block, width), f32),
        jax.ShapeDtypeStruct((8, width), f32),
    ] + [jax.ShapeDtypeStruct((n, per, size), bf16) for size in sizes]
    results = pl.pallas_call(
        functools.partial(layer_kernel, n, planes, block, head, group, fw),
        out_shape=shapes,
        in_specs=[vmem] * 10 + [hbm] * 7,
        out_specs=[vmem] * len(shapes),
        scratch_shapes=scratch,
        compiler_params=pltpu.CompilerParams(
            collective_id=0, has_side_effects=True, vmem_limit_bytes=60 * 1024 * 1024),
    )(
        layer_input[0], out_cotangent[0], token_positions, inverse, step_cos, step_sin,
        attention_gain[None], feedforward_gain[None], query_gain[None], key_norm_gain[None],
        query_weight, key_matrix, value_matrix, output_weight, gate_weight, up_weight, down_weight,
    )
    plain = lambda rows, columns, kind=f32: jax.ShapeDtypeStruct((rows, columns), kind)
    finals = [
        plain(block, width, bf16), plain(block, width), plain(1, width),
        plain(per, n * qw), plain(per, n * kw), plain(per, n * kw), plain(1, head), plain(1, head),
        plain(per, n * qw), plain(1, width), plain(per, n * fw), plain(per, n * fw), plain(per, n * fw),
    ]
    done = pl.pallas_call(
        functools.partial(finish_kernel, n, head),
        out_shape=finals,
        in_specs=[vmem] * len(shapes),
        out_specs=[vmem] * len(finals),
    )(*results)
    out, dx, ag, q, k, v, qg, kg, o, fg, g, u, d = done
    return out[None], dx[None], ag[0], q, k, v, qg[0], kg[0], o.T, fg[0], g, u, d.T


def solution(mesh):
    in_specs = (
        P("fsdp", "ctx", None),
        P("fsdp", None),
        P(),
        P("fsdp", None),
        P("fsdp", None),
        P("fsdp", None),
        P(),
        P(),
        P("fsdp", None),
        P(),
        P("fsdp", None),
        P("fsdp", None),
        P("fsdp", None),
        P("fsdp", "ctx", None),
    )
    out_specs = (
        P("fsdp", "ctx", None),
        P("fsdp", "ctx", None),
        P(),
        P(("ctx", "fsdp"), None),
        P(("ctx", "fsdp"), None),
        P(("ctx", "fsdp"), None),
        P(),
        P(),
        P(None, ("ctx", "fsdp")),
        P(),
        P(("ctx", "fsdp"), None),
        P(("ctx", "fsdp"), None),
        P(None, ("ctx", "fsdp")),
    )

    def run(*arguments):
        n, planes = mesh.shape["ctx"], mesh.shape["fsdp"]
        key_heads = arguments[4].shape[1] // arguments[6].shape[0]
        whole_heads = n == 8 and planes == 4 and key_heads == n
        return jax.shard_map(
            plane_device if whole_heads else on_device,
            mesh=mesh, in_specs=in_specs, out_specs=out_specs, check_vma=False,
        )(*arguments)

    return run
```

```python
import functools

import jax
import jax.numpy as jnp
import numpy as np
from jax import lax
from jax.experimental import pallas as pl
from jax.experimental.pallas import tpu as pltpu
from jax.sharding import PartitionSpec as P

epsilon = 1e-06
rope_base = 1000000.0
masked_score = -1e30


def from_behind(block, axis, distance):
    devices = range(lax.axis_size(axis))
    route = [((i - distance) % len(devices), i) for i in devices]
    return lax.ppermute(block, axis, route)


def rotate(value_rows):
    half = value_rows.shape[-1] // 2
    return jnp.concatenate([-value_rows[..., half:], value_rows[..., :half]], -1)


def rotate_back(value_rows):
    half = value_rows.shape[-1] // 2
    return jnp.concatenate([value_rows[..., half:], -value_rows[..., :half]], -1)


def rope_tables(token_offsets, head_size):
    half = head_size // 2
    inverse = rope_base ** (-(jnp.arange(half).astype(jnp.float32) * 2.0) / head_size)
    angles = token_offsets.astype(jnp.float32)[:, None] * inverse[None, :]
    cosine = jnp.cos(angles)
    sine = jnp.sin(angles)
    return (jnp.concatenate([cosine, cosine], -1), jnp.concatenate([sine, sine], -1))


def norm_scale(value_rows):
    return lax.rsqrt(jnp.mean(value_rows * value_rows, -1, keepdims=True) + epsilon)


def norm_back(value_rows, scale, gain, grad):
    weighted = grad * gain
    inner = jnp.mean(weighted * value_rows, -1, keepdims=True)
    result = scale * weighted - value_rows * scale * scale * scale * inner
    gain_part = jnp.sum((grad * value_rows * scale).reshape(-1, gain.shape[0]), 0)
    return (result, gain_part)


def row_products(left, pieces):
    return tuple((jnp.dot(left, piece, preferred_element_type=jnp.float32) for piece in pieces))


def column_products(rights, pieces):
    total = jnp.einsum("tc,rc->tr", rights[0], pieces[0], preferred_element_type=jnp.float32)
    for right, piece in zip(rights[1:], pieces[1:]):
        total = total + jnp.einsum("tc,rc->tr", right, piece, preferred_element_type=jnp.float32)
    return total


def on_device(
    layer_input,
    token_positions,
    attention_gain,
    query_weight,
    key_matrix,
    value_matrix,
    query_gain,
    key_norm_gain,
    output_weight,
    feedforward_gain,
    gate_weight,
    up_weight,
    down_weight,
    out_cotangent,
):
    hidden_in = layer_input[0].astype(jnp.float32)
    count = hidden_in.shape[0]
    head_size = query_gain.shape[0]
    query_width = query_weight.shape[1]
    key_width = key_matrix.shape[1]
    inner_width = gate_weight.shape[1]
    heads = query_width // head_size
    key_heads = key_width // head_size
    group = heads // key_heads
    scale = head_size ** (-0.5)
    cycles = lax.axis_size("ctx")
    own_index = lax.axis_index("ctx")
    sequence_pos = token_positions[0]
    token_offsets = lax.dynamic_slice_in_dim(sequence_pos, own_index * count, count)
    cosine, sine = rope_tables(token_offsets, head_size)
    cosine = cosine[:, None, :]
    sine = sine[:, None, :]
    first_scale = norm_scale(hidden_in)
    first = (hidden_in * first_scale * attention_gain).astype(jnp.bfloat16)
    query_raw, key_unnormed, value_unnormed = row_products(
        first,
        (
            lax.all_gather(query_weight, "fsdp", axis=0, tiled=True),
            lax.all_gather(key_matrix, "fsdp", axis=0, tiled=True),
            lax.all_gather(value_matrix, "fsdp", axis=0, tiled=True),
        ),
    )
    query_heads = query_raw.reshape(count, heads, head_size)
    query_scale = norm_scale(query_heads)
    query_normed = query_heads * query_scale * query_gain
    query_rot = query_normed * cosine + rotate(query_normed) * sine
    query_grouped = (
        query_rot.reshape(count, key_heads, group, head_size)
        .transpose(1, 2, 0, 3)
        .astype(jnp.bfloat16)
    )
    key_heads_raw = key_unnormed.reshape(count, key_heads, head_size)
    key_scale = norm_scale(key_heads_raw)
    key_normed = key_heads_raw * key_scale * key_norm_gain
    key_low = (
        (key_normed * cosine + rotate(key_normed) * sine)
        .reshape(count, key_width)
        .astype(jnp.bfloat16)
    )
    value_low = value_unnormed.astype(jnp.bfloat16)
    rowmax = jnp.full((key_heads, group, count), masked_score, jnp.float32)
    keys_piece = lax.all_gather(key_low, "ctx", axis=0, tiled=True).reshape(
        -1, key_heads, head_size
    )
    values_piece = lax.all_gather(value_low, "ctx", axis=0, tiled=True).reshape(
        -1, key_heads, head_size
    )
    key_pos = sequence_pos
    allowed = token_offsets[:, None] >= key_pos[None, :]
    scores = (
        jnp.einsum("kgtd,skd->kgts", query_grouped, keys_piece, preferred_element_type=jnp.float32)
        * scale
    )
    scores = jnp.where(allowed, scores, masked_score)
    newmax = jnp.maximum(rowmax, jnp.max(scores, -1))
    weights = jnp.where(allowed, jnp.exp(scores - newmax[..., None]), 0.0)
    accum = jnp.einsum(
        "kgts,skd->kgtd",
        weights.astype(jnp.bfloat16),
        values_piece,
        preferred_element_type=jnp.float32,
    )
    rowsum = jnp.sum(weights, -1)
    accum, rowmax, rowsum = (accum, newmax, rowsum)
    normalized = accum / rowsum[..., None]
    logsum = rowmax + jnp.log(rowsum)
    attention_low = (
        normalized.transpose(2, 0, 1, 3).reshape(count, query_width).astype(jnp.bfloat16)
    )
    output_whole = lax.all_gather(output_weight, "fsdp", axis=0, tiled=True)
    branch_out = jnp.dot(attention_low, output_whole, preferred_element_type=jnp.float32)
    middle = hidden_in + branch_out
    second_scale = norm_scale(middle)
    second = (middle * second_scale * feedforward_gain).astype(jnp.bfloat16)
    gate, up = row_products(
        second,
        (
            lax.all_gather(gate_weight, "fsdp", axis=0, tiled=True),
            lax.all_gather(up_weight, "fsdp", axis=0, tiled=True),
        ),
    )
    sigmoid_gate = jax.nn.sigmoid(gate)
    silu_gate = gate * sigmoid_gate
    hidden_low = (silu_gate * up).astype(jnp.bfloat16)
    (down_out,) = row_products(
        hidden_low, (lax.all_gather(down_weight, "fsdp", axis=0, tiled=True),)
    )
    layer_output = (middle + down_out).astype(jnp.bfloat16)[None]
    cotangent = out_cotangent[0]
    hidden_grad = column_products(
        (cotangent,), lax.all_gather((down_weight,), "fsdp", axis=0, tiled=True)
    )
    up_low = (hidden_grad * silu_gate).astype(jnp.bfloat16)
    gate_low = (hidden_grad * up * sigmoid_gate * (1.0 + gate * (1.0 - sigmoid_gate))).astype(
        jnp.bfloat16
    )
    second_grad = column_products(
        (gate_low, up_low), lax.all_gather((gate_weight, up_weight), "fsdp", axis=0, tiled=True)
    )
    middle_part, feedforward_part = norm_back(middle, second_scale, feedforward_gain, second_grad)
    middle_grad = cotangent.astype(jnp.float32) + middle_part
    middle_low = middle_grad.astype(jnp.bfloat16)
    attention_grad = jnp.einsum(
        "tc,rc->tr", middle_low, output_whole, preferred_element_type=jnp.float32
    )
    attention_grad_low = attention_grad.astype(jnp.bfloat16)
    mixed_grad = attention_grad_low.reshape(count, key_heads, group, head_size).transpose(
        1, 2, 0, 3
    )
    delta = jnp.sum(mixed_grad.astype(jnp.float32) * normalized, -1)

    def cycle_step(index, carry):
        keys_held, values_held, key_acc, value_acc, query_acc = carry
        anchor = (own_index - index) % cycles
        key_pos = lax.dynamic_slice_in_dim(sequence_pos, anchor * count, count)
        keys_piece = keys_held.astype(jnp.bfloat16).reshape(count, key_heads, head_size)
        values_piece = values_held.astype(jnp.bfloat16).reshape(count, key_heads, head_size)
        allowed = token_offsets[:, None] >= key_pos[None, :]
        scores = (
            jnp.einsum(
                "kgtd,skd->kgts", query_grouped, keys_piece, preferred_element_type=jnp.float32
            )
            * scale
        )
        probs = jnp.where(allowed, jnp.exp(scores - logsum[..., None]), 0.0)
        value_acc = value_acc + jnp.einsum(
            "kgts,kgtd->skd",
            probs.astype(jnp.bfloat16),
            mixed_grad,
            preferred_element_type=jnp.float32,
        ).reshape(count, key_width)
        prob_grad = jnp.einsum(
            "kgtd,skd->kgts", mixed_grad, values_piece, preferred_element_type=jnp.float32
        )
        score_grad = (probs * (prob_grad - delta[..., None])).astype(jnp.bfloat16)
        query_acc = (
            query_acc
            + jnp.einsum(
                "kgts,skd->kgtd", score_grad, keys_piece, preferred_element_type=jnp.float32
            )
            * scale
        )
        key_acc = (
            key_acc
            + jnp.einsum(
                "kgts,kgtd->skd", score_grad, query_grouped, preferred_element_type=jnp.float32
            ).reshape(count, key_width)
            * scale
        )
        moved = (
            from_behind(keys_held.astype(jnp.bfloat16), "ctx", 1).astype(keys_held.dtype),
            from_behind(values_held.astype(jnp.bfloat16), "ctx", 1).astype(values_held.dtype),
            from_behind(key_acc.astype(jnp.bfloat16), "ctx", 1).astype(key_acc.dtype),
            from_behind(value_acc.astype(jnp.bfloat16), "ctx", 1).astype(value_acc.dtype),
        )
        return (moved[0], moved[1], moved[2], moved[3], query_acc)

    start_cycle = (
        key_low.astype(jnp.float32),
        value_low.astype(jnp.float32),
        jnp.zeros((count, key_width), jnp.float32),
        jnp.zeros((count, key_width), jnp.float32),
        jnp.zeros((key_heads, group, count, head_size), jnp.float32),
    )
    cycle_done = lax.fori_loop(0, cycles, cycle_step, start_cycle)
    key_acc = cycle_done[2]
    value_acc = cycle_done[3]
    query_acc = cycle_done[4]
    query_rot_grad = query_acc.transpose(2, 0, 1, 3).reshape(count, heads, head_size)
    query_normed_grad = query_rot_grad * cosine + rotate_back(query_rot_grad * sine)
    query_heads_grad, query_part = norm_back(
        query_heads, query_scale, query_gain, query_normed_grad
    )
    query_low_grad = query_heads_grad.reshape(count, query_width).astype(jnp.bfloat16)
    key_rot_grad = key_acc.reshape(count, key_heads, head_size)
    key_normed_grad = key_rot_grad * cosine + rotate_back(key_rot_grad * sine)
    key_heads_grad, key_part = norm_back(key_heads_raw, key_scale, key_norm_gain, key_normed_grad)
    key_low_grad = key_heads_grad.reshape(count, key_width).astype(jnp.bfloat16)
    value_low_grad = value_acc.astype(jnp.bfloat16)
    first_grad = column_products(
        (query_low_grad, key_low_grad, value_low_grad),
        lax.all_gather((query_weight, key_matrix, value_matrix), "fsdp", axis=0, tiled=True),
    )
    input_part, attention_part = norm_back(hidden_in, first_scale, attention_gain, first_grad)
    input_gradient = (middle_grad + input_part)[None]
    rights_first = jnp.concatenate([query_low_grad, key_low_grad, value_low_grad], 1)
    rights_second = jnp.concatenate([gate_low, up_low], 1)
    pairs = (
        (first, rights_first),
        (second, rights_second),
        (middle_low, attention_low),
        (cotangent, hidden_low),
    )
    parts = []
    for left, right in pairs:
        parts.append(jnp.einsum("tr,tc->rc", left, right, preferred_element_type=jnp.float32))
    sums = lax.psum_scatter(
        jnp.concatenate(parts, 1), ("ctx", "fsdp"), scatter_dimension=0, tiled=True
    )
    edges = [0, query_width, query_width + key_width, query_width + 2 * key_width]
    edges = edges + [edges[3] + inner_width, edges[3] + 2 * inner_width]
    edges = edges + [edges[5] + query_width, edges[5] + query_width + inner_width]
    query_gradient = sums[:, edges[0] : edges[1]]
    key_gradient = sums[:, edges[1] : edges[2]]
    value_gradient = sums[:, edges[2] : edges[3]]
    gate_gradient = sums[:, edges[3] : edges[4]]
    up_gradient = sums[:, edges[4] : edges[5]]
    output_gradient = sums[:, edges[5] : edges[6]].T
    down_gradient = sums[:, edges[6] : edges[7]].T
    attention_total, query_total, key_total, feedforward_total = lax.psum(
        (attention_part, query_part, key_part, feedforward_part), ("ctx", "fsdp")
    )
    return (
        layer_output,
        input_gradient,
        attention_total,
        query_gradient,
        key_gradient,
        value_gradient,
        query_total,
        key_total,
        output_gradient,
        feedforward_total,
        gate_gradient,
        up_gradient,
        down_gradient,
    )


MESH = pl.DeviceIdType.MESH
f32 = jnp.float32
bf16 = jnp.bfloat16


def dot(left, right):
    return jnp.dot(left, right, preferred_element_type=f32)


def dot_nt(left, right):
    return lax.dot_general(left, right, (((1,), (1,)), ((), ())), preferred_element_type=f32)


def dot_tn(left, right):
    return lax.dot_general(left, right, (((0,), (0,)), ((), ())), preferred_element_type=f32)


def layer_kernel(
    n, planes, block, head, group, fw,
    x_ref, dy_ref, pos_row, inverse_ref, step_cos, step_sin, ag_ref, fg_ref, qg_ref, kg_ref,
    wq, wk, wv, wo, wg, wu, wd,
    out_ref, dx_ref, gains_ref, got_a, got_b, got_c, got_out, got_qkv,
    w_qkv, w_gu, w_out, w_down, t_out, t_down,
    first, dy_all, second, first_t, dy_t, second_t,
    positions, cosine, sine,
    raw, queries, keys, values, keys_t, values_t, probs, sums, mixed_t, mixed_low,
    hidden, d_gu, d_qkv, dk_acc, dv_acc,
    stage_a, stage_b, stage_c, stage_out, stage_qkv,
    land_a, land_b, land_c, land_out, land_qkv,
    rs_sa, rs_ra, rs_sb, rs_rb, rs_kept, rs_acc,
    middle, d_middle, gain_own, gain_plane, gain_all,
    local_sem, wz_send, wz_recv, hand_send, hand_recv,
    ag_send, ag_recv, ra_send, ra_recv, rb_send, rb_recv,
    zr_send, zr_recv, aa_send, aa_recv, gp_send, gp_recv, gz_send, gz_recv,
):
    c = lax.axis_index("ctx")
    z = lax.axis_index("fsdp")
    dmid = first
    dmid_t = second
    cy, cx, ck = lax.div(c, 4), lax.rem(lax.div(c, 2), 2), lax.rem(c, 2)
    ci = lax.rem(c, 4)
    sign = 1 - 2 * ck
    qw, kw = group * head, head
    pw = 128
    thirds = fw // pw
    piece = pw // 4
    width = x_ref.shape[1]
    scale = head ** (-0.5)
    log2e = 1.4426950408889634
    gots = (got_a, got_b, got_c, got_out, got_qkv)
    stages = (stage_a, stage_b, stage_c, stage_out, stage_qkv)
    lands = (land_a, land_b, land_c, land_out, land_qkv)

    def partner(j):
        y = lax.rem(cy + lax.div(j, 4), 2)
        x = lax.rem(cx + lax.rem(lax.div(j, 2), 2), 2)
        k = lax.rem(ck + lax.rem(j, 2), 2)
        return y * 4 + x * 2 + k

    def chip(slot):
        return lax.rem(cy + lax.div(slot, 2), 2) * 2 + lax.rem(cx + lax.rem(slot, 2), 2)

    def rows(start, size):
        return pl.ds(pl.multiple_of(start * size, size), size)

    def remote(src, dst, send, recv, ctx, plane):
        return pltpu.make_async_remote_copy(
            src_ref=src, dst_ref=dst, send_sem=send, recv_sem=recv,
            device_id={"ctx": ctx, "fsdp": plane}, device_id_type=MESH,
        )

    in_plane, along, weight_sends = [], [], []

    def launch(started, copy, when=None):
        if when is None:
            copy().start()
        else:
            pl.when(when)(lambda: copy().start())
        started.append((copy, when))

    def drain(started):
        for copy, when in started:
            if when is None:
                copy().wait_send()
            else:
                pl.when(when)(lambda copy=copy: copy().wait_send())
        started.clear()

    own_rows = wq.shape[0]
    out_rows = wo.shape[0] // n

    def own_slices():
        mine = rows(z, own_rows)
        pairs = [
            (wq.at[:, rows(c, qw)], w_qkv.at[mine, 0:qw]),
            (wk.at[:, rows(c, kw)], w_qkv.at[mine, qw:qw + kw]),
            (wv.at[:, rows(c, kw)], w_qkv.at[mine, qw + kw:qw + 2 * kw]),
            (wo.at[rows(c, out_rows)], t_out.at[rows(z, out_rows)]),
        ]
        for t in range(thirds):
            at = 2 * pw * t
            pairs.append((wg.at[:, rows(c * thirds + t, pw)], w_gu.at[mine, at:at + pw]))
            pairs.append((wu.at[:, rows(c * thirds + t, pw)], w_gu.at[mine, at + pw:at + 2 * pw]))
            pairs.append((wd.at[rows((cy * thirds + t) * 4 + ci, piece)], t_down.at[t, rows(z, piece)]))
        return pairs

    local = [pltpu.make_async_copy(src, dst, local_sem.at[i]) for i, (src, dst) in enumerate(own_slices())]
    for copy in local:
        copy.start()

    for land in lands:
        @pl.when(z == 0)
        def _(land=land):
            land[0] = jnp.zeros(land.shape[1:], bf16)

        @pl.when(z == planes - 1)
        def _(land=land):
            land[planes] = jnp.zeros(land.shape[1:], bf16)

    barrier = pltpu.get_barrier_semaphore()
    for j in range(1, n):
        pl.semaphore_signal(barrier, inc=1, device_id={"ctx": partner(j), "fsdp": z}, device_id_type=MESH)
    for d in range(1, planes):
        pl.semaphore_signal(
            barrier, inc=1, device_id={"ctx": c, "fsdp": lax.rem(z + d, planes)}, device_id_type=MESH)
    x = x_ref[...].astype(f32)
    x_scale = lax.rsqrt(jnp.mean(x * x, -1, keepdims=True) + epsilon)
    first[rows(c, block)] = (x * x_scale * ag_ref[...]).astype(bf16)
    dy_all[rows(c, block)] = dy_ref[...]
    for copy in local[:3]:
        copy.wait()
    pl.semaphore_wait(barrier, n + planes - 2)

    def inside(t):
        return jnp.logical_and(t >= 0, t < planes)

    weights = [
        (lambda o: w_qkv.at[rows(o, own_rows)], None),
        (lambda o: t_out.at[rows(o, out_rows)], 0),
    ]
    for t in range(thirds):
        weights.append((lambda o, t=t: w_gu.at[rows(o, own_rows), 2 * pw * t:2 * pw * (t + 1)], None))
        weights.append((lambda o, t=t: t_down.at[t, rows(o, piece)], 1 + t))

    def weight_copy(w, slot, origin, target):
        part = weights[w][0](origin)
        return remote(part, part, wz_send.at[w, slot], wz_recv.at[w, origin], c, target)

    def hand_split(origin, valid):
        mine = 2 * origin + cy == c
        return jnp.logical_and(valid, jnp.logical_not(mine)), jnp.logical_and(valid, mine)

    def weight_start(w):
        for side in range(2):
            d = sign * (1 - 2 * side)
            launch(weight_sends, lambda side=side, d=d: weight_copy(w, side, z, z + d), inside(z + d))
        if weights[w][1] is not None:
            hand_over(w, z, 0, *hand_split(z, True))

    def hand_target(h):
        if h == 0:
            return lambda i: w_out.at[rows(i, out_rows)]
        return lambda i: w_down.at[rows((h - 1) * 4 + i, piece)]

    def hand_copy(w, origin, slot):
        h = weights[w][1]
        return remote(
            weights[w][0](origin), hand_target(h)(ci), hand_send.at[h, slot], hand_recv.at[h, ci], 2 * origin + cy, z)

    def hand_over(w, origin, slot, away, here):
        launch(in_plane, lambda: hand_copy(w, origin, slot), away)

        @pl.when(here)
        def _():
            hand_target(weights[w][1])(ci)[...] = weights[w][0](origin)[...]

    def hand_arrive(w):
        h = weights[w][1]
        for i in range(4):
            @pl.when(4 * ck + i != c)
            def _(i=i):
                part = hand_target(h)(i)
                remote(part, part, hand_send.at[h, 0], hand_recv.at[h, i], c, z).wait_recv()

    hops = {}
    for d in range(1, planes):
        for side, way in enumerate((1, -1)):
            origin = z - way * d
            valid = inside(origin)
            passed = jnp.logical_and(valid, inside(z + way))
            hops[d, side] = origin, z + way, valid, passed, hand_split(origin, valid)

    def weight_hop(w, d):
        for side in range(2):
            origin, following, valid, passed, split = hops[d, side]
            pl.when(valid)(lambda: weight_copy(w, 0, origin, z).wait_recv())
            if d < planes - 1:
                launch(
                    weight_sends,
                    lambda side=side, origin=origin, following=following: weight_copy(
                        w, 2 * d + side, origin, following),
                    passed)
            if weights[w][1] is not None:
                hand_over(w, origin, 2 * d - 1 + side, *split)

    def gather_copy(buf, g, j, send, origin, target):
        part = buf.at[rows(origin, block)]
        return remote(part, part, ag_send.at[g, send], ag_recv.at[g, j], target, z)

    def gather_start(buf, g):
        for j in (1, 2 + 2 * ck, 4 - 2 * ck):
            launch(in_plane, lambda j=j: gather_copy(buf, g, j, j, c, partner(j)))

    def gather_half(buf, g, j):
        half = block // 2
        part = buf.at[pl.ds(pl.multiple_of(partner(j) * block + (half if j == 2 else 0), half), half)]
        at = 0 if j == 2 else 6
        return remote(part, part, ag_send.at[g, at], ag_recv.at[g, at], partner(6 - j), z)

    def gather_diagonal(buf, g):
        half = block // 2
        for at in (6, 0):
            part = buf.at[pl.ds(pl.multiple_of(partner(6) * block + (0 if at == 6 else half), half), half)]
            remote(part, part, ag_send.at[g, at], ag_recv.at[g, at], c, z).wait_recv()

    def gather_forward(buf, g, j):
        return gather_copy(buf, g, j + 1, j + 1, partner(j), partner(1))

    def gather_take(buf, g, j):
        if j == 6:
            gather_diagonal(buf, g)
        else:
            gather_copy(buf, g, j, j, partner(j), c).wait_recv()
            gather_half(buf, g, j).start()
        gather_forward(buf, g, j).start()

    def gather_sent(buf, g):
        for j in (2, 4, 6):
            in_plane.append((lambda j=j: gather_forward(buf, g, j), None))
            if j < 6:
                in_plane.append((lambda j=j: gather_half(buf, g, j), None))

    def gather_finish(buf, g):
        for j in (2, 4, 6):
            gather_take(buf, g, j)
        gather_sent(buf, g)
        for j in (1, 3, 5, 7):
            gather_copy(buf, g, j, j, partner(j), c).wait_recv()

    def gather_step(buf, g, slot):
        @pl.when(slot == 1)
        def _():
            gather_take(buf, g, 2)
            gather_take(buf, g, 4)

        pl.when(slot == 3)(lambda: gather_take(buf, g, 6))
        gather_copy(buf, g, 2 * slot + 1, 0, partner(2 * slot + 1), c).wait_recv()

    def sum_pair_copy(s, slot):
        return remote(rs_sa.at[s % 2, slot], rs_ra.at[s % 2, slot], ra_send.at[s, slot], ra_recv.at[s, slot], partner(1), z)

    def sum_chip_copy(s, slot):
        return remote(
            rs_sb.at[s % 2, slot], rs_rb.at[s % 2, slot], rb_send.at[s, slot], rb_recv.at[s, slot], partner(2 * slot), z)

    def sum_half_copy(s, slot):
        half = block // 2
        at = pl.ds(pl.multiple_of((slot - 1) * half, half), half)
        return remote(
            rs_sb.at[s % 2, 3, at], rs_rb.at[s % 2, 3, at], rb_send.at[s, 6 - 3 * slot], rb_recv.at[s, 6 - 3 * slot],
            partner(6 - 2 * slot), z)

    def sum_slot(p):
        return jnp.where(p == 0, 3, jnp.where(p == 1, 2 - ck, jnp.where(p == 2, 1 + ck, 0)))

    def sum_start(s, left, partial, prepare=None, ready=None, during=()):
        if prepare is not None:
            prepare(chip(sum_slot(0)))
        if ready is not None:
            ready()

        def body(p, carry):
            slot = sum_slot(p)
            at = [rows(partner(2 * slot + 1), block), rows(partner(2 * slot), block)]
            both = partial(jnp.concatenate([left[i] for i in at], 0))
            rs_sa[s % 2, slot] = both[:block].astype(bf16)
            sum_pair_copy(s, slot).start()
            rs_kept[lax.rem(p, 2)] = both[block:]

            @pl.when(p > 0)
            def _():
                before = sum_slot(p - 1)
                sum_pair_copy(s, before).wait_recv()
                rs_sb[s % 2, before] = (
                    rs_kept[lax.rem(p + 1, 2)] + rs_ra[s % 2, before].astype(f32)).astype(bf16)

            @pl.when(p == 1)
            def _():
                sum_half_copy(s, 1).start()
                sum_half_copy(s, 2).start()

            @pl.when(p > 1)
            def _():
                before = sum_slot(p - 1)
                half = block // 2
                at = pl.ds(pl.multiple_of((before - 1) * half, half), half)
                sum_half_copy(s, before).wait_recv()
                rs_sb[s % 2, before, at] = (
                    rs_sb[s % 2, before, at].astype(f32) + rs_rb[s % 2, 3, at].astype(f32)).astype(bf16)
                sum_chip_copy(s, before).start()

            if prepare is not None:
                @pl.when(p < 3)
                def _():
                    prepare(chip(sum_slot(p + 1)))

            for k, poll in enumerate(during):
                pl.when(p == k)(poll)
            return carry

        lax.fori_loop(0, 4, body, 0)
        for slot in range(4):
            in_plane.append((lambda slot=slot: sum_pair_copy(s, slot), None))
        for slot in (1, 2):
            in_plane.append((lambda slot=slot: sum_half_copy(s, slot), None))
            in_plane.append((lambda slot=slot: sum_chip_copy(s, slot), None))
        sum_pair_copy(s, 0).wait_recv()
        rs_acc[s % 2] = rs_kept[1] + rs_ra[s % 2, 0].astype(f32)

    def sum_finish(s):
        total = rs_acc[s % 2]
        for slot in (1, 2):
            sum_chip_copy(s, slot).wait_recv()
            total = total + rs_rb[s % 2, slot].astype(f32)
        return total

    per = block // planes

    def weight_grad(m, parts):
        def body(i, carry):
            at = 0
            for left, right in parts:
                value = right()
                grad = dot(left[rows(i, 4 * block)], value)
                for k in range(4):
                    for t in range(planes):
                        start = k * block + t * per
                        stages[m][t, 4 * i + k, :, at:at + value.shape[1]] = grad[start:start + per].astype(bf16)
                at += value.shape[1]
            return carry

        lax.fori_loop(0, n // 4, body, 0)
        at_edge = jnp.logical_or(z == 0, z == planes - 1)
        for k in range(planes - 1):
            t = jnp.where(z == 0, planes - 1 - k, k)
            launch(along, lambda t=t: grad_copy(m, t), at_edge)

    def grad_copy(m, t):
        way = jnp.where(z < t, 1, -1)
        last = z + way == t
        slot = jnp.where(jnp.logical_and(last, way < 0), planes, t)
        return remote(
            stages[m].at[t], lands[m].at[slot], zr_send.at[m, t], zr_recv.at[m, slot], c, z + way)

    def grad_arrive(m, slot):
        part = lands[m].at[slot]
        remote(part, part, zr_send.at[m, 0], zr_recv.at[m, slot], c, z).wait_recv()

    def grad_pass(m, t, valid):
        @pl.when(valid)
        def _():
            grad_arrive(m, t)

            def body(i, carry):
                stages[m][t, i] = (stages[m][t, i].astype(f32) + lands[m][t, i].astype(f32)).astype(bf16)
                return carry

            lax.fori_loop(0, n, body, 0)

        launch(along, lambda: grad_copy(m, t), valid)

    def grad_near(m):
        for t in (3, 2):
            grad_pass(m, t, z == 1)
        for t in (0, 1):
            grad_pass(m, t, z == 2)

    def grad_far(m):
        grad_pass(m, 3, z == 2)
        grad_pass(m, 0, z == 1)

    def owner_copy(m, j):
        return remote(lands[m].at[z, partner(j)], gots[m].at[c], aa_send.at[m, j], aa_recv.at[m, j], partner(j), z)

    def hand_out(m):
        pl.when(z > 0)(lambda: grad_arrive(m, z))
        pl.when(z < planes - 1)(lambda: grad_arrive(m, planes))

        def body(i, carry):
            total = stages[m][z, i].astype(f32) + lands[m][z, i].astype(f32) + lands[m][planes, i].astype(f32)
            lands[m][z, i] = total.astype(bf16)
            return carry

        lax.fori_loop(0, n, body, 0)
        for j in (2 + 2 * ck, 3 + 2 * ck, 4 - 2 * ck, 5 - 2 * ck, 6, 7, 1):
            launch(in_plane, lambda j=j: owner_copy(m, j))
        gots[m][c] = lands[m][z, c]

    def hand_receive(m):
        for j in range(1, n):
            owner_copy(m, j).wait_recv()

    weight_start(0)
    gather_start(first, 0)
    for copy in local[3:]:
        copy.wait()

    spread = jnp.broadcast_to(pos_row[...].astype(f32), (head, pos_row.shape[1]))
    positions[...] = spread.T
    side = jnp.where(lax.broadcasted_iota(jnp.int32, (1, head), 1) < head // 2, -1.0, 1.0)

    def table(i, carry):
        run = step_cos.shape[0]
        at = rows(i, run)
        start = positions[pl.ds(pl.multiple_of(i * run, run), 1)] * inverse_ref[...]
        start_cos, start_sin = jnp.cos(start), jnp.sin(start)
        cosine[at] = start_cos * step_cos[...] - start_sin * step_sin[...]
        sine[at] = (start_sin * step_cos[...] + start_cos * step_sin[...]) * side
        return carry

    def turn_over(src, dst):
        def body(i, carry):
            at = rows(i, block)
            dst[:, at] = src[at].T
            return carry

        lax.fori_loop(0, n, body, 0)

    lax.fori_loop(0, 2 * n, table, 0)
    weight_hop(0, 1)
    gather_finish(first, 0)
    weight_hop(0, 2)
    weight_start(1)
    gather_start(dy_all, 1)
    turn_over(first, first_t)
    weight_hop(0, 3)
    weight_start(2)
    weight_start(3)

    def turn(value, at):
        return value * cosine[at] + pltpu.roll(value, head // 2, 1) * sine[at]

    def turn_back(grad, at):
        return grad * cosine[at] - pltpu.roll(grad, head // 2, 1) * sine[at]

    def project(i, carry):
        at = rows(i, 2 * block)
        result = dot(first[at], w_qkv[...])
        raw[at] = result[:, :qw + kw]
        low_values = result[:, qw + kw:].astype(bf16)
        values[at] = low_values
        values_t[:, at] = low_values.T
        for h in range(group + 1):
            part = result[:, h * head:(h + 1) * head]
            inv = lax.rsqrt(jnp.mean(part * part, -1, keepdims=True) + epsilon)
            gain = qg_ref[...] if h < group else kg_ref[...]
            turned = turn(part * inv * gain, at)
            if h < group:
                queries[at, h * head:(h + 1) * head] = (turned * (scale * log2e)).astype(bf16)
            else:
                low_keys = turned.astype(bf16)
                keys[at] = low_keys
                keys_t[:, at] = low_keys.T
        return carry

    lax.fori_loop(0, n // 4, project, 0)
    weight_hop(1, 1)
    lax.fori_loop(n // 4, n // 2, project, 0)
    weight_hop(1, 2)
    gather_finish(dy_all, 1)

    def stack(ref, at):
        return jnp.concatenate([ref[at, h * head:(h + 1) * head] for h in range(group)], 0)

    def attend(place):
        at = rows(place, 2 * block)
        scores = dot_nt(keys[...], stack(queries, at))
        allowed = positions[...] <= pos_row[:, rows(2 * place, block)].astype(f32)
        later = positions[...] <= pos_row[:, rows(2 * place + 1, block)].astype(f32)
        weight = jnp.concatenate(
            [jnp.exp2(jnp.where(later if k % 2 else allowed, scores[:, k * block:(k + 1) * block], masked_score))
             for k in range(2 * group)], 1)
        inv = 1.0 / jnp.sum(weight, 0, keepdims=True)
        low_weight = weight.astype(bf16)
        probs[place] = low_weight
        sums[place] = inv
        result = dot(values_t[...], low_weight) * inv
        mixed_t[place] = result
        for h in range(group):
            mixed_low[at, h * head:(h + 1) * head] = result[:, 2 * h * block:2 * (h + 1) * block].T.astype(bf16)

    def output_ready():
        weight_hop(1, 3)
        weight_start(4)
        weight_start(5)
        hand_arrive(1)
        drain(in_plane)

    def hop_third(t, d):
        weight_hop(2 + 2 * t, d)
        weight_hop(3 + 2 * t, d)

    sum_start(
        0, mixed_low, lambda left: dot(left, w_out[...]), attend, output_ready,
        (lambda: hop_third(0, 1), lambda: hop_third(0, 2), lambda: hop_third(1, 1)))
    weight_start(6)
    weight_start(7)
    hop_third(0, 3)
    turn_over(dy_all, dy_t)
    hop_third(1, 2)
    mid = x_ref[...].astype(f32) + sum_finish(0)
    middle[...] = mid
    mid_scale = lax.rsqrt(jnp.mean(mid * mid, -1, keepdims=True) + epsilon)
    second[rows(c, block)] = (mid * mid_scale * fg_ref[...]).astype(bf16)
    gather_start(second, 2)
    hop_third(2, 1)
    hand_arrive(3)

    def feed(t, at):
        units, pair = slice(t * pw, (t + 1) * pw), 2 * pw * t
        both = dot(second[at], w_gu[:, pair:pair + 2 * pw])
        back = dot_nt(dy_all[at], w_down[units])
        gate, up = both[:, :pw], both[:, pw:]
        sig = 1.0 / (1.0 + jnp.exp(-gate))
        silu = gate * sig
        hidden[at, units] = (silu * up).astype(bf16)
        d_gu[at, pair:pair + pw] = (back * up * sig * (1.0 + gate * (1.0 - sig))).astype(bf16)
        d_gu[at, pair + pw:pair + 2 * pw] = (back * silu).astype(bf16)

    def feed_arriving(slot, carry):
        gather_step(second, 2, slot)
        at = rows(chip(slot), 2 * block)
        feed(0, at)
        second_t[:, at] = second[at].T
        pl.when(slot == 2)(lambda: hop_third(2, 2))
        return carry

    def third_grad(t):
        weight_grad(t, [
            (second_t, lambda: d_gu[:, 2 * pw * t:2 * pw * (t + 1)]),
            (dy_t, lambda: hidden[:, t * pw:(t + 1) * pw]),
        ])

    def feed_third(t):
        def body(i, carry):
            feed(t, rows(i, 2 * block))
            return carry

        lax.fori_loop(0, n // 2, body, 0)

    lax.fori_loop(0, n // 2, feed_arriving, 0)
    gather_sent(second, 2)
    hop_third(1, 3)
    third_grad(0)
    hand_arrive(5)
    feed_third(1)
    hop_third(2, 3)
    hand_arrive(7)
    sum_start(
        1, d_gu, lambda left: dot_nt(left, w_gu[...]),
        lambda place: feed(thirds - 1, rows(place, 2 * block)))
    third_grad(1)
    third_grad(2)
    d_second = sum_finish(1)

    def norm_back(value, gain, grad):
        inv = lax.rsqrt(jnp.mean(value * value, -1, keepdims=True) + epsilon)
        weighted = grad * gain
        inner = jnp.mean(weighted * value, -1, keepdims=True)
        result = inv * weighted - value * (inv * inv * inv * inner)
        return result, jnp.sum(grad * value * inv, 0, keepdims=True)

    gain_own[...] = jnp.zeros_like(gain_own)
    part, gain_own[1:2, :] = norm_back(middle[...], fg_ref[...], d_second)
    d_mid = dy_ref[...].astype(f32) + part
    d_middle[...] = d_mid
    drain(in_plane)
    dmid[rows(c, block)] = d_mid.astype(bf16)
    gather_start(dmid, 3)
    drain(weight_sends)
    grad_near(0)

    dk_acc[...] = jnp.zeros_like(dk_acc)
    dv_acc[...] = jnp.zeros_like(dv_acc)

    def attend_back(slot, q_sum):
        gather_step(dmid, 3, slot)
        place = chip(slot)
        at = rows(place, 2 * block)
        d_mix = dot_nt(w_out[...], dmid[at])
        dmid_t[:, at] = dmid[at].T
        d_mix_t = jnp.concatenate([d_mix[h * head:(h + 1) * head] for h in range(group)], 1)
        d_mix_t = (d_mix_t.astype(bf16).astype(f32) * sums[place]).astype(bf16)
        delta = jnp.sum(d_mix_t.astype(f32) * mixed_t[place], 0, keepdims=True)
        weight = probs[place]
        d_prob = dot(values[...], d_mix_t)
        d_score = (weight.astype(f32) * (d_prob - delta)).astype(bf16)
        d_query = dot(keys_t[...], d_score) * scale
        for h in range(group):
            grad = turn_back(d_query[:, 2 * h * block:2 * (h + 1) * block].T, at)
            part, gain_part = norm_back(raw[at, h * head:(h + 1) * head], qg_ref[...], grad)
            d_qkv[at, h * head:(h + 1) * head] = part.astype(bf16)
            q_sum = q_sum + gain_part
        dv_acc[...] += dot(weight, d_mix_t.T)
        dk_acc[...] += dot(d_score, stack(queries, at))
        return q_sum

    zero = jnp.zeros((1, head), f32)
    gain_own[2:3, 0:head] = lax.fori_loop(0, n // 2, attend_back, zero)
    gather_sent(dmid, 3)
    weight_grad(3, [(dmid_t, lambda: mixed_low[...])])
    grad_far(0)
    grad_near(1)
    drain(in_plane)
    sum_start(2, hidden, lambda left: dot(left, w_down[...]))

    def project_back(i, k_sum):
        at = rows(i, 2 * block)
        grad = turn_back(dk_acc[at] * (1.0 / log2e), at)
        part, gain_part = norm_back(raw[at, qw:qw + kw], kg_ref[...], grad)
        d_qkv[at, qw:qw + kw] = part.astype(bf16)
        d_qkv[at, qw + kw:] = dv_acc[at].astype(bf16)
        return k_sum + gain_part

    gain_own[3:4, 0:head] = lax.fori_loop(0, n // 2, project_back, zero)

    weight_grad(4, [(first_t, lambda: d_qkv[...])])
    sum_start(3, d_qkv, lambda left: dot_nt(left, w_qkv[...]))
    grad_far(1)
    grad_near(2)
    out_ref[...] = (middle[...] + sum_finish(2)).astype(bf16)
    hand_out(0)
    grad_far(2)
    grad_near(3)
    hand_out(1)
    x_part, gain_own[0:1, :] = norm_back(x_ref[...].astype(f32), ag_ref[...], sum_finish(3))
    dx_ref[...] = d_middle[...] + x_part

    def gain_plane_copy(j):
        return remote(gain_own, gain_plane.at[c], gp_send.at[j], gp_recv.at[j], partner(j), z)

    def gain_copy(d):
        return remote(gain_all.at[z], gain_all.at[z], gz_send.at[d], gz_recv.at[d], c, lax.rem(z + d, planes))

    for j in range(1, n):
        launch(in_plane, lambda j=j: gain_plane_copy(j))
    gain_plane[c] = gain_own[...]
    grad_far(3)
    hand_out(2)
    for j in range(1, n):
        gain_plane_copy(j).wait_recv()
    total = gain_plane[0]
    for i in range(1, n):
        total = total + gain_plane[i]
    gain_all[z] = total
    for d in range(1, planes):
        launch(along, lambda d=d: gain_copy(d))
    grad_near(4)
    hand_out(3)
    grad_far(4)
    for d in range(1, planes):
        origin = gain_all.at[lax.rem(z + planes - d, planes)]
        remote(origin, origin, gz_send.at[d], gz_recv.at[d], c, z).wait_recv()
    total = gain_all[0]
    for i in range(1, planes):
        total = total + gain_all[i]
    gains_ref[...] = total

    for m in range(4):
        hand_receive(m)
    drain(in_plane)
    hand_out(4)
    drain(along)
    hand_receive(4)
    drain(in_plane)


def finish_kernel(
    n, head, out_in, dx_in, gains_in, got_a, got_b, got_c, got_out, got_qkv,
    out_ref, dx_ref, ag_ref, q_ref, k_ref, v_ref, qg_ref, kg_ref, o_ref, fg_ref, g_ref, u_ref, d_ref,
):
    out_ref[...] = out_in[...]
    dx_ref[...] = dx_in[...]
    ag_ref[...] = gains_in[0:1, :]
    fg_ref[...] = gains_in[1:2, :]
    qg_ref[...] = gains_in[2:3, 0:head]
    kg_ref[...] = gains_in[3:4, 0:head]
    qw, kw = q_ref.shape[1] // n, k_ref.shape[1] // n
    pw = got_a.shape[2] // 3
    thirds = (got_a, got_b, got_c)
    for i in range(n):
        q_ref[:, i * qw:(i + 1) * qw] = got_qkv[i, :, 0:qw].astype(f32)
        k_ref[:, i * kw:(i + 1) * kw] = got_qkv[i, :, qw:qw + kw].astype(f32)
        v_ref[:, i * kw:(i + 1) * kw] = got_qkv[i, :, qw + kw:].astype(f32)
        o_ref[:, i * qw:(i + 1) * qw] = got_out[i].astype(f32)
        for t, got in enumerate(thirds):
            at = (i * len(thirds) + t) * pw
            g_ref[:, at:at + pw] = got[i, :, 0:pw].astype(f32)
            u_ref[:, at:at + pw] = got[i, :, pw:2 * pw].astype(f32)
            d_ref[:, at:at + pw] = got[i, :, 2 * pw:].astype(f32)


def plane_device(
    layer_input,
    token_positions,
    attention_gain,
    query_weight,
    key_matrix,
    value_matrix,
    query_gain,
    key_norm_gain,
    output_weight,
    feedforward_gain,
    gate_weight,
    up_weight,
    down_weight,
    out_cotangent,
):
    n = lax.axis_size("ctx")
    planes = lax.axis_size("fsdp")
    block, width = layer_input.shape[1:]
    length = token_positions.shape[1]
    head = query_gain.shape[0]
    qw = query_weight.shape[1] // n
    kw = key_matrix.shape[1] // n
    fw = gate_weight.shape[1] // n
    group = qw // head
    per = block // planes
    half = head // 2
    inverse = np.power(rope_base, -np.arange(half) * 2.0 / head).astype(np.float32)
    inverse = np.concatenate([inverse, inverse])[None]
    steps = np.arange(block // 2)[:, None] * inverse.astype(np.float64)
    step_cos, step_sin = (jnp.asarray(f(steps).astype(np.float32)) for f in (np.cos, np.sin))
    inverse = jnp.asarray(inverse)
    vmem = pl.BlockSpec(memory_space=pltpu.VMEM)
    hbm = pl.BlockSpec(memory_space=pl.ANY)
    dma = pltpu.SemaphoreType.DMA
    sizes = (fw, fw, fw, qw, qw + 2 * kw)
    low = lambda *shape: pltpu.VMEM(shape, bf16)
    wide = lambda *shape: pltpu.VMEM(shape, f32)
    scratch = [
        low(width, qw + 2 * kw), low(width, 2 * fw), low(qw, width), low(fw, width),
        low(planes * (output_weight.shape[0] // n), width), low(3, planes * 32, width),
        low(length, width), low(length, width), low(length, width),
        low(width, length), low(width, length), low(width, length),
        wide(length, head), wide(length, head), wide(length, head),
        wide(length, qw + kw), low(length, qw), low(length, kw), low(length, kw),
        low(kw, length), low(kw, length), low(n // 2, length, 2 * group * block), wide(n // 2, 1, 2 * group * block),
        wide(n // 2, head, 2 * group * block), low(length, qw),
        low(length, fw), low(length, 2 * fw), low(length, qw + 2 * kw),
        wide(length, kw), wide(length, kw),
    ]
    scratch += [low(planes, n, per, size) for size in sizes]
    scratch += [low(planes + 1, n, per, size) for size in sizes]
    scratch += [low(2, 4, block, width) for _ in range(4)] + [wide(2, block, width), wide(2, block, width)]
    scratch += [
        wide(block, width), wide(block, width), wide(8, width), wide(n, 8, width), wide(planes, 8, width),
        dma((13,)), dma((8, 6)), dma((8, planes)), dma((4, 7)), dma((4, 4)),
        dma((4, n)), dma((4, n)), dma((4, 4)), dma((4, 4)), dma((4, 4)), dma((4, 4)),
        dma((5, planes)), dma((5, planes + 1)), dma((5, n)), dma((5, n)), dma((n,)), dma((n,)),
        dma((planes,)), dma((planes,)),
    ]
    shapes = [
        jax.ShapeDtypeStruct((block, width), bf16),
        jax.ShapeDtypeStruct((block, width), f32),
        jax.ShapeDtypeStruct((8, width), f32),
    ] + [jax.ShapeDtypeStruct((n, per, size), bf16) for size in sizes]
    results = pl.pallas_call(
        functools.partial(layer_kernel, n, planes, block, head, group, fw),
        out_shape=shapes,
        in_specs=[vmem] * 10 + [hbm] * 7,
        out_specs=[vmem] * len(shapes),
        scratch_shapes=scratch,
        compiler_params=pltpu.CompilerParams(
            collective_id=0, has_side_effects=True, vmem_limit_bytes=60 * 1024 * 1024),
    )(
        layer_input[0], out_cotangent[0], token_positions, inverse, step_cos, step_sin,
        attention_gain[None], feedforward_gain[None], query_gain[None], key_norm_gain[None],
        query_weight, key_matrix, value_matrix, output_weight, gate_weight, up_weight, down_weight,
    )
    plain = lambda rows, columns, kind=f32: jax.ShapeDtypeStruct((rows, columns), kind)
    finals = [
        plain(block, width, bf16), plain(block, width), plain(1, width),
        plain(per, n * qw), plain(per, n * kw), plain(per, n * kw), plain(1, head), plain(1, head),
        plain(per, n * qw), plain(1, width), plain(per, n * fw), plain(per, n * fw), plain(per, n * fw),
    ]
    done = pl.pallas_call(
        functools.partial(finish_kernel, n, head),
        out_shape=finals,
        in_specs=[vmem] * len(shapes),
        out_specs=[vmem] * len(finals),
    )(*results)
    out, dx, ag, q, k, v, qg, kg, o, fg, g, u, d = done
    return out[None], dx[None], ag[0], q, k, v, qg[0], kg[0], o.T, fg[0], g, u, d.T


def solution(mesh):
    in_specs = (
        P("fsdp", "ctx", None),
        P("fsdp", None),
        P(),
        P("fsdp", None),
        P("fsdp", None),
        P("fsdp", None),
        P(),
        P(),
        P("fsdp", None),
        P(),
        P("fsdp", None),
        P("fsdp", None),
        P("fsdp", None),
        P("fsdp", "ctx", None),
    )
    out_specs = (
        P("fsdp", "ctx", None),
        P("fsdp", "ctx", None),
        P(),
        P(("ctx", "fsdp"), None),
        P(("ctx", "fsdp"), None),
        P(("ctx", "fsdp"), None),
        P(),
        P(),
        P(None, ("ctx", "fsdp")),
        P(),
        P(("ctx", "fsdp"), None),
        P(("ctx", "fsdp"), None),
        P(None, ("ctx", "fsdp")),
    )

    def run(*arguments):
        n, planes = mesh.shape["ctx"], mesh.shape["fsdp"]
        key_heads = arguments[4].shape[1] // arguments[6].shape[0]
        whole_heads = n == 8 and planes == 4 and key_heads == n
        return jax.shard_map(
            plane_device if whole_heads else on_device,
            mesh=mesh, in_specs=in_specs, out_specs=out_specs, check_vma=False,
        )(*arguments)

    return run
```

```python
import functools

import jax
import jax.numpy as jnp
import numpy as np
from jax import lax
from jax.experimental import pallas as pl
from jax.experimental.pallas import tpu as pltpu
from jax.sharding import PartitionSpec as P

epsilon = 1e-06
rope_base = 1000000.0
masked_score = -1e30


def from_behind(block, axis, distance):
    devices = range(lax.axis_size(axis))
    route = [((i - distance) % len(devices), i) for i in devices]
    return lax.ppermute(block, axis, route)


def rotate(value_rows):
    half = value_rows.shape[-1] // 2
    return jnp.concatenate([-value_rows[..., half:], value_rows[..., :half]], -1)


def rotate_back(value_rows):
    half = value_rows.shape[-1] // 2
    return jnp.concatenate([value_rows[..., half:], -value_rows[..., :half]], -1)


def rope_tables(token_offsets, head_size):
    half = head_size // 2
    inverse = rope_base ** (-(jnp.arange(half).astype(jnp.float32) * 2.0) / head_size)
    angles = token_offsets.astype(jnp.float32)[:, None] * inverse[None, :]
    cosine = jnp.cos(angles)
    sine = jnp.sin(angles)
    return (jnp.concatenate([cosine, cosine], -1), jnp.concatenate([sine, sine], -1))


def norm_scale(value_rows):
    return lax.rsqrt(jnp.mean(value_rows * value_rows, -1, keepdims=True) + epsilon)


def norm_back(value_rows, scale, gain, grad):
    weighted = grad * gain
    inner = jnp.mean(weighted * value_rows, -1, keepdims=True)
    result = scale * weighted - value_rows * scale * scale * scale * inner
    gain_part = jnp.sum((grad * value_rows * scale).reshape(-1, gain.shape[0]), 0)
    return (result, gain_part)


def row_products(left, pieces):
    return tuple((jnp.dot(left, piece, preferred_element_type=jnp.float32) for piece in pieces))


def column_products(rights, pieces):
    total = jnp.einsum("tc,rc->tr", rights[0], pieces[0], preferred_element_type=jnp.float32)
    for right, piece in zip(rights[1:], pieces[1:]):
        total = total + jnp.einsum("tc,rc->tr", right, piece, preferred_element_type=jnp.float32)
    return total


def on_device(
    layer_input,
    token_positions,
    attention_gain,
    query_weight,
    key_matrix,
    value_matrix,
    query_gain,
    key_norm_gain,
    output_weight,
    feedforward_gain,
    gate_weight,
    up_weight,
    down_weight,
    out_cotangent,
):
    hidden_in = layer_input[0].astype(jnp.float32)
    count = hidden_in.shape[0]
    head_size = query_gain.shape[0]
    query_width = query_weight.shape[1]
    key_width = key_matrix.shape[1]
    inner_width = gate_weight.shape[1]
    heads = query_width // head_size
    key_heads = key_width // head_size
    group = heads // key_heads
    scale = head_size ** (-0.5)
    cycles = lax.axis_size("ctx")
    own_index = lax.axis_index("ctx")
    sequence_pos = token_positions[0]
    token_offsets = lax.dynamic_slice_in_dim(sequence_pos, own_index * count, count)
    cosine, sine = rope_tables(token_offsets, head_size)
    cosine = cosine[:, None, :]
    sine = sine[:, None, :]
    first_scale = norm_scale(hidden_in)
    first = (hidden_in * first_scale * attention_gain).astype(jnp.bfloat16)
    query_raw, key_unnormed, value_unnormed = row_products(
        first,
        (
            lax.all_gather(query_weight, "fsdp", axis=0, tiled=True),
            lax.all_gather(key_matrix, "fsdp", axis=0, tiled=True),
            lax.all_gather(value_matrix, "fsdp", axis=0, tiled=True),
        ),
    )
    query_heads = query_raw.reshape(count, heads, head_size)
    query_scale = norm_scale(query_heads)
    query_normed = query_heads * query_scale * query_gain
    query_rot = query_normed * cosine + rotate(query_normed) * sine
    query_grouped = (
        query_rot.reshape(count, key_heads, group, head_size)
        .transpose(1, 2, 0, 3)
        .astype(jnp.bfloat16)
    )
    key_heads_raw = key_unnormed.reshape(count, key_heads, head_size)
    key_scale = norm_scale(key_heads_raw)
    key_normed = key_heads_raw * key_scale * key_norm_gain
    key_low = (
        (key_normed * cosine + rotate(key_normed) * sine)
        .reshape(count, key_width)
        .astype(jnp.bfloat16)
    )
    value_low = value_unnormed.astype(jnp.bfloat16)
    rowmax = jnp.full((key_heads, group, count), masked_score, jnp.float32)
    keys_piece = lax.all_gather(key_low, "ctx", axis=0, tiled=True).reshape(
        -1, key_heads, head_size
    )
    values_piece = lax.all_gather(value_low, "ctx", axis=0, tiled=True).reshape(
        -1, key_heads, head_size
    )
    key_pos = sequence_pos
    allowed = token_offsets[:, None] >= key_pos[None, :]
    scores = (
        jnp.einsum("kgtd,skd->kgts", query_grouped, keys_piece, preferred_element_type=jnp.float32)
        * scale
    )
    scores = jnp.where(allowed, scores, masked_score)
    newmax = jnp.maximum(rowmax, jnp.max(scores, -1))
    weights = jnp.where(allowed, jnp.exp(scores - newmax[..., None]), 0.0)
    accum = jnp.einsum(
        "kgts,skd->kgtd",
        weights.astype(jnp.bfloat16),
        values_piece,
        preferred_element_type=jnp.float32,
    )
    rowsum = jnp.sum(weights, -1)
    accum, rowmax, rowsum = (accum, newmax, rowsum)
    normalized = accum / rowsum[..., None]
    logsum = rowmax + jnp.log(rowsum)
    attention_low = (
        normalized.transpose(2, 0, 1, 3).reshape(count, query_width).astype(jnp.bfloat16)
    )
    output_whole = lax.all_gather(output_weight, "fsdp", axis=0, tiled=True)
    branch_out = jnp.dot(attention_low, output_whole, preferred_element_type=jnp.float32)
    middle = hidden_in + branch_out
    second_scale = norm_scale(middle)
    second = (middle * second_scale * feedforward_gain).astype(jnp.bfloat16)
    gate, up = row_products(
        second,
        (
            lax.all_gather(gate_weight, "fsdp", axis=0, tiled=True),
            lax.all_gather(up_weight, "fsdp", axis=0, tiled=True),
        ),
    )
    sigmoid_gate = jax.nn.sigmoid(gate)
    silu_gate = gate * sigmoid_gate
    hidden_low = (silu_gate * up).astype(jnp.bfloat16)
    (down_out,) = row_products(
        hidden_low, (lax.all_gather(down_weight, "fsdp", axis=0, tiled=True),)
    )
    layer_output = (middle + down_out).astype(jnp.bfloat16)[None]
    cotangent = out_cotangent[0]
    hidden_grad = column_products(
        (cotangent,), lax.all_gather((down_weight,), "fsdp", axis=0, tiled=True)
    )
    up_low = (hidden_grad * silu_gate).astype(jnp.bfloat16)
    gate_low = (hidden_grad * up * sigmoid_gate * (1.0 + gate * (1.0 - sigmoid_gate))).astype(
        jnp.bfloat16
    )
    second_grad = column_products(
        (gate_low, up_low), lax.all_gather((gate_weight, up_weight), "fsdp", axis=0, tiled=True)
    )
    middle_part, feedforward_part = norm_back(middle, second_scale, feedforward_gain, second_grad)
    middle_grad = cotangent.astype(jnp.float32) + middle_part
    middle_low = middle_grad.astype(jnp.bfloat16)
    attention_grad = jnp.einsum(
        "tc,rc->tr", middle_low, output_whole, preferred_element_type=jnp.float32
    )
    attention_grad_low = attention_grad.astype(jnp.bfloat16)
    mixed_grad = attention_grad_low.reshape(count, key_heads, group, head_size).transpose(
        1, 2, 0, 3
    )
    delta = jnp.sum(mixed_grad.astype(jnp.float32) * normalized, -1)

    def cycle_step(index, carry):
        keys_held, values_held, key_acc, value_acc, query_acc = carry
        anchor = (own_index - index) % cycles
        key_pos = lax.dynamic_slice_in_dim(sequence_pos, anchor * count, count)
        keys_piece = keys_held.astype(jnp.bfloat16).reshape(count, key_heads, head_size)
        values_piece = values_held.astype(jnp.bfloat16).reshape(count, key_heads, head_size)
        allowed = token_offsets[:, None] >= key_pos[None, :]
        scores = (
            jnp.einsum(
                "kgtd,skd->kgts", query_grouped, keys_piece, preferred_element_type=jnp.float32
            )
            * scale
        )
        probs = jnp.where(allowed, jnp.exp(scores - logsum[..., None]), 0.0)
        value_acc = value_acc + jnp.einsum(
            "kgts,kgtd->skd",
            probs.astype(jnp.bfloat16),
            mixed_grad,
            preferred_element_type=jnp.float32,
        ).reshape(count, key_width)
        prob_grad = jnp.einsum(
            "kgtd,skd->kgts", mixed_grad, values_piece, preferred_element_type=jnp.float32
        )
        score_grad = (probs * (prob_grad - delta[..., None])).astype(jnp.bfloat16)
        query_acc = (
            query_acc
            + jnp.einsum(
                "kgts,skd->kgtd", score_grad, keys_piece, preferred_element_type=jnp.float32
            )
            * scale
        )
        key_acc = (
            key_acc
            + jnp.einsum(
                "kgts,kgtd->skd", score_grad, query_grouped, preferred_element_type=jnp.float32
            ).reshape(count, key_width)
            * scale
        )
        moved = (
            from_behind(keys_held.astype(jnp.bfloat16), "ctx", 1).astype(keys_held.dtype),
            from_behind(values_held.astype(jnp.bfloat16), "ctx", 1).astype(values_held.dtype),
            from_behind(key_acc.astype(jnp.bfloat16), "ctx", 1).astype(key_acc.dtype),
            from_behind(value_acc.astype(jnp.bfloat16), "ctx", 1).astype(value_acc.dtype),
        )
        return (moved[0], moved[1], moved[2], moved[3], query_acc)

    start_cycle = (
        key_low.astype(jnp.float32),
        value_low.astype(jnp.float32),
        jnp.zeros((count, key_width), jnp.float32),
        jnp.zeros((count, key_width), jnp.float32),
        jnp.zeros((key_heads, group, count, head_size), jnp.float32),
    )
    cycle_done = lax.fori_loop(0, cycles, cycle_step, start_cycle)
    key_acc = cycle_done[2]
    value_acc = cycle_done[3]
    query_acc = cycle_done[4]
    query_rot_grad = query_acc.transpose(2, 0, 1, 3).reshape(count, heads, head_size)
    query_normed_grad = query_rot_grad * cosine + rotate_back(query_rot_grad * sine)
    query_heads_grad, query_part = norm_back(
        query_heads, query_scale, query_gain, query_normed_grad
    )
    query_low_grad = query_heads_grad.reshape(count, query_width).astype(jnp.bfloat16)
    key_rot_grad = key_acc.reshape(count, key_heads, head_size)
    key_normed_grad = key_rot_grad * cosine + rotate_back(key_rot_grad * sine)
    key_heads_grad, key_part = norm_back(key_heads_raw, key_scale, key_norm_gain, key_normed_grad)
    key_low_grad = key_heads_grad.reshape(count, key_width).astype(jnp.bfloat16)
    value_low_grad = value_acc.astype(jnp.bfloat16)
    first_grad = column_products(
        (query_low_grad, key_low_grad, value_low_grad),
        lax.all_gather((query_weight, key_matrix, value_matrix), "fsdp", axis=0, tiled=True),
    )
    input_part, attention_part = norm_back(hidden_in, first_scale, attention_gain, first_grad)
    input_gradient = (middle_grad + input_part)[None]
    rights_first = jnp.concatenate([query_low_grad, key_low_grad, value_low_grad], 1)
    rights_second = jnp.concatenate([gate_low, up_low], 1)
    pairs = (
        (first, rights_first),
        (second, rights_second),
        (middle_low, attention_low),
        (cotangent, hidden_low),
    )
    parts = []
    for left, right in pairs:
        parts.append(jnp.einsum("tr,tc->rc", left, right, preferred_element_type=jnp.float32))
    sums = lax.psum_scatter(
        jnp.concatenate(parts, 1), ("ctx", "fsdp"), scatter_dimension=0, tiled=True
    )
    edges = [0, query_width, query_width + key_width, query_width + 2 * key_width]
    edges = edges + [edges[3] + inner_width, edges[3] + 2 * inner_width]
    edges = edges + [edges[5] + query_width, edges[5] + query_width + inner_width]
    query_gradient = sums[:, edges[0] : edges[1]]
    key_gradient = sums[:, edges[1] : edges[2]]
    value_gradient = sums[:, edges[2] : edges[3]]
    gate_gradient = sums[:, edges[3] : edges[4]]
    up_gradient = sums[:, edges[4] : edges[5]]
    output_gradient = sums[:, edges[5] : edges[6]].T
    down_gradient = sums[:, edges[6] : edges[7]].T
    attention_total, query_total, key_total, feedforward_total = lax.psum(
        (attention_part, query_part, key_part, feedforward_part), ("ctx", "fsdp")
    )
    return (
        layer_output,
        input_gradient,
        attention_total,
        query_gradient,
        key_gradient,
        value_gradient,
        query_total,
        key_total,
        output_gradient,
        feedforward_total,
        gate_gradient,
        up_gradient,
        down_gradient,
    )


MESH = pl.DeviceIdType.MESH
f32 = jnp.float32
bf16 = jnp.bfloat16


def dot(left, right):
    return jnp.dot(left, right, preferred_element_type=f32)


def dot_nt(left, right):
    return lax.dot_general(left, right, (((1,), (1,)), ((), ())), preferred_element_type=f32)


def dot_tn(left, right):
    return lax.dot_general(left, right, (((0,), (0,)), ((), ())), preferred_element_type=f32)


def layer_kernel(
    n, planes, block, head, group, fw,
    x_ref, dy_ref, pos_row, inverse_ref, step_cos, step_sin, ag_ref, fg_ref, qg_ref, kg_ref,
    wq, wk, wv, wo, wg, wu, wd,
    out_ref, dx_ref, gains_ref, got_a, got_b, got_c, got_out, got_qkv,
    w_qkv, w_gu, w_out, w_down, t_out, t_down,
    first, dy_all, second, first_t, dy_t, second_t,
    positions, cosine, sine,
    raw, queries, keys, values, keys_t, values_t, probs, sums, mixed_t, mixed_low,
    hidden, d_gu, d_qkv, dk_acc, dv_acc,
    stage_a, stage_b, stage_c, stage_out, stage_qkv,
    land_a, land_b, land_c, land_out, land_qkv,
    rs_sa, rs_ra, rs_sb, rs_rb, rs_kept, rs_acc,
    middle, d_middle, gain_own, gain_plane, gain_all,
    local_sem, wz_send, wz_recv, hand_send, hand_recv,
    ag_send, ag_recv, ra_send, ra_recv, rb_send, rb_recv,
    zr_send, zr_recv, aa_send, aa_recv, gp_send, gp_recv, gz_send, gz_recv,
):
    c = lax.axis_index("ctx")
    z = lax.axis_index("fsdp")
    dmid = first
    dmid_t = second
    cy, cx, ck = lax.div(c, 4), lax.rem(lax.div(c, 2), 2), lax.rem(c, 2)
    ci = lax.rem(c, 4)
    sign = 1 - 2 * ck
    qw, kw = group * head, head
    pw = 128
    thirds = fw // pw
    piece = pw // 4
    width = x_ref.shape[1]
    scale = head ** (-0.5)
    log2e = 1.4426950408889634
    gots = (got_a, got_b, got_c, got_out, got_qkv)
    stages = (stage_a, stage_b, stage_c, stage_out, stage_qkv)
    lands = (land_a, land_b, land_c, land_out, land_qkv)

    def partner(j):
        y = lax.rem(cy + lax.div(j, 4), 2)
        x = lax.rem(cx + lax.rem(lax.div(j, 2), 2), 2)
        k = lax.rem(ck + lax.rem(j, 2), 2)
        return y * 4 + x * 2 + k

    def chip(slot):
        return lax.rem(cy + lax.div(slot, 2), 2) * 2 + lax.rem(cx + lax.rem(slot, 2), 2)

    def rows(start, size):
        return pl.ds(pl.multiple_of(start * size, size), size)

    def remote(src, dst, send, recv, ctx, plane):
        return pltpu.make_async_remote_copy(
            src_ref=src, dst_ref=dst, send_sem=send, recv_sem=recv,
            device_id={"ctx": ctx, "fsdp": plane}, device_id_type=MESH,
        )

    in_plane, along, weight_sends = [], [], []

    def launch(started, copy, when=None):
        if when is None:
            copy().start()
        else:
            pl.when(when)(lambda: copy().start())
        started.append((copy, when))

    def drain(started):
        for copy, when in started:
            if when is None:
                copy().wait_send()
            else:
                pl.when(when)(lambda copy=copy: copy().wait_send())
        started.clear()

    own_rows = wq.shape[0]
    out_rows = wo.shape[0] // n

    def own_slices():
        mine = rows(z, own_rows)
        pairs = [
            (wq.at[:, rows(c, qw)], w_qkv.at[mine, 0:qw]),
            (wk.at[:, rows(c, kw)], w_qkv.at[mine, qw:qw + kw]),
            (wv.at[:, rows(c, kw)], w_qkv.at[mine, qw + kw:qw + 2 * kw]),
            (wo.at[rows(c, out_rows)], t_out.at[rows(z, out_rows)]),
        ]
        for t in range(thirds):
            at = 2 * pw * t
            pairs.append((wg.at[:, rows(c * thirds + t, pw)], w_gu.at[mine, at:at + pw]))
            pairs.append((wu.at[:, rows(c * thirds + t, pw)], w_gu.at[mine, at + pw:at + 2 * pw]))
            pairs.append((wd.at[rows((cy * thirds + t) * 4 + ci, piece)], t_down.at[t, rows(z, piece)]))
        return pairs

    local = [pltpu.make_async_copy(src, dst, local_sem.at[i]) for i, (src, dst) in enumerate(own_slices())]
    for copy in local:
        copy.start()

    for land in lands:
        @pl.when(z == 0)
        def _(land=land):
            land[0] = jnp.zeros(land.shape[1:], bf16)

        @pl.when(z == planes - 1)
        def _(land=land):
            land[planes] = jnp.zeros(land.shape[1:], bf16)

    barrier = pltpu.get_barrier_semaphore()
    for j in range(1, n):
        pl.semaphore_signal(barrier, inc=1, device_id={"ctx": partner(j), "fsdp": z}, device_id_type=MESH)
    for d in range(1, planes):
        pl.semaphore_signal(
            barrier, inc=1, device_id={"ctx": c, "fsdp": lax.rem(z + d, planes)}, device_id_type=MESH)
    x = x_ref[...].astype(f32)
    x_scale = lax.rsqrt(jnp.mean(x * x, -1, keepdims=True) + epsilon)
    first[rows(c, block)] = (x * x_scale * ag_ref[...]).astype(bf16)
    dy_all[rows(c, block)] = dy_ref[...]
    for copy in local[:3]:
        copy.wait()
    pl.semaphore_wait(barrier, n + planes - 2)

    def inside(t):
        return jnp.logical_and(t >= 0, t < planes)

    weights = [
        (lambda o: w_qkv.at[rows(o, own_rows)], None),
        (lambda o: t_out.at[rows(o, out_rows)], 0),
    ]
    for t in range(thirds):
        weights.append((lambda o, t=t: w_gu.at[rows(o, own_rows), 2 * pw * t:2 * pw * (t + 1)], None))
        weights.append((lambda o, t=t: t_down.at[t, rows(o, piece)], 1 + t))

    def weight_copy(w, slot, origin, target):
        part = weights[w][0](origin)
        return remote(part, part, wz_send.at[w, slot], wz_recv.at[w, origin], c, target)

    def hand_split(origin, valid):
        mine = 2 * origin + cy == c
        return jnp.logical_and(valid, jnp.logical_not(mine)), jnp.logical_and(valid, mine)

    def weight_start(w):
        for side in range(2):
            d = sign * (1 - 2 * side)
            launch(weight_sends, lambda side=side, d=d: weight_copy(w, side, z, z + d), inside(z + d))
        if weights[w][1] is not None:
            hand_over(w, z, 0, *hand_split(z, True))

    def hand_target(h):
        if h == 0:
            return lambda i: w_out.at[rows(i, out_rows)]
        return lambda i: w_down.at[rows((h - 1) * 4 + i, piece)]

    def hand_copy(w, origin, slot):
        h = weights[w][1]
        return remote(
            weights[w][0](origin), hand_target(h)(ci), hand_send.at[h, slot], hand_recv.at[h, ci], 2 * origin + cy, z)

    def hand_over(w, origin, slot, away, here):
        launch(in_plane, lambda: hand_copy(w, origin, slot), away)

        @pl.when(here)
        def _():
            hand_target(weights[w][1])(ci)[...] = weights[w][0](origin)[...]

    def hand_arrive(w):
        h = weights[w][1]
        for i in range(4):
            @pl.when(4 * ck + i != c)
            def _(i=i):
                part = hand_target(h)(i)
                remote(part, part, hand_send.at[h, 0], hand_recv.at[h, i], c, z).wait_recv()

    hops = {}
    for d in range(1, planes):
        for side, way in enumerate((1, -1)):
            origin = z - way * d
            valid = inside(origin)
            passed = jnp.logical_and(valid, inside(z + way))
            hops[d, side] = origin, z + way, valid, passed, hand_split(origin, valid)

    def weight_hop(w, d):
        for side in range(2):
            origin, following, valid, passed, split = hops[d, side]
            pl.when(valid)(lambda: weight_copy(w, 0, origin, z).wait_recv())
            if d < planes - 1:
                launch(
                    weight_sends,
                    lambda side=side, origin=origin, following=following: weight_copy(
                        w, 2 * d + side, origin, following),
                    passed)
            if weights[w][1] is not None:
                hand_over(w, origin, 2 * d - 1 + side, *split)

    def gather_copy(buf, g, j, send, origin, target):
        part = buf.at[rows(origin, block)]
        return remote(part, part, ag_send.at[g, send], ag_recv.at[g, j], target, z)

    def gather_start(buf, g):
        for j in (1, 2 + 2 * ck, 4 - 2 * ck):
            launch(in_plane, lambda j=j: gather_copy(buf, g, j, j, c, partner(j)))

    def gather_half(buf, g, j):
        half = block // 2
        part = buf.at[pl.ds(pl.multiple_of(partner(j) * block + (half if j == 2 else 0), half), half)]
        at = 0 if j == 2 else 6
        return remote(part, part, ag_send.at[g, at], ag_recv.at[g, at], partner(6 - j), z)

    def gather_diagonal(buf, g):
        half = block // 2
        for at in (6, 0):
            part = buf.at[pl.ds(pl.multiple_of(partner(6) * block + (0 if at == 6 else half), half), half)]
            remote(part, part, ag_send.at[g, at], ag_recv.at[g, at], c, z).wait_recv()

    def gather_forward(buf, g, j):
        return gather_copy(buf, g, j + 1, j + 1, partner(j), partner(1))

    def gather_take(buf, g, j):
        if j == 6:
            gather_diagonal(buf, g)
        else:
            gather_copy(buf, g, j, j, partner(j), c).wait_recv()
            gather_half(buf, g, j).start()
        gather_forward(buf, g, j).start()

    def gather_sent(buf, g):
        for j in (2, 4, 6):
            in_plane.append((lambda j=j: gather_forward(buf, g, j), None))
            if j < 6:
                in_plane.append((lambda j=j: gather_half(buf, g, j), None))

    def gather_finish(buf, g):
        for j in (2, 4, 6):
            gather_take(buf, g, j)
        gather_sent(buf, g)
        for j in (1, 3, 5, 7):
            gather_copy(buf, g, j, j, partner(j), c).wait_recv()

    def gather_step(buf, g, slot):
        @pl.when(slot == 1)
        def _():
            gather_take(buf, g, 2)
            gather_take(buf, g, 4)

        pl.when(slot == 3)(lambda: gather_take(buf, g, 6))
        gather_copy(buf, g, 2 * slot + 1, 0, partner(2 * slot + 1), c).wait_recv()

    def sum_pair_copy(s, slot):
        return remote(rs_sa.at[s % 2, slot], rs_ra.at[s % 2, slot], ra_send.at[s, slot], ra_recv.at[s, slot], partner(1), z)

    def sum_chip_copy(s, slot):
        return remote(
            rs_sb.at[s % 2, slot], rs_rb.at[s % 2, slot], rb_send.at[s, slot], rb_recv.at[s, slot], partner(2 * slot), z)

    def sum_half_copy(s, slot):
        half = block // 2
        at = pl.ds(pl.multiple_of((slot - 1) * half, half), half)
        return remote(
            rs_sb.at[s % 2, 3, at], rs_rb.at[s % 2, 3, at], rb_send.at[s, 6 - 3 * slot], rb_recv.at[s, 6 - 3 * slot],
            partner(6 - 2 * slot), z)

    def sum_slot(p):
        return jnp.where(p == 0, 3, jnp.where(p == 1, 2 - ck, jnp.where(p == 2, 1 + ck, 0)))

    def sum_start(s, left, partial, prepare=None, ready=None, during=()):
        if prepare is not None:
            prepare(chip(sum_slot(0)))
        if ready is not None:
            ready()

        def body(p, carry):
            slot = sum_slot(p)
            at = [rows(partner(2 * slot + 1), block), rows(partner(2 * slot), block)]
            both = partial(jnp.concatenate([left[i] for i in at], 0))
            rs_sa[s % 2, slot] = both[:block].astype(bf16)
            sum_pair_copy(s, slot).start()
            rs_kept[lax.rem(p, 2)] = both[block:]

            @pl.when(p > 0)
            def _():
                before = sum_slot(p - 1)
                sum_pair_copy(s, before).wait_recv()
                rs_sb[s % 2, before] = (
                    rs_kept[lax.rem(p + 1, 2)] + rs_ra[s % 2, before].astype(f32)).astype(bf16)

            @pl.when(p == 1)
            def _():
                sum_half_copy(s, 1).start()
                sum_half_copy(s, 2).start()

            @pl.when(p > 1)
            def _():
                before = sum_slot(p - 1)
                half = block // 2
                at = pl.ds(pl.multiple_of((before - 1) * half, half), half)
                sum_half_copy(s, before).wait_recv()
                rs_sb[s % 2, before, at] = (
                    rs_sb[s % 2, before, at].astype(f32) + rs_rb[s % 2, 3, at].astype(f32)).astype(bf16)
                sum_chip_copy(s, before).start()

            if prepare is not None:
                @pl.when(p < 3)
                def _():
                    prepare(chip(sum_slot(p + 1)))

            for k, poll in enumerate(during):
                pl.when(p == k)(poll)
            return carry

        lax.fori_loop(0, 4, body, 0)
        for slot in range(4):
            in_plane.append((lambda slot=slot: sum_pair_copy(s, slot), None))
        for slot in (1, 2):
            in_plane.append((lambda slot=slot: sum_half_copy(s, slot), None))
            in_plane.append((lambda slot=slot: sum_chip_copy(s, slot), None))
        sum_pair_copy(s, 0).wait_recv()
        rs_acc[s % 2] = rs_kept[1] + rs_ra[s % 2, 0].astype(f32)

    def sum_finish(s):
        total = rs_acc[s % 2]
        for slot in (1, 2):
            sum_chip_copy(s, slot).wait_recv()
            total = total + rs_rb[s % 2, slot].astype(f32)
        return total

    per = block // planes

    def weight_grad(m, parts):
        def body(i, carry):
            at = 0
            for left, right in parts:
                value = right()
                grad = dot(left[rows(i, 4 * block)], value)
                for k in range(4):
                    for t in range(planes):
                        start = k * block + t * per
                        stages[m][t, 4 * i + k, :, at:at + value.shape[1]] = grad[start:start + per].astype(bf16)
                at += value.shape[1]
            return carry

        lax.fori_loop(0, n // 4, body, 0)
        at_edge = jnp.logical_or(z == 0, z == planes - 1)
        for k in range(planes - 1):
            t = jnp.where(z == 0, planes - 1 - k, k)
            launch(along, lambda t=t: grad_copy(m, t), at_edge)

    def grad_copy(m, t):
        way = jnp.where(z < t, 1, -1)
        last = z + way == t
        slot = jnp.where(jnp.logical_and(last, way < 0), planes, t)
        return remote(
            stages[m].at[t], lands[m].at[slot], zr_send.at[m, t], zr_recv.at[m, slot], c, z + way)

    def grad_arrive(m, slot):
        part = lands[m].at[slot]
        remote(part, part, zr_send.at[m, 0], zr_recv.at[m, slot], c, z).wait_recv()

    def grad_pass(m, t, valid):
        @pl.when(valid)
        def _():
            grad_arrive(m, t)

            def body(i, carry):
                stages[m][t, i] = (stages[m][t, i].astype(f32) + lands[m][t, i].astype(f32)).astype(bf16)
                return carry

            lax.fori_loop(0, n, body, 0)

        launch(along, lambda: grad_copy(m, t), valid)

    is_low, is_high = z == 1, z == planes - 2

    def grad_near_far(m):
        grad_pass(m, 3, is_low)
        grad_pass(m, 0, is_high)

    def grad_near_inner(m):
        grad_pass(m, 2, is_low)
        grad_pass(m, 1, is_high)

    def grad_near(m):
        grad_near_far(m)
        grad_near_inner(m)

    def grad_far(m):
        grad_pass(m, 3, is_high)
        grad_pass(m, 0, is_low)

    def owner_copy(m, j):
        return remote(lands[m].at[z, partner(j)], gots[m].at[c], aa_send.at[m, j], aa_recv.at[m, j], partner(j), z)

    def hand_out(m):
        pl.when(z > 0)(lambda: grad_arrive(m, z))
        pl.when(z < planes - 1)(lambda: grad_arrive(m, planes))

        def body(i, carry):
            total = stages[m][z, i].astype(f32) + lands[m][z, i].astype(f32) + lands[m][planes, i].astype(f32)
            lands[m][z, i] = total.astype(bf16)
            return carry

        lax.fori_loop(0, n, body, 0)
        for j in (2 + 2 * ck, 3 + 2 * ck, 4 - 2 * ck, 5 - 2 * ck, 6, 7, 1):
            launch(in_plane, lambda j=j: owner_copy(m, j))
        gots[m][c] = lands[m][z, c]

    def hand_receive(m):
        for j in range(1, n):
            owner_copy(m, j).wait_recv()

    weight_start(0)
    gather_start(first, 0)
    for copy in local[3:]:
        copy.wait()

    spread = jnp.broadcast_to(pos_row[...].astype(f32), (head, pos_row.shape[1]))
    positions[...] = spread.T
    side = jnp.where(lax.broadcasted_iota(jnp.int32, (1, head), 1) < head // 2, -1.0, 1.0)

    def table(i, carry):
        run = step_cos.shape[0]
        at = rows(i, run)
        start = positions[pl.ds(pl.multiple_of(i * run, run), 1)] * inverse_ref[...]
        start_cos, start_sin = jnp.cos(start), jnp.sin(start)
        cosine[at] = start_cos * step_cos[...] - start_sin * step_sin[...]
        sine[at] = (start_sin * step_cos[...] + start_cos * step_sin[...]) * side
        return carry

    def turn_over(src, dst):
        def body(i, carry):
            at = rows(i, block)
            dst[:, at] = src[at].T
            return carry

        lax.fori_loop(0, n, body, 0)

    lax.fori_loop(0, 2 * n, table, 0)
    weight_hop(0, 1)
    gather_finish(first, 0)
    weight_hop(0, 2)
    weight_start(1)
    gather_start(dy_all, 1)
    turn_over(first, first_t)
    weight_hop(0, 3)
    weight_start(2)
    weight_start(3)

    def turn(value, at):
        return value * cosine[at] + pltpu.roll(value, head // 2, 1) * sine[at]

    def turn_back(grad, at):
        return grad * cosine[at] - pltpu.roll(grad, head // 2, 1) * sine[at]

    def project(i, carry):
        at = rows(i, 2 * block)
        result = dot(first[at], w_qkv[...])
        raw[at] = result[:, :qw + kw]
        low_values = result[:, qw + kw:].astype(bf16)
        values[at] = low_values
        values_t[:, at] = low_values.T
        for h in range(group + 1):
            part = result[:, h * head:(h + 1) * head]
            inv = lax.rsqrt(jnp.mean(part * part, -1, keepdims=True) + epsilon)
            gain = qg_ref[...] if h < group else kg_ref[...]
            turned = turn(part * inv * gain, at)
            if h < group:
                queries[at, h * head:(h + 1) * head] = (turned * (scale * log2e)).astype(bf16)
            else:
                low_keys = turned.astype(bf16)
                keys[at] = low_keys
                keys_t[:, at] = low_keys.T
        return carry

    lax.fori_loop(0, n // 4, project, 0)
    weight_hop(1, 1)
    lax.fori_loop(n // 4, n // 2, project, 0)
    weight_hop(1, 2)
    gather_finish(dy_all, 1)

    def stack(ref, at):
        return jnp.concatenate([ref[at, h * head:(h + 1) * head] for h in range(group)], 0)

    def attend(place):
        at = rows(place, 2 * block)
        scores = dot_nt(keys[...], stack(queries, at))
        allowed = positions[...] <= pos_row[:, rows(2 * place, block)].astype(f32)
        later = positions[...] <= pos_row[:, rows(2 * place + 1, block)].astype(f32)
        weight = jnp.concatenate(
            [jnp.exp2(jnp.where(later if k % 2 else allowed, scores[:, k * block:(k + 1) * block], masked_score))
             for k in range(2 * group)], 1)
        inv = 1.0 / jnp.sum(weight, 0, keepdims=True)
        low_weight = weight.astype(bf16)
        probs[place] = low_weight
        sums[place] = inv
        result = dot(values_t[...], low_weight) * inv
        mixed_t[place] = result
        for h in range(group):
            mixed_low[at, h * head:(h + 1) * head] = result[:, 2 * h * block:2 * (h + 1) * block].T.astype(bf16)

    def output_ready():
        weight_hop(1, 3)
        weight_start(4)
        weight_start(5)
        hand_arrive(1)
        drain(in_plane)

    def hop_third(t, d):
        weight_hop(2 + 2 * t, d)
        weight_hop(3 + 2 * t, d)

    sum_start(
        0, mixed_low, lambda left: dot(left, w_out[...]), attend, output_ready,
        (lambda: hop_third(0, 1), lambda: hop_third(0, 2), lambda: hop_third(1, 1)))
    weight_start(6)
    weight_start(7)
    hop_third(0, 3)
    turn_over(dy_all, dy_t)
    hop_third(1, 2)
    mid = x_ref[...].astype(f32) + sum_finish(0)
    middle[...] = mid
    mid_scale = lax.rsqrt(jnp.mean(mid * mid, -1, keepdims=True) + epsilon)
    second[rows(c, block)] = (mid * mid_scale * fg_ref[...]).astype(bf16)
    gather_start(second, 2)
    hop_third(2, 1)
    hand_arrive(3)

    def feed(t, at):
        units, pair = slice(t * pw, (t + 1) * pw), 2 * pw * t
        both = dot(second[at], w_gu[:, pair:pair + 2 * pw])
        back = dot_nt(dy_all[at], w_down[units])
        gate, up = both[:, :pw], both[:, pw:]
        sig = 1.0 / (1.0 + jnp.exp(-gate))
        silu = gate * sig
        hidden[at, units] = (silu * up).astype(bf16)
        d_gu[at, pair:pair + pw] = (back * up * sig * (1.0 + gate * (1.0 - sig))).astype(bf16)
        d_gu[at, pair + pw:pair + 2 * pw] = (back * silu).astype(bf16)

    def feed_arriving(slot, carry):
        gather_step(second, 2, slot)
        at = rows(chip(slot), 2 * block)
        feed(0, at)
        second_t[:, at] = second[at].T
        pl.when(slot == 2)(lambda: hop_third(2, 2))
        return carry

    def third_grad(t):
        weight_grad(t, [
            (second_t, lambda: d_gu[:, 2 * pw * t:2 * pw * (t + 1)]),
            (dy_t, lambda: hidden[:, t * pw:(t + 1) * pw]),
        ])

    def feed_third(t):
        def body(i, carry):
            feed(t, rows(i, 2 * block))
            return carry

        lax.fori_loop(0, n // 2, body, 0)

    lax.fori_loop(0, n // 2, feed_arriving, 0)
    gather_sent(second, 2)
    hop_third(1, 3)
    third_grad(0)
    hand_arrive(5)
    feed_third(1)
    hop_third(2, 3)
    hand_arrive(7)
    sum_start(
        1, d_gu, lambda left: dot_nt(left, w_gu[...]),
        lambda place: feed(thirds - 1, rows(place, 2 * block)))
    third_grad(1)
    third_grad(2)
    d_second = sum_finish(1)

    def norm_back(value, gain, grad):
        inv = lax.rsqrt(jnp.mean(value * value, -1, keepdims=True) + epsilon)
        weighted = grad * gain
        inner = jnp.mean(weighted * value, -1, keepdims=True)
        result = inv * weighted - value * (inv * inv * inv * inner)
        return result, jnp.sum(grad * value * inv, 0, keepdims=True)

    gain_own[...] = jnp.zeros_like(gain_own)
    part, gain_own[1:2, :] = norm_back(middle[...], fg_ref[...], d_second)
    d_mid = dy_ref[...].astype(f32) + part
    d_middle[...] = d_mid
    drain(in_plane)
    dmid[rows(c, block)] = d_mid.astype(bf16)
    gather_start(dmid, 3)
    drain(weight_sends)
    grad_near(0)

    dk_acc[...] = jnp.zeros_like(dk_acc)
    dv_acc[...] = jnp.zeros_like(dv_acc)

    def attend_back(slot, q_sum):
        gather_step(dmid, 3, slot)
        place = chip(slot)
        at = rows(place, 2 * block)
        d_mix = dot_nt(w_out[...], dmid[at])
        dmid_t[:, at] = dmid[at].T
        d_mix_t = jnp.concatenate([d_mix[h * head:(h + 1) * head] for h in range(group)], 1)
        d_mix_t = (d_mix_t.astype(bf16).astype(f32) * sums[place]).astype(bf16)
        delta = jnp.sum(d_mix_t.astype(f32) * mixed_t[place], 0, keepdims=True)
        weight = probs[place]
        d_prob = dot(values[...], d_mix_t)
        d_score = (weight.astype(f32) * (d_prob - delta)).astype(bf16)
        d_query = dot(keys_t[...], d_score) * scale
        for h in range(group):
            grad = turn_back(d_query[:, 2 * h * block:2 * (h + 1) * block].T, at)
            part, gain_part = norm_back(raw[at, h * head:(h + 1) * head], qg_ref[...], grad)
            d_qkv[at, h * head:(h + 1) * head] = part.astype(bf16)
            q_sum = q_sum + gain_part
        pl.when(slot == 2)(lambda: grad_near(1))
        dv_acc[...] += dot(weight, d_mix_t.T)
        dk_acc[...] += dot(d_score, stack(queries, at))
        return q_sum

    zero = jnp.zeros((1, head), f32)
    gain_own[2:3, 0:head] = lax.fori_loop(0, n // 2, attend_back, zero)
    gather_sent(dmid, 3)
    weight_grad(3, [(dmid_t, lambda: mixed_low[...])])
    grad_far(0)
    drain(in_plane)
    sum_start(2, hidden, lambda left: dot(left, w_down[...]))

    def project_back(i, k_sum):
        at = rows(i, 2 * block)
        grad = turn_back(dk_acc[at] * (1.0 / log2e), at)
        part, gain_part = norm_back(raw[at, qw:qw + kw], kg_ref[...], grad)
        d_qkv[at, qw:qw + kw] = part.astype(bf16)
        d_qkv[at, qw + kw:] = dv_acc[at].astype(bf16)
        return k_sum + gain_part

    gain_own[3:4, 0:head] = lax.fori_loop(0, n // 2, project_back, zero)

    weight_grad(4, [(first_t, lambda: d_qkv[...])])
    grad_far(1)
    grad_near(2)
    hand_out(0)
    sum_start(3, d_qkv, lambda left: dot_nt(left, w_qkv[...]))
    grad_far(2)
    grad_near(3)
    grad_near_far(4)
    out_ref[...] = (middle[...] + sum_finish(2)).astype(bf16)
    hand_out(1)
    grad_far(3)
    grad_near_inner(4)
    grad_far(4)
    x_part, gain_own[0:1, :] = norm_back(x_ref[...].astype(f32), ag_ref[...], sum_finish(3))
    dx_ref[...] = d_middle[...] + x_part

    def gain_plane_copy(j):
        return remote(gain_own, gain_plane.at[c], gp_send.at[j], gp_recv.at[j], partner(j), z)

    def gain_copy(d):
        return remote(gain_all.at[z], gain_all.at[z], gz_send.at[d], gz_recv.at[d], c, lax.rem(z + d, planes))

    for j in range(1, n):
        launch(in_plane, lambda j=j: gain_plane_copy(j))
    gain_plane[c] = gain_own[...]
    hand_out(2)
    for j in range(1, n):
        gain_plane_copy(j).wait_recv()
    total = gain_plane[0]
    for i in range(1, n):
        total = total + gain_plane[i]
    gain_all[z] = total
    for d in range(1, planes):
        launch(along, lambda d=d: gain_copy(d))
    hand_out(3)
    for d in range(1, planes):
        origin = gain_all.at[lax.rem(z + planes - d, planes)]
        remote(origin, origin, gz_send.at[d], gz_recv.at[d], c, z).wait_recv()
    total = gain_all[0]
    for i in range(1, planes):
        total = total + gain_all[i]
    gains_ref[...] = total

    for m in range(4):
        hand_receive(m)
    drain(in_plane)
    hand_out(4)
    drain(along)
    hand_receive(4)
    drain(in_plane)


def finish_kernel(
    n, head, out_in, dx_in, gains_in, got_a, got_b, got_c, got_out, got_qkv,
    out_ref, dx_ref, ag_ref, q_ref, k_ref, v_ref, qg_ref, kg_ref, o_ref, fg_ref, g_ref, u_ref, d_ref,
):
    out_ref[...] = out_in[...]
    dx_ref[...] = dx_in[...]
    ag_ref[...] = gains_in[0:1, :]
    fg_ref[...] = gains_in[1:2, :]
    qg_ref[...] = gains_in[2:3, 0:head]
    kg_ref[...] = gains_in[3:4, 0:head]
    qw, kw = q_ref.shape[1] // n, k_ref.shape[1] // n
    pw = got_a.shape[2] // 3
    thirds = (got_a, got_b, got_c)
    for i in range(n):
        q_ref[:, i * qw:(i + 1) * qw] = got_qkv[i, :, 0:qw].astype(f32)
        k_ref[:, i * kw:(i + 1) * kw] = got_qkv[i, :, qw:qw + kw].astype(f32)
        v_ref[:, i * kw:(i + 1) * kw] = got_qkv[i, :, qw + kw:].astype(f32)
        o_ref[:, i * qw:(i + 1) * qw] = got_out[i].astype(f32)
        for t, got in enumerate(thirds):
            at = (i * len(thirds) + t) * pw
            g_ref[:, at:at + pw] = got[i, :, 0:pw].astype(f32)
            u_ref[:, at:at + pw] = got[i, :, pw:2 * pw].astype(f32)
            d_ref[:, at:at + pw] = got[i, :, 2 * pw:].astype(f32)


def plane_device(
    layer_input,
    token_positions,
    attention_gain,
    query_weight,
    key_matrix,
    value_matrix,
    query_gain,
    key_norm_gain,
    output_weight,
    feedforward_gain,
    gate_weight,
    up_weight,
    down_weight,
    out_cotangent,
):
    n = lax.axis_size("ctx")
    planes = lax.axis_size("fsdp")
    block, width = layer_input.shape[1:]
    length = token_positions.shape[1]
    head = query_gain.shape[0]
    qw = query_weight.shape[1] // n
    kw = key_matrix.shape[1] // n
    fw = gate_weight.shape[1] // n
    group = qw // head
    per = block // planes
    half = head // 2
    inverse = np.power(rope_base, -np.arange(half) * 2.0 / head).astype(np.float32)
    inverse = np.concatenate([inverse, inverse])[None]
    steps = np.arange(block // 2)[:, None] * inverse.astype(np.float64)
    step_cos, step_sin = (jnp.asarray(f(steps).astype(np.float32)) for f in (np.cos, np.sin))
    inverse = jnp.asarray(inverse)
    vmem = pl.BlockSpec(memory_space=pltpu.VMEM)
    hbm = pl.BlockSpec(memory_space=pl.ANY)
    dma = pltpu.SemaphoreType.DMA
    sizes = (fw, fw, fw, qw, qw + 2 * kw)
    low = lambda *shape: pltpu.VMEM(shape, bf16)
    wide = lambda *shape: pltpu.VMEM(shape, f32)
    scratch = [
        low(width, qw + 2 * kw), low(width, 2 * fw), low(qw, width), low(fw, width),
        low(planes * (output_weight.shape[0] // n), width), low(3, planes * 32, width),
        low(length, width), low(length, width), low(length, width),
        low(width, length), low(width, length), low(width, length),
        wide(length, head), wide(length, head), wide(length, head),
        wide(length, qw + kw), low(length, qw), low(length, kw), low(length, kw),
        low(kw, length), low(kw, length), low(n // 2, length, 2 * group * block), wide(n // 2, 1, 2 * group * block),
        wide(n // 2, head, 2 * group * block), low(length, qw),
        low(length, fw), low(length, 2 * fw), low(length, qw + 2 * kw),
        wide(length, kw), wide(length, kw),
    ]
    scratch += [low(planes, n, per, size) for size in sizes]
    scratch += [low(planes + 1, n, per, size) for size in sizes]
    scratch += [low(2, 4, block, width) for _ in range(4)] + [wide(2, block, width), wide(2, block, width)]
    scratch += [
        wide(block, width), wide(block, width), wide(8, width), wide(n, 8, width), wide(planes, 8, width),
        dma((13,)), dma((8, 6)), dma((8, planes)), dma((4, 7)), dma((4, 4)),
        dma((4, n)), dma((4, n)), dma((4, 4)), dma((4, 4)), dma((4, 4)), dma((4, 4)),
        dma((5, planes)), dma((5, planes + 1)), dma((5, n)), dma((5, n)), dma((n,)), dma((n,)),
        dma((planes,)), dma((planes,)),
    ]
    shapes = [
        jax.ShapeDtypeStruct((block, width), bf16),
        jax.ShapeDtypeStruct((block, width), f32),
        jax.ShapeDtypeStruct((8, width), f32),
    ] + [jax.ShapeDtypeStruct((n, per, size), bf16) for size in sizes]
    results = pl.pallas_call(
        functools.partial(layer_kernel, n, planes, block, head, group, fw),
        out_shape=shapes,
        in_specs=[vmem] * 10 + [hbm] * 7,
        out_specs=[vmem] * len(shapes),
        scratch_shapes=scratch,
        compiler_params=pltpu.CompilerParams(
            collective_id=0, has_side_effects=True, vmem_limit_bytes=60 * 1024 * 1024),
    )(
        layer_input[0], out_cotangent[0], token_positions, inverse, step_cos, step_sin,
        attention_gain[None], feedforward_gain[None], query_gain[None], key_norm_gain[None],
        query_weight, key_matrix, value_matrix, output_weight, gate_weight, up_weight, down_weight,
    )
    plain = lambda rows, columns, kind=f32: jax.ShapeDtypeStruct((rows, columns), kind)
    finals = [
        plain(block, width, bf16), plain(block, width), plain(1, width),
        plain(per, n * qw), plain(per, n * kw), plain(per, n * kw), plain(1, head), plain(1, head),
        plain(per, n * qw), plain(1, width), plain(per, n * fw), plain(per, n * fw), plain(per, n * fw),
    ]
    done = pl.pallas_call(
        functools.partial(finish_kernel, n, head),
        out_shape=finals,
        in_specs=[vmem] * len(shapes),
        out_specs=[vmem] * len(finals),
    )(*results)
    out, dx, ag, q, k, v, qg, kg, o, fg, g, u, d = done
    return out[None], dx[None], ag[0], q, k, v, qg[0], kg[0], o.T, fg[0], g, u, d.T


def solution(mesh):
    in_specs = (
        P("fsdp", "ctx", None),
        P("fsdp", None),
        P(),
        P("fsdp", None),
        P("fsdp", None),
        P("fsdp", None),
        P(),
        P(),
        P("fsdp", None),
        P(),
        P("fsdp", None),
        P("fsdp", None),
        P("fsdp", None),
        P("fsdp", "ctx", None),
    )
    out_specs = (
        P("fsdp", "ctx", None),
        P("fsdp", "ctx", None),
        P(),
        P(("ctx", "fsdp"), None),
        P(("ctx", "fsdp"), None),
        P(("ctx", "fsdp"), None),
        P(),
        P(),
        P(None, ("ctx", "fsdp")),
        P(),
        P(("ctx", "fsdp"), None),
        P(("ctx", "fsdp"), None),
        P(None, ("ctx", "fsdp")),
    )

    def run(*arguments):
        n, planes = mesh.shape["ctx"], mesh.shape["fsdp"]
        key_heads = arguments[4].shape[1] // arguments[6].shape[0]
        whole_heads = n == 8 and planes == 4 and key_heads == n
        return jax.shard_map(
            plane_device if whole_heads else on_device,
            mesh=mesh, in_specs=in_specs, out_specs=out_specs, check_vma=False,
        )(*arguments)

    return run
```

```python
import functools

import jax
import jax.numpy as jnp
import numpy as np
from jax import lax
from jax.experimental import pallas as pl
from jax.experimental.pallas import tpu as pltpu
from jax.sharding import PartitionSpec as P

epsilon = 1e-06
rope_base = 1000000.0
masked_score = -1e30


def from_behind(block, axis, distance):
    devices = range(lax.axis_size(axis))
    route = [((i - distance) % len(devices), i) for i in devices]
    return lax.ppermute(block, axis, route)


def rotate(value_rows):
    half = value_rows.shape[-1] // 2
    return jnp.concatenate([-value_rows[..., half:], value_rows[..., :half]], -1)


def rotate_back(value_rows):
    half = value_rows.shape[-1] // 2
    return jnp.concatenate([value_rows[..., half:], -value_rows[..., :half]], -1)


def rope_tables(token_offsets, head_size):
    half = head_size // 2
    inverse = rope_base ** (-(jnp.arange(half).astype(jnp.float32) * 2.0) / head_size)
    angles = token_offsets.astype(jnp.float32)[:, None] * inverse[None, :]
    cosine = jnp.cos(angles)
    sine = jnp.sin(angles)
    return (jnp.concatenate([cosine, cosine], -1), jnp.concatenate([sine, sine], -1))


def norm_scale(value_rows):
    return lax.rsqrt(jnp.mean(value_rows * value_rows, -1, keepdims=True) + epsilon)


def norm_back(value_rows, scale, gain, grad):
    weighted = grad * gain
    inner = jnp.mean(weighted * value_rows, -1, keepdims=True)
    result = scale * weighted - value_rows * scale * scale * scale * inner
    gain_part = jnp.sum((grad * value_rows * scale).reshape(-1, gain.shape[0]), 0)
    return (result, gain_part)


def row_products(left, pieces):
    return tuple((jnp.dot(left, piece, preferred_element_type=jnp.float32) for piece in pieces))


def column_products(rights, pieces):
    total = jnp.einsum("tc,rc->tr", rights[0], pieces[0], preferred_element_type=jnp.float32)
    for right, piece in zip(rights[1:], pieces[1:]):
        total = total + jnp.einsum("tc,rc->tr", right, piece, preferred_element_type=jnp.float32)
    return total


def on_device(
    layer_input,
    token_positions,
    attention_gain,
    query_weight,
    key_matrix,
    value_matrix,
    query_gain,
    key_norm_gain,
    output_weight,
    feedforward_gain,
    gate_weight,
    up_weight,
    down_weight,
    out_cotangent,
):
    hidden_in = layer_input[0].astype(jnp.float32)
    count = hidden_in.shape[0]
    head_size = query_gain.shape[0]
    query_width = query_weight.shape[1]
    key_width = key_matrix.shape[1]
    inner_width = gate_weight.shape[1]
    heads = query_width // head_size
    key_heads = key_width // head_size
    group = heads // key_heads
    scale = head_size ** (-0.5)
    cycles = lax.axis_size("ctx")
    own_index = lax.axis_index("ctx")
    sequence_pos = token_positions[0]
    token_offsets = lax.dynamic_slice_in_dim(sequence_pos, own_index * count, count)
    cosine, sine = rope_tables(token_offsets, head_size)
    cosine = cosine[:, None, :]
    sine = sine[:, None, :]
    first_scale = norm_scale(hidden_in)
    first = (hidden_in * first_scale * attention_gain).astype(jnp.bfloat16)
    query_raw, key_unnormed, value_unnormed = row_products(
        first,
        (
            lax.all_gather(query_weight, "fsdp", axis=0, tiled=True),
            lax.all_gather(key_matrix, "fsdp", axis=0, tiled=True),
            lax.all_gather(value_matrix, "fsdp", axis=0, tiled=True),
        ),
    )
    query_heads = query_raw.reshape(count, heads, head_size)
    query_scale = norm_scale(query_heads)
    query_normed = query_heads * query_scale * query_gain
    query_rot = query_normed * cosine + rotate(query_normed) * sine
    query_grouped = (
        query_rot.reshape(count, key_heads, group, head_size)
        .transpose(1, 2, 0, 3)
        .astype(jnp.bfloat16)
    )
    key_heads_raw = key_unnormed.reshape(count, key_heads, head_size)
    key_scale = norm_scale(key_heads_raw)
    key_normed = key_heads_raw * key_scale * key_norm_gain
    key_low = (
        (key_normed * cosine + rotate(key_normed) * sine)
        .reshape(count, key_width)
        .astype(jnp.bfloat16)
    )
    value_low = value_unnormed.astype(jnp.bfloat16)
    rowmax = jnp.full((key_heads, group, count), masked_score, jnp.float32)
    keys_piece = lax.all_gather(key_low, "ctx", axis=0, tiled=True).reshape(
        -1, key_heads, head_size
    )
    values_piece = lax.all_gather(value_low, "ctx", axis=0, tiled=True).reshape(
        -1, key_heads, head_size
    )
    key_pos = sequence_pos
    allowed = token_offsets[:, None] >= key_pos[None, :]
    scores = (
        jnp.einsum("kgtd,skd->kgts", query_grouped, keys_piece, preferred_element_type=jnp.float32)
        * scale
    )
    scores = jnp.where(allowed, scores, masked_score)
    newmax = jnp.maximum(rowmax, jnp.max(scores, -1))
    weights = jnp.where(allowed, jnp.exp(scores - newmax[..., None]), 0.0)
    accum = jnp.einsum(
        "kgts,skd->kgtd",
        weights.astype(jnp.bfloat16),
        values_piece,
        preferred_element_type=jnp.float32,
    )
    rowsum = jnp.sum(weights, -1)
    accum, rowmax, rowsum = (accum, newmax, rowsum)
    normalized = accum / rowsum[..., None]
    logsum = rowmax + jnp.log(rowsum)
    attention_low = (
        normalized.transpose(2, 0, 1, 3).reshape(count, query_width).astype(jnp.bfloat16)
    )
    output_whole = lax.all_gather(output_weight, "fsdp", axis=0, tiled=True)
    branch_out = jnp.dot(attention_low, output_whole, preferred_element_type=jnp.float32)
    middle = hidden_in + branch_out
    second_scale = norm_scale(middle)
    second = (middle * second_scale * feedforward_gain).astype(jnp.bfloat16)
    gate, up = row_products(
        second,
        (
            lax.all_gather(gate_weight, "fsdp", axis=0, tiled=True),
            lax.all_gather(up_weight, "fsdp", axis=0, tiled=True),
        ),
    )
    sigmoid_gate = jax.nn.sigmoid(gate)
    silu_gate = gate * sigmoid_gate
    hidden_low = (silu_gate * up).astype(jnp.bfloat16)
    (down_out,) = row_products(
        hidden_low, (lax.all_gather(down_weight, "fsdp", axis=0, tiled=True),)
    )
    layer_output = (middle + down_out).astype(jnp.bfloat16)[None]
    cotangent = out_cotangent[0]
    hidden_grad = column_products(
        (cotangent,), lax.all_gather((down_weight,), "fsdp", axis=0, tiled=True)
    )
    up_low = (hidden_grad * silu_gate).astype(jnp.bfloat16)
    gate_low = (hidden_grad * up * sigmoid_gate * (1.0 + gate * (1.0 - sigmoid_gate))).astype(
        jnp.bfloat16
    )
    second_grad = column_products(
        (gate_low, up_low), lax.all_gather((gate_weight, up_weight), "fsdp", axis=0, tiled=True)
    )
    middle_part, feedforward_part = norm_back(middle, second_scale, feedforward_gain, second_grad)
    middle_grad = cotangent.astype(jnp.float32) + middle_part
    middle_low = middle_grad.astype(jnp.bfloat16)
    attention_grad = jnp.einsum(
        "tc,rc->tr", middle_low, output_whole, preferred_element_type=jnp.float32
    )
    attention_grad_low = attention_grad.astype(jnp.bfloat16)
    mixed_grad = attention_grad_low.reshape(count, key_heads, group, head_size).transpose(
        1, 2, 0, 3
    )
    delta = jnp.sum(mixed_grad.astype(jnp.float32) * normalized, -1)

    def cycle_step(index, carry):
        keys_held, values_held, key_acc, value_acc, query_acc = carry
        anchor = (own_index - index) % cycles
        key_pos = lax.dynamic_slice_in_dim(sequence_pos, anchor * count, count)
        keys_piece = keys_held.astype(jnp.bfloat16).reshape(count, key_heads, head_size)
        values_piece = values_held.astype(jnp.bfloat16).reshape(count, key_heads, head_size)
        allowed = token_offsets[:, None] >= key_pos[None, :]
        scores = (
            jnp.einsum(
                "kgtd,skd->kgts", query_grouped, keys_piece, preferred_element_type=jnp.float32
            )
            * scale
        )
        probs = jnp.where(allowed, jnp.exp(scores - logsum[..., None]), 0.0)
        value_acc = value_acc + jnp.einsum(
            "kgts,kgtd->skd",
            probs.astype(jnp.bfloat16),
            mixed_grad,
            preferred_element_type=jnp.float32,
        ).reshape(count, key_width)
        prob_grad = jnp.einsum(
            "kgtd,skd->kgts", mixed_grad, values_piece, preferred_element_type=jnp.float32
        )
        score_grad = (probs * (prob_grad - delta[..., None])).astype(jnp.bfloat16)
        query_acc = (
            query_acc
            + jnp.einsum(
                "kgts,skd->kgtd", score_grad, keys_piece, preferred_element_type=jnp.float32
            )
            * scale
        )
        key_acc = (
            key_acc
            + jnp.einsum(
                "kgts,kgtd->skd", score_grad, query_grouped, preferred_element_type=jnp.float32
            ).reshape(count, key_width)
            * scale
        )
        moved = (
            from_behind(keys_held.astype(jnp.bfloat16), "ctx", 1).astype(keys_held.dtype),
            from_behind(values_held.astype(jnp.bfloat16), "ctx", 1).astype(values_held.dtype),
            from_behind(key_acc.astype(jnp.bfloat16), "ctx", 1).astype(key_acc.dtype),
            from_behind(value_acc.astype(jnp.bfloat16), "ctx", 1).astype(value_acc.dtype),
        )
        return (moved[0], moved[1], moved[2], moved[3], query_acc)

    start_cycle = (
        key_low.astype(jnp.float32),
        value_low.astype(jnp.float32),
        jnp.zeros((count, key_width), jnp.float32),
        jnp.zeros((count, key_width), jnp.float32),
        jnp.zeros((key_heads, group, count, head_size), jnp.float32),
    )
    cycle_done = lax.fori_loop(0, cycles, cycle_step, start_cycle)
    key_acc = cycle_done[2]
    value_acc = cycle_done[3]
    query_acc = cycle_done[4]
    query_rot_grad = query_acc.transpose(2, 0, 1, 3).reshape(count, heads, head_size)
    query_normed_grad = query_rot_grad * cosine + rotate_back(query_rot_grad * sine)
    query_heads_grad, query_part = norm_back(
        query_heads, query_scale, query_gain, query_normed_grad
    )
    query_low_grad = query_heads_grad.reshape(count, query_width).astype(jnp.bfloat16)
    key_rot_grad = key_acc.reshape(count, key_heads, head_size)
    key_normed_grad = key_rot_grad * cosine + rotate_back(key_rot_grad * sine)
    key_heads_grad, key_part = norm_back(key_heads_raw, key_scale, key_norm_gain, key_normed_grad)
    key_low_grad = key_heads_grad.reshape(count, key_width).astype(jnp.bfloat16)
    value_low_grad = value_acc.astype(jnp.bfloat16)
    first_grad = column_products(
        (query_low_grad, key_low_grad, value_low_grad),
        lax.all_gather((query_weight, key_matrix, value_matrix), "fsdp", axis=0, tiled=True),
    )
    input_part, attention_part = norm_back(hidden_in, first_scale, attention_gain, first_grad)
    input_gradient = (middle_grad + input_part)[None]
    rights_first = jnp.concatenate([query_low_grad, key_low_grad, value_low_grad], 1)
    rights_second = jnp.concatenate([gate_low, up_low], 1)
    pairs = (
        (first, rights_first),
        (second, rights_second),
        (middle_low, attention_low),
        (cotangent, hidden_low),
    )
    parts = []
    for left, right in pairs:
        parts.append(jnp.einsum("tr,tc->rc", left, right, preferred_element_type=jnp.float32))
    sums = lax.psum_scatter(
        jnp.concatenate(parts, 1), ("ctx", "fsdp"), scatter_dimension=0, tiled=True
    )
    edges = [0, query_width, query_width + key_width, query_width + 2 * key_width]
    edges = edges + [edges[3] + inner_width, edges[3] + 2 * inner_width]
    edges = edges + [edges[5] + query_width, edges[5] + query_width + inner_width]
    query_gradient = sums[:, edges[0] : edges[1]]
    key_gradient = sums[:, edges[1] : edges[2]]
    value_gradient = sums[:, edges[2] : edges[3]]
    gate_gradient = sums[:, edges[3] : edges[4]]
    up_gradient = sums[:, edges[4] : edges[5]]
    output_gradient = sums[:, edges[5] : edges[6]].T
    down_gradient = sums[:, edges[6] : edges[7]].T
    attention_total, query_total, key_total, feedforward_total = lax.psum(
        (attention_part, query_part, key_part, feedforward_part), ("ctx", "fsdp")
    )
    return (
        layer_output,
        input_gradient,
        attention_total,
        query_gradient,
        key_gradient,
        value_gradient,
        query_total,
        key_total,
        output_gradient,
        feedforward_total,
        gate_gradient,
        up_gradient,
        down_gradient,
    )


MESH = pl.DeviceIdType.MESH
f32 = jnp.float32
bf16 = jnp.bfloat16


def dot(left, right):
    return jnp.dot(left, right, preferred_element_type=f32)


def dot_nt(left, right):
    return lax.dot_general(left, right, (((1,), (1,)), ((), ())), preferred_element_type=f32)


def dot_tn(left, right):
    return lax.dot_general(left, right, (((0,), (0,)), ((), ())), preferred_element_type=f32)


def hidden_block(device, third):
    def plane(i, t):
        return ((3, 1, 2), (0, 2, 1), (0, 3, 2), (3, 0, 1))[i // 4 * 2 + i % 2][t]

    own = plane(device, third)
    return own, sum(plane(i, t) == own for i in range(device) for t in range(3))


def layer_kernel(
    n, planes, block, head, group, fw,
    x_ref, dy_ref, pos_row, inverse_ref, step_cos, step_sin, ag_ref, fg_ref, qg_ref, kg_ref,
    wq, wk, wv, wo, wg, wu, wd,
    out_ref, dx_ref, gains_ref, got_a, got_b, got_c, got_out, got_qkv,
    w_qkv, w_gu, w_out, w_down, t_out,
    first, dy_all, second, first_t, dy_t, second_t,
    positions, cosine, sine,
    raw, queries, keys, values, keys_t, values_t, probs, sums, mixed_t, mixed_low,
    hidden, d_gu, d_qkv, dk_acc, dv_acc,
    stage_a, stage_b, stage_c, stage_out, stage_qkv,
    land_a, land_b, land_c, land_out, land_qkv,
    rs_sa, rs_ra, rs_sb, rs_rb, rs_kept, rs_acc,
    middle, d_middle, gain_own, gain_plane, gain_all,
    local_sem, wz_send, wz_recv, hand_send, hand_recv,
    ag_send, ag_recv, ra_send, ra_recv, rb_send, rb_recv,
    zr_send, zr_recv, aa_send, aa_recv, gp_send, gp_recv, gz_send, gz_recv,
):
    c = lax.axis_index("ctx")
    z = lax.axis_index("fsdp")
    dmid = first
    dmid_t = second
    cy, cx, ck = lax.div(c, 4), lax.rem(lax.div(c, 2), 2), lax.rem(c, 2)
    ci = lax.rem(c, 4)
    sign = 1 - 2 * ck
    qw, kw = group * head, head
    pw = 128
    thirds = fw // pw
    width = x_ref.shape[1]
    scale = head ** (-0.5)
    log2e = 1.4426950408889634
    gots = (got_a, got_b, got_c, got_out, got_qkv)
    stages = (stage_a, stage_b, stage_c, stage_out, stage_qkv)
    lands = (land_a, land_b, land_c, land_out, land_qkv)

    def partner(j):
        y = lax.rem(cy + lax.div(j, 4), 2)
        x = lax.rem(cx + lax.rem(lax.div(j, 2), 2), 2)
        k = lax.rem(ck + lax.rem(j, 2), 2)
        return y * 4 + x * 2 + k

    def chip(slot):
        return lax.rem(cy + lax.div(slot, 2), 2) * 2 + lax.rem(cx + lax.rem(slot, 2), 2)

    def rows(start, size):
        return pl.ds(pl.multiple_of(start * size, size), size)

    def remote(src, dst, send, recv, ctx, plane):
        return pltpu.make_async_remote_copy(
            src_ref=src, dst_ref=dst, send_sem=send, recv_sem=recv,
            device_id={"ctx": ctx, "fsdp": plane}, device_id_type=MESH,
        )

    in_plane, along, weight_sends = [], [], []

    def launch(started, copy, when=None):
        if when is None:
            copy().start()
        else:
            pl.when(when)(lambda: copy().start())
        started.append((copy, when))

    def drain(started):
        for copy, when in started:
            if when is None:
                copy().wait_send()
            else:
                pl.when(when)(lambda copy=copy: copy().wait_send())
        started.clear()

    def pick(values):
        return sum(jnp.where(c == i, value, 0) for i, value in enumerate(values))

    unit_plane = [pick([hidden_block(i, t)[0] for i in range(n)]) for t in range(thirds)]
    unit_block = [pick([hidden_block(i, t)[1] for i in range(n)]) for t in range(thirds)]
    plane_blocks = wd.shape[0] // pw

    own_rows = wq.shape[0]
    out_rows = wo.shape[0] // n

    def own_slices():
        mine = rows(z, own_rows)
        pairs = [
            (wq.at[:, rows(c, qw)], w_qkv.at[mine, 0:qw]),
            (wk.at[:, rows(c, kw)], w_qkv.at[mine, qw:qw + kw]),
            (wv.at[:, rows(c, kw)], w_qkv.at[mine, qw + kw:qw + 2 * kw]),
            (wo.at[rows(c, out_rows)], t_out.at[rows(z, out_rows)]),
        ]
        for t in range(thirds):
            at = 2 * pw * t
            unit = unit_plane[t] * plane_blocks + unit_block[t]
            pairs.append((wg.at[:, rows(unit, pw)], w_gu.at[mine, at:at + pw]))
            pairs.append((wu.at[:, rows(unit, pw)], w_gu.at[mine, at + pw:at + 2 * pw]))
        return pairs

    local = [pltpu.make_async_copy(src, dst, local_sem.at[i]) for i, (src, dst) in enumerate(own_slices())]
    for copy in local:
        copy.start()

    def own_down(t):
        return pltpu.make_async_copy(
            wd.at[rows(unit_block[t], pw)], w_down.at[t * pw:(t + 1) * pw], local_sem.at[4 + 2 * thirds + t])

    holds = [unit_plane[t] == z for t in range(thirds)]
    for t in range(thirds):
        pl.when(holds[t])(lambda t=t: own_down(t).start())

    for land in lands:
        @pl.when(z == 0)
        def _(land=land):
            land[0] = jnp.zeros(land.shape[1:], bf16)

        @pl.when(z == planes - 1)
        def _(land=land):
            land[planes] = jnp.zeros(land.shape[1:], bf16)

    barrier = pltpu.get_barrier_semaphore()
    for j in range(1, n):
        pl.semaphore_signal(barrier, inc=1, device_id={"ctx": partner(j), "fsdp": z}, device_id_type=MESH)
    for d in range(1, planes):
        pl.semaphore_signal(
            barrier, inc=1, device_id={"ctx": c, "fsdp": lax.rem(z + d, planes)}, device_id_type=MESH)
    x = x_ref[...].astype(f32)
    x_scale = lax.rsqrt(jnp.mean(x * x, -1, keepdims=True) + epsilon)
    first[rows(c, block)] = (x * x_scale * ag_ref[...]).astype(bf16)
    dy_all[rows(c, block)] = dy_ref[...]
    for copy in local[:3]:
        copy.wait()
    pl.semaphore_wait(barrier, n + planes - 2)

    def inside(t):
        return jnp.logical_and(t >= 0, t < planes)

    weights = [
        (lambda o: w_qkv.at[rows(o, own_rows)], None),
        (lambda o: t_out.at[rows(o, out_rows)], 0),
    ]
    for t in range(thirds):
        weights.append((lambda o, t=t: w_gu.at[rows(o, own_rows), 2 * pw * t:2 * pw * (t + 1)], None))
        weights.append((lambda o, t=t: w_down.at[t * pw:(t + 1) * pw], None))

    def weight_copy(w, slot, origin, target):
        part = weights[w][0](origin)
        return remote(part, part, wz_send.at[w, slot], wz_recv.at[w, origin], c, target)

    def from_plane(w, origin):
        return origin == unit_plane[(w - 3) // 2] if w >= 3 and w % 2 else None

    def both(one, other):
        return one if other is None else jnp.logical_and(one, other)

    def hand_split(origin, valid):
        mine = 2 * origin + cy == c
        return jnp.logical_and(valid, jnp.logical_not(mine)), jnp.logical_and(valid, mine)

    def weight_start(w):
        for side in range(2):
            d = sign * (1 - 2 * side)
            launch(
                weight_sends, lambda side=side, d=d: weight_copy(w, side, z, z + d),
                both(inside(z + d), from_plane(w, z)))
        if weights[w][1] is not None:
            hand_over(w, z, 0, *hand_split(z, True))

    def hand_target(h):
        return lambda i: w_out.at[rows(i, out_rows)]

    def hand_copy(w, origin, slot):
        h = weights[w][1]
        return remote(
            weights[w][0](origin), hand_target(h)(ci), hand_send.at[h, slot], hand_recv.at[h, ci], 2 * origin + cy, z)

    def hand_over(w, origin, slot, away, here):
        launch(in_plane, lambda: hand_copy(w, origin, slot), away)

        @pl.when(here)
        def _():
            hand_target(weights[w][1])(ci)[...] = weights[w][0](origin)[...]

    def hand_arrive(w):
        h = weights[w][1]
        for i in range(4):
            @pl.when(4 * ck + i != c)
            def _(i=i):
                part = hand_target(h)(i)
                remote(part, part, hand_send.at[h, 0], hand_recv.at[h, i], c, z).wait_recv()

    hops = {}
    for w in range(len(weights)):
        for d in range(1, planes):
            for side, way in enumerate((1, -1)):
                origin = z - way * d
                valid = both(inside(origin), from_plane(w, origin))
                passed = jnp.logical_and(valid, inside(z + way))
                split = None if weights[w][1] is None else hand_split(origin, valid)
                hops[w, d, side] = origin, z + way, valid, passed, split

    def weight_hop(w, d):
        for side in range(2):
            origin, following, valid, passed, split = hops[w, d, side]
            pl.when(valid)(lambda: weight_copy(w, 0, origin, z).wait_recv())
            if d < planes - 1:
                launch(
                    weight_sends,
                    lambda side=side, origin=origin, following=following: weight_copy(
                        w, 2 * d + side, origin, following),
                    passed)
            if split is not None:
                hand_over(w, origin, 2 * d - 1 + side, *split)

    def gather_copy(buf, g, j, send, origin, target):
        part = buf.at[rows(origin, block)]
        return remote(part, part, ag_send.at[g, send], ag_recv.at[g, j], target, z)

    def gather_start(buf, g):
        for j in (1, 2 + 2 * ck, 4 - 2 * ck):
            launch(in_plane, lambda j=j: gather_copy(buf, g, j, j, c, partner(j)))

    def gather_half(buf, g, j):
        half = block // 2
        part = buf.at[pl.ds(pl.multiple_of(partner(j) * block + (half if j == 2 else 0), half), half)]
        at = 0 if j == 2 else 6
        return remote(part, part, ag_send.at[g, at], ag_recv.at[g, at], partner(6 - j), z)

    def gather_diagonal(buf, g):
        half = block // 2
        for at in (6, 0):
            part = buf.at[pl.ds(pl.multiple_of(partner(6) * block + (0 if at == 6 else half), half), half)]
            remote(part, part, ag_send.at[g, at], ag_recv.at[g, at], c, z).wait_recv()

    def gather_forward(buf, g, j):
        return gather_copy(buf, g, j + 1, j + 1, partner(j), partner(1))

    def gather_take(buf, g, j):
        if j == 6:
            gather_diagonal(buf, g)
        else:
            gather_copy(buf, g, j, j, partner(j), c).wait_recv()
            gather_half(buf, g, j).start()
        gather_forward(buf, g, j).start()

    def gather_sent(buf, g):
        for j in (2, 4, 6):
            in_plane.append((lambda j=j: gather_forward(buf, g, j), None))
            if j < 6:
                in_plane.append((lambda j=j: gather_half(buf, g, j), None))

    def gather_finish(buf, g):
        for j in (2, 4, 6):
            gather_take(buf, g, j)
        gather_sent(buf, g)
        for j in (1, 3, 5, 7):
            gather_copy(buf, g, j, j, partner(j), c).wait_recv()

    def gather_step(buf, g, slot):
        @pl.when(slot == 1)
        def _():
            gather_take(buf, g, 2)
            gather_take(buf, g, 4)

        pl.when(slot == 3)(lambda: gather_take(buf, g, 6))
        gather_copy(buf, g, 2 * slot + 1, 0, partner(2 * slot + 1), c).wait_recv()

    def sum_pair_copy(s, slot):
        return remote(rs_sa.at[s % 2, slot], rs_ra.at[s % 2, slot], ra_send.at[s, slot], ra_recv.at[s, slot], partner(1), z)

    def sum_chip_copy(s, slot):
        return remote(
            rs_sb.at[s % 2, slot], rs_rb.at[s % 2, slot], rb_send.at[s, slot], rb_recv.at[s, slot], partner(2 * slot), z)

    def sum_half_copy(s, slot):
        half = block // 2
        at = pl.ds(pl.multiple_of((slot - 1) * half, half), half)
        return remote(
            rs_sb.at[s % 2, 3, at], rs_rb.at[s % 2, 3, at], rb_send.at[s, 6 - 3 * slot], rb_recv.at[s, 6 - 3 * slot],
            partner(6 - 2 * slot), z)

    def sum_slot(p):
        return jnp.where(p == 0, 3, jnp.where(p == 1, 2 - ck, jnp.where(p == 2, 1 + ck, 0)))

    def sum_start(s, left, partial, prepare=None, ready=None, during=()):
        if prepare is not None:
            prepare(chip(sum_slot(0)))
        if ready is not None:
            ready()

        def body(p, carry):
            slot = sum_slot(p)
            at = [rows(partner(2 * slot + 1), block), rows(partner(2 * slot), block)]
            both = partial(jnp.concatenate([left[i] for i in at], 0))
            rs_sa[s % 2, slot] = both[:block].astype(bf16)
            sum_pair_copy(s, slot).start()
            rs_kept[lax.rem(p, 2)] = both[block:]

            @pl.when(p > 0)
            def _():
                before = sum_slot(p - 1)
                sum_pair_copy(s, before).wait_recv()
                rs_sb[s % 2, before] = (
                    rs_kept[lax.rem(p + 1, 2)] + rs_ra[s % 2, before].astype(f32)).astype(bf16)

            @pl.when(p == 1)
            def _():
                sum_half_copy(s, 1).start()
                sum_half_copy(s, 2).start()

            @pl.when(p > 1)
            def _():
                before = sum_slot(p - 1)
                half = block // 2
                at = pl.ds(pl.multiple_of((before - 1) * half, half), half)
                sum_half_copy(s, before).wait_recv()
                rs_sb[s % 2, before, at] = (
                    rs_sb[s % 2, before, at].astype(f32) + rs_rb[s % 2, 3, at].astype(f32)).astype(bf16)
                sum_chip_copy(s, before).start()

            if prepare is not None:
                @pl.when(p < 3)
                def _():
                    prepare(chip(sum_slot(p + 1)))

            for k, poll in enumerate(during):
                pl.when(p == k)(poll)
            return carry

        lax.fori_loop(0, 4, body, 0)
        for slot in range(4):
            in_plane.append((lambda slot=slot: sum_pair_copy(s, slot), None))
        for slot in (1, 2):
            in_plane.append((lambda slot=slot: sum_half_copy(s, slot), None))
            in_plane.append((lambda slot=slot: sum_chip_copy(s, slot), None))
        sum_pair_copy(s, 0).wait_recv()
        rs_acc[s % 2] = rs_kept[1] + rs_ra[s % 2, 0].astype(f32)

    def sum_finish(s):
        total = rs_acc[s % 2]
        for slot in (1, 2):
            sum_chip_copy(s, slot).wait_recv()
            total = total + rs_rb[s % 2, slot].astype(f32)
        return total

    per = block // planes

    def weight_grad(m, parts):
        def body(i, carry):
            at = 0
            for left, right in parts:
                value = right()
                grad = dot(left[rows(i, 4 * block)], value)
                for k in range(4):
                    for t in range(planes):
                        start = k * block + t * per
                        stages[m][t, 4 * i + k, :, at:at + value.shape[1]] = grad[start:start + per].astype(bf16)
                at += value.shape[1]
            return carry

        lax.fori_loop(0, n // 4, body, 0)
        at_edge = jnp.logical_or(z == 0, z == planes - 1)
        for k in range(planes - 1):
            t = jnp.where(z == 0, planes - 1 - k, k)
            launch(along, lambda t=t: grad_copy(m, t), at_edge)

    def grad_copy(m, t):
        way = jnp.where(z < t, 1, -1)
        last = z + way == t
        slot = jnp.where(jnp.logical_and(last, way < 0), planes, t)
        return remote(
            stages[m].at[t], lands[m].at[slot], zr_send.at[m, t], zr_recv.at[m, slot], c, z + way)

    def grad_arrive(m, slot):
        part = lands[m].at[slot]
        remote(part, part, zr_send.at[m, 0], zr_recv.at[m, slot], c, z).wait_recv()

    def grad_pass(m, t, valid):
        @pl.when(valid)
        def _():
            grad_arrive(m, t)

            def body(i, carry):
                stages[m][t, i] = (stages[m][t, i].astype(f32) + lands[m][t, i].astype(f32)).astype(bf16)
                return carry

            lax.fori_loop(0, n, body, 0)

        launch(along, lambda: grad_copy(m, t), valid)

    is_low, is_high = z == 1, z == planes - 2

    def grad_near_far(m):
        grad_pass(m, 3, is_low)
        grad_pass(m, 0, is_high)

    def grad_near_inner(m):
        grad_pass(m, 2, is_low)
        grad_pass(m, 1, is_high)

    def grad_near(m):
        grad_near_far(m)
        grad_near_inner(m)

    def grad_far(m):
        grad_pass(m, 3, is_high)
        grad_pass(m, 0, is_low)

    def owner_copy(m, j):
        return remote(lands[m].at[z, partner(j)], gots[m].at[c], aa_send.at[m, j], aa_recv.at[m, j], partner(j), z)

    def hand_out(m):
        pl.when(z > 0)(lambda: grad_arrive(m, z))
        pl.when(z < planes - 1)(lambda: grad_arrive(m, planes))

        def body(i, carry):
            total = stages[m][z, i].astype(f32) + lands[m][z, i].astype(f32) + lands[m][planes, i].astype(f32)
            lands[m][z, i] = total.astype(bf16)
            return carry

        lax.fori_loop(0, n, body, 0)
        for j in (2 + 2 * ck, 3 + 2 * ck, 4 - 2 * ck, 5 - 2 * ck, 6, 7, 1):
            launch(in_plane, lambda j=j: owner_copy(m, j))
        gots[m][c] = lands[m][z, c]

    def hand_receive(m):
        for j in range(1, n):
            owner_copy(m, j).wait_recv()

    weight_start(0)
    gather_start(first, 0)
    for copy in local[3:]:
        copy.wait()
    for t in range(thirds):
        pl.when(holds[t])(lambda t=t: own_down(t).wait())

    spread = jnp.broadcast_to(pos_row[...].astype(f32), (head, pos_row.shape[1]))
    positions[...] = spread.T
    side = jnp.where(lax.broadcasted_iota(jnp.int32, (1, head), 1) < head // 2, -1.0, 1.0)

    def table(i, carry):
        run = step_cos.shape[0]
        at = rows(i, run)
        start = positions[pl.ds(pl.multiple_of(i * run, run), 1)] * inverse_ref[...]
        start_cos, start_sin = jnp.cos(start), jnp.sin(start)
        cosine[at] = start_cos * step_cos[...] - start_sin * step_sin[...]
        sine[at] = (start_sin * step_cos[...] + start_cos * step_sin[...]) * side
        return carry

    def turn_over(src, dst):
        def body(i, carry):
            at = rows(i, block)
            dst[:, at] = src[at].T
            return carry

        lax.fori_loop(0, n, body, 0)

    lax.fori_loop(0, 2 * n, table, 0)
    weight_hop(0, 1)
    gather_finish(first, 0)
    weight_hop(0, 2)
    weight_start(1)
    gather_start(dy_all, 1)
    turn_over(first, first_t)
    weight_hop(0, 3)
    weight_start(2)
    weight_start(3)

    def turn(value, at):
        return value * cosine[at] + pltpu.roll(value, head // 2, 1) * sine[at]

    def turn_back(grad, at):
        return grad * cosine[at] - pltpu.roll(grad, head // 2, 1) * sine[at]

    def project(i, carry):
        at = rows(i, 2 * block)
        result = dot(first[at], w_qkv[...])
        raw[at] = result[:, :qw + kw]
        low_values = result[:, qw + kw:].astype(bf16)
        values[at] = low_values
        values_t[:, at] = low_values.T
        for h in range(group + 1):
            part = result[:, h * head:(h + 1) * head]
            inv = lax.rsqrt(jnp.mean(part * part, -1, keepdims=True) + epsilon)
            gain = qg_ref[...] if h < group else kg_ref[...]
            turned = turn(part * inv * gain, at)
            if h < group:
                queries[at, h * head:(h + 1) * head] = (turned * (scale * log2e)).astype(bf16)
            else:
                low_keys = turned.astype(bf16)
                keys[at] = low_keys
                keys_t[:, at] = low_keys.T
        return carry

    lax.fori_loop(0, n // 4, project, 0)
    weight_hop(1, 1)
    lax.fori_loop(n // 4, n // 2, project, 0)
    weight_hop(1, 2)
    gather_finish(dy_all, 1)

    def stack(ref, at):
        return jnp.concatenate([ref[at, h * head:(h + 1) * head] for h in range(group)], 0)

    def attend(place):
        at = rows(place, 2 * block)
        scores = dot_nt(keys[...], stack(queries, at))
        allowed = positions[...] <= pos_row[:, rows(2 * place, block)].astype(f32)
        later = positions[...] <= pos_row[:, rows(2 * place + 1, block)].astype(f32)
        weight = jnp.concatenate(
            [jnp.exp2(jnp.where(later if k % 2 else allowed, scores[:, k * block:(k + 1) * block], masked_score))
             for k in range(2 * group)], 1)
        inv = 1.0 / jnp.sum(weight, 0, keepdims=True)
        low_weight = weight.astype(bf16)
        probs[place] = low_weight
        sums[place] = inv
        result = dot(values_t[...], low_weight) * inv
        mixed_t[place] = result
        for h in range(group):
            mixed_low[at, h * head:(h + 1) * head] = result[:, 2 * h * block:2 * (h + 1) * block].T.astype(bf16)

    def output_ready():
        weight_hop(1, 3)
        weight_start(4)
        weight_start(5)
        hand_arrive(1)
        drain(in_plane)

    def hop_third(t, d):
        weight_hop(2 + 2 * t, d)
        weight_hop(3 + 2 * t, d)

    sum_start(
        0, mixed_low, lambda left: dot(left, w_out[...]), attend, output_ready,
        (lambda: hop_third(0, 1), lambda: hop_third(0, 2), lambda: hop_third(1, 1)))
    weight_start(6)
    weight_start(7)
    hop_third(0, 3)
    turn_over(dy_all, dy_t)
    hop_third(1, 2)
    mid = x_ref[...].astype(f32) + sum_finish(0)
    middle[...] = mid
    mid_scale = lax.rsqrt(jnp.mean(mid * mid, -1, keepdims=True) + epsilon)
    second[rows(c, block)] = (mid * mid_scale * fg_ref[...]).astype(bf16)
    gather_start(second, 2)
    hop_third(2, 1)

    def feed(t, at):
        units, pair = slice(t * pw, (t + 1) * pw), 2 * pw * t
        both = dot(second[at], w_gu[:, pair:pair + 2 * pw])
        back = dot_nt(dy_all[at], w_down[units])
        gate, up = both[:, :pw], both[:, pw:]
        sig = 1.0 / (1.0 + jnp.exp(-gate))
        silu = gate * sig
        hidden[at, units] = (silu * up).astype(bf16)
        d_gu[at, pair:pair + pw] = (back * up * sig * (1.0 + gate * (1.0 - sig))).astype(bf16)
        d_gu[at, pair + pw:pair + 2 * pw] = (back * silu).astype(bf16)

    def feed_arriving(slot, carry):
        gather_step(second, 2, slot)
        at = rows(chip(slot), 2 * block)
        feed(0, at)
        second_t[:, at] = second[at].T
        pl.when(slot == 2)(lambda: hop_third(2, 2))
        return carry

    def third_grad(t):
        weight_grad(t, [
            (second_t, lambda: d_gu[:, 2 * pw * t:2 * pw * (t + 1)]),
            (dy_t, lambda: hidden[:, t * pw:(t + 1) * pw]),
        ])

    def feed_third(t):
        def body(i, carry):
            feed(t, rows(i, 2 * block))
            return carry

        lax.fori_loop(0, n // 2, body, 0)

    lax.fori_loop(0, n // 2, feed_arriving, 0)
    gather_sent(second, 2)
    hop_third(1, 3)
    third_grad(0)
    feed_third(1)
    hop_third(2, 3)
    sum_start(
        1, d_gu, lambda left: dot_nt(left, w_gu[...]),
        lambda place: feed(thirds - 1, rows(place, 2 * block)))
    third_grad(1)
    third_grad(2)
    d_second = sum_finish(1)

    def norm_back(value, gain, grad):
        inv = lax.rsqrt(jnp.mean(value * value, -1, keepdims=True) + epsilon)
        weighted = grad * gain
        inner = jnp.mean(weighted * value, -1, keepdims=True)
        result = inv * weighted - value * (inv * inv * inv * inner)
        return result, jnp.sum(grad * value * inv, 0, keepdims=True)

    gain_own[...] = jnp.zeros_like(gain_own)
    part, gain_own[1:2, :] = norm_back(middle[...], fg_ref[...], d_second)
    d_mid = dy_ref[...].astype(f32) + part
    d_middle[...] = d_mid
    drain(in_plane)
    dmid[rows(c, block)] = d_mid.astype(bf16)
    gather_start(dmid, 3)
    drain(weight_sends)
    grad_near(0)

    dk_acc[...] = jnp.zeros_like(dk_acc)
    dv_acc[...] = jnp.zeros_like(dv_acc)

    def attend_back(slot, q_sum):
        gather_step(dmid, 3, slot)
        place = chip(slot)
        at = rows(place, 2 * block)
        d_mix = dot_nt(w_out[...], dmid[at])
        dmid_t[:, at] = dmid[at].T
        d_mix_t = jnp.concatenate([d_mix[h * head:(h + 1) * head] for h in range(group)], 1)
        d_mix_t = (d_mix_t.astype(bf16).astype(f32) * sums[place]).astype(bf16)
        delta = jnp.sum(d_mix_t.astype(f32) * mixed_t[place], 0, keepdims=True)
        weight = probs[place]
        d_prob = dot(values[...], d_mix_t)
        d_score = (weight.astype(f32) * (d_prob - delta)).astype(bf16)
        d_query = dot(keys_t[...], d_score) * scale
        for h in range(group):
            grad = turn_back(d_query[:, 2 * h * block:2 * (h + 1) * block].T, at)
            part, gain_part = norm_back(raw[at, h * head:(h + 1) * head], qg_ref[...], grad)
            d_qkv[at, h * head:(h + 1) * head] = part.astype(bf16)
            q_sum = q_sum + gain_part
        pl.when(slot == 2)(lambda: grad_near(1))
        dv_acc[...] += dot(weight, d_mix_t.T)
        dk_acc[...] += dot(d_score, stack(queries, at))
        return q_sum

    zero = jnp.zeros((1, head), f32)
    gain_own[2:3, 0:head] = lax.fori_loop(0, n // 2, attend_back, zero)
    gather_sent(dmid, 3)
    weight_grad(3, [(dmid_t, lambda: mixed_low[...])])
    grad_far(0)
    drain(in_plane)
    sum_start(2, hidden, lambda left: dot(left, w_down[...]))

    def project_back(i, k_sum):
        at = rows(i, 2 * block)
        grad = turn_back(dk_acc[at] * (1.0 / log2e), at)
        part, gain_part = norm_back(raw[at, qw:qw + kw], kg_ref[...], grad)
        d_qkv[at, qw:qw + kw] = part.astype(bf16)
        d_qkv[at, qw + kw:] = dv_acc[at].astype(bf16)
        return k_sum + gain_part

    gain_own[3:4, 0:head] = lax.fori_loop(0, n // 2, project_back, zero)

    weight_grad(4, [(first_t, lambda: d_qkv[...])])
    grad_far(1)
    grad_near(2)
    hand_out(0)
    sum_start(3, d_qkv, lambda left: dot_nt(left, w_qkv[...]))
    grad_far(2)
    grad_near(3)
    grad_near_far(4)
    out_ref[...] = (middle[...] + sum_finish(2)).astype(bf16)
    hand_out(1)
    grad_far(3)
    grad_near_inner(4)
    grad_far(4)
    x_part, gain_own[0:1, :] = norm_back(x_ref[...].astype(f32), ag_ref[...], sum_finish(3))
    dx_ref[...] = d_middle[...] + x_part

    def gain_plane_copy(j):
        return remote(gain_own, gain_plane.at[c], gp_send.at[j], gp_recv.at[j], partner(j), z)

    def gain_copy(d):
        return remote(gain_all.at[z], gain_all.at[z], gz_send.at[d], gz_recv.at[d], c, lax.rem(z + d, planes))

    for j in range(1, n):
        launch(in_plane, lambda j=j: gain_plane_copy(j))
    gain_plane[c] = gain_own[...]
    hand_out(2)
    for j in range(1, n):
        gain_plane_copy(j).wait_recv()
    total = gain_plane[0]
    for i in range(1, n):
        total = total + gain_plane[i]
    gain_all[z] = total
    for d in range(1, planes):
        launch(along, lambda d=d: gain_copy(d))
    hand_out(3)
    for d in range(1, planes):
        origin = gain_all.at[lax.rem(z + planes - d, planes)]
        remote(origin, origin, gz_send.at[d], gz_recv.at[d], c, z).wait_recv()
    total = gain_all[0]
    for i in range(1, planes):
        total = total + gain_all[i]
    gains_ref[...] = total

    for m in range(4):
        hand_receive(m)
    drain(in_plane)
    hand_out(4)
    drain(along)
    hand_receive(4)
    drain(in_plane)


def finish_kernel(
    n, head, out_in, dx_in, gains_in, got_a, got_b, got_c, got_out, got_qkv,
    out_ref, dx_ref, ag_ref, q_ref, k_ref, v_ref, qg_ref, kg_ref, o_ref, fg_ref, g_ref, u_ref, d_ref,
):
    out_ref[...] = out_in[...]
    dx_ref[...] = dx_in[...]
    ag_ref[...] = gains_in[0:1, :]
    fg_ref[...] = gains_in[1:2, :]
    qg_ref[...] = gains_in[2:3, 0:head]
    kg_ref[...] = gains_in[3:4, 0:head]
    qw, kw = q_ref.shape[1] // n, k_ref.shape[1] // n
    pw = got_a.shape[2] // 3
    thirds = (got_a, got_b, got_c)
    for i in range(n):
        q_ref[:, i * qw:(i + 1) * qw] = got_qkv[i, :, 0:qw].astype(f32)
        k_ref[:, i * kw:(i + 1) * kw] = got_qkv[i, :, qw:qw + kw].astype(f32)
        v_ref[:, i * kw:(i + 1) * kw] = got_qkv[i, :, qw + kw:].astype(f32)
        o_ref[:, i * qw:(i + 1) * qw] = got_out[i].astype(f32)
        for t, got in enumerate(thirds):
            plane, unit = hidden_block(i, t)
            at = plane * (g_ref.shape[1] // 4) + unit * pw
            g_ref[:, at:at + pw] = got[i, :, 0:pw].astype(f32)
            u_ref[:, at:at + pw] = got[i, :, pw:2 * pw].astype(f32)
            d_ref[:, at:at + pw] = got[i, :, 2 * pw:].astype(f32)


def plane_device(
    layer_input,
    token_positions,
    attention_gain,
    query_weight,
    key_matrix,
    value_matrix,
    query_gain,
    key_norm_gain,
    output_weight,
    feedforward_gain,
    gate_weight,
    up_weight,
    down_weight,
    out_cotangent,
):
    n = lax.axis_size("ctx")
    planes = lax.axis_size("fsdp")
    block, width = layer_input.shape[1:]
    length = token_positions.shape[1]
    head = query_gain.shape[0]
    qw = query_weight.shape[1] // n
    kw = key_matrix.shape[1] // n
    fw = gate_weight.shape[1] // n
    group = qw // head
    per = block // planes
    half = head // 2
    inverse = np.power(rope_base, -np.arange(half) * 2.0 / head).astype(np.float32)
    inverse = np.concatenate([inverse, inverse])[None]
    steps = np.arange(block // 2)[:, None] * inverse.astype(np.float64)
    step_cos, step_sin = (jnp.asarray(f(steps).astype(np.float32)) for f in (np.cos, np.sin))
    inverse = jnp.asarray(inverse)
    vmem = pl.BlockSpec(memory_space=pltpu.VMEM)
    hbm = pl.BlockSpec(memory_space=pl.ANY)
    dma = pltpu.SemaphoreType.DMA
    sizes = (fw, fw, fw, qw, qw + 2 * kw)
    low = lambda *shape: pltpu.VMEM(shape, bf16)
    wide = lambda *shape: pltpu.VMEM(shape, f32)
    scratch = [
        low(width, qw + 2 * kw), low(width, 2 * fw), low(qw, width), low(fw, width),
        low(planes * (output_weight.shape[0] // n), width),
        low(length, width), low(length, width), low(length, width),
        low(width, length), low(width, length), low(width, length),
        wide(length, head), wide(length, head), wide(length, head),
        wide(length, qw + kw), low(length, qw), low(length, kw), low(length, kw),
        low(kw, length), low(kw, length), low(n // 2, length, 2 * group * block), wide(n // 2, 1, 2 * group * block),
        wide(n // 2, head, 2 * group * block), low(length, qw),
        low(length, fw), low(length, 2 * fw), low(length, qw + 2 * kw),
        wide(length, kw), wide(length, kw),
    ]
    scratch += [low(planes, n, per, size) for size in sizes]
    scratch += [low(planes + 1, n, per, size) for size in sizes]
    scratch += [low(2, 4, block, width) for _ in range(4)] + [wide(2, block, width), wide(2, block, width)]
    scratch += [
        wide(block, width), wide(block, width), wide(8, width), wide(n, 8, width), wide(planes, 8, width),
        dma((13,)), dma((8, 6)), dma((8, planes)), dma((1, 7)), dma((1, 4)),
        dma((4, n)), dma((4, n)), dma((4, 4)), dma((4, 4)), dma((4, 4)), dma((4, 4)),
        dma((5, planes)), dma((5, planes + 1)), dma((5, n)), dma((5, n)), dma((n,)), dma((n,)),
        dma((planes,)), dma((planes,)),
    ]
    shapes = [
        jax.ShapeDtypeStruct((block, width), bf16),
        jax.ShapeDtypeStruct((block, width), f32),
        jax.ShapeDtypeStruct((8, width), f32),
    ] + [jax.ShapeDtypeStruct((n, per, size), bf16) for size in sizes]
    results = pl.pallas_call(
        functools.partial(layer_kernel, n, planes, block, head, group, fw),
        out_shape=shapes,
        in_specs=[vmem] * 10 + [hbm] * 7,
        out_specs=[vmem] * len(shapes),
        scratch_shapes=scratch,
        compiler_params=pltpu.CompilerParams(
            collective_id=0, has_side_effects=True, vmem_limit_bytes=60 * 1024 * 1024),
    )(
        layer_input[0], out_cotangent[0], token_positions, inverse, step_cos, step_sin,
        attention_gain[None], feedforward_gain[None], query_gain[None], key_norm_gain[None],
        query_weight, key_matrix, value_matrix, output_weight, gate_weight, up_weight, down_weight,
    )
    plain = lambda rows, columns, kind=f32: jax.ShapeDtypeStruct((rows, columns), kind)
    finals = [
        plain(block, width, bf16), plain(block, width), plain(1, width),
        plain(per, n * qw), plain(per, n * kw), plain(per, n * kw), plain(1, head), plain(1, head),
        plain(per, n * qw), plain(1, width), plain(per, n * fw), plain(per, n * fw), plain(per, n * fw),
    ]
    done = pl.pallas_call(
        functools.partial(finish_kernel, n, head),
        out_shape=finals,
        in_specs=[vmem] * len(shapes),
        out_specs=[vmem] * len(finals),
    )(*results)
    out, dx, ag, q, k, v, qg, kg, o, fg, g, u, d = done
    return out[None], dx[None], ag[0], q, k, v, qg[0], kg[0], o.T, fg[0], g, u, d.T


def solution(mesh):
    in_specs = (
        P("fsdp", "ctx", None),
        P("fsdp", None),
        P(),
        P("fsdp", None),
        P("fsdp", None),
        P("fsdp", None),
        P(),
        P(),
        P("fsdp", None),
        P(),
        P("fsdp", None),
        P("fsdp", None),
        P("fsdp", None),
        P("fsdp", "ctx", None),
    )
    out_specs = (
        P("fsdp", "ctx", None),
        P("fsdp", "ctx", None),
        P(),
        P(("ctx", "fsdp"), None),
        P(("ctx", "fsdp"), None),
        P(("ctx", "fsdp"), None),
        P(),
        P(),
        P(None, ("ctx", "fsdp")),
        P(),
        P(("ctx", "fsdp"), None),
        P(("ctx", "fsdp"), None),
        P(None, ("ctx", "fsdp")),
    )

    def run(*arguments):
        n, planes = mesh.shape["ctx"], mesh.shape["fsdp"]
        key_heads = arguments[4].shape[1] // arguments[6].shape[0]
        whole_heads = n == 8 and planes == 4 and key_heads == n
        return jax.shard_map(
            plane_device if whole_heads else on_device,
            mesh=mesh, in_specs=in_specs, out_specs=out_specs, check_vma=False,
        )(*arguments)

    return run
```

```python
import functools

import jax
import jax.numpy as jnp
import numpy as np
from jax import lax
from jax.experimental import pallas as pl
from jax.experimental.pallas import tpu as pltpu
from jax.sharding import PartitionSpec as P

epsilon = 1e-06
rope_base = 1000000.0
masked_score = -1e30


def from_behind(block, axis, distance):
    devices = range(lax.axis_size(axis))
    route = [((i - distance) % len(devices), i) for i in devices]
    return lax.ppermute(block, axis, route)


def rotate(value_rows):
    half = value_rows.shape[-1] // 2
    return jnp.concatenate([-value_rows[..., half:], value_rows[..., :half]], -1)


def rotate_back(value_rows):
    half = value_rows.shape[-1] // 2
    return jnp.concatenate([value_rows[..., half:], -value_rows[..., :half]], -1)


def rope_tables(token_offsets, head_size):
    half = head_size // 2
    inverse = rope_base ** (-(jnp.arange(half).astype(jnp.float32) * 2.0) / head_size)
    angles = token_offsets.astype(jnp.float32)[:, None] * inverse[None, :]
    cosine = jnp.cos(angles)
    sine = jnp.sin(angles)
    return (jnp.concatenate([cosine, cosine], -1), jnp.concatenate([sine, sine], -1))


def norm_scale(value_rows):
    return lax.rsqrt(jnp.mean(value_rows * value_rows, -1, keepdims=True) + epsilon)


def norm_back(value_rows, scale, gain, grad):
    weighted = grad * gain
    inner = jnp.mean(weighted * value_rows, -1, keepdims=True)
    result = scale * weighted - value_rows * scale * scale * scale * inner
    gain_part = jnp.sum((grad * value_rows * scale).reshape(-1, gain.shape[0]), 0)
    return (result, gain_part)


def row_products(left, pieces):
    return tuple((jnp.dot(left, piece, preferred_element_type=jnp.float32) for piece in pieces))


def column_products(rights, pieces):
    total = jnp.einsum("tc,rc->tr", rights[0], pieces[0], preferred_element_type=jnp.float32)
    for right, piece in zip(rights[1:], pieces[1:]):
        total = total + jnp.einsum("tc,rc->tr", right, piece, preferred_element_type=jnp.float32)
    return total


def on_device(
    layer_input,
    token_positions,
    attention_gain,
    query_weight,
    key_matrix,
    value_matrix,
    query_gain,
    key_norm_gain,
    output_weight,
    feedforward_gain,
    gate_weight,
    up_weight,
    down_weight,
    out_cotangent,
):
    hidden_in = layer_input[0].astype(jnp.float32)
    count = hidden_in.shape[0]
    head_size = query_gain.shape[0]
    query_width = query_weight.shape[1]
    key_width = key_matrix.shape[1]
    inner_width = gate_weight.shape[1]
    heads = query_width // head_size
    key_heads = key_width // head_size
    group = heads // key_heads
    scale = head_size ** (-0.5)
    cycles = lax.axis_size("ctx")
    own_index = lax.axis_index("ctx")
    sequence_pos = token_positions[0]
    token_offsets = lax.dynamic_slice_in_dim(sequence_pos, own_index * count, count)
    cosine, sine = rope_tables(token_offsets, head_size)
    cosine = cosine[:, None, :]
    sine = sine[:, None, :]
    first_scale = norm_scale(hidden_in)
    first = (hidden_in * first_scale * attention_gain).astype(jnp.bfloat16)
    query_raw, key_unnormed, value_unnormed = row_products(
        first,
        (
            lax.all_gather(query_weight, "fsdp", axis=0, tiled=True),
            lax.all_gather(key_matrix, "fsdp", axis=0, tiled=True),
            lax.all_gather(value_matrix, "fsdp", axis=0, tiled=True),
        ),
    )
    query_heads = query_raw.reshape(count, heads, head_size)
    query_scale = norm_scale(query_heads)
    query_normed = query_heads * query_scale * query_gain
    query_rot = query_normed * cosine + rotate(query_normed) * sine
    query_grouped = (
        query_rot.reshape(count, key_heads, group, head_size)
        .transpose(1, 2, 0, 3)
        .astype(jnp.bfloat16)
    )
    key_heads_raw = key_unnormed.reshape(count, key_heads, head_size)
    key_scale = norm_scale(key_heads_raw)
    key_normed = key_heads_raw * key_scale * key_norm_gain
    key_low = (
        (key_normed * cosine + rotate(key_normed) * sine)
        .reshape(count, key_width)
        .astype(jnp.bfloat16)
    )
    value_low = value_unnormed.astype(jnp.bfloat16)
    rowmax = jnp.full((key_heads, group, count), masked_score, jnp.float32)
    keys_piece = lax.all_gather(key_low, "ctx", axis=0, tiled=True).reshape(
        -1, key_heads, head_size
    )
    values_piece = lax.all_gather(value_low, "ctx", axis=0, tiled=True).reshape(
        -1, key_heads, head_size
    )
    key_pos = sequence_pos
    allowed = token_offsets[:, None] >= key_pos[None, :]
    scores = (
        jnp.einsum("kgtd,skd->kgts", query_grouped, keys_piece, preferred_element_type=jnp.float32)
        * scale
    )
    scores = jnp.where(allowed, scores, masked_score)
    newmax = jnp.maximum(rowmax, jnp.max(scores, -1))
    weights = jnp.where(allowed, jnp.exp(scores - newmax[..., None]), 0.0)
    accum = jnp.einsum(
        "kgts,skd->kgtd",
        weights.astype(jnp.bfloat16),
        values_piece,
        preferred_element_type=jnp.float32,
    )
    rowsum = jnp.sum(weights, -1)
    accum, rowmax, rowsum = (accum, newmax, rowsum)
    normalized = accum / rowsum[..., None]
    logsum = rowmax + jnp.log(rowsum)
    attention_low = (
        normalized.transpose(2, 0, 1, 3).reshape(count, query_width).astype(jnp.bfloat16)
    )
    output_whole = lax.all_gather(output_weight, "fsdp", axis=0, tiled=True)
    branch_out = jnp.dot(attention_low, output_whole, preferred_element_type=jnp.float32)
    middle = hidden_in + branch_out
    second_scale = norm_scale(middle)
    second = (middle * second_scale * feedforward_gain).astype(jnp.bfloat16)
    gate, up = row_products(
        second,
        (
            lax.all_gather(gate_weight, "fsdp", axis=0, tiled=True),
            lax.all_gather(up_weight, "fsdp", axis=0, tiled=True),
        ),
    )
    sigmoid_gate = jax.nn.sigmoid(gate)
    silu_gate = gate * sigmoid_gate
    hidden_low = (silu_gate * up).astype(jnp.bfloat16)
    (down_out,) = row_products(
        hidden_low, (lax.all_gather(down_weight, "fsdp", axis=0, tiled=True),)
    )
    layer_output = (middle + down_out).astype(jnp.bfloat16)[None]
    cotangent = out_cotangent[0]
    hidden_grad = column_products(
        (cotangent,), lax.all_gather((down_weight,), "fsdp", axis=0, tiled=True)
    )
    up_low = (hidden_grad * silu_gate).astype(jnp.bfloat16)
    gate_low = (hidden_grad * up * sigmoid_gate * (1.0 + gate * (1.0 - sigmoid_gate))).astype(
        jnp.bfloat16
    )
    second_grad = column_products(
        (gate_low, up_low), lax.all_gather((gate_weight, up_weight), "fsdp", axis=0, tiled=True)
    )
    middle_part, feedforward_part = norm_back(middle, second_scale, feedforward_gain, second_grad)
    middle_grad = cotangent.astype(jnp.float32) + middle_part
    middle_low = middle_grad.astype(jnp.bfloat16)
    attention_grad = jnp.einsum(
        "tc,rc->tr", middle_low, output_whole, preferred_element_type=jnp.float32
    )
    attention_grad_low = attention_grad.astype(jnp.bfloat16)
    mixed_grad = attention_grad_low.reshape(count, key_heads, group, head_size).transpose(
        1, 2, 0, 3
    )
    delta = jnp.sum(mixed_grad.astype(jnp.float32) * normalized, -1)

    def cycle_step(index, carry):
        keys_held, values_held, key_acc, value_acc, query_acc = carry
        anchor = (own_index - index) % cycles
        key_pos = lax.dynamic_slice_in_dim(sequence_pos, anchor * count, count)
        keys_piece = keys_held.astype(jnp.bfloat16).reshape(count, key_heads, head_size)
        values_piece = values_held.astype(jnp.bfloat16).reshape(count, key_heads, head_size)
        allowed = token_offsets[:, None] >= key_pos[None, :]
        scores = (
            jnp.einsum(
                "kgtd,skd->kgts", query_grouped, keys_piece, preferred_element_type=jnp.float32
            )
            * scale
        )
        probs = jnp.where(allowed, jnp.exp(scores - logsum[..., None]), 0.0)
        value_acc = value_acc + jnp.einsum(
            "kgts,kgtd->skd",
            probs.astype(jnp.bfloat16),
            mixed_grad,
            preferred_element_type=jnp.float32,
        ).reshape(count, key_width)
        prob_grad = jnp.einsum(
            "kgtd,skd->kgts", mixed_grad, values_piece, preferred_element_type=jnp.float32
        )
        score_grad = (probs * (prob_grad - delta[..., None])).astype(jnp.bfloat16)
        query_acc = (
            query_acc
            + jnp.einsum(
                "kgts,skd->kgtd", score_grad, keys_piece, preferred_element_type=jnp.float32
            )
            * scale
        )
        key_acc = (
            key_acc
            + jnp.einsum(
                "kgts,kgtd->skd", score_grad, query_grouped, preferred_element_type=jnp.float32
            ).reshape(count, key_width)
            * scale
        )
        moved = (
            from_behind(keys_held.astype(jnp.bfloat16), "ctx", 1).astype(keys_held.dtype),
            from_behind(values_held.astype(jnp.bfloat16), "ctx", 1).astype(values_held.dtype),
            from_behind(key_acc.astype(jnp.bfloat16), "ctx", 1).astype(key_acc.dtype),
            from_behind(value_acc.astype(jnp.bfloat16), "ctx", 1).astype(value_acc.dtype),
        )
        return (moved[0], moved[1], moved[2], moved[3], query_acc)

    start_cycle = (
        key_low.astype(jnp.float32),
        value_low.astype(jnp.float32),
        jnp.zeros((count, key_width), jnp.float32),
        jnp.zeros((count, key_width), jnp.float32),
        jnp.zeros((key_heads, group, count, head_size), jnp.float32),
    )
    cycle_done = lax.fori_loop(0, cycles, cycle_step, start_cycle)
    key_acc = cycle_done[2]
    value_acc = cycle_done[3]
    query_acc = cycle_done[4]
    query_rot_grad = query_acc.transpose(2, 0, 1, 3).reshape(count, heads, head_size)
    query_normed_grad = query_rot_grad * cosine + rotate_back(query_rot_grad * sine)
    query_heads_grad, query_part = norm_back(
        query_heads, query_scale, query_gain, query_normed_grad
    )
    query_low_grad = query_heads_grad.reshape(count, query_width).astype(jnp.bfloat16)
    key_rot_grad = key_acc.reshape(count, key_heads, head_size)
    key_normed_grad = key_rot_grad * cosine + rotate_back(key_rot_grad * sine)
    key_heads_grad, key_part = norm_back(key_heads_raw, key_scale, key_norm_gain, key_normed_grad)
    key_low_grad = key_heads_grad.reshape(count, key_width).astype(jnp.bfloat16)
    value_low_grad = value_acc.astype(jnp.bfloat16)
    first_grad = column_products(
        (query_low_grad, key_low_grad, value_low_grad),
        lax.all_gather((query_weight, key_matrix, value_matrix), "fsdp", axis=0, tiled=True),
    )
    input_part, attention_part = norm_back(hidden_in, first_scale, attention_gain, first_grad)
    input_gradient = (middle_grad + input_part)[None]
    rights_first = jnp.concatenate([query_low_grad, key_low_grad, value_low_grad], 1)
    rights_second = jnp.concatenate([gate_low, up_low], 1)
    pairs = (
        (first, rights_first),
        (second, rights_second),
        (middle_low, attention_low),
        (cotangent, hidden_low),
    )
    parts = []
    for left, right in pairs:
        parts.append(jnp.einsum("tr,tc->rc", left, right, preferred_element_type=jnp.float32))
    sums = lax.psum_scatter(
        jnp.concatenate(parts, 1), ("ctx", "fsdp"), scatter_dimension=0, tiled=True
    )
    edges = [0, query_width, query_width + key_width, query_width + 2 * key_width]
    edges = edges + [edges[3] + inner_width, edges[3] + 2 * inner_width]
    edges = edges + [edges[5] + query_width, edges[5] + query_width + inner_width]
    query_gradient = sums[:, edges[0] : edges[1]]
    key_gradient = sums[:, edges[1] : edges[2]]
    value_gradient = sums[:, edges[2] : edges[3]]
    gate_gradient = sums[:, edges[3] : edges[4]]
    up_gradient = sums[:, edges[4] : edges[5]]
    output_gradient = sums[:, edges[5] : edges[6]].T
    down_gradient = sums[:, edges[6] : edges[7]].T
    attention_total, query_total, key_total, feedforward_total = lax.psum(
        (attention_part, query_part, key_part, feedforward_part), ("ctx", "fsdp")
    )
    return (
        layer_output,
        input_gradient,
        attention_total,
        query_gradient,
        key_gradient,
        value_gradient,
        query_total,
        key_total,
        output_gradient,
        feedforward_total,
        gate_gradient,
        up_gradient,
        down_gradient,
    )


MESH = pl.DeviceIdType.MESH
f32 = jnp.float32
bf16 = jnp.bfloat16


def dot(left, right):
    return jnp.dot(left, right, preferred_element_type=f32)


def dot_nt(left, right):
    return lax.dot_general(left, right, (((1,), (1,)), ((), ())), preferred_element_type=f32)


def dot_tn(left, right):
    return lax.dot_general(left, right, (((0,), (0,)), ((), ())), preferred_element_type=f32)


def hidden_block(device, third):
    def plane(i, t):
        return ((3, 1, 2), (0, 2, 1), (0, 3, 2), (3, 0, 1))[i // 4 * 2 + i % 2][t]

    own = plane(device, third)
    return own, sum(plane(i, t) == own for i in range(device) for t in range(3))


def layer_kernel(
    n, planes, block, head, group, fw,
    x_ref, dy_ref, pos_row, inverse_ref, step_cos, step_sin, ag_ref, fg_ref, qg_ref, kg_ref,
    wq, wk, wv, wo, wg, wu, wd,
    out_ref, dx_ref, gains_ref, got_a, got_b, got_c, got_out, got_q, got_kv,
    w_qkv, w_gu, w_out, w_down, t_out,
    first, dy_all, second, first_t, dy_t, second_t,
    positions, cosine, sine,
    raw, queries, keys, values, keys_t, values_t, probs, sums, mixed_t, mixed_low,
    hidden, d_gu, d_qkv, dk_acc, dv_acc,
    stage_a, stage_b, stage_c, stage_out, stage_q, stage_kv,
    land_a, land_b, land_c, land_out, land_q, land_kv,
    rs_sa, rs_ra, rs_sb, rs_rb, rs_kept, rs_acc,
    middle, d_middle, gain_own, gain_plane, gain_all,
    local_sem, wz_send, wz_recv, hand_send, hand_recv,
    ag_send, ag_recv, ra_send, ra_recv, rb_send, rb_recv,
    zr_send, zr_recv, aa_send, aa_recv, gp_send, gp_recv, gz_send, gz_recv,
):
    c = lax.axis_index("ctx")
    z = lax.axis_index("fsdp")
    dmid = first
    dmid_t = second
    cy, cx, ck = lax.div(c, 4), lax.rem(lax.div(c, 2), 2), lax.rem(c, 2)
    ci = lax.rem(c, 4)
    sign = 1 - 2 * ck
    qw, kw = group * head, head
    pw = 128
    thirds = fw // pw
    width = x_ref.shape[1]
    scale = head ** (-0.5)
    log2e = 1.4426950408889634
    gots = (got_a, got_b, got_c, got_out, got_q, got_kv)
    stages = (stage_a, stage_b, stage_c, stage_out, stage_q, stage_kv)
    lands = (land_a, land_b, land_c, land_out, land_q, land_kv)

    def partner(j):
        y = lax.rem(cy + lax.div(j, 4), 2)
        x = lax.rem(cx + lax.rem(lax.div(j, 2), 2), 2)
        k = lax.rem(ck + lax.rem(j, 2), 2)
        return y * 4 + x * 2 + k

    def chip(slot):
        return lax.rem(cy + lax.div(slot, 2), 2) * 2 + lax.rem(cx + lax.rem(slot, 2), 2)

    def rows(start, size):
        return pl.ds(pl.multiple_of(start * size, size), size)

    def remote(src, dst, send, recv, ctx, plane):
        return pltpu.make_async_remote_copy(
            src_ref=src, dst_ref=dst, send_sem=send, recv_sem=recv,
            device_id={"ctx": ctx, "fsdp": plane}, device_id_type=MESH,
        )

    in_plane, along, weight_sends = [], [], []

    def launch(started, copy, when=None):
        if when is None:
            copy().start()
        else:
            pl.when(when)(lambda: copy().start())
        started.append((copy, when))

    def drain(started):
        for copy, when in started:
            if when is None:
                copy().wait_send()
            else:
                pl.when(when)(lambda copy=copy: copy().wait_send())
        started.clear()

    def pick(values):
        return sum(jnp.where(c == i, value, 0) for i, value in enumerate(values))

    unit_plane = [pick([hidden_block(i, t)[0] for i in range(n)]) for t in range(thirds)]
    unit_block = [pick([hidden_block(i, t)[1] for i in range(n)]) for t in range(thirds)]
    plane_blocks = wd.shape[0] // pw

    own_rows = wq.shape[0]
    out_rows = wo.shape[0] // n

    def own_slices():
        mine = rows(z, own_rows)
        pairs = [
            (wq.at[:, rows(c, qw)], w_qkv.at[mine, 0:qw]),
            (wk.at[:, rows(c, kw)], w_qkv.at[mine, qw:qw + kw]),
            (wv.at[:, rows(c, kw)], w_qkv.at[mine, qw + kw:qw + 2 * kw]),
            (wo.at[rows(c, out_rows)], t_out.at[rows(z, out_rows)]),
        ]
        for t in range(thirds):
            at = 2 * pw * t
            unit = unit_plane[t] * plane_blocks + unit_block[t]
            pairs.append((wg.at[:, rows(unit, pw)], w_gu.at[mine, at:at + pw]))
            pairs.append((wu.at[:, rows(unit, pw)], w_gu.at[mine, at + pw:at + 2 * pw]))
        return pairs

    local = [pltpu.make_async_copy(src, dst, local_sem.at[i]) for i, (src, dst) in enumerate(own_slices())]
    for copy in local:
        copy.start()

    def own_down(t):
        return pltpu.make_async_copy(
            wd.at[rows(unit_block[t], pw)], w_down.at[t * pw:(t + 1) * pw], local_sem.at[4 + 2 * thirds + t])

    holds = [unit_plane[t] == z for t in range(thirds)]
    for t in range(thirds):
        pl.when(holds[t])(lambda t=t: own_down(t).start())

    for land in lands:
        @pl.when(z == 0)
        def _(land=land):
            land[0] = jnp.zeros(land.shape[1:], bf16)

        @pl.when(z == planes - 1)
        def _(land=land):
            land[planes] = jnp.zeros(land.shape[1:], bf16)

    barrier = pltpu.get_barrier_semaphore()
    for j in range(1, n):
        pl.semaphore_signal(barrier, inc=1, device_id={"ctx": partner(j), "fsdp": z}, device_id_type=MESH)
    for d in range(1, planes):
        pl.semaphore_signal(
            barrier, inc=1, device_id={"ctx": c, "fsdp": lax.rem(z + d, planes)}, device_id_type=MESH)
    x = x_ref[...].astype(f32)
    x_scale = lax.rsqrt(jnp.mean(x * x, -1, keepdims=True) + epsilon)
    first[rows(c, block)] = (x * x_scale * ag_ref[...]).astype(bf16)
    dy_all[rows(c, block)] = dy_ref[...]
    for copy in local[:3]:
        copy.wait()
    pl.semaphore_wait(barrier, n + planes - 2)

    def inside(t):
        return jnp.logical_and(t >= 0, t < planes)

    weights = [
        (lambda o: w_qkv.at[rows(o, own_rows)], None),
        (lambda o: t_out.at[rows(o, out_rows)], 0),
    ]
    for t in range(thirds):
        weights.append((lambda o, t=t: w_gu.at[rows(o, own_rows), 2 * pw * t:2 * pw * (t + 1)], None))
        weights.append((lambda o, t=t: w_down.at[t * pw:(t + 1) * pw], None))

    def weight_copy(w, slot, origin, target):
        part = weights[w][0](origin)
        return remote(part, part, wz_send.at[w, slot], wz_recv.at[w, origin], c, target)

    def from_plane(w, origin):
        return origin == unit_plane[(w - 3) // 2] if w >= 3 and w % 2 else None

    def both(one, other):
        return one if other is None else jnp.logical_and(one, other)

    def hand_split(origin, valid):
        mine = 2 * origin + cy == c
        return jnp.logical_and(valid, jnp.logical_not(mine)), jnp.logical_and(valid, mine)

    def weight_start(w):
        for side in range(2):
            d = sign * (1 - 2 * side)
            launch(
                weight_sends, lambda side=side, d=d: weight_copy(w, side, z, z + d),
                both(inside(z + d), from_plane(w, z)))
        if weights[w][1] is not None:
            hand_over(w, z, 0, *hand_split(z, True))

    def hand_target(h):
        return lambda i: w_out.at[rows(i, out_rows)]

    def hand_copy(w, origin, slot):
        h = weights[w][1]
        return remote(
            weights[w][0](origin), hand_target(h)(ci), hand_send.at[h, slot], hand_recv.at[h, ci], 2 * origin + cy, z)

    def hand_over(w, origin, slot, away, here):
        launch(in_plane, lambda: hand_copy(w, origin, slot), away)

        @pl.when(here)
        def _():
            hand_target(weights[w][1])(ci)[...] = weights[w][0](origin)[...]

    def hand_arrive(w):
        h = weights[w][1]
        for i in range(4):
            @pl.when(4 * ck + i != c)
            def _(i=i):
                part = hand_target(h)(i)
                remote(part, part, hand_send.at[h, 0], hand_recv.at[h, i], c, z).wait_recv()

    hops = {}
    for w in range(len(weights)):
        for d in range(1, planes):
            for side, way in enumerate((1, -1)):
                origin = z - way * d
                valid = both(inside(origin), from_plane(w, origin))
                passed = jnp.logical_and(valid, inside(z + way))
                split = None if weights[w][1] is None else hand_split(origin, valid)
                hops[w, d, side] = origin, z + way, valid, passed, split

    def weight_hop(w, d):
        for side in range(2):
            origin, following, valid, passed, split = hops[w, d, side]
            pl.when(valid)(lambda: weight_copy(w, 0, origin, z).wait_recv())
            if d < planes - 1:
                launch(
                    weight_sends,
                    lambda side=side, origin=origin, following=following: weight_copy(
                        w, 2 * d + side, origin, following),
                    passed)
            if split is not None:
                hand_over(w, origin, 2 * d - 1 + side, *split)

    def gather_copy(buf, g, j, send, origin, target):
        part = buf.at[rows(origin, block)]
        return remote(part, part, ag_send.at[g, send], ag_recv.at[g, j], target, z)

    def gather_start(buf, g):
        for j in (1, 2 + 2 * ck, 4 - 2 * ck):
            launch(in_plane, lambda j=j: gather_copy(buf, g, j, j, c, partner(j)))

    def gather_half(buf, g, j):
        half = block // 2
        part = buf.at[pl.ds(pl.multiple_of(partner(j) * block + (half if j == 2 else 0), half), half)]
        at = 0 if j == 2 else 6
        return remote(part, part, ag_send.at[g, at], ag_recv.at[g, at], partner(6 - j), z)

    def gather_diagonal(buf, g):
        half = block // 2
        for at in (6, 0):
            part = buf.at[pl.ds(pl.multiple_of(partner(6) * block + (0 if at == 6 else half), half), half)]
            remote(part, part, ag_send.at[g, at], ag_recv.at[g, at], c, z).wait_recv()

    def gather_forward(buf, g, j):
        return gather_copy(buf, g, j + 1, j + 1, partner(j), partner(1))

    def gather_take(buf, g, j):
        if j == 6:
            gather_diagonal(buf, g)
        else:
            gather_copy(buf, g, j, j, partner(j), c).wait_recv()
            gather_half(buf, g, j).start()
        gather_forward(buf, g, j).start()

    def gather_sent(buf, g):
        for j in (2, 4, 6):
            in_plane.append((lambda j=j: gather_forward(buf, g, j), None))
            if j < 6:
                in_plane.append((lambda j=j: gather_half(buf, g, j), None))

    def gather_finish(buf, g):
        for j in (2, 4, 6):
            gather_take(buf, g, j)
        gather_sent(buf, g)
        for j in (1, 3, 5, 7):
            gather_copy(buf, g, j, j, partner(j), c).wait_recv()

    def gather_step(buf, g, slot):
        @pl.when(slot == 1)
        def _():
            gather_take(buf, g, 2)
            gather_take(buf, g, 4)

        pl.when(slot == 3)(lambda: gather_take(buf, g, 6))
        gather_copy(buf, g, 2 * slot + 1, 0, partner(2 * slot + 1), c).wait_recv()

    def sum_pair_copy(s, slot):
        return remote(rs_sa.at[s % 2, slot], rs_ra.at[s % 2, slot], ra_send.at[s, slot], ra_recv.at[s, slot], partner(1), z)

    def sum_chip_copy(s, slot):
        return remote(
            rs_sb.at[s % 2, slot], rs_rb.at[s % 2, slot], rb_send.at[s, slot], rb_recv.at[s, slot], partner(2 * slot), z)

    def sum_half_copy(s, slot):
        half = block // 2
        at = pl.ds(pl.multiple_of((slot - 1) * half, half), half)
        return remote(
            rs_sb.at[s % 2, 3, at], rs_rb.at[s % 2, 3, at], rb_send.at[s, 6 - 3 * slot], rb_recv.at[s, 6 - 3 * slot],
            partner(6 - 2 * slot), z)

    def sum_slot(p):
        return jnp.where(p == 0, 3, jnp.where(p == 1, 2 - ck, jnp.where(p == 2, 1 + ck, 0)))

    def sum_start(s, left, partial, prepare=None, ready=None, during=()):
        if prepare is not None:
            prepare(chip(sum_slot(0)))
        if ready is not None:
            ready()

        def body(p, carry):
            slot = sum_slot(p)
            at = [rows(partner(2 * slot + 1), block), rows(partner(2 * slot), block)]
            both = partial(jnp.concatenate([left[i] for i in at], 0))
            rs_sa[s % 2, slot] = both[:block].astype(bf16)
            sum_pair_copy(s, slot).start()
            rs_kept[lax.rem(p, 2)] = both[block:]

            @pl.when(p > 0)
            def _():
                before = sum_slot(p - 1)
                sum_pair_copy(s, before).wait_recv()
                rs_sb[s % 2, before] = (
                    rs_kept[lax.rem(p + 1, 2)] + rs_ra[s % 2, before].astype(f32)).astype(bf16)

            @pl.when(p == 1)
            def _():
                sum_half_copy(s, 1).start()
                sum_half_copy(s, 2).start()

            @pl.when(p > 1)
            def _():
                before = sum_slot(p - 1)
                half = block // 2
                at = pl.ds(pl.multiple_of((before - 1) * half, half), half)
                sum_half_copy(s, before).wait_recv()
                rs_sb[s % 2, before, at] = (
                    rs_sb[s % 2, before, at].astype(f32) + rs_rb[s % 2, 3, at].astype(f32)).astype(bf16)
                sum_chip_copy(s, before).start()

            if prepare is not None:
                @pl.when(p < 3)
                def _():
                    prepare(chip(sum_slot(p + 1)))

            for k, poll in enumerate(during):
                pl.when(p == k)(poll)
            return carry

        lax.fori_loop(0, 4, body, 0)
        for slot in range(4):
            in_plane.append((lambda slot=slot: sum_pair_copy(s, slot), None))
        for slot in (1, 2):
            in_plane.append((lambda slot=slot: sum_half_copy(s, slot), None))
            in_plane.append((lambda slot=slot: sum_chip_copy(s, slot), None))
        sum_pair_copy(s, 0).wait_recv()
        rs_acc[s % 2] = rs_kept[1] + rs_ra[s % 2, 0].astype(f32)

    def sum_finish(s):
        total = rs_acc[s % 2]
        for slot in (1, 2):
            sum_chip_copy(s, slot).wait_recv()
            total = total + rs_rb[s % 2, slot].astype(f32)
        return total

    per = block // planes

    at_edge = jnp.logical_or(z == 0, z == planes - 1)
    edge_targets = [jnp.where(z == 0, planes - 1 - k, k) for k in range(planes - 1)]

    def weight_grad(m, parts):
        def body(i, carry):
            at = 0
            for left, right in parts:
                value = right()
                grad = dot(left[rows(i, 4 * block)], value)
                for k in range(4):
                    for t in range(planes):
                        start = k * block + t * per
                        stages[m][t, 4 * i + k, :, at:at + value.shape[1]] = grad[start:start + per].astype(bf16)
                at += value.shape[1]
            return carry

        lax.fori_loop(0, n // 4, body, 0)
        for t in edge_targets:
            launch(along, lambda t=t: grad_copy(m, t), at_edge)

    def grad_copy(m, t):
        way = jnp.where(z < t, 1, -1)
        last = z + way == t
        slot = jnp.where(jnp.logical_and(last, way < 0), planes, t)
        return remote(
            stages[m].at[t], lands[m].at[slot], zr_send.at[m, t], zr_recv.at[m, slot], c, z + way)

    def grad_arrive(m, slot):
        part = lands[m].at[slot]
        remote(part, part, zr_send.at[m, 0], zr_recv.at[m, slot], c, z).wait_recv()

    def grad_pass(m, t, valid):
        @pl.when(valid)
        def _():
            grad_arrive(m, t)

            def body(i, carry):
                stages[m][t, i] = (stages[m][t, i].astype(f32) + lands[m][t, i].astype(f32)).astype(bf16)
                return carry

            lax.fori_loop(0, n, body, 0)

        launch(along, lambda: grad_copy(m, t), valid)

    is_low, is_high = z == 1, z == planes - 2

    def grad_near_far(m):
        grad_pass(m, 3, is_low)
        grad_pass(m, 0, is_high)

    def grad_near_inner(m):
        grad_pass(m, 2, is_low)
        grad_pass(m, 1, is_high)

    def grad_near(m):
        grad_near_far(m)
        grad_near_inner(m)

    def grad_far(m):
        grad_pass(m, 3, is_high)
        grad_pass(m, 0, is_low)

    def owner_copy(m, j):
        return remote(lands[m].at[z, partner(j)], gots[m].at[c], aa_send.at[m, j], aa_recv.at[m, j], partner(j), z)

    def hand_out(m):
        pl.when(z > 0)(lambda: grad_arrive(m, z))
        pl.when(z < planes - 1)(lambda: grad_arrive(m, planes))

        def body(i, carry):
            total = stages[m][z, i].astype(f32) + lands[m][z, i].astype(f32) + lands[m][planes, i].astype(f32)
            lands[m][z, i] = total.astype(bf16)
            return carry

        lax.fori_loop(0, n, body, 0)
        for j in (2 + 2 * ck, 3 + 2 * ck, 4 - 2 * ck, 5 - 2 * ck, 6, 7, 1):
            launch(in_plane, lambda j=j: owner_copy(m, j))
        gots[m][c] = lands[m][z, c]

    def hand_receive(m):
        for j in range(1, n):
            owner_copy(m, j).wait_recv()

    weight_start(0)
    gather_start(first, 0)
    for copy in local[3:]:
        copy.wait()
    for t in range(thirds):
        pl.when(holds[t])(lambda t=t: own_down(t).wait())

    spread = jnp.broadcast_to(pos_row[...].astype(f32), (head, pos_row.shape[1]))
    positions[...] = spread.T
    side = jnp.where(lax.broadcasted_iota(jnp.int32, (1, head), 1) < head // 2, -1.0, 1.0)

    def table(i, carry):
        run = step_cos.shape[0]
        at = rows(i, run)
        start = positions[pl.ds(pl.multiple_of(i * run, run), 1)] * inverse_ref[...]
        start_cos, start_sin = jnp.cos(start), jnp.sin(start)
        cosine[at] = start_cos * step_cos[...] - start_sin * step_sin[...]
        sine[at] = (start_sin * step_cos[...] + start_cos * step_sin[...]) * side
        return carry

    def turn_over(src, dst):
        def body(i, carry):
            at = rows(i, block)
            dst[:, at] = src[at].T
            return carry

        lax.fori_loop(0, n, body, 0)

    lax.fori_loop(0, 2 * n, table, 0)
    weight_hop(0, 1)
    gather_finish(first, 0)
    weight_hop(0, 2)
    weight_start(1)
    gather_start(dy_all, 1)
    turn_over(first, first_t)
    weight_hop(0, 3)
    weight_start(2)
    weight_start(3)

    def turn(value, at):
        return value * cosine[at] + pltpu.roll(value, head // 2, 1) * sine[at]

    def turn_back(grad, at):
        return grad * cosine[at] - pltpu.roll(grad, head // 2, 1) * sine[at]

    def project(i, carry):
        at = rows(i, 2 * block)
        result = dot(first[at], w_qkv[...])
        raw[at] = result[:, :qw + kw]
        low_values = result[:, qw + kw:].astype(bf16)
        values[at] = low_values
        values_t[:, at] = low_values.T
        for h in range(group + 1):
            part = result[:, h * head:(h + 1) * head]
            inv = lax.rsqrt(jnp.mean(part * part, -1, keepdims=True) + epsilon)
            gain = qg_ref[...] if h < group else kg_ref[...]
            turned = turn(part * inv * gain, at)
            if h < group:
                queries[at, h * head:(h + 1) * head] = (turned * (scale * log2e)).astype(bf16)
            else:
                low_keys = turned.astype(bf16)
                keys[at] = low_keys
                keys_t[:, at] = low_keys.T
        return carry

    lax.fori_loop(0, n // 4, project, 0)
    weight_hop(1, 1)
    lax.fori_loop(n // 4, n // 2, project, 0)
    weight_hop(1, 2)
    gather_finish(dy_all, 1)

    def stack(ref, at):
        return jnp.concatenate([ref[at, h * head:(h + 1) * head] for h in range(group)], 0)

    def attend(place):
        at = rows(place, 2 * block)
        scores = dot_nt(keys[...], stack(queries, at))
        allowed = positions[...] <= pos_row[:, rows(2 * place, block)].astype(f32)
        later = positions[...] <= pos_row[:, rows(2 * place + 1, block)].astype(f32)
        weight = jnp.concatenate(
            [jnp.exp2(jnp.where(later if k % 2 else allowed, scores[:, k * block:(k + 1) * block], masked_score))
             for k in range(2 * group)], 1)
        inv = 1.0 / jnp.sum(weight, 0, keepdims=True)
        low_weight = weight.astype(bf16)
        probs[place] = low_weight
        sums[place] = inv
        result = dot(values_t[...], low_weight) * inv
        mixed_t[place] = result
        for h in range(group):
            mixed_low[at, h * head:(h + 1) * head] = result[:, 2 * h * block:2 * (h + 1) * block].T.astype(bf16)

    def output_ready():
        weight_hop(1, 3)
        weight_start(4)
        weight_start(5)
        hand_arrive(1)
        drain(in_plane)

    def hop_third(t, d):
        weight_hop(2 + 2 * t, d)
        weight_hop(3 + 2 * t, d)

    sum_start(
        0, mixed_low, lambda left: dot(left, w_out[...]), attend, output_ready,
        (lambda: hop_third(0, 1), lambda: hop_third(0, 2), lambda: hop_third(1, 1)))
    weight_start(6)
    weight_start(7)
    hop_third(0, 3)
    turn_over(dy_all, dy_t)
    hop_third(1, 2)
    mid = x_ref[...].astype(f32) + sum_finish(0)
    middle[...] = mid
    mid_scale = lax.rsqrt(jnp.mean(mid * mid, -1, keepdims=True) + epsilon)
    second[rows(c, block)] = (mid * mid_scale * fg_ref[...]).astype(bf16)
    gather_start(second, 2)
    hop_third(2, 1)

    def feed(t, at):
        units, pair = slice(t * pw, (t + 1) * pw), 2 * pw * t
        both = dot(second[at], w_gu[:, pair:pair + 2 * pw])
        back = dot_nt(dy_all[at], w_down[units])
        gate, up = both[:, :pw], both[:, pw:]
        sig = 1.0 / (1.0 + jnp.exp(-gate))
        silu = gate * sig
        hidden[at, units] = (silu * up).astype(bf16)
        d_gu[at, pair:pair + pw] = (back * up * sig * (1.0 + gate * (1.0 - sig))).astype(bf16)
        d_gu[at, pair + pw:pair + 2 * pw] = (back * silu).astype(bf16)

    def feed_arriving(slot, carry):
        gather_step(second, 2, slot)
        at = rows(chip(slot), 2 * block)
        feed(0, at)
        second_t[:, at] = second[at].T
        pl.when(slot == 2)(lambda: hop_third(2, 2))
        return carry

    def third_grad(t):
        weight_grad(t, [
            (second_t, lambda: d_gu[:, 2 * pw * t:2 * pw * (t + 1)]),
            (dy_t, lambda: hidden[:, t * pw:(t + 1) * pw]),
        ])

    def feed_third(t):
        def body(i, carry):
            feed(t, rows(i, 2 * block))
            return carry

        lax.fori_loop(0, n // 2, body, 0)

    lax.fori_loop(0, n // 2, feed_arriving, 0)
    gather_sent(second, 2)
    hop_third(1, 3)
    third_grad(0)
    feed_third(1)
    hop_third(2, 3)
    sum_start(
        1, d_gu, lambda left: dot_nt(left, w_gu[...]),
        lambda place: feed(thirds - 1, rows(place, 2 * block)))
    third_grad(1)
    third_grad(2)
    d_second = sum_finish(1)

    def norm_back(value, gain, grad):
        inv = lax.rsqrt(jnp.mean(value * value, -1, keepdims=True) + epsilon)
        weighted = grad * gain
        inner = jnp.mean(weighted * value, -1, keepdims=True)
        result = inv * weighted - value * (inv * inv * inv * inner)
        return result, jnp.sum(grad * value * inv, 0, keepdims=True)

    gain_own[...] = jnp.zeros_like(gain_own)
    part, gain_own[1:2, :] = norm_back(middle[...], fg_ref[...], d_second)
    d_mid = dy_ref[...].astype(f32) + part
    d_middle[...] = d_mid
    drain(in_plane)
    dmid[rows(c, block)] = d_mid.astype(bf16)
    gather_start(dmid, 3)
    sum_start(2, hidden, lambda left: dot(left, w_down[...]))
    drain(weight_sends)
    grad_near(0)

    dk_acc[...] = jnp.zeros_like(dk_acc)
    dv_acc[...] = jnp.zeros_like(dv_acc)

    def attend_back(slot, q_sum):
        gather_step(dmid, 3, slot)
        place = chip(slot)
        at = rows(place, 2 * block)
        d_mix = dot_nt(w_out[...], dmid[at])
        dmid_t[:, at] = dmid[at].T
        pl.when(slot == 3)(lambda: weight_grad(3, [(dmid_t, lambda: mixed_low[...])]))
        d_mix_t = jnp.concatenate([d_mix[h * head:(h + 1) * head] for h in range(group)], 1)
        d_mix_t = (d_mix_t.astype(bf16).astype(f32) * sums[place]).astype(bf16)
        delta = jnp.sum(d_mix_t.astype(f32) * mixed_t[place], 0, keepdims=True)
        weight = probs[place]
        d_prob = dot(values[...], d_mix_t)
        d_score = (weight.astype(f32) * (d_prob - delta)).astype(bf16)
        d_query = dot(keys_t[...], d_score) * scale
        for h in range(group):
            grad = turn_back(d_query[:, 2 * h * block:2 * (h + 1) * block].T, at)
            part, gain_part = norm_back(raw[at, h * head:(h + 1) * head], qg_ref[...], grad)
            d_qkv[at, h * head:(h + 1) * head] = part.astype(bf16)
            q_sum = q_sum + gain_part
        pl.when(slot == 2)(lambda: grad_near(1))
        dv_acc[...] += dot(weight, d_mix_t.T)
        dk_acc[...] += dot(d_score, stack(queries, at))
        return q_sum

    zero = jnp.zeros((1, head), f32)
    gain_own[2:3, 0:head] = lax.fori_loop(0, n // 2, attend_back, zero)
    gather_sent(dmid, 3)
    weight_grad(4, [(first_t, lambda: d_qkv[:, :qw])])
    grad_far(0)

    def project_back(i, k_sum):
        at = rows(i, 2 * block)
        grad = turn_back(dk_acc[at] * (1.0 / log2e), at)
        part, gain_part = norm_back(raw[at, qw:qw + kw], kg_ref[...], grad)
        d_qkv[at, qw:qw + kw] = part.astype(bf16)
        d_qkv[at, qw + kw:] = dv_acc[at].astype(bf16)
        return k_sum + gain_part

    gain_own[3:4, 0:head] = lax.fori_loop(0, n // 2, project_back, zero)

    weight_grad(5, [(first_t, lambda: d_qkv[:, qw:])])
    grad_far(1)
    grad_near(2)
    hand_out(0)
    drain(in_plane)
    sum_start(3, d_qkv, lambda left: dot_nt(left, w_qkv[...]))
    grad_far(2)
    grad_near(3)
    hand_out(1)
    grad_far(3)
    grad_near(4)
    out_ref[...] = (middle[...] + sum_finish(2)).astype(bf16)
    grad_far(4)
    grad_near_far(5)
    hand_out(2)
    grad_near_inner(5)
    grad_far(5)
    x_part, gain_own[0:1, :] = norm_back(x_ref[...].astype(f32), ag_ref[...], sum_finish(3))
    dx_ref[...] = d_middle[...] + x_part

    def gain_plane_copy(j):
        return remote(gain_own, gain_plane.at[c], gp_send.at[j], gp_recv.at[j], partner(j), z)

    def gain_copy(d):
        return remote(gain_all.at[z], gain_all.at[z], gz_send.at[d], gz_recv.at[d], c, lax.rem(z + d, planes))

    for j in range(1, n):
        launch(in_plane, lambda j=j: gain_plane_copy(j))
    gain_plane[c] = gain_own[...]
    hand_out(3)
    for j in range(1, n):
        gain_plane_copy(j).wait_recv()
    total = gain_plane[0]
    for i in range(1, n):
        total = total + gain_plane[i]
    gain_all[z] = total
    for d in range(1, planes):
        launch(along, lambda d=d: gain_copy(d))
    hand_out(4)
    for d in range(1, planes):
        origin = gain_all.at[lax.rem(z + planes - d, planes)]
        remote(origin, origin, gz_send.at[d], gz_recv.at[d], c, z).wait_recv()
    total = gain_all[0]
    for i in range(1, planes):
        total = total + gain_all[i]
    gains_ref[...] = total

    for m in range(4):
        hand_receive(m)
    hand_out(5)
    drain(along)
    hand_receive(4)
    hand_receive(5)
    drain(in_plane)


def finish_kernel(
    n, head, out_in, dx_in, gains_in, got_a, got_b, got_c, got_out, got_q, got_kv,
    out_ref, dx_ref, ag_ref, q_ref, k_ref, v_ref, qg_ref, kg_ref, o_ref, fg_ref, g_ref, u_ref, d_ref,
):
    out_ref[...] = out_in[...]
    dx_ref[...] = dx_in[...]
    ag_ref[...] = gains_in[0:1, :]
    fg_ref[...] = gains_in[1:2, :]
    qg_ref[...] = gains_in[2:3, 0:head]
    kg_ref[...] = gains_in[3:4, 0:head]
    qw, kw = q_ref.shape[1] // n, k_ref.shape[1] // n
    pw = got_a.shape[2] // 3
    thirds = (got_a, got_b, got_c)
    for i in range(n):
        q_ref[:, i * qw:(i + 1) * qw] = got_q[i].astype(f32)
        k_ref[:, i * kw:(i + 1) * kw] = got_kv[i, :, 0:kw].astype(f32)
        v_ref[:, i * kw:(i + 1) * kw] = got_kv[i, :, kw:].astype(f32)
        o_ref[:, i * qw:(i + 1) * qw] = got_out[i].astype(f32)
        for t, got in enumerate(thirds):
            plane, unit = hidden_block(i, t)
            at = plane * (g_ref.shape[1] // 4) + unit * pw
            g_ref[:, at:at + pw] = got[i, :, 0:pw].astype(f32)
            u_ref[:, at:at + pw] = got[i, :, pw:2 * pw].astype(f32)
            d_ref[:, at:at + pw] = got[i, :, 2 * pw:].astype(f32)


def plane_device(
    layer_input,
    token_positions,
    attention_gain,
    query_weight,
    key_matrix,
    value_matrix,
    query_gain,
    key_norm_gain,
    output_weight,
    feedforward_gain,
    gate_weight,
    up_weight,
    down_weight,
    out_cotangent,
):
    n = lax.axis_size("ctx")
    planes = lax.axis_size("fsdp")
    block, width = layer_input.shape[1:]
    length = token_positions.shape[1]
    head = query_gain.shape[0]
    qw = query_weight.shape[1] // n
    kw = key_matrix.shape[1] // n
    fw = gate_weight.shape[1] // n
    group = qw // head
    per = block // planes
    half = head // 2
    inverse = np.power(rope_base, -np.arange(half) * 2.0 / head).astype(np.float32)
    inverse = np.concatenate([inverse, inverse])[None]
    steps = np.arange(block // 2)[:, None] * inverse.astype(np.float64)
    step_cos, step_sin = (jnp.asarray(f(steps).astype(np.float32)) for f in (np.cos, np.sin))
    inverse = jnp.asarray(inverse)
    vmem = pl.BlockSpec(memory_space=pltpu.VMEM)
    hbm = pl.BlockSpec(memory_space=pl.ANY)
    dma = pltpu.SemaphoreType.DMA
    sizes = (fw, fw, fw, qw, qw, 2 * kw)
    low = lambda *shape: pltpu.VMEM(shape, bf16)
    wide = lambda *shape: pltpu.VMEM(shape, f32)
    scratch = [
        low(width, qw + 2 * kw), low(width, 2 * fw), low(qw, width), low(fw, width),
        low(planes * (output_weight.shape[0] // n), width),
        low(length, width), low(length, width), low(length, width),
        low(width, length), low(width, length), low(width, length),
        wide(length, head), wide(length, head), wide(length, head),
        wide(length, qw + kw), low(length, qw), low(length, kw), low(length, kw),
        low(kw, length), low(kw, length), low(n // 2, length, 2 * group * block), wide(n // 2, 1, 2 * group * block),
        wide(n // 2, head, 2 * group * block), low(length, qw),
        low(length, fw), low(length, 2 * fw), low(length, qw + 2 * kw),
        wide(length, kw), wide(length, kw),
    ]
    scratch += [low(planes, n, per, size) for size in sizes]
    scratch += [low(planes + 1, n, per, size) for size in sizes]
    scratch += [low(2, 4, block, width) for _ in range(4)] + [wide(2, block, width), wide(2, block, width)]
    scratch += [
        wide(block, width), wide(block, width), wide(8, width), wide(n, 8, width), wide(planes, 8, width),
        dma((13,)), dma((8, 6)), dma((8, planes)), dma((1, 7)), dma((1, 4)),
        dma((4, n)), dma((4, n)), dma((4, 4)), dma((4, 4)), dma((4, 4)), dma((4, 4)),
        dma((6, planes)), dma((6, planes + 1)), dma((6, n)), dma((6, n)), dma((n,)), dma((n,)),
        dma((planes,)), dma((planes,)),
    ]
    shapes = [
        jax.ShapeDtypeStruct((block, width), bf16),
        jax.ShapeDtypeStruct((block, width), f32),
        jax.ShapeDtypeStruct((8, width), f32),
    ] + [jax.ShapeDtypeStruct((n, per, size), bf16) for size in sizes]
    results = pl.pallas_call(
        functools.partial(layer_kernel, n, planes, block, head, group, fw),
        out_shape=shapes,
        in_specs=[vmem] * 10 + [hbm] * 7,
        out_specs=[vmem] * len(shapes),
        scratch_shapes=scratch,
        compiler_params=pltpu.CompilerParams(
            collective_id=0, has_side_effects=True, vmem_limit_bytes=60 * 1024 * 1024),
    )(
        layer_input[0], out_cotangent[0], token_positions, inverse, step_cos, step_sin,
        attention_gain[None], feedforward_gain[None], query_gain[None], key_norm_gain[None],
        query_weight, key_matrix, value_matrix, output_weight, gate_weight, up_weight, down_weight,
    )
    plain = lambda rows, columns, kind=f32: jax.ShapeDtypeStruct((rows, columns), kind)
    finals = [
        plain(block, width, bf16), plain(block, width), plain(1, width),
        plain(per, n * qw), plain(per, n * kw), plain(per, n * kw), plain(1, head), plain(1, head),
        plain(per, n * qw), plain(1, width), plain(per, n * fw), plain(per, n * fw), plain(per, n * fw),
    ]
    done = pl.pallas_call(
        functools.partial(finish_kernel, n, head),
        out_shape=finals,
        in_specs=[vmem] * len(shapes),
        out_specs=[vmem] * len(finals),
    )(*results)
    out, dx, ag, q, k, v, qg, kg, o, fg, g, u, d = done
    return out[None], dx[None], ag[0], q, k, v, qg[0], kg[0], o.T, fg[0], g, u, d.T


def solution(mesh):
    in_specs = (
        P("fsdp", "ctx", None),
        P("fsdp", None),
        P(),
        P("fsdp", None),
        P("fsdp", None),
        P("fsdp", None),
        P(),
        P(),
        P("fsdp", None),
        P(),
        P("fsdp", None),
        P("fsdp", None),
        P("fsdp", None),
        P("fsdp", "ctx", None),
    )
    out_specs = (
        P("fsdp", "ctx", None),
        P("fsdp", "ctx", None),
        P(),
        P(("ctx", "fsdp"), None),
        P(("ctx", "fsdp"), None),
        P(("ctx", "fsdp"), None),
        P(),
        P(),
        P(None, ("ctx", "fsdp")),
        P(),
        P(("ctx", "fsdp"), None),
        P(("ctx", "fsdp"), None),
        P(None, ("ctx", "fsdp")),
    )

    def run(*arguments):
        n, planes = mesh.shape["ctx"], mesh.shape["fsdp"]
        key_heads = arguments[4].shape[1] // arguments[6].shape[0]
        whole_heads = n == 8 and planes == 4 and key_heads == n
        return jax.shard_map(
            plane_device if whole_heads else on_device,
            mesh=mesh, in_specs=in_specs, out_specs=out_specs, check_vma=False,
        )(*arguments)

    return run
```

```python
import functools

import jax
import jax.numpy as jnp
import numpy as np
from jax import lax
from jax.experimental import pallas as pl
from jax.experimental.pallas import tpu as pltpu
from jax.sharding import PartitionSpec as P

epsilon = 1e-06
rope_base = 1000000.0
masked_score = -1e30


def from_behind(block, axis, distance):
    devices = range(lax.axis_size(axis))
    route = [((i - distance) % len(devices), i) for i in devices]
    return lax.ppermute(block, axis, route)


def rotate(value_rows):
    half = value_rows.shape[-1] // 2
    return jnp.concatenate([-value_rows[..., half:], value_rows[..., :half]], -1)


def rotate_back(value_rows):
    half = value_rows.shape[-1] // 2
    return jnp.concatenate([value_rows[..., half:], -value_rows[..., :half]], -1)


def rope_tables(token_offsets, head_size):
    half = head_size // 2
    inverse = rope_base ** (-(jnp.arange(half).astype(jnp.float32) * 2.0) / head_size)
    angles = token_offsets.astype(jnp.float32)[:, None] * inverse[None, :]
    cosine = jnp.cos(angles)
    sine = jnp.sin(angles)
    return (jnp.concatenate([cosine, cosine], -1), jnp.concatenate([sine, sine], -1))


def norm_scale(value_rows):
    return lax.rsqrt(jnp.mean(value_rows * value_rows, -1, keepdims=True) + epsilon)


def norm_back(value_rows, scale, gain, grad):
    weighted = grad * gain
    inner = jnp.mean(weighted * value_rows, -1, keepdims=True)
    result = scale * weighted - value_rows * scale * scale * scale * inner
    gain_part = jnp.sum((grad * value_rows * scale).reshape(-1, gain.shape[0]), 0)
    return (result, gain_part)


def row_products(left, pieces):
    return tuple((jnp.dot(left, piece, preferred_element_type=jnp.float32) for piece in pieces))


def column_products(rights, pieces):
    total = jnp.einsum("tc,rc->tr", rights[0], pieces[0], preferred_element_type=jnp.float32)
    for right, piece in zip(rights[1:], pieces[1:]):
        total = total + jnp.einsum("tc,rc->tr", right, piece, preferred_element_type=jnp.float32)
    return total


def on_device(
    layer_input,
    token_positions,
    attention_gain,
    query_weight,
    key_matrix,
    value_matrix,
    query_gain,
    key_norm_gain,
    output_weight,
    feedforward_gain,
    gate_weight,
    up_weight,
    down_weight,
    out_cotangent,
):
    hidden_in = layer_input[0].astype(jnp.float32)
    count = hidden_in.shape[0]
    head_size = query_gain.shape[0]
    query_width = query_weight.shape[1]
    key_width = key_matrix.shape[1]
    inner_width = gate_weight.shape[1]
    heads = query_width // head_size
    key_heads = key_width // head_size
    group = heads // key_heads
    scale = head_size ** (-0.5)
    cycles = lax.axis_size("ctx")
    own_index = lax.axis_index("ctx")
    sequence_pos = token_positions[0]
    token_offsets = lax.dynamic_slice_in_dim(sequence_pos, own_index * count, count)
    cosine, sine = rope_tables(token_offsets, head_size)
    cosine = cosine[:, None, :]
    sine = sine[:, None, :]
    first_scale = norm_scale(hidden_in)
    first = (hidden_in * first_scale * attention_gain).astype(jnp.bfloat16)
    query_raw, key_unnormed, value_unnormed = row_products(
        first,
        (
            lax.all_gather(query_weight, "fsdp", axis=0, tiled=True),
            lax.all_gather(key_matrix, "fsdp", axis=0, tiled=True),
            lax.all_gather(value_matrix, "fsdp", axis=0, tiled=True),
        ),
    )
    query_heads = query_raw.reshape(count, heads, head_size)
    query_scale = norm_scale(query_heads)
    query_normed = query_heads * query_scale * query_gain
    query_rot = query_normed * cosine + rotate(query_normed) * sine
    query_grouped = (
        query_rot.reshape(count, key_heads, group, head_size)
        .transpose(1, 2, 0, 3)
        .astype(jnp.bfloat16)
    )
    key_heads_raw = key_unnormed.reshape(count, key_heads, head_size)
    key_scale = norm_scale(key_heads_raw)
    key_normed = key_heads_raw * key_scale * key_norm_gain
    key_low = (
        (key_normed * cosine + rotate(key_normed) * sine)
        .reshape(count, key_width)
        .astype(jnp.bfloat16)
    )
    value_low = value_unnormed.astype(jnp.bfloat16)
    rowmax = jnp.full((key_heads, group, count), masked_score, jnp.float32)
    keys_piece = lax.all_gather(key_low, "ctx", axis=0, tiled=True).reshape(
        -1, key_heads, head_size
    )
    values_piece = lax.all_gather(value_low, "ctx", axis=0, tiled=True).reshape(
        -1, key_heads, head_size
    )
    key_pos = sequence_pos
    allowed = token_offsets[:, None] >= key_pos[None, :]
    scores = (
        jnp.einsum("kgtd,skd->kgts", query_grouped, keys_piece, preferred_element_type=jnp.float32)
        * scale
    )
    scores = jnp.where(allowed, scores, masked_score)
    newmax = jnp.maximum(rowmax, jnp.max(scores, -1))
    weights = jnp.where(allowed, jnp.exp(scores - newmax[..., None]), 0.0)
    accum = jnp.einsum(
        "kgts,skd->kgtd",
        weights.astype(jnp.bfloat16),
        values_piece,
        preferred_element_type=jnp.float32,
    )
    rowsum = jnp.sum(weights, -1)
    accum, rowmax, rowsum = (accum, newmax, rowsum)
    normalized = accum / rowsum[..., None]
    logsum = rowmax + jnp.log(rowsum)
    attention_low = (
        normalized.transpose(2, 0, 1, 3).reshape(count, query_width).astype(jnp.bfloat16)
    )
    output_whole = lax.all_gather(output_weight, "fsdp", axis=0, tiled=True)
    branch_out = jnp.dot(attention_low, output_whole, preferred_element_type=jnp.float32)
    middle = hidden_in + branch_out
    second_scale = norm_scale(middle)
    second = (middle * second_scale * feedforward_gain).astype(jnp.bfloat16)
    gate, up = row_products(
        second,
        (
            lax.all_gather(gate_weight, "fsdp", axis=0, tiled=True),
            lax.all_gather(up_weight, "fsdp", axis=0, tiled=True),
        ),
    )
    sigmoid_gate = jax.nn.sigmoid(gate)
    silu_gate = gate * sigmoid_gate
    hidden_low = (silu_gate * up).astype(jnp.bfloat16)
    (down_out,) = row_products(
        hidden_low, (lax.all_gather(down_weight, "fsdp", axis=0, tiled=True),)
    )
    layer_output = (middle + down_out).astype(jnp.bfloat16)[None]
    cotangent = out_cotangent[0]
    hidden_grad = column_products(
        (cotangent,), lax.all_gather((down_weight,), "fsdp", axis=0, tiled=True)
    )
    up_low = (hidden_grad * silu_gate).astype(jnp.bfloat16)
    gate_low = (hidden_grad * up * sigmoid_gate * (1.0 + gate * (1.0 - sigmoid_gate))).astype(
        jnp.bfloat16
    )
    second_grad = column_products(
        (gate_low, up_low), lax.all_gather((gate_weight, up_weight), "fsdp", axis=0, tiled=True)
    )
    middle_part, feedforward_part = norm_back(middle, second_scale, feedforward_gain, second_grad)
    middle_grad = cotangent.astype(jnp.float32) + middle_part
    middle_low = middle_grad.astype(jnp.bfloat16)
    attention_grad = jnp.einsum(
        "tc,rc->tr", middle_low, output_whole, preferred_element_type=jnp.float32
    )
    attention_grad_low = attention_grad.astype(jnp.bfloat16)
    mixed_grad = attention_grad_low.reshape(count, key_heads, group, head_size).transpose(
        1, 2, 0, 3
    )
    delta = jnp.sum(mixed_grad.astype(jnp.float32) * normalized, -1)

    def cycle_step(index, carry):
        keys_held, values_held, key_acc, value_acc, query_acc = carry
        anchor = (own_index - index) % cycles
        key_pos = lax.dynamic_slice_in_dim(sequence_pos, anchor * count, count)
        keys_piece = keys_held.astype(jnp.bfloat16).reshape(count, key_heads, head_size)
        values_piece = values_held.astype(jnp.bfloat16).reshape(count, key_heads, head_size)
        allowed = token_offsets[:, None] >= key_pos[None, :]
        scores = (
            jnp.einsum(
                "kgtd,skd->kgts", query_grouped, keys_piece, preferred_element_type=jnp.float32
            )
            * scale
        )
        probs = jnp.where(allowed, jnp.exp(scores - logsum[..., None]), 0.0)
        value_acc = value_acc + jnp.einsum(
            "kgts,kgtd->skd",
            probs.astype(jnp.bfloat16),
            mixed_grad,
            preferred_element_type=jnp.float32,
        ).reshape(count, key_width)
        prob_grad = jnp.einsum(
            "kgtd,skd->kgts", mixed_grad, values_piece, preferred_element_type=jnp.float32
        )
        score_grad = (probs * (prob_grad - delta[..., None])).astype(jnp.bfloat16)
        query_acc = (
            query_acc
            + jnp.einsum(
                "kgts,skd->kgtd", score_grad, keys_piece, preferred_element_type=jnp.float32
            )
            * scale
        )
        key_acc = (
            key_acc
            + jnp.einsum(
                "kgts,kgtd->skd", score_grad, query_grouped, preferred_element_type=jnp.float32
            ).reshape(count, key_width)
            * scale
        )
        moved = (
            from_behind(keys_held.astype(jnp.bfloat16), "ctx", 1).astype(keys_held.dtype),
            from_behind(values_held.astype(jnp.bfloat16), "ctx", 1).astype(values_held.dtype),
            from_behind(key_acc.astype(jnp.bfloat16), "ctx", 1).astype(key_acc.dtype),
            from_behind(value_acc.astype(jnp.bfloat16), "ctx", 1).astype(value_acc.dtype),
        )
        return (moved[0], moved[1], moved[2], moved[3], query_acc)

    start_cycle = (
        key_low.astype(jnp.float32),
        value_low.astype(jnp.float32),
        jnp.zeros((count, key_width), jnp.float32),
        jnp.zeros((count, key_width), jnp.float32),
        jnp.zeros((key_heads, group, count, head_size), jnp.float32),
    )
    cycle_done = lax.fori_loop(0, cycles, cycle_step, start_cycle)
    key_acc = cycle_done[2]
    value_acc = cycle_done[3]
    query_acc = cycle_done[4]
    query_rot_grad = query_acc.transpose(2, 0, 1, 3).reshape(count, heads, head_size)
    query_normed_grad = query_rot_grad * cosine + rotate_back(query_rot_grad * sine)
    query_heads_grad, query_part = norm_back(
        query_heads, query_scale, query_gain, query_normed_grad
    )
    query_low_grad = query_heads_grad.reshape(count, query_width).astype(jnp.bfloat16)
    key_rot_grad = key_acc.reshape(count, key_heads, head_size)
    key_normed_grad = key_rot_grad * cosine + rotate_back(key_rot_grad * sine)
    key_heads_grad, key_part = norm_back(key_heads_raw, key_scale, key_norm_gain, key_normed_grad)
    key_low_grad = key_heads_grad.reshape(count, key_width).astype(jnp.bfloat16)
    value_low_grad = value_acc.astype(jnp.bfloat16)
    first_grad = column_products(
        (query_low_grad, key_low_grad, value_low_grad),
        lax.all_gather((query_weight, key_matrix, value_matrix), "fsdp", axis=0, tiled=True),
    )
    input_part, attention_part = norm_back(hidden_in, first_scale, attention_gain, first_grad)
    input_gradient = (middle_grad + input_part)[None]
    rights_first = jnp.concatenate([query_low_grad, key_low_grad, value_low_grad], 1)
    rights_second = jnp.concatenate([gate_low, up_low], 1)
    pairs = (
        (first, rights_first),
        (second, rights_second),
        (middle_low, attention_low),
        (cotangent, hidden_low),
    )
    parts = []
    for left, right in pairs:
        parts.append(jnp.einsum("tr,tc->rc", left, right, preferred_element_type=jnp.float32))
    sums = lax.psum_scatter(
        jnp.concatenate(parts, 1), ("ctx", "fsdp"), scatter_dimension=0, tiled=True
    )
    edges = [0, query_width, query_width + key_width, query_width + 2 * key_width]
    edges = edges + [edges[3] + inner_width, edges[3] + 2 * inner_width]
    edges = edges + [edges[5] + query_width, edges[5] + query_width + inner_width]
    query_gradient = sums[:, edges[0] : edges[1]]
    key_gradient = sums[:, edges[1] : edges[2]]
    value_gradient = sums[:, edges[2] : edges[3]]
    gate_gradient = sums[:, edges[3] : edges[4]]
    up_gradient = sums[:, edges[4] : edges[5]]
    output_gradient = sums[:, edges[5] : edges[6]].T
    down_gradient = sums[:, edges[6] : edges[7]].T
    attention_total, query_total, key_total, feedforward_total = lax.psum(
        (attention_part, query_part, key_part, feedforward_part), ("ctx", "fsdp")
    )
    return (
        layer_output,
        input_gradient,
        attention_total,
        query_gradient,
        key_gradient,
        value_gradient,
        query_total,
        key_total,
        output_gradient,
        feedforward_total,
        gate_gradient,
        up_gradient,
        down_gradient,
    )


MESH = pl.DeviceIdType.MESH
f32 = jnp.float32
bf16 = jnp.bfloat16


def dot(left, right):
    return jnp.dot(left, right, preferred_element_type=f32)


def dot_nt(left, right):
    return lax.dot_general(left, right, (((1,), (1,)), ((), ())), preferred_element_type=f32)


def dot_tn(left, right):
    return lax.dot_general(left, right, (((0,), (0,)), ((), ())), preferred_element_type=f32)


def hidden_block(device, third):
    def plane(i, t):
        return ((3, 1, 2), (0, 2, 1), (0, 3, 2), (3, 0, 1))[i // 4 * 2 + i % 2][t]

    own = plane(device, third)
    return own, sum(plane(i, t) == own for i in range(device) for t in range(3))


def layer_kernel(
    n, planes, block, head, group, fw,
    x_ref, dy_ref, pos_row, inverse_ref, step_cos, step_sin, ag_ref, fg_ref, qg_ref, kg_ref,
    wq, wk, wv, wo, wg, wu, wd,
    out_ref, dx_ref, gains_ref, got_a, got_b, got_c, got_out, got_q, got_kv,
    w_qkv, w_gu, w_out, w_down, t_out,
    first, dy_all, second, first_t, dy_t, second_t,
    positions, cosine, sine,
    raw, queries, keys, values, keys_t, values_t, probs, sums, mixed_t, mixed_low,
    hidden, d_gu, d_qkv, dk_acc, dv_acc,
    stage_a, stage_b, stage_c, stage_out, stage_q, stage_kv,
    land_a, land_b, land_c, land_out, land_q, land_kv,
    rs_sa, rs_ra, rs_sb, rs_rb, rs_kept, rs_acc,
    middle, d_middle, gain_own, gain_plane, gain_all,
    local_sem, wz_send, wz_recv, hand_send, hand_recv,
    ag_send, ag_recv, ra_send, ra_recv, rb_send, rb_recv,
    zr_send, zr_recv, aa_send, aa_recv, gp_send, gp_recv, gz_send, gz_recv,
):
    c = lax.axis_index("ctx")
    z = lax.axis_index("fsdp")
    dmid = first
    dmid_t = second
    cy, cx, ck = lax.div(c, 4), lax.rem(lax.div(c, 2), 2), lax.rem(c, 2)
    ci = lax.rem(c, 4)
    sign = 1 - 2 * ck
    qw, kw = group * head, head
    pw = 128
    thirds = fw // pw
    width = x_ref.shape[1]
    scale = head ** (-0.5)
    log2e = 1.4426950408889634
    gots = (got_a, got_b, got_c, got_out, got_q, got_kv)
    stages = (stage_a, stage_b, stage_c, stage_out, stage_q, stage_kv)
    lands = (land_a, land_b, land_c, land_out, land_q, land_kv)

    def partner(j):
        y = lax.rem(cy + lax.div(j, 4), 2)
        x = lax.rem(cx + lax.rem(lax.div(j, 2), 2), 2)
        k = lax.rem(ck + lax.rem(j, 2), 2)
        return y * 4 + x * 2 + k

    def chip(slot):
        return lax.rem(cy + lax.div(slot, 2), 2) * 2 + lax.rem(cx + lax.rem(slot, 2), 2)

    def rows(start, size):
        return pl.ds(pl.multiple_of(start * size, size), size)

    def remote(src, dst, send, recv, ctx, plane):
        return pltpu.make_async_remote_copy(
            src_ref=src, dst_ref=dst, send_sem=send, recv_sem=recv,
            device_id={"ctx": ctx, "fsdp": plane}, device_id_type=MESH,
        )

    in_plane, along, weight_sends = [], [], []

    def launch(started, copy, when=None):
        if when is None:
            copy().start()
        else:
            pl.when(when)(lambda: copy().start())
        started.append((copy, when))

    def drain(started):
        for copy, when in started:
            if when is None:
                copy().wait_send()
            else:
                pl.when(when)(lambda copy=copy: copy().wait_send())
        started.clear()

    def pick(values):
        return sum(jnp.where(c == i, value, 0) for i, value in enumerate(values))

    unit_plane = [pick([hidden_block(i, t)[0] for i in range(n)]) for t in range(thirds)]
    unit_block = [pick([hidden_block(i, t)[1] for i in range(n)]) for t in range(thirds)]
    plane_blocks = wd.shape[0] // pw

    own_rows = wq.shape[0]
    out_rows = wo.shape[0] // n

    def own_slices():
        mine = rows(z, own_rows)
        pairs = [
            (wq.at[:, rows(c, qw)], w_qkv.at[mine, 0:qw]),
            (wk.at[:, rows(c, kw)], w_qkv.at[mine, qw:qw + kw]),
            (wv.at[:, rows(c, kw)], w_qkv.at[mine, qw + kw:qw + 2 * kw]),
            (wo.at[rows(c, out_rows)], t_out.at[rows(z, out_rows)]),
        ]
        for t in range(thirds):
            at = 2 * pw * t
            unit = unit_plane[t] * plane_blocks + unit_block[t]
            pairs.append((wg.at[:, rows(unit, pw)], w_gu.at[mine, at:at + pw]))
            pairs.append((wu.at[:, rows(unit, pw)], w_gu.at[mine, at + pw:at + 2 * pw]))
        return pairs

    local = [pltpu.make_async_copy(src, dst, local_sem.at[i]) for i, (src, dst) in enumerate(own_slices())]
    for copy in local:
        copy.start()

    def own_down(t):
        return pltpu.make_async_copy(
            wd.at[rows(unit_block[t], pw)], w_down.at[t * pw:(t + 1) * pw], local_sem.at[4 + 2 * thirds + t])

    holds = [unit_plane[t] == z for t in range(thirds)]
    for t in range(thirds):
        pl.when(holds[t])(lambda t=t: own_down(t).start())

    for land in lands:
        @pl.when(z == 0)
        def _(land=land):
            land[0] = jnp.zeros(land.shape[1:], bf16)

        @pl.when(z == planes - 1)
        def _(land=land):
            land[planes] = jnp.zeros(land.shape[1:], bf16)

    barrier = pltpu.get_barrier_semaphore()
    for j in range(1, n):
        pl.semaphore_signal(barrier, inc=1, device_id={"ctx": partner(j), "fsdp": z}, device_id_type=MESH)
    for d in range(1, planes):
        pl.semaphore_signal(
            barrier, inc=1, device_id={"ctx": c, "fsdp": lax.rem(z + d, planes)}, device_id_type=MESH)
    x = x_ref[...].astype(f32)
    x_scale = lax.rsqrt(jnp.mean(x * x, -1, keepdims=True) + epsilon)
    first[rows(c, block)] = (x * x_scale * ag_ref[...]).astype(bf16)
    dy_all[rows(c, block)] = dy_ref[...]
    for copy in local[:3]:
        copy.wait()
    pl.semaphore_wait(barrier, n + planes - 2)

    def inside(t):
        return jnp.logical_and(t >= 0, t < planes)

    weights = [
        (lambda o: w_qkv.at[rows(o, own_rows), 0:qw + kw], None),
        (lambda o: t_out.at[rows(o, out_rows)], 0),
    ]
    for t in range(thirds):
        weights.append((lambda o, t=t: w_gu.at[rows(o, own_rows), 2 * pw * t:2 * pw * (t + 1)], None))
        weights.append((lambda o, t=t: w_down.at[t * pw:(t + 1) * pw], None))
    weights.append((lambda o: w_qkv.at[rows(o, own_rows), qw + kw:qw + 2 * kw], None))
    value_index = len(weights) - 1

    def weight_copy(w, slot, origin, target):
        part = weights[w][0](origin)
        return remote(part, part, wz_send.at[w, slot], wz_recv.at[w, origin], c, target)

    def from_plane(w, origin):
        return origin == unit_plane[(w - 3) // 2] if 3 <= w <= 1 + 2 * thirds and w % 2 else None

    def both(one, other):
        return one if other is None else jnp.logical_and(one, other)

    def hand_split(origin, valid):
        mine = 2 * origin + cy == c
        return jnp.logical_and(valid, jnp.logical_not(mine)), jnp.logical_and(valid, mine)

    def weight_start(w):
        for side in range(2):
            d = sign * (1 - 2 * side)
            launch(
                weight_sends, lambda side=side, d=d: weight_copy(w, side, z, z + d),
                both(inside(z + d), from_plane(w, z)))
        if weights[w][1] is not None:
            hand_over(w, z, 0, *hand_split(z, True))

    def hand_target(h):
        return lambda i: w_out.at[rows(i, out_rows)]

    def hand_copy(w, origin, slot):
        h = weights[w][1]
        return remote(
            weights[w][0](origin), hand_target(h)(ci), hand_send.at[h, slot], hand_recv.at[h, ci], 2 * origin + cy, z)

    def hand_over(w, origin, slot, away, here):
        launch(in_plane, lambda: hand_copy(w, origin, slot), away)

        @pl.when(here)
        def _():
            hand_target(weights[w][1])(ci)[...] = weights[w][0](origin)[...]

    def hand_arrive(w):
        h = weights[w][1]
        for i in range(4):
            @pl.when(4 * ck + i != c)
            def _(i=i):
                part = hand_target(h)(i)
                remote(part, part, hand_send.at[h, 0], hand_recv.at[h, i], c, z).wait_recv()

    hops = {}
    for w in range(len(weights)):
        for d in range(1, planes):
            for side, way in enumerate((1, -1)):
                origin = z - way * d
                valid = both(inside(origin), from_plane(w, origin))
                passed = jnp.logical_and(valid, inside(z + way))
                split = None if weights[w][1] is None else hand_split(origin, valid)
                hops[w, d, side] = origin, z + way, valid, passed, split

    def weight_hop(w, d):
        for side in range(2):
            origin, following, valid, passed, split = hops[w, d, side]
            pl.when(valid)(lambda: weight_copy(w, 0, origin, z).wait_recv())
            if d < planes - 1:
                launch(
                    weight_sends,
                    lambda side=side, origin=origin, following=following: weight_copy(
                        w, 2 * d + side, origin, following),
                    passed)
            if split is not None:
                hand_over(w, origin, 2 * d - 1 + side, *split)

    def gather_copy(buf, g, j, send, origin, target):
        part = buf.at[rows(origin, block)]
        return remote(part, part, ag_send.at[g, send], ag_recv.at[g, j], target, z)

    def gather_start(buf, g):
        for j in (1, 2 + 2 * ck, 4 - 2 * ck):
            launch(in_plane, lambda j=j: gather_copy(buf, g, j, j, c, partner(j)))

    def gather_half(buf, g, j):
        half = block // 2
        part = buf.at[pl.ds(pl.multiple_of(partner(j) * block + (half if j == 2 else 0), half), half)]
        at = 0 if j == 2 else 6
        return remote(part, part, ag_send.at[g, at], ag_recv.at[g, at], partner(6 - j), z)

    def gather_diagonal(buf, g):
        half = block // 2
        for at in (6, 0):
            part = buf.at[pl.ds(pl.multiple_of(partner(6) * block + (0 if at == 6 else half), half), half)]
            remote(part, part, ag_send.at[g, at], ag_recv.at[g, at], c, z).wait_recv()

    def gather_forward(buf, g, j):
        return gather_copy(buf, g, j + 1, j + 1, partner(j), partner(1))

    def gather_take(buf, g, j):
        if j == 6:
            gather_diagonal(buf, g)
        else:
            gather_copy(buf, g, j, j, partner(j), c).wait_recv()
            gather_half(buf, g, j).start()
        gather_forward(buf, g, j).start()

    def gather_sent(buf, g):
        for j in (2, 4, 6):
            in_plane.append((lambda j=j: gather_forward(buf, g, j), None))
            if j < 6:
                in_plane.append((lambda j=j: gather_half(buf, g, j), None))

    def gather_finish(buf, g):
        for j in (2, 4, 6):
            gather_take(buf, g, j)
        gather_sent(buf, g)
        for j in (1, 3, 5, 7):
            gather_copy(buf, g, j, j, partner(j), c).wait_recv()

    def gather_step(buf, g, slot):
        @pl.when(slot == 1)
        def _():
            gather_take(buf, g, 2)
            gather_take(buf, g, 4)

        pl.when(slot == 3)(lambda: gather_take(buf, g, 6))
        gather_copy(buf, g, 2 * slot + 1, 0, partner(2 * slot + 1), c).wait_recv()

    def sum_pair_copy(s, slot):
        return remote(rs_sa.at[s % 2, slot], rs_ra.at[s % 2, slot], ra_send.at[s, slot], ra_recv.at[s, slot], partner(1), z)

    def sum_chip_copy(s, slot):
        return remote(
            rs_sb.at[s % 2, slot], rs_rb.at[s % 2, slot], rb_send.at[s, slot], rb_recv.at[s, slot], partner(2 * slot), z)

    def sum_half_copy(s, slot):
        half = block // 2
        at = pl.ds(pl.multiple_of((slot - 1) * half, half), half)
        return remote(
            rs_sb.at[s % 2, 3, at], rs_rb.at[s % 2, 3, at], rb_send.at[s, 6 - 3 * slot], rb_recv.at[s, 6 - 3 * slot],
            partner(6 - 2 * slot), z)

    def sum_slot(p):
        return jnp.where(p == 0, 3, jnp.where(p == 1, 2 - ck, jnp.where(p == 2, 1 + ck, 0)))

    def sum_start(s, left, partial, prepare=None, ready=None, during=()):
        if prepare is not None:
            prepare(chip(sum_slot(0)))
        if ready is not None:
            ready()

        def body(p, carry):
            slot = sum_slot(p)
            at = [rows(partner(2 * slot + 1), block), rows(partner(2 * slot), block)]
            both = partial(jnp.concatenate([left[i] for i in at], 0))
            rs_sa[s % 2, slot] = both[:block].astype(bf16)
            sum_pair_copy(s, slot).start()
            rs_kept[lax.rem(p, 2)] = both[block:]

            @pl.when(p > 0)
            def _():
                before = sum_slot(p - 1)
                sum_pair_copy(s, before).wait_recv()
                rs_sb[s % 2, before] = (
                    rs_kept[lax.rem(p + 1, 2)] + rs_ra[s % 2, before].astype(f32)).astype(bf16)

            @pl.when(p == 1)
            def _():
                sum_half_copy(s, 1).start()
                sum_half_copy(s, 2).start()

            @pl.when(p > 1)
            def _():
                before = sum_slot(p - 1)
                half = block // 2
                at = pl.ds(pl.multiple_of((before - 1) * half, half), half)
                sum_half_copy(s, before).wait_recv()
                rs_sb[s % 2, before, at] = (
                    rs_sb[s % 2, before, at].astype(f32) + rs_rb[s % 2, 3, at].astype(f32)).astype(bf16)
                sum_chip_copy(s, before).start()

            if prepare is not None:
                @pl.when(p < 3)
                def _():
                    prepare(chip(sum_slot(p + 1)))

            for k, poll in enumerate(during):
                pl.when(p == k)(poll)
            return carry

        lax.fori_loop(0, 4, body, 0)
        for slot in range(4):
            in_plane.append((lambda slot=slot: sum_pair_copy(s, slot), None))
        for slot in (1, 2):
            in_plane.append((lambda slot=slot: sum_half_copy(s, slot), None))
            in_plane.append((lambda slot=slot: sum_chip_copy(s, slot), None))
        sum_pair_copy(s, 0).wait_recv()
        rs_acc[s % 2] = rs_kept[1] + rs_ra[s % 2, 0].astype(f32)

    def sum_finish(s):
        total = rs_acc[s % 2]
        for slot in (1, 2):
            sum_chip_copy(s, slot).wait_recv()
            total = total + rs_rb[s % 2, slot].astype(f32)
        return total

    per = block // planes

    at_edge = jnp.logical_or(z == 0, z == planes - 1)
    edge_targets = [jnp.where(z == 0, planes - 1 - k, k) for k in range(planes - 1)]

    def weight_grad(m, parts):
        def body(i, carry):
            at = 0
            for left, right in parts:
                value = right()
                grad = dot(left[rows(i, 4 * block)], value)
                for k in range(4):
                    for t in range(planes):
                        start = k * block + t * per
                        stages[m][t, 4 * i + k, :, at:at + value.shape[1]] = grad[start:start + per].astype(bf16)
                at += value.shape[1]
            return carry

        lax.fori_loop(0, n // 4, body, 0)
        for t in edge_targets:
            launch(along, lambda t=t: grad_copy(m, t), at_edge)

    def grad_copy(m, t):
        way = jnp.where(z < t, 1, -1)
        last = z + way == t
        slot = jnp.where(jnp.logical_and(last, way < 0), planes, t)
        return remote(
            stages[m].at[t], lands[m].at[slot], zr_send.at[m, t], zr_recv.at[m, slot], c, z + way)

    def grad_arrive(m, slot):
        part = lands[m].at[slot]
        remote(part, part, zr_send.at[m, 0], zr_recv.at[m, slot], c, z).wait_recv()

    def grad_pass(m, t, valid):
        @pl.when(valid)
        def _():
            grad_arrive(m, t)

            def body(i, carry):
                stages[m][t, i] = (stages[m][t, i].astype(f32) + lands[m][t, i].astype(f32)).astype(bf16)
                return carry

            lax.fori_loop(0, n, body, 0)

        launch(along, lambda: grad_copy(m, t), valid)

    is_low, is_high = z == 1, z == planes - 2

    def grad_near_far(m):
        grad_pass(m, 3, is_low)
        grad_pass(m, 0, is_high)

    def grad_near_inner(m):
        grad_pass(m, 2, is_low)
        grad_pass(m, 1, is_high)

    def grad_near(m):
        grad_near_far(m)
        grad_near_inner(m)

    def grad_far(m):
        grad_pass(m, 3, is_high)
        grad_pass(m, 0, is_low)

    def owner_copy(m, j):
        return remote(lands[m].at[z, partner(j)], gots[m].at[c], aa_send.at[m, j], aa_recv.at[m, j], partner(j), z)

    def hand_out(m):
        pl.when(z > 0)(lambda: grad_arrive(m, z))
        pl.when(z < planes - 1)(lambda: grad_arrive(m, planes))

        def body(i, carry):
            total = stages[m][z, i].astype(f32) + lands[m][z, i].astype(f32) + lands[m][planes, i].astype(f32)
            lands[m][z, i] = total.astype(bf16)
            return carry

        lax.fori_loop(0, n, body, 0)
        for j in (2 + 2 * ck, 3 + 2 * ck, 4 - 2 * ck, 5 - 2 * ck, 6, 7, 1):
            launch(in_plane, lambda j=j: owner_copy(m, j))
        gots[m][c] = lands[m][z, c]

    def hand_receive(m):
        for j in range(1, n):
            owner_copy(m, j).wait_recv()

    weight_start(0)
    gather_start(first, 0)
    for copy in local[3:]:
        copy.wait()
    for t in range(thirds):
        pl.when(holds[t])(lambda t=t: own_down(t).wait())

    spread = jnp.broadcast_to(pos_row[...].astype(f32), (head, pos_row.shape[1]))
    positions[...] = spread.T
    side = jnp.where(lax.broadcasted_iota(jnp.int32, (1, head), 1) < head // 2, -1.0, 1.0)

    def table(i, carry):
        run = step_cos.shape[0]
        at = rows(i, run)
        start = positions[pl.ds(pl.multiple_of(i * run, run), 1)] * inverse_ref[...]
        start_cos, start_sin = jnp.cos(start), jnp.sin(start)
        cosine[at] = start_cos * step_cos[...] - start_sin * step_sin[...]
        sine[at] = (start_sin * step_cos[...] + start_cos * step_sin[...]) * side
        return carry

    def turn_over(src, dst):
        def body(i, carry):
            at = rows(i, block)
            dst[:, at] = src[at].T
            return carry

        lax.fori_loop(0, n, body, 0)

    lax.fori_loop(0, 2 * n, table, 0)
    weight_hop(0, 1)
    gather_finish(first, 0)
    weight_hop(0, 2)
    weight_start(1)
    weight_start(value_index)
    gather_start(dy_all, 1)
    turn_over(first, first_t)
    weight_hop(0, 3)
    weight_start(2)
    weight_start(3)

    def turn(value, at):
        return value * cosine[at] + pltpu.roll(value, head // 2, 1) * sine[at]

    def turn_back(grad, at):
        return grad * cosine[at] - pltpu.roll(grad, head // 2, 1) * sine[at]

    def project(i, carry):
        at = rows(i, 2 * block)
        result = dot(first[at], w_qkv[:, :qw + kw])
        raw[at] = result
        for h in range(group + 1):
            part = result[:, h * head:(h + 1) * head]
            inv = lax.rsqrt(jnp.mean(part * part, -1, keepdims=True) + epsilon)
            gain = qg_ref[...] if h < group else kg_ref[...]
            turned = turn(part * inv * gain, at)
            if h < group:
                queries[at, h * head:(h + 1) * head] = (turned * (scale * log2e)).astype(bf16)
            else:
                low_keys = turned.astype(bf16)
                keys[at] = low_keys
                keys_t[:, at] = low_keys.T
        return carry

    def project_values(i, carry):
        at = rows(i, 4 * block)
        low_values = dot(first[at], w_qkv[:, qw + kw:]).astype(bf16)
        values[at] = low_values
        values_t[:, at] = low_values.T
        return carry

    lax.fori_loop(0, n // 4, project, 0)
    weight_hop(1, 1)
    weight_hop(value_index, 1)
    lax.fori_loop(n // 4, n // 2, project, 0)
    weight_hop(1, 2)
    weight_hop(value_index, 2)
    gather_finish(dy_all, 1)

    def stack(ref, at):
        return jnp.concatenate([ref[at, h * head:(h + 1) * head] for h in range(group)], 0)

    def attend(place, carry):
        at = rows(place, 2 * block)
        scores = dot_nt(keys[...], stack(queries, at))
        allowed = positions[...] <= pos_row[:, rows(2 * place, block)].astype(f32)
        later = positions[...] <= pos_row[:, rows(2 * place + 1, block)].astype(f32)
        weight = jnp.concatenate(
            [jnp.exp2(jnp.where(later if k % 2 else allowed, scores[:, k * block:(k + 1) * block], masked_score))
             for k in range(2 * group)], 1)
        probs[place] = weight.astype(bf16)
        sums[place] = 1.0 / jnp.sum(weight, 0, keepdims=True)
        pl.when(place == 1)(lambda: weight_hop(1, 3))
        pl.when(place == 2)(lambda: hop_third(0, 1))
        pl.when(place == 3)(lambda: weight_hop(value_index, 3))
        return carry

    def attend_mix(place):
        at = rows(place, 2 * block)
        result = dot(values_t[...], probs[place]) * sums[place]
        mixed_t[place] = result
        for h in range(group):
            mixed_low[at, h * head:(h + 1) * head] = result[:, 2 * h * block:2 * (h + 1) * block].T.astype(bf16)

    def hop_third(t, d):
        weight_hop(2 + 2 * t, d)
        weight_hop(3 + 2 * t, d)

    lax.fori_loop(0, n // 2, attend, 0)
    hop_third(0, 2)
    weight_start(4)
    weight_start(5)
    lax.fori_loop(0, n // 4, project_values, 0)
    hand_arrive(1)
    drain(in_plane)
    sum_start(
        0, mixed_low, lambda left: dot(left, w_out[...]), attend_mix, None,
        (lambda: None, lambda: hop_third(1, 1)))
    weight_start(6)
    weight_start(7)
    hop_third(0, 3)
    turn_over(dy_all, dy_t)
    hop_third(1, 2)
    mid = x_ref[...].astype(f32) + sum_finish(0)
    middle[...] = mid
    mid_scale = lax.rsqrt(jnp.mean(mid * mid, -1, keepdims=True) + epsilon)
    second[rows(c, block)] = (mid * mid_scale * fg_ref[...]).astype(bf16)
    gather_start(second, 2)
    hop_third(2, 1)

    def feed(t, at):
        units, pair = slice(t * pw, (t + 1) * pw), 2 * pw * t
        both = dot(second[at], w_gu[:, pair:pair + 2 * pw])
        back = dot_nt(dy_all[at], w_down[units])
        gate, up = both[:, :pw], both[:, pw:]
        sig = 1.0 / (1.0 + jnp.exp(-gate))
        silu = gate * sig
        hidden[at, units] = (silu * up).astype(bf16)
        d_gu[at, pair:pair + pw] = (back * up * sig * (1.0 + gate * (1.0 - sig))).astype(bf16)
        d_gu[at, pair + pw:pair + 2 * pw] = (back * silu).astype(bf16)

    def feed_arriving(slot, carry):
        gather_step(second, 2, slot)
        at = rows(chip(slot), 2 * block)
        feed(0, at)
        second_t[:, at] = second[at].T
        pl.when(slot == 2)(lambda: hop_third(2, 2))
        return carry

    def third_grad(t):
        weight_grad(t, [
            (second_t, lambda: d_gu[:, 2 * pw * t:2 * pw * (t + 1)]),
            (dy_t, lambda: hidden[:, t * pw:(t + 1) * pw]),
        ])

    def feed_third(t):
        def body(i, carry):
            feed(t, rows(i, 2 * block))
            return carry

        lax.fori_loop(0, n // 2, body, 0)

    lax.fori_loop(0, n // 2, feed_arriving, 0)
    gather_sent(second, 2)
    hop_third(1, 3)
    third_grad(0)
    feed_third(1)
    hop_third(2, 3)
    sum_start(
        1, d_gu, lambda left: dot_nt(left, w_gu[...]),
        lambda place: feed(thirds - 1, rows(place, 2 * block)))
    third_grad(1)
    third_grad(2)
    d_second = sum_finish(1)

    def norm_back(value, gain, grad):
        inv = lax.rsqrt(jnp.mean(value * value, -1, keepdims=True) + epsilon)
        weighted = grad * gain
        inner = jnp.mean(weighted * value, -1, keepdims=True)
        result = inv * weighted - value * (inv * inv * inv * inner)
        return result, jnp.sum(grad * value * inv, 0, keepdims=True)

    gain_own[...] = jnp.zeros_like(gain_own)
    part, gain_own[1:2, :] = norm_back(middle[...], fg_ref[...], d_second)
    d_mid = dy_ref[...].astype(f32) + part
    d_middle[...] = d_mid
    drain(in_plane)
    dmid[rows(c, block)] = d_mid.astype(bf16)
    gather_start(dmid, 3)
    sum_start(2, hidden, lambda left: dot(left, w_down[...]))
    drain(weight_sends)
    grad_near(0)

    dk_acc[...] = jnp.zeros_like(dk_acc)
    dv_acc[...] = jnp.zeros_like(dv_acc)

    def attend_back(slot, q_sum):
        gather_step(dmid, 3, slot)
        place = chip(slot)
        at = rows(place, 2 * block)
        d_mix = dot_nt(w_out[...], dmid[at])
        dmid_t[:, at] = dmid[at].T
        pl.when(slot == 3)(lambda: weight_grad(3, [(dmid_t, lambda: mixed_low[...])]))
        d_mix_t = jnp.concatenate([d_mix[h * head:(h + 1) * head] for h in range(group)], 1)
        d_mix_t = (d_mix_t.astype(bf16).astype(f32) * sums[place]).astype(bf16)
        delta = jnp.sum(d_mix_t.astype(f32) * mixed_t[place], 0, keepdims=True)
        weight = probs[place]
        d_prob = dot(values[...], d_mix_t)
        d_score = (weight.astype(f32) * (d_prob - delta)).astype(bf16)
        d_query = dot(keys_t[...], d_score) * scale
        for h in range(group):
            grad = turn_back(d_query[:, 2 * h * block:2 * (h + 1) * block].T, at)
            part, gain_part = norm_back(raw[at, h * head:(h + 1) * head], qg_ref[...], grad)
            d_qkv[at, h * head:(h + 1) * head] = part.astype(bf16)
            q_sum = q_sum + gain_part
        pl.when(slot == 2)(lambda: grad_near(1))
        dv_acc[...] += dot(weight, d_mix_t.T)
        dk_acc[...] += dot(d_score, stack(queries, at))
        return q_sum

    zero = jnp.zeros((1, head), f32)
    gain_own[2:3, 0:head] = lax.fori_loop(0, n // 2, attend_back, zero)
    gather_sent(dmid, 3)
    weight_grad(4, [(first_t, lambda: d_qkv[:, :qw])])
    grad_far(0)

    def project_back(i, k_sum):
        at = rows(i, 2 * block)
        grad = turn_back(dk_acc[at] * (1.0 / log2e), at)
        part, gain_part = norm_back(raw[at, qw:qw + kw], kg_ref[...], grad)
        d_qkv[at, qw:qw + kw] = part.astype(bf16)
        d_qkv[at, qw + kw:] = dv_acc[at].astype(bf16)
        return k_sum + gain_part

    gain_own[3:4, 0:head] = lax.fori_loop(0, n // 2, project_back, zero)

    weight_grad(5, [(first_t, lambda: d_qkv[:, qw:])])
    grad_far(1)
    grad_near(2)
    hand_out(0)
    drain(in_plane)
    sum_start(3, d_qkv, lambda left: dot_nt(left, w_qkv[...]))
    grad_far(2)
    grad_near(3)
    hand_out(1)
    grad_far(3)
    grad_near(4)
    out_ref[...] = (middle[...] + sum_finish(2)).astype(bf16)
    grad_far(4)
    grad_near_far(5)
    hand_out(2)
    grad_near_inner(5)
    grad_far(5)
    x_part, gain_own[0:1, :] = norm_back(x_ref[...].astype(f32), ag_ref[...], sum_finish(3))
    dx_ref[...] = d_middle[...] + x_part

    def gain_plane_copy(j):
        return remote(gain_own, gain_plane.at[c], gp_send.at[j], gp_recv.at[j], partner(j), z)

    def gain_copy(d):
        return remote(gain_all.at[z], gain_all.at[z], gz_send.at[d], gz_recv.at[d], c, lax.rem(z + d, planes))

    for j in range(1, n):
        launch(in_plane, lambda j=j: gain_plane_copy(j))
    gain_plane[c] = gain_own[...]
    hand_out(3)
    for j in range(1, n):
        gain_plane_copy(j).wait_recv()
    total = gain_plane[0]
    for i in range(1, n):
        total = total + gain_plane[i]
    gain_all[z] = total
    for d in range(1, planes):
        launch(along, lambda d=d: gain_copy(d))
    hand_out(4)
    for d in range(1, planes):
        origin = gain_all.at[lax.rem(z + planes - d, planes)]
        remote(origin, origin, gz_send.at[d], gz_recv.at[d], c, z).wait_recv()
    total = gain_all[0]
    for i in range(1, planes):
        total = total + gain_all[i]
    gains_ref[...] = total

    for m in range(4):
        hand_receive(m)
    hand_out(5)
    drain(along)
    hand_receive(4)
    hand_receive(5)
    drain(in_plane)


def finish_kernel(
    n, head, out_in, dx_in, gains_in, got_a, got_b, got_c, got_out, got_q, got_kv,
    out_ref, dx_ref, ag_ref, q_ref, k_ref, v_ref, qg_ref, kg_ref, o_ref, fg_ref, g_ref, u_ref, d_ref,
):
    out_ref[...] = out_in[...]
    dx_ref[...] = dx_in[...]
    ag_ref[...] = gains_in[0:1, :]
    fg_ref[...] = gains_in[1:2, :]
    qg_ref[...] = gains_in[2:3, 0:head]
    kg_ref[...] = gains_in[3:4, 0:head]
    qw, kw = q_ref.shape[1] // n, k_ref.shape[1] // n
    pw = got_a.shape[2] // 3
    thirds = (got_a, got_b, got_c)
    for i in range(n):
        q_ref[:, i * qw:(i + 1) * qw] = got_q[i].astype(f32)
        k_ref[:, i * kw:(i + 1) * kw] = got_kv[i, :, 0:kw].astype(f32)
        v_ref[:, i * kw:(i + 1) * kw] = got_kv[i, :, kw:].astype(f32)
        o_ref[:, i * qw:(i + 1) * qw] = got_out[i].astype(f32)
        for t, got in enumerate(thirds):
            plane, unit = hidden_block(i, t)
            at = plane * (g_ref.shape[1] // 4) + unit * pw
            g_ref[:, at:at + pw] = got[i, :, 0:pw].astype(f32)
            u_ref[:, at:at + pw] = got[i, :, pw:2 * pw].astype(f32)
            d_ref[:, at:at + pw] = got[i, :, 2 * pw:].astype(f32)


def plane_device(
    layer_input,
    token_positions,
    attention_gain,
    query_weight,
    key_matrix,
    value_matrix,
    query_gain,
    key_norm_gain,
    output_weight,
    feedforward_gain,
    gate_weight,
    up_weight,
    down_weight,
    out_cotangent,
):
    n = lax.axis_size("ctx")
    planes = lax.axis_size("fsdp")
    block, width = layer_input.shape[1:]
    length = token_positions.shape[1]
    head = query_gain.shape[0]
    qw = query_weight.shape[1] // n
    kw = key_matrix.shape[1] // n
    fw = gate_weight.shape[1] // n
    group = qw // head
    per = block // planes
    half = head // 2
    inverse = np.power(rope_base, -np.arange(half) * 2.0 / head).astype(np.float32)
    inverse = np.concatenate([inverse, inverse])[None]
    steps = np.arange(block // 2)[:, None] * inverse.astype(np.float64)
    step_cos, step_sin = (jnp.asarray(f(steps).astype(np.float32)) for f in (np.cos, np.sin))
    inverse = jnp.asarray(inverse)
    vmem = pl.BlockSpec(memory_space=pltpu.VMEM)
    hbm = pl.BlockSpec(memory_space=pl.ANY)
    dma = pltpu.SemaphoreType.DMA
    sizes = (fw, fw, fw, qw, qw, 2 * kw)
    low = lambda *shape: pltpu.VMEM(shape, bf16)
    wide = lambda *shape: pltpu.VMEM(shape, f32)
    scratch = [
        low(width, qw + 2 * kw), low(width, 2 * fw), low(qw, width), low(fw, width),
        low(planes * (output_weight.shape[0] // n), width),
        low(length, width), low(length, width), low(length, width),
        low(width, length), low(width, length), low(width, length),
        wide(length, head), wide(length, head), wide(length, head),
        wide(length, qw + kw), low(length, qw), low(length, kw), low(length, kw),
        low(kw, length), low(kw, length), low(n // 2, length, 2 * group * block), wide(n // 2, 1, 2 * group * block),
        wide(n // 2, head, 2 * group * block), low(length, qw),
        low(length, fw), low(length, 2 * fw), low(length, qw + 2 * kw),
        wide(length, kw), wide(length, kw),
    ]
    scratch += [low(planes, n, per, size) for size in sizes]
    scratch += [low(planes + 1, n, per, size) for size in sizes]
    scratch += [low(2, 4, block, width) for _ in range(4)] + [wide(2, block, width), wide(2, block, width)]
    scratch += [
        wide(block, width), wide(block, width), wide(8, width), wide(n, 8, width), wide(planes, 8, width),
        dma((13,)), dma((9, 6)), dma((9, planes)), dma((1, 7)), dma((1, 4)),
        dma((4, n)), dma((4, n)), dma((4, 4)), dma((4, 4)), dma((4, 4)), dma((4, 4)),
        dma((6, planes)), dma((6, planes + 1)), dma((6, n)), dma((6, n)), dma((n,)), dma((n,)),
        dma((planes,)), dma((planes,)),
    ]
    shapes = [
        jax.ShapeDtypeStruct((block, width), bf16),
        jax.ShapeDtypeStruct((block, width), f32),
        jax.ShapeDtypeStruct((8, width), f32),
    ] + [jax.ShapeDtypeStruct((n, per, size), bf16) for size in sizes]
    results = pl.pallas_call(
        functools.partial(layer_kernel, n, planes, block, head, group, fw),
        out_shape=shapes,
        in_specs=[vmem] * 10 + [hbm] * 7,
        out_specs=[vmem] * len(shapes),
        scratch_shapes=scratch,
        compiler_params=pltpu.CompilerParams(
            collective_id=0, has_side_effects=True, vmem_limit_bytes=60 * 1024 * 1024),
    )(
        layer_input[0], out_cotangent[0], token_positions, inverse, step_cos, step_sin,
        attention_gain[None], feedforward_gain[None], query_gain[None], key_norm_gain[None],
        query_weight, key_matrix, value_matrix, output_weight, gate_weight, up_weight, down_weight,
    )
    plain = lambda rows, columns, kind=f32: jax.ShapeDtypeStruct((rows, columns), kind)
    finals = [
        plain(block, width, bf16), plain(block, width), plain(1, width),
        plain(per, n * qw), plain(per, n * kw), plain(per, n * kw), plain(1, head), plain(1, head),
        plain(per, n * qw), plain(1, width), plain(per, n * fw), plain(per, n * fw), plain(per, n * fw),
    ]
    done = pl.pallas_call(
        functools.partial(finish_kernel, n, head),
        out_shape=finals,
        in_specs=[vmem] * len(shapes),
        out_specs=[vmem] * len(finals),
    )(*results)
    out, dx, ag, q, k, v, qg, kg, o, fg, g, u, d = done
    return out[None], dx[None], ag[0], q, k, v, qg[0], kg[0], o.T, fg[0], g, u, d.T


def solution(mesh):
    in_specs = (
        P("fsdp", "ctx", None),
        P("fsdp", None),
        P(),
        P("fsdp", None),
        P("fsdp", None),
        P("fsdp", None),
        P(),
        P(),
        P("fsdp", None),
        P(),
        P("fsdp", None),
        P("fsdp", None),
        P("fsdp", None),
        P("fsdp", "ctx", None),
    )
    out_specs = (
        P("fsdp", "ctx", None),
        P("fsdp", "ctx", None),
        P(),
        P(("ctx", "fsdp"), None),
        P(("ctx", "fsdp"), None),
        P(("ctx", "fsdp"), None),
        P(),
        P(),
        P(None, ("ctx", "fsdp")),
        P(),
        P(("ctx", "fsdp"), None),
        P(("ctx", "fsdp"), None),
        P(None, ("ctx", "fsdp")),
    )

    def run(*arguments):
        n, planes = mesh.shape["ctx"], mesh.shape["fsdp"]
        key_heads = arguments[4].shape[1] // arguments[6].shape[0]
        whole_heads = n == 8 and planes == 4 and key_heads == n
        return jax.shard_map(
            plane_device if whole_heads else on_device,
            mesh=mesh, in_specs=in_specs, out_specs=out_specs, check_vma=False,
        )(*arguments)

    return run
```

```python
import functools

import jax
import jax.numpy as jnp
import numpy as np
from jax import lax
from jax.experimental import pallas as pl
from jax.experimental.pallas import tpu as pltpu
from jax.sharding import PartitionSpec as P

epsilon = 1e-06
rope_base = 1000000.0
masked_score = -1e30


def from_behind(block, axis, distance):
    devices = range(lax.axis_size(axis))
    route = [((i - distance) % len(devices), i) for i in devices]
    return lax.ppermute(block, axis, route)


def rotate(value_rows):
    half = value_rows.shape[-1] // 2
    return jnp.concatenate([-value_rows[..., half:], value_rows[..., :half]], -1)


def rotate_back(value_rows):
    half = value_rows.shape[-1] // 2
    return jnp.concatenate([value_rows[..., half:], -value_rows[..., :half]], -1)


def rope_tables(token_offsets, head_size):
    half = head_size // 2
    inverse = rope_base ** (-(jnp.arange(half).astype(jnp.float32) * 2.0) / head_size)
    angles = token_offsets.astype(jnp.float32)[:, None] * inverse[None, :]
    cosine = jnp.cos(angles)
    sine = jnp.sin(angles)
    return (jnp.concatenate([cosine, cosine], -1), jnp.concatenate([sine, sine], -1))


def norm_scale(value_rows):
    return lax.rsqrt(jnp.mean(value_rows * value_rows, -1, keepdims=True) + epsilon)


def norm_back(value_rows, scale, gain, grad):
    weighted = grad * gain
    inner = jnp.mean(weighted * value_rows, -1, keepdims=True)
    result = scale * weighted - value_rows * scale * scale * scale * inner
    gain_part = jnp.sum((grad * value_rows * scale).reshape(-1, gain.shape[0]), 0)
    return (result, gain_part)


def row_products(left, pieces):
    return tuple((jnp.dot(left, piece, preferred_element_type=jnp.float32) for piece in pieces))


def column_products(rights, pieces):
    total = jnp.einsum("tc,rc->tr", rights[0], pieces[0], preferred_element_type=jnp.float32)
    for right, piece in zip(rights[1:], pieces[1:]):
        total = total + jnp.einsum("tc,rc->tr", right, piece, preferred_element_type=jnp.float32)
    return total


def on_device(
    layer_input,
    token_positions,
    attention_gain,
    query_weight,
    key_matrix,
    value_matrix,
    query_gain,
    key_norm_gain,
    output_weight,
    feedforward_gain,
    gate_weight,
    up_weight,
    down_weight,
    out_cotangent,
):
    hidden_in = layer_input[0].astype(jnp.float32)
    count = hidden_in.shape[0]
    head_size = query_gain.shape[0]
    query_width = query_weight.shape[1]
    key_width = key_matrix.shape[1]
    inner_width = gate_weight.shape[1]
    heads = query_width // head_size
    key_heads = key_width // head_size
    group = heads // key_heads
    scale = head_size ** (-0.5)
    cycles = lax.axis_size("ctx")
    own_index = lax.axis_index("ctx")
    sequence_pos = token_positions[0]
    token_offsets = lax.dynamic_slice_in_dim(sequence_pos, own_index * count, count)
    cosine, sine = rope_tables(token_offsets, head_size)
    cosine = cosine[:, None, :]
    sine = sine[:, None, :]
    first_scale = norm_scale(hidden_in)
    first = (hidden_in * first_scale * attention_gain).astype(jnp.bfloat16)
    query_raw, key_unnormed, value_unnormed = row_products(
        first,
        (
            lax.all_gather(query_weight, "fsdp", axis=0, tiled=True),
            lax.all_gather(key_matrix, "fsdp", axis=0, tiled=True),
            lax.all_gather(value_matrix, "fsdp", axis=0, tiled=True),
        ),
    )
    query_heads = query_raw.reshape(count, heads, head_size)
    query_scale = norm_scale(query_heads)
    query_normed = query_heads * query_scale * query_gain
    query_rot = query_normed * cosine + rotate(query_normed) * sine
    query_grouped = (
        query_rot.reshape(count, key_heads, group, head_size)
        .transpose(1, 2, 0, 3)
        .astype(jnp.bfloat16)
    )
    key_heads_raw = key_unnormed.reshape(count, key_heads, head_size)
    key_scale = norm_scale(key_heads_raw)
    key_normed = key_heads_raw * key_scale * key_norm_gain
    key_low = (
        (key_normed * cosine + rotate(key_normed) * sine)
        .reshape(count, key_width)
        .astype(jnp.bfloat16)
    )
    value_low = value_unnormed.astype(jnp.bfloat16)
    rowmax = jnp.full((key_heads, group, count), masked_score, jnp.float32)
    keys_piece = lax.all_gather(key_low, "ctx", axis=0, tiled=True).reshape(
        -1, key_heads, head_size
    )
    values_piece = lax.all_gather(value_low, "ctx", axis=0, tiled=True).reshape(
        -1, key_heads, head_size
    )
    key_pos = sequence_pos
    allowed = token_offsets[:, None] >= key_pos[None, :]
    scores = (
        jnp.einsum("kgtd,skd->kgts", query_grouped, keys_piece, preferred_element_type=jnp.float32)
        * scale
    )
    scores = jnp.where(allowed, scores, masked_score)
    newmax = jnp.maximum(rowmax, jnp.max(scores, -1))
    weights = jnp.where(allowed, jnp.exp(scores - newmax[..., None]), 0.0)
    accum = jnp.einsum(
        "kgts,skd->kgtd",
        weights.astype(jnp.bfloat16),
        values_piece,
        preferred_element_type=jnp.float32,
    )
    rowsum = jnp.sum(weights, -1)
    accum, rowmax, rowsum = (accum, newmax, rowsum)
    normalized = accum / rowsum[..., None]
    logsum = rowmax + jnp.log(rowsum)
    attention_low = (
        normalized.transpose(2, 0, 1, 3).reshape(count, query_width).astype(jnp.bfloat16)
    )
    output_whole = lax.all_gather(output_weight, "fsdp", axis=0, tiled=True)
    branch_out = jnp.dot(attention_low, output_whole, preferred_element_type=jnp.float32)
    middle = hidden_in + branch_out
    second_scale = norm_scale(middle)
    second = (middle * second_scale * feedforward_gain).astype(jnp.bfloat16)
    gate, up = row_products(
        second,
        (
            lax.all_gather(gate_weight, "fsdp", axis=0, tiled=True),
            lax.all_gather(up_weight, "fsdp", axis=0, tiled=True),
        ),
    )
    sigmoid_gate = jax.nn.sigmoid(gate)
    silu_gate = gate * sigmoid_gate
    hidden_low = (silu_gate * up).astype(jnp.bfloat16)
    (down_out,) = row_products(
        hidden_low, (lax.all_gather(down_weight, "fsdp", axis=0, tiled=True),)
    )
    layer_output = (middle + down_out).astype(jnp.bfloat16)[None]
    cotangent = out_cotangent[0]
    hidden_grad = column_products(
        (cotangent,), lax.all_gather((down_weight,), "fsdp", axis=0, tiled=True)
    )
    up_low = (hidden_grad * silu_gate).astype(jnp.bfloat16)
    gate_low = (hidden_grad * up * sigmoid_gate * (1.0 + gate * (1.0 - sigmoid_gate))).astype(
        jnp.bfloat16
    )
    second_grad = column_products(
        (gate_low, up_low), lax.all_gather((gate_weight, up_weight), "fsdp", axis=0, tiled=True)
    )
    middle_part, feedforward_part = norm_back(middle, second_scale, feedforward_gain, second_grad)
    middle_grad = cotangent.astype(jnp.float32) + middle_part
    middle_low = middle_grad.astype(jnp.bfloat16)
    attention_grad = jnp.einsum(
        "tc,rc->tr", middle_low, output_whole, preferred_element_type=jnp.float32
    )
    attention_grad_low = attention_grad.astype(jnp.bfloat16)
    mixed_grad = attention_grad_low.reshape(count, key_heads, group, head_size).transpose(
        1, 2, 0, 3
    )
    delta = jnp.sum(mixed_grad.astype(jnp.float32) * normalized, -1)

    def cycle_step(index, carry):
        keys_held, values_held, key_acc, value_acc, query_acc = carry
        anchor = (own_index - index) % cycles
        key_pos = lax.dynamic_slice_in_dim(sequence_pos, anchor * count, count)
        keys_piece = keys_held.astype(jnp.bfloat16).reshape(count, key_heads, head_size)
        values_piece = values_held.astype(jnp.bfloat16).reshape(count, key_heads, head_size)
        allowed = token_offsets[:, None] >= key_pos[None, :]
        scores = (
            jnp.einsum(
                "kgtd,skd->kgts", query_grouped, keys_piece, preferred_element_type=jnp.float32
            )
            * scale
        )
        probs = jnp.where(allowed, jnp.exp(scores - logsum[..., None]), 0.0)
        value_acc = value_acc + jnp.einsum(
            "kgts,kgtd->skd",
            probs.astype(jnp.bfloat16),
            mixed_grad,
            preferred_element_type=jnp.float32,
        ).reshape(count, key_width)
        prob_grad = jnp.einsum(
            "kgtd,skd->kgts", mixed_grad, values_piece, preferred_element_type=jnp.float32
        )
        score_grad = (probs * (prob_grad - delta[..., None])).astype(jnp.bfloat16)
        query_acc = (
            query_acc
            + jnp.einsum(
                "kgts,skd->kgtd", score_grad, keys_piece, preferred_element_type=jnp.float32
            )
            * scale
        )
        key_acc = (
            key_acc
            + jnp.einsum(
                "kgts,kgtd->skd", score_grad, query_grouped, preferred_element_type=jnp.float32
            ).reshape(count, key_width)
            * scale
        )
        moved = (
            from_behind(keys_held.astype(jnp.bfloat16), "ctx", 1).astype(keys_held.dtype),
            from_behind(values_held.astype(jnp.bfloat16), "ctx", 1).astype(values_held.dtype),
            from_behind(key_acc.astype(jnp.bfloat16), "ctx", 1).astype(key_acc.dtype),
            from_behind(value_acc.astype(jnp.bfloat16), "ctx", 1).astype(value_acc.dtype),
        )
        return (moved[0], moved[1], moved[2], moved[3], query_acc)

    start_cycle = (
        key_low.astype(jnp.float32),
        value_low.astype(jnp.float32),
        jnp.zeros((count, key_width), jnp.float32),
        jnp.zeros((count, key_width), jnp.float32),
        jnp.zeros((key_heads, group, count, head_size), jnp.float32),
    )
    cycle_done = lax.fori_loop(0, cycles, cycle_step, start_cycle)
    key_acc = cycle_done[2]
    value_acc = cycle_done[3]
    query_acc = cycle_done[4]
    query_rot_grad = query_acc.transpose(2, 0, 1, 3).reshape(count, heads, head_size)
    query_normed_grad = query_rot_grad * cosine + rotate_back(query_rot_grad * sine)
    query_heads_grad, query_part = norm_back(
        query_heads, query_scale, query_gain, query_normed_grad
    )
    query_low_grad = query_heads_grad.reshape(count, query_width).astype(jnp.bfloat16)
    key_rot_grad = key_acc.reshape(count, key_heads, head_size)
    key_normed_grad = key_rot_grad * cosine + rotate_back(key_rot_grad * sine)
    key_heads_grad, key_part = norm_back(key_heads_raw, key_scale, key_norm_gain, key_normed_grad)
    key_low_grad = key_heads_grad.reshape(count, key_width).astype(jnp.bfloat16)
    value_low_grad = value_acc.astype(jnp.bfloat16)
    first_grad = column_products(
        (query_low_grad, key_low_grad, value_low_grad),
        lax.all_gather((query_weight, key_matrix, value_matrix), "fsdp", axis=0, tiled=True),
    )
    input_part, attention_part = norm_back(hidden_in, first_scale, attention_gain, first_grad)
    input_gradient = (middle_grad + input_part)[None]
    rights_first = jnp.concatenate([query_low_grad, key_low_grad, value_low_grad], 1)
    rights_second = jnp.concatenate([gate_low, up_low], 1)
    pairs = (
        (first, rights_first),
        (second, rights_second),
        (middle_low, attention_low),
        (cotangent, hidden_low),
    )
    parts = []
    for left, right in pairs:
        parts.append(jnp.einsum("tr,tc->rc", left, right, preferred_element_type=jnp.float32))
    sums = lax.psum_scatter(
        jnp.concatenate(parts, 1), ("ctx", "fsdp"), scatter_dimension=0, tiled=True
    )
    edges = [0, query_width, query_width + key_width, query_width + 2 * key_width]
    edges = edges + [edges[3] + inner_width, edges[3] + 2 * inner_width]
    edges = edges + [edges[5] + query_width, edges[5] + query_width + inner_width]
    query_gradient = sums[:, edges[0] : edges[1]]
    key_gradient = sums[:, edges[1] : edges[2]]
    value_gradient = sums[:, edges[2] : edges[3]]
    gate_gradient = sums[:, edges[3] : edges[4]]
    up_gradient = sums[:, edges[4] : edges[5]]
    output_gradient = sums[:, edges[5] : edges[6]].T
    down_gradient = sums[:, edges[6] : edges[7]].T
    attention_total, query_total, key_total, feedforward_total = lax.psum(
        (attention_part, query_part, key_part, feedforward_part), ("ctx", "fsdp")
    )
    return (
        layer_output,
        input_gradient,
        attention_total,
        query_gradient,
        key_gradient,
        value_gradient,
        query_total,
        key_total,
        output_gradient,
        feedforward_total,
        gate_gradient,
        up_gradient,
        down_gradient,
    )


MESH = pl.DeviceIdType.MESH
f32 = jnp.float32
bf16 = jnp.bfloat16


def dot(left, right):
    return jnp.dot(left, right, preferred_element_type=f32)


def dot_nt(left, right):
    return lax.dot_general(left, right, (((1,), (1,)), ((), ())), preferred_element_type=f32)


def dot_tn(left, right):
    return lax.dot_general(left, right, (((0,), (0,)), ((), ())), preferred_element_type=f32)


def hidden_block(device, third):
    def plane(i, t):
        return ((3, 1, 2), (0, 2, 1), (0, 3, 2), (3, 0, 1))[i // 4 * 2 + i % 2][t]

    own = plane(device, third)
    return own, sum(plane(i, t) == own for i in range(device) for t in range(3))


def layer_kernel(
    n, planes, block, head, group, fw,
    x_ref, dy_ref, pos_row, inverse_ref, step_cos, step_sin, ag_ref, fg_ref, qg_ref, kg_ref,
    wq, wk, wv, wo, wg, wu, wd,
    out_ref, dx_ref, gains_ref, got_a, got_b, got_c, got_out, got_q, got_kv,
    w_qkv, w_gu, w_out, w_down, t_out,
    first, dy_all, second, first_t, dy_t, second_t,
    positions, cosine, sine,
    raw, queries, keys, values, keys_t, values_t, probs, sums, mixed_t, mixed_low,
    hidden, d_gu, d_qkv, dk_acc, dv_acc,
    stage_a, stage_b, stage_c, stage_out, stage_q, stage_kv,
    land_a, land_b, land_c, land_out, land_q, land_kv,
    rs_sa, rs_ra, rs_sb, rs_rb, rs_kept, rs_acc,
    middle, d_middle, gain_own, gain_plane, gain_all,
    local_sem, wz_send, wz_recv, hand_send, hand_recv,
    ag_send, ag_recv, ra_send, ra_recv, rb_send, rb_recv,
    zr_send, zr_recv, aa_send, aa_recv, gp_send, gp_recv, gz_send, gz_recv,
):
    c = lax.axis_index("ctx")
    z = lax.axis_index("fsdp")
    dmid = first
    dmid_t = second
    cy, cx, ck = lax.div(c, 4), lax.rem(lax.div(c, 2), 2), lax.rem(c, 2)
    ci = lax.rem(c, 4)
    sign = 1 - 2 * ck
    qw, kw = group * head, head
    pw = 128
    thirds = fw // pw
    width = x_ref.shape[1]
    scale = head ** (-0.5)
    log2e = 1.4426950408889634
    gots = (got_a, got_b, got_c, got_out, got_q, got_kv)
    stages = (stage_a, stage_b, stage_c, stage_out, stage_q, stage_kv)
    lands = (land_a, land_b, land_c, land_out, land_q, land_kv)

    def partner(j):
        y = lax.rem(cy + lax.div(j, 4), 2)
        x = lax.rem(cx + lax.rem(lax.div(j, 2), 2), 2)
        k = lax.rem(ck + lax.rem(j, 2), 2)
        return y * 4 + x * 2 + k

    def chip(slot):
        return lax.rem(cy + lax.div(slot, 2), 2) * 2 + lax.rem(cx + lax.rem(slot, 2), 2)

    def rows(start, size):
        return pl.ds(pl.multiple_of(start * size, size), size)

    def remote(src, dst, send, recv, ctx, plane):
        return pltpu.make_async_remote_copy(
            src_ref=src, dst_ref=dst, send_sem=send, recv_sem=recv,
            device_id={"ctx": ctx, "fsdp": plane}, device_id_type=MESH,
        )

    in_plane, along, weight_sends = [], [], []

    def launch(started, copy, when=None):
        if when is None:
            copy().start()
        else:
            pl.when(when)(lambda: copy().start())
        started.append((copy, when))

    def drain(started):
        for copy, when in started:
            if when is None:
                copy().wait_send()
            else:
                pl.when(when)(lambda copy=copy: copy().wait_send())
        started.clear()

    def pick(values):
        return sum(jnp.where(c == i, value, 0) for i, value in enumerate(values))

    unit_plane = [pick([hidden_block(i, t)[0] for i in range(n)]) for t in range(thirds)]
    unit_block = [pick([hidden_block(i, t)[1] for i in range(n)]) for t in range(thirds)]
    plane_blocks = wd.shape[0] // pw

    own_rows = wq.shape[0]
    out_rows = wo.shape[0] // n

    def own_slices():
        mine = rows(z, own_rows)
        pairs = [
            (wq.at[:, rows(c, qw)], w_qkv.at[mine, 0:qw]),
            (wk.at[:, rows(c, kw)], w_qkv.at[mine, qw:qw + kw]),
            (wv.at[:, rows(c, kw)], w_qkv.at[mine, qw + kw:qw + 2 * kw]),
            (wo.at[rows(c, out_rows)], t_out.at[rows(z, out_rows)]),
        ]
        for t in range(thirds):
            at = 2 * pw * t
            unit = unit_plane[t] * plane_blocks + unit_block[t]
            pairs.append((wg.at[:, rows(unit, pw)], w_gu.at[mine, at:at + pw]))
            pairs.append((wu.at[:, rows(unit, pw)], w_gu.at[mine, at + pw:at + 2 * pw]))
        return pairs

    local = [pltpu.make_async_copy(src, dst, local_sem.at[i]) for i, (src, dst) in enumerate(own_slices())]
    for copy in local:
        copy.start()

    def own_down(t):
        return pltpu.make_async_copy(
            wd.at[rows(unit_block[t], pw)], w_down.at[t * pw:(t + 1) * pw], local_sem.at[4 + 2 * thirds + t])

    holds = [unit_plane[t] == z for t in range(thirds)]
    for t in range(thirds):
        pl.when(holds[t])(lambda t=t: own_down(t).start())

    for land in lands:
        @pl.when(z == 0)
        def _(land=land):
            land[0] = jnp.zeros(land.shape[1:], bf16)

        @pl.when(z == planes - 1)
        def _(land=land):
            land[planes] = jnp.zeros(land.shape[1:], bf16)

    barrier = pltpu.get_barrier_semaphore()
    for j in range(1, n):
        pl.semaphore_signal(barrier, inc=1, device_id={"ctx": partner(j), "fsdp": z}, device_id_type=MESH)
    for d in range(1, planes):
        pl.semaphore_signal(
            barrier, inc=1, device_id={"ctx": c, "fsdp": lax.rem(z + d, planes)}, device_id_type=MESH)
    x = x_ref[...].astype(f32)
    x_scale = lax.rsqrt(jnp.mean(x * x, -1, keepdims=True) + epsilon)
    first[rows(c, block)] = (x * x_scale * ag_ref[...]).astype(bf16)
    dy_all[rows(c, block)] = dy_ref[...]
    for copy in local[:3]:
        copy.wait()
    pl.semaphore_wait(barrier, n + planes - 2)

    def inside(t):
        return jnp.logical_and(t >= 0, t < planes)

    weights = [
        (lambda o: w_qkv.at[rows(o, own_rows)], None),
        (lambda o: t_out.at[rows(o, out_rows)], 0),
    ]
    for t in range(thirds):
        weights.append((lambda o, t=t: w_gu.at[rows(o, own_rows), 2 * pw * t:2 * pw * (t + 1)], None))
        weights.append((lambda o, t=t: w_down.at[t * pw:(t + 1) * pw], None))

    def weight_copy(w, slot, origin, target):
        part = weights[w][0](origin)
        return remote(part, part, wz_send.at[w, slot], wz_recv.at[w, origin], c, target)

    def from_plane(w, origin):
        return origin == unit_plane[(w - 3) // 2] if w >= 3 and w % 2 else None

    def both(one, other):
        return one if other is None else jnp.logical_and(one, other)

    def hand_split(origin, valid):
        mine = 2 * origin + cy == c
        return jnp.logical_and(valid, jnp.logical_not(mine)), jnp.logical_and(valid, mine)

    def weight_start(w):
        for side, k in enumerate((2, -2, 1, -1)):
            d = sign * k
            launch(
                weight_sends, lambda side=side, d=d: weight_copy(w, side, z, z + d),
                both(inside(z + d), from_plane(w, z)))
        if weights[w][1] is not None:
            hand_over(w, z, 0, *hand_split(z, True))

    def hand_target(h):
        return lambda i: w_out.at[rows(i, out_rows)]

    def hand_copy(w, origin, slot):
        h = weights[w][1]
        return remote(
            weights[w][0](origin), hand_target(h)(ci), hand_send.at[h, slot], hand_recv.at[h, ci], 2 * origin + cy, z)

    def hand_over(w, origin, slot, away, here):
        launch(in_plane, lambda: hand_copy(w, origin, slot), away)

        @pl.when(here)
        def _():
            hand_target(weights[w][1])(ci)[...] = weights[w][0](origin)[...]

    def hand_arrive(w):
        h = weights[w][1]
        for i in range(4):
            @pl.when(4 * ck + i != c)
            def _(i=i):
                part = hand_target(h)(i)
                remote(part, part, hand_send.at[h, 0], hand_recv.at[h, i], c, z).wait_recv()

    hops = {}
    for w in range(len(weights)):
        for d in range(1, planes):
            for side, way in enumerate((1, -1)):
                origin = z - way * d
                valid = both(inside(origin), from_plane(w, origin))
                passed = jnp.logical_and(valid, inside(z + way))
                split = None if weights[w][1] is None else hand_split(origin, valid)
                hops[w, d, side] = origin, z + way, valid, passed, split

    def weight_hop(w, d):
        for side in range(2):
            origin, following, valid, passed, split = hops[w, d, side]
            pl.when(valid)(lambda: weight_copy(w, 0, origin, z).wait_recv())
            if d == 2:
                launch(
                    weight_sends,
                    lambda side=side, origin=origin, following=following: weight_copy(
                        w, 4 + side, origin, following),
                    passed)
            if split is not None:
                hand_over(w, origin, 2 * d - 1 + side, *split)

    def gather_copy(buf, g, j, send, origin, target):
        part = buf.at[rows(origin, block)]
        return remote(part, part, ag_send.at[g, send], ag_recv.at[g, j], target, z)

    def gather_start(buf, g):
        for j in (1, 2 + 2 * ck, 4 - 2 * ck):
            launch(in_plane, lambda j=j: gather_copy(buf, g, j, j, c, partner(j)))

    def gather_half(buf, g, j):
        half = block // 2
        part = buf.at[pl.ds(pl.multiple_of(partner(j) * block + (half if j == 2 else 0), half), half)]
        at = 0 if j == 2 else 6
        return remote(part, part, ag_send.at[g, at], ag_recv.at[g, at], partner(6 - j), z)

    def gather_diagonal(buf, g):
        half = block // 2
        for at in (6, 0):
            part = buf.at[pl.ds(pl.multiple_of(partner(6) * block + (0 if at == 6 else half), half), half)]
            remote(part, part, ag_send.at[g, at], ag_recv.at[g, at], c, z).wait_recv()

    def gather_forward(buf, g, j):
        return gather_copy(buf, g, j + 1, j + 1, partner(j), partner(1))

    def gather_take(buf, g, j):
        if j == 6:
            gather_diagonal(buf, g)
        else:
            gather_copy(buf, g, j, j, partner(j), c).wait_recv()
            gather_half(buf, g, j).start()
        gather_forward(buf, g, j).start()

    def gather_sent(buf, g):
        for j in (2, 4, 6):
            in_plane.append((lambda j=j: gather_forward(buf, g, j), None))
            if j < 6:
                in_plane.append((lambda j=j: gather_half(buf, g, j), None))

    def gather_finish(buf, g):
        for j in (2, 4, 6):
            gather_take(buf, g, j)
        gather_sent(buf, g)
        for j in (1, 3, 5, 7):
            gather_copy(buf, g, j, j, partner(j), c).wait_recv()

    def gather_step(buf, g, slot):
        @pl.when(slot == 1)
        def _():
            gather_take(buf, g, 2)
            gather_take(buf, g, 4)

        pl.when(slot == 3)(lambda: gather_take(buf, g, 6))
        gather_copy(buf, g, 2 * slot + 1, 0, partner(2 * slot + 1), c).wait_recv()

    def sum_pair_copy(s, slot):
        return remote(rs_sa.at[s % 2, slot], rs_ra.at[s % 2, slot], ra_send.at[s, slot], ra_recv.at[s, slot], partner(1), z)

    def sum_chip_copy(s, slot):
        return remote(
            rs_sb.at[s % 2, slot], rs_rb.at[s % 2, slot], rb_send.at[s, slot], rb_recv.at[s, slot], partner(2 * slot), z)

    def sum_half_copy(s, slot):
        half = block // 2
        at = pl.ds(pl.multiple_of((slot - 1) * half, half), half)
        return remote(
            rs_sb.at[s % 2, 3, at], rs_rb.at[s % 2, 3, at], rb_send.at[s, 6 - 3 * slot], rb_recv.at[s, 6 - 3 * slot],
            partner(6 - 2 * slot), z)

    def sum_slot(p):
        return jnp.where(p == 0, 3, jnp.where(p == 1, 2 - ck, jnp.where(p == 2, 1 + ck, 0)))

    def sum_start(s, left, partial, prepare=None, ready=None, during=()):
        if prepare is not None:
            prepare(chip(sum_slot(0)))
        if ready is not None:
            ready()

        def body(p, carry):
            slot = sum_slot(p)
            at = [rows(partner(2 * slot + 1), block), rows(partner(2 * slot), block)]
            both = partial(jnp.concatenate([left[i] for i in at], 0))
            rs_sa[s % 2, slot] = both[:block].astype(bf16)
            sum_pair_copy(s, slot).start()
            rs_kept[lax.rem(p, 2)] = both[block:]

            @pl.when(p > 0)
            def _():
                before = sum_slot(p - 1)
                sum_pair_copy(s, before).wait_recv()
                rs_sb[s % 2, before] = (
                    rs_kept[lax.rem(p + 1, 2)] + rs_ra[s % 2, before].astype(f32)).astype(bf16)

            @pl.when(p == 1)
            def _():
                sum_half_copy(s, 1).start()
                sum_half_copy(s, 2).start()

            @pl.when(p > 1)
            def _():
                before = sum_slot(p - 1)
                half = block // 2
                at = pl.ds(pl.multiple_of((before - 1) * half, half), half)
                sum_half_copy(s, before).wait_recv()
                rs_sb[s % 2, before, at] = (
                    rs_sb[s % 2, before, at].astype(f32) + rs_rb[s % 2, 3, at].astype(f32)).astype(bf16)
                sum_chip_copy(s, before).start()

            if prepare is not None:
                @pl.when(p < 3)
                def _():
                    prepare(chip(sum_slot(p + 1)))

            for k, poll in enumerate(during):
                pl.when(p == k)(poll)
            return carry

        lax.fori_loop(0, 4, body, 0)
        for slot in range(4):
            in_plane.append((lambda slot=slot: sum_pair_copy(s, slot), None))
        for slot in (1, 2):
            in_plane.append((lambda slot=slot: sum_half_copy(s, slot), None))
            in_plane.append((lambda slot=slot: sum_chip_copy(s, slot), None))
        sum_pair_copy(s, 0).wait_recv()
        rs_acc[s % 2] = rs_kept[1] + rs_ra[s % 2, 0].astype(f32)

    def sum_finish(s):
        total = rs_acc[s % 2]
        for slot in (1, 2):
            sum_chip_copy(s, slot).wait_recv()
            total = total + rs_rb[s % 2, slot].astype(f32)
        return total

    per = block // planes

    at_edge = jnp.logical_or(z == 0, z == planes - 1)
    edge_targets = [jnp.where(z == 0, planes - 1 - k, k) for k in range(planes - 1)]

    def weight_grad(m, parts):
        def body(i, carry):
            at = 0
            for left, right in parts:
                value = right()
                grad = dot(left[rows(i, 4 * block)], value)
                for k in range(4):
                    for t in range(planes):
                        start = k * block + t * per
                        stages[m][t, 4 * i + k, :, at:at + value.shape[1]] = grad[start:start + per].astype(bf16)
                at += value.shape[1]
            return carry

        lax.fori_loop(0, n // 4, body, 0)
        for t in edge_targets:
            launch(along, lambda t=t: grad_copy(m, t), at_edge)

    def grad_copy(m, t):
        way = jnp.where(z < t, 1, -1)
        last = z + way == t
        slot = jnp.where(jnp.logical_and(last, way < 0), planes, t)
        return remote(
            stages[m].at[t], lands[m].at[slot], zr_send.at[m, t], zr_recv.at[m, slot], c, z + way)

    def grad_arrive(m, slot):
        part = lands[m].at[slot]
        remote(part, part, zr_send.at[m, 0], zr_recv.at[m, slot], c, z).wait_recv()

    def grad_pass(m, t, valid):
        @pl.when(valid)
        def _():
            grad_arrive(m, t)

            def body(i, carry):
                stages[m][t, i] = (stages[m][t, i].astype(f32) + lands[m][t, i].astype(f32)).astype(bf16)
                return carry

            lax.fori_loop(0, n, body, 0)

        launch(along, lambda: grad_copy(m, t), valid)

    is_low, is_high = z == 1, z == planes - 2

    def grad_near_far(m):
        grad_pass(m, 3, is_low)
        grad_pass(m, 0, is_high)

    def grad_near_inner(m):
        grad_pass(m, 2, is_low)
        grad_pass(m, 1, is_high)

    def grad_near(m):
        grad_near_far(m)
        grad_near_inner(m)

    def grad_far(m):
        grad_pass(m, 3, is_high)
        grad_pass(m, 0, is_low)

    def owner_copy(m, j):
        return remote(lands[m].at[z, partner(j)], gots[m].at[c], aa_send.at[m, j], aa_recv.at[m, j], partner(j), z)

    def hand_out(m):
        pl.when(z > 0)(lambda: grad_arrive(m, z))
        pl.when(z < planes - 1)(lambda: grad_arrive(m, planes))

        def body(i, carry):
            total = stages[m][z, i].astype(f32) + lands[m][z, i].astype(f32) + lands[m][planes, i].astype(f32)
            lands[m][z, i] = total.astype(bf16)
            return carry

        lax.fori_loop(0, n, body, 0)
        for j in (2 + 2 * ck, 3 + 2 * ck, 4 - 2 * ck, 5 - 2 * ck, 6, 7, 1):
            launch(in_plane, lambda j=j: owner_copy(m, j))
        gots[m][c] = lands[m][z, c]

    def hand_receive(m):
        for j in range(1, n):
            owner_copy(m, j).wait_recv()

    weight_start(0)
    gather_start(first, 0)
    for copy in local[3:]:
        copy.wait()
    for t in range(thirds):
        pl.when(holds[t])(lambda t=t: own_down(t).wait())

    spread = jnp.broadcast_to(pos_row[...].astype(f32), (head, pos_row.shape[1]))
    positions[...] = spread.T
    side = jnp.where(lax.broadcasted_iota(jnp.int32, (1, head), 1) < head // 2, -1.0, 1.0)

    def table(i, carry):
        run = step_cos.shape[0]
        at = rows(i, run)
        start = positions[pl.ds(pl.multiple_of(i * run, run), 1)] * inverse_ref[...]
        start_cos, start_sin = jnp.cos(start), jnp.sin(start)
        cosine[at] = start_cos * step_cos[...] - start_sin * step_sin[...]
        sine[at] = (start_sin * step_cos[...] + start_cos * step_sin[...]) * side
        return carry

    def turn_over(src, dst):
        def body(i, carry):
            at = rows(i, block)
            dst[:, at] = src[at].T
            return carry

        lax.fori_loop(0, n, body, 0)

    lax.fori_loop(0, 2 * n, table, 0)
    weight_hop(0, 1)
    gather_finish(first, 0)
    weight_hop(0, 2)
    weight_start(1)
    gather_start(dy_all, 1)
    turn_over(first, first_t)
    weight_hop(0, 3)
    weight_start(2)
    weight_start(3)

    def turn(value, at):
        return value * cosine[at] + pltpu.roll(value, head // 2, 1) * sine[at]

    def turn_back(grad, at):
        return grad * cosine[at] - pltpu.roll(grad, head // 2, 1) * sine[at]

    def project(i, carry):
        at = rows(i, 2 * block)
        result = dot(first[at], w_qkv[...])
        raw[at] = result[:, :qw + kw]
        low_values = result[:, qw + kw:].astype(bf16)
        values[at] = low_values
        values_t[:, at] = low_values.T
        for h in range(group + 1):
            part = result[:, h * head:(h + 1) * head]
            inv = lax.rsqrt(jnp.mean(part * part, -1, keepdims=True) + epsilon)
            gain = qg_ref[...] if h < group else kg_ref[...]
            turned = turn(part * inv * gain, at)
            if h < group:
                queries[at, h * head:(h + 1) * head] = (turned * (scale * log2e)).astype(bf16)
            else:
                low_keys = turned.astype(bf16)
                keys[at] = low_keys
                keys_t[:, at] = low_keys.T
        return carry

    lax.fori_loop(0, n // 4, project, 0)
    weight_hop(1, 1)
    lax.fori_loop(n // 4, n // 2, project, 0)
    weight_hop(1, 2)
    gather_finish(dy_all, 1)

    def stack(ref, at):
        return jnp.concatenate([ref[at, h * head:(h + 1) * head] for h in range(group)], 0)

    def attend(place):
        at = rows(place, 2 * block)
        scores = dot_nt(keys[...], stack(queries, at))
        allowed = positions[...] <= pos_row[:, rows(2 * place, block)].astype(f32)
        later = positions[...] <= pos_row[:, rows(2 * place + 1, block)].astype(f32)
        weight = jnp.concatenate(
            [jnp.exp2(jnp.where(later if k % 2 else allowed, scores[:, k * block:(k + 1) * block], masked_score))
             for k in range(2 * group)], 1)
        inv = 1.0 / jnp.sum(weight, 0, keepdims=True)
        low_weight = weight.astype(bf16)
        probs[place] = low_weight
        sums[place] = inv
        result = dot(values_t[...], low_weight) * inv
        mixed_t[place] = result
        for h in range(group):
            mixed_low[at, h * head:(h + 1) * head] = result[:, 2 * h * block:2 * (h + 1) * block].T.astype(bf16)

    def output_ready():
        weight_hop(1, 3)
        weight_start(4)
        weight_start(5)
        hand_arrive(1)
        drain(in_plane)

    def hop_third(t, d):
        weight_hop(2 + 2 * t, d)
        weight_hop(3 + 2 * t, d)

    sum_start(
        0, mixed_low, lambda left: dot(left, w_out[...]), attend, output_ready,
        (lambda: None, lambda: hop_third(0, 2)))
    weight_start(6)
    weight_start(7)
    turn_over(dy_all, dy_t)
    hop_third(0, 1)
    hop_third(0, 3)
    mid = x_ref[...].astype(f32) + sum_finish(0)
    middle[...] = mid
    mid_scale = lax.rsqrt(jnp.mean(mid * mid, -1, keepdims=True) + epsilon)
    second[rows(c, block)] = (mid * mid_scale * fg_ref[...]).astype(bf16)
    gather_start(second, 2)
    hop_third(1, 2)

    def feed(t, at):
        units, pair = slice(t * pw, (t + 1) * pw), 2 * pw * t
        both = dot(second[at], w_gu[:, pair:pair + 2 * pw])
        back = dot_nt(dy_all[at], w_down[units])
        gate, up = both[:, :pw], both[:, pw:]
        sig = 1.0 / (1.0 + jnp.exp(-gate))
        silu = gate * sig
        hidden[at, units] = (silu * up).astype(bf16)
        d_gu[at, pair:pair + pw] = (back * up * sig * (1.0 + gate * (1.0 - sig))).astype(bf16)
        d_gu[at, pair + pw:pair + 2 * pw] = (back * silu).astype(bf16)

    def feed_arriving(slot, carry):
        gather_step(second, 2, slot)
        at = rows(chip(slot), 2 * block)
        feed(0, at)
        second_t[:, at] = second[at].T
        return carry

    def third_grad(t):
        weight_grad(t, [
            (second_t, lambda: d_gu[:, 2 * pw * t:2 * pw * (t + 1)]),
            (dy_t, lambda: hidden[:, t * pw:(t + 1) * pw]),
        ])

    def feed_third(t):
        def body(i, carry):
            feed(t, rows(i, 2 * block))
            return carry

        lax.fori_loop(0, n // 2, body, 0)

    lax.fori_loop(0, n // 2, feed_arriving, 0)
    gather_sent(second, 2)
    hop_third(1, 1)
    hop_third(1, 3)
    third_grad(0)
    hop_third(2, 2)
    feed_third(1)
    hop_third(2, 1)
    hop_third(2, 3)
    sum_start(
        1, d_gu, lambda left: dot_nt(left, w_gu[...]),
        lambda place: feed(thirds - 1, rows(place, 2 * block)))
    third_grad(1)
    third_grad(2)
    d_second = sum_finish(1)

    def norm_back(value, gain, grad):
        inv = lax.rsqrt(jnp.mean(value * value, -1, keepdims=True) + epsilon)
        weighted = grad * gain
        inner = jnp.mean(weighted * value, -1, keepdims=True)
        result = inv * weighted - value * (inv * inv * inv * inner)
        return result, jnp.sum(grad * value * inv, 0, keepdims=True)

    gain_own[...] = jnp.zeros_like(gain_own)
    part, gain_own[1:2, :] = norm_back(middle[...], fg_ref[...], d_second)
    d_mid = dy_ref[...].astype(f32) + part
    d_middle[...] = d_mid
    drain(in_plane)
    dmid[rows(c, block)] = d_mid.astype(bf16)
    gather_start(dmid, 3)
    sum_start(2, hidden, lambda left: dot(left, w_down[...]))
    drain(weight_sends)
    grad_near(0)

    dk_acc[...] = jnp.zeros_like(dk_acc)
    dv_acc[...] = jnp.zeros_like(dv_acc)

    def attend_back(slot, q_sum):
        gather_step(dmid, 3, slot)
        place = chip(slot)
        at = rows(place, 2 * block)
        d_mix = dot_nt(w_out[...], dmid[at])
        dmid_t[:, at] = dmid[at].T
        pl.when(slot == 3)(lambda: weight_grad(3, [(dmid_t, lambda: mixed_low[...])]))
        d_mix_t = jnp.concatenate([d_mix[h * head:(h + 1) * head] for h in range(group)], 1)
        d_mix_t = (d_mix_t.astype(bf16).astype(f32) * sums[place]).astype(bf16)
        delta = jnp.sum(d_mix_t.astype(f32) * mixed_t[place], 0, keepdims=True)
        weight = probs[place]
        d_prob = dot(values[...], d_mix_t)
        d_score = (weight.astype(f32) * (d_prob - delta)).astype(bf16)
        d_query = dot(keys_t[...], d_score) * scale
        for h in range(group):
            grad = turn_back(d_query[:, 2 * h * block:2 * (h + 1) * block].T, at)
            part, gain_part = norm_back(raw[at, h * head:(h + 1) * head], qg_ref[...], grad)
            d_qkv[at, h * head:(h + 1) * head] = part.astype(bf16)
            q_sum = q_sum + gain_part
        pl.when(slot == 2)(lambda: grad_near(1))
        dv_acc[...] += dot(weight, d_mix_t.T)
        dk_acc[...] += dot(d_score, stack(queries, at))
        return q_sum

    zero = jnp.zeros((1, head), f32)
    gain_own[2:3, 0:head] = lax.fori_loop(0, n // 2, attend_back, zero)
    gather_sent(dmid, 3)
    weight_grad(4, [(first_t, lambda: d_qkv[:, :qw])])
    grad_far(0)

    def project_back(i, k_sum):
        at = rows(i, 2 * block)
        grad = turn_back(dk_acc[at] * (1.0 / log2e), at)
        part, gain_part = norm_back(raw[at, qw:qw + kw], kg_ref[...], grad)
        d_qkv[at, qw:qw + kw] = part.astype(bf16)
        d_qkv[at, qw + kw:] = dv_acc[at].astype(bf16)
        return k_sum + gain_part

    gain_own[3:4, 0:head] = lax.fori_loop(0, n // 2, project_back, zero)

    weight_grad(5, [(first_t, lambda: d_qkv[:, qw:])])
    grad_far(1)
    grad_near(2)
    hand_out(0)
    drain(in_plane)
    sum_start(3, d_qkv, lambda left: dot_nt(left, w_qkv[...]))
    grad_far(2)
    grad_near(3)
    hand_out(1)
    grad_far(3)
    grad_near(4)
    out_ref[...] = (middle[...] + sum_finish(2)).astype(bf16)
    grad_far(4)
    grad_near_far(5)
    hand_out(2)
    grad_near_inner(5)
    grad_far(5)
    x_part, gain_own[0:1, :] = norm_back(x_ref[...].astype(f32), ag_ref[...], sum_finish(3))
    dx_ref[...] = d_middle[...] + x_part

    def gain_plane_copy(j):
        return remote(gain_own, gain_plane.at[c], gp_send.at[j], gp_recv.at[j], partner(j), z)

    def gain_copy(d):
        return remote(gain_all.at[z], gain_all.at[z], gz_send.at[d], gz_recv.at[d], c, lax.rem(z + d, planes))

    for j in range(1, n):
        launch(in_plane, lambda j=j: gain_plane_copy(j))
    gain_plane[c] = gain_own[...]
    hand_out(3)
    for j in range(1, n):
        gain_plane_copy(j).wait_recv()
    total = gain_plane[0]
    for i in range(1, n):
        total = total + gain_plane[i]
    gain_all[z] = total
    for d in range(1, planes):
        launch(along, lambda d=d: gain_copy(d))
    hand_out(4)
    for d in range(1, planes):
        origin = gain_all.at[lax.rem(z + planes - d, planes)]
        remote(origin, origin, gz_send.at[d], gz_recv.at[d], c, z).wait_recv()
    total = gain_all[0]
    for i in range(1, planes):
        total = total + gain_all[i]
    gains_ref[...] = total

    for m in range(4):
        hand_receive(m)
    hand_out(5)
    drain(along)
    hand_receive(4)
    hand_receive(5)
    drain(in_plane)


def finish_kernel(
    n, head, out_in, dx_in, gains_in, got_a, got_b, got_c, got_out, got_q, got_kv,
    out_ref, dx_ref, ag_ref, q_ref, k_ref, v_ref, qg_ref, kg_ref, o_ref, fg_ref, g_ref, u_ref, d_ref,
):
    out_ref[...] = out_in[...]
    dx_ref[...] = dx_in[...]
    ag_ref[...] = gains_in[0:1, :]
    fg_ref[...] = gains_in[1:2, :]
    qg_ref[...] = gains_in[2:3, 0:head]
    kg_ref[...] = gains_in[3:4, 0:head]
    qw, kw = q_ref.shape[1] // n, k_ref.shape[1] // n
    pw = got_a.shape[2] // 3
    thirds = (got_a, got_b, got_c)
    for i in range(n):
        q_ref[:, i * qw:(i + 1) * qw] = got_q[i].astype(f32)
        k_ref[:, i * kw:(i + 1) * kw] = got_kv[i, :, 0:kw].astype(f32)
        v_ref[:, i * kw:(i + 1) * kw] = got_kv[i, :, kw:].astype(f32)
        o_ref[:, i * qw:(i + 1) * qw] = got_out[i].astype(f32)
        for t, got in enumerate(thirds):
            plane, unit = hidden_block(i, t)
            at = plane * (g_ref.shape[1] // 4) + unit * pw
            g_ref[:, at:at + pw] = got[i, :, 0:pw].astype(f32)
            u_ref[:, at:at + pw] = got[i, :, pw:2 * pw].astype(f32)
            d_ref[:, at:at + pw] = got[i, :, 2 * pw:].astype(f32)


def plane_device(
    layer_input,
    token_positions,
    attention_gain,
    query_weight,
    key_matrix,
    value_matrix,
    query_gain,
    key_norm_gain,
    output_weight,
    feedforward_gain,
    gate_weight,
    up_weight,
    down_weight,
    out_cotangent,
):
    n = lax.axis_size("ctx")
    planes = lax.axis_size("fsdp")
    block, width = layer_input.shape[1:]
    length = token_positions.shape[1]
    head = query_gain.shape[0]
    qw = query_weight.shape[1] // n
    kw = key_matrix.shape[1] // n
    fw = gate_weight.shape[1] // n
    group = qw // head
    per = block // planes
    half = head // 2
    inverse = np.power(rope_base, -np.arange(half) * 2.0 / head).astype(np.float32)
    inverse = np.concatenate([inverse, inverse])[None]
    steps = np.arange(block // 2)[:, None] * inverse.astype(np.float64)
    step_cos, step_sin = (jnp.asarray(f(steps).astype(np.float32)) for f in (np.cos, np.sin))
    inverse = jnp.asarray(inverse)
    vmem = pl.BlockSpec(memory_space=pltpu.VMEM)
    hbm = pl.BlockSpec(memory_space=pl.ANY)
    dma = pltpu.SemaphoreType.DMA
    sizes = (fw, fw, fw, qw, qw, 2 * kw)
    low = lambda *shape: pltpu.VMEM(shape, bf16)
    wide = lambda *shape: pltpu.VMEM(shape, f32)
    scratch = [
        low(width, qw + 2 * kw), low(width, 2 * fw), low(qw, width), low(fw, width),
        low(planes * (output_weight.shape[0] // n), width),
        low(length, width), low(length, width), low(length, width),
        low(width, length), low(width, length), low(width, length),
        wide(length, head), wide(length, head), wide(length, head),
        wide(length, qw + kw), low(length, qw), low(length, kw), low(length, kw),
        low(kw, length), low(kw, length), low(n // 2, length, 2 * group * block), wide(n // 2, 1, 2 * group * block),
        wide(n // 2, head, 2 * group * block), low(length, qw),
        low(length, fw), low(length, 2 * fw), low(length, qw + 2 * kw),
        wide(length, kw), wide(length, kw),
    ]
    scratch += [low(planes, n, per, size) for size in sizes]
    scratch += [low(planes + 1, n, per, size) for size in sizes]
    scratch += [low(2, 4, block, width) for _ in range(4)] + [wide(2, block, width), wide(2, block, width)]
    scratch += [
        wide(block, width), wide(block, width), wide(8, width), wide(n, 8, width), wide(planes, 8, width),
        dma((13,)), dma((8, 6)), dma((8, planes)), dma((1, 7)), dma((1, 4)),
        dma((4, n)), dma((4, n)), dma((4, 4)), dma((4, 4)), dma((4, 4)), dma((4, 4)),
        dma((6, planes)), dma((6, planes + 1)), dma((6, n)), dma((6, n)), dma((n,)), dma((n,)),
        dma((planes,)), dma((planes,)),
    ]
    shapes = [
        jax.ShapeDtypeStruct((block, width), bf16),
        jax.ShapeDtypeStruct((block, width), f32),
        jax.ShapeDtypeStruct((8, width), f32),
    ] + [jax.ShapeDtypeStruct((n, per, size), bf16) for size in sizes]
    results = pl.pallas_call(
        functools.partial(layer_kernel, n, planes, block, head, group, fw),
        out_shape=shapes,
        in_specs=[vmem] * 10 + [hbm] * 7,
        out_specs=[vmem] * len(shapes),
        scratch_shapes=scratch,
        compiler_params=pltpu.CompilerParams(
            collective_id=0, has_side_effects=True, vmem_limit_bytes=60 * 1024 * 1024),
    )(
        layer_input[0], out_cotangent[0], token_positions, inverse, step_cos, step_sin,
        attention_gain[None], feedforward_gain[None], query_gain[None], key_norm_gain[None],
        query_weight, key_matrix, value_matrix, output_weight, gate_weight, up_weight, down_weight,
    )
    plain = lambda rows, columns, kind=f32: jax.ShapeDtypeStruct((rows, columns), kind)
    finals = [
        plain(block, width, bf16), plain(block, width), plain(1, width),
        plain(per, n * qw), plain(per, n * kw), plain(per, n * kw), plain(1, head), plain(1, head),
        plain(per, n * qw), plain(1, width), plain(per, n * fw), plain(per, n * fw), plain(per, n * fw),
    ]
    done = pl.pallas_call(
        functools.partial(finish_kernel, n, head),
        out_shape=finals,
        in_specs=[vmem] * len(shapes),
        out_specs=[vmem] * len(finals),
    )(*results)
    out, dx, ag, q, k, v, qg, kg, o, fg, g, u, d = done
    return out[None], dx[None], ag[0], q, k, v, qg[0], kg[0], o.T, fg[0], g, u, d.T


def solution(mesh):
    in_specs = (
        P("fsdp", "ctx", None),
        P("fsdp", None),
        P(),
        P("fsdp", None),
        P("fsdp", None),
        P("fsdp", None),
        P(),
        P(),
        P("fsdp", None),
        P(),
        P("fsdp", None),
        P("fsdp", None),
        P("fsdp", None),
        P("fsdp", "ctx", None),
    )
    out_specs = (
        P("fsdp", "ctx", None),
        P("fsdp", "ctx", None),
        P(),
        P(("ctx", "fsdp"), None),
        P(("ctx", "fsdp"), None),
        P(("ctx", "fsdp"), None),
        P(),
        P(),
        P(None, ("ctx", "fsdp")),
        P(),
        P(("ctx", "fsdp"), None),
        P(("ctx", "fsdp"), None),
        P(None, ("ctx", "fsdp")),
    )

    def run(*arguments):
        n, planes = mesh.shape["ctx"], mesh.shape["fsdp"]
        key_heads = arguments[4].shape[1] // arguments[6].shape[0]
        whole_heads = n == 8 and planes == 4 and key_heads == n
        return jax.shard_map(
            plane_device if whole_heads else on_device,
            mesh=mesh, in_specs=in_specs, out_specs=out_specs, check_vma=False,
        )(*arguments)

    return run
```

```python
import functools

import jax
import jax.numpy as jnp
import numpy as np
from jax import lax
from jax.experimental import pallas as pl
from jax.experimental.pallas import tpu as pltpu
from jax.sharding import PartitionSpec as P

epsilon = 1e-06
rope_base = 1000000.0
masked_score = -1e30


def from_behind(block, axis, distance):
    devices = range(lax.axis_size(axis))
    route = [((i - distance) % len(devices), i) for i in devices]
    return lax.ppermute(block, axis, route)


def rotate(value_rows):
    half = value_rows.shape[-1] // 2
    return jnp.concatenate([-value_rows[..., half:], value_rows[..., :half]], -1)


def rotate_back(value_rows):
    half = value_rows.shape[-1] // 2
    return jnp.concatenate([value_rows[..., half:], -value_rows[..., :half]], -1)


def rope_tables(token_offsets, head_size):
    half = head_size // 2
    inverse = rope_base ** (-(jnp.arange(half).astype(jnp.float32) * 2.0) / head_size)
    angles = token_offsets.astype(jnp.float32)[:, None] * inverse[None, :]
    cosine = jnp.cos(angles)
    sine = jnp.sin(angles)
    return (jnp.concatenate([cosine, cosine], -1), jnp.concatenate([sine, sine], -1))


def norm_scale(value_rows):
    return lax.rsqrt(jnp.mean(value_rows * value_rows, -1, keepdims=True) + epsilon)


def norm_back(value_rows, scale, gain, grad):
    weighted = grad * gain
    inner = jnp.mean(weighted * value_rows, -1, keepdims=True)
    result = scale * weighted - value_rows * scale * scale * scale * inner
    gain_part = jnp.sum((grad * value_rows * scale).reshape(-1, gain.shape[0]), 0)
    return (result, gain_part)


def row_products(left, pieces):
    return tuple((jnp.dot(left, piece, preferred_element_type=jnp.float32) for piece in pieces))


def column_products(rights, pieces):
    total = jnp.einsum("tc,rc->tr", rights[0], pieces[0], preferred_element_type=jnp.float32)
    for right, piece in zip(rights[1:], pieces[1:]):
        total = total + jnp.einsum("tc,rc->tr", right, piece, preferred_element_type=jnp.float32)
    return total


def on_device(
    layer_input,
    token_positions,
    attention_gain,
    query_weight,
    key_matrix,
    value_matrix,
    query_gain,
    key_norm_gain,
    output_weight,
    feedforward_gain,
    gate_weight,
    up_weight,
    down_weight,
    out_cotangent,
):
    hidden_in = layer_input[0].astype(jnp.float32)
    count = hidden_in.shape[0]
    head_size = query_gain.shape[0]
    query_width = query_weight.shape[1]
    key_width = key_matrix.shape[1]
    inner_width = gate_weight.shape[1]
    heads = query_width // head_size
    key_heads = key_width // head_size
    group = heads // key_heads
    scale = head_size ** (-0.5)
    cycles = lax.axis_size("ctx")
    own_index = lax.axis_index("ctx")
    sequence_pos = token_positions[0]
    token_offsets = lax.dynamic_slice_in_dim(sequence_pos, own_index * count, count)
    cosine, sine = rope_tables(token_offsets, head_size)
    cosine = cosine[:, None, :]
    sine = sine[:, None, :]
    first_scale = norm_scale(hidden_in)
    first = (hidden_in * first_scale * attention_gain).astype(jnp.bfloat16)
    query_raw, key_unnormed, value_unnormed = row_products(
        first,
        (
            lax.all_gather(query_weight, "fsdp", axis=0, tiled=True),
            lax.all_gather(key_matrix, "fsdp", axis=0, tiled=True),
            lax.all_gather(value_matrix, "fsdp", axis=0, tiled=True),
        ),
    )
    query_heads = query_raw.reshape(count, heads, head_size)
    query_scale = norm_scale(query_heads)
    query_normed = query_heads * query_scale * query_gain
    query_rot = query_normed * cosine + rotate(query_normed) * sine
    query_grouped = (
        query_rot.reshape(count, key_heads, group, head_size)
        .transpose(1, 2, 0, 3)
        .astype(jnp.bfloat16)
    )
    key_heads_raw = key_unnormed.reshape(count, key_heads, head_size)
    key_scale = norm_scale(key_heads_raw)
    key_normed = key_heads_raw * key_scale * key_norm_gain
    key_low = (
        (key_normed * cosine + rotate(key_normed) * sine)
        .reshape(count, key_width)
        .astype(jnp.bfloat16)
    )
    value_low = value_unnormed.astype(jnp.bfloat16)
    rowmax = jnp.full((key_heads, group, count), masked_score, jnp.float32)
    keys_piece = lax.all_gather(key_low, "ctx", axis=0, tiled=True).reshape(
        -1, key_heads, head_size
    )
    values_piece = lax.all_gather(value_low, "ctx", axis=0, tiled=True).reshape(
        -1, key_heads, head_size
    )
    key_pos = sequence_pos
    allowed = token_offsets[:, None] >= key_pos[None, :]
    scores = (
        jnp.einsum("kgtd,skd->kgts", query_grouped, keys_piece, preferred_element_type=jnp.float32)
        * scale
    )
    scores = jnp.where(allowed, scores, masked_score)
    newmax = jnp.maximum(rowmax, jnp.max(scores, -1))
    weights = jnp.where(allowed, jnp.exp(scores - newmax[..., None]), 0.0)
    accum = jnp.einsum(
        "kgts,skd->kgtd",
        weights.astype(jnp.bfloat16),
        values_piece,
        preferred_element_type=jnp.float32,
    )
    rowsum = jnp.sum(weights, -1)
    accum, rowmax, rowsum = (accum, newmax, rowsum)
    normalized = accum / rowsum[..., None]
    logsum = rowmax + jnp.log(rowsum)
    attention_low = (
        normalized.transpose(2, 0, 1, 3).reshape(count, query_width).astype(jnp.bfloat16)
    )
    output_whole = lax.all_gather(output_weight, "fsdp", axis=0, tiled=True)
    branch_out = jnp.dot(attention_low, output_whole, preferred_element_type=jnp.float32)
    middle = hidden_in + branch_out
    second_scale = norm_scale(middle)
    second = (middle * second_scale * feedforward_gain).astype(jnp.bfloat16)
    gate, up = row_products(
        second,
        (
            lax.all_gather(gate_weight, "fsdp", axis=0, tiled=True),
            lax.all_gather(up_weight, "fsdp", axis=0, tiled=True),
        ),
    )
    sigmoid_gate = jax.nn.sigmoid(gate)
    silu_gate = gate * sigmoid_gate
    hidden_low = (silu_gate * up).astype(jnp.bfloat16)
    (down_out,) = row_products(
        hidden_low, (lax.all_gather(down_weight, "fsdp", axis=0, tiled=True),)
    )
    layer_output = (middle + down_out).astype(jnp.bfloat16)[None]
    cotangent = out_cotangent[0]
    hidden_grad = column_products(
        (cotangent,), lax.all_gather((down_weight,), "fsdp", axis=0, tiled=True)
    )
    up_low = (hidden_grad * silu_gate).astype(jnp.bfloat16)
    gate_low = (hidden_grad * up * sigmoid_gate * (1.0 + gate * (1.0 - sigmoid_gate))).astype(
        jnp.bfloat16
    )
    second_grad = column_products(
        (gate_low, up_low), lax.all_gather((gate_weight, up_weight), "fsdp", axis=0, tiled=True)
    )
    middle_part, feedforward_part = norm_back(middle, second_scale, feedforward_gain, second_grad)
    middle_grad = cotangent.astype(jnp.float32) + middle_part
    middle_low = middle_grad.astype(jnp.bfloat16)
    attention_grad = jnp.einsum(
        "tc,rc->tr", middle_low, output_whole, preferred_element_type=jnp.float32
    )
    attention_grad_low = attention_grad.astype(jnp.bfloat16)
    mixed_grad = attention_grad_low.reshape(count, key_heads, group, head_size).transpose(
        1, 2, 0, 3
    )
    delta = jnp.sum(mixed_grad.astype(jnp.float32) * normalized, -1)

    def cycle_step(index, carry):
        keys_held, values_held, key_acc, value_acc, query_acc = carry
        anchor = (own_index - index) % cycles
        key_pos = lax.dynamic_slice_in_dim(sequence_pos, anchor * count, count)
        keys_piece = keys_held.astype(jnp.bfloat16).reshape(count, key_heads, head_size)
        values_piece = values_held.astype(jnp.bfloat16).reshape(count, key_heads, head_size)
        allowed = token_offsets[:, None] >= key_pos[None, :]
        scores = (
            jnp.einsum(
                "kgtd,skd->kgts", query_grouped, keys_piece, preferred_element_type=jnp.float32
            )
            * scale
        )
        probs = jnp.where(allowed, jnp.exp(scores - logsum[..., None]), 0.0)
        value_acc = value_acc + jnp.einsum(
            "kgts,kgtd->skd",
            probs.astype(jnp.bfloat16),
            mixed_grad,
            preferred_element_type=jnp.float32,
        ).reshape(count, key_width)
        prob_grad = jnp.einsum(
            "kgtd,skd->kgts", mixed_grad, values_piece, preferred_element_type=jnp.float32
        )
        score_grad = (probs * (prob_grad - delta[..., None])).astype(jnp.bfloat16)
        query_acc = (
            query_acc
            + jnp.einsum(
                "kgts,skd->kgtd", score_grad, keys_piece, preferred_element_type=jnp.float32
            )
            * scale
        )
        key_acc = (
            key_acc
            + jnp.einsum(
                "kgts,kgtd->skd", score_grad, query_grouped, preferred_element_type=jnp.float32
            ).reshape(count, key_width)
            * scale
        )
        moved = (
            from_behind(keys_held.astype(jnp.bfloat16), "ctx", 1).astype(keys_held.dtype),
            from_behind(values_held.astype(jnp.bfloat16), "ctx", 1).astype(values_held.dtype),
            from_behind(key_acc.astype(jnp.bfloat16), "ctx", 1).astype(key_acc.dtype),
            from_behind(value_acc.astype(jnp.bfloat16), "ctx", 1).astype(value_acc.dtype),
        )
        return (moved[0], moved[1], moved[2], moved[3], query_acc)

    start_cycle = (
        key_low.astype(jnp.float32),
        value_low.astype(jnp.float32),
        jnp.zeros((count, key_width), jnp.float32),
        jnp.zeros((count, key_width), jnp.float32),
        jnp.zeros((key_heads, group, count, head_size), jnp.float32),
    )
    cycle_done = lax.fori_loop(0, cycles, cycle_step, start_cycle)
    key_acc = cycle_done[2]
    value_acc = cycle_done[3]
    query_acc = cycle_done[4]
    query_rot_grad = query_acc.transpose(2, 0, 1, 3).reshape(count, heads, head_size)
    query_normed_grad = query_rot_grad * cosine + rotate_back(query_rot_grad * sine)
    query_heads_grad, query_part = norm_back(
        query_heads, query_scale, query_gain, query_normed_grad
    )
    query_low_grad = query_heads_grad.reshape(count, query_width).astype(jnp.bfloat16)
    key_rot_grad = key_acc.reshape(count, key_heads, head_size)
    key_normed_grad = key_rot_grad * cosine + rotate_back(key_rot_grad * sine)
    key_heads_grad, key_part = norm_back(key_heads_raw, key_scale, key_norm_gain, key_normed_grad)
    key_low_grad = key_heads_grad.reshape(count, key_width).astype(jnp.bfloat16)
    value_low_grad = value_acc.astype(jnp.bfloat16)
    first_grad = column_products(
        (query_low_grad, key_low_grad, value_low_grad),
        lax.all_gather((query_weight, key_matrix, value_matrix), "fsdp", axis=0, tiled=True),
    )
    input_part, attention_part = norm_back(hidden_in, first_scale, attention_gain, first_grad)
    input_gradient = (middle_grad + input_part)[None]
    rights_first = jnp.concatenate([query_low_grad, key_low_grad, value_low_grad], 1)
    rights_second = jnp.concatenate([gate_low, up_low], 1)
    pairs = (
        (first, rights_first),
        (second, rights_second),
        (middle_low, attention_low),
        (cotangent, hidden_low),
    )
    parts = []
    for left, right in pairs:
        parts.append(jnp.einsum("tr,tc->rc", left, right, preferred_element_type=jnp.float32))
    sums = lax.psum_scatter(
        jnp.concatenate(parts, 1), ("ctx", "fsdp"), scatter_dimension=0, tiled=True
    )
    edges = [0, query_width, query_width + key_width, query_width + 2 * key_width]
    edges = edges + [edges[3] + inner_width, edges[3] + 2 * inner_width]
    edges = edges + [edges[5] + query_width, edges[5] + query_width + inner_width]
    query_gradient = sums[:, edges[0] : edges[1]]
    key_gradient = sums[:, edges[1] : edges[2]]
    value_gradient = sums[:, edges[2] : edges[3]]
    gate_gradient = sums[:, edges[3] : edges[4]]
    up_gradient = sums[:, edges[4] : edges[5]]
    output_gradient = sums[:, edges[5] : edges[6]].T
    down_gradient = sums[:, edges[6] : edges[7]].T
    attention_total, query_total, key_total, feedforward_total = lax.psum(
        (attention_part, query_part, key_part, feedforward_part), ("ctx", "fsdp")
    )
    return (
        layer_output,
        input_gradient,
        attention_total,
        query_gradient,
        key_gradient,
        value_gradient,
        query_total,
        key_total,
        output_gradient,
        feedforward_total,
        gate_gradient,
        up_gradient,
        down_gradient,
    )


MESH = pl.DeviceIdType.MESH
f32 = jnp.float32
bf16 = jnp.bfloat16


def dot(left, right):
    return jnp.dot(left, right, preferred_element_type=f32)


def dot_nt(left, right):
    return lax.dot_general(left, right, (((1,), (1,)), ((), ())), preferred_element_type=f32)


def dot_tn(left, right):
    return lax.dot_general(left, right, (((0,), (0,)), ((), ())), preferred_element_type=f32)


def hidden_block(device, third):
    def plane(i, t):
        return ((3, 1, 2), (0, 2, 1), (0, 3, 2), (3, 0, 1))[i // 4 * 2 + i % 2][t]

    own = plane(device, third)
    return own, sum(plane(i, t) == own for i in range(device) for t in range(3))


def layer_kernel(
    n, planes, block, head, group, fw,
    x_ref, dy_ref, pos_row, inverse_ref, step_cos, step_sin, ag_ref, fg_ref, qg_ref, kg_ref,
    wq, wk, wv, wo, wg, wu, wd,
    out_ref, dx_ref, gains_ref, got_a, got_b, got_c, got_out, got_q, got_kv,
    w_qkv, w_gu, w_out, w_down, t_out,
    first, dy_all, second, first_t, dy_t, second_t,
    positions, cosine, sine,
    raw, queries, keys, values, keys_t, values_t, probs, sums, mixed_t, mixed_low,
    hidden, d_gu, d_qkv, dk_acc, dv_acc,
    stage_a, stage_b, stage_c, stage_out, stage_q, stage_kv,
    land_a, land_b, land_c, land_out, land_q, land_kv,
    rs_sa, rs_ra, rs_sb, rs_rb, rs_kept, rs_acc,
    middle, d_middle, gain_own, gain_plane, gain_all,
    local_sem, wz_send, wz_recv, hand_send, hand_recv,
    ag_send, ag_recv, ra_send, ra_recv, rb_send, rb_recv,
    zr_send, zr_recv, aa_send, aa_recv, gp_send, gp_recv, gz_send, gz_recv,
):
    c = lax.axis_index("ctx")
    z = lax.axis_index("fsdp")
    dmid = first
    dmid_t = second
    cy, cx, ck = lax.div(c, 4), lax.rem(lax.div(c, 2), 2), lax.rem(c, 2)
    ci = lax.rem(c, 4)
    sign = 1 - 2 * ck
    qw, kw = group * head, head
    pw = 128
    thirds = fw // pw
    width = x_ref.shape[1]
    scale = head ** (-0.5)
    log2e = 1.4426950408889634
    gots = (got_a, got_b, got_c, got_out, got_q, got_kv)
    stages = (stage_a, stage_b, stage_c, stage_out, stage_q, stage_kv)
    lands = (land_a, land_b, land_c, land_out, land_q, land_kv)

    def partner(j):
        y = lax.rem(cy + lax.div(j, 4), 2)
        x = lax.rem(cx + lax.rem(lax.div(j, 2), 2), 2)
        k = lax.rem(ck + lax.rem(j, 2), 2)
        return y * 4 + x * 2 + k

    def chip(slot):
        return lax.rem(cy + lax.div(slot, 2), 2) * 2 + lax.rem(cx + lax.rem(slot, 2), 2)

    def rows(start, size):
        return pl.ds(pl.multiple_of(start * size, size), size)

    def remote(src, dst, send, recv, ctx, plane):
        return pltpu.make_async_remote_copy(
            src_ref=src, dst_ref=dst, send_sem=send, recv_sem=recv,
            device_id={"ctx": ctx, "fsdp": plane}, device_id_type=MESH,
        )

    in_plane, along, weight_sends = [], [], []

    def launch(started, copy, when=None):
        if when is None:
            copy().start()
        else:
            pl.when(when)(lambda: copy().start())
        started.append((copy, when))

    def drain(started):
        for copy, when in started:
            if when is None:
                copy().wait_send()
            else:
                pl.when(when)(lambda copy=copy: copy().wait_send())
        started.clear()

    def pick(values):
        return sum(jnp.where(c == i, value, 0) for i, value in enumerate(values))

    unit_plane = [pick([hidden_block(i, t)[0] for i in range(n)]) for t in range(thirds)]
    unit_block = [pick([hidden_block(i, t)[1] for i in range(n)]) for t in range(thirds)]
    plane_blocks = wd.shape[0] // pw

    own_rows = wq.shape[0]
    out_rows = wo.shape[0] // n

    def own_slices():
        mine = rows(z, own_rows)
        pairs = [
            (wq.at[:, rows(c, qw)], w_qkv.at[mine, 0:qw]),
            (wk.at[:, rows(c, kw)], w_qkv.at[mine, qw:qw + kw]),
            (wv.at[:, rows(c, kw)], w_qkv.at[mine, qw + kw:qw + 2 * kw]),
            (wo.at[rows(c, out_rows)], t_out.at[rows(z, out_rows)]),
        ]
        for t in range(thirds):
            at = 2 * pw * t
            unit = unit_plane[t] * plane_blocks + unit_block[t]
            pairs.append((wg.at[:, rows(unit, pw)], w_gu.at[mine, at:at + pw]))
            pairs.append((wu.at[:, rows(unit, pw)], w_gu.at[mine, at + pw:at + 2 * pw]))
        return pairs

    local = [pltpu.make_async_copy(src, dst, local_sem.at[i]) for i, (src, dst) in enumerate(own_slices())]
    for copy in local:
        copy.start()

    def own_down(t):
        return pltpu.make_async_copy(
            wd.at[rows(unit_block[t], pw)], w_down.at[t * pw:(t + 1) * pw], local_sem.at[4 + 2 * thirds + t])

    holds = [unit_plane[t] == z for t in range(thirds)]
    for t in range(thirds):
        pl.when(holds[t])(lambda t=t: own_down(t).start())

    for land in lands:
        @pl.when(z == 0)
        def _(land=land):
            land[0] = jnp.zeros(land.shape[1:], bf16)

        @pl.when(z == planes - 1)
        def _(land=land):
            land[planes] = jnp.zeros(land.shape[1:], bf16)

    barrier = pltpu.get_barrier_semaphore()
    for j in range(1, n):
        pl.semaphore_signal(barrier, inc=1, device_id={"ctx": partner(j), "fsdp": z}, device_id_type=MESH)
    for d in range(1, planes):
        pl.semaphore_signal(
            barrier, inc=1, device_id={"ctx": c, "fsdp": lax.rem(z + d, planes)}, device_id_type=MESH)
    x = x_ref[...].astype(f32)
    x_scale = lax.rsqrt(jnp.mean(x * x, -1, keepdims=True) + epsilon)
    first[rows(c, block)] = (x * x_scale * ag_ref[...]).astype(bf16)
    dy_all[rows(c, block)] = dy_ref[...]
    for copy in local[:3]:
        copy.wait()
    pl.semaphore_wait(barrier, n + planes - 2)

    def inside(t):
        return jnp.logical_and(t >= 0, t < planes)

    weights = [
        (lambda o: w_qkv.at[rows(o, own_rows)], None),
        (lambda o: t_out.at[rows(o, out_rows)], 0),
    ]
    for t in range(thirds):
        weights.append((lambda o, t=t: w_gu.at[rows(o, own_rows), 2 * pw * t:2 * pw * (t + 1)], None))
        weights.append((lambda o, t=t: w_down.at[t * pw:(t + 1) * pw], None))

    def weight_copy(w, slot, origin, target):
        part = weights[w][0](origin)
        return remote(part, part, wz_send.at[w, slot], wz_recv.at[w, origin], c, target)

    def from_plane(w, origin):
        return origin == unit_plane[(w - 3) // 2] if w >= 3 and w % 2 else None

    def both(one, other):
        return one if other is None else jnp.logical_and(one, other)

    def hand_split(origin, valid):
        mine = 2 * origin + cy == c
        return jnp.logical_and(valid, jnp.logical_not(mine)), jnp.logical_and(valid, mine)

    def weight_start(w):
        for side in range(2):
            d = sign * (1 - 2 * side)
            launch(
                weight_sends, lambda side=side, d=d: weight_copy(w, side, z, z + d),
                both(inside(z + d), from_plane(w, z)))
        if weights[w][1] is not None:
            hand_over(w, z, 0, *hand_split(z, True))

    def hand_target(h):
        return lambda i: w_out.at[rows(i, out_rows)]

    def hand_copy(w, origin, slot):
        h = weights[w][1]
        return remote(
            weights[w][0](origin), hand_target(h)(ci), hand_send.at[h, slot], hand_recv.at[h, ci], 2 * origin + cy, z)

    def hand_over(w, origin, slot, away, here):
        launch(in_plane, lambda: hand_copy(w, origin, slot), away)

        @pl.when(here)
        def _():
            hand_target(weights[w][1])(ci)[...] = weights[w][0](origin)[...]

    def hand_arrive(w):
        h = weights[w][1]
        for i in range(4):
            @pl.when(4 * ck + i != c)
            def _(i=i):
                part = hand_target(h)(i)
                remote(part, part, hand_send.at[h, 0], hand_recv.at[h, i], c, z).wait_recv()

    hops = {}
    for w in range(len(weights)):
        for d in range(1, planes):
            for side, way in enumerate((1, -1)):
                origin = z - way * d
                valid = both(inside(origin), from_plane(w, origin))
                passed = jnp.logical_and(valid, inside(z + way))
                split = None if weights[w][1] is None else hand_split(origin, valid)
                hops[w, d, side] = origin, z + way, valid, passed, split

    def weight_hop(w, d):
        for side in range(2):
            origin, following, valid, passed, split = hops[w, d, side]
            pl.when(valid)(lambda: weight_copy(w, 0, origin, z).wait_recv())
            if d < planes - 1:
                launch(
                    weight_sends,
                    lambda side=side, origin=origin, following=following: weight_copy(
                        w, 2 * d + side, origin, following),
                    passed)
            if split is not None:
                hand_over(w, origin, 2 * d - 1 + side, *split)

    def gather_copy(buf, g, j, send, origin, target):
        part = buf.at[rows(origin, block)]
        return remote(part, part, ag_send.at[g, send], ag_recv.at[g, j], target, z)

    def gather_start(buf, g):
        for j in (1, 2 + 2 * ck, 4 - 2 * ck):
            launch(in_plane, lambda j=j: gather_copy(buf, g, j, j, c, partner(j)))

    def gather_half(buf, g, j):
        half = block // 2
        part = buf.at[pl.ds(pl.multiple_of(partner(j) * block + (half if j == 2 else 0), half), half)]
        at = 0 if j == 2 else 6
        return remote(part, part, ag_send.at[g, at], ag_recv.at[g, at], partner(6 - j), z)

    def gather_diagonal(buf, g):
        half = block // 2
        for at in (6, 0):
            part = buf.at[pl.ds(pl.multiple_of(partner(6) * block + (0 if at == 6 else half), half), half)]
            remote(part, part, ag_send.at[g, at], ag_recv.at[g, at], c, z).wait_recv()

    def gather_forward(buf, g, j):
        return gather_copy(buf, g, j + 1, j + 1, partner(j), partner(1))

    def gather_take(buf, g, j):
        if j == 6:
            gather_diagonal(buf, g)
        else:
            gather_copy(buf, g, j, j, partner(j), c).wait_recv()
            gather_half(buf, g, j).start()
        gather_forward(buf, g, j).start()

    def gather_sent(buf, g):
        for j in (2, 4, 6):
            in_plane.append((lambda j=j: gather_forward(buf, g, j), None))
            if j < 6:
                in_plane.append((lambda j=j: gather_half(buf, g, j), None))

    def gather_finish(buf, g):
        for j in (2, 4, 6):
            gather_take(buf, g, j)
        gather_sent(buf, g)
        for j in (1, 3, 5, 7):
            gather_copy(buf, g, j, j, partner(j), c).wait_recv()

    def gather_step(buf, g, slot):
        @pl.when(slot == 1)
        def _():
            gather_take(buf, g, 2)
            gather_take(buf, g, 4)

        pl.when(slot == 3)(lambda: gather_take(buf, g, 6))
        gather_copy(buf, g, 2 * slot + 1, 0, partner(2 * slot + 1), c).wait_recv()

    def sum_pair_copy(s, slot):
        return remote(rs_sa.at[s % 2, slot], rs_ra.at[s % 2, slot], ra_send.at[s, slot], ra_recv.at[s, slot], partner(1), z)

    def sum_chip_copy(s, slot):
        return remote(
            rs_sb.at[s % 2, slot], rs_rb.at[s % 2, slot], rb_send.at[s, slot], rb_recv.at[s, slot], partner(2 * slot), z)

    def sum_half_copy(s, slot):
        half = block // 2
        at = pl.ds(pl.multiple_of((slot - 1) * half, half), half)
        return remote(
            rs_sb.at[s % 2, 3, at], rs_rb.at[s % 2, 3, at], rb_send.at[s, 6 - 3 * slot], rb_recv.at[s, 6 - 3 * slot],
            partner(6 - 2 * slot), z)

    def sum_slot(p):
        return jnp.where(p == 0, 3, jnp.where(p == 1, 2 - ck, jnp.where(p == 2, 1 + ck, 0)))

    def sum_start(s, left, partial, prepare=None, ready=None, during=()):
        if prepare is not None:
            prepare(chip(sum_slot(0)))
        if ready is not None:
            ready()

        def body(p, carry):
            slot = sum_slot(p)
            at = [rows(partner(2 * slot + 1), block), rows(partner(2 * slot), block)]
            both = partial(jnp.concatenate([left[i] for i in at], 0))
            rs_sa[s % 2, slot] = both[:block].astype(bf16)
            sum_pair_copy(s, slot).start()
            rs_kept[lax.rem(p, 2)] = both[block:]

            @pl.when(p > 0)
            def _():
                before = sum_slot(p - 1)
                sum_pair_copy(s, before).wait_recv()
                rs_sb[s % 2, before] = (
                    rs_kept[lax.rem(p + 1, 2)] + rs_ra[s % 2, before].astype(f32)).astype(bf16)

            @pl.when(p == 1)
            def _():
                sum_half_copy(s, 1).start()
                sum_half_copy(s, 2).start()

            @pl.when(p > 1)
            def _():
                before = sum_slot(p - 1)
                half = block // 2
                at = pl.ds(pl.multiple_of((before - 1) * half, half), half)
                sum_half_copy(s, before).wait_recv()
                rs_sb[s % 2, before, at] = (
                    rs_sb[s % 2, before, at].astype(f32) + rs_rb[s % 2, 3, at].astype(f32)).astype(bf16)
                sum_chip_copy(s, before).start()

            if prepare is not None:
                @pl.when(p < 3)
                def _():
                    prepare(chip(sum_slot(p + 1)))

            for k, poll in enumerate(during):
                pl.when(p == k)(poll)
            return carry

        lax.fori_loop(0, 4, body, 0)
        for slot in range(4):
            in_plane.append((lambda slot=slot: sum_pair_copy(s, slot), None))
        for slot in (1, 2):
            in_plane.append((lambda slot=slot: sum_half_copy(s, slot), None))
            in_plane.append((lambda slot=slot: sum_chip_copy(s, slot), None))
        sum_pair_copy(s, 0).wait_recv()
        rs_acc[s % 2] = rs_kept[1] + rs_ra[s % 2, 0].astype(f32)

    def sum_finish(s):
        total = rs_acc[s % 2]
        for slot in (1, 2):
            sum_chip_copy(s, slot).wait_recv()
            total = total + rs_rb[s % 2, slot].astype(f32)
        return total

    per = block // planes

    at_edge = jnp.logical_or(z == 0, z == planes - 1)
    edge_targets = [jnp.where(z == 0, planes - 1 - k, k) for k in range(planes - 1)]

    def weight_grad(m, parts):
        def body(i, carry):
            at = 0
            for left, right in parts:
                value = right()
                grad = dot(left[rows(i, 4 * block)], value)
                for k in range(4):
                    for t in range(planes):
                        start = k * block + t * per
                        stages[m][t, 4 * i + k, :, at:at + value.shape[1]] = grad[start:start + per].astype(bf16)
                at += value.shape[1]
            return carry

        lax.fori_loop(0, n // 4, body, 0)
        for t in edge_targets:
            launch(along, lambda t=t: grad_copy(m, t), at_edge)

    def grad_copy(m, t):
        way = jnp.where(z < t, 1, -1)
        last = z + way == t
        slot = jnp.where(jnp.logical_and(last, way < 0), planes, t)
        return remote(
            stages[m].at[t], lands[m].at[slot], zr_send.at[m, t], zr_recv.at[m, slot], c, z + way)

    def grad_arrive(m, slot):
        part = lands[m].at[slot]
        remote(part, part, zr_send.at[m, 0], zr_recv.at[m, slot], c, z).wait_recv()

    def grad_pass(m, t, valid):
        @pl.when(valid)
        def _():
            grad_arrive(m, t)

            def body(i, carry):
                stages[m][t, i] = (stages[m][t, i].astype(f32) + lands[m][t, i].astype(f32)).astype(bf16)
                return carry

            lax.fori_loop(0, n, body, 0)

        launch(along, lambda: grad_copy(m, t), valid)

    is_low, is_high = z == 1, z == planes - 2

    def grad_near_far(m):
        grad_pass(m, 3, is_low)
        grad_pass(m, 0, is_high)

    def grad_near_inner(m):
        grad_pass(m, 2, is_low)
        grad_pass(m, 1, is_high)

    def grad_near(m):
        grad_near_far(m)
        grad_near_inner(m)

    def grad_far(m):
        grad_pass(m, 3, is_high)
        grad_pass(m, 0, is_low)

    def owner_copy(m, j):
        return remote(lands[m].at[z, partner(j)], gots[m].at[c], aa_send.at[m, j], aa_recv.at[m, j], partner(j), z)

    def hand_out(m):
        pl.when(z > 0)(lambda: grad_arrive(m, z))
        pl.when(z < planes - 1)(lambda: grad_arrive(m, planes))

        def body(i, carry):
            total = stages[m][z, i].astype(f32) + lands[m][z, i].astype(f32) + lands[m][planes, i].astype(f32)
            lands[m][z, i] = total.astype(bf16)
            return carry

        lax.fori_loop(0, n, body, 0)
        for j in (2 + 2 * ck, 3 + 2 * ck, 4 - 2 * ck, 5 - 2 * ck, 6, 7, 1):
            launch(in_plane, lambda j=j: owner_copy(m, j))
        gots[m][c] = lands[m][z, c]

    def hand_receive(m):
        for j in range(1, n):
            owner_copy(m, j).wait_recv()

    weight_start(0)
    gather_start(first, 0)
    for copy in local[3:]:
        copy.wait()
    for t in range(thirds):
        pl.when(holds[t])(lambda t=t: own_down(t).wait())

    spread = jnp.broadcast_to(pos_row[...].astype(f32), (head, pos_row.shape[1]))
    positions[...] = spread.T
    side = jnp.where(lax.broadcasted_iota(jnp.int32, (1, head), 1) < head // 2, -1.0, 1.0)

    def table(i, carry):
        run = step_cos.shape[0]
        at = rows(i, run)
        start = positions[pl.ds(pl.multiple_of(i * run, run), 1)] * inverse_ref[...]
        start_cos, start_sin = jnp.cos(start), jnp.sin(start)
        cosine[at] = start_cos * step_cos[...] - start_sin * step_sin[...]
        sine[at] = (start_sin * step_cos[...] + start_cos * step_sin[...]) * side
        return carry

    def turn_over(src, dst):
        def body(i, carry):
            at = rows(i, block)
            dst[:, at] = src[at].T
            return carry

        lax.fori_loop(0, n, body, 0)

    lax.fori_loop(0, 2 * n, table, 0)
    weight_hop(0, 1)
    gather_finish(first, 0)
    weight_hop(0, 2)
    weight_start(1)
    gather_start(dy_all, 1)
    turn_over(first, first_t)
    weight_hop(0, 3)
    weight_start(2)
    weight_start(3)

    def turn(value, at):
        return value * cosine[at] + pltpu.roll(value, head // 2, 1) * sine[at]

    def turn_back(grad, at):
        return grad * cosine[at] - pltpu.roll(grad, head // 2, 1) * sine[at]

    def project(i, carry):
        at = rows(i, 2 * block)
        result = dot(first[at], w_qkv[...])
        raw[at] = result[:, :qw + kw]
        low_values = result[:, qw + kw:].astype(bf16)
        values[at] = low_values
        values_t[:, at] = low_values.T
        for h in range(group + 1):
            part = result[:, h * head:(h + 1) * head]
            inv = lax.rsqrt(jnp.mean(part * part, -1, keepdims=True) + epsilon)
            gain = qg_ref[...] if h < group else kg_ref[...]
            turned = turn(part * inv * gain, at)
            if h < group:
                queries[at, h * head:(h + 1) * head] = (turned * (scale * log2e)).astype(bf16)
            else:
                low_keys = turned.astype(bf16)
                keys[at] = low_keys
                keys_t[:, at] = low_keys.T
        return carry

    lax.fori_loop(0, n // 4, project, 0)
    weight_hop(1, 1)
    lax.fori_loop(n // 4, n // 2, project, 0)
    weight_hop(1, 2)
    gather_finish(dy_all, 1)

    def stack(ref, at):
        return jnp.concatenate([ref[at, h * head:(h + 1) * head] for h in range(group)], 0)

    def attend(place):
        at = rows(place, 2 * block)
        scores = dot_nt(keys[...], stack(queries, at))
        allowed = positions[...] <= pos_row[:, rows(2 * place, block)].astype(f32)
        later = positions[...] <= pos_row[:, rows(2 * place + 1, block)].astype(f32)
        weight = jnp.concatenate(
            [jnp.exp2(jnp.where(later if k % 2 else allowed, scores[:, k * block:(k + 1) * block], masked_score))
             for k in range(2 * group)], 1)
        inv = 1.0 / jnp.sum(weight, 0, keepdims=True)
        low_weight = weight.astype(bf16)
        probs[place] = low_weight
        sums[place] = inv
        result = dot(values_t[...], low_weight) * inv
        mixed_t[place] = result
        for h in range(group):
            mixed_low[at, h * head:(h + 1) * head] = result[:, 2 * h * block:2 * (h + 1) * block].T.astype(bf16)

    def output_ready():
        weight_hop(1, 3)
        weight_start(4)
        weight_start(5)
        hand_arrive(1)
        drain(in_plane)

    def hop_third(t, d):
        weight_hop(2 + 2 * t, d)
        weight_hop(3 + 2 * t, d)

    sum_start(
        0, mixed_low, lambda left: dot(left, w_out[...]), attend, output_ready,
        (lambda: hop_third(0, 1), lambda: hop_third(0, 2), lambda: hop_third(1, 1)))
    weight_start(6)
    weight_start(7)
    hop_third(0, 3)
    turn_over(dy_all, dy_t)
    hop_third(1, 2)
    mid = x_ref[...].astype(f32) + sum_finish(0)
    middle[...] = mid
    mid_scale = lax.rsqrt(jnp.mean(mid * mid, -1, keepdims=True) + epsilon)
    second[rows(c, block)] = (mid * mid_scale * fg_ref[...]).astype(bf16)
    gather_start(second, 2)
    hop_third(2, 1)

    def feed(t, at):
        units, pair = slice(t * pw, (t + 1) * pw), 2 * pw * t
        both = dot(second[at], w_gu[:, pair:pair + 2 * pw])
        back = dot_nt(dy_all[at], w_down[units])
        gate, up = both[:, :pw], both[:, pw:]
        sig = 1.0 / (1.0 + jnp.exp(-gate))
        silu = gate * sig
        hidden[at, units] = (silu * up).astype(bf16)
        d_gu[at, pair:pair + pw] = (back * up * sig * (1.0 + gate * (1.0 - sig))).astype(bf16)
        d_gu[at, pair + pw:pair + 2 * pw] = (back * silu).astype(bf16)

    def feed_arriving(slot, carry):
        gather_step(second, 2, slot)
        at = rows(chip(slot), 2 * block)
        feed(0, at)
        second_t[:, at] = second[at].T
        pl.when(slot == 2)(lambda: hop_third(2, 2))
        return carry

    def third_grad(t):
        weight_grad(t, [
            (second_t, lambda: d_gu[:, 2 * pw * t:2 * pw * (t + 1)]),
            (dy_t, lambda: hidden[:, t * pw:(t + 1) * pw]),
        ])

    def feed_third(t):
        def body(i, carry):
            feed(t, rows(i, 2 * block))
            return carry

        lax.fori_loop(0, n // 2, body, 0)

    lax.fori_loop(0, n // 2, feed_arriving, 0)
    gather_sent(second, 2)
    hop_third(1, 3)
    third_grad(0)
    feed_third(1)
    third_grad(1)
    hop_third(2, 3)
    sum_start(
        1, d_gu, lambda left: dot_nt(left, w_gu[...]),
        lambda place: feed(thirds - 1, rows(place, 2 * block)))
    third_grad(2)
    d_second = sum_finish(1)

    def norm_back(value, gain, grad):
        inv = lax.rsqrt(jnp.mean(value * value, -1, keepdims=True) + epsilon)
        weighted = grad * gain
        inner = jnp.mean(weighted * value, -1, keepdims=True)
        result = inv * weighted - value * (inv * inv * inv * inner)
        return result, jnp.sum(grad * value * inv, 0, keepdims=True)

    gain_own[...] = jnp.zeros_like(gain_own)
    part, gain_own[1:2, :] = norm_back(middle[...], fg_ref[...], d_second)
    d_mid = dy_ref[...].astype(f32) + part
    d_middle[...] = d_mid
    drain(in_plane)
    dmid[rows(c, block)] = d_mid.astype(bf16)
    gather_start(dmid, 3)
    sum_start(2, hidden, lambda left: dot(left, w_down[...]))
    drain(weight_sends)
    grad_near(0)

    dk_acc[...] = jnp.zeros_like(dk_acc)
    dv_acc[...] = jnp.zeros_like(dv_acc)

    def attend_back(slot, q_sum):
        gather_step(dmid, 3, slot)
        place = chip(slot)
        at = rows(place, 2 * block)
        d_mix = dot_nt(w_out[...], dmid[at])
        dmid_t[:, at] = dmid[at].T
        pl.when(slot == 3)(lambda: weight_grad(3, [(dmid_t, lambda: mixed_low[...])]))
        d_mix_t = jnp.concatenate([d_mix[h * head:(h + 1) * head] for h in range(group)], 1)
        d_mix_t = (d_mix_t.astype(bf16).astype(f32) * sums[place]).astype(bf16)
        delta = jnp.sum(d_mix_t.astype(f32) * mixed_t[place], 0, keepdims=True)
        weight = probs[place]
        d_prob = dot(values[...], d_mix_t)
        d_score = (weight.astype(f32) * (d_prob - delta)).astype(bf16)
        d_query = dot(keys_t[...], d_score) * scale
        for h in range(group):
            grad = turn_back(d_query[:, 2 * h * block:2 * (h + 1) * block].T, at)
            part, gain_part = norm_back(raw[at, h * head:(h + 1) * head], qg_ref[...], grad)
            d_qkv[at, h * head:(h + 1) * head] = part.astype(bf16)
            q_sum = q_sum + gain_part
        pl.when(slot == 2)(lambda: grad_near(1))
        dv_acc[...] += dot(weight, d_mix_t.T)
        dk_acc[...] += dot(d_score, stack(queries, at))
        return q_sum

    zero = jnp.zeros((1, head), f32)
    gain_own[2:3, 0:head] = lax.fori_loop(0, n // 2, attend_back, zero)
    gather_sent(dmid, 3)
    weight_grad(4, [(first_t, lambda: d_qkv[:, :qw])])
    grad_far(0)

    def project_back(i, k_sum):
        at = rows(i, 2 * block)
        grad = turn_back(dk_acc[at] * (1.0 / log2e), at)
        part, gain_part = norm_back(raw[at, qw:qw + kw], kg_ref[...], grad)
        d_qkv[at, qw:qw + kw] = part.astype(bf16)
        d_qkv[at, qw + kw:] = dv_acc[at].astype(bf16)
        return k_sum + gain_part

    gain_own[3:4, 0:head] = lax.fori_loop(0, n // 2, project_back, zero)

    weight_grad(5, [(first_t, lambda: d_qkv[:, qw:])])
    grad_far(1)
    grad_near(2)
    hand_out(0)
    drain(in_plane)
    sum_start(3, d_qkv, lambda left: dot_nt(left, w_qkv[...]))
    grad_far(2)
    grad_near(3)
    hand_out(1)
    grad_far(3)
    grad_near(4)
    out_ref[...] = (middle[...] + sum_finish(2)).astype(bf16)
    grad_far(4)
    grad_near_far(5)
    hand_out(2)
    grad_near_inner(5)
    grad_far(5)
    x_part, gain_own[0:1, :] = norm_back(x_ref[...].astype(f32), ag_ref[...], sum_finish(3))
    dx_ref[...] = d_middle[...] + x_part

    def gain_plane_copy(j):
        return remote(gain_own, gain_plane.at[c], gp_send.at[j], gp_recv.at[j], partner(j), z)

    def gain_copy(d):
        return remote(gain_all.at[z], gain_all.at[z], gz_send.at[d], gz_recv.at[d], c, lax.rem(z + d, planes))

    for j in range(1, n):
        launch(in_plane, lambda j=j: gain_plane_copy(j))
    gain_plane[c] = gain_own[...]
    hand_out(3)
    for j in range(1, n):
        gain_plane_copy(j).wait_recv()
    total = gain_plane[0]
    for i in range(1, n):
        total = total + gain_plane[i]
    gain_all[z] = total
    for d in range(1, planes):
        launch(along, lambda d=d: gain_copy(d))
    hand_out(4)
    for d in range(1, planes):
        origin = gain_all.at[lax.rem(z + planes - d, planes)]
        remote(origin, origin, gz_send.at[d], gz_recv.at[d], c, z).wait_recv()
    total = gain_all[0]
    for i in range(1, planes):
        total = total + gain_all[i]
    gains_ref[...] = total

    for m in range(4):
        hand_receive(m)
    hand_out(5)
    drain(along)
    hand_receive(4)
    hand_receive(5)
    drain(in_plane)


def finish_kernel(
    n, head, out_in, dx_in, gains_in, got_a, got_b, got_c, got_out, got_q, got_kv,
    out_ref, dx_ref, ag_ref, q_ref, k_ref, v_ref, qg_ref, kg_ref, o_ref, fg_ref, g_ref, u_ref, d_ref,
):
    out_ref[...] = out_in[...]
    dx_ref[...] = dx_in[...]
    ag_ref[...] = gains_in[0:1, :]
    fg_ref[...] = gains_in[1:2, :]
    qg_ref[...] = gains_in[2:3, 0:head]
    kg_ref[...] = gains_in[3:4, 0:head]
    qw, kw = q_ref.shape[1] // n, k_ref.shape[1] // n
    pw = got_a.shape[2] // 3
    thirds = (got_a, got_b, got_c)
    for i in range(n):
        q_ref[:, i * qw:(i + 1) * qw] = got_q[i].astype(f32)
        k_ref[:, i * kw:(i + 1) * kw] = got_kv[i, :, 0:kw].astype(f32)
        v_ref[:, i * kw:(i + 1) * kw] = got_kv[i, :, kw:].astype(f32)
        o_ref[:, i * qw:(i + 1) * qw] = got_out[i].astype(f32)
        for t, got in enumerate(thirds):
            plane, unit = hidden_block(i, t)
            at = plane * (g_ref.shape[1] // 4) + unit * pw
            g_ref[:, at:at + pw] = got[i, :, 0:pw].astype(f32)
            u_ref[:, at:at + pw] = got[i, :, pw:2 * pw].astype(f32)
            d_ref[:, at:at + pw] = got[i, :, 2 * pw:].astype(f32)


def plane_device(
    layer_input,
    token_positions,
    attention_gain,
    query_weight,
    key_matrix,
    value_matrix,
    query_gain,
    key_norm_gain,
    output_weight,
    feedforward_gain,
    gate_weight,
    up_weight,
    down_weight,
    out_cotangent,
):
    n = lax.axis_size("ctx")
    planes = lax.axis_size("fsdp")
    block, width = layer_input.shape[1:]
    length = token_positions.shape[1]
    head = query_gain.shape[0]
    qw = query_weight.shape[1] // n
    kw = key_matrix.shape[1] // n
    fw = gate_weight.shape[1] // n
    group = qw // head
    per = block // planes
    half = head // 2
    inverse = np.power(rope_base, -np.arange(half) * 2.0 / head).astype(np.float32)
    inverse = np.concatenate([inverse, inverse])[None]
    steps = np.arange(block // 2)[:, None] * inverse.astype(np.float64)
    step_cos, step_sin = (jnp.asarray(f(steps).astype(np.float32)) for f in (np.cos, np.sin))
    inverse = jnp.asarray(inverse)
    vmem = pl.BlockSpec(memory_space=pltpu.VMEM)
    hbm = pl.BlockSpec(memory_space=pl.ANY)
    dma = pltpu.SemaphoreType.DMA
    sizes = (fw, fw, fw, qw, qw, 2 * kw)
    low = lambda *shape: pltpu.VMEM(shape, bf16)
    wide = lambda *shape: pltpu.VMEM(shape, f32)
    scratch = [
        low(width, qw + 2 * kw), low(width, 2 * fw), low(qw, width), low(fw, width),
        low(planes * (output_weight.shape[0] // n), width),
        low(length, width), low(length, width), low(length, width),
        low(width, length), low(width, length), low(width, length),
        wide(length, head), wide(length, head), wide(length, head),
        wide(length, qw + kw), low(length, qw), low(length, kw), low(length, kw),
        low(kw, length), low(kw, length), low(n // 2, length, 2 * group * block), wide(n // 2, 1, 2 * group * block),
        wide(n // 2, head, 2 * group * block), low(length, qw),
        low(length, fw), low(length, 2 * fw), low(length, qw + 2 * kw),
        wide(length, kw), wide(length, kw),
    ]
    scratch += [low(planes, n, per, size) for size in sizes]
    scratch += [low(planes + 1, n, per, size) for size in sizes]
    scratch += [low(2, 4, block, width) for _ in range(4)] + [wide(2, block, width), wide(2, block, width)]
    scratch += [
        wide(block, width), wide(block, width), wide(8, width), wide(n, 8, width), wide(planes, 8, width),
        dma((13,)), dma((8, 6)), dma((8, planes)), dma((1, 7)), dma((1, 4)),
        dma((4, n)), dma((4, n)), dma((4, 4)), dma((4, 4)), dma((4, 4)), dma((4, 4)),
        dma((6, planes)), dma((6, planes + 1)), dma((6, n)), dma((6, n)), dma((n,)), dma((n,)),
        dma((planes,)), dma((planes,)),
    ]
    shapes = [
        jax.ShapeDtypeStruct((block, width), bf16),
        jax.ShapeDtypeStruct((block, width), f32),
        jax.ShapeDtypeStruct((8, width), f32),
    ] + [jax.ShapeDtypeStruct((n, per, size), bf16) for size in sizes]
    results = pl.pallas_call(
        functools.partial(layer_kernel, n, planes, block, head, group, fw),
        out_shape=shapes,
        in_specs=[vmem] * 10 + [hbm] * 7,
        out_specs=[vmem] * len(shapes),
        scratch_shapes=scratch,
        compiler_params=pltpu.CompilerParams(
            collective_id=0, has_side_effects=True, vmem_limit_bytes=60 * 1024 * 1024),
    )(
        layer_input[0], out_cotangent[0], token_positions, inverse, step_cos, step_sin,
        attention_gain[None], feedforward_gain[None], query_gain[None], key_norm_gain[None],
        query_weight, key_matrix, value_matrix, output_weight, gate_weight, up_weight, down_weight,
    )
    plain = lambda rows, columns, kind=f32: jax.ShapeDtypeStruct((rows, columns), kind)
    finals = [
        plain(block, width, bf16), plain(block, width), plain(1, width),
        plain(per, n * qw), plain(per, n * kw), plain(per, n * kw), plain(1, head), plain(1, head),
        plain(per, n * qw), plain(1, width), plain(per, n * fw), plain(per, n * fw), plain(per, n * fw),
    ]
    done = pl.pallas_call(
        functools.partial(finish_kernel, n, head),
        out_shape=finals,
        in_specs=[vmem] * len(shapes),
        out_specs=[vmem] * len(finals),
    )(*results)
    out, dx, ag, q, k, v, qg, kg, o, fg, g, u, d = done
    return out[None], dx[None], ag[0], q, k, v, qg[0], kg[0], o.T, fg[0], g, u, d.T


def solution(mesh):
    in_specs = (
        P("fsdp", "ctx", None),
        P("fsdp", None),
        P(),
        P("fsdp", None),
        P("fsdp", None),
        P("fsdp", None),
        P(),
        P(),
        P("fsdp", None),
        P(),
        P("fsdp", None),
        P("fsdp", None),
        P("fsdp", None),
        P("fsdp", "ctx", None),
    )
    out_specs = (
        P("fsdp", "ctx", None),
        P("fsdp", "ctx", None),
        P(),
        P(("ctx", "fsdp"), None),
        P(("ctx", "fsdp"), None),
        P(("ctx", "fsdp"), None),
        P(),
        P(),
        P(None, ("ctx", "fsdp")),
        P(),
        P(("ctx", "fsdp"), None),
        P(("ctx", "fsdp"), None),
        P(None, ("ctx", "fsdp")),
    )

    def run(*arguments):
        n, planes = mesh.shape["ctx"], mesh.shape["fsdp"]
        key_heads = arguments[4].shape[1] // arguments[6].shape[0]
        whole_heads = n == 8 and planes == 4 and key_heads == n
        return jax.shard_map(
            plane_device if whole_heads else on_device,
            mesh=mesh, in_specs=in_specs, out_specs=out_specs, check_vma=False,
        )(*arguments)

    return run
```

```python
import functools

import jax
import jax.numpy as jnp
import numpy as np
from jax import lax
from jax.experimental import pallas as pl
from jax.experimental.pallas import tpu as pltpu
from jax.sharding import PartitionSpec as P

epsilon = 1e-06
rope_base = 1000000.0
masked_score = -1e30


def from_behind(block, axis, distance):
    devices = range(lax.axis_size(axis))
    route = [((i - distance) % len(devices), i) for i in devices]
    return lax.ppermute(block, axis, route)


def rotate(value_rows):
    half = value_rows.shape[-1] // 2
    return jnp.concatenate([-value_rows[..., half:], value_rows[..., :half]], -1)


def rotate_back(value_rows):
    half = value_rows.shape[-1] // 2
    return jnp.concatenate([value_rows[..., half:], -value_rows[..., :half]], -1)


def rope_tables(token_offsets, head_size):
    half = head_size // 2
    inverse = rope_base ** (-(jnp.arange(half).astype(jnp.float32) * 2.0) / head_size)
    angles = token_offsets.astype(jnp.float32)[:, None] * inverse[None, :]
    cosine = jnp.cos(angles)
    sine = jnp.sin(angles)
    return (jnp.concatenate([cosine, cosine], -1), jnp.concatenate([sine, sine], -1))


def norm_scale(value_rows):
    return lax.rsqrt(jnp.mean(value_rows * value_rows, -1, keepdims=True) + epsilon)


def norm_back(value_rows, scale, gain, grad):
    weighted = grad * gain
    inner = jnp.mean(weighted * value_rows, -1, keepdims=True)
    result = scale * weighted - value_rows * scale * scale * scale * inner
    gain_part = jnp.sum((grad * value_rows * scale).reshape(-1, gain.shape[0]), 0)
    return (result, gain_part)


def row_products(left, pieces):
    return tuple((jnp.dot(left, piece, preferred_element_type=jnp.float32) for piece in pieces))


def column_products(rights, pieces):
    total = jnp.einsum("tc,rc->tr", rights[0], pieces[0], preferred_element_type=jnp.float32)
    for right, piece in zip(rights[1:], pieces[1:]):
        total = total + jnp.einsum("tc,rc->tr", right, piece, preferred_element_type=jnp.float32)
    return total


def on_device(
    layer_input,
    token_positions,
    attention_gain,
    query_weight,
    key_matrix,
    value_matrix,
    query_gain,
    key_norm_gain,
    output_weight,
    feedforward_gain,
    gate_weight,
    up_weight,
    down_weight,
    out_cotangent,
):
    hidden_in = layer_input[0].astype(jnp.float32)
    count = hidden_in.shape[0]
    head_size = query_gain.shape[0]
    query_width = query_weight.shape[1]
    key_width = key_matrix.shape[1]
    inner_width = gate_weight.shape[1]
    heads = query_width // head_size
    key_heads = key_width // head_size
    group = heads // key_heads
    scale = head_size ** (-0.5)
    cycles = lax.axis_size("ctx")
    own_index = lax.axis_index("ctx")
    sequence_pos = token_positions[0]
    token_offsets = lax.dynamic_slice_in_dim(sequence_pos, own_index * count, count)
    cosine, sine = rope_tables(token_offsets, head_size)
    cosine = cosine[:, None, :]
    sine = sine[:, None, :]
    first_scale = norm_scale(hidden_in)
    first = (hidden_in * first_scale * attention_gain).astype(jnp.bfloat16)
    query_raw, key_unnormed, value_unnormed = row_products(
        first,
        (
            lax.all_gather(query_weight, "fsdp", axis=0, tiled=True),
            lax.all_gather(key_matrix, "fsdp", axis=0, tiled=True),
            lax.all_gather(value_matrix, "fsdp", axis=0, tiled=True),
        ),
    )
    query_heads = query_raw.reshape(count, heads, head_size)
    query_scale = norm_scale(query_heads)
    query_normed = query_heads * query_scale * query_gain
    query_rot = query_normed * cosine + rotate(query_normed) * sine
    query_grouped = (
        query_rot.reshape(count, key_heads, group, head_size)
        .transpose(1, 2, 0, 3)
        .astype(jnp.bfloat16)
    )
    key_heads_raw = key_unnormed.reshape(count, key_heads, head_size)
    key_scale = norm_scale(key_heads_raw)
    key_normed = key_heads_raw * key_scale * key_norm_gain
    key_low = (
        (key_normed * cosine + rotate(key_normed) * sine)
        .reshape(count, key_width)
        .astype(jnp.bfloat16)
    )
    value_low = value_unnormed.astype(jnp.bfloat16)
    rowmax = jnp.full((key_heads, group, count), masked_score, jnp.float32)
    keys_piece = lax.all_gather(key_low, "ctx", axis=0, tiled=True).reshape(
        -1, key_heads, head_size
    )
    values_piece = lax.all_gather(value_low, "ctx", axis=0, tiled=True).reshape(
        -1, key_heads, head_size
    )
    key_pos = sequence_pos
    allowed = token_offsets[:, None] >= key_pos[None, :]
    scores = (
        jnp.einsum("kgtd,skd->kgts", query_grouped, keys_piece, preferred_element_type=jnp.float32)
        * scale
    )
    scores = jnp.where(allowed, scores, masked_score)
    newmax = jnp.maximum(rowmax, jnp.max(scores, -1))
    weights = jnp.where(allowed, jnp.exp(scores - newmax[..., None]), 0.0)
    accum = jnp.einsum(
        "kgts,skd->kgtd",
        weights.astype(jnp.bfloat16),
        values_piece,
        preferred_element_type=jnp.float32,
    )
    rowsum = jnp.sum(weights, -1)
    accum, rowmax, rowsum = (accum, newmax, rowsum)
    normalized = accum / rowsum[..., None]
    logsum = rowmax + jnp.log(rowsum)
    attention_low = (
        normalized.transpose(2, 0, 1, 3).reshape(count, query_width).astype(jnp.bfloat16)
    )
    output_whole = lax.all_gather(output_weight, "fsdp", axis=0, tiled=True)
    branch_out = jnp.dot(attention_low, output_whole, preferred_element_type=jnp.float32)
    middle = hidden_in + branch_out
    second_scale = norm_scale(middle)
    second = (middle * second_scale * feedforward_gain).astype(jnp.bfloat16)
    gate, up = row_products(
        second,
        (
            lax.all_gather(gate_weight, "fsdp", axis=0, tiled=True),
            lax.all_gather(up_weight, "fsdp", axis=0, tiled=True),
        ),
    )
    sigmoid_gate = jax.nn.sigmoid(gate)
    silu_gate = gate * sigmoid_gate
    hidden_low = (silu_gate * up).astype(jnp.bfloat16)
    (down_out,) = row_products(
        hidden_low, (lax.all_gather(down_weight, "fsdp", axis=0, tiled=True),)
    )
    layer_output = (middle + down_out).astype(jnp.bfloat16)[None]
    cotangent = out_cotangent[0]
    hidden_grad = column_products(
        (cotangent,), lax.all_gather((down_weight,), "fsdp", axis=0, tiled=True)
    )
    up_low = (hidden_grad * silu_gate).astype(jnp.bfloat16)
    gate_low = (hidden_grad * up * sigmoid_gate * (1.0 + gate * (1.0 - sigmoid_gate))).astype(
        jnp.bfloat16
    )
    second_grad = column_products(
        (gate_low, up_low), lax.all_gather((gate_weight, up_weight), "fsdp", axis=0, tiled=True)
    )
    middle_part, feedforward_part = norm_back(middle, second_scale, feedforward_gain, second_grad)
    middle_grad = cotangent.astype(jnp.float32) + middle_part
    middle_low = middle_grad.astype(jnp.bfloat16)
    attention_grad = jnp.einsum(
        "tc,rc->tr", middle_low, output_whole, preferred_element_type=jnp.float32
    )
    attention_grad_low = attention_grad.astype(jnp.bfloat16)
    mixed_grad = attention_grad_low.reshape(count, key_heads, group, head_size).transpose(
        1, 2, 0, 3
    )
    delta = jnp.sum(mixed_grad.astype(jnp.float32) * normalized, -1)

    def cycle_step(index, carry):
        keys_held, values_held, key_acc, value_acc, query_acc = carry
        anchor = (own_index - index) % cycles
        key_pos = lax.dynamic_slice_in_dim(sequence_pos, anchor * count, count)
        keys_piece = keys_held.astype(jnp.bfloat16).reshape(count, key_heads, head_size)
        values_piece = values_held.astype(jnp.bfloat16).reshape(count, key_heads, head_size)
        allowed = token_offsets[:, None] >= key_pos[None, :]
        scores = (
            jnp.einsum(
                "kgtd,skd->kgts", query_grouped, keys_piece, preferred_element_type=jnp.float32
            )
            * scale
        )
        probs = jnp.where(allowed, jnp.exp(scores - logsum[..., None]), 0.0)
        value_acc = value_acc + jnp.einsum(
            "kgts,kgtd->skd",
            probs.astype(jnp.bfloat16),
            mixed_grad,
            preferred_element_type=jnp.float32,
        ).reshape(count, key_width)
        prob_grad = jnp.einsum(
            "kgtd,skd->kgts", mixed_grad, values_piece, preferred_element_type=jnp.float32
        )
        score_grad = (probs * (prob_grad - delta[..., None])).astype(jnp.bfloat16)
        query_acc = (
            query_acc
            + jnp.einsum(
                "kgts,skd->kgtd", score_grad, keys_piece, preferred_element_type=jnp.float32
            )
            * scale
        )
        key_acc = (
            key_acc
            + jnp.einsum(
                "kgts,kgtd->skd", score_grad, query_grouped, preferred_element_type=jnp.float32
            ).reshape(count, key_width)
            * scale
        )
        moved = (
            from_behind(keys_held.astype(jnp.bfloat16), "ctx", 1).astype(keys_held.dtype),
            from_behind(values_held.astype(jnp.bfloat16), "ctx", 1).astype(values_held.dtype),
            from_behind(key_acc.astype(jnp.bfloat16), "ctx", 1).astype(key_acc.dtype),
            from_behind(value_acc.astype(jnp.bfloat16), "ctx", 1).astype(value_acc.dtype),
        )
        return (moved[0], moved[1], moved[2], moved[3], query_acc)

    start_cycle = (
        key_low.astype(jnp.float32),
        value_low.astype(jnp.float32),
        jnp.zeros((count, key_width), jnp.float32),
        jnp.zeros((count, key_width), jnp.float32),
        jnp.zeros((key_heads, group, count, head_size), jnp.float32),
    )
    cycle_done = lax.fori_loop(0, cycles, cycle_step, start_cycle)
    key_acc = cycle_done[2]
    value_acc = cycle_done[3]
    query_acc = cycle_done[4]
    query_rot_grad = query_acc.transpose(2, 0, 1, 3).reshape(count, heads, head_size)
    query_normed_grad = query_rot_grad * cosine + rotate_back(query_rot_grad * sine)
    query_heads_grad, query_part = norm_back(
        query_heads, query_scale, query_gain, query_normed_grad
    )
    query_low_grad = query_heads_grad.reshape(count, query_width).astype(jnp.bfloat16)
    key_rot_grad = key_acc.reshape(count, key_heads, head_size)
    key_normed_grad = key_rot_grad * cosine + rotate_back(key_rot_grad * sine)
    key_heads_grad, key_part = norm_back(key_heads_raw, key_scale, key_norm_gain, key_normed_grad)
    key_low_grad = key_heads_grad.reshape(count, key_width).astype(jnp.bfloat16)
    value_low_grad = value_acc.astype(jnp.bfloat16)
    first_grad = column_products(
        (query_low_grad, key_low_grad, value_low_grad),
        lax.all_gather((query_weight, key_matrix, value_matrix), "fsdp", axis=0, tiled=True),
    )
    input_part, attention_part = norm_back(hidden_in, first_scale, attention_gain, first_grad)
    input_gradient = (middle_grad + input_part)[None]
    rights_first = jnp.concatenate([query_low_grad, key_low_grad, value_low_grad], 1)
    rights_second = jnp.concatenate([gate_low, up_low], 1)
    pairs = (
        (first, rights_first),
        (second, rights_second),
        (middle_low, attention_low),
        (cotangent, hidden_low),
    )
    parts = []
    for left, right in pairs:
        parts.append(jnp.einsum("tr,tc->rc", left, right, preferred_element_type=jnp.float32))
    sums = lax.psum_scatter(
        jnp.concatenate(parts, 1), ("ctx", "fsdp"), scatter_dimension=0, tiled=True
    )
    edges = [0, query_width, query_width + key_width, query_width + 2 * key_width]
    edges = edges + [edges[3] + inner_width, edges[3] + 2 * inner_width]
    edges = edges + [edges[5] + query_width, edges[5] + query_width + inner_width]
    query_gradient = sums[:, edges[0] : edges[1]]
    key_gradient = sums[:, edges[1] : edges[2]]
    value_gradient = sums[:, edges[2] : edges[3]]
    gate_gradient = sums[:, edges[3] : edges[4]]
    up_gradient = sums[:, edges[4] : edges[5]]
    output_gradient = sums[:, edges[5] : edges[6]].T
    down_gradient = sums[:, edges[6] : edges[7]].T
    attention_total, query_total, key_total, feedforward_total = lax.psum(
        (attention_part, query_part, key_part, feedforward_part), ("ctx", "fsdp")
    )
    return (
        layer_output,
        input_gradient,
        attention_total,
        query_gradient,
        key_gradient,
        value_gradient,
        query_total,
        key_total,
        output_gradient,
        feedforward_total,
        gate_gradient,
        up_gradient,
        down_gradient,
    )


MESH = pl.DeviceIdType.MESH
f32 = jnp.float32
bf16 = jnp.bfloat16


def dot(left, right):
    return jnp.dot(left, right, preferred_element_type=f32)


def dot_nt(left, right):
    return lax.dot_general(left, right, (((1,), (1,)), ((), ())), preferred_element_type=f32)


def dot_tn(left, right):
    return lax.dot_general(left, right, (((0,), (0,)), ((), ())), preferred_element_type=f32)


def hidden_block(device, third):
    def plane(i, t):
        return ((3, 1, 2), (0, 2, 1), (0, 3, 2), (3, 0, 1))[i // 4 * 2 + i % 2][t]

    own = plane(device, third)
    return own, sum(plane(i, t) == own for i in range(device) for t in range(3))


def layer_kernel(
    n, planes, block, head, group, fw,
    x_ref, dy_ref, pos_row, inverse_ref, step_cos, step_sin, ag_ref, fg_ref, qg_ref, kg_ref,
    wq, wk, wv, wo, wg, wu, wd,
    out_ref, dx_ref, gains_ref, got_ab, got_co, got_qkv,
    w_qkv, w_gu, w_out, w_down, t_out,
    first, dy_all, second, first_t, dy_t, second_t,
    positions, cosine, sine,
    raw, queries, keys, values, keys_t, values_t, probs, sums, mixed_t, mixed_low, mixed_low_t,
    hidden, d_gu, d_qkv, dk_acc, dv_acc,
    stage_a, stage_b, stage_c, stage_out, stage_q, stage_kv,
    land_a, land_b, land_c, land_out, land_q, land_kv,
    own_ab, own_co, own_qkv,
    rs_sa, rs_ra, rs_sb, rs_rb, rs_kept, rs_acc,
    middle, d_middle, gain_own, gain_plane, gain_all,
    local_sem, wz_send, wz_recv, hand_send, hand_recv,
    ag_send, ag_recv, ra_send, ra_recv, rb_send, rb_recv,
    zr_send, zr_recv, aa_send, aa_recv, gp_send, gp_recv, gz_send, gz_recv,
):
    c = lax.axis_index("ctx")
    z = lax.axis_index("fsdp")
    dmid = first
    cy, cx, ck = lax.div(c, 4), lax.rem(lax.div(c, 2), 2), lax.rem(c, 2)
    ci = lax.rem(c, 4)
    sign = 1 - 2 * ck
    qw, kw = group * head, head
    pw = 128
    thirds = fw // pw
    width = x_ref.shape[1]
    scale = head ** (-0.5)
    log2e = 1.4426950408889634
    gots = (got_ab, got_co, got_qkv)
    owns = (own_ab, own_co, own_qkv)
    stages = (stage_a, stage_b, stage_c, stage_out, stage_q, stage_kv)
    lands = (land_a, land_b, land_c, land_out, land_q, land_kv)

    def partner(j):
        y = lax.rem(cy + lax.div(j, 4), 2)
        x = lax.rem(cx + lax.rem(lax.div(j, 2), 2), 2)
        k = lax.rem(ck + lax.rem(j, 2), 2)
        return y * 4 + x * 2 + k

    def chip(slot):
        return lax.rem(cy + lax.div(slot, 2), 2) * 2 + lax.rem(cx + lax.rem(slot, 2), 2)

    def rows(start, size):
        return pl.ds(pl.multiple_of(start * size, size), size)

    def remote(src, dst, send, recv, ctx, plane):
        return pltpu.make_async_remote_copy(
            src_ref=src, dst_ref=dst, send_sem=send, recv_sem=recv,
            device_id={"ctx": ctx, "fsdp": plane}, device_id_type=MESH,
        )

    in_plane, along, weight_sends = [], [], []

    def launch(started, copy, when=None):
        if when is None:
            copy().start()
        else:
            pl.when(when)(lambda: copy().start())
        started.append((copy, when))

    def drain(started):
        for copy, when in started:
            if when is None:
                copy().wait_send()
            else:
                pl.when(when)(lambda copy=copy: copy().wait_send())
        started.clear()

    def pick(values):
        return sum(jnp.where(c == i, value, 0) for i, value in enumerate(values))

    unit_plane = [pick([hidden_block(i, t)[0] for i in range(n)]) for t in range(thirds)]
    unit_block = [pick([hidden_block(i, t)[1] for i in range(n)]) for t in range(thirds)]
    plane_blocks = wd.shape[0] // pw

    own_rows = wq.shape[0]
    out_rows = wo.shape[0] // n

    def own_slices():
        mine = rows(z, own_rows)
        pairs = [
            (wq.at[:, rows(c, qw)], w_qkv.at[mine, 0:qw]),
            (wk.at[:, rows(c, kw)], w_qkv.at[mine, qw:qw + kw]),
            (wv.at[:, rows(c, kw)], w_qkv.at[mine, qw + kw:qw + 2 * kw]),
            (wo.at[rows(c, out_rows)], t_out.at[rows(z, out_rows)]),
        ]
        for t in range(thirds):
            at = 2 * pw * t
            unit = unit_plane[t] * plane_blocks + unit_block[t]
            pairs.append((wg.at[:, rows(unit, pw)], w_gu.at[mine, at:at + pw]))
            pairs.append((wu.at[:, rows(unit, pw)], w_gu.at[mine, at + pw:at + 2 * pw]))
        return pairs

    local = [pltpu.make_async_copy(src, dst, local_sem.at[i]) for i, (src, dst) in enumerate(own_slices())]
    for copy in local:
        copy.start()

    def own_down(t):
        return pltpu.make_async_copy(
            wd.at[rows(unit_block[t], pw)], w_down.at[t * pw:(t + 1) * pw], local_sem.at[4 + 2 * thirds + t])

    holds = [unit_plane[t] == z for t in range(thirds)]
    for t in range(thirds):
        pl.when(holds[t])(lambda t=t: own_down(t).start())

    for land in lands:
        @pl.when(z == 0)
        def _(land=land):
            land[0] = jnp.zeros(land.shape[1:], bf16)

        @pl.when(z == planes - 1)
        def _(land=land):
            land[planes] = jnp.zeros(land.shape[1:], bf16)

    barrier = pltpu.get_barrier_semaphore()
    for j in range(1, n):
        pl.semaphore_signal(barrier, inc=1, device_id={"ctx": partner(j), "fsdp": z}, device_id_type=MESH)
    for d in range(1, planes):
        pl.semaphore_signal(
            barrier, inc=1, device_id={"ctx": c, "fsdp": lax.rem(z + d, planes)}, device_id_type=MESH)
    x = x_ref[...].astype(f32)
    x_scale = lax.rsqrt(jnp.mean(x * x, -1, keepdims=True) + epsilon)
    first[rows(c, block)] = (x * x_scale * ag_ref[...]).astype(bf16)
    dy_all[rows(c, block)] = dy_ref[...]
    for copy in local[:3]:
        copy.wait()
    pl.semaphore_wait(barrier, n + planes - 2)

    def inside(t):
        return jnp.logical_and(t >= 0, t < planes)

    weights = [
        (lambda o: w_qkv.at[rows(o, own_rows)], None),
        (lambda o: t_out.at[rows(o, out_rows)], 0),
    ]
    for t in range(thirds):
        weights.append((lambda o, t=t: w_gu.at[rows(o, own_rows), 2 * pw * t:2 * pw * (t + 1)], None))
        weights.append((lambda o, t=t: w_down.at[t * pw:(t + 1) * pw], None))

    def weight_copy(w, slot, origin, target):
        part = weights[w][0](origin)
        return remote(part, part, wz_send.at[w, slot], wz_recv.at[w, origin], c, target)

    def from_plane(w, origin):
        return origin == unit_plane[(w - 3) // 2] if w >= 3 and w % 2 else None

    def both(one, other):
        return one if other is None else jnp.logical_and(one, other)

    def hand_split(origin, valid):
        mine = 2 * origin + cy == c
        return jnp.logical_and(valid, jnp.logical_not(mine)), jnp.logical_and(valid, mine)

    def weight_start(w):
        for side in range(2):
            d = sign * (1 - 2 * side)
            launch(
                weight_sends, lambda side=side, d=d: weight_copy(w, side, z, z + d),
                both(inside(z + d), from_plane(w, z)))
        if weights[w][1] is not None:
            hand_over(w, z, 0, *hand_split(z, True))

    def hand_target(h):
        return lambda i: w_out.at[rows(i, out_rows)]

    def hand_copy(w, origin, slot):
        h = weights[w][1]
        return remote(
            weights[w][0](origin), hand_target(h)(ci), hand_send.at[h, slot], hand_recv.at[h, ci], 2 * origin + cy, z)

    def hand_over(w, origin, slot, away, here):
        launch(in_plane, lambda: hand_copy(w, origin, slot), away)

        @pl.when(here)
        def _():
            hand_target(weights[w][1])(ci)[...] = weights[w][0](origin)[...]

    def hand_arrive(w):
        h = weights[w][1]
        for i in range(4):
            @pl.when(4 * ck + i != c)
            def _(i=i):
                part = hand_target(h)(i)
                remote(part, part, hand_send.at[h, 0], hand_recv.at[h, i], c, z).wait_recv()

    hops = {}
    for w in range(len(weights)):
        for d in range(1, planes):
            for side, way in enumerate((1, -1)):
                origin = z - way * d
                valid = both(inside(origin), from_plane(w, origin))
                passed = jnp.logical_and(valid, inside(z + way))
                split = None if weights[w][1] is None else hand_split(origin, valid)
                hops[w, d, side] = origin, z + way, valid, passed, split

    def weight_hop(w, d):
        for side in range(2):
            origin, following, valid, passed, split = hops[w, d, side]
            pl.when(valid)(lambda: weight_copy(w, 0, origin, z).wait_recv())
            if d < planes - 1:
                launch(
                    weight_sends,
                    lambda side=side, origin=origin, following=following: weight_copy(
                        w, 2 * d + side, origin, following),
                    passed)
            if split is not None:
                hand_over(w, origin, 2 * d - 1 + side, *split)

    def gather_copy(buf, g, j, send, origin, target):
        part = buf.at[rows(origin, block)]
        return remote(part, part, ag_send.at[g, send], ag_recv.at[g, j], target, z)

    def gather_start(buf, g):
        for j in (1, 2 + 2 * ck, 4 - 2 * ck):
            launch(in_plane, lambda j=j: gather_copy(buf, g, j, j, c, partner(j)))

    def gather_half(buf, g, j):
        half = block // 2
        part = buf.at[pl.ds(pl.multiple_of(partner(j) * block + (half if j == 2 else 0), half), half)]
        at = 0 if j == 2 else 6
        return remote(part, part, ag_send.at[g, at], ag_recv.at[g, at], partner(6 - j), z)

    def gather_diagonal(buf, g):
        half = block // 2
        for at in (6, 0):
            part = buf.at[pl.ds(pl.multiple_of(partner(6) * block + (0 if at == 6 else half), half), half)]
            remote(part, part, ag_send.at[g, at], ag_recv.at[g, at], c, z).wait_recv()

    def gather_forward(buf, g, j):
        return gather_copy(buf, g, j + 1, j + 1, partner(j), partner(1))

    def gather_take(buf, g, j):
        if j == 6:
            gather_diagonal(buf, g)
        else:
            gather_copy(buf, g, j, j, partner(j), c).wait_recv()
            gather_half(buf, g, j).start()
        gather_forward(buf, g, j).start()

    def gather_sent(buf, g):
        for j in (2, 4, 6):
            in_plane.append((lambda j=j: gather_forward(buf, g, j), None))
            if j < 6:
                in_plane.append((lambda j=j: gather_half(buf, g, j), None))

    def gather_finish(buf, g):
        for j in (2, 4, 6):
            gather_take(buf, g, j)
        gather_sent(buf, g)
        for j in (1, 3, 5, 7):
            gather_copy(buf, g, j, j, partner(j), c).wait_recv()

    def gather_step(buf, g, slot):
        @pl.when(slot == 1)
        def _():
            gather_take(buf, g, 2)
            gather_take(buf, g, 4)

        pl.when(slot == 3)(lambda: gather_take(buf, g, 6))
        gather_copy(buf, g, 2 * slot + 1, 0, partner(2 * slot + 1), c).wait_recv()

    def sum_pair_copy(s, slot):
        return remote(rs_sa.at[s % 2, slot], rs_ra.at[s % 2, slot], ra_send.at[s, slot], ra_recv.at[s, slot], partner(1), z)

    def sum_chip_copy(s, slot):
        return remote(
            rs_sb.at[s % 2, slot - 1], rs_rb.at[s % 2, slot - 1], rb_send.at[s, slot], rb_recv.at[s, slot], partner(2 * slot), z)

    def sum_half_copy(s, slot):
        half = block // 2
        at = pl.ds(pl.multiple_of((slot - 1) * half, half), half)
        return remote(
            rs_sb.at[s % 2, 2, at], rs_rb.at[s % 2, 2, at], rb_send.at[s, 6 - 3 * slot], rb_recv.at[s, 6 - 3 * slot],
            partner(6 - 2 * slot), z)

    def sum_slot(p):
        return jnp.where(p == 0, 3, jnp.where(p == 1, 2 - ck, jnp.where(p == 2, 1 + ck, 0)))

    def sum_start(s, left, partial, prepare=None, ready=None, during=()):
        if prepare is not None:
            prepare(chip(sum_slot(0)))
        if ready is not None:
            ready()

        def body(p, carry):
            slot = sum_slot(p)
            at = [rows(partner(2 * slot + 1), block), rows(partner(2 * slot), block)]
            both = partial(jnp.concatenate([left[i] for i in at], 0))
            rs_sa[s % 2, slot] = both[:block].astype(bf16)
            sum_pair_copy(s, slot).start()
            rs_kept[lax.rem(p, 2)] = both[block:]

            @pl.when(p > 0)
            def _():
                before = sum_slot(p - 1)
                sum_pair_copy(s, before).wait_recv()
                rs_sb[s % 2, before - 1] = (
                    rs_kept[lax.rem(p + 1, 2)] + rs_ra[s % 2, before].astype(f32)).astype(bf16)

            @pl.when(p == 1)
            def _():
                sum_half_copy(s, 1).start()
                sum_half_copy(s, 2).start()

            @pl.when(p > 1)
            def _():
                before = sum_slot(p - 1)
                half = block // 2
                at = pl.ds(pl.multiple_of((before - 1) * half, half), half)
                sum_half_copy(s, before).wait_recv()
                rs_sb[s % 2, before - 1, at] = (
                    rs_sb[s % 2, before - 1, at].astype(f32) + rs_rb[s % 2, 2, at].astype(f32)).astype(bf16)
                sum_chip_copy(s, before).start()

            if prepare is not None:
                @pl.when(p < 3)
                def _():
                    prepare(chip(sum_slot(p + 1)))

            for k, poll in enumerate(during):
                pl.when(p == k)(poll)
            return carry

        lax.fori_loop(0, 4, body, 0)
        for slot in range(4):
            in_plane.append((lambda slot=slot: sum_pair_copy(s, slot), None))
        for slot in (1, 2):
            in_plane.append((lambda slot=slot: sum_half_copy(s, slot), None))
            in_plane.append((lambda slot=slot: sum_chip_copy(s, slot), None))
        sum_pair_copy(s, 0).wait_recv()
        rs_acc[s % 2] = rs_kept[1] + rs_ra[s % 2, 0].astype(f32)

    def sum_finish(s):
        total = rs_acc[s % 2]
        for slot in (1, 2):
            sum_chip_copy(s, slot).wait_recv()
            total = total + rs_rb[s % 2, slot - 1].astype(f32)
        return total

    per = block // planes

    at_edge = jnp.logical_or(z == 0, z == planes - 1)
    edge_targets = [jnp.where(z == 0, planes - 1 - k, k) for k in range(planes - 1)]

    def weight_grad(m, parts):
        def body(i, carry):
            at = 0
            for left, right in parts:
                value = right()
                grad = dot(left[rows(i, 4 * block)], value)
                for k in range(4):
                    for t in range(planes):
                        start = k * block + t * per
                        stages[m][t, 4 * i + k, :, at:at + value.shape[1]] = grad[start:start + per].astype(bf16)
                at += value.shape[1]
            return carry

        lax.fori_loop(0, n // 4, body, 0)
        grad_send(m)

    def grad_send(m):
        for t in edge_targets:
            launch(along, lambda t=t: grad_copy(m, t), at_edge)

    def grad_copy(m, t):
        way = jnp.where(z < t, 1, -1)
        last = z + way == t
        slot = jnp.where(jnp.logical_and(last, way < 0), planes, t)
        return remote(
            stages[m].at[t], lands[m].at[slot], zr_send.at[m, t], zr_recv.at[m, slot], c, z + way)

    def grad_arrive(m, slot):
        part = lands[m].at[slot]
        remote(part, part, zr_send.at[m, 0], zr_recv.at[m, slot], c, z).wait_recv()

    def grad_pass(m, t, valid):
        @pl.when(valid)
        def _():
            grad_arrive(m, t)
            stages[m][t] = stages[m][t] + lands[m][t]

        launch(along, lambda: grad_copy(m, t), valid)

    is_low, is_high = z == 1, z == planes - 2

    def grad_near_far(m):
        grad_pass(m, 3, is_low)
        grad_pass(m, 0, is_high)

    def grad_near_inner(m):
        grad_pass(m, 2, is_low)
        grad_pass(m, 1, is_high)

    def grad_near(m):
        grad_near_far(m)
        grad_near_inner(m)

    def grad_far(m):
        grad_pass(m, 3, is_high)
        grad_pass(m, 0, is_low)

    def owner_copy(g, j):
        return remote(owns[g].at[partner(j)], gots[g].at[c], aa_send.at[g, j], aa_recv.at[g, j], partner(j), z)

    def own_sum(m):
        pl.when(z > 0)(lambda: grad_arrive(m, z))
        pl.when(z < planes - 1)(lambda: grad_arrive(m, planes))
        total = stages[m][z].astype(f32) + lands[m][z].astype(f32) + lands[m][planes].astype(f32)
        first_size = stages[m // 2 * 2].shape[3]
        if m % 2:
            owns[m // 2][:, :, first_size:] = total.astype(bf16)
        else:
            owns[m // 2][:, :, :first_size] = total.astype(bf16)

    def hand_out(g):
        for j in (2 + 2 * ck, 3 + 2 * ck, 4 - 2 * ck, 5 - 2 * ck, 6, 7, 1):
            launch(in_plane, lambda j=j: owner_copy(g, j))
        gots[g][c] = owns[g][c]

    def hand_receive(g):
        for j in range(1, n):
            owner_copy(g, j).wait_recv()

    weight_start(0)
    gather_start(first, 0)
    for copy in local[3:]:
        copy.wait()
    for t in range(thirds):
        pl.when(holds[t])(lambda t=t: own_down(t).wait())

    spread = jnp.broadcast_to(pos_row[...].astype(f32), (head, pos_row.shape[1]))
    positions[...] = spread.T
    side = jnp.where(lax.broadcasted_iota(jnp.int32, (1, head), 1) < head // 2, -1.0, 1.0)

    def table(i, carry):
        run = step_cos.shape[0]
        at = rows(i, run)
        start = positions[pl.ds(pl.multiple_of(i * run, run), 1)] * inverse_ref[...]
        start_cos, start_sin = jnp.cos(start), jnp.sin(start)
        cosine[at] = start_cos * step_cos[...] - start_sin * step_sin[...]
        sine[at] = (start_sin * step_cos[...] + start_cos * step_sin[...]) * side
        return carry

    def turn_over(src, dst):
        def body(i, carry):
            at = rows(i, block)
            dst[:, at] = src[at].T
            return carry

        lax.fori_loop(0, n, body, 0)

    lax.fori_loop(0, 2 * n, table, 0)
    weight_hop(0, 1)
    gather_finish(first, 0)
    weight_hop(0, 2)
    weight_start(1)
    gather_start(dy_all, 1)
    turn_over(first, first_t)
    weight_hop(0, 3)
    weight_start(2)
    weight_start(3)

    def turn(value, at):
        return value * cosine[at] + pltpu.roll(value, head // 2, 1) * sine[at]

    def turn_back(grad, at):
        return grad * cosine[at] - pltpu.roll(grad, head // 2, 1) * sine[at]

    def project(i, carry):
        at = rows(i, 2 * block)
        result = dot(first[at], w_qkv[...])
        raw[at] = result[:, :qw + kw]
        low_values = result[:, qw + kw:].astype(bf16)
        values[at] = low_values
        values_t[:, at] = low_values.T
        for h in range(group + 1):
            part = result[:, h * head:(h + 1) * head]
            inv = lax.rsqrt(jnp.mean(part * part, -1, keepdims=True) + epsilon)
            gain = qg_ref[...] if h < group else kg_ref[...]
            turned = turn(part * inv * gain, at)
            if h < group:
                queries[at, h * head:(h + 1) * head] = (turned * (scale * log2e)).astype(bf16)
            else:
                low_keys = turned.astype(bf16)
                keys[at] = low_keys
                keys_t[:, at] = low_keys.T
        return carry

    lax.fori_loop(0, n // 4, project, 0)
    weight_hop(1, 1)
    lax.fori_loop(n // 4, n // 2, project, 0)
    weight_hop(1, 2)
    gather_finish(dy_all, 1)

    def stack(ref, at):
        return jnp.concatenate([ref[at, h * head:(h + 1) * head] for h in range(group)], 0)

    def attend(place):
        at = rows(place, 2 * block)
        scores = dot_nt(keys[...], stack(queries, at))
        allowed = positions[...] <= pos_row[:, rows(2 * place, block)].astype(f32)
        later = positions[...] <= pos_row[:, rows(2 * place + 1, block)].astype(f32)
        weight = jnp.concatenate(
            [jnp.exp2(jnp.where(later if k % 2 else allowed, scores[:, k * block:(k + 1) * block], masked_score))
             for k in range(2 * group)], 1)
        inv = 1.0 / jnp.sum(weight, 0, keepdims=True)
        low_weight = weight.astype(bf16)
        probs[place] = low_weight
        sums[place] = inv
        result = dot(values_t[...], low_weight) * inv
        mixed_t[place] = result
        for h in range(group):
            low_result = result[:, 2 * h * block:2 * (h + 1) * block].astype(bf16)
            mixed_low_t[h * head:(h + 1) * head, at] = low_result
            mixed_low[at, h * head:(h + 1) * head] = low_result.T

    def output_ready():
        weight_hop(1, 3)
        weight_start(4)
        weight_start(5)
        hand_arrive(1)
        drain(in_plane)

    def hop_third(t, d):
        weight_hop(2 + 2 * t, d)
        weight_hop(3 + 2 * t, d)

    sum_start(
        0, mixed_low, lambda left: dot(left, w_out[...]), attend, output_ready,
        (lambda: hop_third(0, 1), lambda: hop_third(0, 2), lambda: hop_third(1, 1)))
    weight_start(6)
    weight_start(7)
    hop_third(0, 3)
    turn_over(dy_all, dy_t)
    hop_third(1, 2)
    mid = x_ref[...].astype(f32) + sum_finish(0)
    middle[...] = mid
    mid_scale = lax.rsqrt(jnp.mean(mid * mid, -1, keepdims=True) + epsilon)
    second[rows(c, block)] = (mid * mid_scale * fg_ref[...]).astype(bf16)
    gather_start(second, 2)
    hop_third(2, 1)

    def feed(t, at):
        units, pair = slice(t * pw, (t + 1) * pw), 2 * pw * t
        both = dot(second[at], w_gu[:, pair:pair + 2 * pw])
        back = dot_nt(dy_all[at], w_down[units])
        gate, up = both[:, :pw], both[:, pw:]
        sig = 1.0 / (1.0 + jnp.exp(-gate))
        silu = gate * sig
        hidden[at, units] = (silu * up).astype(bf16)
        d_gu[at, pair:pair + pw] = (back * up * sig * (1.0 + gate * (1.0 - sig))).astype(bf16)
        d_gu[at, pair + pw:pair + 2 * pw] = (back * silu).astype(bf16)

    def feed_arriving(slot, carry):
        gather_step(second, 2, slot)
        at = rows(chip(slot), 2 * block)
        feed(0, at)
        second_t[:, at] = second[at].T
        pl.when(slot == 2)(lambda: hop_third(2, 2))
        return carry

    def third_grad(t):
        weight_grad(t, [
            (second_t, lambda: d_gu[:, 2 * pw * t:2 * pw * (t + 1)]),
            (dy_t, lambda: hidden[:, t * pw:(t + 1) * pw]),
        ])

    def feed_third(t):
        def body(i, carry):
            feed(t, rows(i, 2 * block))
            return carry

        lax.fori_loop(0, n // 2, body, 0)

    lax.fori_loop(0, n // 2, feed_arriving, 0)
    gather_sent(second, 2)
    hop_third(1, 3)
    third_grad(0)
    feed_third(1)
    hop_third(2, 3)
    sum_start(
        1, d_gu, lambda left: dot_nt(left, w_gu[...]),
        lambda place: feed(thirds - 1, rows(place, 2 * block)))
    third_grad(1)
    third_grad(2)
    d_second = sum_finish(1)

    def norm_back(value, gain, grad):
        inv = lax.rsqrt(jnp.mean(value * value, -1, keepdims=True) + epsilon)
        weighted = grad * gain
        inner = jnp.mean(weighted * value, -1, keepdims=True)
        result = inv * weighted - value * (inv * inv * inv * inner)
        return result, jnp.sum(grad * value * inv, 0, keepdims=True)

    gain_own[...] = jnp.zeros_like(gain_own)
    part, gain_own[1:2, :] = norm_back(middle[...], fg_ref[...], d_second)
    d_mid = dy_ref[...].astype(f32) + part
    d_middle[...] = d_mid
    drain(in_plane)
    dmid[rows(c, block)] = d_mid.astype(bf16)
    gather_start(dmid, 3)
    sum_start(2, hidden, lambda left: dot(left, w_down[...]))
    drain(weight_sends)
    grad_near(0)

    dk_acc[...] = jnp.zeros_like(dk_acc)
    dv_acc[...] = jnp.zeros_like(dv_acc)

    def output_grad():
        def body(i, carry):
            grad = dot(mixed_low_t[...], dmid[:, rows(i, 2 * block)]).astype(bf16).T
            for k in range(2):
                for t in range(planes):
                    start = k * block + t * per
                    stage_out[t, 2 * i + k] = grad[start:start + per]
            return carry

        lax.fori_loop(0, n // 2, body, 0)
        grad_send(3)

    def attend_back(slot, q_sum):
        gather_step(dmid, 3, slot)
        place = chip(slot)
        at = rows(place, 2 * block)
        d_mix = dot_nt(w_out[...], dmid[at])
        pl.when(slot == 3)(output_grad)
        d_mix_t = jnp.concatenate([d_mix[h * head:(h + 1) * head] for h in range(group)], 1)
        d_mix_t = (d_mix_t.astype(bf16).astype(f32) * sums[place]).astype(bf16)
        delta = jnp.sum(d_mix_t.astype(f32) * mixed_t[place], 0, keepdims=True)
        weight = probs[place]
        d_prob = dot(values[...], d_mix_t)
        d_score = (weight.astype(f32) * (d_prob - delta)).astype(bf16)
        d_query = dot(keys_t[...], d_score) * scale
        for h in range(group):
            grad = turn_back(d_query[:, 2 * h * block:2 * (h + 1) * block].T, at)
            part, gain_part = norm_back(raw[at, h * head:(h + 1) * head], qg_ref[...], grad)
            d_qkv[at, h * head:(h + 1) * head] = part.astype(bf16)
            q_sum = q_sum + gain_part
        pl.when(slot == 2)(lambda: grad_near(1))
        dv_acc[...] += dot(weight, d_mix_t.T)
        dk_acc[...] += dot(d_score, stack(queries, at))
        return q_sum

    zero = jnp.zeros((1, head), f32)
    gain_own[2:3, 0:head] = lax.fori_loop(0, n // 2, attend_back, zero)
    gather_sent(dmid, 3)
    weight_grad(4, [(first_t, lambda: d_qkv[:, :qw])])
    grad_far(0)

    def project_back(i, k_sum):
        at = rows(i, 2 * block)
        grad = turn_back(dk_acc[at] * (1.0 / log2e), at)
        part, gain_part = norm_back(raw[at, qw:qw + kw], kg_ref[...], grad)
        d_qkv[at, qw:qw + kw] = part.astype(bf16)
        d_qkv[at, qw + kw:] = dv_acc[at].astype(bf16)
        return k_sum + gain_part

    gain_own[3:4, 0:head] = lax.fori_loop(0, n // 2, project_back, zero)

    weight_grad(5, [(first_t, lambda: d_qkv[:, qw:])])
    grad_far(1)
    grad_near(2)
    own_sum(0)
    drain(in_plane)
    sum_start(3, d_qkv, lambda left: dot_nt(left, w_qkv[...]))
    grad_far(2)
    grad_near(3)
    own_sum(1)
    hand_out(0)
    grad_far(3)
    grad_near(4)
    out_ref[...] = (middle[...] + sum_finish(2)).astype(bf16)
    grad_far(4)
    grad_near_far(5)
    own_sum(2)
    grad_near_inner(5)
    grad_far(5)
    x_part, gain_own[0:1, :] = norm_back(x_ref[...].astype(f32), ag_ref[...], sum_finish(3))
    dx_ref[...] = d_middle[...] + x_part

    def gain_plane_copy(j):
        return remote(gain_own, gain_plane.at[c], gp_send.at[j], gp_recv.at[j], partner(j), z)

    def gain_copy(d):
        return remote(gain_all.at[z], gain_all.at[z], gz_send.at[d], gz_recv.at[d], c, lax.rem(z + d, planes))

    for j in range(1, n):
        launch(in_plane, lambda j=j: gain_plane_copy(j))
    gain_plane[c] = gain_own[...]
    own_sum(3)
    hand_out(1)
    for j in range(1, n):
        gain_plane_copy(j).wait_recv()
    total = gain_plane[0]
    for i in range(1, n):
        total = total + gain_plane[i]
    gain_all[z] = total
    for d in range(1, planes):
        launch(along, lambda d=d: gain_copy(d))
    own_sum(4)
    for d in range(1, planes):
        origin = gain_all.at[lax.rem(z + planes - d, planes)]
        remote(origin, origin, gz_send.at[d], gz_recv.at[d], c, z).wait_recv()
    total = gain_all[0]
    for i in range(1, planes):
        total = total + gain_all[i]
    gains_ref[...] = total

    hand_receive(0)
    own_sum(5)
    hand_out(2)
    drain(along)
    hand_receive(1)
    hand_receive(2)
    drain(in_plane)


def finish_kernel(
    n, head, out_in, dx_in, gains_in, got_ab, got_co, got_qkv,
    out_ref, dx_ref, ag_ref, q_ref, k_ref, v_ref, qg_ref, kg_ref, o_ref, fg_ref, g_ref, u_ref, d_ref,
):
    out_ref[...] = out_in[...]
    dx_ref[...] = dx_in[...]
    ag_ref[...] = gains_in[0:1, :]
    fg_ref[...] = gains_in[1:2, :]
    qg_ref[...] = gains_in[2:3, 0:head]
    kg_ref[...] = gains_in[3:4, 0:head]
    qw, kw = q_ref.shape[1] // n, k_ref.shape[1] // n
    fw = g_ref.shape[1] // n
    pw = fw // 3
    thirds = ((got_ab, 0), (got_ab, fw), (got_co, 0))
    for i in range(n):
        q_ref[:, i * qw:(i + 1) * qw] = got_qkv[i, :, 0:qw].astype(f32)
        k_ref[:, i * kw:(i + 1) * kw] = got_qkv[i, :, qw:qw + kw].astype(f32)
        v_ref[:, i * kw:(i + 1) * kw] = got_qkv[i, :, qw + kw:].astype(f32)
        o_ref[:, i * qw:(i + 1) * qw] = got_co[i, :, fw:].astype(f32)
        for t, (got, start) in enumerate(thirds):
            plane, unit = hidden_block(i, t)
            at = plane * (g_ref.shape[1] // 4) + unit * pw
            g_ref[:, at:at + pw] = got[i, :, start:start + pw].astype(f32)
            u_ref[:, at:at + pw] = got[i, :, start + pw:start + 2 * pw].astype(f32)
            d_ref[:, at:at + pw] = got[i, :, start + 2 * pw:start + 3 * pw].astype(f32)


def plane_device(
    layer_input,
    token_positions,
    attention_gain,
    query_weight,
    key_matrix,
    value_matrix,
    query_gain,
    key_norm_gain,
    output_weight,
    feedforward_gain,
    gate_weight,
    up_weight,
    down_weight,
    out_cotangent,
):
    n = lax.axis_size("ctx")
    planes = lax.axis_size("fsdp")
    block, width = layer_input.shape[1:]
    length = token_positions.shape[1]
    head = query_gain.shape[0]
    qw = query_weight.shape[1] // n
    kw = key_matrix.shape[1] // n
    fw = gate_weight.shape[1] // n
    group = qw // head
    per = block // planes
    half = head // 2
    inverse = np.power(rope_base, -np.arange(half) * 2.0 / head).astype(np.float32)
    inverse = np.concatenate([inverse, inverse])[None]
    steps = np.arange(block // 2)[:, None] * inverse.astype(np.float64)
    step_cos, step_sin = (jnp.asarray(f(steps).astype(np.float32)) for f in (np.cos, np.sin))
    inverse = jnp.asarray(inverse)
    vmem = pl.BlockSpec(memory_space=pltpu.VMEM)
    hbm = pl.BlockSpec(memory_space=pl.ANY)
    dma = pltpu.SemaphoreType.DMA
    sizes = (fw, fw, fw, qw, qw, 2 * kw)
    low = lambda *shape: pltpu.VMEM(shape, bf16)
    wide = lambda *shape: pltpu.VMEM(shape, f32)
    scratch = [
        low(width, qw + 2 * kw), low(width, 2 * fw), low(qw, width), low(fw, width),
        low(planes * (output_weight.shape[0] // n), width),
        low(length, width), low(length, width), low(length, width),
        low(width, length), low(width, length), low(width, length),
        wide(length, head), wide(length, head), wide(length, head),
        wide(length, qw + kw), low(length, qw), low(length, kw), low(length, kw),
        low(kw, length), low(kw, length), low(n // 2, length, 2 * group * block), wide(n // 2, 1, 2 * group * block),
        wide(n // 2, head, 2 * group * block), low(length, qw), low(qw, length),
        low(length, fw), low(length, 2 * fw), low(length, qw + 2 * kw),
        wide(length, kw), wide(length, kw),
    ]
    scratch += [low(planes, n, per, size) for size in sizes]
    scratch += [low(planes + 1, n, per, size) for size in sizes]
    scratch += [low(n, per, sizes[m] + sizes[m + 1]) for m in (0, 2, 4)]
    scratch += [low(2, 4, block, width)] * 2 + [low(2, 3, block, width)] * 2 + [wide(2, block, width), wide(2, block, width)]
    scratch += [
        wide(block, width), wide(block, width), wide(8, width), wide(n, 8, width), wide(planes, 8, width),
        dma((13,)), dma((8, 6)), dma((8, planes)), dma((1, 7)), dma((1, 4)),
        dma((4, n)), dma((4, n)), dma((4, 4)), dma((4, 4)), dma((4, 4)), dma((4, 4)),
        dma((6, planes)), dma((6, planes + 1)), dma((3, n)), dma((3, n)), dma((n,)), dma((n,)),
        dma((planes,)), dma((planes,)),
    ]
    shapes = [
        jax.ShapeDtypeStruct((block, width), bf16),
        jax.ShapeDtypeStruct((block, width), f32),
        jax.ShapeDtypeStruct((8, width), f32),
    ] + [jax.ShapeDtypeStruct((n, per, sizes[m] + sizes[m + 1]), bf16) for m in (0, 2, 4)]
    results = pl.pallas_call(
        functools.partial(layer_kernel, n, planes, block, head, group, fw),
        out_shape=shapes,
        in_specs=[vmem] * 10 + [hbm] * 7,
        out_specs=[vmem] * len(shapes),
        scratch_shapes=scratch,
        compiler_params=pltpu.CompilerParams(
            collective_id=0, has_side_effects=True, vmem_limit_bytes=60 * 1024 * 1024),
    )(
        layer_input[0], out_cotangent[0], token_positions, inverse, step_cos, step_sin,
        attention_gain[None], feedforward_gain[None], query_gain[None], key_norm_gain[None],
        query_weight, key_matrix, value_matrix, output_weight, gate_weight, up_weight, down_weight,
    )
    plain = lambda rows, columns, kind=f32: jax.ShapeDtypeStruct((rows, columns), kind)
    finals = [
        plain(block, width, bf16), plain(block, width), plain(1, width),
        plain(per, n * qw), plain(per, n * kw), plain(per, n * kw), plain(1, head), plain(1, head),
        plain(per, n * qw), plain(1, width), plain(per, n * fw), plain(per, n * fw), plain(per, n * fw),
    ]
    done = pl.pallas_call(
        functools.partial(finish_kernel, n, head),
        out_shape=finals,
        in_specs=[vmem] * len(shapes),
        out_specs=[vmem] * len(finals),
    )(*results)
    out, dx, ag, q, k, v, qg, kg, o, fg, g, u, d = done
    return out[None], dx[None], ag[0], q, k, v, qg[0], kg[0], o.T, fg[0], g, u, d.T


def solution(mesh):
    in_specs = (
        P("fsdp", "ctx", None),
        P("fsdp", None),
        P(),
        P("fsdp", None),
        P("fsdp", None),
        P("fsdp", None),
        P(),
        P(),
        P("fsdp", None),
        P(),
        P("fsdp", None),
        P("fsdp", None),
        P("fsdp", None),
        P("fsdp", "ctx", None),
    )
    out_specs = (
        P("fsdp", "ctx", None),
        P("fsdp", "ctx", None),
        P(),
        P(("ctx", "fsdp"), None),
        P(("ctx", "fsdp"), None),
        P(("ctx", "fsdp"), None),
        P(),
        P(),
        P(None, ("ctx", "fsdp")),
        P(),
        P(("ctx", "fsdp"), None),
        P(("ctx", "fsdp"), None),
        P(None, ("ctx", "fsdp")),
    )

    def run(*arguments):
        n, planes = mesh.shape["ctx"], mesh.shape["fsdp"]
        key_heads = arguments[4].shape[1] // arguments[6].shape[0]
        whole_heads = n == 8 and planes == 4 and key_heads == n
        return jax.shard_map(
            plane_device if whole_heads else on_device,
            mesh=mesh, in_specs=in_specs, out_specs=out_specs, check_vma=False,
        )(*arguments)

    return run
```

```python
import functools

import jax
import jax.numpy as jnp
import numpy as np
from jax import lax
from jax.experimental import pallas as pl
from jax.experimental.pallas import tpu as pltpu
from jax.sharding import PartitionSpec as P

epsilon = 1e-06
rope_base = 1000000.0
masked_score = -1e30


def from_behind(block, axis, distance):
    devices = range(lax.axis_size(axis))
    route = [((i - distance) % len(devices), i) for i in devices]
    return lax.ppermute(block, axis, route)


def rotate(value_rows):
    half = value_rows.shape[-1] // 2
    return jnp.concatenate([-value_rows[..., half:], value_rows[..., :half]], -1)


def rotate_back(value_rows):
    half = value_rows.shape[-1] // 2
    return jnp.concatenate([value_rows[..., half:], -value_rows[..., :half]], -1)


def rope_tables(token_offsets, head_size):
    half = head_size // 2
    inverse = rope_base ** (-(jnp.arange(half).astype(jnp.float32) * 2.0) / head_size)
    angles = token_offsets.astype(jnp.float32)[:, None] * inverse[None, :]
    cosine = jnp.cos(angles)
    sine = jnp.sin(angles)
    return (jnp.concatenate([cosine, cosine], -1), jnp.concatenate([sine, sine], -1))


def norm_scale(value_rows):
    return lax.rsqrt(jnp.mean(value_rows * value_rows, -1, keepdims=True) + epsilon)


def norm_back(value_rows, scale, gain, grad):
    weighted = grad * gain
    inner = jnp.mean(weighted * value_rows, -1, keepdims=True)
    result = scale * weighted - value_rows * scale * scale * scale * inner
    gain_part = jnp.sum((grad * value_rows * scale).reshape(-1, gain.shape[0]), 0)
    return (result, gain_part)


def row_products(left, pieces):
    return tuple((jnp.dot(left, piece, preferred_element_type=jnp.float32) for piece in pieces))


def column_products(rights, pieces):
    total = jnp.einsum("tc,rc->tr", rights[0], pieces[0], preferred_element_type=jnp.float32)
    for right, piece in zip(rights[1:], pieces[1:]):
        total = total + jnp.einsum("tc,rc->tr", right, piece, preferred_element_type=jnp.float32)
    return total


def on_device(
    layer_input,
    token_positions,
    attention_gain,
    query_weight,
    key_matrix,
    value_matrix,
    query_gain,
    key_norm_gain,
    output_weight,
    feedforward_gain,
    gate_weight,
    up_weight,
    down_weight,
    out_cotangent,
):
    hidden_in = layer_input[0].astype(jnp.float32)
    count = hidden_in.shape[0]
    head_size = query_gain.shape[0]
    query_width = query_weight.shape[1]
    key_width = key_matrix.shape[1]
    inner_width = gate_weight.shape[1]
    heads = query_width // head_size
    key_heads = key_width // head_size
    group = heads // key_heads
    scale = head_size ** (-0.5)
    cycles = lax.axis_size("ctx")
    own_index = lax.axis_index("ctx")
    sequence_pos = token_positions[0]
    token_offsets = lax.dynamic_slice_in_dim(sequence_pos, own_index * count, count)
    cosine, sine = rope_tables(token_offsets, head_size)
    cosine = cosine[:, None, :]
    sine = sine[:, None, :]
    first_scale = norm_scale(hidden_in)
    first = (hidden_in * first_scale * attention_gain).astype(jnp.bfloat16)
    query_raw, key_unnormed, value_unnormed = row_products(
        first,
        (
            lax.all_gather(query_weight, "fsdp", axis=0, tiled=True),
            lax.all_gather(key_matrix, "fsdp", axis=0, tiled=True),
            lax.all_gather(value_matrix, "fsdp", axis=0, tiled=True),
        ),
    )
    query_heads = query_raw.reshape(count, heads, head_size)
    query_scale = norm_scale(query_heads)
    query_normed = query_heads * query_scale * query_gain
    query_rot = query_normed * cosine + rotate(query_normed) * sine
    query_grouped = (
        query_rot.reshape(count, key_heads, group, head_size)
        .transpose(1, 2, 0, 3)
        .astype(jnp.bfloat16)
    )
    key_heads_raw = key_unnormed.reshape(count, key_heads, head_size)
    key_scale = norm_scale(key_heads_raw)
    key_normed = key_heads_raw * key_scale * key_norm_gain
    key_low = (
        (key_normed * cosine + rotate(key_normed) * sine)
        .reshape(count, key_width)
        .astype(jnp.bfloat16)
    )
    value_low = value_unnormed.astype(jnp.bfloat16)
    rowmax = jnp.full((key_heads, group, count), masked_score, jnp.float32)
    keys_piece = lax.all_gather(key_low, "ctx", axis=0, tiled=True).reshape(
        -1, key_heads, head_size
    )
    values_piece = lax.all_gather(value_low, "ctx", axis=0, tiled=True).reshape(
        -1, key_heads, head_size
    )
    key_pos = sequence_pos
    allowed = token_offsets[:, None] >= key_pos[None, :]
    scores = (
        jnp.einsum("kgtd,skd->kgts", query_grouped, keys_piece, preferred_element_type=jnp.float32)
        * scale
    )
    scores = jnp.where(allowed, scores, masked_score)
    newmax = jnp.maximum(rowmax, jnp.max(scores, -1))
    weights = jnp.where(allowed, jnp.exp(scores - newmax[..., None]), 0.0)
    accum = jnp.einsum(
        "kgts,skd->kgtd",
        weights.astype(jnp.bfloat16),
        values_piece,
        preferred_element_type=jnp.float32,
    )
    rowsum = jnp.sum(weights, -1)
    accum, rowmax, rowsum = (accum, newmax, rowsum)
    normalized = accum / rowsum[..., None]
    logsum = rowmax + jnp.log(rowsum)
    attention_low = (
        normalized.transpose(2, 0, 1, 3).reshape(count, query_width).astype(jnp.bfloat16)
    )
    output_whole = lax.all_gather(output_weight, "fsdp", axis=0, tiled=True)
    branch_out = jnp.dot(attention_low, output_whole, preferred_element_type=jnp.float32)
    middle = hidden_in + branch_out
    second_scale = norm_scale(middle)
    second = (middle * second_scale * feedforward_gain).astype(jnp.bfloat16)
    gate, up = row_products(
        second,
        (
            lax.all_gather(gate_weight, "fsdp", axis=0, tiled=True),
            lax.all_gather(up_weight, "fsdp", axis=0, tiled=True),
        ),
    )
    sigmoid_gate = jax.nn.sigmoid(gate)
    silu_gate = gate * sigmoid_gate
    hidden_low = (silu_gate * up).astype(jnp.bfloat16)
    (down_out,) = row_products(
        hidden_low, (lax.all_gather(down_weight, "fsdp", axis=0, tiled=True),)
    )
    layer_output = (middle + down_out).astype(jnp.bfloat16)[None]
    cotangent = out_cotangent[0]
    hidden_grad = column_products(
        (cotangent,), lax.all_gather((down_weight,), "fsdp", axis=0, tiled=True)
    )
    up_low = (hidden_grad * silu_gate).astype(jnp.bfloat16)
    gate_low = (hidden_grad * up * sigmoid_gate * (1.0 + gate * (1.0 - sigmoid_gate))).astype(
        jnp.bfloat16
    )
    second_grad = column_products(
        (gate_low, up_low), lax.all_gather((gate_weight, up_weight), "fsdp", axis=0, tiled=True)
    )
    middle_part, feedforward_part = norm_back(middle, second_scale, feedforward_gain, second_grad)
    middle_grad = cotangent.astype(jnp.float32) + middle_part
    middle_low = middle_grad.astype(jnp.bfloat16)
    attention_grad = jnp.einsum(
        "tc,rc->tr", middle_low, output_whole, preferred_element_type=jnp.float32
    )
    attention_grad_low = attention_grad.astype(jnp.bfloat16)
    mixed_grad = attention_grad_low.reshape(count, key_heads, group, head_size).transpose(
        1, 2, 0, 3
    )
    delta = jnp.sum(mixed_grad.astype(jnp.float32) * normalized, -1)

    def cycle_step(index, carry):
        keys_held, values_held, key_acc, value_acc, query_acc = carry
        anchor = (own_index - index) % cycles
        key_pos = lax.dynamic_slice_in_dim(sequence_pos, anchor * count, count)
        keys_piece = keys_held.astype(jnp.bfloat16).reshape(count, key_heads, head_size)
        values_piece = values_held.astype(jnp.bfloat16).reshape(count, key_heads, head_size)
        allowed = token_offsets[:, None] >= key_pos[None, :]
        scores = (
            jnp.einsum(
                "kgtd,skd->kgts", query_grouped, keys_piece, preferred_element_type=jnp.float32
            )
            * scale
        )
        probs = jnp.where(allowed, jnp.exp(scores - logsum[..., None]), 0.0)
        value_acc = value_acc + jnp.einsum(
            "kgts,kgtd->skd",
            probs.astype(jnp.bfloat16),
            mixed_grad,
            preferred_element_type=jnp.float32,
        ).reshape(count, key_width)
        prob_grad = jnp.einsum(
            "kgtd,skd->kgts", mixed_grad, values_piece, preferred_element_type=jnp.float32
        )
        score_grad = (probs * (prob_grad - delta[..., None])).astype(jnp.bfloat16)
        query_acc = (
            query_acc
            + jnp.einsum(
                "kgts,skd->kgtd", score_grad, keys_piece, preferred_element_type=jnp.float32
            )
            * scale
        )
        key_acc = (
            key_acc
            + jnp.einsum(
                "kgts,kgtd->skd", score_grad, query_grouped, preferred_element_type=jnp.float32
            ).reshape(count, key_width)
            * scale
        )
        moved = (
            from_behind(keys_held.astype(jnp.bfloat16), "ctx", 1).astype(keys_held.dtype),
            from_behind(values_held.astype(jnp.bfloat16), "ctx", 1).astype(values_held.dtype),
            from_behind(key_acc.astype(jnp.bfloat16), "ctx", 1).astype(key_acc.dtype),
            from_behind(value_acc.astype(jnp.bfloat16), "ctx", 1).astype(value_acc.dtype),
        )
        return (moved[0], moved[1], moved[2], moved[3], query_acc)

    start_cycle = (
        key_low.astype(jnp.float32),
        value_low.astype(jnp.float32),
        jnp.zeros((count, key_width), jnp.float32),
        jnp.zeros((count, key_width), jnp.float32),
        jnp.zeros((key_heads, group, count, head_size), jnp.float32),
    )
    cycle_done = lax.fori_loop(0, cycles, cycle_step, start_cycle)
    key_acc = cycle_done[2]
    value_acc = cycle_done[3]
    query_acc = cycle_done[4]
    query_rot_grad = query_acc.transpose(2, 0, 1, 3).reshape(count, heads, head_size)
    query_normed_grad = query_rot_grad * cosine + rotate_back(query_rot_grad * sine)
    query_heads_grad, query_part = norm_back(
        query_heads, query_scale, query_gain, query_normed_grad
    )
    query_low_grad = query_heads_grad.reshape(count, query_width).astype(jnp.bfloat16)
    key_rot_grad = key_acc.reshape(count, key_heads, head_size)
    key_normed_grad = key_rot_grad * cosine + rotate_back(key_rot_grad * sine)
    key_heads_grad, key_part = norm_back(key_heads_raw, key_scale, key_norm_gain, key_normed_grad)
    key_low_grad = key_heads_grad.reshape(count, key_width).astype(jnp.bfloat16)
    value_low_grad = value_acc.astype(jnp.bfloat16)
    first_grad = column_products(
        (query_low_grad, key_low_grad, value_low_grad),
        lax.all_gather((query_weight, key_matrix, value_matrix), "fsdp", axis=0, tiled=True),
    )
    input_part, attention_part = norm_back(hidden_in, first_scale, attention_gain, first_grad)
    input_gradient = (middle_grad + input_part)[None]
    rights_first = jnp.concatenate([query_low_grad, key_low_grad, value_low_grad], 1)
    rights_second = jnp.concatenate([gate_low, up_low], 1)
    pairs = (
        (first, rights_first),
        (second, rights_second),
        (middle_low, attention_low),
        (cotangent, hidden_low),
    )
    parts = []
    for left, right in pairs:
        parts.append(jnp.einsum("tr,tc->rc", left, right, preferred_element_type=jnp.float32))
    sums = lax.psum_scatter(
        jnp.concatenate(parts, 1), ("ctx", "fsdp"), scatter_dimension=0, tiled=True
    )
    edges = [0, query_width, query_width + key_width, query_width + 2 * key_width]
    edges = edges + [edges[3] + inner_width, edges[3] + 2 * inner_width]
    edges = edges + [edges[5] + query_width, edges[5] + query_width + inner_width]
    query_gradient = sums[:, edges[0] : edges[1]]
    key_gradient = sums[:, edges[1] : edges[2]]
    value_gradient = sums[:, edges[2] : edges[3]]
    gate_gradient = sums[:, edges[3] : edges[4]]
    up_gradient = sums[:, edges[4] : edges[5]]
    output_gradient = sums[:, edges[5] : edges[6]].T
    down_gradient = sums[:, edges[6] : edges[7]].T
    attention_total, query_total, key_total, feedforward_total = lax.psum(
        (attention_part, query_part, key_part, feedforward_part), ("ctx", "fsdp")
    )
    return (
        layer_output,
        input_gradient,
        attention_total,
        query_gradient,
        key_gradient,
        value_gradient,
        query_total,
        key_total,
        output_gradient,
        feedforward_total,
        gate_gradient,
        up_gradient,
        down_gradient,
    )


MESH = pl.DeviceIdType.MESH
f32 = jnp.float32
bf16 = jnp.bfloat16


def dot(left, right):
    return jnp.dot(left, right, preferred_element_type=f32)


def dot_nt(left, right):
    return lax.dot_general(left, right, (((1,), (1,)), ((), ())), preferred_element_type=f32)


def dot_tn(left, right):
    return lax.dot_general(left, right, (((0,), (0,)), ((), ())), preferred_element_type=f32)


def hidden_block(device, third):
    def plane(i, t):
        return ((3, 1, 2), (0, 2, 1), (0, 3, 2), (3, 0, 1))[i // 4 * 2 + i % 2][t]

    own = plane(device, third)
    return own, sum(plane(i, t) == own for i in range(device) for t in range(3))


def layer_kernel(
    n, planes, block, head, group, fw,
    x_ref, dy_ref, pos_row, inverse_ref, step_cos, step_sin, ag_ref, fg_ref, qg_ref, kg_ref,
    wq, wk, wv, wo, wg, wu, wd,
    out_ref, dx_ref, gains_ref, got_ab, got_co, got_qkv,
    w_qkv, w_gu, w_out, w_down, t_out,
    first, dy_all, second, first_t, dy_t, second_t,
    positions, cosine, sine,
    raw, queries, keys, values, keys_t, values_t, probs, sums, mixed_t, mixed_low, mixed_low_t,
    hidden, d_gu, d_qkv, dk_acc, dv_acc,
    stage_a, stage_b, stage_c, stage_out, stage_q, stage_kv,
    land_a, land_b, land_c, land_out, land_q, land_kv,
    own_ab, own_co, own_qkv,
    rs_sa, rs_ra, rs_sb, rs_rb, rs_kept, rs_acc,
    middle, d_middle, gain_own, gain_plane, gain_all,
    local_sem, wz_send, wz_recv, hand_send, hand_recv,
    ag_send, ag_recv, ra_send, ra_recv, rb_send, rb_recv,
    zr_send, zr_recv, aa_send, aa_recv, gp_send, gp_recv, gz_send, gz_recv,
):
    c = lax.axis_index("ctx")
    z = lax.axis_index("fsdp")
    dmid = first
    cy, cx, ck = lax.div(c, 4), lax.rem(lax.div(c, 2), 2), lax.rem(c, 2)
    ci = lax.rem(c, 4)
    sign = 1 - 2 * ck
    qw, kw = group * head, head
    pw = 128
    thirds = fw // pw
    width = x_ref.shape[1]
    scale = head ** (-0.5)
    log2e = 1.4426950408889634
    gots = (got_ab, got_co, got_qkv)
    owns = (own_ab, own_co, own_qkv)
    stages = (stage_a, stage_b, stage_c, stage_out, stage_q, stage_kv)
    lands = (land_a, land_b, land_c, land_out, land_q, land_kv)

    def partner(j):
        y = lax.rem(cy + lax.div(j, 4), 2)
        x = lax.rem(cx + lax.rem(lax.div(j, 2), 2), 2)
        k = lax.rem(ck + lax.rem(j, 2), 2)
        return y * 4 + x * 2 + k

    def chip(slot):
        return lax.rem(cy + lax.div(slot, 2), 2) * 2 + lax.rem(cx + lax.rem(slot, 2), 2)

    def rows(start, size):
        return pl.ds(pl.multiple_of(start * size, size), size)

    def remote(src, dst, send, recv, ctx, plane):
        return pltpu.make_async_remote_copy(
            src_ref=src, dst_ref=dst, send_sem=send, recv_sem=recv,
            device_id={"ctx": ctx, "fsdp": plane}, device_id_type=MESH,
        )

    in_plane, along, weight_sends = [], [], []

    def launch(started, copy, when=None):
        if when is None:
            copy().start()
        else:
            pl.when(when)(lambda: copy().start())
        started.append((copy, when))

    def drain(started):
        for copy, when in started:
            if when is None:
                copy().wait_send()
            else:
                pl.when(when)(lambda copy=copy: copy().wait_send())
        started.clear()

    def pick(values):
        return sum(jnp.where(c == i, value, 0) for i, value in enumerate(values))

    unit_plane = [pick([hidden_block(i, t)[0] for i in range(n)]) for t in range(thirds)]
    unit_block = [pick([hidden_block(i, t)[1] for i in range(n)]) for t in range(thirds)]
    plane_blocks = wd.shape[0] // pw

    own_rows = wq.shape[0]
    out_rows = wo.shape[0] // n

    def own_slices():
        mine = rows(z, own_rows)
        pairs = [
            (wq.at[:, rows(c, qw)], w_qkv.at[mine, 0:qw]),
            (wk.at[:, rows(c, kw)], w_qkv.at[mine, qw:qw + kw]),
            (wv.at[:, rows(c, kw)], w_qkv.at[mine, qw + kw:qw + 2 * kw]),
            (wo.at[rows(c, out_rows)], t_out.at[rows(z, out_rows)]),
        ]
        for t in range(thirds):
            at = 2 * pw * t
            unit = unit_plane[t] * plane_blocks + unit_block[t]
            pairs.append((wg.at[:, rows(unit, pw)], w_gu.at[mine, at:at + pw]))
            pairs.append((wu.at[:, rows(unit, pw)], w_gu.at[mine, at + pw:at + 2 * pw]))
        return pairs

    local = [pltpu.make_async_copy(src, dst, local_sem.at[i]) for i, (src, dst) in enumerate(own_slices())]
    for copy in local:
        copy.start()

    def own_down(t):
        return pltpu.make_async_copy(
            wd.at[rows(unit_block[t], pw)], w_down.at[t * pw:(t + 1) * pw], local_sem.at[4 + 2 * thirds + t])

    holds = [unit_plane[t] == z for t in range(thirds)]
    for t in range(thirds):
        pl.when(holds[t])(lambda t=t: own_down(t).start())

    for land in lands:
        @pl.when(z == 0)
        def _(land=land):
            land[0] = jnp.zeros(land.shape[1:], bf16)

        @pl.when(z == planes - 1)
        def _(land=land):
            land[planes] = jnp.zeros(land.shape[1:], bf16)

    barrier = pltpu.get_barrier_semaphore()
    for j in range(1, n):
        pl.semaphore_signal(barrier, inc=1, device_id={"ctx": partner(j), "fsdp": z}, device_id_type=MESH)
    for d in range(1, planes):
        pl.semaphore_signal(
            barrier, inc=1, device_id={"ctx": c, "fsdp": lax.rem(z + d, planes)}, device_id_type=MESH)
    x = x_ref[...].astype(f32)
    x_scale = lax.rsqrt(jnp.mean(x * x, -1, keepdims=True) + epsilon)
    first[rows(c, block)] = (x * x_scale * ag_ref[...]).astype(bf16)
    dy_all[rows(c, block)] = dy_ref[...]
    for copy in local[:3]:
        copy.wait()
    pl.semaphore_wait(barrier, n + planes - 2)

    def inside(t):
        return jnp.logical_and(t >= 0, t < planes)

    weights = [
        (lambda o: w_qkv.at[rows(o, own_rows)], None),
        (lambda o: t_out.at[rows(o, out_rows)], 0),
    ]
    for t in range(thirds):
        weights.append((lambda o, t=t: w_gu.at[rows(o, own_rows), 2 * pw * t:2 * pw * (t + 1)], None))
        weights.append((lambda o, t=t: w_down.at[t * pw:(t + 1) * pw], None))

    def weight_copy(w, slot, origin, target):
        part = weights[w][0](origin)
        return remote(part, part, wz_send.at[w, slot], wz_recv.at[w, origin], c, target)

    def from_plane(w, origin):
        return origin == unit_plane[(w - 3) // 2] if w >= 3 and w % 2 else None

    def both(one, other):
        return one if other is None else jnp.logical_and(one, other)

    def hand_split(origin, valid):
        mine = 2 * origin + cy == c
        return jnp.logical_and(valid, jnp.logical_not(mine)), jnp.logical_and(valid, mine)

    def weight_start(w):
        for side in range(2):
            d = sign * (1 - 2 * side)
            launch(
                weight_sends, lambda side=side, d=d: weight_copy(w, side, z, z + d),
                both(inside(z + d), from_plane(w, z)))
        if weights[w][1] is not None:
            hand_over(w, z, 0, *hand_split(z, True))

    def hand_target(h):
        return lambda i: w_out.at[rows(i, out_rows)]

    def hand_copy(w, origin, slot):
        h = weights[w][1]
        return remote(
            weights[w][0](origin), hand_target(h)(ci), hand_send.at[h, slot], hand_recv.at[h, ci], 2 * origin + cy, z)

    def hand_over(w, origin, slot, away, here):
        launch(in_plane, lambda: hand_copy(w, origin, slot), away)

        @pl.when(here)
        def _():
            hand_target(weights[w][1])(ci)[...] = weights[w][0](origin)[...]

    def hand_arrive(w):
        h = weights[w][1]
        for i in range(4):
            @pl.when(4 * ck + i != c)
            def _(i=i):
                part = hand_target(h)(i)
                remote(part, part, hand_send.at[h, 0], hand_recv.at[h, i], c, z).wait_recv()

    hops = {}
    for w in range(len(weights)):
        for d in range(1, planes):
            for side, way in enumerate((1, -1)):
                origin = z - way * d
                valid = both(inside(origin), from_plane(w, origin))
                passed = jnp.logical_and(valid, inside(z + way))
                split = None if weights[w][1] is None else hand_split(origin, valid)
                hops[w, d, side] = origin, z + way, valid, passed, split

    def weight_hop(w, d):
        for side in range(2):
            origin, following, valid, passed, split = hops[w, d, side]
            pl.when(valid)(lambda: weight_copy(w, 0, origin, z).wait_recv())
            if d < planes - 1:
                launch(
                    weight_sends,
                    lambda side=side, origin=origin, following=following: weight_copy(
                        w, 2 * d + side, origin, following),
                    passed)
            if split is not None:
                hand_over(w, origin, 2 * d - 1 + side, *split)

    def gather_copy(buf, g, j, send, origin, target):
        part = buf.at[rows(origin, block)]
        return remote(part, part, ag_send.at[g, send], ag_recv.at[g, j], target, z)

    def gather_start(buf, g):
        for j in (1, 2 + 2 * ck, 4 - 2 * ck):
            launch(in_plane, lambda j=j: gather_copy(buf, g, j, j, c, partner(j)))

    def gather_half(buf, g, j):
        half = block // 2
        part = buf.at[pl.ds(pl.multiple_of(partner(j) * block + (half if j == 2 else 0), half), half)]
        at = 0 if j == 2 else 6
        return remote(part, part, ag_send.at[g, at], ag_recv.at[g, at], partner(6 - j), z)

    def gather_diagonal(buf, g):
        half = block // 2
        for at in (6, 0):
            part = buf.at[pl.ds(pl.multiple_of(partner(6) * block + (0 if at == 6 else half), half), half)]
            remote(part, part, ag_send.at[g, at], ag_recv.at[g, at], c, z).wait_recv()

    def gather_forward(buf, g, j):
        return gather_copy(buf, g, j + 1, j + 1, partner(j), partner(1))

    def gather_take(buf, g, j):
        if j == 6:
            gather_diagonal(buf, g)
        else:
            gather_copy(buf, g, j, j, partner(j), c).wait_recv()
            gather_half(buf, g, j).start()
        gather_forward(buf, g, j).start()

    def gather_sent(buf, g):
        for j in (2, 4, 6):
            in_plane.append((lambda j=j: gather_forward(buf, g, j), None))
            if j < 6:
                in_plane.append((lambda j=j: gather_half(buf, g, j), None))

    def gather_finish(buf, g):
        for j in (2, 4, 6):
            gather_take(buf, g, j)
        gather_sent(buf, g)
        for j in (1, 3, 5, 7):
            gather_copy(buf, g, j, j, partner(j), c).wait_recv()

    def gather_step(buf, g, slot):
        @pl.when(slot == 1)
        def _():
            gather_take(buf, g, 2)
            gather_take(buf, g, 4)

        pl.when(slot == 3)(lambda: gather_take(buf, g, 6))
        gather_copy(buf, g, 2 * slot + 1, 0, partner(2 * slot + 1), c).wait_recv()

    def sum_pair_copy(s, slot):
        return remote(rs_sa.at[s % 2, slot], rs_ra.at[s % 2, slot], ra_send.at[s, slot], ra_recv.at[s, slot], partner(1), z)

    def sum_chip_copy(s, slot):
        return remote(
            rs_sb.at[s % 2, slot - 1], rs_rb.at[s % 2, slot - 1], rb_send.at[s, slot], rb_recv.at[s, slot], partner(2 * slot), z)

    def sum_half_copy(s, slot):
        half = block // 2
        at = pl.ds(pl.multiple_of((slot - 1) * half, half), half)
        return remote(
            rs_sb.at[s % 2, 2, at], rs_rb.at[s % 2, 2, at], rb_send.at[s, 6 - 3 * slot], rb_recv.at[s, 6 - 3 * slot],
            partner(6 - 2 * slot), z)

    def sum_slot(p):
        return jnp.where(p == 0, 3, jnp.where(p == 1, 2 - ck, jnp.where(p == 2, 1 + ck, 0)))

    def sum_start(s, left, partial, prepare=None, ready=None, during=()):
        if prepare is not None:
            for step in prepare:
                step(chip(sum_slot(0)))
        if ready is not None:
            ready()

        def body(p, carry):
            slot = sum_slot(p)
            at = [rows(partner(2 * slot + 1), block), rows(partner(2 * slot), block)]
            both = partial(jnp.concatenate([left[i] for i in at], 0))
            rs_sa[s % 2, slot] = both[:block].astype(bf16)
            sum_pair_copy(s, slot).start()
            rs_kept[lax.rem(p, 2)] = both[block:]

            def pair_sum(q):
                before = sum_slot(q)
                sum_pair_copy(s, before).wait_recv()
                rs_sb[s % 2, before - 1] = (
                    rs_kept[lax.rem(q, 2)] + rs_ra[s % 2, before].astype(f32)).astype(bf16)

            def chip_send(q):
                before = sum_slot(q)
                half = block // 2
                at = pl.ds(pl.multiple_of((before - 1) * half, half), half)
                sum_half_copy(s, before).wait_recv()
                rs_sb[s % 2, before - 1, at] = (
                    rs_sb[s % 2, before - 1, at].astype(f32) + rs_rb[s % 2, 2, at].astype(f32)).astype(bf16)
                sum_chip_copy(s, before).start()

            early = prepare is not None and len(prepare) > 1

            @pl.when(p == 1)
            def _():
                pair_sum(0)
                sum_half_copy(s, 1).start()
                sum_half_copy(s, 2).start()

            @pl.when(p == 2 if early else p > 1)
            def _():
                pair_sum(p - 1)
                chip_send(p - 1)

            if prepare is not None:
                @pl.when(p < 3)
                def _():
                    prepare[0](chip(sum_slot(p + 1)))

            if early:
                @pl.when(p == 2)
                def _():
                    pair_sum(2)
                    chip_send(2)

                @pl.when(p < 3)
                def _():
                    for step in prepare[1:]:
                        step(chip(sum_slot(p + 1)))

            for k, poll in enumerate(during):
                pl.when(p == k)(poll)
            return carry

        lax.fori_loop(0, 4, body, 0)
        for slot in range(4):
            in_plane.append((lambda slot=slot: sum_pair_copy(s, slot), None))
        for slot in (1, 2):
            in_plane.append((lambda slot=slot: sum_half_copy(s, slot), None))
            in_plane.append((lambda slot=slot: sum_chip_copy(s, slot), None))
        sum_pair_copy(s, 0).wait_recv()
        rs_acc[s % 2] = rs_kept[1] + rs_ra[s % 2, 0].astype(f32)

    def sum_finish(s):
        total = rs_acc[s % 2]
        for slot in (1, 2):
            sum_chip_copy(s, slot).wait_recv()
            total = total + rs_rb[s % 2, slot - 1].astype(f32)
        return total

    per = block // planes

    at_edge = jnp.logical_or(z == 0, z == planes - 1)
    edge_targets = [jnp.where(z == 0, planes - 1 - k, k) for k in range(planes - 1)]

    def weight_grad(m, parts):
        def body(i, carry):
            at = 0
            for left, right in parts:
                value = right()
                grad = dot(left[rows(i, 4 * block)], value)
                for k in range(4):
                    for t in range(planes):
                        start = k * block + t * per
                        stages[m][t, 4 * i + k, :, at:at + value.shape[1]] = grad[start:start + per].astype(bf16)
                at += value.shape[1]
            return carry

        lax.fori_loop(0, n // 4, body, 0)
        grad_send(m)

    def grad_send(m):
        for t in edge_targets:
            launch(along, lambda t=t: grad_copy(m, t), at_edge)

    def grad_copy(m, t):
        way = jnp.where(z < t, 1, -1)
        last = z + way == t
        slot = jnp.where(jnp.logical_and(last, way < 0), planes, t)
        return remote(
            stages[m].at[t], lands[m].at[slot], zr_send.at[m, t], zr_recv.at[m, slot], c, z + way)

    def grad_arrive(m, slot):
        part = lands[m].at[slot]
        remote(part, part, zr_send.at[m, 0], zr_recv.at[m, slot], c, z).wait_recv()

    def grad_pass(m, t, valid):
        @pl.when(valid)
        def _():
            grad_arrive(m, t)
            stages[m][t] = stages[m][t] + lands[m][t]

        launch(along, lambda: grad_copy(m, t), valid)

    is_low, is_high = z == 1, z == planes - 2

    def grad_near_far(m):
        grad_pass(m, 3, is_low)
        grad_pass(m, 0, is_high)

    def grad_near_inner(m):
        grad_pass(m, 2, is_low)
        grad_pass(m, 1, is_high)

    def grad_near(m):
        grad_near_far(m)
        grad_near_inner(m)

    def grad_far(m):
        grad_pass(m, 3, is_high)
        grad_pass(m, 0, is_low)

    def owner_copy(g, j):
        return remote(owns[g].at[partner(j)], gots[g].at[c], aa_send.at[g, j], aa_recv.at[g, j], partner(j), z)

    def own_sum(m):
        pl.when(z > 0)(lambda: grad_arrive(m, z))
        pl.when(z < planes - 1)(lambda: grad_arrive(m, planes))
        total = stages[m][z].astype(f32) + lands[m][z].astype(f32) + lands[m][planes].astype(f32)
        first_size = stages[m // 2 * 2].shape[3]
        if m % 2:
            owns[m // 2][:, :, first_size:] = total.astype(bf16)
        else:
            owns[m // 2][:, :, :first_size] = total.astype(bf16)

    def hand_out(g):
        for j in (2 + 2 * ck, 3 + 2 * ck, 4 - 2 * ck, 5 - 2 * ck, 6, 7, 1):
            launch(in_plane, lambda j=j: owner_copy(g, j))
        gots[g][c] = owns[g][c]

    def hand_receive(g):
        for j in range(1, n):
            owner_copy(g, j).wait_recv()

    weight_start(0)
    gather_start(first, 0)
    for copy in local[3:]:
        copy.wait()
    for t in range(thirds):
        pl.when(holds[t])(lambda t=t: own_down(t).wait())

    spread = jnp.broadcast_to(pos_row[...].astype(f32), (head, pos_row.shape[1]))
    positions[...] = spread.T
    side = jnp.where(lax.broadcasted_iota(jnp.int32, (1, head), 1) < head // 2, -1.0, 1.0)

    def table(i, carry):
        run = step_cos.shape[0]
        at = rows(i, run)
        start = positions[pl.ds(pl.multiple_of(i * run, run), 1)] * inverse_ref[...]
        start_cos, start_sin = jnp.cos(start), jnp.sin(start)
        cosine[at] = start_cos * step_cos[...] - start_sin * step_sin[...]
        sine[at] = (start_sin * step_cos[...] + start_cos * step_sin[...]) * side
        return carry

    def turn_over(src, dst):
        def body(i, carry):
            at = rows(i, block)
            dst[:, at] = src[at].T
            return carry

        lax.fori_loop(0, n, body, 0)

    lax.fori_loop(0, 2 * n, table, 0)
    weight_hop(0, 1)
    gather_finish(first, 0)
    weight_hop(0, 2)
    weight_start(1)
    gather_start(dy_all, 1)
    turn_over(first, first_t)
    weight_hop(0, 3)
    weight_start(2)
    weight_start(3)

    def turn(value, at):
        return value * cosine[at] + pltpu.roll(value, head // 2, 1) * sine[at]

    def turn_back(grad, at):
        return grad * cosine[at] - pltpu.roll(grad, head // 2, 1) * sine[at]

    def project(i, carry):
        at = rows(i, 2 * block)
        result = dot(first[at], w_qkv[...])
        raw[at] = result[:, :qw + kw]
        low_values = result[:, qw + kw:].astype(bf16)
        values[at] = low_values
        values_t[:, at] = low_values.T
        for h in range(group + 1):
            part = result[:, h * head:(h + 1) * head]
            inv = lax.rsqrt(jnp.mean(part * part, -1, keepdims=True) + epsilon)
            gain = qg_ref[...] if h < group else kg_ref[...]
            turned = turn(part * inv * gain, at)
            if h < group:
                queries[at, h * head:(h + 1) * head] = (turned * (scale * log2e)).astype(bf16)
            else:
                low_keys = turned.astype(bf16)
                keys[at] = low_keys
                keys_t[:, at] = low_keys.T
        return carry

    lax.fori_loop(0, n // 4, project, 0)
    weight_hop(1, 1)
    lax.fori_loop(n // 4, n // 2, project, 0)
    weight_hop(1, 2)
    gather_finish(dy_all, 1)

    def stack(ref, at):
        return jnp.concatenate([ref[at, h * head:(h + 1) * head] for h in range(group)], 0)

    def attend(place, h):
        at = rows(place, 2 * block)
        columns = slice(h * head, (h + 1) * head)
        tokens = slice(2 * h * block, 2 * (h + 1) * block)
        scores = dot_nt(keys[...], queries[at, columns])
        weight = jnp.concatenate(
            [jnp.exp2(jnp.where(
                positions[...] <= pos_row[:, rows(2 * place + k, block)].astype(f32),
                scores[:, k * block:(k + 1) * block], masked_score)) for k in range(2)], 1)
        inv = 1.0 / jnp.sum(weight, 0, keepdims=True)
        low_weight = weight.astype(bf16)
        probs[place, :, tokens] = low_weight
        sums[place, :, tokens] = inv
        result = dot(values_t[...], low_weight) * inv
        mixed_t[place, :, tokens] = result
        low_result = result.astype(bf16)
        mixed_low_t[columns, at] = low_result
        mixed_low[at, columns] = low_result.T

    def output_ready():
        weight_hop(1, 3)
        weight_start(4)
        weight_start(5)
        hand_arrive(1)
        drain(in_plane)

    def hop_third(t, d):
        weight_hop(2 + 2 * t, d)
        weight_hop(3 + 2 * t, d)

    sum_start(
        0, mixed_low, lambda left: dot(left, w_out[...]),
        [lambda place, h=h: attend(place, h) for h in range(group)], output_ready,
        (lambda: hop_third(0, 1), lambda: hop_third(0, 2), lambda: hop_third(1, 1)))
    weight_start(6)
    weight_start(7)
    hop_third(0, 3)
    hop_third(1, 2)
    mid = x_ref[...].astype(f32) + sum_finish(0)
    middle[...] = mid
    mid_scale = lax.rsqrt(jnp.mean(mid * mid, -1, keepdims=True) + epsilon)
    second[rows(c, block)] = (mid * mid_scale * fg_ref[...]).astype(bf16)
    gather_start(second, 2)
    turn_over(dy_all, dy_t)
    hop_third(2, 1)

    def feed(t, at):
        units, pair = slice(t * pw, (t + 1) * pw), 2 * pw * t
        both = dot(second[at], w_gu[:, pair:pair + 2 * pw])
        back = dot_nt(dy_all[at], w_down[units])
        gate, up = both[:, :pw], both[:, pw:]
        sig = 1.0 / (1.0 + jnp.exp(-gate))
        silu = gate * sig
        hidden[at, units] = (silu * up).astype(bf16)
        d_gu[at, pair:pair + pw] = (back * up * sig * (1.0 + gate * (1.0 - sig))).astype(bf16)
        d_gu[at, pair + pw:pair + 2 * pw] = (back * silu).astype(bf16)

    def feed_arriving(slot, carry):
        gather_step(second, 2, slot)
        at = rows(chip(slot), 2 * block)
        feed(0, at)
        second_t[:, at] = second[at].T
        pl.when(slot == 2)(lambda: hop_third(2, 2))
        return carry

    def third_grad(t):
        weight_grad(t, [
            (second_t, lambda: d_gu[:, 2 * pw * t:2 * pw * (t + 1)]),
            (dy_t, lambda: hidden[:, t * pw:(t + 1) * pw]),
        ])

    def feed_third(t):
        def body(i, carry):
            feed(t, rows(i, 2 * block))
            return carry

        lax.fori_loop(0, n // 2, body, 0)

    lax.fori_loop(0, n // 2, feed_arriving, 0)
    gather_sent(second, 2)
    hop_third(1, 3)
    third_grad(0)
    feed_third(1)
    hop_third(2, 3)
    sum_start(
        1, d_gu, lambda left: dot_nt(left, w_gu[...]),
        [lambda place: feed(thirds - 1, rows(place, 2 * block))])
    third_grad(1)
    third_grad(2)
    d_second = sum_finish(1)

    def norm_back(value, gain, grad):
        inv = lax.rsqrt(jnp.mean(value * value, -1, keepdims=True) + epsilon)
        weighted = grad * gain
        inner = jnp.mean(weighted * value, -1, keepdims=True)
        result = inv * weighted - value * (inv * inv * inv * inner)
        return result, jnp.sum(grad * value * inv, 0, keepdims=True)

    gain_own[...] = jnp.zeros_like(gain_own)
    part, gain_own[1:2, :] = norm_back(middle[...], fg_ref[...], d_second)
    d_mid = dy_ref[...].astype(f32) + part
    d_middle[...] = d_mid
    drain(in_plane)
    dmid[rows(c, block)] = d_mid.astype(bf16)
    gather_start(dmid, 3)
    sum_start(2, hidden, lambda left: dot(left, w_down[...]))
    drain(weight_sends)
    grad_near(0)

    dk_acc[...] = jnp.zeros_like(dk_acc)
    dv_acc[...] = jnp.zeros_like(dv_acc)

    def output_grad():
        def body(i, carry):
            grad = dot(mixed_low_t[...], dmid[:, rows(i, 2 * block)]).astype(bf16).T
            for k in range(2):
                for t in range(planes):
                    start = k * block + t * per
                    stage_out[t, 2 * i + k] = grad[start:start + per]
            return carry

        lax.fori_loop(0, n // 2, body, 0)
        grad_send(3)

    def attend_back(slot, q_sum):
        gather_step(dmid, 3, slot)
        place = chip(slot)
        at = rows(place, 2 * block)
        d_mix = dot_nt(w_out[...], dmid[at])
        pl.when(slot == 3)(output_grad)
        d_mix_t = jnp.concatenate([d_mix[h * head:(h + 1) * head] for h in range(group)], 1)
        d_mix_t = (d_mix_t.astype(bf16).astype(f32) * sums[place]).astype(bf16)
        delta = jnp.sum(d_mix_t.astype(f32) * mixed_t[place], 0, keepdims=True)
        weight = probs[place]
        d_prob = dot(values[...], d_mix_t)
        d_score = (weight.astype(f32) * (d_prob - delta)).astype(bf16)
        d_query = dot(keys_t[...], d_score) * scale
        for h in range(group):
            grad = turn_back(d_query[:, 2 * h * block:2 * (h + 1) * block].T, at)
            part, gain_part = norm_back(raw[at, h * head:(h + 1) * head], qg_ref[...], grad)
            d_qkv[at, h * head:(h + 1) * head] = part.astype(bf16)
            q_sum = q_sum + gain_part
        pl.when(slot == 2)(lambda: grad_near(1))
        dv_acc[...] += dot(weight, d_mix_t.T)
        dk_acc[...] += dot(d_score, stack(queries, at))
        return q_sum

    zero = jnp.zeros((1, head), f32)
    gain_own[2:3, 0:head] = lax.fori_loop(0, n // 2, attend_back, zero)
    gather_sent(dmid, 3)
    weight_grad(4, [(first_t, lambda: d_qkv[:, :qw])])
    grad_far(0)

    def project_back(i, k_sum):
        at = rows(i, 2 * block)
        grad = turn_back(dk_acc[at] * (1.0 / log2e), at)
        part, gain_part = norm_back(raw[at, qw:qw + kw], kg_ref[...], grad)
        d_qkv[at, qw:qw + kw] = part.astype(bf16)
        d_qkv[at, qw + kw:] = dv_acc[at].astype(bf16)
        return k_sum + gain_part

    gain_own[3:4, 0:head] = lax.fori_loop(0, n // 2, project_back, zero)

    weight_grad(5, [(first_t, lambda: d_qkv[:, qw:])])
    grad_far(1)
    grad_near(2)
    own_sum(0)
    drain(in_plane)
    sum_start(3, d_qkv, lambda left: dot_nt(left, w_qkv[...]))
    grad_far(2)
    grad_near(3)
    own_sum(1)
    hand_out(0)
    grad_far(3)
    grad_near(4)
    out_ref[...] = (middle[...] + sum_finish(2)).astype(bf16)
    grad_far(4)
    grad_near_far(5)
    own_sum(2)
    grad_near_inner(5)
    grad_far(5)
    x_part, gain_own[0:1, :] = norm_back(x_ref[...].astype(f32), ag_ref[...], sum_finish(3))
    dx_ref[...] = d_middle[...] + x_part

    def gain_plane_copy(j):
        return remote(gain_own, gain_plane.at[c], gp_send.at[j], gp_recv.at[j], partner(j), z)

    def gain_copy(d):
        return remote(gain_all.at[z], gain_all.at[z], gz_send.at[d], gz_recv.at[d], c, lax.rem(z + d, planes))

    for j in range(1, n):
        launch(in_plane, lambda j=j: gain_plane_copy(j))
    gain_plane[c] = gain_own[...]
    own_sum(3)
    hand_out(1)
    for j in range(1, n):
        gain_plane_copy(j).wait_recv()
    total = gain_plane[0]
    for i in range(1, n):
        total = total + gain_plane[i]
    gain_all[z] = total
    for d in range(1, planes):
        launch(along, lambda d=d: gain_copy(d))
    own_sum(4)
    for d in range(1, planes):
        origin = gain_all.at[lax.rem(z + planes - d, planes)]
        remote(origin, origin, gz_send.at[d], gz_recv.at[d], c, z).wait_recv()
    total = gain_all[0]
    for i in range(1, planes):
        total = total + gain_all[i]
    gains_ref[...] = total

    hand_receive(0)
    own_sum(5)
    hand_out(2)
    drain(along)
    hand_receive(1)
    hand_receive(2)
    drain(in_plane)


def finish_kernel(
    n, head, out_in, dx_in, gains_in, got_ab, got_co, got_qkv,
    out_ref, dx_ref, ag_ref, q_ref, k_ref, v_ref, qg_ref, kg_ref, o_ref, fg_ref, g_ref, u_ref, d_ref,
):
    out_ref[...] = out_in[...]
    dx_ref[...] = dx_in[...]
    ag_ref[...] = gains_in[0:1, :]
    fg_ref[...] = gains_in[1:2, :]
    qg_ref[...] = gains_in[2:3, 0:head]
    kg_ref[...] = gains_in[3:4, 0:head]
    qw, kw = q_ref.shape[1] // n, k_ref.shape[1] // n
    fw = g_ref.shape[1] // n
    pw = fw // 3
    thirds = ((got_ab, 0), (got_ab, fw), (got_co, 0))
    for i in range(n):
        q_ref[:, i * qw:(i + 1) * qw] = got_qkv[i, :, 0:qw].astype(f32)
        k_ref[:, i * kw:(i + 1) * kw] = got_qkv[i, :, qw:qw + kw].astype(f32)
        v_ref[:, i * kw:(i + 1) * kw] = got_qkv[i, :, qw + kw:].astype(f32)
        o_ref[:, i * qw:(i + 1) * qw] = got_co[i, :, fw:].astype(f32)
        for t, (got, start) in enumerate(thirds):
            plane, unit = hidden_block(i, t)
            at = plane * (g_ref.shape[1] // 4) + unit * pw
            g_ref[:, at:at + pw] = got[i, :, start:start + pw].astype(f32)
            u_ref[:, at:at + pw] = got[i, :, start + pw:start + 2 * pw].astype(f32)
            d_ref[:, at:at + pw] = got[i, :, start + 2 * pw:start + 3 * pw].astype(f32)


def plane_device(
    layer_input,
    token_positions,
    attention_gain,
    query_weight,
    key_matrix,
    value_matrix,
    query_gain,
    key_norm_gain,
    output_weight,
    feedforward_gain,
    gate_weight,
    up_weight,
    down_weight,
    out_cotangent,
):
    n = lax.axis_size("ctx")
    planes = lax.axis_size("fsdp")
    block, width = layer_input.shape[1:]
    length = token_positions.shape[1]
    head = query_gain.shape[0]
    qw = query_weight.shape[1] // n
    kw = key_matrix.shape[1] // n
    fw = gate_weight.shape[1] // n
    group = qw // head
    per = block // planes
    half = head // 2
    inverse = np.power(rope_base, -np.arange(half) * 2.0 / head).astype(np.float32)
    inverse = np.concatenate([inverse, inverse])[None]
    steps = np.arange(block // 2)[:, None] * inverse.astype(np.float64)
    step_cos, step_sin = (jnp.asarray(f(steps).astype(np.float32)) for f in (np.cos, np.sin))
    inverse = jnp.asarray(inverse)
    vmem = pl.BlockSpec(memory_space=pltpu.VMEM)
    hbm = pl.BlockSpec(memory_space=pl.ANY)
    dma = pltpu.SemaphoreType.DMA
    sizes = (fw, fw, fw, qw, qw, 2 * kw)
    low = lambda *shape: pltpu.VMEM(shape, bf16)
    wide = lambda *shape: pltpu.VMEM(shape, f32)
    scratch = [
        low(width, qw + 2 * kw), low(width, 2 * fw), low(qw, width), low(fw, width),
        low(planes * (output_weight.shape[0] // n), width),
        low(length, width), low(length, width), low(length, width),
        low(width, length), low(width, length), low(width, length),
        wide(length, head), wide(length, head), wide(length, head),
        wide(length, qw + kw), low(length, qw), low(length, kw), low(length, kw),
        low(kw, length), low(kw, length), low(n // 2, length, 2 * group * block), wide(n // 2, 1, 2 * group * block),
        wide(n // 2, head, 2 * group * block), low(length, qw), low(qw, length),
        low(length, fw), low(length, 2 * fw), low(length, qw + 2 * kw),
        wide(length, kw), wide(length, kw),
    ]
    scratch += [low(planes, n, per, size) for size in sizes]
    scratch += [low(planes + 1, n, per, size) for size in sizes]
    scratch += [low(n, per, sizes[m] + sizes[m + 1]) for m in (0, 2, 4)]
    scratch += [low(2, 4, block, width)] * 2 + [low(2, 3, block, width)] * 2 + [wide(2, block, width), wide(2, block, width)]
    scratch += [
        wide(block, width), wide(block, width), wide(8, width), wide(n, 8, width), wide(planes, 8, width),
        dma((13,)), dma((8, 6)), dma((8, planes)), dma((1, 7)), dma((1, 4)),
        dma((4, n)), dma((4, n)), dma((4, 4)), dma((4, 4)), dma((4, 4)), dma((4, 4)),
        dma((6, planes)), dma((6, planes + 1)), dma((3, n)), dma((3, n)), dma((n,)), dma((n,)),
        dma((planes,)), dma((planes,)),
    ]
    shapes = [
        jax.ShapeDtypeStruct((block, width), bf16),
        jax.ShapeDtypeStruct((block, width), f32),
        jax.ShapeDtypeStruct((8, width), f32),
    ] + [jax.ShapeDtypeStruct((n, per, sizes[m] + sizes[m + 1]), bf16) for m in (0, 2, 4)]
    results = pl.pallas_call(
        functools.partial(layer_kernel, n, planes, block, head, group, fw),
        out_shape=shapes,
        in_specs=[vmem] * 10 + [hbm] * 7,
        out_specs=[vmem] * len(shapes),
        scratch_shapes=scratch,
        compiler_params=pltpu.CompilerParams(
            collective_id=0, has_side_effects=True, vmem_limit_bytes=60 * 1024 * 1024),
    )(
        layer_input[0], out_cotangent[0], token_positions, inverse, step_cos, step_sin,
        attention_gain[None], feedforward_gain[None], query_gain[None], key_norm_gain[None],
        query_weight, key_matrix, value_matrix, output_weight, gate_weight, up_weight, down_weight,
    )
    plain = lambda rows, columns, kind=f32: jax.ShapeDtypeStruct((rows, columns), kind)
    finals = [
        plain(block, width, bf16), plain(block, width), plain(1, width),
        plain(per, n * qw), plain(per, n * kw), plain(per, n * kw), plain(1, head), plain(1, head),
        plain(per, n * qw), plain(1, width), plain(per, n * fw), plain(per, n * fw), plain(per, n * fw),
    ]
    done = pl.pallas_call(
        functools.partial(finish_kernel, n, head),
        out_shape=finals,
        in_specs=[vmem] * len(shapes),
        out_specs=[vmem] * len(finals),
    )(*results)
    out, dx, ag, q, k, v, qg, kg, o, fg, g, u, d = done
    return out[None], dx[None], ag[0], q, k, v, qg[0], kg[0], o.T, fg[0], g, u, d.T


def solution(mesh):
    in_specs = (
        P("fsdp", "ctx", None),
        P("fsdp", None),
        P(),
        P("fsdp", None),
        P("fsdp", None),
        P("fsdp", None),
        P(),
        P(),
        P("fsdp", None),
        P(),
        P("fsdp", None),
        P("fsdp", None),
        P("fsdp", None),
        P("fsdp", "ctx", None),
    )
    out_specs = (
        P("fsdp", "ctx", None),
        P("fsdp", "ctx", None),
        P(),
        P(("ctx", "fsdp"), None),
        P(("ctx", "fsdp"), None),
        P(("ctx", "fsdp"), None),
        P(),
        P(),
        P(None, ("ctx", "fsdp")),
        P(),
        P(("ctx", "fsdp"), None),
        P(("ctx", "fsdp"), None),
        P(None, ("ctx", "fsdp")),
    )

    def run(*arguments):
        n, planes = mesh.shape["ctx"], mesh.shape["fsdp"]
        key_heads = arguments[4].shape[1] // arguments[6].shape[0]
        whole_heads = n == 8 and planes == 4 and key_heads == n
        return jax.shard_map(
            plane_device if whole_heads else on_device,
            mesh=mesh, in_specs=in_specs, out_specs=out_specs, check_vma=False,
        )(*arguments)

    return run
```

```python
import functools

import jax
import jax.numpy as jnp
import numpy as np
from jax import lax
from jax.experimental import pallas as pl
from jax.experimental.pallas import tpu as pltpu
from jax.sharding import PartitionSpec as P

epsilon = 1e-06
rope_base = 1000000.0
masked_score = -1e30


def from_behind(block, axis, distance):
    devices = range(lax.axis_size(axis))
    route = [((i - distance) % len(devices), i) for i in devices]
    return lax.ppermute(block, axis, route)


def rotate(value_rows):
    half = value_rows.shape[-1] // 2
    return jnp.concatenate([-value_rows[..., half:], value_rows[..., :half]], -1)


def rotate_back(value_rows):
    half = value_rows.shape[-1] // 2
    return jnp.concatenate([value_rows[..., half:], -value_rows[..., :half]], -1)


def rope_tables(token_offsets, head_size):
    half = head_size // 2
    inverse = rope_base ** (-(jnp.arange(half).astype(jnp.float32) * 2.0) / head_size)
    angles = token_offsets.astype(jnp.float32)[:, None] * inverse[None, :]
    cosine = jnp.cos(angles)
    sine = jnp.sin(angles)
    return (jnp.concatenate([cosine, cosine], -1), jnp.concatenate([sine, sine], -1))


def norm_scale(value_rows):
    return lax.rsqrt(jnp.mean(value_rows * value_rows, -1, keepdims=True) + epsilon)


def norm_back(value_rows, scale, gain, grad):
    weighted = grad * gain
    inner = jnp.mean(weighted * value_rows, -1, keepdims=True)
    result = scale * weighted - value_rows * scale * scale * scale * inner
    gain_part = jnp.sum((grad * value_rows * scale).reshape(-1, gain.shape[0]), 0)
    return (result, gain_part)


def row_products(left, pieces):
    return tuple((jnp.dot(left, piece, preferred_element_type=jnp.float32) for piece in pieces))


def column_products(rights, pieces):
    total = jnp.einsum("tc,rc->tr", rights[0], pieces[0], preferred_element_type=jnp.float32)
    for right, piece in zip(rights[1:], pieces[1:]):
        total = total + jnp.einsum("tc,rc->tr", right, piece, preferred_element_type=jnp.float32)
    return total


def on_device(
    layer_input,
    token_positions,
    attention_gain,
    query_weight,
    key_matrix,
    value_matrix,
    query_gain,
    key_norm_gain,
    output_weight,
    feedforward_gain,
    gate_weight,
    up_weight,
    down_weight,
    out_cotangent,
):
    hidden_in = layer_input[0].astype(jnp.float32)
    count = hidden_in.shape[0]
    head_size = query_gain.shape[0]
    query_width = query_weight.shape[1]
    key_width = key_matrix.shape[1]
    inner_width = gate_weight.shape[1]
    heads = query_width // head_size
    key_heads = key_width // head_size
    group = heads // key_heads
    scale = head_size ** (-0.5)
    cycles = lax.axis_size("ctx")
    own_index = lax.axis_index("ctx")
    sequence_pos = token_positions[0]
    token_offsets = lax.dynamic_slice_in_dim(sequence_pos, own_index * count, count)
    cosine, sine = rope_tables(token_offsets, head_size)
    cosine = cosine[:, None, :]
    sine = sine[:, None, :]
    first_scale = norm_scale(hidden_in)
    first = (hidden_in * first_scale * attention_gain).astype(jnp.bfloat16)
    query_raw, key_unnormed, value_unnormed = row_products(
        first,
        (
            lax.all_gather(query_weight, "fsdp", axis=0, tiled=True),
            lax.all_gather(key_matrix, "fsdp", axis=0, tiled=True),
            lax.all_gather(value_matrix, "fsdp", axis=0, tiled=True),
        ),
    )
    query_heads = query_raw.reshape(count, heads, head_size)
    query_scale = norm_scale(query_heads)
    query_normed = query_heads * query_scale * query_gain
    query_rot = query_normed * cosine + rotate(query_normed) * sine
    query_grouped = (
        query_rot.reshape(count, key_heads, group, head_size)
        .transpose(1, 2, 0, 3)
        .astype(jnp.bfloat16)
    )
    key_heads_raw = key_unnormed.reshape(count, key_heads, head_size)
    key_scale = norm_scale(key_heads_raw)
    key_normed = key_heads_raw * key_scale * key_norm_gain
    key_low = (
        (key_normed * cosine + rotate(key_normed) * sine)
        .reshape(count, key_width)
        .astype(jnp.bfloat16)
    )
    value_low = value_unnormed.astype(jnp.bfloat16)
    rowmax = jnp.full((key_heads, group, count), masked_score, jnp.float32)
    keys_piece = lax.all_gather(key_low, "ctx", axis=0, tiled=True).reshape(
        -1, key_heads, head_size
    )
    values_piece = lax.all_gather(value_low, "ctx", axis=0, tiled=True).reshape(
        -1, key_heads, head_size
    )
    key_pos = sequence_pos
    allowed = token_offsets[:, None] >= key_pos[None, :]
    scores = (
        jnp.einsum("kgtd,skd->kgts", query_grouped, keys_piece, preferred_element_type=jnp.float32)
        * scale
    )
    scores = jnp.where(allowed, scores, masked_score)
    newmax = jnp.maximum(rowmax, jnp.max(scores, -1))
    weights = jnp.where(allowed, jnp.exp(scores - newmax[..., None]), 0.0)
    accum = jnp.einsum(
        "kgts,skd->kgtd",
        weights.astype(jnp.bfloat16),
        values_piece,
        preferred_element_type=jnp.float32,
    )
    rowsum = jnp.sum(weights, -1)
    accum, rowmax, rowsum = (accum, newmax, rowsum)
    normalized = accum / rowsum[..., None]
    logsum = rowmax + jnp.log(rowsum)
    attention_low = (
        normalized.transpose(2, 0, 1, 3).reshape(count, query_width).astype(jnp.bfloat16)
    )
    output_whole = lax.all_gather(output_weight, "fsdp", axis=0, tiled=True)
    branch_out = jnp.dot(attention_low, output_whole, preferred_element_type=jnp.float32)
    middle = hidden_in + branch_out
    second_scale = norm_scale(middle)
    second = (middle * second_scale * feedforward_gain).astype(jnp.bfloat16)
    gate, up = row_products(
        second,
        (
            lax.all_gather(gate_weight, "fsdp", axis=0, tiled=True),
            lax.all_gather(up_weight, "fsdp", axis=0, tiled=True),
        ),
    )
    sigmoid_gate = jax.nn.sigmoid(gate)
    silu_gate = gate * sigmoid_gate
    hidden_low = (silu_gate * up).astype(jnp.bfloat16)
    (down_out,) = row_products(
        hidden_low, (lax.all_gather(down_weight, "fsdp", axis=0, tiled=True),)
    )
    layer_output = (middle + down_out).astype(jnp.bfloat16)[None]
    cotangent = out_cotangent[0]
    hidden_grad = column_products(
        (cotangent,), lax.all_gather((down_weight,), "fsdp", axis=0, tiled=True)
    )
    up_low = (hidden_grad * silu_gate).astype(jnp.bfloat16)
    gate_low = (hidden_grad * up * sigmoid_gate * (1.0 + gate * (1.0 - sigmoid_gate))).astype(
        jnp.bfloat16
    )
    second_grad = column_products(
        (gate_low, up_low), lax.all_gather((gate_weight, up_weight), "fsdp", axis=0, tiled=True)
    )
    middle_part, feedforward_part = norm_back(middle, second_scale, feedforward_gain, second_grad)
    middle_grad = cotangent.astype(jnp.float32) + middle_part
    middle_low = middle_grad.astype(jnp.bfloat16)
    attention_grad = jnp.einsum(
        "tc,rc->tr", middle_low, output_whole, preferred_element_type=jnp.float32
    )
    attention_grad_low = attention_grad.astype(jnp.bfloat16)
    mixed_grad = attention_grad_low.reshape(count, key_heads, group, head_size).transpose(
        1, 2, 0, 3
    )
    delta = jnp.sum(mixed_grad.astype(jnp.float32) * normalized, -1)

    def cycle_step(index, carry):
        keys_held, values_held, key_acc, value_acc, query_acc = carry
        anchor = (own_index - index) % cycles
        key_pos = lax.dynamic_slice_in_dim(sequence_pos, anchor * count, count)
        keys_piece = keys_held.astype(jnp.bfloat16).reshape(count, key_heads, head_size)
        values_piece = values_held.astype(jnp.bfloat16).reshape(count, key_heads, head_size)
        allowed = token_offsets[:, None] >= key_pos[None, :]
        scores = (
            jnp.einsum(
                "kgtd,skd->kgts", query_grouped, keys_piece, preferred_element_type=jnp.float32
            )
            * scale
        )
        probs = jnp.where(allowed, jnp.exp(scores - logsum[..., None]), 0.0)
        value_acc = value_acc + jnp.einsum(
            "kgts,kgtd->skd",
            probs.astype(jnp.bfloat16),
            mixed_grad,
            preferred_element_type=jnp.float32,
        ).reshape(count, key_width)
        prob_grad = jnp.einsum(
            "kgtd,skd->kgts", mixed_grad, values_piece, preferred_element_type=jnp.float32
        )
        score_grad = (probs * (prob_grad - delta[..., None])).astype(jnp.bfloat16)
        query_acc = (
            query_acc
            + jnp.einsum(
                "kgts,skd->kgtd", score_grad, keys_piece, preferred_element_type=jnp.float32
            )
            * scale
        )
        key_acc = (
            key_acc
            + jnp.einsum(
                "kgts,kgtd->skd", score_grad, query_grouped, preferred_element_type=jnp.float32
            ).reshape(count, key_width)
            * scale
        )
        moved = (
            from_behind(keys_held.astype(jnp.bfloat16), "ctx", 1).astype(keys_held.dtype),
            from_behind(values_held.astype(jnp.bfloat16), "ctx", 1).astype(values_held.dtype),
            from_behind(key_acc.astype(jnp.bfloat16), "ctx", 1).astype(key_acc.dtype),
            from_behind(value_acc.astype(jnp.bfloat16), "ctx", 1).astype(value_acc.dtype),
        )
        return (moved[0], moved[1], moved[2], moved[3], query_acc)

    start_cycle = (
        key_low.astype(jnp.float32),
        value_low.astype(jnp.float32),
        jnp.zeros((count, key_width), jnp.float32),
        jnp.zeros((count, key_width), jnp.float32),
        jnp.zeros((key_heads, group, count, head_size), jnp.float32),
    )
    cycle_done = lax.fori_loop(0, cycles, cycle_step, start_cycle)
    key_acc = cycle_done[2]
    value_acc = cycle_done[3]
    query_acc = cycle_done[4]
    query_rot_grad = query_acc.transpose(2, 0, 1, 3).reshape(count, heads, head_size)
    query_normed_grad = query_rot_grad * cosine + rotate_back(query_rot_grad * sine)
    query_heads_grad, query_part = norm_back(
        query_heads, query_scale, query_gain, query_normed_grad
    )
    query_low_grad = query_heads_grad.reshape(count, query_width).astype(jnp.bfloat16)
    key_rot_grad = key_acc.reshape(count, key_heads, head_size)
    key_normed_grad = key_rot_grad * cosine + rotate_back(key_rot_grad * sine)
    key_heads_grad, key_part = norm_back(key_heads_raw, key_scale, key_norm_gain, key_normed_grad)
    key_low_grad = key_heads_grad.reshape(count, key_width).astype(jnp.bfloat16)
    value_low_grad = value_acc.astype(jnp.bfloat16)
    first_grad = column_products(
        (query_low_grad, key_low_grad, value_low_grad),
        lax.all_gather((query_weight, key_matrix, value_matrix), "fsdp", axis=0, tiled=True),
    )
    input_part, attention_part = norm_back(hidden_in, first_scale, attention_gain, first_grad)
    input_gradient = (middle_grad + input_part)[None]
    rights_first = jnp.concatenate([query_low_grad, key_low_grad, value_low_grad], 1)
    rights_second = jnp.concatenate([gate_low, up_low], 1)
    pairs = (
        (first, rights_first),
        (second, rights_second),
        (middle_low, attention_low),
        (cotangent, hidden_low),
    )
    parts = []
    for left, right in pairs:
        parts.append(jnp.einsum("tr,tc->rc", left, right, preferred_element_type=jnp.float32))
    sums = lax.psum_scatter(
        jnp.concatenate(parts, 1), ("ctx", "fsdp"), scatter_dimension=0, tiled=True
    )
    edges = [0, query_width, query_width + key_width, query_width + 2 * key_width]
    edges = edges + [edges[3] + inner_width, edges[3] + 2 * inner_width]
    edges = edges + [edges[5] + query_width, edges[5] + query_width + inner_width]
    query_gradient = sums[:, edges[0] : edges[1]]
    key_gradient = sums[:, edges[1] : edges[2]]
    value_gradient = sums[:, edges[2] : edges[3]]
    gate_gradient = sums[:, edges[3] : edges[4]]
    up_gradient = sums[:, edges[4] : edges[5]]
    output_gradient = sums[:, edges[5] : edges[6]].T
    down_gradient = sums[:, edges[6] : edges[7]].T
    attention_total, query_total, key_total, feedforward_total = lax.psum(
        (attention_part, query_part, key_part, feedforward_part), ("ctx", "fsdp")
    )
    return (
        layer_output,
        input_gradient,
        attention_total,
        query_gradient,
        key_gradient,
        value_gradient,
        query_total,
        key_total,
        output_gradient,
        feedforward_total,
        gate_gradient,
        up_gradient,
        down_gradient,
    )


MESH = pl.DeviceIdType.MESH
f32 = jnp.float32
bf16 = jnp.bfloat16


def dot(left, right):
    return jnp.dot(left, right, preferred_element_type=f32)


def dot_nt(left, right):
    return lax.dot_general(left, right, (((1,), (1,)), ((), ())), preferred_element_type=f32)


def dot_tn(left, right):
    return lax.dot_general(left, right, (((0,), (0,)), ((), ())), preferred_element_type=f32)


def hidden_block(device, third):
    def plane(i, t):
        return ((3, 1, 2), (0, 2, 1), (0, 3, 2), (3, 0, 1))[i // 4 * 2 + i % 2][t]

    own = plane(device, third)
    return own, sum(plane(i, t) == own for i in range(device) for t in range(3))


def layer_kernel(
    n, planes, block, head, group, fw,
    x_ref, dy_ref, pos_row, inverse_ref, step_cos, step_sin, ag_ref, fg_ref, qg_ref, kg_ref,
    wq, wk, wv, wo, wg, wu, wd,
    out_ref, dx_ref, gains_ref, got_ab, got_co, got_qkv,
    w_qkv, w_gu, w_out, w_down, t_out,
    first, dy_all, second, first_t, dy_t, second_t,
    positions, cosine, sine,
    raw, queries, keys, values, keys_t, values_t, probs, sums, mixed_t, mixed_low, mixed_low_t,
    hidden, d_gu, d_qkv, dk_acc, dv_acc,
    stage_a, stage_b, stage_c, stage_out, stage_q, stage_kv,
    land_a, land_b, land_c, land_out, land_q, land_kv,
    own_ab, own_co, own_qkv,
    rs_sa, rs_ra, rs_sb, rs_rb, rs_kept, rs_acc,
    middle, d_middle, gain_own, gain_plane, gain_all,
    local_sem, wz_send, wz_recv, hand_send, hand_recv,
    ag_send, ag_recv, ra_send, ra_recv, rb_send, rb_recv,
    zr_send, zr_recv, aa_send, aa_recv, gp_send, gp_recv, gz_send, gz_recv,
):
    c = lax.axis_index("ctx")
    z = lax.axis_index("fsdp")
    dmid = first
    cy, cx, ck = lax.div(c, 4), lax.rem(lax.div(c, 2), 2), lax.rem(c, 2)
    ci = lax.rem(c, 4)
    sign = 1 - 2 * ck
    qw, kw = group * head, head
    pw = 128
    thirds = fw // pw
    width = x_ref.shape[1]
    scale = head ** (-0.5)
    log2e = 1.4426950408889634
    gots = (got_ab, got_co, got_qkv)
    owns = (own_ab, own_co, own_qkv)
    stages = (stage_a, stage_b, stage_c, stage_out, stage_q, stage_kv)
    lands = (land_a, land_b, land_c, land_out, land_q, land_kv)

    def partner(j):
        y = lax.rem(cy + lax.div(j, 4), 2)
        x = lax.rem(cx + lax.rem(lax.div(j, 2), 2), 2)
        k = lax.rem(ck + lax.rem(j, 2), 2)
        return y * 4 + x * 2 + k

    def chip(slot):
        return lax.rem(cy + lax.div(slot, 2), 2) * 2 + lax.rem(cx + lax.rem(slot, 2), 2)

    def rows(start, size):
        return pl.ds(pl.multiple_of(start * size, size), size)

    def remote(src, dst, send, recv, ctx, plane):
        return pltpu.make_async_remote_copy(
            src_ref=src, dst_ref=dst, send_sem=send, recv_sem=recv,
            device_id={"ctx": ctx, "fsdp": plane}, device_id_type=MESH,
        )

    in_plane, along, weight_sends = [], [], []

    def launch(started, copy, when=None):
        if when is None:
            copy().start()
        else:
            pl.when(when)(lambda: copy().start())
        started.append((copy, when))

    def drain(started):
        for copy, when in started:
            if when is None:
                copy().wait_send()
            else:
                pl.when(when)(lambda copy=copy: copy().wait_send())
        started.clear()

    def pick(values):
        return sum(jnp.where(c == i, value, 0) for i, value in enumerate(values))

    unit_plane = [pick([hidden_block(i, t)[0] for i in range(n)]) for t in range(thirds)]
    unit_block = [pick([hidden_block(i, t)[1] for i in range(n)]) for t in range(thirds)]
    plane_blocks = wd.shape[0] // pw

    own_rows = wq.shape[0]
    out_rows = wo.shape[0] // n

    def own_slices():
        mine = rows(z, own_rows)
        pairs = [
            (wq.at[:, rows(c, qw)], w_qkv.at[mine, 0:qw]),
            (wk.at[:, rows(c, kw)], w_qkv.at[mine, qw:qw + kw]),
            (wv.at[:, rows(c, kw)], w_qkv.at[mine, qw + kw:qw + 2 * kw]),
            (wo.at[rows(c, out_rows)], t_out.at[rows(z, out_rows)]),
        ]
        for t in range(thirds):
            at = 2 * pw * t
            unit = unit_plane[t] * plane_blocks + unit_block[t]
            pairs.append((wg.at[:, rows(unit, pw)], w_gu.at[mine, at:at + pw]))
            pairs.append((wu.at[:, rows(unit, pw)], w_gu.at[mine, at + pw:at + 2 * pw]))
        return pairs

    local = [pltpu.make_async_copy(src, dst, local_sem.at[i]) for i, (src, dst) in enumerate(own_slices())]
    for copy in local:
        copy.start()

    def own_down(t):
        return pltpu.make_async_copy(
            wd.at[rows(unit_block[t], pw)], w_down.at[t * pw:(t + 1) * pw], local_sem.at[4 + 2 * thirds + t])

    holds = [unit_plane[t] == z for t in range(thirds)]
    for t in range(thirds):
        pl.when(holds[t])(lambda t=t: own_down(t).start())

    for land in lands:
        @pl.when(z == 0)
        def _(land=land):
            land[0] = jnp.zeros(land.shape[1:], bf16)

        @pl.when(z == planes - 1)
        def _(land=land):
            land[planes] = jnp.zeros(land.shape[1:], bf16)

    barrier = pltpu.get_barrier_semaphore()
    for j in range(1, n):
        pl.semaphore_signal(barrier, inc=1, device_id={"ctx": partner(j), "fsdp": z}, device_id_type=MESH)
    for d in range(1, planes):
        pl.semaphore_signal(
            barrier, inc=1, device_id={"ctx": c, "fsdp": lax.rem(z + d, planes)}, device_id_type=MESH)
    x = x_ref[...].astype(f32)
    x_scale = lax.rsqrt(jnp.mean(x * x, -1, keepdims=True) + epsilon)
    first[rows(c, block)] = (x * x_scale * ag_ref[...]).astype(bf16)
    dy_all[rows(c, block)] = dy_ref[...]
    for copy in local[:3]:
        copy.wait()
    pl.semaphore_wait(barrier, n + planes - 2)

    def inside(t):
        return jnp.logical_and(t >= 0, t < planes)

    weights = [
        (lambda o: w_qkv.at[rows(o, own_rows)], None),
        (lambda o: t_out.at[rows(o, out_rows)], 0),
    ]
    for t in range(thirds):
        weights.append((lambda o, t=t: w_gu.at[rows(o, own_rows), 2 * pw * t:2 * pw * (t + 1)], None))
        weights.append((lambda o, t=t: w_down.at[t * pw:(t + 1) * pw], None))

    def weight_copy(w, slot, origin, target):
        part = weights[w][0](origin)
        return remote(part, part, wz_send.at[w, slot], wz_recv.at[w, origin], c, target)

    def from_plane(w, origin):
        return origin == unit_plane[(w - 3) // 2] if w >= 3 and w % 2 else None

    def both(one, other):
        return one if other is None else jnp.logical_and(one, other)

    def hand_split(origin, valid):
        mine = 2 * origin + cy == c
        return jnp.logical_and(valid, jnp.logical_not(mine)), jnp.logical_and(valid, mine)

    def weight_start(w):
        for side in range(2):
            launch(
                weight_sends, lambda side=side: weight_copy(w, side, z, z + sign * (1 - 2 * side)), starts[w, side])
        if weights[w][1] is not None:
            hand_over(w, z, 0, *hand_split(z, True))

    def hand_target(h):
        return lambda i: w_out.at[rows(i, out_rows)]

    def hand_copy(w, origin, slot):
        h = weights[w][1]
        return remote(
            weights[w][0](origin), hand_target(h)(ci), hand_send.at[h, slot], hand_recv.at[h, ci], 2 * origin + cy, z)

    def hand_over(w, origin, slot, away, here):
        launch(in_plane, lambda: hand_copy(w, origin, slot), away)

        @pl.when(here)
        def _():
            hand_target(weights[w][1])(ci)[...] = weights[w][0](origin)[...]

    def hand_arrive(w):
        h = weights[w][1]
        for i in range(4):
            @pl.when(4 * ck + i != c)
            def _(i=i):
                part = hand_target(h)(i)
                remote(part, part, hand_send.at[h, 0], hand_recv.at[h, i], c, z).wait_recv()

    hops, starts = {}, {}
    for w in range(len(weights)):
        for side in range(2):
            starts[w, side] = both(inside(z + sign * (1 - 2 * side)), from_plane(w, z))
        for d in range(1, planes):
            for side, way in enumerate((1, -1)):
                origin = z - way * d
                valid = both(inside(origin), from_plane(w, origin))
                passed = jnp.logical_and(valid, inside(z + way))
                split = None if weights[w][1] is None else hand_split(origin, valid)
                hops[w, d, side] = origin, z + way, valid, passed, split

    def weight_hop(w, d):
        for side in range(2):
            origin, following, valid, passed, split = hops[w, d, side]
            pl.when(valid)(lambda: weight_copy(w, 0, origin, z).wait_recv())
            if d < planes - 1:
                launch(
                    weight_sends,
                    lambda side=side, origin=origin, following=following: weight_copy(
                        w, 2 * d + side, origin, following),
                    passed)
            if split is not None:
                hand_over(w, origin, 2 * d - 1 + side, *split)

    def gather_copy(buf, g, j, send, origin, target):
        part = buf.at[rows(origin, block)]
        return remote(part, part, ag_send.at[g, send], ag_recv.at[g, j], target, z)

    def gather_start(buf, g):
        for j in (1, 2 + 2 * ck, 4 - 2 * ck):
            launch(in_plane, lambda j=j: gather_copy(buf, g, j, j, c, partner(j)))

    def gather_half(buf, g, j):
        half = block // 2
        part = buf.at[pl.ds(pl.multiple_of(partner(j) * block + (half if j == 2 else 0), half), half)]
        at = 0 if j == 2 else 6
        return remote(part, part, ag_send.at[g, at], ag_recv.at[g, at], partner(6 - j), z)

    def gather_diagonal(buf, g):
        half = block // 2
        for at in (6, 0):
            part = buf.at[pl.ds(pl.multiple_of(partner(6) * block + (0 if at == 6 else half), half), half)]
            remote(part, part, ag_send.at[g, at], ag_recv.at[g, at], c, z).wait_recv()

    def gather_forward(buf, g, j):
        return gather_copy(buf, g, j + 1, j + 1, partner(j), partner(1))

    def gather_take(buf, g, j):
        if j == 6:
            gather_diagonal(buf, g)
        else:
            gather_copy(buf, g, j, j, partner(j), c).wait_recv()
            gather_half(buf, g, j).start()
        gather_forward(buf, g, j).start()

    def gather_sent(buf, g):
        for j in (2, 4, 6):
            in_plane.append((lambda j=j: gather_forward(buf, g, j), None))
            if j < 6:
                in_plane.append((lambda j=j: gather_half(buf, g, j), None))

    def gather_finish(buf, g):
        for j in (2, 4, 6):
            gather_take(buf, g, j)
        gather_sent(buf, g)
        for j in (1, 3, 5, 7):
            gather_copy(buf, g, j, j, partner(j), c).wait_recv()

    def gather_step(buf, g, slot):
        @pl.when(slot == 1)
        def _():
            gather_take(buf, g, 2)
            gather_take(buf, g, 4)

        pl.when(slot == 3)(lambda: gather_take(buf, g, 6))
        gather_copy(buf, g, 2 * slot + 1, 0, partner(2 * slot + 1), c).wait_recv()

    def sum_pair_copy(s, slot):
        return remote(rs_sa.at[s % 2, slot], rs_ra.at[s % 2, slot], ra_send.at[s, slot], ra_recv.at[s, slot], partner(1), z)

    def sum_chip_copy(s, slot):
        return remote(
            rs_sb.at[s % 2, slot - 1], rs_rb.at[s % 2, slot - 1], rb_send.at[s, slot], rb_recv.at[s, slot], partner(2 * slot), z)

    def sum_half_copy(s, slot):
        half = block // 2
        at = pl.ds(pl.multiple_of((slot - 1) * half, half), half)
        return remote(
            rs_sb.at[s % 2, 2, at], rs_rb.at[s % 2, 2, at], rb_send.at[s, 6 - 3 * slot], rb_recv.at[s, 6 - 3 * slot],
            partner(6 - 2 * slot), z)

    def sum_slot(p):
        return jnp.where(p == 0, 3, jnp.where(p == 1, 2 - ck, jnp.where(p == 2, 1 + ck, 0)))

    def sum_start(s, left, partial, prepare=None, ready=None, during=()):
        if prepare is not None:
            for step in prepare:
                step(chip(sum_slot(0)))
        if ready is not None:
            ready()

        def body(p, carry):
            slot = sum_slot(p)
            at = [rows(partner(2 * slot + 1), block), rows(partner(2 * slot), block)]
            both = partial(jnp.concatenate([left[i] for i in at], 0))
            rs_sa[s % 2, slot] = both[:block].astype(bf16)
            sum_pair_copy(s, slot).start()
            rs_kept[lax.rem(p, 2)] = both[block:]

            def pair_sum(q):
                before = sum_slot(q)
                sum_pair_copy(s, before).wait_recv()
                rs_sb[s % 2, before - 1] = (
                    rs_kept[lax.rem(q, 2)] + rs_ra[s % 2, before].astype(f32)).astype(bf16)

            def chip_send(q):
                before = sum_slot(q)
                half = block // 2
                at = pl.ds(pl.multiple_of((before - 1) * half, half), half)
                sum_half_copy(s, before).wait_recv()
                rs_sb[s % 2, before - 1, at] = (
                    rs_sb[s % 2, before - 1, at].astype(f32) + rs_rb[s % 2, 2, at].astype(f32)).astype(bf16)
                sum_chip_copy(s, before).start()

            early = prepare is not None and len(prepare) > 1

            @pl.when(p == 1)
            def _():
                pair_sum(0)
                sum_half_copy(s, 1).start()
                sum_half_copy(s, 2).start()

            @pl.when(p == 2 if early else p > 1)
            def _():
                pair_sum(p - 1)
                chip_send(p - 1)

            if prepare is not None:
                @pl.when(p < 3)
                def _():
                    prepare[0](chip(sum_slot(p + 1)))

            if early:
                @pl.when(p == 2)
                def _():
                    pair_sum(2)
                    chip_send(2)

                @pl.when(p < 3)
                def _():
                    for step in prepare[1:]:
                        step(chip(sum_slot(p + 1)))

            for k, poll in enumerate(during):
                pl.when(p == k)(poll)
            return carry

        lax.fori_loop(0, 4, body, 0)
        for slot in range(4):
            in_plane.append((lambda slot=slot: sum_pair_copy(s, slot), None))
        for slot in (1, 2):
            in_plane.append((lambda slot=slot: sum_half_copy(s, slot), None))
            in_plane.append((lambda slot=slot: sum_chip_copy(s, slot), None))
        sum_pair_copy(s, 0).wait_recv()
        rs_acc[s % 2] = rs_kept[1] + rs_ra[s % 2, 0].astype(f32)

    def sum_finish(s):
        total = rs_acc[s % 2]
        for slot in (1, 2):
            sum_chip_copy(s, slot).wait_recv()
            total = total + rs_rb[s % 2, slot - 1].astype(f32)
        return total

    per = block // planes

    at_edge = jnp.logical_or(z == 0, z == planes - 1)
    edge_targets = [jnp.where(z == 0, planes - 1 - k, k) for k in range(planes - 1)]

    def weight_grad(m, parts):
        def body(i, carry):
            at = 0
            for left, right in parts:
                value = right()
                grad = dot(left[rows(i, 4 * block)], value)
                for k in range(4):
                    for t in range(planes):
                        start = k * block + t * per
                        stages[m][t, 4 * i + k, :, at:at + value.shape[1]] = grad[start:start + per].astype(bf16)
                at += value.shape[1]
            return carry

        lax.fori_loop(0, n // 4, body, 0)
        grad_send(m)

    def grad_send(m):
        for t in edge_targets:
            launch(along, lambda t=t: grad_copy(m, t), at_edge)

    def grad_copy(m, t):
        way = jnp.where(z < t, 1, -1)
        last = z + way == t
        slot = jnp.where(jnp.logical_and(last, way < 0), planes, t)
        return remote(
            stages[m].at[t], lands[m].at[slot], zr_send.at[m, t], zr_recv.at[m, slot], c, z + way)

    def grad_arrive(m, slot):
        part = lands[m].at[slot]
        remote(part, part, zr_send.at[m, 0], zr_recv.at[m, slot], c, z).wait_recv()

    def grad_pass(m, t, valid):
        @pl.when(valid)
        def _():
            grad_arrive(m, t)
            stages[m][t] = stages[m][t] + lands[m][t]

        launch(along, lambda: grad_copy(m, t), valid)

    is_low, is_high = z == 1, z == planes - 2

    def grad_near_far(m):
        grad_pass(m, 3, is_low)
        grad_pass(m, 0, is_high)

    def grad_near_inner(m):
        grad_pass(m, 2, is_low)
        grad_pass(m, 1, is_high)

    def grad_near(m):
        grad_near_far(m)
        grad_near_inner(m)

    def grad_far(m):
        grad_pass(m, 3, is_high)
        grad_pass(m, 0, is_low)

    def owner_copy(g, j):
        return remote(owns[g].at[partner(j)], gots[g].at[c], aa_send.at[g, j], aa_recv.at[g, j], partner(j), z)

    def own_sum(m):
        pl.when(z > 0)(lambda: grad_arrive(m, z))
        pl.when(z < planes - 1)(lambda: grad_arrive(m, planes))
        total = stages[m][z].astype(f32) + lands[m][z].astype(f32) + lands[m][planes].astype(f32)
        first_size = stages[m // 2 * 2].shape[3]
        if m % 2:
            owns[m // 2][:, :, first_size:] = total.astype(bf16)
        else:
            owns[m // 2][:, :, :first_size] = total.astype(bf16)

    def hand_out(g):
        for j in (2 + 2 * ck, 3 + 2 * ck, 4 - 2 * ck, 5 - 2 * ck, 6, 7, 1):
            launch(in_plane, lambda j=j: owner_copy(g, j))
        gots[g][c] = owns[g][c]

    def hand_receive(g):
        for j in range(1, n):
            owner_copy(g, j).wait_recv()

    weight_start(0)
    gather_start(first, 0)
    for copy in local[3:]:
        copy.wait()
    for t in range(thirds):
        pl.when(holds[t])(lambda t=t: own_down(t).wait())

    spread = jnp.broadcast_to(pos_row[...].astype(f32), (head, pos_row.shape[1]))
    positions[...] = spread.T
    side = jnp.where(lax.broadcasted_iota(jnp.int32, (1, head), 1) < head // 2, -1.0, 1.0)

    def table(i, carry):
        run = step_cos.shape[0]
        at = rows(i, run)
        start = positions[pl.ds(pl.multiple_of(i * run, run), 1)] * inverse_ref[...]
        start_cos, start_sin = jnp.cos(start), jnp.sin(start)
        cosine[at] = start_cos * step_cos[...] - start_sin * step_sin[...]
        sine[at] = (start_sin * step_cos[...] + start_cos * step_sin[...]) * side
        return carry

    def turn_over(src, dst):
        def body(i, carry):
            at = rows(i, block)
            dst[:, at] = src[at].T
            return carry

        lax.fori_loop(0, n, body, 0)

    lax.fori_loop(0, 2 * n, table, 0)
    weight_hop(0, 1)
    gather_finish(first, 0)
    weight_hop(0, 2)
    weight_start(1)
    gather_start(dy_all, 1)
    turn_over(first, first_t)
    weight_hop(0, 3)
    weight_start(2)
    weight_start(3)

    def turn(value, at):
        return value * cosine[at] + pltpu.roll(value, head // 2, 1) * sine[at]

    def turn_back(grad, at):
        return grad * cosine[at] - pltpu.roll(grad, head // 2, 1) * sine[at]

    def project(i, carry):
        at = rows(i, 2 * block)
        result = dot(first[at], w_qkv[...])
        raw[at] = result[:, :qw + kw]
        low_values = result[:, qw + kw:].astype(bf16)
        values[at] = low_values
        values_t[:, at] = low_values.T
        for h in range(group + 1):
            part = result[:, h * head:(h + 1) * head]
            inv = lax.rsqrt(jnp.mean(part * part, -1, keepdims=True) + epsilon)
            gain = qg_ref[...] if h < group else kg_ref[...]
            turned = turn(part * inv * gain, at)
            if h < group:
                queries[at, h * head:(h + 1) * head] = (turned * (scale * log2e)).astype(bf16)
            else:
                low_keys = turned.astype(bf16)
                keys[at] = low_keys
                keys_t[:, at] = low_keys.T
        return carry

    lax.fori_loop(0, n // 4, project, 0)
    weight_hop(1, 1)
    lax.fori_loop(n // 4, n // 2, project, 0)
    weight_hop(1, 2)
    gather_finish(dy_all, 1)

    def stack(ref, at):
        return jnp.concatenate([ref[at, h * head:(h + 1) * head] for h in range(group)], 0)

    def attend(place, h):
        at = rows(place, 2 * block)
        columns = slice(h * head, (h + 1) * head)
        tokens = slice(2 * h * block, 2 * (h + 1) * block)
        scores = dot_nt(keys[...], queries[at, columns])
        weight = jnp.concatenate(
            [jnp.exp2(jnp.where(
                positions[...] <= pos_row[:, rows(2 * place + k, block)].astype(f32),
                scores[:, k * block:(k + 1) * block], masked_score)) for k in range(2)], 1)
        inv = 1.0 / jnp.sum(weight, 0, keepdims=True)
        low_weight = weight.astype(bf16)
        probs[place, :, tokens] = low_weight
        sums[place, :, tokens] = inv
        result = dot(values_t[...], low_weight) * inv
        mixed_t[place, :, tokens] = result
        low_result = result.astype(bf16)
        mixed_low_t[columns, at] = low_result
        mixed_low[at, columns] = low_result.T

    def output_ready():
        weight_hop(1, 3)
        weight_start(4)
        weight_start(5)
        hand_arrive(1)
        drain(in_plane)

    def hop_third(t, d):
        weight_hop(2 + 2 * t, d)
        weight_hop(3 + 2 * t, d)

    def last_third():
        hop_third(0, 2)
        weight_start(6)
        weight_start(7)

    sum_start(
        0, mixed_low, lambda left: dot(left, w_out[...]),
        [lambda place, h=h: attend(place, h) for h in range(group)], output_ready,
        (lambda: hop_third(0, 1), last_third, lambda: hop_third(1, 1), lambda: hop_third(1, 2)))
    hop_third(0, 3)
    mid = x_ref[...].astype(f32) + sum_finish(0)
    middle[...] = mid
    mid_scale = lax.rsqrt(jnp.mean(mid * mid, -1, keepdims=True) + epsilon)
    second[rows(c, block)] = (mid * mid_scale * fg_ref[...]).astype(bf16)
    gather_start(second, 2)
    hop_third(2, 1)
    turn_over(dy_all, dy_t)

    def feed(t, at):
        units, pair = slice(t * pw, (t + 1) * pw), 2 * pw * t
        both = dot(second[at], w_gu[:, pair:pair + 2 * pw])
        back = dot_nt(dy_all[at], w_down[units])
        gate, up = both[:, :pw], both[:, pw:]
        sig = 1.0 / (1.0 + jnp.exp(-gate))
        silu = gate * sig
        hidden[at, units] = (silu * up).astype(bf16)
        d_gu[at, pair:pair + pw] = (back * up * sig * (1.0 + gate * (1.0 - sig))).astype(bf16)
        d_gu[at, pair + pw:pair + 2 * pw] = (back * silu).astype(bf16)

    def feed_arriving(slot, carry):
        gather_step(second, 2, slot)
        at = rows(chip(slot), 2 * block)
        feed(0, at)
        second_t[:, at] = second[at].T
        pl.when(slot == 1)(lambda: hop_third(2, 2))
        return carry

    def third_grad(t):
        weight_grad(t, [
            (second_t, lambda: d_gu[:, 2 * pw * t:2 * pw * (t + 1)]),
            (dy_t, lambda: hidden[:, t * pw:(t + 1) * pw]),
        ])

    def feed_third(t):
        def body(i, carry):
            feed(t, rows(i, 2 * block))
            return carry

        lax.fori_loop(0, n // 2, body, 0)

    lax.fori_loop(0, n // 2, feed_arriving, 0)
    gather_sent(second, 2)
    hop_third(1, 3)
    third_grad(0)
    feed_third(1)
    hop_third(2, 3)
    sum_start(
        1, d_gu, lambda left: dot_nt(left, w_gu[...]),
        [lambda place: feed(thirds - 1, rows(place, 2 * block))])
    third_grad(1)
    third_grad(2)
    d_second = sum_finish(1)

    def norm_back(value, gain, grad):
        inv = lax.rsqrt(jnp.mean(value * value, -1, keepdims=True) + epsilon)
        weighted = grad * gain
        inner = jnp.mean(weighted * value, -1, keepdims=True)
        result = inv * weighted - value * (inv * inv * inv * inner)
        return result, jnp.sum(grad * value * inv, 0, keepdims=True)

    gain_own[...] = jnp.zeros_like(gain_own)
    part, gain_own[1:2, :] = norm_back(middle[...], fg_ref[...], d_second)
    d_mid = dy_ref[...].astype(f32) + part
    d_middle[...] = d_mid
    drain(in_plane)
    dmid[rows(c, block)] = d_mid.astype(bf16)
    gather_start(dmid, 3)
    sum_start(2, hidden, lambda left: dot(left, w_down[...]))
    drain(weight_sends)
    grad_near(0)

    dk_acc[...] = jnp.zeros_like(dk_acc)
    dv_acc[...] = jnp.zeros_like(dv_acc)

    def output_grad():
        def body(i, carry):
            grad = dot(mixed_low_t[...], dmid[:, rows(i, 2 * block)]).astype(bf16).T
            for k in range(2):
                for t in range(planes):
                    start = k * block + t * per
                    stage_out[t, 2 * i + k] = grad[start:start + per]
            return carry

        lax.fori_loop(0, n // 2, body, 0)
        grad_send(3)

    def attend_back(slot, q_sum):
        gather_step(dmid, 3, slot)
        place = chip(slot)
        at = rows(place, 2 * block)
        d_mix = dot_nt(w_out[...], dmid[at])
        pl.when(slot == 3)(output_grad)
        d_mix_t = jnp.concatenate([d_mix[h * head:(h + 1) * head] for h in range(group)], 1)
        d_mix_t = (d_mix_t.astype(bf16).astype(f32) * sums[place]).astype(bf16)
        delta = jnp.sum(d_mix_t.astype(f32) * mixed_t[place], 0, keepdims=True)
        weight = probs[place]
        d_prob = dot(values[...], d_mix_t)
        d_score = (weight.astype(f32) * (d_prob - delta)).astype(bf16)
        d_query = dot(keys_t[...], d_score) * scale
        for h in range(group):
            grad = turn_back(d_query[:, 2 * h * block:2 * (h + 1) * block].T, at)
            part, gain_part = norm_back(raw[at, h * head:(h + 1) * head], qg_ref[...], grad)
            d_qkv[at, h * head:(h + 1) * head] = part.astype(bf16)
            q_sum = q_sum + gain_part
        pl.when(slot == 2)(lambda: grad_near(1))
        dv_acc[...] += dot(weight, d_mix_t.T)
        dk_acc[...] += dot(d_score, stack(queries, at))
        return q_sum

    zero = jnp.zeros((1, head), f32)
    gain_own[2:3, 0:head] = lax.fori_loop(0, n // 2, attend_back, zero)
    gather_sent(dmid, 3)
    weight_grad(4, [(first_t, lambda: d_qkv[:, :qw])])
    grad_far(0)

    def project_back(i, k_sum):
        at = rows(i, 2 * block)
        grad = turn_back(dk_acc[at] * (1.0 / log2e), at)
        part, gain_part = norm_back(raw[at, qw:qw + kw], kg_ref[...], grad)
        d_qkv[at, qw:qw + kw] = part.astype(bf16)
        d_qkv[at, qw + kw:] = dv_acc[at].astype(bf16)
        return k_sum + gain_part

    gain_own[3:4, 0:head] = lax.fori_loop(0, n // 2, project_back, zero)

    weight_grad(5, [(first_t, lambda: d_qkv[:, qw:])])
    grad_far(1)
    grad_near(2)
    own_sum(0)
    drain(in_plane)
    sum_start(3, d_qkv, lambda left: dot_nt(left, w_qkv[...]))
    grad_far(2)
    grad_near(3)
    own_sum(1)
    hand_out(0)
    grad_far(3)
    grad_near(4)
    out_ref[...] = (middle[...] + sum_finish(2)).astype(bf16)
    grad_far(4)
    grad_near_far(5)
    own_sum(2)
    grad_near_inner(5)
    grad_far(5)
    x_part, gain_own[0:1, :] = norm_back(x_ref[...].astype(f32), ag_ref[...], sum_finish(3))
    dx_ref[...] = d_middle[...] + x_part

    def gain_plane_copy(j):
        return remote(gain_own, gain_plane.at[c], gp_send.at[j], gp_recv.at[j], partner(j), z)

    def gain_copy(d):
        return remote(gain_all.at[z], gain_all.at[z], gz_send.at[d], gz_recv.at[d], c, lax.rem(z + d, planes))

    for j in range(1, n):
        launch(in_plane, lambda j=j: gain_plane_copy(j))
    gain_plane[c] = gain_own[...]
    own_sum(3)
    hand_out(1)
    for j in range(1, n):
        gain_plane_copy(j).wait_recv()
    total = gain_plane[0]
    for i in range(1, n):
        total = total + gain_plane[i]
    gain_all[z] = total
    for d in range(1, planes):
        launch(along, lambda d=d: gain_copy(d))
    own_sum(4)
    for d in range(1, planes):
        origin = gain_all.at[lax.rem(z + planes - d, planes)]
        remote(origin, origin, gz_send.at[d], gz_recv.at[d], c, z).wait_recv()
    total = gain_all[0]
    for i in range(1, planes):
        total = total + gain_all[i]
    gains_ref[...] = total

    hand_receive(0)
    own_sum(5)
    hand_out(2)
    drain(along)
    hand_receive(1)
    hand_receive(2)
    drain(in_plane)


def finish_kernel(
    n, head, out_in, dx_in, gains_in, got_ab, got_co, got_qkv,
    out_ref, dx_ref, ag_ref, q_ref, k_ref, v_ref, qg_ref, kg_ref, o_ref, fg_ref, g_ref, u_ref, d_ref,
):
    out_ref[...] = out_in[...]
    dx_ref[...] = dx_in[...]
    ag_ref[...] = gains_in[0:1, :]
    fg_ref[...] = gains_in[1:2, :]
    qg_ref[...] = gains_in[2:3, 0:head]
    kg_ref[...] = gains_in[3:4, 0:head]
    qw, kw = q_ref.shape[1] // n, k_ref.shape[1] // n
    fw = g_ref.shape[1] // n
    pw = fw // 3
    thirds = ((got_ab, 0), (got_ab, fw), (got_co, 0))
    for i in range(n):
        q_ref[:, i * qw:(i + 1) * qw] = got_qkv[i, :, 0:qw].astype(f32)
        k_ref[:, i * kw:(i + 1) * kw] = got_qkv[i, :, qw:qw + kw].astype(f32)
        v_ref[:, i * kw:(i + 1) * kw] = got_qkv[i, :, qw + kw:].astype(f32)
        o_ref[:, i * qw:(i + 1) * qw] = got_co[i, :, fw:].astype(f32)
        for t, (got, start) in enumerate(thirds):
            plane, unit = hidden_block(i, t)
            at = plane * (g_ref.shape[1] // 4) + unit * pw
            g_ref[:, at:at + pw] = got[i, :, start:start + pw].astype(f32)
            u_ref[:, at:at + pw] = got[i, :, start + pw:start + 2 * pw].astype(f32)
            d_ref[:, at:at + pw] = got[i, :, start + 2 * pw:start + 3 * pw].astype(f32)


def plane_device(
    layer_input,
    token_positions,
    attention_gain,
    query_weight,
    key_matrix,
    value_matrix,
    query_gain,
    key_norm_gain,
    output_weight,
    feedforward_gain,
    gate_weight,
    up_weight,
    down_weight,
    out_cotangent,
):
    n = lax.axis_size("ctx")
    planes = lax.axis_size("fsdp")
    block, width = layer_input.shape[1:]
    length = token_positions.shape[1]
    head = query_gain.shape[0]
    qw = query_weight.shape[1] // n
    kw = key_matrix.shape[1] // n
    fw = gate_weight.shape[1] // n
    group = qw // head
    per = block // planes
    half = head // 2
    inverse = np.power(rope_base, -np.arange(half) * 2.0 / head).astype(np.float32)
    inverse = np.concatenate([inverse, inverse])[None]
    steps = np.arange(block // 2)[:, None] * inverse.astype(np.float64)
    step_cos, step_sin = (jnp.asarray(f(steps).astype(np.float32)) for f in (np.cos, np.sin))
    inverse = jnp.asarray(inverse)
    vmem = pl.BlockSpec(memory_space=pltpu.VMEM)
    hbm = pl.BlockSpec(memory_space=pl.ANY)
    dma = pltpu.SemaphoreType.DMA
    sizes = (fw, fw, fw, qw, qw, 2 * kw)
    low = lambda *shape: pltpu.VMEM(shape, bf16)
    wide = lambda *shape: pltpu.VMEM(shape, f32)
    scratch = [
        low(width, qw + 2 * kw), low(width, 2 * fw), low(qw, width), low(fw, width),
        low(planes * (output_weight.shape[0] // n), width),
        low(length, width), low(length, width), low(length, width),
        low(width, length), low(width, length), low(width, length),
        wide(length, head), wide(length, head), wide(length, head),
        wide(length, qw + kw), low(length, qw), low(length, kw), low(length, kw),
        low(kw, length), low(kw, length), low(n // 2, length, 2 * group * block), wide(n // 2, 1, 2 * group * block),
        wide(n // 2, head, 2 * group * block), low(length, qw), low(qw, length),
        low(length, fw), low(length, 2 * fw), low(length, qw + 2 * kw),
        wide(length, kw), wide(length, kw),
    ]
    scratch += [low(planes, n, per, size) for size in sizes]
    scratch += [low(planes + 1, n, per, size) for size in sizes]
    scratch += [low(n, per, sizes[m] + sizes[m + 1]) for m in (0, 2, 4)]
    scratch += [low(2, 4, block, width)] * 2 + [low(2, 3, block, width)] * 2 + [wide(2, block, width), wide(2, block, width)]
    scratch += [
        wide(block, width), wide(block, width), wide(8, width), wide(n, 8, width), wide(planes, 8, width),
        dma((13,)), dma((8, 6)), dma((8, planes)), dma((1, 7)), dma((1, 4)),
        dma((4, n)), dma((4, n)), dma((4, 4)), dma((4, 4)), dma((4, 4)), dma((4, 4)),
        dma((6, planes)), dma((6, planes + 1)), dma((3, n)), dma((3, n)), dma((n,)), dma((n,)),
        dma((planes,)), dma((planes,)),
    ]
    shapes = [
        jax.ShapeDtypeStruct((block, width), bf16),
        jax.ShapeDtypeStruct((block, width), f32),
        jax.ShapeDtypeStruct((8, width), f32),
    ] + [jax.ShapeDtypeStruct((n, per, sizes[m] + sizes[m + 1]), bf16) for m in (0, 2, 4)]
    results = pl.pallas_call(
        functools.partial(layer_kernel, n, planes, block, head, group, fw),
        out_shape=shapes,
        in_specs=[vmem] * 10 + [hbm] * 7,
        out_specs=[vmem] * len(shapes),
        scratch_shapes=scratch,
        compiler_params=pltpu.CompilerParams(
            collective_id=0, has_side_effects=True, vmem_limit_bytes=60 * 1024 * 1024),
    )(
        layer_input[0], out_cotangent[0], token_positions, inverse, step_cos, step_sin,
        attention_gain[None], feedforward_gain[None], query_gain[None], key_norm_gain[None],
        query_weight, key_matrix, value_matrix, output_weight, gate_weight, up_weight, down_weight,
    )
    plain = lambda rows, columns, kind=f32: jax.ShapeDtypeStruct((rows, columns), kind)
    finals = [
        plain(block, width, bf16), plain(block, width), plain(1, width),
        plain(per, n * qw), plain(per, n * kw), plain(per, n * kw), plain(1, head), plain(1, head),
        plain(per, n * qw), plain(1, width), plain(per, n * fw), plain(per, n * fw), plain(per, n * fw),
    ]
    done = pl.pallas_call(
        functools.partial(finish_kernel, n, head),
        out_shape=finals,
        in_specs=[vmem] * len(shapes),
        out_specs=[vmem] * len(finals),
    )(*results)
    out, dx, ag, q, k, v, qg, kg, o, fg, g, u, d = done
    return out[None], dx[None], ag[0], q, k, v, qg[0], kg[0], o.T, fg[0], g, u, d.T


def solution(mesh):
    in_specs = (
        P("fsdp", "ctx", None),
        P("fsdp", None),
        P(),
        P("fsdp", None),
        P("fsdp", None),
        P("fsdp", None),
        P(),
        P(),
        P("fsdp", None),
        P(),
        P("fsdp", None),
        P("fsdp", None),
        P("fsdp", None),
        P("fsdp", "ctx", None),
    )
    out_specs = (
        P("fsdp", "ctx", None),
        P("fsdp", "ctx", None),
        P(),
        P(("ctx", "fsdp"), None),
        P(("ctx", "fsdp"), None),
        P(("ctx", "fsdp"), None),
        P(),
        P(),
        P(None, ("ctx", "fsdp")),
        P(),
        P(("ctx", "fsdp"), None),
        P(("ctx", "fsdp"), None),
        P(None, ("ctx", "fsdp")),
    )

    def run(*arguments):
        n, planes = mesh.shape["ctx"], mesh.shape["fsdp"]
        key_heads = arguments[4].shape[1] // arguments[6].shape[0]
        whole_heads = n == 8 and planes == 4 and key_heads == n
        return jax.shard_map(
            plane_device if whole_heads else on_device,
            mesh=mesh, in_specs=in_specs, out_specs=out_specs, check_vma=False,
        )(*arguments)

    return run
```

```python
import functools

import jax
import jax.numpy as jnp
import numpy as np
from jax import lax
from jax.experimental import pallas as pl
from jax.experimental.pallas import tpu as pltpu
from jax.sharding import PartitionSpec as P

epsilon = 1e-06
rope_base = 1000000.0
masked_score = -1e30


def from_behind(block, axis, distance):
    devices = range(lax.axis_size(axis))
    route = [((i - distance) % len(devices), i) for i in devices]
    return lax.ppermute(block, axis, route)


def rotate(value_rows):
    half = value_rows.shape[-1] // 2
    return jnp.concatenate([-value_rows[..., half:], value_rows[..., :half]], -1)


def rotate_back(value_rows):
    half = value_rows.shape[-1] // 2
    return jnp.concatenate([value_rows[..., half:], -value_rows[..., :half]], -1)


def rope_tables(token_offsets, head_size):
    half = head_size // 2
    inverse = rope_base ** (-(jnp.arange(half).astype(jnp.float32) * 2.0) / head_size)
    angles = token_offsets.astype(jnp.float32)[:, None] * inverse[None, :]
    cosine = jnp.cos(angles)
    sine = jnp.sin(angles)
    return (jnp.concatenate([cosine, cosine], -1), jnp.concatenate([sine, sine], -1))


def norm_scale(value_rows):
    return lax.rsqrt(jnp.mean(value_rows * value_rows, -1, keepdims=True) + epsilon)


def norm_back(value_rows, scale, gain, grad):
    weighted = grad * gain
    inner = jnp.mean(weighted * value_rows, -1, keepdims=True)
    result = scale * weighted - value_rows * scale * scale * scale * inner
    gain_part = jnp.sum((grad * value_rows * scale).reshape(-1, gain.shape[0]), 0)
    return (result, gain_part)


def row_products(left, pieces):
    return tuple((jnp.dot(left, piece, preferred_element_type=jnp.float32) for piece in pieces))


def column_products(rights, pieces):
    total = jnp.einsum("tc,rc->tr", rights[0], pieces[0], preferred_element_type=jnp.float32)
    for right, piece in zip(rights[1:], pieces[1:]):
        total = total + jnp.einsum("tc,rc->tr", right, piece, preferred_element_type=jnp.float32)
    return total


def on_device(
    layer_input,
    token_positions,
    attention_gain,
    query_weight,
    key_matrix,
    value_matrix,
    query_gain,
    key_norm_gain,
    output_weight,
    feedforward_gain,
    gate_weight,
    up_weight,
    down_weight,
    out_cotangent,
):
    hidden_in = layer_input[0].astype(jnp.float32)
    count = hidden_in.shape[0]
    head_size = query_gain.shape[0]
    query_width = query_weight.shape[1]
    key_width = key_matrix.shape[1]
    inner_width = gate_weight.shape[1]
    heads = query_width // head_size
    key_heads = key_width // head_size
    group = heads // key_heads
    scale = head_size ** (-0.5)
    cycles = lax.axis_size("ctx")
    own_index = lax.axis_index("ctx")
    sequence_pos = token_positions[0]
    token_offsets = lax.dynamic_slice_in_dim(sequence_pos, own_index * count, count)
    cosine, sine = rope_tables(token_offsets, head_size)
    cosine = cosine[:, None, :]
    sine = sine[:, None, :]
    first_scale = norm_scale(hidden_in)
    first = (hidden_in * first_scale * attention_gain).astype(jnp.bfloat16)
    query_raw, key_unnormed, value_unnormed = row_products(
        first,
        (
            lax.all_gather(query_weight, "fsdp", axis=0, tiled=True),
            lax.all_gather(key_matrix, "fsdp", axis=0, tiled=True),
            lax.all_gather(value_matrix, "fsdp", axis=0, tiled=True),
        ),
    )
    query_heads = query_raw.reshape(count, heads, head_size)
    query_scale = norm_scale(query_heads)
    query_normed = query_heads * query_scale * query_gain
    query_rot = query_normed * cosine + rotate(query_normed) * sine
    query_grouped = (
        query_rot.reshape(count, key_heads, group, head_size)
        .transpose(1, 2, 0, 3)
        .astype(jnp.bfloat16)
    )
    key_heads_raw = key_unnormed.reshape(count, key_heads, head_size)
    key_scale = norm_scale(key_heads_raw)
    key_normed = key_heads_raw * key_scale * key_norm_gain
    key_low = (
        (key_normed * cosine + rotate(key_normed) * sine)
        .reshape(count, key_width)
        .astype(jnp.bfloat16)
    )
    value_low = value_unnormed.astype(jnp.bfloat16)
    rowmax = jnp.full((key_heads, group, count), masked_score, jnp.float32)
    keys_piece = lax.all_gather(key_low, "ctx", axis=0, tiled=True).reshape(
        -1, key_heads, head_size
    )
    values_piece = lax.all_gather(value_low, "ctx", axis=0, tiled=True).reshape(
        -1, key_heads, head_size
    )
    key_pos = sequence_pos
    allowed = token_offsets[:, None] >= key_pos[None, :]
    scores = (
        jnp.einsum("kgtd,skd->kgts", query_grouped, keys_piece, preferred_element_type=jnp.float32)
        * scale
    )
    scores = jnp.where(allowed, scores, masked_score)
    newmax = jnp.maximum(rowmax, jnp.max(scores, -1))
    weights = jnp.where(allowed, jnp.exp(scores - newmax[..., None]), 0.0)
    accum = jnp.einsum(
        "kgts,skd->kgtd",
        weights.astype(jnp.bfloat16),
        values_piece,
        preferred_element_type=jnp.float32,
    )
    rowsum = jnp.sum(weights, -1)
    accum, rowmax, rowsum = (accum, newmax, rowsum)
    normalized = accum / rowsum[..., None]
    logsum = rowmax + jnp.log(rowsum)
    attention_low = (
        normalized.transpose(2, 0, 1, 3).reshape(count, query_width).astype(jnp.bfloat16)
    )
    output_whole = lax.all_gather(output_weight, "fsdp", axis=0, tiled=True)
    branch_out = jnp.dot(attention_low, output_whole, preferred_element_type=jnp.float32)
    middle = hidden_in + branch_out
    second_scale = norm_scale(middle)
    second = (middle * second_scale * feedforward_gain).astype(jnp.bfloat16)
    gate, up = row_products(
        second,
        (
            lax.all_gather(gate_weight, "fsdp", axis=0, tiled=True),
            lax.all_gather(up_weight, "fsdp", axis=0, tiled=True),
        ),
    )
    sigmoid_gate = jax.nn.sigmoid(gate)
    silu_gate = gate * sigmoid_gate
    hidden_low = (silu_gate * up).astype(jnp.bfloat16)
    (down_out,) = row_products(
        hidden_low, (lax.all_gather(down_weight, "fsdp", axis=0, tiled=True),)
    )
    layer_output = (middle + down_out).astype(jnp.bfloat16)[None]
    cotangent = out_cotangent[0]
    hidden_grad = column_products(
        (cotangent,), lax.all_gather((down_weight,), "fsdp", axis=0, tiled=True)
    )
    up_low = (hidden_grad * silu_gate).astype(jnp.bfloat16)
    gate_low = (hidden_grad * up * sigmoid_gate * (1.0 + gate * (1.0 - sigmoid_gate))).astype(
        jnp.bfloat16
    )
    second_grad = column_products(
        (gate_low, up_low), lax.all_gather((gate_weight, up_weight), "fsdp", axis=0, tiled=True)
    )
    middle_part, feedforward_part = norm_back(middle, second_scale, feedforward_gain, second_grad)
    middle_grad = cotangent.astype(jnp.float32) + middle_part
    middle_low = middle_grad.astype(jnp.bfloat16)
    attention_grad = jnp.einsum(
        "tc,rc->tr", middle_low, output_whole, preferred_element_type=jnp.float32
    )
    attention_grad_low = attention_grad.astype(jnp.bfloat16)
    mixed_grad = attention_grad_low.reshape(count, key_heads, group, head_size).transpose(
        1, 2, 0, 3
    )
    delta = jnp.sum(mixed_grad.astype(jnp.float32) * normalized, -1)

    def cycle_step(index, carry):
        keys_held, values_held, key_acc, value_acc, query_acc = carry
        anchor = (own_index - index) % cycles
        key_pos = lax.dynamic_slice_in_dim(sequence_pos, anchor * count, count)
        keys_piece = keys_held.astype(jnp.bfloat16).reshape(count, key_heads, head_size)
        values_piece = values_held.astype(jnp.bfloat16).reshape(count, key_heads, head_size)
        allowed = token_offsets[:, None] >= key_pos[None, :]
        scores = (
            jnp.einsum(
                "kgtd,skd->kgts", query_grouped, keys_piece, preferred_element_type=jnp.float32
            )
            * scale
        )
        probs = jnp.where(allowed, jnp.exp(scores - logsum[..., None]), 0.0)
        value_acc = value_acc + jnp.einsum(
            "kgts,kgtd->skd",
            probs.astype(jnp.bfloat16),
            mixed_grad,
            preferred_element_type=jnp.float32,
        ).reshape(count, key_width)
        prob_grad = jnp.einsum(
            "kgtd,skd->kgts", mixed_grad, values_piece, preferred_element_type=jnp.float32
        )
        score_grad = (probs * (prob_grad - delta[..., None])).astype(jnp.bfloat16)
        query_acc = (
            query_acc
            + jnp.einsum(
                "kgts,skd->kgtd", score_grad, keys_piece, preferred_element_type=jnp.float32
            )
            * scale
        )
        key_acc = (
            key_acc
            + jnp.einsum(
                "kgts,kgtd->skd", score_grad, query_grouped, preferred_element_type=jnp.float32
            ).reshape(count, key_width)
            * scale
        )
        moved = (
            from_behind(keys_held.astype(jnp.bfloat16), "ctx", 1).astype(keys_held.dtype),
            from_behind(values_held.astype(jnp.bfloat16), "ctx", 1).astype(values_held.dtype),
            from_behind(key_acc.astype(jnp.bfloat16), "ctx", 1).astype(key_acc.dtype),
            from_behind(value_acc.astype(jnp.bfloat16), "ctx", 1).astype(value_acc.dtype),
        )
        return (moved[0], moved[1], moved[2], moved[3], query_acc)

    start_cycle = (
        key_low.astype(jnp.float32),
        value_low.astype(jnp.float32),
        jnp.zeros((count, key_width), jnp.float32),
        jnp.zeros((count, key_width), jnp.float32),
        jnp.zeros((key_heads, group, count, head_size), jnp.float32),
    )
    cycle_done = lax.fori_loop(0, cycles, cycle_step, start_cycle)
    key_acc = cycle_done[2]
    value_acc = cycle_done[3]
    query_acc = cycle_done[4]
    query_rot_grad = query_acc.transpose(2, 0, 1, 3).reshape(count, heads, head_size)
    query_normed_grad = query_rot_grad * cosine + rotate_back(query_rot_grad * sine)
    query_heads_grad, query_part = norm_back(
        query_heads, query_scale, query_gain, query_normed_grad
    )
    query_low_grad = query_heads_grad.reshape(count, query_width).astype(jnp.bfloat16)
    key_rot_grad = key_acc.reshape(count, key_heads, head_size)
    key_normed_grad = key_rot_grad * cosine + rotate_back(key_rot_grad * sine)
    key_heads_grad, key_part = norm_back(key_heads_raw, key_scale, key_norm_gain, key_normed_grad)
    key_low_grad = key_heads_grad.reshape(count, key_width).astype(jnp.bfloat16)
    value_low_grad = value_acc.astype(jnp.bfloat16)
    first_grad = column_products(
        (query_low_grad, key_low_grad, value_low_grad),
        lax.all_gather((query_weight, key_matrix, value_matrix), "fsdp", axis=0, tiled=True),
    )
    input_part, attention_part = norm_back(hidden_in, first_scale, attention_gain, first_grad)
    input_gradient = (middle_grad + input_part)[None]
    rights_first = jnp.concatenate([query_low_grad, key_low_grad, value_low_grad], 1)
    rights_second = jnp.concatenate([gate_low, up_low], 1)
    pairs = (
        (first, rights_first),
        (second, rights_second),
        (middle_low, attention_low),
        (cotangent, hidden_low),
    )
    parts = []
    for left, right in pairs:
        parts.append(jnp.einsum("tr,tc->rc", left, right, preferred_element_type=jnp.float32))
    sums = lax.psum_scatter(
        jnp.concatenate(parts, 1), ("ctx", "fsdp"), scatter_dimension=0, tiled=True
    )
    edges = [0, query_width, query_width + key_width, query_width + 2 * key_width]
    edges = edges + [edges[3] + inner_width, edges[3] + 2 * inner_width]
    edges = edges + [edges[5] + query_width, edges[5] + query_width + inner_width]
    query_gradient = sums[:, edges[0] : edges[1]]
    key_gradient = sums[:, edges[1] : edges[2]]
    value_gradient = sums[:, edges[2] : edges[3]]
    gate_gradient = sums[:, edges[3] : edges[4]]
    up_gradient = sums[:, edges[4] : edges[5]]
    output_gradient = sums[:, edges[5] : edges[6]].T
    down_gradient = sums[:, edges[6] : edges[7]].T
    attention_total, query_total, key_total, feedforward_total = lax.psum(
        (attention_part, query_part, key_part, feedforward_part), ("ctx", "fsdp")
    )
    return (
        layer_output,
        input_gradient,
        attention_total,
        query_gradient,
        key_gradient,
        value_gradient,
        query_total,
        key_total,
        output_gradient,
        feedforward_total,
        gate_gradient,
        up_gradient,
        down_gradient,
    )


MESH = pl.DeviceIdType.MESH
f32 = jnp.float32
bf16 = jnp.bfloat16


def dot(left, right):
    return jnp.dot(left, right, preferred_element_type=f32)


def dot_nt(left, right):
    return lax.dot_general(left, right, (((1,), (1,)), ((), ())), preferred_element_type=f32)


def dot_tn(left, right):
    return lax.dot_general(left, right, (((0,), (0,)), ((), ())), preferred_element_type=f32)


def hidden_block(device, third):
    def plane(i, t):
        return ((3, 1, 2), (0, 2, 1), (0, 3, 2), (3, 0, 1))[i // 4 * 2 + i % 2][t]

    own = plane(device, third)
    return own, sum(plane(i, t) == own for i in range(device) for t in range(3))


def layer_kernel(
    n, planes, block, head, group, fw,
    x_ref, dy_ref, pos_row, inverse_ref, step_cos, step_sin, ag_ref, fg_ref, qg_ref, kg_ref,
    wq, wk, wv, wo, wg, wu, wd,
    out_ref, dx_ref, gains_ref, got_ab, got_co, got_qkv,
    w_qkv, w_gu, w_out, w_down, t_out,
    first, dy_all, second, first_t, dy_t, second_t,
    positions, cosine, sine,
    raw, queries, keys, values, keys_t, values_t, probs, sums, mixed_t, mixed_low, mixed_low_t,
    hidden, d_gu, d_qkv, dk_acc, dv_acc,
    stage_a, stage_b, stage_c, stage_out, stage_q, stage_kv,
    land_a, land_b, land_c, land_out, land_q, land_kv,
    own_ab, own_co, own_qkv,
    rs_sa, rs_ra, rs_sb, rs_rb, rs_kept, rs_acc,
    middle, d_middle, gain_own, gain_plane, gain_all,
    local_sem, wz_send, wz_recv, hand_send, hand_recv,
    ag_send, ag_recv, ra_send, ra_recv, rb_send, rb_recv,
    zr_send, zr_recv, aa_send, aa_recv, gp_send, gp_recv, gz_send, gz_recv,
):
    c = lax.axis_index("ctx")
    z = lax.axis_index("fsdp")
    dmid = first
    cy, cx, ck = lax.div(c, 4), lax.rem(lax.div(c, 2), 2), lax.rem(c, 2)
    ci = lax.rem(c, 4)
    sign = 1 - 2 * ck
    qw, kw = group * head, head
    pw = 128
    thirds = fw // pw
    width = x_ref.shape[1]
    scale = head ** (-0.5)
    log2e = 1.4426950408889634
    gots = (got_ab, got_co, got_qkv)
    owns = (own_ab, own_co, own_qkv)
    stages = (stage_a, stage_b, stage_c, stage_out, stage_q, stage_kv)
    lands = (land_a, land_b, land_c, land_out, land_q, land_kv)

    def partner(j):
        y = lax.rem(cy + lax.div(j, 4), 2)
        x = lax.rem(cx + lax.rem(lax.div(j, 2), 2), 2)
        k = lax.rem(ck + lax.rem(j, 2), 2)
        return y * 4 + x * 2 + k

    def chip(slot):
        return lax.rem(cy + lax.div(slot, 2), 2) * 2 + lax.rem(cx + lax.rem(slot, 2), 2)

    def rows(start, size):
        return pl.ds(pl.multiple_of(start * size, size), size)

    def remote(src, dst, send, recv, ctx, plane):
        return pltpu.make_async_remote_copy(
            src_ref=src, dst_ref=dst, send_sem=send, recv_sem=recv,
            device_id={"ctx": ctx, "fsdp": plane}, device_id_type=MESH,
        )

    in_plane, along, weight_sends = [], [], []

    def launch(started, copy, when=None):
        if when is None:
            copy().start()
        else:
            pl.when(when)(lambda: copy().start())
        started.append((copy, when))

    def drain(started):
        for copy, when in started:
            if when is None:
                copy().wait_send()
            else:
                pl.when(when)(lambda copy=copy: copy().wait_send())
        started.clear()

    def pick(values):
        return sum(jnp.where(c == i, value, 0) for i, value in enumerate(values))

    unit_plane = [pick([hidden_block(i, t)[0] for i in range(n)]) for t in range(thirds)]
    unit_block = [pick([hidden_block(i, t)[1] for i in range(n)]) for t in range(thirds)]
    plane_blocks = wd.shape[0] // pw

    own_rows = wq.shape[0]
    out_rows = wo.shape[0] // n

    def own_slices():
        mine = rows(z, own_rows)
        pairs = [
            (wq.at[:, rows(c, qw)], w_qkv.at[mine, 0:qw]),
            (wk.at[:, rows(c, kw)], w_qkv.at[mine, qw:qw + kw]),
            (wv.at[:, rows(c, kw)], w_qkv.at[mine, qw + kw:qw + 2 * kw]),
            (wo.at[rows(c, out_rows)], t_out.at[rows(z, out_rows)]),
        ]
        for t in range(thirds):
            unit = unit_plane[t] * plane_blocks + unit_block[t]
            pairs.append((wg.at[:, rows(unit, pw)], w_gu.at[t, mine, 0:pw]))
            pairs.append((wu.at[:, rows(unit, pw)], w_gu.at[t, mine, pw:2 * pw]))
        return pairs

    local = [pltpu.make_async_copy(src, dst, local_sem.at[i]) for i, (src, dst) in enumerate(own_slices())]
    for copy in local:
        copy.start()

    def own_down(t):
        return pltpu.make_async_copy(
            wd.at[rows(unit_block[t], pw)], w_down.at[t * pw:(t + 1) * pw], local_sem.at[4 + 2 * thirds + t])

    holds = [unit_plane[t] == z for t in range(thirds)]
    for t in range(thirds):
        pl.when(holds[t])(lambda t=t: own_down(t).start())

    for land in lands:
        @pl.when(z == 0)
        def _(land=land):
            land[0] = jnp.zeros(land.shape[1:], bf16)

        @pl.when(z == planes - 1)
        def _(land=land):
            land[planes] = jnp.zeros(land.shape[1:], bf16)

    barrier = pltpu.get_barrier_semaphore()
    for j in range(1, n):
        pl.semaphore_signal(barrier, inc=1, device_id={"ctx": partner(j), "fsdp": z}, device_id_type=MESH)
    for d in range(1, planes):
        pl.semaphore_signal(
            barrier, inc=1, device_id={"ctx": c, "fsdp": lax.rem(z + d, planes)}, device_id_type=MESH)
    x = x_ref[...].astype(f32)
    x_scale = lax.rsqrt(jnp.mean(x * x, -1, keepdims=True) + epsilon)
    first[rows(c, block)] = (x * x_scale * ag_ref[...]).astype(bf16)
    dy_all[rows(c, block)] = dy_ref[...]
    for copy in local[:3]:
        copy.wait()
    pl.semaphore_wait(barrier, n + planes - 2)

    def inside(t):
        return jnp.logical_and(t >= 0, t < planes)

    weights = [
        (lambda o: w_qkv.at[rows(o, own_rows)], None),
        (lambda o: t_out.at[rows(o, out_rows)], 0),
    ]
    for t in range(thirds):
        weights.append((lambda o, t=t: w_gu.at[t, rows(o, own_rows)], None))
        weights.append((lambda o, t=t: w_down.at[t * pw:(t + 1) * pw], None))

    def weight_copy(w, slot, origin, target):
        part = weights[w][0](origin)
        return remote(part, part, wz_send.at[w, slot], wz_recv.at[w, origin], c, target)

    def from_plane(w, origin):
        return origin == unit_plane[(w - 3) // 2] if w >= 3 and w % 2 else None

    def both(one, other):
        return one if other is None else jnp.logical_and(one, other)

    def hand_split(origin, valid):
        mine = 2 * origin + cy == c
        return jnp.logical_and(valid, jnp.logical_not(mine)), jnp.logical_and(valid, mine)

    def weight_start(w):
        for side in range(2):
            d = sign * (1 - 2 * side)
            launch(
                weight_sends, lambda side=side, d=d: weight_copy(w, side, z, z + d),
                both(inside(z + d), from_plane(w, z)))
        if weights[w][1] is not None:
            hand_over(w, z, 0, *hand_split(z, True))

    def hand_target(h):
        return lambda i: w_out.at[rows(i, out_rows)]

    def hand_copy(w, origin, slot):
        h = weights[w][1]
        return remote(
            weights[w][0](origin), hand_target(h)(ci), hand_send.at[h, slot], hand_recv.at[h, ci], 2 * origin + cy, z)

    def hand_over(w, origin, slot, away, here):
        launch(in_plane, lambda: hand_copy(w, origin, slot), away)

        @pl.when(here)
        def _():
            hand_target(weights[w][1])(ci)[...] = weights[w][0](origin)[...]

    def hand_arrive(w):
        h = weights[w][1]
        for i in range(4):
            @pl.when(4 * ck + i != c)
            def _(i=i):
                part = hand_target(h)(i)
                remote(part, part, hand_send.at[h, 0], hand_recv.at[h, i], c, z).wait_recv()

    hops = {}
    for w in range(len(weights)):
        for d in range(1, planes):
            for side, way in enumerate((1, -1)):
                origin = z - way * d
                valid = both(inside(origin), from_plane(w, origin))
                passed = jnp.logical_and(valid, inside(z + way))
                split = None if weights[w][1] is None else hand_split(origin, valid)
                hops[w, d, side] = origin, z + way, valid, passed, split

    def weight_hop(w, d):
        for side in range(2):
            origin, following, valid, passed, split = hops[w, d, side]
            pl.when(valid)(lambda: weight_copy(w, 0, origin, z).wait_recv())
            if d < planes - 1:
                launch(
                    weight_sends,
                    lambda side=side, origin=origin, following=following: weight_copy(
                        w, 2 * d + side, origin, following),
                    passed)
            if split is not None:
                hand_over(w, origin, 2 * d - 1 + side, *split)

    def gather_copy(buf, g, j, send, origin, target):
        part = buf.at[rows(origin, block)]
        return remote(part, part, ag_send.at[g, send], ag_recv.at[g, j], target, z)

    def gather_start(buf, g):
        for j in (1, 2 + 2 * ck, 4 - 2 * ck):
            launch(in_plane, lambda j=j: gather_copy(buf, g, j, j, c, partner(j)))

    def gather_half(buf, g, j):
        half = block // 2
        part = buf.at[pl.ds(pl.multiple_of(partner(j) * block + (half if j == 2 else 0), half), half)]
        at = 0 if j == 2 else 6
        return remote(part, part, ag_send.at[g, at], ag_recv.at[g, at], partner(6 - j), z)

    def gather_diagonal(buf, g):
        half = block // 2
        for at in (6, 0):
            part = buf.at[pl.ds(pl.multiple_of(partner(6) * block + (0 if at == 6 else half), half), half)]
            remote(part, part, ag_send.at[g, at], ag_recv.at[g, at], c, z).wait_recv()

    def gather_forward(buf, g, j):
        return gather_copy(buf, g, j + 1, j + 1, partner(j), partner(1))

    def gather_take(buf, g, j):
        if j == 6:
            gather_diagonal(buf, g)
        else:
            gather_copy(buf, g, j, j, partner(j), c).wait_recv()
            gather_half(buf, g, j).start()
        gather_forward(buf, g, j).start()

    def gather_sent(buf, g):
        for j in (2, 4, 6):
            in_plane.append((lambda j=j: gather_forward(buf, g, j), None))
            if j < 6:
                in_plane.append((lambda j=j: gather_half(buf, g, j), None))

    def gather_finish(buf, g):
        for j in (2, 4, 6):
            gather_take(buf, g, j)
        gather_sent(buf, g)
        for j in (1, 3, 5, 7):
            gather_copy(buf, g, j, j, partner(j), c).wait_recv()

    def gather_step(buf, g, slot):
        @pl.when(slot == 1)
        def _():
            gather_take(buf, g, 2)
            gather_take(buf, g, 4)

        pl.when(slot == 3)(lambda: gather_take(buf, g, 6))
        gather_copy(buf, g, 2 * slot + 1, 0, partner(2 * slot + 1), c).wait_recv()

    def sum_pair_copy(s, slot):
        return remote(rs_sa.at[s % 2, slot], rs_ra.at[s % 2, slot], ra_send.at[s, slot], ra_recv.at[s, slot], partner(1), z)

    def sum_chip_copy(s, slot):
        return remote(
            rs_sb.at[s % 2, slot - 1], rs_rb.at[s % 2, slot - 1], rb_send.at[s, slot], rb_recv.at[s, slot], partner(2 * slot), z)

    def sum_half_copy(s, slot):
        half = block // 2
        at = pl.ds(pl.multiple_of((slot - 1) * half, half), half)
        return remote(
            rs_sb.at[s % 2, 2, at], rs_rb.at[s % 2, 2, at], rb_send.at[s, 6 - 3 * slot], rb_recv.at[s, 6 - 3 * slot],
            partner(6 - 2 * slot), z)

    def sum_slot(p):
        return jnp.where(p == 0, 3, jnp.where(p == 1, 2 - ck, jnp.where(p == 2, 1 + ck, 0)))

    def sum_start(s, left, partial, prepare=None, ready=None, during=()):
        if prepare is not None:
            prepare(chip(sum_slot(0)))
        if ready is not None:
            ready()

        def body(p, carry):
            slot = sum_slot(p)
            at = [rows(partner(2 * slot + 1), block), rows(partner(2 * slot), block)]
            both = partial(jnp.concatenate([left[i] for i in at], 0))
            rs_sa[s % 2, slot] = both[:block].astype(bf16)
            sum_pair_copy(s, slot).start()
            rs_kept[lax.rem(p, 2)] = both[block:]

            @pl.when(p > 0)
            def _():
                before = sum_slot(p - 1)
                sum_pair_copy(s, before).wait_recv()
                rs_sb[s % 2, before - 1] = (
                    rs_kept[lax.rem(p + 1, 2)] + rs_ra[s % 2, before].astype(f32)).astype(bf16)

            @pl.when(p == 1)
            def _():
                sum_half_copy(s, 1).start()
                sum_half_copy(s, 2).start()

            @pl.when(p > 1)
            def _():
                before = sum_slot(p - 1)
                half = block // 2
                at = pl.ds(pl.multiple_of((before - 1) * half, half), half)
                sum_half_copy(s, before).wait_recv()
                rs_sb[s % 2, before - 1, at] = (
                    rs_sb[s % 2, before - 1, at].astype(f32) + rs_rb[s % 2, 2, at].astype(f32)).astype(bf16)
                sum_chip_copy(s, before).start()

            if prepare is not None:
                @pl.when(p < 3)
                def _():
                    prepare(chip(sum_slot(p + 1)))

            for k, poll in enumerate(during):
                pl.when(p == k)(poll)
            return carry

        lax.fori_loop(0, 4, body, 0)
        for slot in range(4):
            in_plane.append((lambda slot=slot: sum_pair_copy(s, slot), None))
        for slot in (1, 2):
            in_plane.append((lambda slot=slot: sum_half_copy(s, slot), None))
            in_plane.append((lambda slot=slot: sum_chip_copy(s, slot), None))
        sum_pair_copy(s, 0).wait_recv()
        rs_acc[s % 2] = rs_kept[1] + rs_ra[s % 2, 0].astype(f32)

    def sum_finish(s):
        total = rs_acc[s % 2]
        for slot in (1, 2):
            sum_chip_copy(s, slot).wait_recv()
            total = total + rs_rb[s % 2, slot - 1].astype(f32)
        return total

    per = block // planes

    at_edge = jnp.logical_or(z == 0, z == planes - 1)
    edge_targets = [jnp.where(z == 0, planes - 1 - k, k) for k in range(planes - 1)]

    def weight_grad(m, parts):
        def body(i, carry):
            at = 0
            for left, right in parts:
                value = right()
                grad = dot(left[rows(i, 4 * block)], value)
                for k in range(4):
                    for t in range(planes):
                        start = k * block + t * per
                        stages[m][t, 4 * i + k, :, at:at + value.shape[1]] = grad[start:start + per].astype(bf16)
                at += value.shape[1]
            return carry

        lax.fori_loop(0, n // 4, body, 0)
        grad_send(m)

    def grad_send(m):
        for t in edge_targets:
            launch(along, lambda t=t: grad_copy(m, t), at_edge)

    def grad_copy(m, t):
        way = jnp.where(z < t, 1, -1)
        last = z + way == t
        slot = jnp.where(jnp.logical_and(last, way < 0), planes, t)
        return remote(
            stages[m].at[t], lands[m].at[slot], zr_send.at[m, t], zr_recv.at[m, slot], c, z + way)

    def grad_arrive(m, slot):
        part = lands[m].at[slot]
        remote(part, part, zr_send.at[m, 0], zr_recv.at[m, slot], c, z).wait_recv()

    def grad_pass(m, t, valid):
        @pl.when(valid)
        def _():
            grad_arrive(m, t)
            stages[m][t] = stages[m][t] + lands[m][t]

        launch(along, lambda: grad_copy(m, t), valid)

    is_low, is_high = z == 1, z == planes - 2

    def grad_near_far(m):
        grad_pass(m, 3, is_low)
        grad_pass(m, 0, is_high)

    def grad_near_inner(m):
        grad_pass(m, 2, is_low)
        grad_pass(m, 1, is_high)

    def grad_near(m):
        grad_near_far(m)
        grad_near_inner(m)

    def grad_far(m):
        grad_pass(m, 3, is_high)
        grad_pass(m, 0, is_low)

    def owner_copy(g, j):
        return remote(owns[g].at[partner(j)], gots[g].at[c], aa_send.at[g, j], aa_recv.at[g, j], partner(j), z)

    def own_sum(m):
        pl.when(z > 0)(lambda: grad_arrive(m, z))
        pl.when(z < planes - 1)(lambda: grad_arrive(m, planes))
        total = stages[m][z].astype(f32) + lands[m][z].astype(f32) + lands[m][planes].astype(f32)
        first_size = stages[m // 2 * 2].shape[3]
        if m % 2:
            owns[m // 2][:, :, first_size:] = total.astype(bf16)
        else:
            owns[m // 2][:, :, :first_size] = total.astype(bf16)

    def hand_out(g):
        for j in (2 + 2 * ck, 3 + 2 * ck, 4 - 2 * ck, 5 - 2 * ck, 6, 7, 1):
            launch(in_plane, lambda j=j: owner_copy(g, j))
        gots[g][c] = owns[g][c]

    def hand_receive(g):
        for j in range(1, n):
            owner_copy(g, j).wait_recv()

    weight_start(0)
    gather_start(first, 0)
    for copy in local[3:]:
        copy.wait()
    for t in range(thirds):
        pl.when(holds[t])(lambda t=t: own_down(t).wait())

    spread = jnp.broadcast_to(pos_row[...].astype(f32), (head, pos_row.shape[1]))
    positions[...] = spread.T
    side = jnp.where(lax.broadcasted_iota(jnp.int32, (1, head), 1) < head // 2, -1.0, 1.0)

    def table(i, carry):
        run = step_cos.shape[0]
        at = rows(i, run)
        start = positions[pl.ds(pl.multiple_of(i * run, run), 1)] * inverse_ref[...]
        start_cos, start_sin = jnp.cos(start), jnp.sin(start)
        cosine[at] = start_cos * step_cos[...] - start_sin * step_sin[...]
        sine[at] = (start_sin * step_cos[...] + start_cos * step_sin[...]) * side
        return carry

    def turn_over(src, dst):
        def body(i, carry):
            at = rows(i, block)
            dst[:, at] = src[at].T
            return carry

        lax.fori_loop(0, n, body, 0)

    lax.fori_loop(0, 2 * n, table, 0)
    weight_hop(0, 1)
    gather_finish(first, 0)
    weight_hop(0, 2)
    weight_start(1)
    gather_start(dy_all, 1)
    turn_over(first, first_t)
    weight_hop(0, 3)
    weight_start(2)
    weight_start(3)

    def turn(value, at):
        return value * cosine[at] + pltpu.roll(value, head // 2, 1) * sine[at]

    def turn_back(grad, at):
        return grad * cosine[at] - pltpu.roll(grad, head // 2, 1) * sine[at]

    def project(i, carry):
        at = rows(i, 2 * block)
        result = dot(first[at], w_qkv[...])
        raw[at] = result[:, :qw + kw]
        low_values = result[:, qw + kw:].astype(bf16)
        values[at] = low_values
        values_t[:, at] = low_values.T
        for h in range(group + 1):
            part = result[:, h * head:(h + 1) * head]
            inv = lax.rsqrt(jnp.mean(part * part, -1, keepdims=True) + epsilon)
            gain = qg_ref[...] if h < group else kg_ref[...]
            turned = turn(part * inv * gain, at)
            if h < group:
                queries[at, h * head:(h + 1) * head] = (turned * (scale * log2e)).astype(bf16)
            else:
                low_keys = turned.astype(bf16)
                keys[at] = low_keys
                keys_t[:, at] = low_keys.T
        return carry

    lax.fori_loop(0, n // 4, project, 0)
    weight_hop(1, 1)
    lax.fori_loop(n // 4, n // 2, project, 0)
    weight_hop(1, 2)
    gather_finish(dy_all, 1)

    def stack(ref, at):
        return jnp.concatenate([ref[at, h * head:(h + 1) * head] for h in range(group)], 0)

    def attend(place):
        at = rows(place, 2 * block)
        scores = dot_nt(keys[...], stack(queries, at))
        allowed = positions[...] <= pos_row[:, rows(2 * place, block)].astype(f32)
        later = positions[...] <= pos_row[:, rows(2 * place + 1, block)].astype(f32)
        weight = jnp.concatenate(
            [jnp.exp2(jnp.where(later if k % 2 else allowed, scores[:, k * block:(k + 1) * block], masked_score))
             for k in range(2 * group)], 1)
        inv = 1.0 / jnp.sum(weight, 0, keepdims=True)
        low_weight = weight.astype(bf16)
        probs[place] = low_weight
        sums[place] = inv
        result = dot(values_t[...], low_weight) * inv
        mixed_t[place] = result
        for h in range(group):
            low_result = result[:, 2 * h * block:2 * (h + 1) * block].astype(bf16)
            mixed_low_t[h * head:(h + 1) * head, at] = low_result
            mixed_low[at, h * head:(h + 1) * head] = low_result.T

    def output_ready():
        weight_hop(1, 3)
        weight_start(4)
        weight_start(5)
        hand_arrive(1)
        drain(in_plane)

    def hop_third(t, d):
        weight_hop(2 + 2 * t, d)
        weight_hop(3 + 2 * t, d)

    sum_start(
        0, mixed_low, lambda left: dot(left, w_out[...]), attend, output_ready,
        (lambda: hop_third(0, 1), lambda: hop_third(0, 2), lambda: hop_third(1, 1)))
    weight_start(6)
    weight_start(7)
    hop_third(0, 3)
    turn_over(dy_all, dy_t)
    hop_third(1, 2)
    mid = x_ref[...].astype(f32) + sum_finish(0)
    middle[...] = mid
    mid_scale = lax.rsqrt(jnp.mean(mid * mid, -1, keepdims=True) + epsilon)
    second[rows(c, block)] = (mid * mid_scale * fg_ref[...]).astype(bf16)
    gather_start(second, 2)
    hop_third(2, 1)

    def feed(t, at):
        units, pair = slice(t * pw, (t + 1) * pw), 2 * pw * t
        both = dot(second[at], w_gu[t])
        back = dot_nt(dy_all[at], w_down[units])
        gate, up = both[:, :pw], both[:, pw:]
        sig = 1.0 / (1.0 + jnp.exp(-gate))
        silu = gate * sig
        hidden[at, units] = (silu * up).astype(bf16)
        d_gu[at, pair:pair + pw] = (back * up * sig * (1.0 + gate * (1.0 - sig))).astype(bf16)
        d_gu[at, pair + pw:pair + 2 * pw] = (back * silu).astype(bf16)

    def feed_arriving(slot, carry):
        gather_step(second, 2, slot)
        at = rows(chip(slot), 2 * block)
        feed(0, at)
        second_t[:, at] = second[at].T
        pl.when(slot == 2)(lambda: hop_third(2, 2))
        return carry

    def third_grad(t):
        weight_grad(t, [
            (second_t, lambda: d_gu[:, 2 * pw * t:2 * pw * (t + 1)]),
            (dy_t, lambda: hidden[:, t * pw:(t + 1) * pw]),
        ])

    def feed_third(t):
        def body(i, carry):
            feed(t, rows(i, 2 * block))
            return carry

        lax.fori_loop(0, n // 2, body, 0)

    lax.fori_loop(0, n // 2, feed_arriving, 0)
    gather_sent(second, 2)
    hop_third(1, 3)
    third_grad(0)
    feed_third(1)
    hop_third(2, 3)
    sum_start(
        1, d_gu, lambda left: sum(dot_nt(left[:, 2 * pw * t:2 * pw * (t + 1)], w_gu[t]) for t in range(thirds)),
        lambda place: feed(thirds - 1, rows(place, 2 * block)))
    third_grad(1)
    third_grad(2)
    d_second = sum_finish(1)

    def norm_back(value, gain, grad):
        inv = lax.rsqrt(jnp.mean(value * value, -1, keepdims=True) + epsilon)
        weighted = grad * gain
        inner = jnp.mean(weighted * value, -1, keepdims=True)
        result = inv * weighted - value * (inv * inv * inv * inner)
        return result, jnp.sum(grad * value * inv, 0, keepdims=True)

    gain_own[...] = jnp.zeros_like(gain_own)
    part, gain_own[1:2, :] = norm_back(middle[...], fg_ref[...], d_second)
    d_mid = dy_ref[...].astype(f32) + part
    d_middle[...] = d_mid
    drain(in_plane)
    dmid[rows(c, block)] = d_mid.astype(bf16)
    gather_start(dmid, 3)
    sum_start(2, hidden, lambda left: dot(left, w_down[...]))
    drain(weight_sends)
    grad_near(0)

    dk_acc[...] = jnp.zeros_like(dk_acc)
    dv_acc[...] = jnp.zeros_like(dv_acc)

    def output_grad():
        def body(i, carry):
            grad = dot(mixed_low_t[...], dmid[:, rows(i, 2 * block)]).astype(bf16).T
            for k in range(2):
                for t in range(planes):
                    start = k * block + t * per
                    stage_out[t, 2 * i + k] = grad[start:start + per]
            return carry

        lax.fori_loop(0, n // 2, body, 0)
        grad_send(3)

    def attend_back(slot, q_sum):
        gather_step(dmid, 3, slot)
        place = chip(slot)
        at = rows(place, 2 * block)
        d_mix = dot_nt(w_out[...], dmid[at])
        pl.when(slot == 3)(output_grad)
        d_mix_t = jnp.concatenate([d_mix[h * head:(h + 1) * head] for h in range(group)], 1)
        d_mix_t = (d_mix_t.astype(bf16).astype(f32) * sums[place]).astype(bf16)
        delta = jnp.sum(d_mix_t.astype(f32) * mixed_t[place], 0, keepdims=True)
        weight = probs[place]
        d_prob = dot(values[...], d_mix_t)
        d_score = (weight.astype(f32) * (d_prob - delta)).astype(bf16)
        d_query = dot(keys_t[...], d_score) * scale
        for h in range(group):
            grad = turn_back(d_query[:, 2 * h * block:2 * (h + 1) * block].T, at)
            part, gain_part = norm_back(raw[at, h * head:(h + 1) * head], qg_ref[...], grad)
            d_qkv[at, h * head:(h + 1) * head] = part.astype(bf16)
            q_sum = q_sum + gain_part
        pl.when(slot == 2)(lambda: grad_near(1))
        dv_acc[...] += dot(weight, d_mix_t.T)
        dk_acc[...] += dot(d_score, stack(queries, at))
        return q_sum

    zero = jnp.zeros((1, head), f32)
    gain_own[2:3, 0:head] = lax.fori_loop(0, n // 2, attend_back, zero)
    gather_sent(dmid, 3)
    weight_grad(4, [(first_t, lambda: d_qkv[:, :qw])])
    grad_far(0)

    def project_back(i, k_sum):
        at = rows(i, 2 * block)
        grad = turn_back(dk_acc[at] * (1.0 / log2e), at)
        part, gain_part = norm_back(raw[at, qw:qw + kw], kg_ref[...], grad)
        d_qkv[at, qw:qw + kw] = part.astype(bf16)
        d_qkv[at, qw + kw:] = dv_acc[at].astype(bf16)
        return k_sum + gain_part

    gain_own[3:4, 0:head] = lax.fori_loop(0, n // 2, project_back, zero)

    weight_grad(5, [(first_t, lambda: d_qkv[:, qw:])])
    grad_far(1)
    grad_near(2)
    own_sum(0)
    drain(in_plane)
    sum_start(3, d_qkv, lambda left: dot_nt(left, w_qkv[...]))
    grad_far(2)
    grad_near(3)
    own_sum(1)
    hand_out(0)
    grad_far(3)
    grad_near(4)
    out_ref[...] = (middle[...] + sum_finish(2)).astype(bf16)
    grad_far(4)
    grad_near_far(5)
    own_sum(2)
    grad_near_inner(5)
    grad_far(5)
    x_part, gain_own[0:1, :] = norm_back(x_ref[...].astype(f32), ag_ref[...], sum_finish(3))
    dx_ref[...] = d_middle[...] + x_part

    def gain_plane_copy(j):
        return remote(gain_own, gain_plane.at[c], gp_send.at[j], gp_recv.at[j], partner(j), z)

    def gain_copy(d):
        return remote(gain_all.at[z], gain_all.at[z], gz_send.at[d], gz_recv.at[d], c, lax.rem(z + d, planes))

    for j in range(1, n):
        launch(in_plane, lambda j=j: gain_plane_copy(j))
    gain_plane[c] = gain_own[...]
    own_sum(3)
    hand_out(1)
    for j in range(1, n):
        gain_plane_copy(j).wait_recv()
    total = gain_plane[0]
    for i in range(1, n):
        total = total + gain_plane[i]
    gain_all[z] = total
    for d in range(1, planes):
        launch(along, lambda d=d: gain_copy(d))
    own_sum(4)
    for d in range(1, planes):
        origin = gain_all.at[lax.rem(z + planes - d, planes)]
        remote(origin, origin, gz_send.at[d], gz_recv.at[d], c, z).wait_recv()
    total = gain_all[0]
    for i in range(1, planes):
        total = total + gain_all[i]
    gains_ref[...] = total

    hand_receive(0)
    own_sum(5)
    hand_out(2)
    drain(along)
    hand_receive(1)
    hand_receive(2)
    drain(in_plane)


def finish_kernel(
    n, head, out_in, dx_in, gains_in, got_ab, got_co, got_qkv,
    out_ref, dx_ref, ag_ref, q_ref, k_ref, v_ref, qg_ref, kg_ref, o_ref, fg_ref, g_ref, u_ref, d_ref,
):
    out_ref[...] = out_in[...]
    dx_ref[...] = dx_in[...]
    ag_ref[...] = gains_in[0:1, :]
    fg_ref[...] = gains_in[1:2, :]
    qg_ref[...] = gains_in[2:3, 0:head]
    kg_ref[...] = gains_in[3:4, 0:head]
    qw, kw = q_ref.shape[1] // n, k_ref.shape[1] // n
    fw = g_ref.shape[1] // n
    pw = fw // 3
    thirds = ((got_ab, 0), (got_ab, fw), (got_co, 0))
    for i in range(n):
        q_ref[:, i * qw:(i + 1) * qw] = got_qkv[i, :, 0:qw].astype(f32)
        k_ref[:, i * kw:(i + 1) * kw] = got_qkv[i, :, qw:qw + kw].astype(f32)
        v_ref[:, i * kw:(i + 1) * kw] = got_qkv[i, :, qw + kw:].astype(f32)
        o_ref[:, i * qw:(i + 1) * qw] = got_co[i, :, fw:].astype(f32)
        for t, (got, start) in enumerate(thirds):
            plane, unit = hidden_block(i, t)
            at = plane * (g_ref.shape[1] // 4) + unit * pw
            g_ref[:, at:at + pw] = got[i, :, start:start + pw].astype(f32)
            u_ref[:, at:at + pw] = got[i, :, start + pw:start + 2 * pw].astype(f32)
            d_ref[:, at:at + pw] = got[i, :, start + 2 * pw:start + 3 * pw].astype(f32)


def plane_device(
    layer_input,
    token_positions,
    attention_gain,
    query_weight,
    key_matrix,
    value_matrix,
    query_gain,
    key_norm_gain,
    output_weight,
    feedforward_gain,
    gate_weight,
    up_weight,
    down_weight,
    out_cotangent,
):
    n = lax.axis_size("ctx")
    planes = lax.axis_size("fsdp")
    block, width = layer_input.shape[1:]
    length = token_positions.shape[1]
    head = query_gain.shape[0]
    qw = query_weight.shape[1] // n
    kw = key_matrix.shape[1] // n
    fw = gate_weight.shape[1] // n
    group = qw // head
    per = block // planes
    half = head // 2
    inverse = np.power(rope_base, -np.arange(half) * 2.0 / head).astype(np.float32)
    inverse = np.concatenate([inverse, inverse])[None]
    steps = np.arange(block // 2)[:, None] * inverse.astype(np.float64)
    step_cos, step_sin = (jnp.asarray(f(steps).astype(np.float32)) for f in (np.cos, np.sin))
    inverse = jnp.asarray(inverse)
    vmem = pl.BlockSpec(memory_space=pltpu.VMEM)
    hbm = pl.BlockSpec(memory_space=pl.ANY)
    dma = pltpu.SemaphoreType.DMA
    sizes = (fw, fw, fw, qw, qw, 2 * kw)
    low = lambda *shape: pltpu.VMEM(shape, bf16)
    wide = lambda *shape: pltpu.VMEM(shape, f32)
    scratch = [
        low(width, qw + 2 * kw), low(3, width, 2 * fw // 3), low(qw, width), low(fw, width),
        low(planes * (output_weight.shape[0] // n), width),
        low(length, width), low(length, width), low(length, width),
        low(width, length), low(width, length), low(width, length),
        wide(length, head), wide(length, head), wide(length, head),
        wide(length, qw + kw), low(length, qw), low(length, kw), low(length, kw),
        low(kw, length), low(kw, length), low(n // 2, length, 2 * group * block), wide(n // 2, 1, 2 * group * block),
        wide(n // 2, head, 2 * group * block), low(length, qw), low(qw, length),
        low(length, fw), low(length, 2 * fw), low(length, qw + 2 * kw),
        wide(length, kw), wide(length, kw),
    ]
    scratch += [low(planes, n, per, size) for size in sizes]
    scratch += [low(planes + 1, n, per, size) for size in sizes]
    scratch += [low(n, per, sizes[m] + sizes[m + 1]) for m in (0, 2, 4)]
    scratch += [low(2, 4, block, width)] * 2 + [low(2, 3, block, width)] * 2 + [wide(2, block, width), wide(2, block, width)]
    scratch += [
        wide(block, width), wide(block, width), wide(8, width), wide(n, 8, width), wide(planes, 8, width),
        dma((13,)), dma((8, 6)), dma((8, planes)), dma((1, 7)), dma((1, 4)),
        dma((4, n)), dma((4, n)), dma((4, 4)), dma((4, 4)), dma((4, 4)), dma((4, 4)),
        dma((6, planes)), dma((6, planes + 1)), dma((3, n)), dma((3, n)), dma((n,)), dma((n,)),
        dma((planes,)), dma((planes,)),
    ]
    shapes = [
        jax.ShapeDtypeStruct((block, width), bf16),
        jax.ShapeDtypeStruct((block, width), f32),
        jax.ShapeDtypeStruct((8, width), f32),
    ] + [jax.ShapeDtypeStruct((n, per, sizes[m] + sizes[m + 1]), bf16) for m in (0, 2, 4)]
    results = pl.pallas_call(
        functools.partial(layer_kernel, n, planes, block, head, group, fw),
        out_shape=shapes,
        in_specs=[vmem] * 10 + [hbm] * 7,
        out_specs=[vmem] * len(shapes),
        scratch_shapes=scratch,
        compiler_params=pltpu.CompilerParams(
            collective_id=0, has_side_effects=True, vmem_limit_bytes=60 * 1024 * 1024),
    )(
        layer_input[0], out_cotangent[0], token_positions, inverse, step_cos, step_sin,
        attention_gain[None], feedforward_gain[None], query_gain[None], key_norm_gain[None],
        query_weight, key_matrix, value_matrix, output_weight, gate_weight, up_weight, down_weight,
    )
    plain = lambda rows, columns, kind=f32: jax.ShapeDtypeStruct((rows, columns), kind)
    finals = [
        plain(block, width, bf16), plain(block, width), plain(1, width),
        plain(per, n * qw), plain(per, n * kw), plain(per, n * kw), plain(1, head), plain(1, head),
        plain(per, n * qw), plain(1, width), plain(per, n * fw), plain(per, n * fw), plain(per, n * fw),
    ]
    done = pl.pallas_call(
        functools.partial(finish_kernel, n, head),
        out_shape=finals,
        in_specs=[vmem] * len(shapes),
        out_specs=[vmem] * len(finals),
    )(*results)
    out, dx, ag, q, k, v, qg, kg, o, fg, g, u, d = done
    return out[None], dx[None], ag[0], q, k, v, qg[0], kg[0], o.T, fg[0], g, u, d.T


def solution(mesh):
    in_specs = (
        P("fsdp", "ctx", None),
        P("fsdp", None),
        P(),
        P("fsdp", None),
        P("fsdp", None),
        P("fsdp", None),
        P(),
        P(),
        P("fsdp", None),
        P(),
        P("fsdp", None),
        P("fsdp", None),
        P("fsdp", None),
        P("fsdp", "ctx", None),
    )
    out_specs = (
        P("fsdp", "ctx", None),
        P("fsdp", "ctx", None),
        P(),
        P(("ctx", "fsdp"), None),
        P(("ctx", "fsdp"), None),
        P(("ctx", "fsdp"), None),
        P(),
        P(),
        P(None, ("ctx", "fsdp")),
        P(),
        P(("ctx", "fsdp"), None),
        P(("ctx", "fsdp"), None),
        P(None, ("ctx", "fsdp")),
    )

    def run(*arguments):
        n, planes = mesh.shape["ctx"], mesh.shape["fsdp"]
        key_heads = arguments[4].shape[1] // arguments[6].shape[0]
        whole_heads = n == 8 and planes == 4 and key_heads == n
        return jax.shard_map(
            plane_device if whole_heads else on_device,
            mesh=mesh, in_specs=in_specs, out_specs=out_specs, check_vma=False,
        )(*arguments)

    return run
```

```python
import functools

import jax
import jax.numpy as jnp
import numpy as np
from jax import lax
from jax.experimental import pallas as pl
from jax.experimental.pallas import tpu as pltpu
from jax.sharding import PartitionSpec as P

epsilon = 1e-06
rope_base = 1000000.0
masked_score = -1e30


def from_behind(block, axis, distance):
    devices = range(lax.axis_size(axis))
    route = [((i - distance) % len(devices), i) for i in devices]
    return lax.ppermute(block, axis, route)


def rotate(value_rows):
    half = value_rows.shape[-1] // 2
    return jnp.concatenate([-value_rows[..., half:], value_rows[..., :half]], -1)


def rotate_back(value_rows):
    half = value_rows.shape[-1] // 2
    return jnp.concatenate([value_rows[..., half:], -value_rows[..., :half]], -1)


def rope_tables(token_offsets, head_size):
    half = head_size // 2
    inverse = rope_base ** (-(jnp.arange(half).astype(jnp.float32) * 2.0) / head_size)
    angles = token_offsets.astype(jnp.float32)[:, None] * inverse[None, :]
    cosine = jnp.cos(angles)
    sine = jnp.sin(angles)
    return (jnp.concatenate([cosine, cosine], -1), jnp.concatenate([sine, sine], -1))


def norm_scale(value_rows):
    return lax.rsqrt(jnp.mean(value_rows * value_rows, -1, keepdims=True) + epsilon)


def norm_back(value_rows, scale, gain, grad):
    weighted = grad * gain
    inner = jnp.mean(weighted * value_rows, -1, keepdims=True)
    result = scale * weighted - value_rows * scale * scale * scale * inner
    gain_part = jnp.sum((grad * value_rows * scale).reshape(-1, gain.shape[0]), 0)
    return (result, gain_part)


def row_products(left, pieces):
    return tuple((jnp.dot(left, piece, preferred_element_type=jnp.float32) for piece in pieces))


def column_products(rights, pieces):
    total = jnp.einsum("tc,rc->tr", rights[0], pieces[0], preferred_element_type=jnp.float32)
    for right, piece in zip(rights[1:], pieces[1:]):
        total = total + jnp.einsum("tc,rc->tr", right, piece, preferred_element_type=jnp.float32)
    return total


def on_device(
    layer_input,
    token_positions,
    attention_gain,
    query_weight,
    key_matrix,
    value_matrix,
    query_gain,
    key_norm_gain,
    output_weight,
    feedforward_gain,
    gate_weight,
    up_weight,
    down_weight,
    out_cotangent,
):
    hidden_in = layer_input[0].astype(jnp.float32)
    count = hidden_in.shape[0]
    head_size = query_gain.shape[0]
    query_width = query_weight.shape[1]
    key_width = key_matrix.shape[1]
    inner_width = gate_weight.shape[1]
    heads = query_width // head_size
    key_heads = key_width // head_size
    group = heads // key_heads
    scale = head_size ** (-0.5)
    cycles = lax.axis_size("ctx")
    own_index = lax.axis_index("ctx")
    sequence_pos = token_positions[0]
    token_offsets = lax.dynamic_slice_in_dim(sequence_pos, own_index * count, count)
    cosine, sine = rope_tables(token_offsets, head_size)
    cosine = cosine[:, None, :]
    sine = sine[:, None, :]
    first_scale = norm_scale(hidden_in)
    first = (hidden_in * first_scale * attention_gain).astype(jnp.bfloat16)
    query_raw, key_unnormed, value_unnormed = row_products(
        first,
        (
            lax.all_gather(query_weight, "fsdp", axis=0, tiled=True),
            lax.all_gather(key_matrix, "fsdp", axis=0, tiled=True),
            lax.all_gather(value_matrix, "fsdp", axis=0, tiled=True),
        ),
    )
    query_heads = query_raw.reshape(count, heads, head_size)
    query_scale = norm_scale(query_heads)
    query_normed = query_heads * query_scale * query_gain
    query_rot = query_normed * cosine + rotate(query_normed) * sine
    query_grouped = (
        query_rot.reshape(count, key_heads, group, head_size)
        .transpose(1, 2, 0, 3)
        .astype(jnp.bfloat16)
    )
    key_heads_raw = key_unnormed.reshape(count, key_heads, head_size)
    key_scale = norm_scale(key_heads_raw)
    key_normed = key_heads_raw * key_scale * key_norm_gain
    key_low = (
        (key_normed * cosine + rotate(key_normed) * sine)
        .reshape(count, key_width)
        .astype(jnp.bfloat16)
    )
    value_low = value_unnormed.astype(jnp.bfloat16)
    rowmax = jnp.full((key_heads, group, count), masked_score, jnp.float32)
    keys_piece = lax.all_gather(key_low, "ctx", axis=0, tiled=True).reshape(
        -1, key_heads, head_size
    )
    values_piece = lax.all_gather(value_low, "ctx", axis=0, tiled=True).reshape(
        -1, key_heads, head_size
    )
    key_pos = sequence_pos
    allowed = token_offsets[:, None] >= key_pos[None, :]
    scores = (
        jnp.einsum("kgtd,skd->kgts", query_grouped, keys_piece, preferred_element_type=jnp.float32)
        * scale
    )
    scores = jnp.where(allowed, scores, masked_score)
    newmax = jnp.maximum(rowmax, jnp.max(scores, -1))
    weights = jnp.where(allowed, jnp.exp(scores - newmax[..., None]), 0.0)
    accum = jnp.einsum(
        "kgts,skd->kgtd",
        weights.astype(jnp.bfloat16),
        values_piece,
        preferred_element_type=jnp.float32,
    )
    rowsum = jnp.sum(weights, -1)
    accum, rowmax, rowsum = (accum, newmax, rowsum)
    normalized = accum / rowsum[..., None]
    logsum = rowmax + jnp.log(rowsum)
    attention_low = (
        normalized.transpose(2, 0, 1, 3).reshape(count, query_width).astype(jnp.bfloat16)
    )
    output_whole = lax.all_gather(output_weight, "fsdp", axis=0, tiled=True)
    branch_out = jnp.dot(attention_low, output_whole, preferred_element_type=jnp.float32)
    middle = hidden_in + branch_out
    second_scale = norm_scale(middle)
    second = (middle * second_scale * feedforward_gain).astype(jnp.bfloat16)
    gate, up = row_products(
        second,
        (
            lax.all_gather(gate_weight, "fsdp", axis=0, tiled=True),
            lax.all_gather(up_weight, "fsdp", axis=0, tiled=True),
        ),
    )
    sigmoid_gate = jax.nn.sigmoid(gate)
    silu_gate = gate * sigmoid_gate
    hidden_low = (silu_gate * up).astype(jnp.bfloat16)
    (down_out,) = row_products(
        hidden_low, (lax.all_gather(down_weight, "fsdp", axis=0, tiled=True),)
    )
    layer_output = (middle + down_out).astype(jnp.bfloat16)[None]
    cotangent = out_cotangent[0]
    hidden_grad = column_products(
        (cotangent,), lax.all_gather((down_weight,), "fsdp", axis=0, tiled=True)
    )
    up_low = (hidden_grad * silu_gate).astype(jnp.bfloat16)
    gate_low = (hidden_grad * up * sigmoid_gate * (1.0 + gate * (1.0 - sigmoid_gate))).astype(
        jnp.bfloat16
    )
    second_grad = column_products(
        (gate_low, up_low), lax.all_gather((gate_weight, up_weight), "fsdp", axis=0, tiled=True)
    )
    middle_part, feedforward_part = norm_back(middle, second_scale, feedforward_gain, second_grad)
    middle_grad = cotangent.astype(jnp.float32) + middle_part
    middle_low = middle_grad.astype(jnp.bfloat16)
    attention_grad = jnp.einsum(
        "tc,rc->tr", middle_low, output_whole, preferred_element_type=jnp.float32
    )
    attention_grad_low = attention_grad.astype(jnp.bfloat16)
    mixed_grad = attention_grad_low.reshape(count, key_heads, group, head_size).transpose(
        1, 2, 0, 3
    )
    delta = jnp.sum(mixed_grad.astype(jnp.float32) * normalized, -1)

    def cycle_step(index, carry):
        keys_held, values_held, key_acc, value_acc, query_acc = carry
        anchor = (own_index - index) % cycles
        key_pos = lax.dynamic_slice_in_dim(sequence_pos, anchor * count, count)
        keys_piece = keys_held.astype(jnp.bfloat16).reshape(count, key_heads, head_size)
        values_piece = values_held.astype(jnp.bfloat16).reshape(count, key_heads, head_size)
        allowed = token_offsets[:, None] >= key_pos[None, :]
        scores = (
            jnp.einsum(
                "kgtd,skd->kgts", query_grouped, keys_piece, preferred_element_type=jnp.float32
            )
            * scale
        )
        probs = jnp.where(allowed, jnp.exp(scores - logsum[..., None]), 0.0)
        value_acc = value_acc + jnp.einsum(
            "kgts,kgtd->skd",
            probs.astype(jnp.bfloat16),
            mixed_grad,
            preferred_element_type=jnp.float32,
        ).reshape(count, key_width)
        prob_grad = jnp.einsum(
            "kgtd,skd->kgts", mixed_grad, values_piece, preferred_element_type=jnp.float32
        )
        score_grad = (probs * (prob_grad - delta[..., None])).astype(jnp.bfloat16)
        query_acc = (
            query_acc
            + jnp.einsum(
                "kgts,skd->kgtd", score_grad, keys_piece, preferred_element_type=jnp.float32
            )
            * scale
        )
        key_acc = (
            key_acc
            + jnp.einsum(
                "kgts,kgtd->skd", score_grad, query_grouped, preferred_element_type=jnp.float32
            ).reshape(count, key_width)
            * scale
        )
        moved = (
            from_behind(keys_held.astype(jnp.bfloat16), "ctx", 1).astype(keys_held.dtype),
            from_behind(values_held.astype(jnp.bfloat16), "ctx", 1).astype(values_held.dtype),
            from_behind(key_acc.astype(jnp.bfloat16), "ctx", 1).astype(key_acc.dtype),
            from_behind(value_acc.astype(jnp.bfloat16), "ctx", 1).astype(value_acc.dtype),
        )
        return (moved[0], moved[1], moved[2], moved[3], query_acc)

    start_cycle = (
        key_low.astype(jnp.float32),
        value_low.astype(jnp.float32),
        jnp.zeros((count, key_width), jnp.float32),
        jnp.zeros((count, key_width), jnp.float32),
        jnp.zeros((key_heads, group, count, head_size), jnp.float32),
    )
    cycle_done = lax.fori_loop(0, cycles, cycle_step, start_cycle)
    key_acc = cycle_done[2]
    value_acc = cycle_done[3]
    query_acc = cycle_done[4]
    query_rot_grad = query_acc.transpose(2, 0, 1, 3).reshape(count, heads, head_size)
    query_normed_grad = query_rot_grad * cosine + rotate_back(query_rot_grad * sine)
    query_heads_grad, query_part = norm_back(
        query_heads, query_scale, query_gain, query_normed_grad
    )
    query_low_grad = query_heads_grad.reshape(count, query_width).astype(jnp.bfloat16)
    key_rot_grad = key_acc.reshape(count, key_heads, head_size)
    key_normed_grad = key_rot_grad * cosine + rotate_back(key_rot_grad * sine)
    key_heads_grad, key_part = norm_back(key_heads_raw, key_scale, key_norm_gain, key_normed_grad)
    key_low_grad = key_heads_grad.reshape(count, key_width).astype(jnp.bfloat16)
    value_low_grad = value_acc.astype(jnp.bfloat16)
    first_grad = column_products(
        (query_low_grad, key_low_grad, value_low_grad),
        lax.all_gather((query_weight, key_matrix, value_matrix), "fsdp", axis=0, tiled=True),
    )
    input_part, attention_part = norm_back(hidden_in, first_scale, attention_gain, first_grad)
    input_gradient = (middle_grad + input_part)[None]
    rights_first = jnp.concatenate([query_low_grad, key_low_grad, value_low_grad], 1)
    rights_second = jnp.concatenate([gate_low, up_low], 1)
    pairs = (
        (first, rights_first),
        (second, rights_second),
        (middle_low, attention_low),
        (cotangent, hidden_low),
    )
    parts = []
    for left, right in pairs:
        parts.append(jnp.einsum("tr,tc->rc", left, right, preferred_element_type=jnp.float32))
    sums = lax.psum_scatter(
        jnp.concatenate(parts, 1), ("ctx", "fsdp"), scatter_dimension=0, tiled=True
    )
    edges = [0, query_width, query_width + key_width, query_width + 2 * key_width]
    edges = edges + [edges[3] + inner_width, edges[3] + 2 * inner_width]
    edges = edges + [edges[5] + query_width, edges[5] + query_width + inner_width]
    query_gradient = sums[:, edges[0] : edges[1]]
    key_gradient = sums[:, edges[1] : edges[2]]
    value_gradient = sums[:, edges[2] : edges[3]]
    gate_gradient = sums[:, edges[3] : edges[4]]
    up_gradient = sums[:, edges[4] : edges[5]]
    output_gradient = sums[:, edges[5] : edges[6]].T
    down_gradient = sums[:, edges[6] : edges[7]].T
    attention_total, query_total, key_total, feedforward_total = lax.psum(
        (attention_part, query_part, key_part, feedforward_part), ("ctx", "fsdp")
    )
    return (
        layer_output,
        input_gradient,
        attention_total,
        query_gradient,
        key_gradient,
        value_gradient,
        query_total,
        key_total,
        output_gradient,
        feedforward_total,
        gate_gradient,
        up_gradient,
        down_gradient,
    )


MESH = pl.DeviceIdType.MESH
f32 = jnp.float32
bf16 = jnp.bfloat16


def dot(left, right):
    return jnp.dot(left, right, preferred_element_type=f32)


def dot_nt(left, right):
    return lax.dot_general(left, right, (((1,), (1,)), ((), ())), preferred_element_type=f32)


def dot_tn(left, right):
    return lax.dot_general(left, right, (((0,), (0,)), ((), ())), preferred_element_type=f32)


def hidden_block(device, third):
    def plane(i, t):
        return ((3, 1, 2), (0, 2, 1), (0, 3, 2), (3, 0, 1))[i // 4 * 2 + i % 2][t]

    own = plane(device, third)
    return own, sum(plane(i, t) == own for i in range(device) for t in range(3))


def layer_kernel(
    n, planes, block, head, group, fw,
    x_ref, dy_ref, pos_row, inverse_ref, step_cos, step_sin, ag_ref, fg_ref, qg_ref, kg_ref,
    wq, wk, wv, wo, wg, wu, wd,
    out_ref, dx_ref, gains_ref, got_ab, got_co, got_qkv,
    w_qkv, w_gu, w_out, w_down, t_out,
    first, dy_all, second, first_t, dy_t, second_t,
    positions, cosine, sine,
    raw, queries, keys, values, keys_t, values_t, probs, sums, mixed_t, mixed_low, mixed_low_t,
    hidden, d_gu, d_qkv, dk_acc, dv_acc,
    stage_a, stage_b, stage_c, stage_out, stage_q, stage_kv,
    land_a, land_b, land_c, land_out, land_q, land_kv,
    own_ab, own_co, own_qkv,
    rs_sa, rs_ra, rs_sb, rs_rb, rs_kept, rs_acc,
    middle, d_middle, gain_own, gain_plane, gain_all,
    local_sem, wz_send, wz_recv, hand_send, hand_recv,
    ag_send, ag_recv, ra_send, ra_recv, rb_send, rb_recv,
    zr_send, zr_recv, aa_send, aa_recv, gp_send, gp_recv, gz_send, gz_recv,
):
    c = lax.axis_index("ctx")
    z = lax.axis_index("fsdp")
    dmid = first
    cy, cx, ck = lax.div(c, 4), lax.rem(lax.div(c, 2), 2), lax.rem(c, 2)
    ci = lax.rem(c, 4)
    sign = 1 - 2 * ck
    qw, kw = group * head, head
    pw = 128
    thirds = fw // pw
    width = x_ref.shape[1]
    scale = head ** (-0.5)
    log2e = 1.4426950408889634
    gots = (got_ab, got_co, got_qkv)
    owns = (own_ab, own_co, own_qkv)
    stages = (stage_a, stage_b, stage_c, stage_out, stage_q, stage_kv)
    lands = (land_a, land_b, land_c, land_out, land_q, land_kv)

    def partner(j):
        y = lax.rem(cy + lax.div(j, 4), 2)
        x = lax.rem(cx + lax.rem(lax.div(j, 2), 2), 2)
        k = lax.rem(ck + lax.rem(j, 2), 2)
        return y * 4 + x * 2 + k

    def chip(slot):
        return lax.rem(cy + lax.div(slot, 2), 2) * 2 + lax.rem(cx + lax.rem(slot, 2), 2)

    def rows(start, size):
        return pl.ds(pl.multiple_of(start * size, size), size)

    def remote(src, dst, send, recv, ctx, plane):
        return pltpu.make_async_remote_copy(
            src_ref=src, dst_ref=dst, send_sem=send, recv_sem=recv,
            device_id={"ctx": ctx, "fsdp": plane}, device_id_type=MESH,
        )

    in_plane, along, weight_sends = [], [], []

    def launch(started, copy, when=None):
        if when is None:
            copy().start()
        else:
            pl.when(when)(lambda: copy().start())
        started.append((copy, when))

    def drain(started):
        for copy, when in started:
            if when is None:
                copy().wait_send()
            else:
                pl.when(when)(lambda copy=copy: copy().wait_send())
        started.clear()

    def pick(values):
        return sum(jnp.where(c == i, value, 0) for i, value in enumerate(values))

    unit_plane = [pick([hidden_block(i, t)[0] for i in range(n)]) for t in range(thirds)]
    unit_block = [pick([hidden_block(i, t)[1] for i in range(n)]) for t in range(thirds)]
    plane_blocks = wd.shape[0] // pw

    own_rows = wq.shape[0]
    out_rows = wo.shape[0] // n

    def own_slices():
        mine = rows(z, own_rows)
        pairs = [
            (wq.at[:, rows(c, qw)], w_qkv.at[mine, 0:qw]),
            (wk.at[:, rows(c, kw)], w_qkv.at[mine, qw:qw + kw]),
            (wv.at[:, rows(c, kw)], w_qkv.at[mine, qw + kw:qw + 2 * kw]),
            (wo.at[rows(c, out_rows)], t_out.at[rows(z, out_rows)]),
        ]
        for t in range(thirds):
            at = 2 * pw * t
            unit = unit_plane[t] * plane_blocks + unit_block[t]
            pairs.append((wg.at[:, rows(unit, pw)], w_gu.at[mine, at:at + pw]))
            pairs.append((wu.at[:, rows(unit, pw)], w_gu.at[mine, at + pw:at + 2 * pw]))
        return pairs

    local = [pltpu.make_async_copy(src, dst, local_sem.at[i]) for i, (src, dst) in enumerate(own_slices())]
    for copy in local:
        copy.start()

    def own_down(t):
        return pltpu.make_async_copy(
            wd.at[rows(unit_block[t], pw)], w_down.at[t * pw:(t + 1) * pw], local_sem.at[4 + 2 * thirds + t])

    holds = [unit_plane[t] == z for t in range(thirds)]
    for t in range(thirds):
        pl.when(holds[t])(lambda t=t: own_down(t).start())

    for land in lands:
        @pl.when(z == 0)
        def _(land=land):
            land[0] = jnp.zeros(land.shape[1:], bf16)

        @pl.when(z == planes - 1)
        def _(land=land):
            land[planes] = jnp.zeros(land.shape[1:], bf16)

    barrier = pltpu.get_barrier_semaphore()
    for j in range(1, n):
        pl.semaphore_signal(barrier, inc=1, device_id={"ctx": partner(j), "fsdp": z}, device_id_type=MESH)
    for d in range(1, planes):
        pl.semaphore_signal(
            barrier, inc=1, device_id={"ctx": c, "fsdp": lax.rem(z + d, planes)}, device_id_type=MESH)
    x = x_ref[...].astype(f32)
    x_scale = lax.rsqrt(jnp.mean(x * x, -1, keepdims=True) + epsilon)
    first[rows(c, block)] = (x * x_scale * ag_ref[...]).astype(bf16)
    dy_all[rows(c, block)] = dy_ref[...]
    for copy in local[:3]:
        copy.wait()
    pl.semaphore_wait(barrier, n + planes - 2)

    def inside(t):
        return jnp.logical_and(t >= 0, t < planes)

    weights = [
        (lambda o: w_qkv.at[rows(o, own_rows)], None),
        (lambda o: t_out.at[rows(o, out_rows)], 0),
    ]
    for t in range(thirds):
        weights.append((lambda o, t=t: w_gu.at[rows(o, own_rows), 2 * pw * t:2 * pw * (t + 1)], None))
        weights.append((lambda o, t=t: w_down.at[t * pw:(t + 1) * pw], None))

    def weight_copy(w, slot, origin, target):
        part = weights[w][0](origin)
        return remote(part, part, wz_send.at[w, slot], wz_recv.at[w, origin], c, target)

    def from_plane(w, origin):
        return origin == unit_plane[(w - 3) // 2] if w >= 3 and w % 2 else None

    def both(one, other):
        return one if other is None else jnp.logical_and(one, other)

    def hand_split(origin, valid):
        mine = 2 * origin + cy == c
        return jnp.logical_and(valid, jnp.logical_not(mine)), jnp.logical_and(valid, mine)

    def weight_start(w):
        for side in range(2):
            d = sign * (1 - 2 * side)
            launch(
                weight_sends, lambda side=side, d=d: weight_copy(w, side, z, z + d),
                both(inside(z + d), from_plane(w, z)))
        if weights[w][1] is not None:
            hand_over(w, z, 0, *hand_split(z, True))

    def hand_target(h):
        return lambda i: w_out.at[rows(i, out_rows)]

    def hand_copy(w, origin, slot):
        h = weights[w][1]
        return remote(
            weights[w][0](origin), hand_target(h)(ci), hand_send.at[h, slot], hand_recv.at[h, ci], 2 * origin + cy, z)

    def hand_over(w, origin, slot, away, here):
        launch(in_plane, lambda: hand_copy(w, origin, slot), away)

        @pl.when(here)
        def _():
            hand_target(weights[w][1])(ci)[...] = weights[w][0](origin)[...]

    def hand_arrive(w):
        h = weights[w][1]
        for i in range(4):
            @pl.when(4 * ck + i != c)
            def _(i=i):
                part = hand_target(h)(i)
                remote(part, part, hand_send.at[h, 0], hand_recv.at[h, i], c, z).wait_recv()

    hops = {}
    for w in range(len(weights)):
        for d in range(1, planes):
            for side, way in enumerate((1, -1)):
                origin = z - way * d
                valid = both(inside(origin), from_plane(w, origin))
                passed = jnp.logical_and(valid, inside(z + way))
                split = None if weights[w][1] is None else hand_split(origin, valid)
                hops[w, d, side] = origin, z + way, valid, passed, split

    def weight_hop(w, d):
        for side in range(2):
            origin, following, valid, passed, split = hops[w, d, side]
            pl.when(valid)(lambda: weight_copy(w, 0, origin, z).wait_recv())
            if d < planes - 1:
                launch(
                    weight_sends,
                    lambda side=side, origin=origin, following=following: weight_copy(
                        w, 2 * d + side, origin, following),
                    passed)
            if split is not None:
                hand_over(w, origin, 2 * d - 1 + side, *split)

    def gather_copy(buf, g, j, send, origin, target):
        part = buf.at[rows(origin, block)]
        return remote(part, part, ag_send.at[g, send], ag_recv.at[g, j], target, z)

    def gather_start(buf, g):
        for j in (1, 2 + 2 * ck, 4 - 2 * ck):
            launch(in_plane, lambda j=j: gather_copy(buf, g, j, j, c, partner(j)))

    def gather_half(buf, g, j):
        half = block // 2
        part = buf.at[pl.ds(pl.multiple_of(partner(j) * block + (half if j == 2 else 0), half), half)]
        at = 0 if j == 2 else 6
        return remote(part, part, ag_send.at[g, at], ag_recv.at[g, at], partner(6 - j), z)

    def gather_diagonal(buf, g):
        half = block // 2
        for at in (6, 0):
            part = buf.at[pl.ds(pl.multiple_of(partner(6) * block + (0 if at == 6 else half), half), half)]
            remote(part, part, ag_send.at[g, at], ag_recv.at[g, at], c, z).wait_recv()

    def gather_forward(buf, g, j):
        return gather_copy(buf, g, j + 1, j + 1, partner(j), partner(1))

    def gather_take(buf, g, j):
        if j == 6:
            gather_diagonal(buf, g)
        else:
            gather_copy(buf, g, j, j, partner(j), c).wait_recv()
            gather_half(buf, g, j).start()
        gather_forward(buf, g, j).start()

    def gather_sent(buf, g):
        for j in (2, 4, 6):
            in_plane.append((lambda j=j: gather_forward(buf, g, j), None))
            if j < 6:
                in_plane.append((lambda j=j: gather_half(buf, g, j), None))

    def gather_finish(buf, g):
        for j in (2, 4, 6):
            gather_take(buf, g, j)
        gather_sent(buf, g)
        for j in (1, 3, 5, 7):
            gather_copy(buf, g, j, j, partner(j), c).wait_recv()

    def gather_step(buf, g, slot):
        @pl.when(slot == 1)
        def _():
            gather_take(buf, g, 2)
            gather_take(buf, g, 4)

        pl.when(slot == 3)(lambda: gather_take(buf, g, 6))
        gather_copy(buf, g, 2 * slot + 1, 0, partner(2 * slot + 1), c).wait_recv()

    def sum_pair_copy(s, slot):
        return remote(rs_sa.at[s % 2, slot], rs_ra.at[s % 2, slot], ra_send.at[s, slot], ra_recv.at[s, slot], partner(1), z)

    def sum_chip_copy(s, slot):
        return remote(
            rs_sb.at[s % 2, slot - 1], rs_rb.at[s % 2, slot - 1], rb_send.at[s, slot], rb_recv.at[s, slot], partner(2 * slot), z)

    def sum_half_copy(s, slot):
        half = block // 2
        at = pl.ds(pl.multiple_of((slot - 1) * half, half), half)
        return remote(
            rs_sb.at[s % 2, 2, at], rs_rb.at[s % 2, 2, at], rb_send.at[s, 6 - 3 * slot], rb_recv.at[s, 6 - 3 * slot],
            partner(6 - 2 * slot), z)

    def sum_slot(p):
        return jnp.where(p == 0, 3, jnp.where(p == 1, 2 - ck, jnp.where(p == 2, 1 + ck, 0)))

    def sum_start(s, left, partial, prepare=None, ready=None, during=()):
        if prepare is not None:
            for step in prepare:
                step(chip(sum_slot(0)))
        if ready is not None:
            ready()

        def body(p, carry):
            slot = sum_slot(p)
            at = [rows(partner(2 * slot + 1), block), rows(partner(2 * slot), block)]
            both = partial(jnp.concatenate([left[i] for i in at], 0))
            rs_sa[s % 2, slot] = both[:block].astype(bf16)
            sum_pair_copy(s, slot).start()
            rs_kept[lax.rem(p, 2)] = both[block:]

            def pair_sum(q):
                before = sum_slot(q)
                sum_pair_copy(s, before).wait_recv()
                rs_sb[s % 2, before - 1] = (
                    rs_kept[lax.rem(q, 2)] + rs_ra[s % 2, before].astype(f32)).astype(bf16)

            def chip_send(q):
                before = sum_slot(q)
                half = block // 2
                at = pl.ds(pl.multiple_of((before - 1) * half, half), half)
                sum_half_copy(s, before).wait_recv()
                rs_sb[s % 2, before - 1, at] = (
                    rs_sb[s % 2, before - 1, at].astype(f32) + rs_rb[s % 2, 2, at].astype(f32)).astype(bf16)
                sum_chip_copy(s, before).start()

            early = prepare is not None and len(prepare) > 1

            @pl.when(p == 1)
            def _():
                pair_sum(0)
                sum_half_copy(s, 1).start()
                sum_half_copy(s, 2).start()

            @pl.when(p == 2 if early else p > 1)
            def _():
                pair_sum(p - 1)
                chip_send(p - 1)

            if prepare is not None:
                @pl.when(p < 3)
                def _():
                    prepare[0](chip(sum_slot(p + 1)))

            if early:
                @pl.when(p == 2)
                def _():
                    pair_sum(2)
                    chip_send(2)

                @pl.when(p < 3)
                def _():
                    for step in prepare[1:]:
                        step(chip(sum_slot(p + 1)))

            for k, poll in enumerate(during):
                pl.when(p == k)(poll)
            return carry

        lax.fori_loop(0, 4, body, 0)
        for slot in range(4):
            in_plane.append((lambda slot=slot: sum_pair_copy(s, slot), None))
        for slot in (1, 2):
            in_plane.append((lambda slot=slot: sum_half_copy(s, slot), None))
            in_plane.append((lambda slot=slot: sum_chip_copy(s, slot), None))
        sum_pair_copy(s, 0).wait_recv()
        rs_acc[s % 2] = rs_kept[1] + rs_ra[s % 2, 0].astype(f32)

    def sum_finish(s):
        total = rs_acc[s % 2]
        for slot in (1, 2):
            sum_chip_copy(s, slot).wait_recv()
            total = total + rs_rb[s % 2, slot - 1].astype(f32)
        return total

    per = block // planes

    at_edge = jnp.logical_or(z == 0, z == planes - 1)
    edge_targets = [jnp.where(z == 0, planes - 1 - k, k) for k in range(planes - 1)]

    def weight_grad(m, parts):
        def body(i, carry):
            at = 0
            for left, right in parts:
                value = right()
                grad = dot(left[rows(i, 4 * block)], value)
                for k in range(4):
                    for t in range(planes):
                        start = k * block + t * per
                        stages[m][t, 4 * i + k, :, at:at + value.shape[1]] = grad[start:start + per].astype(bf16)
                at += value.shape[1]
            return carry

        lax.fori_loop(0, n // 4, body, 0)
        grad_send(m)

    def grad_send(m):
        for t in edge_targets:
            launch(along, lambda t=t: grad_copy(m, t), at_edge)

    def grad_copy(m, t):
        way = jnp.where(z < t, 1, -1)
        last = z + way == t
        slot = jnp.where(jnp.logical_and(last, way < 0), planes, t)
        return remote(
            stages[m].at[t], lands[m].at[slot], zr_send.at[m, t], zr_recv.at[m, slot], c, z + way)

    def grad_arrive(m, slot):
        part = lands[m].at[slot]
        remote(part, part, zr_send.at[m, 0], zr_recv.at[m, slot], c, z).wait_recv()

    def grad_pass(m, t, valid):
        @pl.when(valid)
        def _():
            grad_arrive(m, t)
            stages[m][t] = stages[m][t] + lands[m][t]

        launch(along, lambda: grad_copy(m, t), valid)

    is_low, is_high = z == 1, z == planes - 2

    def grad_near_far(m):
        grad_pass(m, 3, is_low)
        grad_pass(m, 0, is_high)

    def grad_near_inner(m):
        grad_pass(m, 2, is_low)
        grad_pass(m, 1, is_high)

    def grad_near(m):
        grad_near_far(m)
        grad_near_inner(m)

    def grad_far(m):
        grad_pass(m, 3, is_high)
        grad_pass(m, 0, is_low)

    def owner_copy(g, j):
        return remote(owns[g].at[partner(j)], gots[g].at[c], aa_send.at[g, j], aa_recv.at[g, j], partner(j), z)

    def own_sum(m):
        pl.when(z > 0)(lambda: grad_arrive(m, z))
        pl.when(z < planes - 1)(lambda: grad_arrive(m, planes))
        total = stages[m][z].astype(f32) + lands[m][z].astype(f32) + lands[m][planes].astype(f32)
        first_size = stages[m // 2 * 2].shape[3]
        if m % 2:
            owns[m // 2][:, :, first_size:] = total.astype(bf16)
        else:
            owns[m // 2][:, :, :first_size] = total.astype(bf16)

    def hand_out(g):
        for j in (2 + 2 * ck, 3 + 2 * ck, 4 - 2 * ck, 5 - 2 * ck, 6, 7, 1):
            launch(in_plane, lambda j=j: owner_copy(g, j))
        gots[g][c] = owns[g][c]

    def hand_receive(g):
        for j in range(1, n):
            owner_copy(g, j).wait_recv()

    weight_start(0)
    gather_start(first, 0)
    for copy in local[3:]:
        copy.wait()
    for t in range(thirds):
        pl.when(holds[t])(lambda t=t: own_down(t).wait())

    spread = jnp.broadcast_to(pos_row[...].astype(f32), (head, pos_row.shape[1]))
    positions[...] = spread.T
    side = jnp.where(lax.broadcasted_iota(jnp.int32, (1, head), 1) < head // 2, -1.0, 1.0)

    def table(i, carry):
        run = step_cos.shape[0]
        at = rows(i, run)
        start = positions[pl.ds(pl.multiple_of(i * run, run), 1)] * inverse_ref[...]
        start_cos, start_sin = jnp.cos(start), jnp.sin(start)
        cosine[at] = start_cos * step_cos[...] - start_sin * step_sin[...]
        sine[at] = (start_sin * step_cos[...] + start_cos * step_sin[...]) * side
        return carry

    def turn_over(src, dst):
        def body(i, carry):
            at = rows(i, block)
            dst[:, at] = src[at].T
            return carry

        lax.fori_loop(0, n, body, 0)

    lax.fori_loop(0, 2 * n, table, 0)
    weight_hop(0, 1)
    gather_finish(first, 0)
    weight_hop(0, 2)
    weight_start(1)
    gather_start(dy_all, 1)
    turn_over(first, first_t)
    weight_hop(0, 3)
    weight_start(2)
    weight_start(3)

    def turn(value, at):
        return value * cosine[at] + pltpu.roll(value, head // 2, 1) * sine[at]

    def turn_back(grad, at):
        return grad * cosine[at] - pltpu.roll(grad, head // 2, 1) * sine[at]

    def project(i, carry):
        at = rows(i, 2 * block)
        result = dot(first[at], w_qkv[...])
        raw[at] = result[:, :qw + kw]
        low_values = result[:, qw + kw:].astype(bf16)
        values[at] = low_values
        values_t[:, at] = low_values.T
        for h in range(group + 1):
            part = result[:, h * head:(h + 1) * head]
            inv = lax.rsqrt(jnp.mean(part * part, -1, keepdims=True) + epsilon)
            gain = qg_ref[...] if h < group else kg_ref[...]
            turned = turn(part * inv * gain, at)
            if h < group:
                queries[at, h * head:(h + 1) * head] = (turned * (scale * log2e)).astype(bf16)
            else:
                low_keys = turned.astype(bf16)
                keys[at] = low_keys
                keys_t[:, at] = low_keys.T
        return carry

    lax.fori_loop(0, n // 4, project, 0)
    weight_hop(1, 1)
    lax.fori_loop(n // 4, n // 2, project, 0)
    weight_hop(1, 2)
    gather_finish(dy_all, 1)

    def stack(ref, at):
        return jnp.concatenate([ref[at, h * head:(h + 1) * head] for h in range(group)], 0)

    def attend(place, h):
        at = rows(place, 2 * block)
        columns = slice(h * head, (h + 1) * head)
        tokens = slice(2 * h * block, 2 * (h + 1) * block)
        scores = dot_nt(keys[...], queries[at, columns])
        weight = jnp.concatenate(
            [jnp.exp2(jnp.where(
                positions[...] <= pos_row[:, rows(2 * place + k, block)].astype(f32),
                scores[:, k * block:(k + 1) * block], masked_score)) for k in range(2)], 1)
        inv = 1.0 / jnp.sum(weight, 0, keepdims=True)
        low_weight = weight.astype(bf16)
        probs[place, :, tokens] = low_weight
        sums[place, :, tokens] = inv
        result = dot(values_t[...], low_weight) * inv
        mixed_t[place, :, tokens] = result
        low_result = result.astype(bf16)
        mixed_low_t[columns, at] = low_result
        mixed_low[at, columns] = low_result.T

    def output_ready():
        weight_hop(1, 3)
        weight_start(4)
        weight_start(5)
        hand_arrive(1)
        drain(in_plane)

    def hop_third(t, d):
        weight_hop(2 + 2 * t, d)
        weight_hop(3 + 2 * t, d)

    sum_start(
        0, mixed_low, lambda left: dot(left, w_out[...]),
        [lambda place, h=h: attend(place, h) for h in range(group)], output_ready,
        (lambda: hop_third(0, 1), lambda: hop_third(0, 2), lambda: hop_third(1, 1)))
    weight_start(6)
    weight_start(7)
    mid = x_ref[...].astype(f32) + sum_finish(0)
    middle[...] = mid
    mid_scale = lax.rsqrt(jnp.mean(mid * mid, -1, keepdims=True) + epsilon)
    second[rows(c, block)] = (mid * mid_scale * fg_ref[...]).astype(bf16)
    gather_start(second, 2)
    hop_third(1, 2)
    turn_over(dy_all, dy_t)
    hop_third(0, 3)

    def feed(t, at):
        units, pair = slice(t * pw, (t + 1) * pw), 2 * pw * t
        both = dot(second[at], w_gu[:, pair:pair + 2 * pw])
        back = dot_nt(dy_all[at], w_down[units])
        gate, up = both[:, :pw], both[:, pw:]
        sig = 1.0 / (1.0 + jnp.exp(-gate))
        silu = gate * sig
        hidden[at, units] = (silu * up).astype(bf16)
        d_gu[at, pair:pair + pw] = (back * up * sig * (1.0 + gate * (1.0 - sig))).astype(bf16)
        d_gu[at, pair + pw:pair + 2 * pw] = (back * silu).astype(bf16)

    def feed_arriving(slot, carry):
        gather_step(second, 2, slot)
        at = rows(chip(slot), 2 * block)
        feed(0, at)
        second_t[:, at] = second[at].T
        pl.when(slot == 1)(lambda: hop_third(2, 1))
        pl.when(slot == 3)(lambda: hop_third(2, 2))
        return carry

    def third_grad(t):
        weight_grad(t, [
            (second_t, lambda: d_gu[:, 2 * pw * t:2 * pw * (t + 1)]),
            (dy_t, lambda: hidden[:, t * pw:(t + 1) * pw]),
        ])

    def feed_third(t):
        def body(i, carry):
            feed(t, rows(i, 2 * block))
            return carry

        lax.fori_loop(0, n // 2, body, 0)

    lax.fori_loop(0, n // 2, feed_arriving, 0)
    gather_sent(second, 2)
    hop_third(1, 3)
    third_grad(0)
    feed_third(1)
    hop_third(2, 3)
    sum_start(
        1, d_gu, lambda left: dot_nt(left, w_gu[...]),
        [lambda place: feed(thirds - 1, rows(place, 2 * block))])
    third_grad(1)
    third_grad(2)
    d_second = sum_finish(1)

    def norm_back(value, gain, grad):
        inv = lax.rsqrt(jnp.mean(value * value, -1, keepdims=True) + epsilon)
        weighted = grad * gain
        inner = jnp.mean(weighted * value, -1, keepdims=True)
        result = inv * weighted - value * (inv * inv * inv * inner)
        return result, jnp.sum(grad * value * inv, 0, keepdims=True)

    gain_own[...] = jnp.zeros_like(gain_own)
    part, gain_own[1:2, :] = norm_back(middle[...], fg_ref[...], d_second)
    d_mid = dy_ref[...].astype(f32) + part
    d_middle[...] = d_mid
    drain(in_plane)
    dmid[rows(c, block)] = d_mid.astype(bf16)
    gather_start(dmid, 3)
    sum_start(2, hidden, lambda left: dot(left, w_down[...]))
    drain(weight_sends)
    grad_near(0)

    dk_acc[...] = jnp.zeros_like(dk_acc)
    dv_acc[...] = jnp.zeros_like(dv_acc)

    def output_grad():
        def body(i, carry):
            grad = dot(mixed_low_t[...], dmid[:, rows(i, 2 * block)]).astype(bf16).T
            for k in range(2):
                for t in range(planes):
                    start = k * block + t * per
                    stage_out[t, 2 * i + k] = grad[start:start + per]
            return carry

        lax.fori_loop(0, n // 2, body, 0)
        grad_send(3)

    def attend_back(slot, q_sum):
        gather_step(dmid, 3, slot)
        place = chip(slot)
        at = rows(place, 2 * block)
        d_mix = dot_nt(w_out[...], dmid[at])
        pl.when(slot == 3)(output_grad)
        d_mix_t = jnp.concatenate([d_mix[h * head:(h + 1) * head] for h in range(group)], 1)
        d_mix_t = (d_mix_t.astype(bf16).astype(f32) * sums[place]).astype(bf16)
        delta = jnp.sum(d_mix_t.astype(f32) * mixed_t[place], 0, keepdims=True)
        weight = probs[place]
        d_prob = dot(values[...], d_mix_t)
        d_score = (weight.astype(f32) * (d_prob - delta)).astype(bf16)
        d_query = dot(keys_t[...], d_score) * scale
        for h in range(group):
            grad = turn_back(d_query[:, 2 * h * block:2 * (h + 1) * block].T, at)
            part, gain_part = norm_back(raw[at, h * head:(h + 1) * head], qg_ref[...], grad)
            d_qkv[at, h * head:(h + 1) * head] = part.astype(bf16)
            q_sum = q_sum + gain_part
        pl.when(slot == 2)(lambda: grad_near(1))
        dv_acc[...] += dot(weight, d_mix_t.T)
        dk_acc[...] += dot(d_score, stack(queries, at))
        return q_sum

    zero = jnp.zeros((1, head), f32)
    gain_own[2:3, 0:head] = lax.fori_loop(0, n // 2, attend_back, zero)
    gather_sent(dmid, 3)
    weight_grad(4, [(first_t, lambda: d_qkv[:, :qw])])
    grad_far(0)

    def project_back(i, k_sum):
        at = rows(i, 2 * block)
        grad = turn_back(dk_acc[at] * (1.0 / log2e), at)
        part, gain_part = norm_back(raw[at, qw:qw + kw], kg_ref[...], grad)
        d_qkv[at, qw:qw + kw] = part.astype(bf16)
        d_qkv[at, qw + kw:] = dv_acc[at].astype(bf16)
        return k_sum + gain_part

    gain_own[3:4, 0:head] = lax.fori_loop(0, n // 2, project_back, zero)

    weight_grad(5, [(first_t, lambda: d_qkv[:, qw:])])
    grad_far(1)
    grad_near(2)
    own_sum(0)
    drain(in_plane)
    sum_start(3, d_qkv, lambda left: dot_nt(left, w_qkv[...]))
    grad_far(2)
    grad_near(3)
    own_sum(1)
    hand_out(0)
    grad_far(3)
    grad_near(4)
    out_ref[...] = (middle[...] + sum_finish(2)).astype(bf16)
    grad_far(4)
    grad_near_far(5)
    own_sum(2)
    grad_near_inner(5)
    grad_far(5)
    x_part, gain_own[0:1, :] = norm_back(x_ref[...].astype(f32), ag_ref[...], sum_finish(3))
    dx_ref[...] = d_middle[...] + x_part

    def gain_plane_copy(j):
        return remote(gain_own, gain_plane.at[c], gp_send.at[j], gp_recv.at[j], partner(j), z)

    def gain_copy(d):
        return remote(gain_all.at[z], gain_all.at[z], gz_send.at[d], gz_recv.at[d], c, lax.rem(z + d, planes))

    for j in range(1, n):
        launch(in_plane, lambda j=j: gain_plane_copy(j))
    gain_plane[c] = gain_own[...]
    own_sum(3)
    hand_out(1)
    for j in range(1, n):
        gain_plane_copy(j).wait_recv()
    total = gain_plane[0]
    for i in range(1, n):
        total = total + gain_plane[i]
    gain_all[z] = total
    for d in range(1, planes):
        launch(along, lambda d=d: gain_copy(d))
    own_sum(4)
    for d in range(1, planes):
        origin = gain_all.at[lax.rem(z + planes - d, planes)]
        remote(origin, origin, gz_send.at[d], gz_recv.at[d], c, z).wait_recv()
    total = gain_all[0]
    for i in range(1, planes):
        total = total + gain_all[i]
    gains_ref[...] = total

    hand_receive(0)
    own_sum(5)
    hand_out(2)
    drain(along)
    hand_receive(1)
    hand_receive(2)
    drain(in_plane)


def finish_kernel(
    n, head, out_in, dx_in, gains_in, got_ab, got_co, got_qkv,
    out_ref, dx_ref, ag_ref, q_ref, k_ref, v_ref, qg_ref, kg_ref, o_ref, fg_ref, g_ref, u_ref, d_ref,
):
    out_ref[...] = out_in[...]
    dx_ref[...] = dx_in[...]
    ag_ref[...] = gains_in[0:1, :]
    fg_ref[...] = gains_in[1:2, :]
    qg_ref[...] = gains_in[2:3, 0:head]
    kg_ref[...] = gains_in[3:4, 0:head]
    qw, kw = q_ref.shape[1] // n, k_ref.shape[1] // n
    fw = g_ref.shape[1] // n
    pw = fw // 3
    thirds = ((got_ab, 0), (got_ab, fw), (got_co, 0))
    for i in range(n):
        q_ref[:, i * qw:(i + 1) * qw] = got_qkv[i, :, 0:qw].astype(f32)
        k_ref[:, i * kw:(i + 1) * kw] = got_qkv[i, :, qw:qw + kw].astype(f32)
        v_ref[:, i * kw:(i + 1) * kw] = got_qkv[i, :, qw + kw:].astype(f32)
        o_ref[:, i * qw:(i + 1) * qw] = got_co[i, :, fw:].astype(f32)
        for t, (got, start) in enumerate(thirds):
            plane, unit = hidden_block(i, t)
            at = plane * (g_ref.shape[1] // 4) + unit * pw
            g_ref[:, at:at + pw] = got[i, :, start:start + pw].astype(f32)
            u_ref[:, at:at + pw] = got[i, :, start + pw:start + 2 * pw].astype(f32)
            d_ref[:, at:at + pw] = got[i, :, start + 2 * pw:start + 3 * pw].astype(f32)


def plane_device(
    layer_input,
    token_positions,
    attention_gain,
    query_weight,
    key_matrix,
    value_matrix,
    query_gain,
    key_norm_gain,
    output_weight,
    feedforward_gain,
    gate_weight,
    up_weight,
    down_weight,
    out_cotangent,
):
    n = lax.axis_size("ctx")
    planes = lax.axis_size("fsdp")
    block, width = layer_input.shape[1:]
    length = token_positions.shape[1]
    head = query_gain.shape[0]
    qw = query_weight.shape[1] // n
    kw = key_matrix.shape[1] // n
    fw = gate_weight.shape[1] // n
    group = qw // head
    per = block // planes
    half = head // 2
    inverse = np.power(rope_base, -np.arange(half) * 2.0 / head).astype(np.float32)
    inverse = np.concatenate([inverse, inverse])[None]
    steps = np.arange(block // 2)[:, None] * inverse.astype(np.float64)
    step_cos, step_sin = (jnp.asarray(f(steps).astype(np.float32)) for f in (np.cos, np.sin))
    inverse = jnp.asarray(inverse)
    vmem = pl.BlockSpec(memory_space=pltpu.VMEM)
    hbm = pl.BlockSpec(memory_space=pl.ANY)
    dma = pltpu.SemaphoreType.DMA
    sizes = (fw, fw, fw, qw, qw, 2 * kw)
    low = lambda *shape: pltpu.VMEM(shape, bf16)
    wide = lambda *shape: pltpu.VMEM(shape, f32)
    scratch = [
        low(width, qw + 2 * kw), low(width, 2 * fw), low(qw, width), low(fw, width),
        low(planes * (output_weight.shape[0] // n), width),
        low(length, width), low(length, width), low(length, width),
        low(width, length), low(width, length), low(width, length),
        wide(length, head), wide(length, head), wide(length, head),
        wide(length, qw + kw), low(length, qw), low(length, kw), low(length, kw),
        low(kw, length), low(kw, length), low(n // 2, length, 2 * group * block), wide(n // 2, 1, 2 * group * block),
        wide(n // 2, head, 2 * group * block), low(length, qw), low(qw, length),
        low(length, fw), low(length, 2 * fw), low(length, qw + 2 * kw),
        wide(length, kw), wide(length, kw),
    ]
    scratch += [low(planes, n, per, size) for size in sizes]
    scratch += [low(planes + 1, n, per, size) for size in sizes]
    scratch += [low(n, per, sizes[m] + sizes[m + 1]) for m in (0, 2, 4)]
    scratch += [low(2, 4, block, width)] * 2 + [low(2, 3, block, width)] * 2 + [wide(2, block, width), wide(2, block, width)]
    scratch += [
        wide(block, width), wide(block, width), wide(8, width), wide(n, 8, width), wide(planes, 8, width),
        dma((13,)), dma((8, 6)), dma((8, planes)), dma((1, 7)), dma((1, 4)),
        dma((4, n)), dma((4, n)), dma((4, 4)), dma((4, 4)), dma((4, 4)), dma((4, 4)),
        dma((6, planes)), dma((6, planes + 1)), dma((3, n)), dma((3, n)), dma((n,)), dma((n,)),
        dma((planes,)), dma((planes,)),
    ]
    shapes = [
        jax.ShapeDtypeStruct((block, width), bf16),
        jax.ShapeDtypeStruct((block, width), f32),
        jax.ShapeDtypeStruct((8, width), f32),
    ] + [jax.ShapeDtypeStruct((n, per, sizes[m] + sizes[m + 1]), bf16) for m in (0, 2, 4)]
    results = pl.pallas_call(
        functools.partial(layer_kernel, n, planes, block, head, group, fw),
        out_shape=shapes,
        in_specs=[vmem] * 10 + [hbm] * 7,
        out_specs=[vmem] * len(shapes),
        scratch_shapes=scratch,
        compiler_params=pltpu.CompilerParams(
            collective_id=0, has_side_effects=True, vmem_limit_bytes=60 * 1024 * 1024),
    )(
        layer_input[0], out_cotangent[0], token_positions, inverse, step_cos, step_sin,
        attention_gain[None], feedforward_gain[None], query_gain[None], key_norm_gain[None],
        query_weight, key_matrix, value_matrix, output_weight, gate_weight, up_weight, down_weight,
    )
    plain = lambda rows, columns, kind=f32: jax.ShapeDtypeStruct((rows, columns), kind)
    finals = [
        plain(block, width, bf16), plain(block, width), plain(1, width),
        plain(per, n * qw), plain(per, n * kw), plain(per, n * kw), plain(1, head), plain(1, head),
        plain(per, n * qw), plain(1, width), plain(per, n * fw), plain(per, n * fw), plain(per, n * fw),
    ]
    done = pl.pallas_call(
        functools.partial(finish_kernel, n, head),
        out_shape=finals,
        in_specs=[vmem] * len(shapes),
        out_specs=[vmem] * len(finals),
    )(*results)
    out, dx, ag, q, k, v, qg, kg, o, fg, g, u, d = done
    return out[None], dx[None], ag[0], q, k, v, qg[0], kg[0], o.T, fg[0], g, u, d.T


def solution(mesh):
    in_specs = (
        P("fsdp", "ctx", None),
        P("fsdp", None),
        P(),
        P("fsdp", None),
        P("fsdp", None),
        P("fsdp", None),
        P(),
        P(),
        P("fsdp", None),
        P(),
        P("fsdp", None),
        P("fsdp", None),
        P("fsdp", None),
        P("fsdp", "ctx", None),
    )
    out_specs = (
        P("fsdp", "ctx", None),
        P("fsdp", "ctx", None),
        P(),
        P(("ctx", "fsdp"), None),
        P(("ctx", "fsdp"), None),
        P(("ctx", "fsdp"), None),
        P(),
        P(),
        P(None, ("ctx", "fsdp")),
        P(),
        P(("ctx", "fsdp"), None),
        P(("ctx", "fsdp"), None),
        P(None, ("ctx", "fsdp")),
    )

    def run(*arguments):
        n, planes = mesh.shape["ctx"], mesh.shape["fsdp"]
        key_heads = arguments[4].shape[1] // arguments[6].shape[0]
        whole_heads = n == 8 and planes == 4 and key_heads == n
        return jax.shard_map(
            plane_device if whole_heads else on_device,
            mesh=mesh, in_specs=in_specs, out_specs=out_specs, check_vma=False,
        )(*arguments)

    return run
```

```python
import functools

import jax
import jax.numpy as jnp
import numpy as np
from jax import lax
from jax.experimental import pallas as pl
from jax.experimental.pallas import tpu as pltpu
from jax.sharding import PartitionSpec as P

epsilon = 1e-06
rope_base = 1000000.0
masked_score = -1e30


def from_behind(block, axis, distance):
    devices = range(lax.axis_size(axis))
    route = [((i - distance) % len(devices), i) for i in devices]
    return lax.ppermute(block, axis, route)


def rotate(value_rows):
    half = value_rows.shape[-1] // 2
    return jnp.concatenate([-value_rows[..., half:], value_rows[..., :half]], -1)


def rotate_back(value_rows):
    half = value_rows.shape[-1] // 2
    return jnp.concatenate([value_rows[..., half:], -value_rows[..., :half]], -1)


def rope_tables(token_offsets, head_size):
    half = head_size // 2
    inverse = rope_base ** (-(jnp.arange(half).astype(jnp.float32) * 2.0) / head_size)
    angles = token_offsets.astype(jnp.float32)[:, None] * inverse[None, :]
    cosine = jnp.cos(angles)
    sine = jnp.sin(angles)
    return (jnp.concatenate([cosine, cosine], -1), jnp.concatenate([sine, sine], -1))


def norm_scale(value_rows):
    return lax.rsqrt(jnp.mean(value_rows * value_rows, -1, keepdims=True) + epsilon)


def norm_back(value_rows, scale, gain, grad):
    weighted = grad * gain
    inner = jnp.mean(weighted * value_rows, -1, keepdims=True)
    result = scale * weighted - value_rows * scale * scale * scale * inner
    gain_part = jnp.sum((grad * value_rows * scale).reshape(-1, gain.shape[0]), 0)
    return (result, gain_part)


def row_products(left, pieces):
    return tuple((jnp.dot(left, piece, preferred_element_type=jnp.float32) for piece in pieces))


def column_products(rights, pieces):
    total = jnp.einsum("tc,rc->tr", rights[0], pieces[0], preferred_element_type=jnp.float32)
    for right, piece in zip(rights[1:], pieces[1:]):
        total = total + jnp.einsum("tc,rc->tr", right, piece, preferred_element_type=jnp.float32)
    return total


def on_device(
    layer_input,
    token_positions,
    attention_gain,
    query_weight,
    key_matrix,
    value_matrix,
    query_gain,
    key_norm_gain,
    output_weight,
    feedforward_gain,
    gate_weight,
    up_weight,
    down_weight,
    out_cotangent,
):
    hidden_in = layer_input[0].astype(jnp.float32)
    count = hidden_in.shape[0]
    head_size = query_gain.shape[0]
    query_width = query_weight.shape[1]
    key_width = key_matrix.shape[1]
    inner_width = gate_weight.shape[1]
    heads = query_width // head_size
    key_heads = key_width // head_size
    group = heads // key_heads
    scale = head_size ** (-0.5)
    cycles = lax.axis_size("ctx")
    own_index = lax.axis_index("ctx")
    sequence_pos = token_positions[0]
    token_offsets = lax.dynamic_slice_in_dim(sequence_pos, own_index * count, count)
    cosine, sine = rope_tables(token_offsets, head_size)
    cosine = cosine[:, None, :]
    sine = sine[:, None, :]
    first_scale = norm_scale(hidden_in)
    first = (hidden_in * first_scale * attention_gain).astype(jnp.bfloat16)
    query_raw, key_unnormed, value_unnormed = row_products(
        first,
        (
            lax.all_gather(query_weight, "fsdp", axis=0, tiled=True),
            lax.all_gather(key_matrix, "fsdp", axis=0, tiled=True),
            lax.all_gather(value_matrix, "fsdp", axis=0, tiled=True),
        ),
    )
    query_heads = query_raw.reshape(count, heads, head_size)
    query_scale = norm_scale(query_heads)
    query_normed = query_heads * query_scale * query_gain
    query_rot = query_normed * cosine + rotate(query_normed) * sine
    query_grouped = (
        query_rot.reshape(count, key_heads, group, head_size)
        .transpose(1, 2, 0, 3)
        .astype(jnp.bfloat16)
    )
    key_heads_raw = key_unnormed.reshape(count, key_heads, head_size)
    key_scale = norm_scale(key_heads_raw)
    key_normed = key_heads_raw * key_scale * key_norm_gain
    key_low = (
        (key_normed * cosine + rotate(key_normed) * sine)
        .reshape(count, key_width)
        .astype(jnp.bfloat16)
    )
    value_low = value_unnormed.astype(jnp.bfloat16)
    rowmax = jnp.full((key_heads, group, count), masked_score, jnp.float32)
    keys_piece = lax.all_gather(key_low, "ctx", axis=0, tiled=True).reshape(
        -1, key_heads, head_size
    )
    values_piece = lax.all_gather(value_low, "ctx", axis=0, tiled=True).reshape(
        -1, key_heads, head_size
    )
    key_pos = sequence_pos
    allowed = token_offsets[:, None] >= key_pos[None, :]
    scores = (
        jnp.einsum("kgtd,skd->kgts", query_grouped, keys_piece, preferred_element_type=jnp.float32)
        * scale
    )
    scores = jnp.where(allowed, scores, masked_score)
    newmax = jnp.maximum(rowmax, jnp.max(scores, -1))
    weights = jnp.where(allowed, jnp.exp(scores - newmax[..., None]), 0.0)
    accum = jnp.einsum(
        "kgts,skd->kgtd",
        weights.astype(jnp.bfloat16),
        values_piece,
        preferred_element_type=jnp.float32,
    )
    rowsum = jnp.sum(weights, -1)
    accum, rowmax, rowsum = (accum, newmax, rowsum)
    normalized = accum / rowsum[..., None]
    logsum = rowmax + jnp.log(rowsum)
    attention_low = (
        normalized.transpose(2, 0, 1, 3).reshape(count, query_width).astype(jnp.bfloat16)
    )
    output_whole = lax.all_gather(output_weight, "fsdp", axis=0, tiled=True)
    branch_out = jnp.dot(attention_low, output_whole, preferred_element_type=jnp.float32)
    middle = hidden_in + branch_out
    second_scale = norm_scale(middle)
    second = (middle * second_scale * feedforward_gain).astype(jnp.bfloat16)
    gate, up = row_products(
        second,
        (
            lax.all_gather(gate_weight, "fsdp", axis=0, tiled=True),
            lax.all_gather(up_weight, "fsdp", axis=0, tiled=True),
        ),
    )
    sigmoid_gate = jax.nn.sigmoid(gate)
    silu_gate = gate * sigmoid_gate
    hidden_low = (silu_gate * up).astype(jnp.bfloat16)
    (down_out,) = row_products(
        hidden_low, (lax.all_gather(down_weight, "fsdp", axis=0, tiled=True),)
    )
    layer_output = (middle + down_out).astype(jnp.bfloat16)[None]
    cotangent = out_cotangent[0]
    hidden_grad = column_products(
        (cotangent,), lax.all_gather((down_weight,), "fsdp", axis=0, tiled=True)
    )
    up_low = (hidden_grad * silu_gate).astype(jnp.bfloat16)
    gate_low = (hidden_grad * up * sigmoid_gate * (1.0 + gate * (1.0 - sigmoid_gate))).astype(
        jnp.bfloat16
    )
    second_grad = column_products(
        (gate_low, up_low), lax.all_gather((gate_weight, up_weight), "fsdp", axis=0, tiled=True)
    )
    middle_part, feedforward_part = norm_back(middle, second_scale, feedforward_gain, second_grad)
    middle_grad = cotangent.astype(jnp.float32) + middle_part
    middle_low = middle_grad.astype(jnp.bfloat16)
    attention_grad = jnp.einsum(
        "tc,rc->tr", middle_low, output_whole, preferred_element_type=jnp.float32
    )
    attention_grad_low = attention_grad.astype(jnp.bfloat16)
    mixed_grad = attention_grad_low.reshape(count, key_heads, group, head_size).transpose(
        1, 2, 0, 3
    )
    delta = jnp.sum(mixed_grad.astype(jnp.float32) * normalized, -1)

    def cycle_step(index, carry):
        keys_held, values_held, key_acc, value_acc, query_acc = carry
        anchor = (own_index - index) % cycles
        key_pos = lax.dynamic_slice_in_dim(sequence_pos, anchor * count, count)
        keys_piece = keys_held.astype(jnp.bfloat16).reshape(count, key_heads, head_size)
        values_piece = values_held.astype(jnp.bfloat16).reshape(count, key_heads, head_size)
        allowed = token_offsets[:, None] >= key_pos[None, :]
        scores = (
            jnp.einsum(
                "kgtd,skd->kgts", query_grouped, keys_piece, preferred_element_type=jnp.float32
            )
            * scale
        )
        probs = jnp.where(allowed, jnp.exp(scores - logsum[..., None]), 0.0)
        value_acc = value_acc + jnp.einsum(
            "kgts,kgtd->skd",
            probs.astype(jnp.bfloat16),
            mixed_grad,
            preferred_element_type=jnp.float32,
        ).reshape(count, key_width)
        prob_grad = jnp.einsum(
            "kgtd,skd->kgts", mixed_grad, values_piece, preferred_element_type=jnp.float32
        )
        score_grad = (probs * (prob_grad - delta[..., None])).astype(jnp.bfloat16)
        query_acc = (
            query_acc
            + jnp.einsum(
                "kgts,skd->kgtd", score_grad, keys_piece, preferred_element_type=jnp.float32
            )
            * scale
        )
        key_acc = (
            key_acc
            + jnp.einsum(
                "kgts,kgtd->skd", score_grad, query_grouped, preferred_element_type=jnp.float32
            ).reshape(count, key_width)
            * scale
        )
        moved = (
            from_behind(keys_held.astype(jnp.bfloat16), "ctx", 1).astype(keys_held.dtype),
            from_behind(values_held.astype(jnp.bfloat16), "ctx", 1).astype(values_held.dtype),
            from_behind(key_acc.astype(jnp.bfloat16), "ctx", 1).astype(key_acc.dtype),
            from_behind(value_acc.astype(jnp.bfloat16), "ctx", 1).astype(value_acc.dtype),
        )
        return (moved[0], moved[1], moved[2], moved[3], query_acc)

    start_cycle = (
        key_low.astype(jnp.float32),
        value_low.astype(jnp.float32),
        jnp.zeros((count, key_width), jnp.float32),
        jnp.zeros((count, key_width), jnp.float32),
        jnp.zeros((key_heads, group, count, head_size), jnp.float32),
    )
    cycle_done = lax.fori_loop(0, cycles, cycle_step, start_cycle)
    key_acc = cycle_done[2]
    value_acc = cycle_done[3]
    query_acc = cycle_done[4]
    query_rot_grad = query_acc.transpose(2, 0, 1, 3).reshape(count, heads, head_size)
    query_normed_grad = query_rot_grad * cosine + rotate_back(query_rot_grad * sine)
    query_heads_grad, query_part = norm_back(
        query_heads, query_scale, query_gain, query_normed_grad
    )
    query_low_grad = query_heads_grad.reshape(count, query_width).astype(jnp.bfloat16)
    key_rot_grad = key_acc.reshape(count, key_heads, head_size)
    key_normed_grad = key_rot_grad * cosine + rotate_back(key_rot_grad * sine)
    key_heads_grad, key_part = norm_back(key_heads_raw, key_scale, key_norm_gain, key_normed_grad)
    key_low_grad = key_heads_grad.reshape(count, key_width).astype(jnp.bfloat16)
    value_low_grad = value_acc.astype(jnp.bfloat16)
    first_grad = column_products(
        (query_low_grad, key_low_grad, value_low_grad),
        lax.all_gather((query_weight, key_matrix, value_matrix), "fsdp", axis=0, tiled=True),
    )
    input_part, attention_part = norm_back(hidden_in, first_scale, attention_gain, first_grad)
    input_gradient = (middle_grad + input_part)[None]
    rights_first = jnp.concatenate([query_low_grad, key_low_grad, value_low_grad], 1)
    rights_second = jnp.concatenate([gate_low, up_low], 1)
    pairs = (
        (first, rights_first),
        (second, rights_second),
        (middle_low, attention_low),
        (cotangent, hidden_low),
    )
    parts = []
    for left, right in pairs:
        parts.append(jnp.einsum("tr,tc->rc", left, right, preferred_element_type=jnp.float32))
    sums = lax.psum_scatter(
        jnp.concatenate(parts, 1), ("ctx", "fsdp"), scatter_dimension=0, tiled=True
    )
    edges = [0, query_width, query_width + key_width, query_width + 2 * key_width]
    edges = edges + [edges[3] + inner_width, edges[3] + 2 * inner_width]
    edges = edges + [edges[5] + query_width, edges[5] + query_width + inner_width]
    query_gradient = sums[:, edges[0] : edges[1]]
    key_gradient = sums[:, edges[1] : edges[2]]
    value_gradient = sums[:, edges[2] : edges[3]]
    gate_gradient = sums[:, edges[3] : edges[4]]
    up_gradient = sums[:, edges[4] : edges[5]]
    output_gradient = sums[:, edges[5] : edges[6]].T
    down_gradient = sums[:, edges[6] : edges[7]].T
    attention_total, query_total, key_total, feedforward_total = lax.psum(
        (attention_part, query_part, key_part, feedforward_part), ("ctx", "fsdp")
    )
    return (
        layer_output,
        input_gradient,
        attention_total,
        query_gradient,
        key_gradient,
        value_gradient,
        query_total,
        key_total,
        output_gradient,
        feedforward_total,
        gate_gradient,
        up_gradient,
        down_gradient,
    )


MESH = pl.DeviceIdType.MESH
f32 = jnp.float32
bf16 = jnp.bfloat16


def dot(left, right):
    return jnp.dot(left, right, preferred_element_type=f32)


def dot_nt(left, right):
    return lax.dot_general(left, right, (((1,), (1,)), ((), ())), preferred_element_type=f32)


def dot_tn(left, right):
    return lax.dot_general(left, right, (((0,), (0,)), ((), ())), preferred_element_type=f32)


def hidden_block(device, third):
    def plane(i, t):
        return ((3, 1, 2), (0, 2, 1), (0, 3, 2), (3, 0, 1))[i // 4 * 2 + i % 2][t]

    own = plane(device, third)
    return own, sum(plane(i, t) == own for i in range(device) for t in range(3))


def layer_kernel(
    n, planes, block, head, group, fw,
    x_ref, dy_ref, pos_row, inverse_ref, step_cos, step_sin, ag_ref, fg_ref, qg_ref, kg_ref,
    wq, wk, wv, wo, wg, wu, wd,
    out_ref, dx_ref, gains_ref, got_ab, got_co, got_qkv,
    w_qkv, w_gu, w_out, w_down, t_out,
    first, dy_all, second, first_t, dy_t, second_t,
    positions, cosine, sine,
    raw, queries, keys, values, keys_t, values_t, probs, sums, mixed_t, mixed_low, mixed_low_t,
    hidden, d_gu, d_qkv, dk_acc, dv_acc,
    stage_a, stage_b, stage_c, stage_out, stage_q, stage_kv,
    land_a, land_b, land_c, land_out, land_q, land_kv,
    own_ab, own_co, own_qkv,
    rs_sa, rs_ra, rs_sb, rs_rb, rs_kept, rs_acc,
    middle, d_middle, gain_own, gain_plane, gain_all,
    local_sem, wz_send, wz_recv, hand_send, hand_recv,
    ag_send, ag_recv, ra_send, ra_recv, rb_send, rb_recv,
    zr_send, zr_recv, aa_send, aa_recv, gp_send, gp_recv, gz_send, gz_recv,
):
    c = lax.axis_index("ctx")
    z = lax.axis_index("fsdp")
    dmid = first
    cy, cx, ck = lax.div(c, 4), lax.rem(lax.div(c, 2), 2), lax.rem(c, 2)
    ci = lax.rem(c, 4)
    sign = 1 - 2 * ck
    qw, kw = group * head, head
    pw = 128
    thirds = fw // pw
    width = x_ref.shape[1]
    scale = head ** (-0.5)
    log2e = 1.4426950408889634
    gots = (got_ab, got_co, got_qkv)
    owns = (own_ab, own_co, own_qkv)
    stages = (stage_a, stage_b, stage_c, stage_out, stage_q, stage_kv)
    lands = (land_a, land_b, land_c, land_out, land_q, land_kv)

    def partner(j):
        y = lax.rem(cy + lax.div(j, 4), 2)
        x = lax.rem(cx + lax.rem(lax.div(j, 2), 2), 2)
        k = lax.rem(ck + lax.rem(j, 2), 2)
        return y * 4 + x * 2 + k

    def chip(slot):
        return lax.rem(cy + lax.div(slot, 2), 2) * 2 + lax.rem(cx + lax.rem(slot, 2), 2)

    def rows(start, size):
        return pl.ds(pl.multiple_of(start * size, size), size)

    def remote(src, dst, send, recv, ctx, plane):
        return pltpu.make_async_remote_copy(
            src_ref=src, dst_ref=dst, send_sem=send, recv_sem=recv,
            device_id={"ctx": ctx, "fsdp": plane}, device_id_type=MESH,
        )

    in_plane, along, weight_sends = [], [], []

    def launch(started, copy, when=None):
        if when is None:
            copy().start()
        else:
            pl.when(when)(lambda: copy().start())
        started.append((copy, when))

    def drain(started):
        for copy, when in started:
            if when is None:
                copy().wait_send()
            else:
                pl.when(when)(lambda copy=copy: copy().wait_send())
        started.clear()

    def pick(values):
        return sum(jnp.where(c == i, value, 0) for i, value in enumerate(values))

    unit_plane = [pick([hidden_block(i, t)[0] for i in range(n)]) for t in range(thirds)]
    unit_block = [pick([hidden_block(i, t)[1] for i in range(n)]) for t in range(thirds)]
    plane_blocks = wd.shape[0] // pw

    own_rows = wq.shape[0]
    out_rows = wo.shape[0] // n

    def own_slices():
        mine = rows(z, own_rows)
        pairs = [
            (wq.at[:, rows(c, qw)], w_qkv.at[mine, 0:qw]),
            (wk.at[:, rows(c, kw)], w_qkv.at[mine, qw:qw + kw]),
            (wv.at[:, rows(c, kw)], w_qkv.at[mine, qw + kw:qw + 2 * kw]),
            (wo.at[rows(c, out_rows)], t_out.at[rows(z, out_rows)]),
        ]
        for t in range(thirds):
            at = 2 * pw * t
            unit = unit_plane[t] * plane_blocks + unit_block[t]
            pairs.append((wg.at[:, rows(unit, pw)], w_gu.at[mine, at:at + pw]))
            pairs.append((wu.at[:, rows(unit, pw)], w_gu.at[mine, at + pw:at + 2 * pw]))
        return pairs

    local = [pltpu.make_async_copy(src, dst, local_sem.at[i]) for i, (src, dst) in enumerate(own_slices())]
    for copy in local:
        copy.start()

    def own_down(t):
        return pltpu.make_async_copy(
            wd.at[rows(unit_block[t], pw)], w_down.at[t * pw:(t + 1) * pw], local_sem.at[4 + 2 * thirds + t])

    holds = [unit_plane[t] == z for t in range(thirds)]
    for t in range(thirds):
        pl.when(holds[t])(lambda t=t: own_down(t).start())

    for land in lands:
        @pl.when(z == 0)
        def _(land=land):
            land[0] = jnp.zeros(land.shape[1:], bf16)

        @pl.when(z == planes - 1)
        def _(land=land):
            land[planes] = jnp.zeros(land.shape[1:], bf16)

    barrier = pltpu.get_barrier_semaphore()
    for j in range(1, n):
        pl.semaphore_signal(barrier, inc=1, device_id={"ctx": partner(j), "fsdp": z}, device_id_type=MESH)
    for d in range(1, planes):
        pl.semaphore_signal(
            barrier, inc=1, device_id={"ctx": c, "fsdp": lax.rem(z + d, planes)}, device_id_type=MESH)
    x = x_ref[...].astype(f32)
    x_scale = lax.rsqrt(jnp.mean(x * x, -1, keepdims=True) + epsilon)
    first[rows(c, block)] = (x * x_scale * ag_ref[...]).astype(bf16)
    dy_all[rows(c, block)] = dy_ref[...]
    for copy in local[:3]:
        copy.wait()
    pl.semaphore_wait(barrier, n + planes - 2)

    def inside(t):
        return jnp.logical_and(t >= 0, t < planes)

    weights = [
        (lambda o: w_qkv.at[rows(o, own_rows)], None),
        (lambda o: t_out.at[rows(o, out_rows)], 0),
    ]
    for t in range(thirds):
        weights.append((lambda o, t=t: w_gu.at[rows(o, own_rows), 2 * pw * t:2 * pw * (t + 1)], None))
        weights.append((lambda o, t=t: w_down.at[t * pw:(t + 1) * pw], None))

    def weight_copy(w, slot, origin, target):
        part = weights[w][0](origin)
        return remote(part, part, wz_send.at[w, slot], wz_recv.at[w, origin], c, target)

    def from_plane(w, origin):
        return origin == unit_plane[(w - 3) // 2] if w >= 3 and w % 2 else None

    def both(one, other):
        return one if other is None else jnp.logical_and(one, other)

    def hand_split(origin, valid):
        mine = 2 * origin + cy == c
        return jnp.logical_and(valid, jnp.logical_not(mine)), jnp.logical_and(valid, mine)

    def weight_start(w):
        for side in range(2):
            d = sign * (1 - 2 * side)
            launch(
                weight_sends, lambda side=side, d=d: weight_copy(w, side, z, z + d),
                both(inside(z + d), from_plane(w, z)))
        if weights[w][1] is not None:
            hand_over(w, z, 0, *hand_split(z, True))

    def hand_target(h):
        return lambda i: w_out.at[rows(i, out_rows)]

    def hand_copy(w, origin, slot):
        h = weights[w][1]
        return remote(
            weights[w][0](origin), hand_target(h)(ci), hand_send.at[h, slot], hand_recv.at[h, ci], 2 * origin + cy, z)

    def hand_over(w, origin, slot, away, here):
        launch(in_plane, lambda: hand_copy(w, origin, slot), away)

        @pl.when(here)
        def _():
            hand_target(weights[w][1])(ci)[...] = weights[w][0](origin)[...]

    def hand_arrive(w):
        h = weights[w][1]
        for i in range(4):
            @pl.when(4 * ck + i != c)
            def _(i=i):
                part = hand_target(h)(i)
                remote(part, part, hand_send.at[h, 0], hand_recv.at[h, i], c, z).wait_recv()

    hops = {}
    for w in range(len(weights)):
        for d in range(1, planes):
            for side, way in enumerate((1, -1)):
                origin = z - way * d
                valid = both(inside(origin), from_plane(w, origin))
                passed = jnp.logical_and(valid, inside(z + way))
                split = None if weights[w][1] is None else hand_split(origin, valid)
                hops[w, d, side] = origin, z + way, valid, passed, split

    def weight_hop(w, d):
        for side in range(2):
            origin, following, valid, passed, split = hops[w, d, side]
            pl.when(valid)(lambda: weight_copy(w, 0, origin, z).wait_recv())
            if d < planes - 1:
                launch(
                    weight_sends,
                    lambda side=side, origin=origin, following=following: weight_copy(
                        w, 2 * d + side, origin, following),
                    passed)
            if split is not None:
                hand_over(w, origin, 2 * d - 1 + side, *split)

    def gather_copy(buf, g, j, send, origin, target):
        part = buf.at[rows(origin, block)]
        return remote(part, part, ag_send.at[g, send], ag_recv.at[g, j], target, z)

    def gather_start(buf, g):
        for j in (1, 2 + 2 * ck, 4 - 2 * ck):
            launch(in_plane, lambda j=j: gather_copy(buf, g, j, j, c, partner(j)))

    def gather_half(buf, g, j):
        half = block // 2
        part = buf.at[pl.ds(pl.multiple_of(partner(j) * block + (half if j == 2 else 0), half), half)]
        at = 0 if j == 2 else 6
        return remote(part, part, ag_send.at[g, at], ag_recv.at[g, at], partner(6 - j), z)

    def gather_diagonal(buf, g):
        half = block // 2
        for at in (6, 0):
            part = buf.at[pl.ds(pl.multiple_of(partner(6) * block + (0 if at == 6 else half), half), half)]
            remote(part, part, ag_send.at[g, at], ag_recv.at[g, at], c, z).wait_recv()

    def gather_forward(buf, g, j):
        return gather_copy(buf, g, j + 1, j + 1, partner(j), partner(1))

    def gather_take(buf, g, j):
        if j == 6:
            gather_diagonal(buf, g)
        else:
            gather_copy(buf, g, j, j, partner(j), c).wait_recv()
            gather_half(buf, g, j).start()
        gather_forward(buf, g, j).start()

    def gather_sent(buf, g):
        for j in (2, 4, 6):
            in_plane.append((lambda j=j: gather_forward(buf, g, j), None))
            if j < 6:
                in_plane.append((lambda j=j: gather_half(buf, g, j), None))

    def gather_finish(buf, g):
        for j in (2, 4, 6):
            gather_take(buf, g, j)
        gather_sent(buf, g)
        for j in (1, 3, 5, 7):
            gather_copy(buf, g, j, j, partner(j), c).wait_recv()

    def gather_step(buf, g, slot, whole=3):
        @pl.when(slot == 1)
        def _():
            gather_take(buf, g, 2)
            gather_take(buf, g, 4)

        pl.when(slot == whole)(lambda: gather_take(buf, g, 6))

        @pl.when(slot <= whole)
        def _():
            gather_copy(buf, g, 2 * slot + 1, 0, partner(2 * slot + 1), c).wait_recv()

        if whole < 3:
            @pl.when(slot == whole)
            def _():
                gather_copy(buf, g, 7, 0, partner(7), c).wait_recv()


    def sum_pair_copy(s, slot):
        return remote(rs_sa.at[s % 2, slot], rs_ra.at[s % 2, slot], ra_send.at[s, slot], ra_recv.at[s, slot], partner(1), z)

    def sum_chip_copy(s, slot):
        return remote(
            rs_sb.at[s % 2, slot - 1], rs_rb.at[s % 2, slot - 1], rb_send.at[s, slot], rb_recv.at[s, slot], partner(2 * slot), z)

    def sum_half_copy(s, slot):
        half = block // 2
        at = pl.ds(pl.multiple_of((slot - 1) * half, half), half)
        return remote(
            rs_sb.at[s % 2, 2, at], rs_rb.at[s % 2, 2, at], rb_send.at[s, 6 - 3 * slot], rb_recv.at[s, 6 - 3 * slot],
            partner(6 - 2 * slot), z)

    def sum_slot(p):
        return jnp.where(p == 0, 3, jnp.where(p == 1, 2 - ck, jnp.where(p == 2, 1 + ck, 0)))

    def sum_start(s, left, partial, prepare=None, ready=None, during=()):
        if prepare is not None:
            for step in prepare:
                step(chip(sum_slot(0)))
        if ready is not None:
            ready()

        def body(p, carry):
            slot = sum_slot(p)
            at = [rows(partner(2 * slot + 1), block), rows(partner(2 * slot), block)]
            both = partial(jnp.concatenate([left[i] for i in at], 0))
            rs_sa[s % 2, slot] = both[:block].astype(bf16)
            sum_pair_copy(s, slot).start()
            rs_kept[lax.rem(p, 2)] = both[block:]

            def pair_sum(q):
                before = sum_slot(q)
                sum_pair_copy(s, before).wait_recv()
                rs_sb[s % 2, before - 1] = (
                    rs_kept[lax.rem(q, 2)] + rs_ra[s % 2, before].astype(f32)).astype(bf16)

            def chip_send(q):
                before = sum_slot(q)
                half = block // 2
                at = pl.ds(pl.multiple_of((before - 1) * half, half), half)
                sum_half_copy(s, before).wait_recv()
                rs_sb[s % 2, before - 1, at] = (
                    rs_sb[s % 2, before - 1, at].astype(f32) + rs_rb[s % 2, 2, at].astype(f32)).astype(bf16)
                sum_chip_copy(s, before).start()

            early = prepare is not None and len(prepare) > 1

            @pl.when(p == 1)
            def _():
                pair_sum(0)
                sum_half_copy(s, 1).start()
                sum_half_copy(s, 2).start()

            @pl.when(p == 2 if early else p > 1)
            def _():
                pair_sum(p - 1)
                chip_send(p - 1)

            if prepare is not None:
                @pl.when(p < 3)
                def _():
                    prepare[0](chip(sum_slot(p + 1)))

            if early:
                @pl.when(p == 2)
                def _():
                    pair_sum(2)
                    chip_send(2)

                @pl.when(p < 3)
                def _():
                    for step in prepare[1:]:
                        step(chip(sum_slot(p + 1)))

            for k, poll in enumerate(during):
                pl.when(p == k)(poll)
            return carry

        lax.fori_loop(0, 4, body, 0)
        for slot in range(4):
            in_plane.append((lambda slot=slot: sum_pair_copy(s, slot), None))
        for slot in (1, 2):
            in_plane.append((lambda slot=slot: sum_half_copy(s, slot), None))
            in_plane.append((lambda slot=slot: sum_chip_copy(s, slot), None))
        sum_pair_copy(s, 0).wait_recv()
        rs_acc[s % 2] = rs_kept[1] + rs_ra[s % 2, 0].astype(f32)

    def sum_finish(s):
        total = rs_acc[s % 2]
        for slot in (1, 2):
            sum_chip_copy(s, slot).wait_recv()
            total = total + rs_rb[s % 2, slot - 1].astype(f32)
        return total

    per = block // planes

    at_edge = jnp.logical_or(z == 0, z == planes - 1)
    edge_targets = [jnp.where(z == 0, planes - 1 - k, k) for k in range(planes - 1)]

    def weight_grad(m, parts):
        def body(i, carry):
            at = 0
            for left, right in parts:
                value = right()
                grad = dot(left[rows(i, 4 * block)], value)
                for k in range(4):
                    for t in range(planes):
                        start = k * block + t * per
                        stages[m][t, 4 * i + k, :, at:at + value.shape[1]] = grad[start:start + per].astype(bf16)
                at += value.shape[1]
            return carry

        lax.fori_loop(0, n // 4, body, 0)
        grad_send(m)

    def grad_send(m):
        for t in edge_targets:
            launch(along, lambda t=t: grad_copy(m, t), at_edge)

    def grad_copy(m, t):
        way = jnp.where(z < t, 1, -1)
        last = z + way == t
        slot = jnp.where(jnp.logical_and(last, way < 0), planes, t)
        return remote(
            stages[m].at[t], lands[m].at[slot], zr_send.at[m, t], zr_recv.at[m, slot], c, z + way)

    def grad_arrive(m, slot):
        part = lands[m].at[slot]
        remote(part, part, zr_send.at[m, 0], zr_recv.at[m, slot], c, z).wait_recv()

    def grad_pass(m, t, valid):
        @pl.when(valid)
        def _():
            grad_arrive(m, t)
            stages[m][t] = stages[m][t] + lands[m][t]

        launch(along, lambda: grad_copy(m, t), valid)

    is_low, is_high = z == 1, z == planes - 2

    def grad_near_far(m):
        grad_pass(m, 3, is_low)
        grad_pass(m, 0, is_high)

    def grad_near_inner(m):
        grad_pass(m, 2, is_low)
        grad_pass(m, 1, is_high)

    def grad_near(m):
        grad_near_far(m)
        grad_near_inner(m)

    def grad_far(m):
        grad_pass(m, 3, is_high)
        grad_pass(m, 0, is_low)

    def owner_copy(g, j):
        return remote(owns[g].at[partner(j)], gots[g].at[c], aa_send.at[g, j], aa_recv.at[g, j], partner(j), z)

    def own_sum(m):
        pl.when(z > 0)(lambda: grad_arrive(m, z))
        pl.when(z < planes - 1)(lambda: grad_arrive(m, planes))
        total = stages[m][z].astype(f32) + lands[m][z].astype(f32) + lands[m][planes].astype(f32)
        first_size = stages[m // 2 * 2].shape[3]
        if m % 2:
            owns[m // 2][:, :, first_size:] = total.astype(bf16)
        else:
            owns[m // 2][:, :, :first_size] = total.astype(bf16)

    def hand_out(g):
        for j in (2 + 2 * ck, 3 + 2 * ck, 4 - 2 * ck, 5 - 2 * ck, 6, 7, 1):
            launch(in_plane, lambda j=j: owner_copy(g, j))
        gots[g][c] = owns[g][c]

    def hand_receive(g):
        for j in range(1, n):
            owner_copy(g, j).wait_recv()

    weight_start(0)
    gather_start(first, 0)
    for copy in local[3:]:
        copy.wait()
    for t in range(thirds):
        pl.when(holds[t])(lambda t=t: own_down(t).wait())

    spread = jnp.broadcast_to(pos_row[...].astype(f32), (head, pos_row.shape[1]))
    positions[...] = spread.T
    side = jnp.where(lax.broadcasted_iota(jnp.int32, (1, head), 1) < head // 2, -1.0, 1.0)

    def table(i, carry):
        run = step_cos.shape[0]
        at = rows(i, run)
        start = positions[pl.ds(pl.multiple_of(i * run, run), 1)] * inverse_ref[...]
        start_cos, start_sin = jnp.cos(start), jnp.sin(start)
        cosine[at] = start_cos * step_cos[...] - start_sin * step_sin[...]
        sine[at] = (start_sin * step_cos[...] + start_cos * step_sin[...]) * side
        return carry

    def turn_over(src, dst):
        def body(i, carry):
            at = rows(i, block)
            dst[:, at] = src[at].T
            return carry

        lax.fori_loop(0, n, body, 0)

    lax.fori_loop(0, 2 * n, table, 0)
    weight_hop(0, 1)
    gather_finish(first, 0)
    weight_hop(0, 2)
    weight_start(1)
    gather_start(dy_all, 1)
    turn_over(first, first_t)
    weight_hop(0, 3)
    weight_start(2)
    weight_start(3)

    def turn(value, at):
        return value * cosine[at] + pltpu.roll(value, head // 2, 1) * sine[at]

    def turn_back(grad, at):
        return grad * cosine[at] - pltpu.roll(grad, head // 2, 1) * sine[at]

    def project(i, carry):
        at = rows(i, 2 * block)
        result = dot(first[at], w_qkv[...])
        raw[at] = result[:, :qw + kw]
        low_values = result[:, qw + kw:].astype(bf16)
        values[at] = low_values
        values_t[:, at] = low_values.T
        for h in range(group + 1):
            part = result[:, h * head:(h + 1) * head]
            inv = lax.rsqrt(jnp.mean(part * part, -1, keepdims=True) + epsilon)
            gain = qg_ref[...] if h < group else kg_ref[...]
            turned = turn(part * inv * gain, at)
            if h < group:
                queries[at, h * head:(h + 1) * head] = (turned * (scale * log2e)).astype(bf16)
            else:
                low_keys = turned.astype(bf16)
                keys[at] = low_keys
                keys_t[:, at] = low_keys.T
        return carry

    lax.fori_loop(0, n // 4, project, 0)
    weight_hop(1, 1)
    lax.fori_loop(n // 4, n // 2, project, 0)
    weight_hop(1, 2)
    gather_finish(dy_all, 1)

    def stack(ref, at):
        return jnp.concatenate([ref[at, h * head:(h + 1) * head] for h in range(group)], 0)

    def attend(place, h):
        at = rows(place, 2 * block)
        columns = slice(h * head, (h + 1) * head)
        tokens = slice(2 * h * block, 2 * (h + 1) * block)
        scores = dot_nt(keys[...], queries[at, columns])
        weight = jnp.concatenate(
            [jnp.exp2(jnp.where(
                positions[...] <= pos_row[:, rows(2 * place + k, block)].astype(f32),
                scores[:, k * block:(k + 1) * block], masked_score)) for k in range(2)], 1)
        inv = 1.0 / jnp.sum(weight, 0, keepdims=True)
        low_weight = weight.astype(bf16)
        probs[place, :, tokens] = low_weight
        sums[place, :, tokens] = inv
        result = dot(values_t[...], low_weight) * inv
        mixed_t[place, :, tokens] = result
        low_result = result.astype(bf16)
        mixed_low_t[columns, at] = low_result
        mixed_low[at, columns] = low_result.T

    def output_ready():
        weight_hop(1, 3)
        weight_start(4)
        weight_start(5)
        hand_arrive(1)
        drain(in_plane)

    def hop_third(t, d):
        weight_hop(2 + 2 * t, d)
        weight_hop(3 + 2 * t, d)

    sum_start(
        0, mixed_low, lambda left: dot(left, w_out[...]),
        [lambda place, h=h: attend(place, h) for h in range(group)], output_ready,
        (lambda: hop_third(0, 1), lambda: hop_third(0, 2), lambda: hop_third(1, 1)))
    weight_start(6)
    weight_start(7)
    mid = x_ref[...].astype(f32) + sum_finish(0)
    middle[...] = mid
    mid_scale = lax.rsqrt(jnp.mean(mid * mid, -1, keepdims=True) + epsilon)
    second[rows(c, block)] = (mid * mid_scale * fg_ref[...]).astype(bf16)
    gather_start(second, 2)
    hop_third(1, 2)
    turn_over(dy_all, dy_t)
    hop_third(0, 3)

    def feed(t, at):
        units, pair = slice(t * pw, (t + 1) * pw), 2 * pw * t
        both = dot(second[at], w_gu[:, pair:pair + 2 * pw])
        back = dot_nt(dy_all[at], w_down[units])
        gate, up = both[:, :pw], both[:, pw:]
        sig = 1.0 / (1.0 + jnp.exp(-gate))
        silu = gate * sig
        hidden[at, units] = (silu * up).astype(bf16)
        d_gu[at, pair:pair + pw] = (back * up * sig * (1.0 + gate * (1.0 - sig))).astype(bf16)
        d_gu[at, pair + pw:pair + 2 * pw] = (back * silu).astype(bf16)

    def feed_arriving(slot, carry):
        gather_step(second, 2, slot)
        at = rows(chip(slot), 2 * block)
        feed(0, at)
        second_t[:, at] = second[at].T
        pl.when(slot == 1)(lambda: hop_third(2, 1))
        pl.when(slot == 3)(lambda: hop_third(2, 2))
        return carry

    def third_grad(t):
        weight_grad(t, [
            (second_t, lambda: d_gu[:, 2 * pw * t:2 * pw * (t + 1)]),
            (dy_t, lambda: hidden[:, t * pw:(t + 1) * pw]),
        ])

    def feed_third(t):
        def body(i, carry):
            feed(t, rows(i, 2 * block))
            return carry

        lax.fori_loop(0, n // 2, body, 0)

    lax.fori_loop(0, n // 2, feed_arriving, 0)
    gather_sent(second, 2)
    hop_third(1, 3)
    third_grad(0)
    feed_third(1)
    hop_third(2, 3)
    sum_start(
        1, d_gu, lambda left: dot_nt(left, w_gu[...]),
        [lambda place: feed(thirds - 1, rows(place, 2 * block))])
    third_grad(1)
    third_grad(2)
    d_second = sum_finish(1)

    def norm_back(value, gain, grad):
        inv = lax.rsqrt(jnp.mean(value * value, -1, keepdims=True) + epsilon)
        weighted = grad * gain
        inner = jnp.mean(weighted * value, -1, keepdims=True)
        result = inv * weighted - value * (inv * inv * inv * inner)
        return result, jnp.sum(grad * value * inv, 0, keepdims=True)

    gain_own[...] = jnp.zeros_like(gain_own)
    part, gain_own[1:2, :] = norm_back(middle[...], fg_ref[...], d_second)
    d_mid = dy_ref[...].astype(f32) + part
    d_middle[...] = d_mid
    drain(in_plane)
    dmid[rows(c, block)] = d_mid.astype(bf16)
    gather_start(dmid, 3)
    drain(weight_sends)
    grad_near(0)

    dk_acc[...] = jnp.zeros_like(dk_acc)
    dv_acc[...] = jnp.zeros_like(dv_acc)

    def output_grad():
        def body(i, carry):
            grad = dot(mixed_low_t[...], dmid[:, rows(i, 2 * block)]).astype(bf16).T
            for k in range(2):
                for t in range(planes):
                    start = k * block + t * per
                    stage_out[t, 2 * i + k] = grad[start:start + per]
            return carry

        lax.fori_loop(0, n // 2, body, 0)
        grad_send(3)

    def attend_back(slot, q_sum):
        gather_step(dmid, 3, slot, 2)
        place = chip(slot)
        at = rows(place, 2 * block)
        d_mix = dot_nt(w_out[...], dmid[at])
        pl.when(slot == 2)(output_grad)
        d_mix_t = jnp.concatenate([d_mix[h * head:(h + 1) * head] for h in range(group)], 1)
        d_mix_t = (d_mix_t.astype(bf16).astype(f32) * sums[place]).astype(bf16)
        delta = jnp.sum(d_mix_t.astype(f32) * mixed_t[place], 0, keepdims=True)
        weight = probs[place]
        d_prob = dot(values[...], d_mix_t)
        d_score = (weight.astype(f32) * (d_prob - delta)).astype(bf16)
        d_query = dot(keys_t[...], d_score) * scale
        for h in range(group):
            grad = turn_back(d_query[:, 2 * h * block:2 * (h + 1) * block].T, at)
            part, gain_part = norm_back(raw[at, h * head:(h + 1) * head], qg_ref[...], grad)
            d_qkv[at, h * head:(h + 1) * head] = part.astype(bf16)
            q_sum = q_sum + gain_part
        pl.when(slot == 2)(lambda: grad_near(1))
        pl.when(slot == 3)(lambda: grad_far(0))
        dv_acc[...] += dot(weight, d_mix_t.T)
        dk_acc[...] += dot(d_score, stack(queries, at))
        return q_sum

    zero = jnp.zeros((1, head), f32)
    gain_own[2:3, 0:head] = lax.fori_loop(0, n // 2, attend_back, zero)
    gather_sent(dmid, 3)
    weight_grad(4, [(first_t, lambda: d_qkv[:, :qw])])
    def project_back(i, k_sum):
        at = rows(i, 2 * block)
        grad = turn_back(dk_acc[at] * (1.0 / log2e), at)
        part, gain_part = norm_back(raw[at, qw:qw + kw], kg_ref[...], grad)
        d_qkv[at, qw:qw + kw] = part.astype(bf16)
        d_qkv[at, qw + kw:] = dv_acc[at].astype(bf16)
        return k_sum + gain_part

    gain_own[3:4, 0:head] = lax.fori_loop(0, n // 2, project_back, zero)

    weight_grad(5, [(first_t, lambda: d_qkv[:, qw:])])
    grad_far(1)
    grad_near(2)
    sum_start(3, d_qkv, lambda left: dot_nt(left, w_qkv[...]))
    grad_far(2)
    grad_near(3)
    own_sum(0)
    own_sum(1)
    hand_out(0)
    grad_far(3)
    grad_near(4)
    sum_start(2, hidden, lambda left: dot(left, w_down[...]))
    grad_far(4)
    grad_near_far(5)
    own_sum(2)
    grad_near_inner(5)
    grad_far(5)
    x_part, gain_own[0:1, :] = norm_back(x_ref[...].astype(f32), ag_ref[...], sum_finish(3))
    dx_ref[...] = d_middle[...] + x_part

    def gain_plane_copy(j):
        return remote(gain_own, gain_plane.at[c], gp_send.at[j], gp_recv.at[j], partner(j), z)

    def gain_copy(d):
        return remote(gain_all.at[z], gain_all.at[z], gz_send.at[d], gz_recv.at[d], c, lax.rem(z + d, planes))

    for j in range(1, n):
        launch(in_plane, lambda j=j: gain_plane_copy(j))
    gain_plane[c] = gain_own[...]
    own_sum(3)
    hand_out(1)
    out_ref[...] = (middle[...] + sum_finish(2)).astype(bf16)
    for j in range(1, n):
        gain_plane_copy(j).wait_recv()
    total = gain_plane[0]
    for i in range(1, n):
        total = total + gain_plane[i]
    gain_all[z] = total
    for d in range(1, planes):
        launch(along, lambda d=d: gain_copy(d))
    own_sum(4)
    for d in range(1, planes):
        origin = gain_all.at[lax.rem(z + planes - d, planes)]
        remote(origin, origin, gz_send.at[d], gz_recv.at[d], c, z).wait_recv()
    total = gain_all[0]
    for i in range(1, planes):
        total = total + gain_all[i]
    gains_ref[...] = total

    hand_receive(0)
    own_sum(5)
    hand_out(2)
    drain(along)
    hand_receive(1)
    hand_receive(2)
    drain(in_plane)


def finish_kernel(
    n, head, out_in, dx_in, gains_in, got_ab, got_co, got_qkv,
    out_ref, dx_ref, ag_ref, q_ref, k_ref, v_ref, qg_ref, kg_ref, o_ref, fg_ref, g_ref, u_ref, d_ref,
):
    out_ref[...] = out_in[...]
    dx_ref[...] = dx_in[...]
    ag_ref[...] = gains_in[0:1, :]
    fg_ref[...] = gains_in[1:2, :]
    qg_ref[...] = gains_in[2:3, 0:head]
    kg_ref[...] = gains_in[3:4, 0:head]
    qw, kw = q_ref.shape[1] // n, k_ref.shape[1] // n
    fw = g_ref.shape[1] // n
    pw = fw // 3
    thirds = ((got_ab, 0), (got_ab, fw), (got_co, 0))
    for i in range(n):
        q_ref[:, i * qw:(i + 1) * qw] = got_qkv[i, :, 0:qw].astype(f32)
        k_ref[:, i * kw:(i + 1) * kw] = got_qkv[i, :, qw:qw + kw].astype(f32)
        v_ref[:, i * kw:(i + 1) * kw] = got_qkv[i, :, qw + kw:].astype(f32)
        o_ref[:, i * qw:(i + 1) * qw] = got_co[i, :, fw:].astype(f32)
        for t, (got, start) in enumerate(thirds):
            plane, unit = hidden_block(i, t)
            at = plane * (g_ref.shape[1] // 4) + unit * pw
            g_ref[:, at:at + pw] = got[i, :, start:start + pw].astype(f32)
            u_ref[:, at:at + pw] = got[i, :, start + pw:start + 2 * pw].astype(f32)
            d_ref[:, at:at + pw] = got[i, :, start + 2 * pw:start + 3 * pw].astype(f32)


def plane_device(
    layer_input,
    token_positions,
    attention_gain,
    query_weight,
    key_matrix,
    value_matrix,
    query_gain,
    key_norm_gain,
    output_weight,
    feedforward_gain,
    gate_weight,
    up_weight,
    down_weight,
    out_cotangent,
):
    n = lax.axis_size("ctx")
    planes = lax.axis_size("fsdp")
    block, width = layer_input.shape[1:]
    length = token_positions.shape[1]
    head = query_gain.shape[0]
    qw = query_weight.shape[1] // n
    kw = key_matrix.shape[1] // n
    fw = gate_weight.shape[1] // n
    group = qw // head
    per = block // planes
    half = head // 2
    inverse = np.power(rope_base, -np.arange(half) * 2.0 / head).astype(np.float32)
    inverse = np.concatenate([inverse, inverse])[None]
    steps = np.arange(block // 2)[:, None] * inverse.astype(np.float64)
    step_cos, step_sin = (jnp.asarray(f(steps).astype(np.float32)) for f in (np.cos, np.sin))
    inverse = jnp.asarray(inverse)
    vmem = pl.BlockSpec(memory_space=pltpu.VMEM)
    hbm = pl.BlockSpec(memory_space=pl.ANY)
    dma = pltpu.SemaphoreType.DMA
    sizes = (fw, fw, fw, qw, qw, 2 * kw)
    low = lambda *shape: pltpu.VMEM(shape, bf16)
    wide = lambda *shape: pltpu.VMEM(shape, f32)
    scratch = [
        low(width, qw + 2 * kw), low(width, 2 * fw), low(qw, width), low(fw, width),
        low(planes * (output_weight.shape[0] // n), width),
        low(length, width), low(length, width), low(length, width),
        low(width, length), low(width, length), low(width, length),
        wide(length, head), wide(length, head), wide(length, head),
        wide(length, qw + kw), low(length, qw), low(length, kw), low(length, kw),
        low(kw, length), low(kw, length), low(n // 2, length, 2 * group * block), wide(n // 2, 1, 2 * group * block),
        wide(n // 2, head, 2 * group * block), low(length, qw), low(qw, length),
        low(length, fw), low(length, 2 * fw), low(length, qw + 2 * kw),
        wide(length, kw), wide(length, kw),
    ]
    scratch += [low(planes, n, per, size) for size in sizes]
    scratch += [low(planes + 1, n, per, size) for size in sizes]
    scratch += [low(n, per, sizes[m] + sizes[m + 1]) for m in (0, 2, 4)]
    scratch += [low(2, 4, block, width)] * 2 + [low(2, 3, block, width)] * 2 + [wide(2, block, width), wide(2, block, width)]
    scratch += [
        wide(block, width), wide(block, width), wide(8, width), wide(n, 8, width), wide(planes, 8, width),
        dma((13,)), dma((8, 6)), dma((8, planes)), dma((1, 7)), dma((1, 4)),
        dma((4, n)), dma((4, n)), dma((4, 4)), dma((4, 4)), dma((4, 4)), dma((4, 4)),
        dma((6, planes)), dma((6, planes + 1)), dma((3, n)), dma((3, n)), dma((n,)), dma((n,)),
        dma((planes,)), dma((planes,)),
    ]
    shapes = [
        jax.ShapeDtypeStruct((block, width), bf16),
        jax.ShapeDtypeStruct((block, width), f32),
        jax.ShapeDtypeStruct((8, width), f32),
    ] + [jax.ShapeDtypeStruct((n, per, sizes[m] + sizes[m + 1]), bf16) for m in (0, 2, 4)]
    results = pl.pallas_call(
        functools.partial(layer_kernel, n, planes, block, head, group, fw),
        out_shape=shapes,
        in_specs=[vmem] * 10 + [hbm] * 7,
        out_specs=[vmem] * len(shapes),
        scratch_shapes=scratch,
        compiler_params=pltpu.CompilerParams(
            collective_id=0, has_side_effects=True, vmem_limit_bytes=60 * 1024 * 1024),
    )(
        layer_input[0], out_cotangent[0], token_positions, inverse, step_cos, step_sin,
        attention_gain[None], feedforward_gain[None], query_gain[None], key_norm_gain[None],
        query_weight, key_matrix, value_matrix, output_weight, gate_weight, up_weight, down_weight,
    )
    plain = lambda rows, columns, kind=f32: jax.ShapeDtypeStruct((rows, columns), kind)
    finals = [
        plain(block, width, bf16), plain(block, width), plain(1, width),
        plain(per, n * qw), plain(per, n * kw), plain(per, n * kw), plain(1, head), plain(1, head),
        plain(per, n * qw), plain(1, width), plain(per, n * fw), plain(per, n * fw), plain(per, n * fw),
    ]
    done = pl.pallas_call(
        functools.partial(finish_kernel, n, head),
        out_shape=finals,
        in_specs=[vmem] * len(shapes),
        out_specs=[vmem] * len(finals),
    )(*results)
    out, dx, ag, q, k, v, qg, kg, o, fg, g, u, d = done
    return out[None], dx[None], ag[0], q, k, v, qg[0], kg[0], o.T, fg[0], g, u, d.T


def solution(mesh):
    in_specs = (
        P("fsdp", "ctx", None),
        P("fsdp", None),
        P(),
        P("fsdp", None),
        P("fsdp", None),
        P("fsdp", None),
        P(),
        P(),
        P("fsdp", None),
        P(),
        P("fsdp", None),
        P("fsdp", None),
        P("fsdp", None),
        P("fsdp", "ctx", None),
    )
    out_specs = (
        P("fsdp", "ctx", None),
        P("fsdp", "ctx", None),
        P(),
        P(("ctx", "fsdp"), None),
        P(("ctx", "fsdp"), None),
        P(("ctx", "fsdp"), None),
        P(),
        P(),
        P(None, ("ctx", "fsdp")),
        P(),
        P(("ctx", "fsdp"), None),
        P(("ctx", "fsdp"), None),
        P(None, ("ctx", "fsdp")),
    )

    def run(*arguments):
        n, planes = mesh.shape["ctx"], mesh.shape["fsdp"]
        key_heads = arguments[4].shape[1] // arguments[6].shape[0]
        whole_heads = n == 8 and planes == 4 and key_heads == n
        return jax.shard_map(
            plane_device if whole_heads else on_device,
            mesh=mesh, in_specs=in_specs, out_specs=out_specs, check_vma=False,
        )(*arguments)

    return run
```

```python
import functools

import jax
import jax.numpy as jnp
import numpy as np
from jax import lax
from jax.experimental import pallas as pl
from jax.experimental.pallas import tpu as pltpu
from jax.sharding import PartitionSpec as P

epsilon = 1e-06
rope_base = 1000000.0
masked_score = -1e30


def from_behind(block, axis, distance):
    devices = range(lax.axis_size(axis))
    route = [((i - distance) % len(devices), i) for i in devices]
    return lax.ppermute(block, axis, route)


def rotate(value_rows):
    half = value_rows.shape[-1] // 2
    return jnp.concatenate([-value_rows[..., half:], value_rows[..., :half]], -1)


def rotate_back(value_rows):
    half = value_rows.shape[-1] // 2
    return jnp.concatenate([value_rows[..., half:], -value_rows[..., :half]], -1)


def rope_tables(token_offsets, head_size):
    half = head_size // 2
    inverse = rope_base ** (-(jnp.arange(half).astype(jnp.float32) * 2.0) / head_size)
    angles = token_offsets.astype(jnp.float32)[:, None] * inverse[None, :]
    cosine = jnp.cos(angles)
    sine = jnp.sin(angles)
    return (jnp.concatenate([cosine, cosine], -1), jnp.concatenate([sine, sine], -1))


def norm_scale(value_rows):
    return lax.rsqrt(jnp.mean(value_rows * value_rows, -1, keepdims=True) + epsilon)


def norm_back(value_rows, scale, gain, grad):
    weighted = grad * gain
    inner = jnp.mean(weighted * value_rows, -1, keepdims=True)
    result = scale * weighted - value_rows * scale * scale * scale * inner
    gain_part = jnp.sum((grad * value_rows * scale).reshape(-1, gain.shape[0]), 0)
    return (result, gain_part)


def row_products(left, pieces):
    return tuple((jnp.dot(left, piece, preferred_element_type=jnp.float32) for piece in pieces))


def column_products(rights, pieces):
    total = jnp.einsum("tc,rc->tr", rights[0], pieces[0], preferred_element_type=jnp.float32)
    for right, piece in zip(rights[1:], pieces[1:]):
        total = total + jnp.einsum("tc,rc->tr", right, piece, preferred_element_type=jnp.float32)
    return total


def on_device(
    layer_input,
    token_positions,
    attention_gain,
    query_weight,
    key_matrix,
    value_matrix,
    query_gain,
    key_norm_gain,
    output_weight,
    feedforward_gain,
    gate_weight,
    up_weight,
    down_weight,
    out_cotangent,
):
    hidden_in = layer_input[0].astype(jnp.float32)
    count = hidden_in.shape[0]
    head_size = query_gain.shape[0]
    query_width = query_weight.shape[1]
    key_width = key_matrix.shape[1]
    inner_width = gate_weight.shape[1]
    heads = query_width // head_size
    key_heads = key_width // head_size
    group = heads // key_heads
    scale = head_size ** (-0.5)
    cycles = lax.axis_size("ctx")
    own_index = lax.axis_index("ctx")
    sequence_pos = token_positions[0]
    token_offsets = lax.dynamic_slice_in_dim(sequence_pos, own_index * count, count)
    cosine, sine = rope_tables(token_offsets, head_size)
    cosine = cosine[:, None, :]
    sine = sine[:, None, :]
    first_scale = norm_scale(hidden_in)
    first = (hidden_in * first_scale * attention_gain).astype(jnp.bfloat16)
    query_raw, key_unnormed, value_unnormed = row_products(
        first,
        (
            lax.all_gather(query_weight, "fsdp", axis=0, tiled=True),
            lax.all_gather(key_matrix, "fsdp", axis=0, tiled=True),
            lax.all_gather(value_matrix, "fsdp", axis=0, tiled=True),
        ),
    )
    query_heads = query_raw.reshape(count, heads, head_size)
    query_scale = norm_scale(query_heads)
    query_normed = query_heads * query_scale * query_gain
    query_rot = query_normed * cosine + rotate(query_normed) * sine
    query_grouped = (
        query_rot.reshape(count, key_heads, group, head_size)
        .transpose(1, 2, 0, 3)
        .astype(jnp.bfloat16)
    )
    key_heads_raw = key_unnormed.reshape(count, key_heads, head_size)
    key_scale = norm_scale(key_heads_raw)
    key_normed = key_heads_raw * key_scale * key_norm_gain
    key_low = (
        (key_normed * cosine + rotate(key_normed) * sine)
        .reshape(count, key_width)
        .astype(jnp.bfloat16)
    )
    value_low = value_unnormed.astype(jnp.bfloat16)
    rowmax = jnp.full((key_heads, group, count), masked_score, jnp.float32)
    keys_piece = lax.all_gather(key_low, "ctx", axis=0, tiled=True).reshape(
        -1, key_heads, head_size
    )
    values_piece = lax.all_gather(value_low, "ctx", axis=0, tiled=True).reshape(
        -1, key_heads, head_size
    )
    key_pos = sequence_pos
    allowed = token_offsets[:, None] >= key_pos[None, :]
    scores = (
        jnp.einsum("kgtd,skd->kgts", query_grouped, keys_piece, preferred_element_type=jnp.float32)
        * scale
    )
    scores = jnp.where(allowed, scores, masked_score)
    newmax = jnp.maximum(rowmax, jnp.max(scores, -1))
    weights = jnp.where(allowed, jnp.exp(scores - newmax[..., None]), 0.0)
    accum = jnp.einsum(
        "kgts,skd->kgtd",
        weights.astype(jnp.bfloat16),
        values_piece,
        preferred_element_type=jnp.float32,
    )
    rowsum = jnp.sum(weights, -1)
    accum, rowmax, rowsum = (accum, newmax, rowsum)
    normalized = accum / rowsum[..., None]
    logsum = rowmax + jnp.log(rowsum)
    attention_low = (
        normalized.transpose(2, 0, 1, 3).reshape(count, query_width).astype(jnp.bfloat16)
    )
    output_whole = lax.all_gather(output_weight, "fsdp", axis=0, tiled=True)
    branch_out = jnp.dot(attention_low, output_whole, preferred_element_type=jnp.float32)
    middle = hidden_in + branch_out
    second_scale = norm_scale(middle)
    second = (middle * second_scale * feedforward_gain).astype(jnp.bfloat16)
    gate, up = row_products(
        second,
        (
            lax.all_gather(gate_weight, "fsdp", axis=0, tiled=True),
            lax.all_gather(up_weight, "fsdp", axis=0, tiled=True),
        ),
    )
    sigmoid_gate = jax.nn.sigmoid(gate)
    silu_gate = gate * sigmoid_gate
    hidden_low = (silu_gate * up).astype(jnp.bfloat16)
    (down_out,) = row_products(
        hidden_low, (lax.all_gather(down_weight, "fsdp", axis=0, tiled=True),)
    )
    layer_output = (middle + down_out).astype(jnp.bfloat16)[None]
    cotangent = out_cotangent[0]
    hidden_grad = column_products(
        (cotangent,), lax.all_gather((down_weight,), "fsdp", axis=0, tiled=True)
    )
    up_low = (hidden_grad * silu_gate).astype(jnp.bfloat16)
    gate_low = (hidden_grad * up * sigmoid_gate * (1.0 + gate * (1.0 - sigmoid_gate))).astype(
        jnp.bfloat16
    )
    second_grad = column_products(
        (gate_low, up_low), lax.all_gather((gate_weight, up_weight), "fsdp", axis=0, tiled=True)
    )
    middle_part, feedforward_part = norm_back(middle, second_scale, feedforward_gain, second_grad)
    middle_grad = cotangent.astype(jnp.float32) + middle_part
    middle_low = middle_grad.astype(jnp.bfloat16)
    attention_grad = jnp.einsum(
        "tc,rc->tr", middle_low, output_whole, preferred_element_type=jnp.float32
    )
    attention_grad_low = attention_grad.astype(jnp.bfloat16)
    mixed_grad = attention_grad_low.reshape(count, key_heads, group, head_size).transpose(
        1, 2, 0, 3
    )
    delta = jnp.sum(mixed_grad.astype(jnp.float32) * normalized, -1)

    def cycle_step(index, carry):
        keys_held, values_held, key_acc, value_acc, query_acc = carry
        anchor = (own_index - index) % cycles
        key_pos = lax.dynamic_slice_in_dim(sequence_pos, anchor * count, count)
        keys_piece = keys_held.astype(jnp.bfloat16).reshape(count, key_heads, head_size)
        values_piece = values_held.astype(jnp.bfloat16).reshape(count, key_heads, head_size)
        allowed = token_offsets[:, None] >= key_pos[None, :]
        scores = (
            jnp.einsum(
                "kgtd,skd->kgts", query_grouped, keys_piece, preferred_element_type=jnp.float32
            )
            * scale
        )
        probs = jnp.where(allowed, jnp.exp(scores - logsum[..., None]), 0.0)
        value_acc = value_acc + jnp.einsum(
            "kgts,kgtd->skd",
            probs.astype(jnp.bfloat16),
            mixed_grad,
            preferred_element_type=jnp.float32,
        ).reshape(count, key_width)
        prob_grad = jnp.einsum(
            "kgtd,skd->kgts", mixed_grad, values_piece, preferred_element_type=jnp.float32
        )
        score_grad = (probs * (prob_grad - delta[..., None])).astype(jnp.bfloat16)
        query_acc = (
            query_acc
            + jnp.einsum(
                "kgts,skd->kgtd", score_grad, keys_piece, preferred_element_type=jnp.float32
            )
            * scale
        )
        key_acc = (
            key_acc
            + jnp.einsum(
                "kgts,kgtd->skd", score_grad, query_grouped, preferred_element_type=jnp.float32
            ).reshape(count, key_width)
            * scale
        )
        moved = (
            from_behind(keys_held.astype(jnp.bfloat16), "ctx", 1).astype(keys_held.dtype),
            from_behind(values_held.astype(jnp.bfloat16), "ctx", 1).astype(values_held.dtype),
            from_behind(key_acc.astype(jnp.bfloat16), "ctx", 1).astype(key_acc.dtype),
            from_behind(value_acc.astype(jnp.bfloat16), "ctx", 1).astype(value_acc.dtype),
        )
        return (moved[0], moved[1], moved[2], moved[3], query_acc)

    start_cycle = (
        key_low.astype(jnp.float32),
        value_low.astype(jnp.float32),
        jnp.zeros((count, key_width), jnp.float32),
        jnp.zeros((count, key_width), jnp.float32),
        jnp.zeros((key_heads, group, count, head_size), jnp.float32),
    )
    cycle_done = lax.fori_loop(0, cycles, cycle_step, start_cycle)
    key_acc = cycle_done[2]
    value_acc = cycle_done[3]
    query_acc = cycle_done[4]
    query_rot_grad = query_acc.transpose(2, 0, 1, 3).reshape(count, heads, head_size)
    query_normed_grad = query_rot_grad * cosine + rotate_back(query_rot_grad * sine)
    query_heads_grad, query_part = norm_back(
        query_heads, query_scale, query_gain, query_normed_grad
    )
    query_low_grad = query_heads_grad.reshape(count, query_width).astype(jnp.bfloat16)
    key_rot_grad = key_acc.reshape(count, key_heads, head_size)
    key_normed_grad = key_rot_grad * cosine + rotate_back(key_rot_grad * sine)
    key_heads_grad, key_part = norm_back(key_heads_raw, key_scale, key_norm_gain, key_normed_grad)
    key_low_grad = key_heads_grad.reshape(count, key_width).astype(jnp.bfloat16)
    value_low_grad = value_acc.astype(jnp.bfloat16)
    first_grad = column_products(
        (query_low_grad, key_low_grad, value_low_grad),
        lax.all_gather((query_weight, key_matrix, value_matrix), "fsdp", axis=0, tiled=True),
    )
    input_part, attention_part = norm_back(hidden_in, first_scale, attention_gain, first_grad)
    input_gradient = (middle_grad + input_part)[None]
    rights_first = jnp.concatenate([query_low_grad, key_low_grad, value_low_grad], 1)
    rights_second = jnp.concatenate([gate_low, up_low], 1)
    pairs = (
        (first, rights_first),
        (second, rights_second),
        (middle_low, attention_low),
        (cotangent, hidden_low),
    )
    parts = []
    for left, right in pairs:
        parts.append(jnp.einsum("tr,tc->rc", left, right, preferred_element_type=jnp.float32))
    sums = lax.psum_scatter(
        jnp.concatenate(parts, 1), ("ctx", "fsdp"), scatter_dimension=0, tiled=True
    )
    edges = [0, query_width, query_width + key_width, query_width + 2 * key_width]
    edges = edges + [edges[3] + inner_width, edges[3] + 2 * inner_width]
    edges = edges + [edges[5] + query_width, edges[5] + query_width + inner_width]
    query_gradient = sums[:, edges[0] : edges[1]]
    key_gradient = sums[:, edges[1] : edges[2]]
    value_gradient = sums[:, edges[2] : edges[3]]
    gate_gradient = sums[:, edges[3] : edges[4]]
    up_gradient = sums[:, edges[4] : edges[5]]
    output_gradient = sums[:, edges[5] : edges[6]].T
    down_gradient = sums[:, edges[6] : edges[7]].T
    attention_total, query_total, key_total, feedforward_total = lax.psum(
        (attention_part, query_part, key_part, feedforward_part), ("ctx", "fsdp")
    )
    return (
        layer_output,
        input_gradient,
        attention_total,
        query_gradient,
        key_gradient,
        value_gradient,
        query_total,
        key_total,
        output_gradient,
        feedforward_total,
        gate_gradient,
        up_gradient,
        down_gradient,
    )


MESH = pl.DeviceIdType.MESH
f32 = jnp.float32
bf16 = jnp.bfloat16


def dot(left, right):
    return jnp.dot(left, right, preferred_element_type=f32)


def dot_nt(left, right):
    return lax.dot_general(left, right, (((1,), (1,)), ((), ())), preferred_element_type=f32)


def dot_tn(left, right):
    return lax.dot_general(left, right, (((0,), (0,)), ((), ())), preferred_element_type=f32)


def hidden_block(device, third):
    def plane(i, t):
        return ((3, 1, 2), (0, 2, 1), (0, 3, 2), (3, 0, 1))[i // 4 * 2 + i % 2][t]

    own = plane(device, third)
    return own, sum(plane(i, t) == own for i in range(device) for t in range(3))


def layer_kernel(
    n, planes, block, head, group, fw,
    x_ref, dy_ref, pos_row, inverse_ref, step_cos, step_sin, ag_ref, fg_ref, qg_ref, kg_ref,
    wq, wk, wv, wo, wg, wu, wd,
    out_ref, dx_ref, gains_ref, got_ab, got_co, got_qkv,
    w_qkv, w_gu, w_out, w_down, t_out,
    first, dy_all, second, first_t, dy_t, second_t,
    positions, cosine, sine,
    raw, queries, keys, values, keys_t, values_t, probs, sums, mixed_t, mixed_low, mixed_low_t,
    hidden, d_gu, d_qkv, dk_acc, dv_acc,
    stage_a, stage_b, stage_c, stage_out, stage_q, stage_kv,
    land_a, land_b, land_c, land_out, land_q, land_kv,
    own_ab, own_co, own_qkv,
    rs_sa, rs_ra, rs_sb, rs_rb, rs_kept, rs_acc,
    middle, d_middle, gain_own, gain_plane, gain_all,
    local_sem, wz_send, wz_recv, hand_send, hand_recv,
    ag_send, ag_recv, ra_send, ra_recv, rb_send, rb_recv,
    zr_send, zr_recv, aa_send, aa_recv, gp_send, gp_recv, gz_send, gz_recv,
):
    c = lax.axis_index("ctx")
    z = lax.axis_index("fsdp")
    dmid = first
    cy, cx, ck = lax.div(c, 4), lax.rem(lax.div(c, 2), 2), lax.rem(c, 2)
    ci = lax.rem(c, 4)
    sign = 1 - 2 * ck
    qw, kw = group * head, head
    pw = 128
    thirds = fw // pw
    width = x_ref.shape[1]
    scale = head ** (-0.5)
    log2e = 1.4426950408889634
    gots = (got_ab, got_co, got_qkv)
    owns = (own_ab, own_co, own_qkv)
    stages = (stage_a, stage_b, stage_c, stage_out, stage_q, stage_kv)
    lands = (land_a, land_b, land_c, land_out, land_q, land_kv)

    def partner(j):
        y = lax.rem(cy + lax.div(j, 4), 2)
        x = lax.rem(cx + lax.rem(lax.div(j, 2), 2), 2)
        k = lax.rem(ck + lax.rem(j, 2), 2)
        return y * 4 + x * 2 + k

    def chip(slot):
        return lax.rem(cy + lax.div(slot, 2), 2) * 2 + lax.rem(cx + lax.rem(slot, 2), 2)

    def rows(start, size):
        return pl.ds(pl.multiple_of(start * size, size), size)

    def remote(src, dst, send, recv, ctx, plane):
        return pltpu.make_async_remote_copy(
            src_ref=src, dst_ref=dst, send_sem=send, recv_sem=recv,
            device_id={"ctx": ctx, "fsdp": plane}, device_id_type=MESH,
        )

    in_plane, along, weight_sends = [], [], []

    def launch(started, copy, when=None):
        if when is None:
            copy().start()
        else:
            pl.when(when)(lambda: copy().start())
        started.append((copy, when))

    def drain(started):
        for copy, when in started:
            if when is None:
                copy().wait_send()
            else:
                pl.when(when)(lambda copy=copy: copy().wait_send())
        started.clear()

    def pick(values):
        return sum(jnp.where(c == i, value, 0) for i, value in enumerate(values))

    unit_plane = [pick([hidden_block(i, t)[0] for i in range(n)]) for t in range(thirds)]
    unit_block = [pick([hidden_block(i, t)[1] for i in range(n)]) for t in range(thirds)]
    plane_blocks = wd.shape[0] // pw

    own_rows = wq.shape[0]
    out_rows = wo.shape[0] // n

    def own_slices():
        mine = rows(z, own_rows)
        pairs = [
            (wq.at[:, rows(c, qw)], w_qkv.at[mine, 0:qw]),
            (wk.at[:, rows(c, kw)], w_qkv.at[mine, qw:qw + kw]),
            (wv.at[:, rows(c, kw)], w_qkv.at[mine, qw + kw:qw + 2 * kw]),
            (wo.at[rows(c, out_rows)], t_out.at[rows(z, out_rows)]),
        ]
        for t in range(thirds):
            at = 2 * pw * t
            unit = unit_plane[t] * plane_blocks + unit_block[t]
            pairs.append((wg.at[:, rows(unit, pw)], w_gu.at[mine, at:at + pw]))
            pairs.append((wu.at[:, rows(unit, pw)], w_gu.at[mine, at + pw:at + 2 * pw]))
        return pairs

    local = [pltpu.make_async_copy(src, dst, local_sem.at[i]) for i, (src, dst) in enumerate(own_slices())]
    for copy in local:
        copy.start()

    def own_down(t):
        return pltpu.make_async_copy(
            wd.at[rows(unit_block[t], pw)], w_down.at[t * pw:(t + 1) * pw], local_sem.at[4 + 2 * thirds + t])

    holds = [unit_plane[t] == z for t in range(thirds)]
    for t in range(thirds):
        pl.when(holds[t])(lambda t=t: own_down(t).start())

    for land in lands:
        @pl.when(z == 0)
        def _(land=land):
            land[0] = jnp.zeros(land.shape[1:], bf16)

        @pl.when(z == planes - 1)
        def _(land=land):
            land[planes] = jnp.zeros(land.shape[1:], bf16)

    barrier = pltpu.get_barrier_semaphore()
    for j in range(1, n):
        pl.semaphore_signal(barrier, inc=1, device_id={"ctx": partner(j), "fsdp": z}, device_id_type=MESH)
    for d in range(1, planes):
        pl.semaphore_signal(
            barrier, inc=1, device_id={"ctx": c, "fsdp": lax.rem(z + d, planes)}, device_id_type=MESH)
    x = x_ref[...].astype(f32)
    x_scale = lax.rsqrt(jnp.mean(x * x, -1, keepdims=True) + epsilon)
    first[rows(c, block)] = (x * x_scale * ag_ref[...]).astype(bf16)
    dy_all[rows(c, block)] = dy_ref[...]
    for copy in local[:3]:
        copy.wait()
    pl.semaphore_wait(barrier, n + planes - 2)

    def inside(t):
        return jnp.logical_and(t >= 0, t < planes)

    weights = [
        (lambda o: w_qkv.at[rows(o, own_rows)], None),
        (lambda o: t_out.at[rows(o, out_rows)], 0),
    ]
    for t in range(thirds):
        weights.append((lambda o, t=t: w_gu.at[rows(o, own_rows), 2 * pw * t:2 * pw * (t + 1)], None))
        weights.append((lambda o, t=t: w_down.at[t * pw:(t + 1) * pw], None))

    def weight_copy(w, slot, origin, target):
        part = weights[w][0](origin)
        return remote(part, part, wz_send.at[w, slot], wz_recv.at[w, origin], c, target)

    def from_plane(w, origin):
        return origin == unit_plane[(w - 3) // 2] if w >= 3 and w % 2 else None

    def both(one, other):
        return one if other is None else jnp.logical_and(one, other)

    def hand_split(origin, valid):
        mine = 2 * origin + cy == c
        return jnp.logical_and(valid, jnp.logical_not(mine)), jnp.logical_and(valid, mine)

    def weight_start(w):
        for side in range(2):
            launch(
                weight_sends, lambda side=side: weight_copy(w, side, z, z + sign * (1 - 2 * side)), starts[w, side])
        if weights[w][1] is not None:
            hand_over(w, z, 0, *hand_split(z, True))

    def hand_target(h):
        return lambda i: w_out.at[rows(i, out_rows)]

    def hand_copy(w, origin, slot):
        h = weights[w][1]
        return remote(
            weights[w][0](origin), hand_target(h)(ci), hand_send.at[h, slot], hand_recv.at[h, ci], 2 * origin + cy, z)

    def hand_over(w, origin, slot, away, here):
        launch(in_plane, lambda: hand_copy(w, origin, slot), away)

        @pl.when(here)
        def _():
            hand_target(weights[w][1])(ci)[...] = weights[w][0](origin)[...]

    def hand_arrive(w):
        h = weights[w][1]
        for i in range(4):
            @pl.when(4 * ck + i != c)
            def _(i=i):
                part = hand_target(h)(i)
                remote(part, part, hand_send.at[h, 0], hand_recv.at[h, i], c, z).wait_recv()

    hops, starts = {}, {}
    for w in range(len(weights)):
        for side in range(2):
            starts[w, side] = both(inside(z + sign * (1 - 2 * side)), from_plane(w, z))
        for d in range(1, planes):
            for side, way in enumerate((1, -1)):
                origin = z - way * d
                valid = both(inside(origin), from_plane(w, origin))
                passed = jnp.logical_and(valid, inside(z + way))
                split = None if weights[w][1] is None else hand_split(origin, valid)
                hops[w, d, side] = origin, z + way, valid, passed, split

    def weight_hop(w, d):
        for side in range(2):
            origin, following, valid, passed, split = hops[w, d, side]
            pl.when(valid)(lambda: weight_copy(w, 0, origin, z).wait_recv())
            if d < planes - 1:
                launch(
                    weight_sends,
                    lambda side=side, origin=origin, following=following: weight_copy(
                        w, 2 * d + side, origin, following),
                    passed)
            if split is not None:
                hand_over(w, origin, 2 * d - 1 + side, *split)

    def gather_copy(buf, g, j, send, origin, target):
        part = buf.at[rows(origin, block)]
        return remote(part, part, ag_send.at[g, send], ag_recv.at[g, j], target, z)

    def gather_start(buf, g):
        for j in (1, 2 + 2 * ck, 4 - 2 * ck):
            launch(in_plane, lambda j=j: gather_copy(buf, g, j, j, c, partner(j)))

    def gather_half(buf, g, j):
        half = block // 2
        part = buf.at[pl.ds(pl.multiple_of(partner(j) * block + (half if j == 2 else 0), half), half)]
        at = 0 if j == 2 else 6
        return remote(part, part, ag_send.at[g, at], ag_recv.at[g, at], partner(6 - j), z)

    def gather_diagonal(buf, g):
        half = block // 2
        for at in (6, 0):
            part = buf.at[pl.ds(pl.multiple_of(partner(6) * block + (0 if at == 6 else half), half), half)]
            remote(part, part, ag_send.at[g, at], ag_recv.at[g, at], c, z).wait_recv()

    def gather_forward(buf, g, j):
        return gather_copy(buf, g, j + 1, j + 1, partner(j), partner(1))

    def gather_take(buf, g, j):
        if j == 6:
            gather_diagonal(buf, g)
        else:
            gather_copy(buf, g, j, j, partner(j), c).wait_recv()
            gather_half(buf, g, j).start()
        gather_forward(buf, g, j).start()

    def gather_sent(buf, g):
        for j in (2, 4, 6):
            in_plane.append((lambda j=j: gather_forward(buf, g, j), None))
            if j < 6:
                in_plane.append((lambda j=j: gather_half(buf, g, j), None))

    def gather_finish(buf, g):
        for j in (2, 4, 6):
            gather_take(buf, g, j)
        gather_sent(buf, g)
        for j in (1, 3, 5, 7):
            gather_copy(buf, g, j, j, partner(j), c).wait_recv()

    def gather_step(buf, g, slot):
        @pl.when(slot == 1)
        def _():
            gather_take(buf, g, 2)
            gather_take(buf, g, 4)

        pl.when(slot == 3)(lambda: gather_take(buf, g, 6))
        gather_copy(buf, g, 2 * slot + 1, 0, partner(2 * slot + 1), c).wait_recv()

    def sum_pair_copy(s, slot):
        return remote(rs_sa.at[s % 2, slot], rs_ra.at[s % 2, slot], ra_send.at[s, slot], ra_recv.at[s, slot], partner(1), z)

    def sum_chip_copy(s, slot):
        return remote(
            rs_sb.at[s % 2, slot - 1], rs_rb.at[s % 2, slot - 1], rb_send.at[s, slot], rb_recv.at[s, slot], partner(2 * slot), z)

    def sum_half_copy(s, slot):
        half = block // 2
        at = pl.ds(pl.multiple_of((slot - 1) * half, half), half)
        return remote(
            rs_sb.at[s % 2, 2, at], rs_rb.at[s % 2, 2, at], rb_send.at[s, 6 - 3 * slot], rb_recv.at[s, 6 - 3 * slot],
            partner(6 - 2 * slot), z)

    def sum_slot(p):
        return jnp.where(p == 0, 3, jnp.where(p == 1, 2 - ck, jnp.where(p == 2, 1 + ck, 0)))

    def sum_start(s, left, partial, prepare=None, ready=None, during=()):
        if prepare is not None:
            for step in prepare:
                step(chip(sum_slot(0)))
        if ready is not None:
            ready()

        def body(p, carry):
            slot = sum_slot(p)
            at = [rows(partner(2 * slot + 1), block), rows(partner(2 * slot), block)]
            both = partial(jnp.concatenate([left[i] for i in at], 0))
            rs_sa[s % 2, slot] = both[:block].astype(bf16)
            sum_pair_copy(s, slot).start()
            rs_kept[lax.rem(p, 2)] = both[block:]

            def pair_sum(q):
                before = sum_slot(q)
                sum_pair_copy(s, before).wait_recv()
                rs_sb[s % 2, before - 1] = (
                    rs_kept[lax.rem(q, 2)] + rs_ra[s % 2, before].astype(f32)).astype(bf16)

            def chip_send(q):
                before = sum_slot(q)
                half = block // 2
                at = pl.ds(pl.multiple_of((before - 1) * half, half), half)
                sum_half_copy(s, before).wait_recv()
                rs_sb[s % 2, before - 1, at] = (
                    rs_sb[s % 2, before - 1, at].astype(f32) + rs_rb[s % 2, 2, at].astype(f32)).astype(bf16)
                sum_chip_copy(s, before).start()

            early = prepare is not None and len(prepare) > 1

            @pl.when(p == 1)
            def _():
                pair_sum(0)
                sum_half_copy(s, 1).start()
                sum_half_copy(s, 2).start()

            @pl.when(p == 2 if early else p > 1)
            def _():
                pair_sum(p - 1)
                chip_send(p - 1)

            if prepare is not None:
                @pl.when(p < 3)
                def _():
                    prepare[0](chip(sum_slot(p + 1)))

            if early:
                @pl.when(p == 2)
                def _():
                    pair_sum(2)
                    chip_send(2)

                @pl.when(p < 3)
                def _():
                    for step in prepare[1:]:
                        step(chip(sum_slot(p + 1)))

            for k, poll in enumerate(during):
                pl.when(p == k)(poll)
            return carry

        lax.fori_loop(0, 4, body, 0)
        for slot in range(4):
            in_plane.append((lambda slot=slot: sum_pair_copy(s, slot), None))
        for slot in (1, 2):
            in_plane.append((lambda slot=slot: sum_half_copy(s, slot), None))
            in_plane.append((lambda slot=slot: sum_chip_copy(s, slot), None))
        sum_pair_copy(s, 0).wait_recv()
        rs_acc[s % 2] = rs_kept[1] + rs_ra[s % 2, 0].astype(f32)

    def sum_finish(s):
        total = rs_acc[s % 2]
        for slot in (1, 2):
            sum_chip_copy(s, slot).wait_recv()
            total = total + rs_rb[s % 2, slot - 1].astype(f32)
        return total

    per = block // planes

    at_edge = jnp.logical_or(z == 0, z == planes - 1)
    edge_targets = [jnp.where(z == 0, planes - 1 - k, k) for k in range(planes - 1)]

    def weight_grad(m, parts):
        def body(i, carry):
            at = 0
            for left, right in parts:
                value = right()
                grad = dot(left[rows(i, 4 * block)], value)
                for k in range(4):
                    for t in range(planes):
                        start = k * block + t * per
                        stages[m][t, 4 * i + k, :, at:at + value.shape[1]] = grad[start:start + per].astype(bf16)
                at += value.shape[1]
            return carry

        lax.fori_loop(0, n // 4, body, 0)
        grad_send(m)

    def grad_send(m):
        for t in edge_targets:
            launch(along, lambda t=t: grad_copy(m, t), at_edge)

    def grad_copy(m, t):
        way = jnp.where(z < t, 1, -1)
        last = z + way == t
        slot = jnp.where(jnp.logical_and(last, way < 0), planes, t)
        return remote(
            stages[m].at[t], lands[m].at[slot], zr_send.at[m, t], zr_recv.at[m, slot], c, z + way)

    def grad_arrive(m, slot):
        part = lands[m].at[slot]
        remote(part, part, zr_send.at[m, 0], zr_recv.at[m, slot], c, z).wait_recv()

    def grad_pass(m, t, valid):
        @pl.when(valid)
        def _():
            grad_arrive(m, t)
            stages[m][t] = stages[m][t] + lands[m][t]

        launch(along, lambda: grad_copy(m, t), valid)

    is_low, is_high = z == 1, z == planes - 2

    def grad_near_far(m):
        grad_pass(m, 3, is_low)
        grad_pass(m, 0, is_high)

    def grad_near_inner(m):
        grad_pass(m, 2, is_low)
        grad_pass(m, 1, is_high)

    def grad_near(m):
        grad_near_far(m)
        grad_near_inner(m)

    def grad_far(m):
        grad_pass(m, 3, is_high)
        grad_pass(m, 0, is_low)

    def owner_copy(g, j):
        return remote(owns[g].at[partner(j)], gots[g].at[c], aa_send.at[g, j], aa_recv.at[g, j], partner(j), z)

    def own_sum(m):
        pl.when(z > 0)(lambda: grad_arrive(m, z))
        pl.when(z < planes - 1)(lambda: grad_arrive(m, planes))
        total = stages[m][z].astype(f32) + lands[m][z].astype(f32) + lands[m][planes].astype(f32)
        first_size = stages[m // 2 * 2].shape[3]
        if m % 2:
            owns[m // 2][:, :, first_size:] = total.astype(bf16)
        else:
            owns[m // 2][:, :, :first_size] = total.astype(bf16)

    def hand_out(g):
        for j in (2 + 2 * ck, 3 + 2 * ck, 4 - 2 * ck, 5 - 2 * ck, 6, 7, 1):
            launch(in_plane, lambda j=j: owner_copy(g, j))
        gots[g][c] = owns[g][c]

    def hand_receive(g):
        for j in range(1, n):
            owner_copy(g, j).wait_recv()

    weight_start(0)
    gather_start(first, 0)
    for copy in local[3:]:
        copy.wait()
    for t in range(thirds):
        pl.when(holds[t])(lambda t=t: own_down(t).wait())

    spread = jnp.broadcast_to(pos_row[...].astype(f32), (head, pos_row.shape[1]))
    positions[...] = spread.T
    side = jnp.where(lax.broadcasted_iota(jnp.int32, (1, head), 1) < head // 2, -1.0, 1.0)

    def table(i, carry):
        run = step_cos.shape[0]
        at = rows(i, run)
        start = positions[pl.ds(pl.multiple_of(i * run, run), 1)] * inverse_ref[...]
        start_cos, start_sin = jnp.cos(start), jnp.sin(start)
        cosine[at] = start_cos * step_cos[...] - start_sin * step_sin[...]
        sine[at] = (start_sin * step_cos[...] + start_cos * step_sin[...]) * side
        return carry

    def turn_over(src, dst):
        def body(i, carry):
            at = rows(i, block)
            dst[:, at] = src[at].T
            return carry

        lax.fori_loop(0, n, body, 0)

    lax.fori_loop(0, 2 * n, table, 0)
    weight_hop(0, 1)
    gather_finish(first, 0)
    weight_hop(0, 2)
    weight_start(1)
    gather_start(dy_all, 1)
    turn_over(first, first_t)
    weight_hop(0, 3)
    weight_start(2)
    weight_start(3)

    def turn(value, at):
        return value * cosine[at] + pltpu.roll(value, head // 2, 1) * sine[at]

    def turn_back(grad, at):
        return grad * cosine[at] - pltpu.roll(grad, head // 2, 1) * sine[at]

    def project(i, carry):
        at = rows(i, 2 * block)
        result = dot(first[at], w_qkv[...])
        raw[at] = result[:, :qw + kw]
        low_values = result[:, qw + kw:].astype(bf16)
        values[at] = low_values
        values_t[:, at] = low_values.T
        for h in range(group + 1):
            part = result[:, h * head:(h + 1) * head]
            inv = lax.rsqrt(jnp.mean(part * part, -1, keepdims=True) + epsilon)
            gain = qg_ref[...] if h < group else kg_ref[...]
            turned = turn(part * inv * gain, at)
            if h < group:
                queries[at, h * head:(h + 1) * head] = (turned * (scale * log2e)).astype(bf16)
            else:
                low_keys = turned.astype(bf16)
                keys[at] = low_keys
                keys_t[:, at] = low_keys.T
        return carry

    lax.fori_loop(0, n // 4, project, 0)
    weight_hop(1, 1)
    lax.fori_loop(n // 4, n // 2, project, 0)
    weight_hop(1, 2)
    gather_finish(dy_all, 1)

    def stack(ref, at):
        return jnp.concatenate([ref[at, h * head:(h + 1) * head] for h in range(group)], 0)

    def attend(place, h):
        at = rows(place, 2 * block)
        columns = slice(h * head, (h + 1) * head)
        tokens = slice(2 * h * block, 2 * (h + 1) * block)
        scores = dot_nt(keys[...], queries[at, columns])
        weight = jnp.concatenate(
            [jnp.exp2(jnp.where(
                positions[...] <= pos_row[:, rows(2 * place + k, block)].astype(f32),
                scores[:, k * block:(k + 1) * block], masked_score)) for k in range(2)], 1)
        inv = 1.0 / jnp.sum(weight, 0, keepdims=True)
        low_weight = weight.astype(bf16)
        probs[place, :, tokens] = low_weight
        sums[place, :, tokens] = inv
        result = dot(values_t[...], low_weight) * inv
        mixed_t[place, :, tokens] = result
        low_result = result.astype(bf16)
        mixed_low_t[columns, at] = low_result
        mixed_low[at, columns] = low_result.T

    def output_ready():
        weight_hop(1, 3)
        hand_arrive(1)
        drain(in_plane)

    def hop_third(t, d):
        weight_hop(2 + 2 * t, d)
        weight_hop(3 + 2 * t, d)

    def second_third():
        hop_third(0, 2)
        weight_start(4)
        weight_start(5)

    sum_start(
        0, mixed_low, lambda left: dot(left, w_out[...]),
        [lambda place, h=h: attend(place, h) for h in range(group)], output_ready,
        (lambda: hop_third(0, 1), second_third, lambda: hop_third(1, 1)))
    weight_start(6)
    weight_start(7)
    mid = x_ref[...].astype(f32) + sum_finish(0)
    middle[...] = mid
    mid_scale = lax.rsqrt(jnp.mean(mid * mid, -1, keepdims=True) + epsilon)
    second[rows(c, block)] = (mid * mid_scale * fg_ref[...]).astype(bf16)
    gather_start(second, 2)
    hop_third(1, 2)
    turn_over(dy_all, dy_t)
    hop_third(0, 3)

    def feed(t, at):
        units, pair = slice(t * pw, (t + 1) * pw), 2 * pw * t
        both = dot(second[at], w_gu[:, pair:pair + 2 * pw])
        back = dot_nt(dy_all[at], w_down[units])
        gate, up = both[:, :pw], both[:, pw:]
        sig = 1.0 / (1.0 + jnp.exp(-gate))
        silu = gate * sig
        hidden[at, units] = (silu * up).astype(bf16)
        d_gu[at, pair:pair + pw] = (back * up * sig * (1.0 + gate * (1.0 - sig))).astype(bf16)
        d_gu[at, pair + pw:pair + 2 * pw] = (back * silu).astype(bf16)

    def feed_arriving(slot, carry):
        gather_step(second, 2, slot)
        at = rows(chip(slot), 2 * block)
        feed(0, at)
        second_t[:, at] = second[at].T
        pl.when(slot == 1)(lambda: hop_third(2, 1))
        pl.when(slot == 3)(lambda: hop_third(2, 2))
        return carry

    def third_grad(t):
        weight_grad(t, [
            (second_t, lambda: d_gu[:, 2 * pw * t:2 * pw * (t + 1)]),
            (dy_t, lambda: hidden[:, t * pw:(t + 1) * pw]),
        ])

    def feed_third(t):
        def body(i, carry):
            feed(t, rows(i, 2 * block))
            return carry

        lax.fori_loop(0, n // 2, body, 0)

    lax.fori_loop(0, n // 2, feed_arriving, 0)
    gather_sent(second, 2)
    hop_third(1, 3)
    third_grad(0)
    feed_third(1)
    hop_third(2, 3)
    sum_start(
        1, d_gu, lambda left: dot_nt(left, w_gu[...]),
        [lambda place: feed(thirds - 1, rows(place, 2 * block))])
    third_grad(1)
    third_grad(2)
    d_second = sum_finish(1)

    def norm_back(value, gain, grad):
        inv = lax.rsqrt(jnp.mean(value * value, -1, keepdims=True) + epsilon)
        weighted = grad * gain
        inner = jnp.mean(weighted * value, -1, keepdims=True)
        result = inv * weighted - value * (inv * inv * inv * inner)
        return result, jnp.sum(grad * value * inv, 0, keepdims=True)

    gain_own[...] = jnp.zeros_like(gain_own)
    part, gain_own[1:2, :] = norm_back(middle[...], fg_ref[...], d_second)
    d_mid = dy_ref[...].astype(f32) + part
    d_middle[...] = d_mid
    drain(in_plane)
    dmid[rows(c, block)] = d_mid.astype(bf16)
    gather_start(dmid, 3)
    sum_start(2, hidden, lambda left: dot(left, w_down[...]))
    drain(weight_sends)
    grad_near(0)

    dk_acc[...] = jnp.zeros_like(dk_acc)
    dv_acc[...] = jnp.zeros_like(dv_acc)

    def output_grad():
        def body(i, carry):
            grad = dot(mixed_low_t[...], dmid[:, rows(i, 2 * block)]).astype(bf16).T
            for k in range(2):
                for t in range(planes):
                    start = k * block + t * per
                    stage_out[t, 2 * i + k] = grad[start:start + per]
            return carry

        lax.fori_loop(0, n // 2, body, 0)
        grad_send(3)

    def attend_back(slot, q_sum):
        gather_step(dmid, 3, slot)
        place = chip(slot)
        at = rows(place, 2 * block)
        d_mix = dot_nt(w_out[...], dmid[at])
        pl.when(slot == 3)(output_grad)
        d_mix_t = jnp.concatenate([d_mix[h * head:(h + 1) * head] for h in range(group)], 1)
        d_mix_t = (d_mix_t.astype(bf16).astype(f32) * sums[place]).astype(bf16)
        delta = jnp.sum(d_mix_t.astype(f32) * mixed_t[place], 0, keepdims=True)
        weight = probs[place]
        d_prob = dot(values[...], d_mix_t)
        d_score = (weight.astype(f32) * (d_prob - delta)).astype(bf16)
        d_query = dot(keys_t[...], d_score) * scale
        for h in range(group):
            grad = turn_back(d_query[:, 2 * h * block:2 * (h + 1) * block].T, at)
            part, gain_part = norm_back(raw[at, h * head:(h + 1) * head], qg_ref[...], grad)
            d_qkv[at, h * head:(h + 1) * head] = part.astype(bf16)
            q_sum = q_sum + gain_part
        pl.when(slot == 2)(lambda: grad_near(1))
        dv_acc[...] += dot(weight, d_mix_t.T)
        dk_acc[...] += dot(d_score, stack(queries, at))
        return q_sum

    zero = jnp.zeros((1, head), f32)
    gain_own[2:3, 0:head] = lax.fori_loop(0, n // 2, attend_back, zero)
    gather_sent(dmid, 3)
    weight_grad(4, [(first_t, lambda: d_qkv[:, :qw])])
    grad_far(0)

    def project_back(i, k_sum):
        at = rows(i, 2 * block)
        grad = turn_back(dk_acc[at] * (1.0 / log2e), at)
        part, gain_part = norm_back(raw[at, qw:qw + kw], kg_ref[...], grad)
        d_qkv[at, qw:qw + kw] = part.astype(bf16)
        d_qkv[at, qw + kw:] = dv_acc[at].astype(bf16)
        return k_sum + gain_part

    gain_own[3:4, 0:head] = lax.fori_loop(0, n // 2, project_back, zero)

    weight_grad(5, [(first_t, lambda: d_qkv[:, qw:])])
    grad_far(1)
    grad_near(2)
    own_sum(0)
    drain(in_plane)
    sum_start(3, d_qkv, lambda left: dot_nt(left, w_qkv[...]))
    grad_far(2)
    grad_near(3)
    own_sum(1)
    hand_out(0)
    grad_far(3)
    grad_near(4)
    out_ref[...] = (middle[...] + sum_finish(2)).astype(bf16)
    grad_far(4)
    grad_near_far(5)
    own_sum(2)
    grad_near_inner(5)
    grad_far(5)
    x_part, gain_own[0:1, :] = norm_back(x_ref[...].astype(f32), ag_ref[...], sum_finish(3))
    dx_ref[...] = d_middle[...] + x_part

    def gain_plane_copy(j):
        return remote(gain_own, gain_plane.at[c], gp_send.at[j], gp_recv.at[j], partner(j), z)

    def gain_copy(d):
        return remote(gain_all.at[z], gain_all.at[z], gz_send.at[d], gz_recv.at[d], c, lax.rem(z + d, planes))

    for j in range(1, n):
        launch(in_plane, lambda j=j: gain_plane_copy(j))
    gain_plane[c] = gain_own[...]
    own_sum(3)
    hand_out(1)
    for j in range(1, n):
        gain_plane_copy(j).wait_recv()
    total = gain_plane[0]
    for i in range(1, n):
        total = total + gain_plane[i]
    gain_all[z] = total
    for d in range(1, planes):
        launch(along, lambda d=d: gain_copy(d))
    own_sum(4)
    for d in range(1, planes):
        origin = gain_all.at[lax.rem(z + planes - d, planes)]
        remote(origin, origin, gz_send.at[d], gz_recv.at[d], c, z).wait_recv()
    total = gain_all[0]
    for i in range(1, planes):
        total = total + gain_all[i]
    gains_ref[...] = total

    hand_receive(0)
    own_sum(5)
    hand_out(2)
    drain(along)
    hand_receive(1)
    hand_receive(2)
    drain(in_plane)


def finish_kernel(
    n, head, out_in, dx_in, gains_in, got_ab, got_co, got_qkv,
    out_ref, dx_ref, ag_ref, q_ref, k_ref, v_ref, qg_ref, kg_ref, o_ref, fg_ref, g_ref, u_ref, d_ref,
):
    out_ref[...] = out_in[...]
    dx_ref[...] = dx_in[...]
    ag_ref[...] = gains_in[0:1, :]
    fg_ref[...] = gains_in[1:2, :]
    qg_ref[...] = gains_in[2:3, 0:head]
    kg_ref[...] = gains_in[3:4, 0:head]
    qw, kw = q_ref.shape[1] // n, k_ref.shape[1] // n
    fw = g_ref.shape[1] // n
    pw = fw // 3
    thirds = ((got_ab, 0), (got_ab, fw), (got_co, 0))
    for i in range(n):
        q_ref[:, i * qw:(i + 1) * qw] = got_qkv[i, :, 0:qw].astype(f32)
        k_ref[:, i * kw:(i + 1) * kw] = got_qkv[i, :, qw:qw + kw].astype(f32)
        v_ref[:, i * kw:(i + 1) * kw] = got_qkv[i, :, qw + kw:].astype(f32)
        o_ref[:, i * qw:(i + 1) * qw] = got_co[i, :, fw:].astype(f32)
        for t, (got, start) in enumerate(thirds):
            plane, unit = hidden_block(i, t)
            at = plane * (g_ref.shape[1] // 4) + unit * pw
            g_ref[:, at:at + pw] = got[i, :, start:start + pw].astype(f32)
            u_ref[:, at:at + pw] = got[i, :, start + pw:start + 2 * pw].astype(f32)
            d_ref[:, at:at + pw] = got[i, :, start + 2 * pw:start + 3 * pw].astype(f32)


def plane_device(
    layer_input,
    token_positions,
    attention_gain,
    query_weight,
    key_matrix,
    value_matrix,
    query_gain,
    key_norm_gain,
    output_weight,
    feedforward_gain,
    gate_weight,
    up_weight,
    down_weight,
    out_cotangent,
):
    n = lax.axis_size("ctx")
    planes = lax.axis_size("fsdp")
    block, width = layer_input.shape[1:]
    length = token_positions.shape[1]
    head = query_gain.shape[0]
    qw = query_weight.shape[1] // n
    kw = key_matrix.shape[1] // n
    fw = gate_weight.shape[1] // n
    group = qw // head
    per = block // planes
    half = head // 2
    inverse = np.power(rope_base, -np.arange(half) * 2.0 / head).astype(np.float32)
    inverse = np.concatenate([inverse, inverse])[None]
    steps = np.arange(block // 2)[:, None] * inverse.astype(np.float64)
    step_cos, step_sin = (jnp.asarray(f(steps).astype(np.float32)) for f in (np.cos, np.sin))
    inverse = jnp.asarray(inverse)
    vmem = pl.BlockSpec(memory_space=pltpu.VMEM)
    hbm = pl.BlockSpec(memory_space=pl.ANY)
    dma = pltpu.SemaphoreType.DMA
    sizes = (fw, fw, fw, qw, qw, 2 * kw)
    low = lambda *shape: pltpu.VMEM(shape, bf16)
    wide = lambda *shape: pltpu.VMEM(shape, f32)
    scratch = [
        low(width, qw + 2 * kw), low(width, 2 * fw), low(qw, width), low(fw, width),
        low(planes * (output_weight.shape[0] // n), width),
        low(length, width), low(length, width), low(length, width),
        low(width, length), low(width, length), low(width, length),
        wide(length, head), wide(length, head), wide(length, head),
        wide(length, qw + kw), low(length, qw), low(length, kw), low(length, kw),
        low(kw, length), low(kw, length), low(n // 2, length, 2 * group * block), wide(n // 2, 1, 2 * group * block),
        wide(n // 2, head, 2 * group * block), low(length, qw), low(qw, length),
        low(length, fw), low(length, 2 * fw), low(length, qw + 2 * kw),
        wide(length, kw), wide(length, kw),
    ]
    scratch += [low(planes, n, per, size) for size in sizes]
    scratch += [low(planes + 1, n, per, size) for size in sizes]
    scratch += [low(n, per, sizes[m] + sizes[m + 1]) for m in (0, 2, 4)]
    scratch += [low(2, 4, block, width)] * 2 + [low(2, 3, block, width)] * 2 + [wide(2, block, width), wide(2, block, width)]
    scratch += [
        wide(block, width), wide(block, width), wide(8, width), wide(n, 8, width), wide(planes, 8, width),
        dma((13,)), dma((8, 6)), dma((8, planes)), dma((1, 7)), dma((1, 4)),
        dma((4, n)), dma((4, n)), dma((4, 4)), dma((4, 4)), dma((4, 4)), dma((4, 4)),
        dma((6, planes)), dma((6, planes + 1)), dma((3, n)), dma((3, n)), dma((n,)), dma((n,)),
        dma((planes,)), dma((planes,)),
    ]
    shapes = [
        jax.ShapeDtypeStruct((block, width), bf16),
        jax.ShapeDtypeStruct((block, width), f32),
        jax.ShapeDtypeStruct((8, width), f32),
    ] + [jax.ShapeDtypeStruct((n, per, sizes[m] + sizes[m + 1]), bf16) for m in (0, 2, 4)]
    results = pl.pallas_call(
        functools.partial(layer_kernel, n, planes, block, head, group, fw),
        out_shape=shapes,
        in_specs=[vmem] * 10 + [hbm] * 7,
        out_specs=[vmem] * len(shapes),
        scratch_shapes=scratch,
        compiler_params=pltpu.CompilerParams(
            collective_id=0, has_side_effects=True, vmem_limit_bytes=60 * 1024 * 1024),
    )(
        layer_input[0], out_cotangent[0], token_positions, inverse, step_cos, step_sin,
        attention_gain[None], feedforward_gain[None], query_gain[None], key_norm_gain[None],
        query_weight, key_matrix, value_matrix, output_weight, gate_weight, up_weight, down_weight,
    )
    plain = lambda rows, columns, kind=f32: jax.ShapeDtypeStruct((rows, columns), kind)
    finals = [
        plain(block, width, bf16), plain(block, width), plain(1, width),
        plain(per, n * qw), plain(per, n * kw), plain(per, n * kw), plain(1, head), plain(1, head),
        plain(per, n * qw), plain(1, width), plain(per, n * fw), plain(per, n * fw), plain(per, n * fw),
    ]
    done = pl.pallas_call(
        functools.partial(finish_kernel, n, head),
        out_shape=finals,
        in_specs=[vmem] * len(shapes),
        out_specs=[vmem] * len(finals),
    )(*results)
    out, dx, ag, q, k, v, qg, kg, o, fg, g, u, d = done
    return out[None], dx[None], ag[0], q, k, v, qg[0], kg[0], o.T, fg[0], g, u, d.T


def solution(mesh):
    in_specs = (
        P("fsdp", "ctx", None),
        P("fsdp", None),
        P(),
        P("fsdp", None),
        P("fsdp", None),
        P("fsdp", None),
        P(),
        P(),
        P("fsdp", None),
        P(),
        P("fsdp", None),
        P("fsdp", None),
        P("fsdp", None),
        P("fsdp", "ctx", None),
    )
    out_specs = (
        P("fsdp", "ctx", None),
        P("fsdp", "ctx", None),
        P(),
        P(("ctx", "fsdp"), None),
        P(("ctx", "fsdp"), None),
        P(("ctx", "fsdp"), None),
        P(),
        P(),
        P(None, ("ctx", "fsdp")),
        P(),
        P(("ctx", "fsdp"), None),
        P(("ctx", "fsdp"), None),
        P(None, ("ctx", "fsdp")),
    )

    def run(*arguments):
        n, planes = mesh.shape["ctx"], mesh.shape["fsdp"]
        key_heads = arguments[4].shape[1] // arguments[6].shape[0]
        whole_heads = n == 8 and planes == 4 and key_heads == n
        return jax.shard_map(
            plane_device if whole_heads else on_device,
            mesh=mesh, in_specs=in_specs, out_specs=out_specs, check_vma=False,
        )(*arguments)

    return run
```

```python
import functools

import jax
import jax.numpy as jnp
import numpy as np
from jax import lax
from jax.experimental import pallas as pl
from jax.experimental.pallas import tpu as pltpu
from jax.sharding import PartitionSpec as P

epsilon = 1e-06
rope_base = 1000000.0
masked_score = -1e30


def from_behind(block, axis, distance):
    devices = range(lax.axis_size(axis))
    route = [((i - distance) % len(devices), i) for i in devices]
    return lax.ppermute(block, axis, route)


def rotate(value_rows):
    half = value_rows.shape[-1] // 2
    return jnp.concatenate([-value_rows[..., half:], value_rows[..., :half]], -1)


def rotate_back(value_rows):
    half = value_rows.shape[-1] // 2
    return jnp.concatenate([value_rows[..., half:], -value_rows[..., :half]], -1)


def rope_tables(token_offsets, head_size):
    half = head_size // 2
    inverse = rope_base ** (-(jnp.arange(half).astype(jnp.float32) * 2.0) / head_size)
    angles = token_offsets.astype(jnp.float32)[:, None] * inverse[None, :]
    cosine = jnp.cos(angles)
    sine = jnp.sin(angles)
    return (jnp.concatenate([cosine, cosine], -1), jnp.concatenate([sine, sine], -1))


def norm_scale(value_rows):
    return lax.rsqrt(jnp.mean(value_rows * value_rows, -1, keepdims=True) + epsilon)


def norm_back(value_rows, scale, gain, grad):
    weighted = grad * gain
    inner = jnp.mean(weighted * value_rows, -1, keepdims=True)
    result = scale * weighted - value_rows * scale * scale * scale * inner
    gain_part = jnp.sum((grad * value_rows * scale).reshape(-1, gain.shape[0]), 0)
    return (result, gain_part)


def row_products(left, pieces):
    return tuple((jnp.dot(left, piece, preferred_element_type=jnp.float32) for piece in pieces))


def column_products(rights, pieces):
    total = jnp.einsum("tc,rc->tr", rights[0], pieces[0], preferred_element_type=jnp.float32)
    for right, piece in zip(rights[1:], pieces[1:]):
        total = total + jnp.einsum("tc,rc->tr", right, piece, preferred_element_type=jnp.float32)
    return total


def on_device(
    layer_input,
    token_positions,
    attention_gain,
    query_weight,
    key_matrix,
    value_matrix,
    query_gain,
    key_norm_gain,
    output_weight,
    feedforward_gain,
    gate_weight,
    up_weight,
    down_weight,
    out_cotangent,
):
    hidden_in = layer_input[0].astype(jnp.float32)
    count = hidden_in.shape[0]
    head_size = query_gain.shape[0]
    query_width = query_weight.shape[1]
    key_width = key_matrix.shape[1]
    inner_width = gate_weight.shape[1]
    heads = query_width // head_size
    key_heads = key_width // head_size
    group = heads // key_heads
    scale = head_size ** (-0.5)
    cycles = lax.axis_size("ctx")
    own_index = lax.axis_index("ctx")
    sequence_pos = token_positions[0]
    token_offsets = lax.dynamic_slice_in_dim(sequence_pos, own_index * count, count)
    cosine, sine = rope_tables(token_offsets, head_size)
    cosine = cosine[:, None, :]
    sine = sine[:, None, :]
    first_scale = norm_scale(hidden_in)
    first = (hidden_in * first_scale * attention_gain).astype(jnp.bfloat16)
    query_raw, key_unnormed, value_unnormed = row_products(
        first,
        (
            lax.all_gather(query_weight, "fsdp", axis=0, tiled=True),
            lax.all_gather(key_matrix, "fsdp", axis=0, tiled=True),
            lax.all_gather(value_matrix, "fsdp", axis=0, tiled=True),
        ),
    )
    query_heads = query_raw.reshape(count, heads, head_size)
    query_scale = norm_scale(query_heads)
    query_normed = query_heads * query_scale * query_gain
    query_rot = query_normed * cosine + rotate(query_normed) * sine
    query_grouped = (
        query_rot.reshape(count, key_heads, group, head_size)
        .transpose(1, 2, 0, 3)
        .astype(jnp.bfloat16)
    )
    key_heads_raw = key_unnormed.reshape(count, key_heads, head_size)
    key_scale = norm_scale(key_heads_raw)
    key_normed = key_heads_raw * key_scale * key_norm_gain
    key_low = (
        (key_normed * cosine + rotate(key_normed) * sine)
        .reshape(count, key_width)
        .astype(jnp.bfloat16)
    )
    value_low = value_unnormed.astype(jnp.bfloat16)
    rowmax = jnp.full((key_heads, group, count), masked_score, jnp.float32)
    keys_piece = lax.all_gather(key_low, "ctx", axis=0, tiled=True).reshape(
        -1, key_heads, head_size
    )
    values_piece = lax.all_gather(value_low, "ctx", axis=0, tiled=True).reshape(
        -1, key_heads, head_size
    )
    key_pos = sequence_pos
    allowed = token_offsets[:, None] >= key_pos[None, :]
    scores = (
        jnp.einsum("kgtd,skd->kgts", query_grouped, keys_piece, preferred_element_type=jnp.float32)
        * scale
    )
    scores = jnp.where(allowed, scores, masked_score)
    newmax = jnp.maximum(rowmax, jnp.max(scores, -1))
    weights = jnp.where(allowed, jnp.exp(scores - newmax[..., None]), 0.0)
    accum = jnp.einsum(
        "kgts,skd->kgtd",
        weights.astype(jnp.bfloat16),
        values_piece,
        preferred_element_type=jnp.float32,
    )
    rowsum = jnp.sum(weights, -1)
    accum, rowmax, rowsum = (accum, newmax, rowsum)
    normalized = accum / rowsum[..., None]
    logsum = rowmax + jnp.log(rowsum)
    attention_low = (
        normalized.transpose(2, 0, 1, 3).reshape(count, query_width).astype(jnp.bfloat16)
    )
    output_whole = lax.all_gather(output_weight, "fsdp", axis=0, tiled=True)
    branch_out = jnp.dot(attention_low, output_whole, preferred_element_type=jnp.float32)
    middle = hidden_in + branch_out
    second_scale = norm_scale(middle)
    second = (middle * second_scale * feedforward_gain).astype(jnp.bfloat16)
    gate, up = row_products(
        second,
        (
            lax.all_gather(gate_weight, "fsdp", axis=0, tiled=True),
            lax.all_gather(up_weight, "fsdp", axis=0, tiled=True),
        ),
    )
    sigmoid_gate = jax.nn.sigmoid(gate)
    silu_gate = gate * sigmoid_gate
    hidden_low = (silu_gate * up).astype(jnp.bfloat16)
    (down_out,) = row_products(
        hidden_low, (lax.all_gather(down_weight, "fsdp", axis=0, tiled=True),)
    )
    layer_output = (middle + down_out).astype(jnp.bfloat16)[None]
    cotangent = out_cotangent[0]
    hidden_grad = column_products(
        (cotangent,), lax.all_gather((down_weight,), "fsdp", axis=0, tiled=True)
    )
    up_low = (hidden_grad * silu_gate).astype(jnp.bfloat16)
    gate_low = (hidden_grad * up * sigmoid_gate * (1.0 + gate * (1.0 - sigmoid_gate))).astype(
        jnp.bfloat16
    )
    second_grad = column_products(
        (gate_low, up_low), lax.all_gather((gate_weight, up_weight), "fsdp", axis=0, tiled=True)
    )
    middle_part, feedforward_part = norm_back(middle, second_scale, feedforward_gain, second_grad)
    middle_grad = cotangent.astype(jnp.float32) + middle_part
    middle_low = middle_grad.astype(jnp.bfloat16)
    attention_grad = jnp.einsum(
        "tc,rc->tr", middle_low, output_whole, preferred_element_type=jnp.float32
    )
    attention_grad_low = attention_grad.astype(jnp.bfloat16)
    mixed_grad = attention_grad_low.reshape(count, key_heads, group, head_size).transpose(
        1, 2, 0, 3
    )
    delta = jnp.sum(mixed_grad.astype(jnp.float32) * normalized, -1)

    def cycle_step(index, carry):
        keys_held, values_held, key_acc, value_acc, query_acc = carry
        anchor = (own_index - index) % cycles
        key_pos = lax.dynamic_slice_in_dim(sequence_pos, anchor * count, count)
        keys_piece = keys_held.astype(jnp.bfloat16).reshape(count, key_heads, head_size)
        values_piece = values_held.astype(jnp.bfloat16).reshape(count, key_heads, head_size)
        allowed = token_offsets[:, None] >= key_pos[None, :]
        scores = (
            jnp.einsum(
                "kgtd,skd->kgts", query_grouped, keys_piece, preferred_element_type=jnp.float32
            )
            * scale
        )
        probs = jnp.where(allowed, jnp.exp(scores - logsum[..., None]), 0.0)
        value_acc = value_acc + jnp.einsum(
            "kgts,kgtd->skd",
            probs.astype(jnp.bfloat16),
            mixed_grad,
            preferred_element_type=jnp.float32,
        ).reshape(count, key_width)
        prob_grad = jnp.einsum(
            "kgtd,skd->kgts", mixed_grad, values_piece, preferred_element_type=jnp.float32
        )
        score_grad = (probs * (prob_grad - delta[..., None])).astype(jnp.bfloat16)
        query_acc = (
            query_acc
            + jnp.einsum(
                "kgts,skd->kgtd", score_grad, keys_piece, preferred_element_type=jnp.float32
            )
            * scale
        )
        key_acc = (
            key_acc
            + jnp.einsum(
                "kgts,kgtd->skd", score_grad, query_grouped, preferred_element_type=jnp.float32
            ).reshape(count, key_width)
            * scale
        )
        moved = (
            from_behind(keys_held.astype(jnp.bfloat16), "ctx", 1).astype(keys_held.dtype),
            from_behind(values_held.astype(jnp.bfloat16), "ctx", 1).astype(values_held.dtype),
            from_behind(key_acc.astype(jnp.bfloat16), "ctx", 1).astype(key_acc.dtype),
            from_behind(value_acc.astype(jnp.bfloat16), "ctx", 1).astype(value_acc.dtype),
        )
        return (moved[0], moved[1], moved[2], moved[3], query_acc)

    start_cycle = (
        key_low.astype(jnp.float32),
        value_low.astype(jnp.float32),
        jnp.zeros((count, key_width), jnp.float32),
        jnp.zeros((count, key_width), jnp.float32),
        jnp.zeros((key_heads, group, count, head_size), jnp.float32),
    )
    cycle_done = lax.fori_loop(0, cycles, cycle_step, start_cycle)
    key_acc = cycle_done[2]
    value_acc = cycle_done[3]
    query_acc = cycle_done[4]
    query_rot_grad = query_acc.transpose(2, 0, 1, 3).reshape(count, heads, head_size)
    query_normed_grad = query_rot_grad * cosine + rotate_back(query_rot_grad * sine)
    query_heads_grad, query_part = norm_back(
        query_heads, query_scale, query_gain, query_normed_grad
    )
    query_low_grad = query_heads_grad.reshape(count, query_width).astype(jnp.bfloat16)
    key_rot_grad = key_acc.reshape(count, key_heads, head_size)
    key_normed_grad = key_rot_grad * cosine + rotate_back(key_rot_grad * sine)
    key_heads_grad, key_part = norm_back(key_heads_raw, key_scale, key_norm_gain, key_normed_grad)
    key_low_grad = key_heads_grad.reshape(count, key_width).astype(jnp.bfloat16)
    value_low_grad = value_acc.astype(jnp.bfloat16)
    first_grad = column_products(
        (query_low_grad, key_low_grad, value_low_grad),
        lax.all_gather((query_weight, key_matrix, value_matrix), "fsdp", axis=0, tiled=True),
    )
    input_part, attention_part = norm_back(hidden_in, first_scale, attention_gain, first_grad)
    input_gradient = (middle_grad + input_part)[None]
    rights_first = jnp.concatenate([query_low_grad, key_low_grad, value_low_grad], 1)
    rights_second = jnp.concatenate([gate_low, up_low], 1)
    pairs = (
        (first, rights_first),
        (second, rights_second),
        (middle_low, attention_low),
        (cotangent, hidden_low),
    )
    parts = []
    for left, right in pairs:
        parts.append(jnp.einsum("tr,tc->rc", left, right, preferred_element_type=jnp.float32))
    sums = lax.psum_scatter(
        jnp.concatenate(parts, 1), ("ctx", "fsdp"), scatter_dimension=0, tiled=True
    )
    edges = [0, query_width, query_width + key_width, query_width + 2 * key_width]
    edges = edges + [edges[3] + inner_width, edges[3] + 2 * inner_width]
    edges = edges + [edges[5] + query_width, edges[5] + query_width + inner_width]
    query_gradient = sums[:, edges[0] : edges[1]]
    key_gradient = sums[:, edges[1] : edges[2]]
    value_gradient = sums[:, edges[2] : edges[3]]
    gate_gradient = sums[:, edges[3] : edges[4]]
    up_gradient = sums[:, edges[4] : edges[5]]
    output_gradient = sums[:, edges[5] : edges[6]].T
    down_gradient = sums[:, edges[6] : edges[7]].T
    attention_total, query_total, key_total, feedforward_total = lax.psum(
        (attention_part, query_part, key_part, feedforward_part), ("ctx", "fsdp")
    )
    return (
        layer_output,
        input_gradient,
        attention_total,
        query_gradient,
        key_gradient,
        value_gradient,
        query_total,
        key_total,
        output_gradient,
        feedforward_total,
        gate_gradient,
        up_gradient,
        down_gradient,
    )


MESH = pl.DeviceIdType.MESH
f32 = jnp.float32
bf16 = jnp.bfloat16


def dot(left, right):
    return jnp.dot(left, right, preferred_element_type=f32)


def dot_nt(left, right):
    return lax.dot_general(left, right, (((1,), (1,)), ((), ())), preferred_element_type=f32)


def dot_tn(left, right):
    return lax.dot_general(left, right, (((0,), (0,)), ((), ())), preferred_element_type=f32)


def hidden_block(device, third):
    def plane(i, t):
        return ((3, 1, 2), (0, 2, 1), (0, 3, 2), (3, 0, 1))[i // 4 * 2 + i % 2][t]

    own = plane(device, third)
    return own, sum(plane(i, t) == own for i in range(device) for t in range(3))


def layer_kernel(
    n, planes, block, head, group, fw,
    x_ref, dy_ref, pos_row, inverse_ref, step_cos, step_sin, ag_ref, fg_ref, qg_ref, kg_ref,
    wq, wk, wv, wo, wg, wu, wd,
    out_ref, dx_ref, gains_ref, got_ab, got_co, got_qkv,
    w_qkv, w_gu, w_out, w_down, t_out,
    first, dy_all, second, first_t, dy_t, second_t,
    positions, cosine, sine,
    raw, queries, keys, values, keys_t, values_t, probs, sums, mixed_t, mixed_low, mixed_low_t,
    hidden, d_gu, d_qkv, dk_acc, dv_acc,
    stage_a, stage_b, stage_c, stage_out, stage_q, stage_kv,
    land_a, land_b, land_c, land_out, land_q, land_kv,
    own_ab, own_co, own_qkv,
    rs_sa, rs_ra, rs_sb, rs_rb, rs_kept, rs_acc,
    middle, d_middle, gain_own, gain_plane, gain_all,
    local_sem, wz_send, wz_recv, hand_send, hand_recv,
    ag_send, ag_recv, ra_send, ra_recv, rb_send, rb_recv,
    zr_send, zr_recv, aa_send, aa_recv, gp_send, gp_recv, gz_send, gz_recv,
):
    c = lax.axis_index("ctx")
    z = lax.axis_index("fsdp")
    dmid = first
    cy, cx, ck = lax.div(c, 4), lax.rem(lax.div(c, 2), 2), lax.rem(c, 2)
    ci = lax.rem(c, 4)
    sign = 1 - 2 * ck
    qw, kw = group * head, head
    pw = 128
    thirds = fw // pw
    width = x_ref.shape[1]
    scale = head ** (-0.5)
    log2e = 1.4426950408889634
    gots = (got_ab, got_co, got_qkv)
    owns = (own_ab, own_co, own_qkv)
    stages = (stage_a, stage_b, stage_c, stage_out, stage_q, stage_kv)
    lands = (land_a, land_b, land_c, land_out, land_q, land_kv)

    def partner(j):
        y = lax.rem(cy + lax.div(j, 4), 2)
        x = lax.rem(cx + lax.rem(lax.div(j, 2), 2), 2)
        k = lax.rem(ck + lax.rem(j, 2), 2)
        return y * 4 + x * 2 + k

    def chip(slot):
        return lax.rem(cy + lax.div(slot, 2), 2) * 2 + lax.rem(cx + lax.rem(slot, 2), 2)

    def rows(start, size):
        return pl.ds(pl.multiple_of(start * size, size), size)

    def remote(src, dst, send, recv, ctx, plane):
        return pltpu.make_async_remote_copy(
            src_ref=src, dst_ref=dst, send_sem=send, recv_sem=recv,
            device_id={"ctx": ctx, "fsdp": plane}, device_id_type=MESH,
        )

    in_plane, along, weight_sends = [], [], []

    def launch(started, copy, when=None):
        if when is None:
            copy().start()
        else:
            pl.when(when)(lambda: copy().start())
        started.append((copy, when))

    def drain(started):
        for copy, when in started:
            if when is None:
                copy().wait_send()
            else:
                pl.when(when)(lambda copy=copy: copy().wait_send())
        started.clear()

    def pick(values):
        return sum(jnp.where(c == i, value, 0) for i, value in enumerate(values))

    unit_plane = [pick([hidden_block(i, t)[0] for i in range(n)]) for t in range(thirds)]
    unit_block = [pick([hidden_block(i, t)[1] for i in range(n)]) for t in range(thirds)]
    plane_blocks = wd.shape[0] // pw

    own_rows = wq.shape[0]
    out_rows = wo.shape[0] // n

    def own_slices():
        mine = rows(z, own_rows)
        pairs = [
            (wq.at[:, rows(c, qw)], w_qkv.at[mine, 0:qw]),
            (wk.at[:, rows(c, kw)], w_qkv.at[mine, qw:qw + kw]),
            (wv.at[:, rows(c, kw)], w_qkv.at[mine, qw + kw:qw + 2 * kw]),
            (wo.at[rows(c, out_rows)], t_out.at[rows(z, out_rows)]),
        ]
        for t in range(thirds):
            at = 2 * pw * t
            unit = unit_plane[t] * plane_blocks + unit_block[t]
            pairs.append((wg.at[:, rows(unit, pw)], w_gu.at[mine, at:at + pw]))
            pairs.append((wu.at[:, rows(unit, pw)], w_gu.at[mine, at + pw:at + 2 * pw]))
        return pairs

    local = [pltpu.make_async_copy(src, dst, local_sem.at[i]) for i, (src, dst) in enumerate(own_slices())]
    for copy in local:
        copy.start()

    def own_down(t):
        return pltpu.make_async_copy(
            wd.at[rows(unit_block[t], pw)], w_down.at[t * pw:(t + 1) * pw], local_sem.at[4 + 2 * thirds + t])

    holds = [unit_plane[t] == z for t in range(thirds)]
    for t in range(thirds):
        pl.when(holds[t])(lambda t=t: own_down(t).start())

    for land in lands:
        @pl.when(z == 0)
        def _(land=land):
            land[0] = jnp.zeros(land.shape[1:], bf16)

        @pl.when(z == planes - 1)
        def _(land=land):
            land[planes] = jnp.zeros(land.shape[1:], bf16)

    barrier = pltpu.get_barrier_semaphore()
    for j in range(1, n):
        pl.semaphore_signal(barrier, inc=1, device_id={"ctx": partner(j), "fsdp": z}, device_id_type=MESH)
    for d in range(1, planes):
        pl.semaphore_signal(
            barrier, inc=1, device_id={"ctx": c, "fsdp": lax.rem(z + d, planes)}, device_id_type=MESH)
    x = x_ref[...].astype(f32)
    x_scale = lax.rsqrt(jnp.mean(x * x, -1, keepdims=True) + epsilon)
    first[rows(c, block)] = (x * x_scale * ag_ref[...]).astype(bf16)
    dy_all[rows(c, block)] = dy_ref[...]
    for copy in local[:3]:
        copy.wait()
    pl.semaphore_wait(barrier, n + planes - 2)

    def inside(t):
        return jnp.logical_and(t >= 0, t < planes)

    weights = [
        (lambda o: w_qkv.at[rows(o, own_rows)], None),
        (lambda o: t_out.at[rows(o, out_rows)], 0),
    ]
    for t in range(thirds):
        weights.append((lambda o, t=t: w_gu.at[rows(o, own_rows), 2 * pw * t:2 * pw * (t + 1)], None))
        weights.append((lambda o, t=t: w_down.at[t * pw:(t + 1) * pw], None))

    def weight_copy(w, slot, origin, target):
        part = weights[w][0](origin)
        return remote(part, part, wz_send.at[w, slot], wz_recv.at[w, origin], c, target)

    def from_plane(w, origin):
        return origin == unit_plane[(w - 3) // 2] if w >= 3 and w % 2 else None

    def both(one, other):
        return one if other is None else jnp.logical_and(one, other)

    def hand_split(origin, valid):
        mine = 2 * origin + cy == c
        return jnp.logical_and(valid, jnp.logical_not(mine)), jnp.logical_and(valid, mine)

    def weight_start(w):
        for side in range(2):
            d = sign * (1 - 2 * side)
            launch(
                weight_sends, lambda side=side, d=d: weight_copy(w, side, z, z + d),
                both(inside(z + d), from_plane(w, z)))
        if weights[w][1] is not None:
            hand_over(w, z, 0, *hand_split(z, True))

    def hand_target(h):
        return lambda i: w_out.at[rows(i, out_rows)]

    def hand_copy(w, origin, slot):
        h = weights[w][1]
        return remote(
            weights[w][0](origin), hand_target(h)(ci), hand_send.at[h, slot], hand_recv.at[h, ci], 2 * origin + cy, z)

    def hand_over(w, origin, slot, away, here):
        launch(in_plane, lambda: hand_copy(w, origin, slot), away)

        @pl.when(here)
        def _():
            hand_target(weights[w][1])(ci)[...] = weights[w][0](origin)[...]

    def hand_arrive(w):
        h = weights[w][1]
        for i in range(4):
            @pl.when(4 * ck + i != c)
            def _(i=i):
                part = hand_target(h)(i)
                remote(part, part, hand_send.at[h, 0], hand_recv.at[h, i], c, z).wait_recv()

    hops = {}
    for w in range(len(weights)):
        for d in range(1, planes):
            for side, way in enumerate((1, -1)):
                origin = z - way * d
                valid = both(inside(origin), from_plane(w, origin))
                passed = jnp.logical_and(valid, inside(z + way))
                split = None if weights[w][1] is None else hand_split(origin, valid)
                hops[w, d, side] = origin, z + way, valid, passed, split

    def weight_hop(w, d):
        for side in range(2):
            origin, following, valid, passed, split = hops[w, d, side]
            pl.when(valid)(lambda: weight_copy(w, 0, origin, z).wait_recv())
            if d < planes - 1:
                launch(
                    weight_sends,
                    lambda side=side, origin=origin, following=following: weight_copy(
                        w, 2 * d + side, origin, following),
                    passed)
            if split is not None:
                hand_over(w, origin, 2 * d - 1 + side, *split)

    def gather_copy(buf, g, j, send, origin, target):
        part = buf.at[rows(origin, block)]
        return remote(part, part, ag_send.at[g, send], ag_recv.at[g, j], target, z)

    def gather_start(buf, g):
        for j in (1, 2 + 2 * ck, 4 - 2 * ck):
            launch(in_plane, lambda j=j: gather_copy(buf, g, j, j, c, partner(j)))

    def gather_half(buf, g, j):
        half = block // 2
        part = buf.at[pl.ds(pl.multiple_of(partner(j) * block + (half if j == 2 else 0), half), half)]
        at = 0 if j == 2 else 6
        return remote(part, part, ag_send.at[g, at], ag_recv.at[g, at], partner(6 - j), z)

    def gather_diagonal(buf, g):
        half = block // 2
        for at in (6, 0):
            part = buf.at[pl.ds(pl.multiple_of(partner(6) * block + (0 if at == 6 else half), half), half)]
            remote(part, part, ag_send.at[g, at], ag_recv.at[g, at], c, z).wait_recv()

    def gather_forward(buf, g, j):
        return gather_copy(buf, g, j + 1, j + 1, partner(j), partner(1))

    def gather_take(buf, g, j):
        if j == 6:
            gather_diagonal(buf, g)
        else:
            gather_copy(buf, g, j, j, partner(j), c).wait_recv()
            gather_half(buf, g, j).start()
        gather_forward(buf, g, j).start()

    def gather_sent(buf, g):
        for j in (2, 4, 6):
            in_plane.append((lambda j=j: gather_forward(buf, g, j), None))
            if j < 6:
                in_plane.append((lambda j=j: gather_half(buf, g, j), None))

    def gather_finish(buf, g):
        for j in (2, 4, 6):
            gather_take(buf, g, j)
        gather_sent(buf, g)
        for j in (1, 3, 5, 7):
            gather_copy(buf, g, j, j, partner(j), c).wait_recv()

    def gather_step(buf, g, slot):
        @pl.when(slot == 1)
        def _():
            gather_take(buf, g, 2)
            gather_take(buf, g, 4)

        pl.when(slot == 3)(lambda: gather_take(buf, g, 6))
        gather_copy(buf, g, 2 * slot + 1, 0, partner(2 * slot + 1), c).wait_recv()

    def sum_pair_copy(s, slot):
        return remote(rs_sa.at[s % 2, slot], rs_ra.at[s % 2, slot], ra_send.at[s, slot], ra_recv.at[s, slot], partner(1), z)

    def sum_chip_copy(s, slot):
        return remote(
            rs_sb.at[s % 2, slot - 1], rs_rb.at[s % 2, slot - 1], rb_send.at[s, slot], rb_recv.at[s, slot], partner(2 * slot), z)

    def sum_half_copy(s, slot):
        half = block // 2
        at = pl.ds(pl.multiple_of((slot - 1) * half, half), half)
        return remote(
            rs_sb.at[s % 2, 2, at], rs_rb.at[s % 2, 2, at], rb_send.at[s, 6 - 3 * slot], rb_recv.at[s, 6 - 3 * slot],
            partner(6 - 2 * slot), z)

    def sum_slot(p):
        return jnp.where(p == 0, 3, jnp.where(p == 1, 2 - ck, jnp.where(p == 2, 1 + ck, 0)))

    def sum_start(s, left, partial, prepare=None, ready=None, during=()):
        if prepare is not None:
            for step in prepare:
                step(chip(sum_slot(0)))
        if ready is not None:
            ready()

        def body(p, carry):
            slot = sum_slot(p)
            at = [rows(partner(2 * slot + 1), block), rows(partner(2 * slot), block)]
            both = partial(jnp.concatenate([left[i] for i in at], 0), at)
            rs_sa[s % 2, slot] = both[:block].astype(bf16)
            sum_pair_copy(s, slot).start()
            rs_kept[lax.rem(p, 2)] = both[block:]

            def pair_sum(q):
                before = sum_slot(q)
                sum_pair_copy(s, before).wait_recv()
                rs_sb[s % 2, before - 1] = (
                    rs_kept[lax.rem(q, 2)] + rs_ra[s % 2, before].astype(f32)).astype(bf16)

            def chip_send(q):
                before = sum_slot(q)
                half = block // 2
                at = pl.ds(pl.multiple_of((before - 1) * half, half), half)
                sum_half_copy(s, before).wait_recv()
                rs_sb[s % 2, before - 1, at] = (
                    rs_sb[s % 2, before - 1, at].astype(f32) + rs_rb[s % 2, 2, at].astype(f32)).astype(bf16)
                sum_chip_copy(s, before).start()

            early = prepare is not None and len(prepare) > 1

            @pl.when(p == 1)
            def _():
                pair_sum(0)
                sum_half_copy(s, 1).start()
                sum_half_copy(s, 2).start()

            @pl.when(p == 2 if early else p > 1)
            def _():
                pair_sum(p - 1)
                chip_send(p - 1)

            if prepare is not None:
                @pl.when(p < 3)
                def _():
                    prepare[0](chip(sum_slot(p + 1)))

            if early:
                @pl.when(p == 2)
                def _():
                    pair_sum(2)
                    chip_send(2)

                @pl.when(p < 3)
                def _():
                    for step in prepare[1:]:
                        step(chip(sum_slot(p + 1)))

            for k, poll in enumerate(during):
                pl.when(p == k)(poll)
            return carry

        lax.fori_loop(0, 4, body, 0)
        for slot in range(4):
            in_plane.append((lambda slot=slot: sum_pair_copy(s, slot), None))
        for slot in (1, 2):
            in_plane.append((lambda slot=slot: sum_half_copy(s, slot), None))
            in_plane.append((lambda slot=slot: sum_chip_copy(s, slot), None))
        sum_pair_copy(s, 0).wait_recv()
        rs_acc[s % 2] = rs_kept[1] + rs_ra[s % 2, 0].astype(f32)

    def sum_finish(s):
        total = rs_acc[s % 2]
        for slot in (1, 2):
            sum_chip_copy(s, slot).wait_recv()
            total = total + rs_rb[s % 2, slot - 1].astype(f32)
        return total

    per = block // planes

    at_edge = jnp.logical_or(z == 0, z == planes - 1)
    edge_targets = [jnp.where(z == 0, planes - 1 - k, k) for k in range(planes - 1)]

    def weight_grad(m, parts):
        def body(i, carry):
            at = 0
            for left, right in parts:
                value = right()
                grad = dot(left[rows(i, 4 * block)], value)
                for k in range(4):
                    for t in range(planes):
                        start = k * block + t * per
                        stages[m][t, 4 * i + k, :, at:at + value.shape[1]] = grad[start:start + per].astype(bf16)
                at += value.shape[1]
            return carry

        lax.fori_loop(0, n // 4, body, 0)
        grad_send(m)

    def grad_send(m):
        for t in edge_targets:
            launch(along, lambda t=t: grad_copy(m, t), at_edge)

    def grad_copy(m, t):
        way = jnp.where(z < t, 1, -1)
        last = z + way == t
        slot = jnp.where(jnp.logical_and(last, way < 0), planes, t)
        return remote(
            stages[m].at[t], lands[m].at[slot], zr_send.at[m, t], zr_recv.at[m, slot], c, z + way)

    def grad_arrive(m, slot):
        part = lands[m].at[slot]
        remote(part, part, zr_send.at[m, 0], zr_recv.at[m, slot], c, z).wait_recv()

    def grad_pass(m, t, valid):
        @pl.when(valid)
        def _():
            grad_arrive(m, t)
            stages[m][t] = stages[m][t] + lands[m][t]

        launch(along, lambda: grad_copy(m, t), valid)

    is_low, is_high = z == 1, z == planes - 2

    def grad_near_far(m):
        grad_pass(m, 3, is_low)
        grad_pass(m, 0, is_high)

    def grad_near_inner(m):
        grad_pass(m, 2, is_low)
        grad_pass(m, 1, is_high)

    def grad_near(m):
        grad_near_far(m)
        grad_near_inner(m)

    def grad_far(m):
        grad_pass(m, 3, is_high)
        grad_pass(m, 0, is_low)

    def owner_copy(g, j):
        return remote(owns[g].at[partner(j)], gots[g].at[c], aa_send.at[g, j], aa_recv.at[g, j], partner(j), z)

    def own_sum(m):
        pl.when(z > 0)(lambda: grad_arrive(m, z))
        pl.when(z < planes - 1)(lambda: grad_arrive(m, planes))
        total = stages[m][z].astype(f32) + lands[m][z].astype(f32) + lands[m][planes].astype(f32)
        first_size = stages[m // 2 * 2].shape[3]
        if m % 2:
            owns[m // 2][:, :, first_size:] = total.astype(bf16)
        else:
            owns[m // 2][:, :, :first_size] = total.astype(bf16)

    def hand_out(g):
        for j in (2 + 2 * ck, 3 + 2 * ck, 4 - 2 * ck, 5 - 2 * ck, 6, 7, 1):
            launch(in_plane, lambda j=j: owner_copy(g, j))
        gots[g][c] = owns[g][c]

    def hand_receive(g):
        for j in range(1, n):
            owner_copy(g, j).wait_recv()

    weight_start(0)
    gather_start(first, 0)
    for copy in local[3:]:
        copy.wait()
    for t in range(thirds):
        pl.when(holds[t])(lambda t=t: own_down(t).wait())

    spread = jnp.broadcast_to(pos_row[...].astype(f32), (head, pos_row.shape[1]))
    positions[...] = spread.T
    side = jnp.where(lax.broadcasted_iota(jnp.int32, (1, head), 1) < head // 2, -1.0, 1.0)

    def table(i, carry):
        run = step_cos.shape[0]
        at = rows(i, run)
        start = positions[pl.ds(pl.multiple_of(i * run, run), 1)] * inverse_ref[...]
        start_cos, start_sin = jnp.cos(start), jnp.sin(start)
        cosine[at] = start_cos * step_cos[...] - start_sin * step_sin[...]
        sine[at] = (start_sin * step_cos[...] + start_cos * step_sin[...]) * side
        return carry

    def turn_over(src, dst):
        def body(i, carry):
            at = rows(i, block)
            dst[:, at] = src[at].T
            return carry

        lax.fori_loop(0, n, body, 0)

    lax.fori_loop(0, 2 * n, table, 0)
    weight_hop(0, 1)
    gather_finish(first, 0)
    weight_hop(0, 2)
    weight_start(1)
    gather_start(dy_all, 1)
    turn_over(first, first_t)
    weight_hop(0, 3)
    weight_start(2)
    weight_start(3)

    def turn(value, at):
        return value * cosine[at] + pltpu.roll(value, head // 2, 1) * sine[at]

    def turn_back(grad, at):
        return grad * cosine[at] - pltpu.roll(grad, head // 2, 1) * sine[at]

    def project(i, carry):
        at = rows(i, 2 * block)
        result = dot(first[at], w_qkv[...])
        raw[at] = result[:, :qw + kw]
        low_values = result[:, qw + kw:].astype(bf16)
        values[at] = low_values
        values_t[:, at] = low_values.T
        for h in range(group + 1):
            part = result[:, h * head:(h + 1) * head]
            inv = lax.rsqrt(jnp.mean(part * part, -1, keepdims=True) + epsilon)
            gain = qg_ref[...] if h < group else kg_ref[...]
            turned = turn(part * inv * gain, at)
            if h < group:
                queries[at, h * head:(h + 1) * head] = (turned * (scale * log2e)).astype(bf16)
            else:
                low_keys = turned.astype(bf16)
                keys[at] = low_keys
                keys_t[:, at] = low_keys.T
        return carry

    lax.fori_loop(0, n // 4, project, 0)
    weight_hop(1, 1)
    lax.fori_loop(n // 4, n // 2, project, 0)
    weight_hop(1, 2)
    gather_finish(dy_all, 1)

    def stack(ref, at):
        return jnp.concatenate([ref[at, h * head:(h + 1) * head] for h in range(group)], 0)

    def attend(place, h):
        at = rows(place, 2 * block)
        columns = slice(h * head, (h + 1) * head)
        tokens = slice(2 * h * block, 2 * (h + 1) * block)
        scores = dot_nt(keys[...], queries[at, columns])
        weight = jnp.concatenate(
            [jnp.exp2(jnp.where(
                positions[...] <= pos_row[:, rows(2 * place + k, block)].astype(f32),
                scores[:, k * block:(k + 1) * block], masked_score)) for k in range(2)], 1)
        inv = 1.0 / jnp.sum(weight, 0, keepdims=True)
        low_weight = weight.astype(bf16)
        probs[place, :, tokens] = low_weight
        sums[place, :, tokens] = inv
        result = dot(values_t[...], low_weight) * inv
        mixed_t[place, :, tokens] = result
        low_result = result.astype(bf16)
        mixed_low_t[columns, at] = low_result
        mixed_low[at, columns] = low_result.T

    def output_ready():
        weight_hop(1, 3)
        weight_start(4)
        weight_start(5)
        hand_arrive(1)
        drain(in_plane)

    def hop_third(t, d):
        weight_hop(2 + 2 * t, d)
        weight_hop(3 + 2 * t, d)

    sum_start(
        0, mixed_low, lambda left, at: dot(left, w_out[...]),
        [lambda place, h=h: attend(place, h) for h in range(group)], output_ready,
        (lambda: hop_third(0, 1), lambda: hop_third(0, 2), lambda: hop_third(1, 1)))
    weight_start(6)
    weight_start(7)
    mid = x_ref[...].astype(f32) + sum_finish(0)
    middle[...] = mid
    mid_scale = lax.rsqrt(jnp.mean(mid * mid, -1, keepdims=True) + epsilon)
    second[rows(c, block)] = (mid * mid_scale * fg_ref[...]).astype(bf16)
    gather_start(second, 2)
    hop_third(1, 2)
    turn_over(dy_all, dy_t)
    hop_third(0, 3)

    def feed(t, at):
        units, pair = slice(t * pw, (t + 1) * pw), 2 * pw * t
        both = dot(second[at], w_gu[:, pair:pair + 2 * pw])
        back = dot_nt(dy_all[at], w_down[units])
        gate, up = both[:, :pw], both[:, pw:]
        sig = 1.0 / (1.0 + jnp.exp(-gate))
        silu = gate * sig
        hidden[at, units] = (silu * up).astype(bf16)
        d_gu[at, pair:pair + pw] = (back * up * sig * (1.0 + gate * (1.0 - sig))).astype(bf16)
        d_gu[at, pair + pw:pair + 2 * pw] = (back * silu).astype(bf16)

    def feed_arriving(slot, carry):
        gather_step(second, 2, slot)
        at = rows(chip(slot), 2 * block)
        feed(0, at)
        second_t[:, at] = second[at].T
        pl.when(slot == 1)(lambda: hop_third(2, 1))
        pl.when(slot == 3)(lambda: hop_third(2, 2))
        return carry

    def third_grad(t):
        weight_grad(t, [
            (second_t, lambda: d_gu[:, 2 * pw * t:2 * pw * (t + 1)]),
            (dy_t, lambda: hidden[:, t * pw:(t + 1) * pw]),
        ])

    def feed_third(t):
        def body(i, carry):
            feed(t, rows(i, 2 * block))
            return carry

        lax.fori_loop(0, n // 2, body, 0)

    lax.fori_loop(0, n // 2, feed_arriving, 0)
    gather_sent(second, 2)
    hop_third(1, 3)
    third_grad(0)
    feed_third(1)
    third_grad(1)
    done = 2 * pw * (thirds - 1)

    def early_part(i, carry):
        at = rows(i, 2 * block)
        first[at] = dot_nt(d_gu[at, :done], w_gu[:, :done]).astype(bf16)
        return carry

    def last_part(left, at):
        return dot_nt(left[:, done:], w_gu[:, done:]) + jnp.concatenate([first[i] for i in at], 0).astype(f32)

    lax.fori_loop(0, n // 2, early_part, 0)
    hop_third(2, 3)
    sum_start(
        1, d_gu, last_part,
        [lambda place: feed(thirds - 1, rows(place, 2 * block))])
    third_grad(2)
    d_second = sum_finish(1)

    def norm_back(value, gain, grad):
        inv = lax.rsqrt(jnp.mean(value * value, -1, keepdims=True) + epsilon)
        weighted = grad * gain
        inner = jnp.mean(weighted * value, -1, keepdims=True)
        result = inv * weighted - value * (inv * inv * inv * inner)
        return result, jnp.sum(grad * value * inv, 0, keepdims=True)

    gain_own[...] = jnp.zeros_like(gain_own)
    part, gain_own[1:2, :] = norm_back(middle[...], fg_ref[...], d_second)
    d_mid = dy_ref[...].astype(f32) + part
    d_middle[...] = d_mid
    drain(in_plane)
    dmid[rows(c, block)] = d_mid.astype(bf16)
    gather_start(dmid, 3)
    sum_start(2, hidden, lambda left, at: dot(left, w_down[...]))
    drain(weight_sends)
    grad_near(0)

    dk_acc[...] = jnp.zeros_like(dk_acc)
    dv_acc[...] = jnp.zeros_like(dv_acc)

    def output_grad():
        def body(i, carry):
            grad = dot(mixed_low_t[...], dmid[:, rows(i, 2 * block)]).astype(bf16).T
            for k in range(2):
                for t in range(planes):
                    start = k * block + t * per
                    stage_out[t, 2 * i + k] = grad[start:start + per]
            return carry

        lax.fori_loop(0, n // 2, body, 0)
        grad_send(3)

    def attend_back(slot, q_sum):
        gather_step(dmid, 3, slot)
        place = chip(slot)
        at = rows(place, 2 * block)
        d_mix = dot_nt(w_out[...], dmid[at])
        pl.when(slot == 3)(output_grad)
        d_mix_t = jnp.concatenate([d_mix[h * head:(h + 1) * head] for h in range(group)], 1)
        d_mix_t = (d_mix_t.astype(bf16).astype(f32) * sums[place]).astype(bf16)
        delta = jnp.sum(d_mix_t.astype(f32) * mixed_t[place], 0, keepdims=True)
        weight = probs[place]
        d_prob = dot(values[...], d_mix_t)
        d_score = (weight.astype(f32) * (d_prob - delta)).astype(bf16)
        d_query = dot(keys_t[...], d_score) * scale
        for h in range(group):
            grad = turn_back(d_query[:, 2 * h * block:2 * (h + 1) * block].T, at)
            part, gain_part = norm_back(raw[at, h * head:(h + 1) * head], qg_ref[...], grad)
            d_qkv[at, h * head:(h + 1) * head] = part.astype(bf16)
            q_sum = q_sum + gain_part
        pl.when(slot == 2)(lambda: grad_near(1))
        dv_acc[...] += dot(weight, d_mix_t.T)
        dk_acc[...] += dot(d_score, stack(queries, at))
        return q_sum

    zero = jnp.zeros((1, head), f32)
    gain_own[2:3, 0:head] = lax.fori_loop(0, n // 2, attend_back, zero)
    gather_sent(dmid, 3)
    weight_grad(4, [(first_t, lambda: d_qkv[:, :qw])])
    grad_far(0)

    def project_back(i, k_sum):
        at = rows(i, 2 * block)
        grad = turn_back(dk_acc[at] * (1.0 / log2e), at)
        part, gain_part = norm_back(raw[at, qw:qw + kw], kg_ref[...], grad)
        d_qkv[at, qw:qw + kw] = part.astype(bf16)
        d_qkv[at, qw + kw:] = dv_acc[at].astype(bf16)
        return k_sum + gain_part

    gain_own[3:4, 0:head] = lax.fori_loop(0, n // 2, project_back, zero)

    weight_grad(5, [(first_t, lambda: d_qkv[:, qw:])])
    grad_far(1)
    grad_near(2)
    own_sum(0)
    drain(in_plane)
    sum_start(3, d_qkv, lambda left, at: dot_nt(left, w_qkv[...]))
    grad_far(2)
    grad_near(3)
    own_sum(1)
    hand_out(0)
    grad_far(3)
    grad_near(4)
    out_ref[...] = (middle[...] + sum_finish(2)).astype(bf16)
    grad_far(4)
    grad_near_far(5)
    own_sum(2)
    grad_near_inner(5)
    grad_far(5)
    x_part, gain_own[0:1, :] = norm_back(x_ref[...].astype(f32), ag_ref[...], sum_finish(3))
    dx_ref[...] = d_middle[...] + x_part

    def gain_plane_copy(j):
        return remote(gain_own, gain_plane.at[c], gp_send.at[j], gp_recv.at[j], partner(j), z)

    def gain_copy(d):
        return remote(gain_all.at[z], gain_all.at[z], gz_send.at[d], gz_recv.at[d], c, lax.rem(z + d, planes))

    for j in range(1, n):
        launch(in_plane, lambda j=j: gain_plane_copy(j))
    gain_plane[c] = gain_own[...]
    own_sum(3)
    hand_out(1)
    for j in range(1, n):
        gain_plane_copy(j).wait_recv()
    total = gain_plane[0]
    for i in range(1, n):
        total = total + gain_plane[i]
    gain_all[z] = total
    for d in range(1, planes):
        launch(along, lambda d=d: gain_copy(d))
    own_sum(4)
    for d in range(1, planes):
        origin = gain_all.at[lax.rem(z + planes - d, planes)]
        remote(origin, origin, gz_send.at[d], gz_recv.at[d], c, z).wait_recv()
    total = gain_all[0]
    for i in range(1, planes):
        total = total + gain_all[i]
    gains_ref[...] = total

    hand_receive(0)
    own_sum(5)
    hand_out(2)
    drain(along)
    hand_receive(1)
    hand_receive(2)
    drain(in_plane)


def finish_kernel(
    n, head, out_in, dx_in, gains_in, got_ab, got_co, got_qkv,
    out_ref, dx_ref, ag_ref, q_ref, k_ref, v_ref, qg_ref, kg_ref, o_ref, fg_ref, g_ref, u_ref, d_ref,
):
    out_ref[...] = out_in[...]
    dx_ref[...] = dx_in[...]
    ag_ref[...] = gains_in[0:1, :]
    fg_ref[...] = gains_in[1:2, :]
    qg_ref[...] = gains_in[2:3, 0:head]
    kg_ref[...] = gains_in[3:4, 0:head]
    qw, kw = q_ref.shape[1] // n, k_ref.shape[1] // n
    fw = g_ref.shape[1] // n
    pw = fw // 3
    thirds = ((got_ab, 0), (got_ab, fw), (got_co, 0))
    for i in range(n):
        q_ref[:, i * qw:(i + 1) * qw] = got_qkv[i, :, 0:qw].astype(f32)
        k_ref[:, i * kw:(i + 1) * kw] = got_qkv[i, :, qw:qw + kw].astype(f32)
        v_ref[:, i * kw:(i + 1) * kw] = got_qkv[i, :, qw + kw:].astype(f32)
        o_ref[:, i * qw:(i + 1) * qw] = got_co[i, :, fw:].astype(f32)
        for t, (got, start) in enumerate(thirds):
            plane, unit = hidden_block(i, t)
            at = plane * (g_ref.shape[1] // 4) + unit * pw
            g_ref[:, at:at + pw] = got[i, :, start:start + pw].astype(f32)
            u_ref[:, at:at + pw] = got[i, :, start + pw:start + 2 * pw].astype(f32)
            d_ref[:, at:at + pw] = got[i, :, start + 2 * pw:start + 3 * pw].astype(f32)


def plane_device(
    layer_input,
    token_positions,
    attention_gain,
    query_weight,
    key_matrix,
    value_matrix,
    query_gain,
    key_norm_gain,
    output_weight,
    feedforward_gain,
    gate_weight,
    up_weight,
    down_weight,
    out_cotangent,
):
    n = lax.axis_size("ctx")
    planes = lax.axis_size("fsdp")
    block, width = layer_input.shape[1:]
    length = token_positions.shape[1]
    head = query_gain.shape[0]
    qw = query_weight.shape[1] // n
    kw = key_matrix.shape[1] // n
    fw = gate_weight.shape[1] // n
    group = qw // head
    per = block // planes
    half = head // 2
    inverse = np.power(rope_base, -np.arange(half) * 2.0 / head).astype(np.float32)
    inverse = np.concatenate([inverse, inverse])[None]
    steps = np.arange(block // 2)[:, None] * inverse.astype(np.float64)
    step_cos, step_sin = (jnp.asarray(f(steps).astype(np.float32)) for f in (np.cos, np.sin))
    inverse = jnp.asarray(inverse)
    vmem = pl.BlockSpec(memory_space=pltpu.VMEM)
    hbm = pl.BlockSpec(memory_space=pl.ANY)
    dma = pltpu.SemaphoreType.DMA
    sizes = (fw, fw, fw, qw, qw, 2 * kw)
    low = lambda *shape: pltpu.VMEM(shape, bf16)
    wide = lambda *shape: pltpu.VMEM(shape, f32)
    scratch = [
        low(width, qw + 2 * kw), low(width, 2 * fw), low(qw, width), low(fw, width),
        low(planes * (output_weight.shape[0] // n), width),
        low(length, width), low(length, width), low(length, width),
        low(width, length), low(width, length), low(width, length),
        wide(length, head), wide(length, head), wide(length, head),
        wide(length, qw + kw), low(length, qw), low(length, kw), low(length, kw),
        low(kw, length), low(kw, length), low(n // 2, length, 2 * group * block), wide(n // 2, 1, 2 * group * block),
        wide(n // 2, head, 2 * group * block), low(length, qw), low(qw, length),
        low(length, fw), low(length, 2 * fw), low(length, qw + 2 * kw),
        wide(length, kw), wide(length, kw),
    ]
    scratch += [low(planes, n, per, size) for size in sizes]
    scratch += [low(planes + 1, n, per, size) for size in sizes]
    scratch += [low(n, per, sizes[m] + sizes[m + 1]) for m in (0, 2, 4)]
    scratch += [low(2, 4, block, width)] * 2 + [low(2, 3, block, width)] * 2 + [wide(2, block, width), wide(2, block, width)]
    scratch += [
        wide(block, width), wide(block, width), wide(8, width), wide(n, 8, width), wide(planes, 8, width),
        dma((13,)), dma((8, 6)), dma((8, planes)), dma((1, 7)), dma((1, 4)),
        dma((4, n)), dma((4, n)), dma((4, 4)), dma((4, 4)), dma((4, 4)), dma((4, 4)),
        dma((6, planes)), dma((6, planes + 1)), dma((3, n)), dma((3, n)), dma((n,)), dma((n,)),
        dma((planes,)), dma((planes,)),
    ]
    shapes = [
        jax.ShapeDtypeStruct((block, width), bf16),
        jax.ShapeDtypeStruct((block, width), f32),
        jax.ShapeDtypeStruct((8, width), f32),
    ] + [jax.ShapeDtypeStruct((n, per, sizes[m] + sizes[m + 1]), bf16) for m in (0, 2, 4)]
    results = pl.pallas_call(
        functools.partial(layer_kernel, n, planes, block, head, group, fw),
        out_shape=shapes,
        in_specs=[vmem] * 10 + [hbm] * 7,
        out_specs=[vmem] * len(shapes),
        scratch_shapes=scratch,
        compiler_params=pltpu.CompilerParams(
            collective_id=0, has_side_effects=True, vmem_limit_bytes=60 * 1024 * 1024),
    )(
        layer_input[0], out_cotangent[0], token_positions, inverse, step_cos, step_sin,
        attention_gain[None], feedforward_gain[None], query_gain[None], key_norm_gain[None],
        query_weight, key_matrix, value_matrix, output_weight, gate_weight, up_weight, down_weight,
    )
    plain = lambda rows, columns, kind=f32: jax.ShapeDtypeStruct((rows, columns), kind)
    finals = [
        plain(block, width, bf16), plain(block, width), plain(1, width),
        plain(per, n * qw), plain(per, n * kw), plain(per, n * kw), plain(1, head), plain(1, head),
        plain(per, n * qw), plain(1, width), plain(per, n * fw), plain(per, n * fw), plain(per, n * fw),
    ]
    done = pl.pallas_call(
        functools.partial(finish_kernel, n, head),
        out_shape=finals,
        in_specs=[vmem] * len(shapes),
        out_specs=[vmem] * len(finals),
    )(*results)
    out, dx, ag, q, k, v, qg, kg, o, fg, g, u, d = done
    return out[None], dx[None], ag[0], q, k, v, qg[0], kg[0], o.T, fg[0], g, u, d.T


def solution(mesh):
    in_specs = (
        P("fsdp", "ctx", None),
        P("fsdp", None),
        P(),
        P("fsdp", None),
        P("fsdp", None),
        P("fsdp", None),
        P(),
        P(),
        P("fsdp", None),
        P(),
        P("fsdp", None),
        P("fsdp", None),
        P("fsdp", None),
        P("fsdp", "ctx", None),
    )
    out_specs = (
        P("fsdp", "ctx", None),
        P("fsdp", "ctx", None),
        P(),
        P(("ctx", "fsdp"), None),
        P(("ctx", "fsdp"), None),
        P(("ctx", "fsdp"), None),
        P(),
        P(),
        P(None, ("ctx", "fsdp")),
        P(),
        P(("ctx", "fsdp"), None),
        P(("ctx", "fsdp"), None),
        P(None, ("ctx", "fsdp")),
    )

    def run(*arguments):
        n, planes = mesh.shape["ctx"], mesh.shape["fsdp"]
        key_heads = arguments[4].shape[1] // arguments[6].shape[0]
        whole_heads = n == 8 and planes == 4 and key_heads == n
        return jax.shard_map(
            plane_device if whole_heads else on_device,
            mesh=mesh, in_specs=in_specs, out_specs=out_specs, check_vma=False,
        )(*arguments)

    return run
```

```python
import functools

import jax
import jax.numpy as jnp
import numpy as np
from jax import lax
from jax.experimental import pallas as pl
from jax.experimental.pallas import tpu as pltpu
from jax.sharding import PartitionSpec as P

epsilon = 1e-06
rope_base = 1000000.0
masked_score = -1e30


def from_behind(block, axis, distance):
    devices = range(lax.axis_size(axis))
    route = [((i - distance) % len(devices), i) for i in devices]
    return lax.ppermute(block, axis, route)


def rotate(value_rows):
    half = value_rows.shape[-1] // 2
    return jnp.concatenate([-value_rows[..., half:], value_rows[..., :half]], -1)


def rotate_back(value_rows):
    half = value_rows.shape[-1] // 2
    return jnp.concatenate([value_rows[..., half:], -value_rows[..., :half]], -1)


def rope_tables(token_offsets, head_size):
    half = head_size // 2
    inverse = rope_base ** (-(jnp.arange(half).astype(jnp.float32) * 2.0) / head_size)
    angles = token_offsets.astype(jnp.float32)[:, None] * inverse[None, :]
    cosine = jnp.cos(angles)
    sine = jnp.sin(angles)
    return (jnp.concatenate([cosine, cosine], -1), jnp.concatenate([sine, sine], -1))


def norm_scale(value_rows):
    return lax.rsqrt(jnp.mean(value_rows * value_rows, -1, keepdims=True) + epsilon)


def norm_back(value_rows, scale, gain, grad):
    weighted = grad * gain
    inner = jnp.mean(weighted * value_rows, -1, keepdims=True)
    result = scale * weighted - value_rows * scale * scale * scale * inner
    gain_part = jnp.sum((grad * value_rows * scale).reshape(-1, gain.shape[0]), 0)
    return (result, gain_part)


def row_products(left, pieces):
    return tuple((jnp.dot(left, piece, preferred_element_type=jnp.float32) for piece in pieces))


def column_products(rights, pieces):
    total = jnp.einsum("tc,rc->tr", rights[0], pieces[0], preferred_element_type=jnp.float32)
    for right, piece in zip(rights[1:], pieces[1:]):
        total = total + jnp.einsum("tc,rc->tr", right, piece, preferred_element_type=jnp.float32)
    return total


def on_device(
    layer_input,
    token_positions,
    attention_gain,
    query_weight,
    key_matrix,
    value_matrix,
    query_gain,
    key_norm_gain,
    output_weight,
    feedforward_gain,
    gate_weight,
    up_weight,
    down_weight,
    out_cotangent,
):
    hidden_in = layer_input[0].astype(jnp.float32)
    count = hidden_in.shape[0]
    head_size = query_gain.shape[0]
    query_width = query_weight.shape[1]
    key_width = key_matrix.shape[1]
    inner_width = gate_weight.shape[1]
    heads = query_width // head_size
    key_heads = key_width // head_size
    group = heads // key_heads
    scale = head_size ** (-0.5)
    cycles = lax.axis_size("ctx")
    own_index = lax.axis_index("ctx")
    sequence_pos = token_positions[0]
    token_offsets = lax.dynamic_slice_in_dim(sequence_pos, own_index * count, count)
    cosine, sine = rope_tables(token_offsets, head_size)
    cosine = cosine[:, None, :]
    sine = sine[:, None, :]
    first_scale = norm_scale(hidden_in)
    first = (hidden_in * first_scale * attention_gain).astype(jnp.bfloat16)
    query_raw, key_unnormed, value_unnormed = row_products(
        first,
        (
            lax.all_gather(query_weight, "fsdp", axis=0, tiled=True),
            lax.all_gather(key_matrix, "fsdp", axis=0, tiled=True),
            lax.all_gather(value_matrix, "fsdp", axis=0, tiled=True),
        ),
    )
    query_heads = query_raw.reshape(count, heads, head_size)
    query_scale = norm_scale(query_heads)
    query_normed = query_heads * query_scale * query_gain
    query_rot = query_normed * cosine + rotate(query_normed) * sine
    query_grouped = (
        query_rot.reshape(count, key_heads, group, head_size)
        .transpose(1, 2, 0, 3)
        .astype(jnp.bfloat16)
    )
    key_heads_raw = key_unnormed.reshape(count, key_heads, head_size)
    key_scale = norm_scale(key_heads_raw)
    key_normed = key_heads_raw * key_scale * key_norm_gain
    key_low = (
        (key_normed * cosine + rotate(key_normed) * sine)
        .reshape(count, key_width)
        .astype(jnp.bfloat16)
    )
    value_low = value_unnormed.astype(jnp.bfloat16)
    rowmax = jnp.full((key_heads, group, count), masked_score, jnp.float32)
    keys_piece = lax.all_gather(key_low, "ctx", axis=0, tiled=True).reshape(
        -1, key_heads, head_size
    )
    values_piece = lax.all_gather(value_low, "ctx", axis=0, tiled=True).reshape(
        -1, key_heads, head_size
    )
    key_pos = sequence_pos
    allowed = token_offsets[:, None] >= key_pos[None, :]
    scores = (
        jnp.einsum("kgtd,skd->kgts", query_grouped, keys_piece, preferred_element_type=jnp.float32)
        * scale
    )
    scores = jnp.where(allowed, scores, masked_score)
    newmax = jnp.maximum(rowmax, jnp.max(scores, -1))
    weights = jnp.where(allowed, jnp.exp(scores - newmax[..., None]), 0.0)
    accum = jnp.einsum(
        "kgts,skd->kgtd",
        weights.astype(jnp.bfloat16),
        values_piece,
        preferred_element_type=jnp.float32,
    )
    rowsum = jnp.sum(weights, -1)
    accum, rowmax, rowsum = (accum, newmax, rowsum)
    normalized = accum / rowsum[..., None]
    logsum = rowmax + jnp.log(rowsum)
    attention_low = (
        normalized.transpose(2, 0, 1, 3).reshape(count, query_width).astype(jnp.bfloat16)
    )
    output_whole = lax.all_gather(output_weight, "fsdp", axis=0, tiled=True)
    branch_out = jnp.dot(attention_low, output_whole, preferred_element_type=jnp.float32)
    middle = hidden_in + branch_out
    second_scale = norm_scale(middle)
    second = (middle * second_scale * feedforward_gain).astype(jnp.bfloat16)
    gate, up = row_products(
        second,
        (
            lax.all_gather(gate_weight, "fsdp", axis=0, tiled=True),
            lax.all_gather(up_weight, "fsdp", axis=0, tiled=True),
        ),
    )
    sigmoid_gate = jax.nn.sigmoid(gate)
    silu_gate = gate * sigmoid_gate
    hidden_low = (silu_gate * up).astype(jnp.bfloat16)
    (down_out,) = row_products(
        hidden_low, (lax.all_gather(down_weight, "fsdp", axis=0, tiled=True),)
    )
    layer_output = (middle + down_out).astype(jnp.bfloat16)[None]
    cotangent = out_cotangent[0]
    hidden_grad = column_products(
        (cotangent,), lax.all_gather((down_weight,), "fsdp", axis=0, tiled=True)
    )
    up_low = (hidden_grad * silu_gate).astype(jnp.bfloat16)
    gate_low = (hidden_grad * up * sigmoid_gate * (1.0 + gate * (1.0 - sigmoid_gate))).astype(
        jnp.bfloat16
    )
    second_grad = column_products(
        (gate_low, up_low), lax.all_gather((gate_weight, up_weight), "fsdp", axis=0, tiled=True)
    )
    middle_part, feedforward_part = norm_back(middle, second_scale, feedforward_gain, second_grad)
    middle_grad = cotangent.astype(jnp.float32) + middle_part
    middle_low = middle_grad.astype(jnp.bfloat16)
    attention_grad = jnp.einsum(
        "tc,rc->tr", middle_low, output_whole, preferred_element_type=jnp.float32
    )
    attention_grad_low = attention_grad.astype(jnp.bfloat16)
    mixed_grad = attention_grad_low.reshape(count, key_heads, group, head_size).transpose(
        1, 2, 0, 3
    )
    delta = jnp.sum(mixed_grad.astype(jnp.float32) * normalized, -1)

    def cycle_step(index, carry):
        keys_held, values_held, key_acc, value_acc, query_acc = carry
        anchor = (own_index - index) % cycles
        key_pos = lax.dynamic_slice_in_dim(sequence_pos, anchor * count, count)
        keys_piece = keys_held.astype(jnp.bfloat16).reshape(count, key_heads, head_size)
        values_piece = values_held.astype(jnp.bfloat16).reshape(count, key_heads, head_size)
        allowed = token_offsets[:, None] >= key_pos[None, :]
        scores = (
            jnp.einsum(
                "kgtd,skd->kgts", query_grouped, keys_piece, preferred_element_type=jnp.float32
            )
            * scale
        )
        probs = jnp.where(allowed, jnp.exp(scores - logsum[..., None]), 0.0)
        value_acc = value_acc + jnp.einsum(
            "kgts,kgtd->skd",
            probs.astype(jnp.bfloat16),
            mixed_grad,
            preferred_element_type=jnp.float32,
        ).reshape(count, key_width)
        prob_grad = jnp.einsum(
            "kgtd,skd->kgts", mixed_grad, values_piece, preferred_element_type=jnp.float32
        )
        score_grad = (probs * (prob_grad - delta[..., None])).astype(jnp.bfloat16)
        query_acc = (
            query_acc
            + jnp.einsum(
                "kgts,skd->kgtd", score_grad, keys_piece, preferred_element_type=jnp.float32
            )
            * scale
        )
        key_acc = (
            key_acc
            + jnp.einsum(
                "kgts,kgtd->skd", score_grad, query_grouped, preferred_element_type=jnp.float32
            ).reshape(count, key_width)
            * scale
        )
        moved = (
            from_behind(keys_held.astype(jnp.bfloat16), "ctx", 1).astype(keys_held.dtype),
            from_behind(values_held.astype(jnp.bfloat16), "ctx", 1).astype(values_held.dtype),
            from_behind(key_acc.astype(jnp.bfloat16), "ctx", 1).astype(key_acc.dtype),
            from_behind(value_acc.astype(jnp.bfloat16), "ctx", 1).astype(value_acc.dtype),
        )
        return (moved[0], moved[1], moved[2], moved[3], query_acc)

    start_cycle = (
        key_low.astype(jnp.float32),
        value_low.astype(jnp.float32),
        jnp.zeros((count, key_width), jnp.float32),
        jnp.zeros((count, key_width), jnp.float32),
        jnp.zeros((key_heads, group, count, head_size), jnp.float32),
    )
    cycle_done = lax.fori_loop(0, cycles, cycle_step, start_cycle)
    key_acc = cycle_done[2]
    value_acc = cycle_done[3]
    query_acc = cycle_done[4]
    query_rot_grad = query_acc.transpose(2, 0, 1, 3).reshape(count, heads, head_size)
    query_normed_grad = query_rot_grad * cosine + rotate_back(query_rot_grad * sine)
    query_heads_grad, query_part = norm_back(
        query_heads, query_scale, query_gain, query_normed_grad
    )
    query_low_grad = query_heads_grad.reshape(count, query_width).astype(jnp.bfloat16)
    key_rot_grad = key_acc.reshape(count, key_heads, head_size)
    key_normed_grad = key_rot_grad * cosine + rotate_back(key_rot_grad * sine)
    key_heads_grad, key_part = norm_back(key_heads_raw, key_scale, key_norm_gain, key_normed_grad)
    key_low_grad = key_heads_grad.reshape(count, key_width).astype(jnp.bfloat16)
    value_low_grad = value_acc.astype(jnp.bfloat16)
    first_grad = column_products(
        (query_low_grad, key_low_grad, value_low_grad),
        lax.all_gather((query_weight, key_matrix, value_matrix), "fsdp", axis=0, tiled=True),
    )
    input_part, attention_part = norm_back(hidden_in, first_scale, attention_gain, first_grad)
    input_gradient = (middle_grad + input_part)[None]
    rights_first = jnp.concatenate([query_low_grad, key_low_grad, value_low_grad], 1)
    rights_second = jnp.concatenate([gate_low, up_low], 1)
    pairs = (
        (first, rights_first),
        (second, rights_second),
        (middle_low, attention_low),
        (cotangent, hidden_low),
    )
    parts = []
    for left, right in pairs:
        parts.append(jnp.einsum("tr,tc->rc", left, right, preferred_element_type=jnp.float32))
    sums = lax.psum_scatter(
        jnp.concatenate(parts, 1), ("ctx", "fsdp"), scatter_dimension=0, tiled=True
    )
    edges = [0, query_width, query_width + key_width, query_width + 2 * key_width]
    edges = edges + [edges[3] + inner_width, edges[3] + 2 * inner_width]
    edges = edges + [edges[5] + query_width, edges[5] + query_width + inner_width]
    query_gradient = sums[:, edges[0] : edges[1]]
    key_gradient = sums[:, edges[1] : edges[2]]
    value_gradient = sums[:, edges[2] : edges[3]]
    gate_gradient = sums[:, edges[3] : edges[4]]
    up_gradient = sums[:, edges[4] : edges[5]]
    output_gradient = sums[:, edges[5] : edges[6]].T
    down_gradient = sums[:, edges[6] : edges[7]].T
    attention_total, query_total, key_total, feedforward_total = lax.psum(
        (attention_part, query_part, key_part, feedforward_part), ("ctx", "fsdp")
    )
    return (
        layer_output,
        input_gradient,
        attention_total,
        query_gradient,
        key_gradient,
        value_gradient,
        query_total,
        key_total,
        output_gradient,
        feedforward_total,
        gate_gradient,
        up_gradient,
        down_gradient,
    )


MESH = pl.DeviceIdType.MESH
f32 = jnp.float32
bf16 = jnp.bfloat16


def dot(left, right):
    return jnp.dot(left, right, preferred_element_type=f32)


def dot_nt(left, right):
    return lax.dot_general(left, right, (((1,), (1,)), ((), ())), preferred_element_type=f32)


def dot_tn(left, right):
    return lax.dot_general(left, right, (((0,), (0,)), ((), ())), preferred_element_type=f32)


def hidden_block(device, third):
    def plane(i, t):
        return ((3, 1, 2), (0, 2, 1), (0, 3, 2), (3, 0, 1))[i // 4 * 2 + i % 2][t]

    own = plane(device, third)
    return own, sum(plane(i, t) == own for i in range(device) for t in range(3))


def layer_kernel(
    n, planes, block, head, group, fw,
    x_ref, dy_ref, pos_row, inverse_ref, step_cos, step_sin, ag_ref, fg_ref, qg_ref, kg_ref,
    wq, wk, wv, wo, wg, wu, wd,
    out_ref, dx_ref, gains_ref, got_ab, got_co, got_qkv,
    w_qkv, w_gu, w_out, w_down, t_out,
    first, dy_all, second, first_t, dy_t, second_t,
    positions, cosine, sine,
    raw, queries, keys, values, keys_t, values_t, probs, sums, mixed_t, mixed_low, mixed_low_t,
    hidden, d_gu, d_qkv, dk_acc, dv_acc,
    stage_a, stage_b, stage_c, stage_out, stage_q, stage_kv,
    land_a, land_b, land_c, land_out, land_q, land_kv,
    own_ab, own_co, own_qkv,
    rs_sa, rs_ra, rs_sb, rs_rb, rs_acc,
    middle, d_middle, gain_own, gain_plane, gain_all,
    local_sem, wz_send, wz_recv, hand_send, hand_recv,
    ag_send, ag_recv, ra_send, ra_recv, rb_send, rb_recv,
    zr_send, zr_recv, aa_send, aa_recv, gp_send, gp_recv, gz_send, gz_recv,
):
    c = lax.axis_index("ctx")
    z = lax.axis_index("fsdp")
    dmid = first
    cy, cx, ck = lax.div(c, 4), lax.rem(lax.div(c, 2), 2), lax.rem(c, 2)
    ci = lax.rem(c, 4)
    sign = 1 - 2 * ck
    qw, kw = group * head, head
    pw = 128
    thirds = fw // pw
    width = x_ref.shape[1]
    scale = head ** (-0.5)
    log2e = 1.4426950408889634
    gots = (got_ab, got_co, got_qkv)
    owns = (own_ab, own_co, own_qkv)
    stages = (stage_a, stage_b, stage_c, stage_out, stage_q, stage_kv)
    lands = (land_a, land_b, land_c, land_out, land_q, land_kv)

    def partner(j):
        y = lax.rem(cy + lax.div(j, 4), 2)
        x = lax.rem(cx + lax.rem(lax.div(j, 2), 2), 2)
        k = lax.rem(ck + lax.rem(j, 2), 2)
        return y * 4 + x * 2 + k

    def chip(slot):
        return lax.rem(cy + lax.div(slot, 2), 2) * 2 + lax.rem(cx + lax.rem(slot, 2), 2)

    def rows(start, size):
        return pl.ds(pl.multiple_of(start * size, size), size)

    def remote(src, dst, send, recv, ctx, plane):
        return pltpu.make_async_remote_copy(
            src_ref=src, dst_ref=dst, send_sem=send, recv_sem=recv,
            device_id={"ctx": ctx, "fsdp": plane}, device_id_type=MESH,
        )

    in_plane, along, weight_sends = [], [], []

    def launch(started, copy, when=None):
        if when is None:
            copy().start()
        else:
            pl.when(when)(lambda: copy().start())
        started.append((copy, when))

    def drain(started):
        for copy, when in started:
            if when is None:
                copy().wait_send()
            else:
                pl.when(when)(lambda copy=copy: copy().wait_send())
        started.clear()

    def pick(values):
        return sum(jnp.where(c == i, value, 0) for i, value in enumerate(values))

    unit_plane = [pick([hidden_block(i, t)[0] for i in range(n)]) for t in range(thirds)]
    unit_block = [pick([hidden_block(i, t)[1] for i in range(n)]) for t in range(thirds)]
    plane_blocks = wd.shape[0] // pw

    own_rows = wq.shape[0]
    out_rows = wo.shape[0] // n

    def own_slices():
        mine = rows(z, own_rows)
        pairs = [
            (wq.at[:, rows(c, qw)], w_qkv.at[mine, 0:qw]),
            (wk.at[:, rows(c, kw)], w_qkv.at[mine, qw:qw + kw]),
            (wv.at[:, rows(c, kw)], w_qkv.at[mine, qw + kw:qw + 2 * kw]),
            (wo.at[rows(c, out_rows)], t_out.at[rows(z, out_rows)]),
        ]
        for t in range(thirds):
            at = 2 * pw * t
            unit = unit_plane[t] * plane_blocks + unit_block[t]
            pairs.append((wg.at[:, rows(unit, pw)], w_gu.at[mine, at:at + pw]))
            pairs.append((wu.at[:, rows(unit, pw)], w_gu.at[mine, at + pw:at + 2 * pw]))
        return pairs

    local = [pltpu.make_async_copy(src, dst, local_sem.at[i]) for i, (src, dst) in enumerate(own_slices())]
    for copy in local:
        copy.start()

    def own_down(t):
        return pltpu.make_async_copy(
            wd.at[rows(unit_block[t], pw)], w_down.at[t * pw:(t + 1) * pw], local_sem.at[4 + 2 * thirds + t])

    holds = [unit_plane[t] == z for t in range(thirds)]
    for t in range(thirds):
        pl.when(holds[t])(lambda t=t: own_down(t).start())

    for land in lands:
        @pl.when(z == 0)
        def _(land=land):
            land[0] = jnp.zeros(land.shape[1:], bf16)

        @pl.when(z == planes - 1)
        def _(land=land):
            land[planes] = jnp.zeros(land.shape[1:], bf16)

    barrier = pltpu.get_barrier_semaphore()
    for j in range(1, n):
        pl.semaphore_signal(barrier, inc=1, device_id={"ctx": partner(j), "fsdp": z}, device_id_type=MESH)
    for d in range(1, planes):
        pl.semaphore_signal(
            barrier, inc=1, device_id={"ctx": c, "fsdp": lax.rem(z + d, planes)}, device_id_type=MESH)
    x = x_ref[...].astype(f32)
    x_scale = lax.rsqrt(jnp.mean(x * x, -1, keepdims=True) + epsilon)
    first[rows(c, block)] = (x * x_scale * ag_ref[...]).astype(bf16)
    dy_all[rows(c, block)] = dy_ref[...]
    for copy in local[:3]:
        copy.wait()
    pl.semaphore_wait(barrier, n + planes - 2)

    def inside(t):
        return jnp.logical_and(t >= 0, t < planes)

    weights = [
        (lambda o: w_qkv.at[rows(o, own_rows)], None),
        (lambda o: t_out.at[rows(o, out_rows)], 0),
    ]
    for t in range(thirds):
        weights.append((lambda o, t=t: w_gu.at[rows(o, own_rows), 2 * pw * t:2 * pw * (t + 1)], None))
        weights.append((lambda o, t=t: w_down.at[t * pw:(t + 1) * pw], None))

    def weight_copy(w, slot, origin, target):
        part = weights[w][0](origin)
        return remote(part, part, wz_send.at[w, slot], wz_recv.at[w, origin], c, target)

    def from_plane(w, origin):
        return origin == unit_plane[(w - 3) // 2] if w >= 3 and w % 2 else None

    def both(one, other):
        return one if other is None else jnp.logical_and(one, other)

    def hand_split(origin, valid):
        mine = 2 * origin + cy == c
        return jnp.logical_and(valid, jnp.logical_not(mine)), jnp.logical_and(valid, mine)

    def weight_start(w):
        for side in range(2):
            d = sign * (1 - 2 * side)
            launch(
                weight_sends, lambda side=side, d=d: weight_copy(w, side, z, z + d),
                both(inside(z + d), from_plane(w, z)))
        if weights[w][1] is not None:
            hand_over(w, z, 0, *hand_split(z, True))

    def hand_target(h):
        return lambda i: w_out.at[rows(i, out_rows)]

    def hand_copy(w, origin, slot):
        h = weights[w][1]
        return remote(
            weights[w][0](origin), hand_target(h)(ci), hand_send.at[h, slot], hand_recv.at[h, ci], 2 * origin + cy, z)

    def hand_over(w, origin, slot, away, here):
        launch(in_plane, lambda: hand_copy(w, origin, slot), away)

        @pl.when(here)
        def _():
            hand_target(weights[w][1])(ci)[...] = weights[w][0](origin)[...]

    def hand_arrive(w):
        h = weights[w][1]
        for i in range(4):
            @pl.when(4 * ck + i != c)
            def _(i=i):
                part = hand_target(h)(i)
                remote(part, part, hand_send.at[h, 0], hand_recv.at[h, i], c, z).wait_recv()

    hops = {}
    for w in range(len(weights)):
        for d in range(1, planes):
            for side, way in enumerate((1, -1)):
                origin = z - way * d
                valid = both(inside(origin), from_plane(w, origin))
                passed = jnp.logical_and(valid, inside(z + way))
                split = None if weights[w][1] is None else hand_split(origin, valid)
                hops[w, d, side] = origin, z + way, valid, passed, split

    def weight_hop(w, d):
        for side in range(2):
            origin, following, valid, passed, split = hops[w, d, side]
            pl.when(valid)(lambda: weight_copy(w, 0, origin, z).wait_recv())
            if d < planes - 1:
                launch(
                    weight_sends,
                    lambda side=side, origin=origin, following=following: weight_copy(
                        w, 2 * d + side, origin, following),
                    passed)
            if split is not None:
                hand_over(w, origin, 2 * d - 1 + side, *split)

    def gather_copy(buf, g, j, send, origin, target):
        part = buf.at[rows(origin, block)]
        return remote(part, part, ag_send.at[g, send], ag_recv.at[g, j], target, z)

    def gather_start(buf, g):
        for j in (1, 2 + 2 * ck, 4 - 2 * ck):
            launch(in_plane, lambda j=j: gather_copy(buf, g, j, j, c, partner(j)))

    def gather_half(buf, g, j):
        half = block // 2
        part = buf.at[pl.ds(pl.multiple_of(partner(j) * block + (half if j == 2 else 0), half), half)]
        at = 0 if j == 2 else 6
        return remote(part, part, ag_send.at[g, at], ag_recv.at[g, at], partner(6 - j), z)

    def gather_diagonal(buf, g):
        half = block // 2
        for at in (6, 0):
            part = buf.at[pl.ds(pl.multiple_of(partner(6) * block + (0 if at == 6 else half), half), half)]
            remote(part, part, ag_send.at[g, at], ag_recv.at[g, at], c, z).wait_recv()

    def gather_forward(buf, g, j):
        return gather_copy(buf, g, j + 1, j + 1, partner(j), partner(1))

    def gather_take(buf, g, j):
        if j == 6:
            gather_diagonal(buf, g)
        else:
            gather_copy(buf, g, j, j, partner(j), c).wait_recv()
            gather_half(buf, g, j).start()
        gather_forward(buf, g, j).start()

    def gather_sent(buf, g):
        for j in (2, 4, 6):
            in_plane.append((lambda j=j: gather_forward(buf, g, j), None))
            if j < 6:
                in_plane.append((lambda j=j: gather_half(buf, g, j), None))

    def gather_finish(buf, g):
        for j in (2, 4, 6):
            gather_take(buf, g, j)
        gather_sent(buf, g)
        for j in (1, 3, 5, 7):
            gather_copy(buf, g, j, j, partner(j), c).wait_recv()

    def gather_step(buf, g, slot):
        @pl.when(slot == 1)
        def _():
            gather_take(buf, g, 2)
            gather_take(buf, g, 4)

        pl.when(slot == 3)(lambda: gather_take(buf, g, 6))
        gather_copy(buf, g, 2 * slot + 1, 0, partner(2 * slot + 1), c).wait_recv()

    def sum_pair_copy(s, slot):
        return remote(rs_sa.at[s % 2, slot], rs_ra.at[s % 2, slot], ra_send.at[s, slot], ra_recv.at[s, slot], partner(1), z)

    def sum_chip_copy(s, slot):
        return remote(
            rs_sb.at[s % 2, slot - 1], rs_rb.at[s % 2, slot - 1], rb_send.at[s, slot], rb_recv.at[s, slot], partner(2 * slot), z)

    def sum_half_copy(s, slot):
        half = block // 2
        at = pl.ds(pl.multiple_of((slot - 1) * half, half), half)
        return remote(
            rs_sb.at[s % 2, 2, at], rs_rb.at[s % 2, 2, at], rb_send.at[s, 6 - 3 * slot], rb_recv.at[s, 6 - 3 * slot],
            partner(6 - 2 * slot), z)

    def sum_slot(p):
        return jnp.where(p == 0, 3, jnp.where(p == 1, 2 - ck, jnp.where(p == 2, 1 + ck, 0)))

    def sum_start(s, left, partial, prepare=None, ready=None, during=()):
        if prepare is not None:
            for step in prepare:
                step(chip(sum_slot(0)))
        if ready is not None:
            ready()

        def body(p, carry):
            slot = sum_slot(p)
            at = [rows(partner(2 * slot + 1), block), rows(partner(2 * slot), block)]
            both = partial(jnp.concatenate([left[i] for i in at], 0))
            rs_sa[s % 2, slot] = both[:block].astype(bf16)
            sum_pair_copy(s, slot).start()

            @pl.when(p < 3)
            def _():
                rs_sb[s % 2, slot - 1] = both[block:].astype(bf16)

            @pl.when(p == 3)
            def _():
                rs_acc[s % 2] = both[block:]


            def pair_sum(q):
                before = sum_slot(q)
                sum_pair_copy(s, before).wait_recv()
                rs_sb[s % 2, before - 1] = rs_sb[s % 2, before - 1] + rs_ra[s % 2, before]

            def chip_send(q):
                before = sum_slot(q)
                half = block // 2
                at = pl.ds(pl.multiple_of((before - 1) * half, half), half)
                sum_half_copy(s, before).wait_recv()
                rs_sb[s % 2, before - 1, at] = rs_sb[s % 2, before - 1, at] + rs_rb[s % 2, 2, at]
                sum_chip_copy(s, before).start()

            early = prepare is not None and len(prepare) > 1

            @pl.when(p == 1)
            def _():
                pair_sum(0)
                sum_half_copy(s, 1).start()
                sum_half_copy(s, 2).start()

            @pl.when(p == 2 if early else p > 1)
            def _():
                pair_sum(p - 1)
                chip_send(p - 1)

            if prepare is not None:
                @pl.when(p < 3)
                def _():
                    prepare[0](chip(sum_slot(p + 1)))

            if early:
                @pl.when(p == 2)
                def _():
                    pair_sum(2)
                    chip_send(2)

                @pl.when(p < 3)
                def _():
                    for step in prepare[1:]:
                        step(chip(sum_slot(p + 1)))

            for k, poll in enumerate(during):
                pl.when(p == k)(poll)
            return carry

        lax.fori_loop(0, 4, body, 0)
        for slot in range(4):
            in_plane.append((lambda slot=slot: sum_pair_copy(s, slot), None))
        for slot in (1, 2):
            in_plane.append((lambda slot=slot: sum_half_copy(s, slot), None))
            in_plane.append((lambda slot=slot: sum_chip_copy(s, slot), None))
        sum_pair_copy(s, 0).wait_recv()
        rs_acc[s % 2] = rs_acc[s % 2] + rs_ra[s % 2, 0].astype(f32)

    def sum_finish(s):
        total = rs_acc[s % 2]
        for slot in (1, 2):
            sum_chip_copy(s, slot).wait_recv()
            total = total + rs_rb[s % 2, slot - 1].astype(f32)
        return total

    per = block // planes

    at_edge = jnp.logical_or(z == 0, z == planes - 1)
    edge_targets = [jnp.where(z == 0, planes - 1 - k, k) for k in range(planes - 1)]

    def weight_grad(m, parts):
        def body(i, carry):
            at = 0
            for left, right in parts:
                value = right()
                grad = dot(left[rows(i, 4 * block)], value)
                for k in range(4):
                    for t in range(planes):
                        start = k * block + t * per
                        stages[m][t, 4 * i + k, :, at:at + value.shape[1]] = grad[start:start + per].astype(bf16)
                at += value.shape[1]
            return carry

        lax.fori_loop(0, n // 4, body, 0)
        grad_send(m)

    def grad_send(m):
        for t in edge_targets:
            launch(along, lambda t=t: grad_copy(m, t), at_edge)

    def grad_copy(m, t):
        way = jnp.where(z < t, 1, -1)
        last = z + way == t
        slot = jnp.where(jnp.logical_and(last, way < 0), planes, t)
        return remote(
            stages[m].at[t], lands[m].at[slot], zr_send.at[m, t], zr_recv.at[m, slot], c, z + way)

    def grad_arrive(m, slot):
        part = lands[m].at[slot]
        remote(part, part, zr_send.at[m, 0], zr_recv.at[m, slot], c, z).wait_recv()

    def grad_pass(m, t, valid):
        @pl.when(valid)
        def _():
            grad_arrive(m, t)
            stages[m][t] = stages[m][t] + lands[m][t]

        launch(along, lambda: grad_copy(m, t), valid)

    is_low, is_high = z == 1, z == planes - 2

    def grad_near_far(m):
        grad_pass(m, 3, is_low)
        grad_pass(m, 0, is_high)

    def grad_near_inner(m):
        grad_pass(m, 2, is_low)
        grad_pass(m, 1, is_high)

    def grad_near(m):
        grad_near_far(m)
        grad_near_inner(m)

    def grad_far(m):
        grad_pass(m, 3, is_high)
        grad_pass(m, 0, is_low)

    def owner_copy(g, j):
        return remote(owns[g].at[partner(j)], gots[g].at[c], aa_send.at[g, j], aa_recv.at[g, j], partner(j), z)

    def own_sum(m):
        pl.when(z > 0)(lambda: grad_arrive(m, z))
        pl.when(z < planes - 1)(lambda: grad_arrive(m, planes))
        total = stages[m][z].astype(f32) + lands[m][z].astype(f32) + lands[m][planes].astype(f32)
        first_size = stages[m // 2 * 2].shape[3]
        if m % 2:
            owns[m // 2][:, :, first_size:] = total.astype(bf16)
        else:
            owns[m // 2][:, :, :first_size] = total.astype(bf16)

    def hand_out(g):
        for j in (2 + 2 * ck, 3 + 2 * ck, 4 - 2 * ck, 5 - 2 * ck, 6, 7, 1):
            launch(in_plane, lambda j=j: owner_copy(g, j))
        gots[g][c] = owns[g][c]

    def hand_receive(g):
        for j in range(1, n):
            owner_copy(g, j).wait_recv()

    weight_start(0)
    gather_start(first, 0)
    for copy in local[3:]:
        copy.wait()
    for t in range(thirds):
        pl.when(holds[t])(lambda t=t: own_down(t).wait())

    spread = jnp.broadcast_to(pos_row[...].astype(f32), (head, pos_row.shape[1]))
    positions[...] = spread.T
    side = jnp.where(lax.broadcasted_iota(jnp.int32, (1, head), 1) < head // 2, -1.0, 1.0)

    def table(i, carry):
        run = step_cos.shape[0]
        at = rows(i, run)
        start = positions[pl.ds(pl.multiple_of(i * run, run), 1)] * inverse_ref[...]
        start_cos, start_sin = jnp.cos(start), jnp.sin(start)
        cosine[at] = start_cos * step_cos[...] - start_sin * step_sin[...]
        sine[at] = (start_sin * step_cos[...] + start_cos * step_sin[...]) * side
        return carry

    def turn_over(src, dst):
        def body(i, carry):
            at = rows(i, block)
            dst[:, at] = src[at].T
            return carry

        lax.fori_loop(0, n, body, 0)

    lax.fori_loop(0, 2 * n, table, 0)
    weight_hop(0, 1)
    gather_finish(first, 0)
    weight_hop(0, 2)
    weight_start(1)
    gather_start(dy_all, 1)
    turn_over(first, first_t)
    weight_hop(0, 3)
    weight_start(2)
    weight_start(3)

    def turn(value, at):
        return value * cosine[at] + pltpu.roll(value, head // 2, 1) * sine[at]

    def turn_back(grad, at):
        return grad * cosine[at] - pltpu.roll(grad, head // 2, 1) * sine[at]

    def project(i, carry):
        at = rows(i, 2 * block)
        result = dot(first[at], w_qkv[...])
        raw[at] = result[:, :qw + kw]
        low_values = result[:, qw + kw:].astype(bf16)
        values[at] = low_values
        values_t[:, at] = low_values.T
        for h in range(group + 1):
            part = result[:, h * head:(h + 1) * head]
            inv = lax.rsqrt(jnp.mean(part * part, -1, keepdims=True) + epsilon)
            gain = qg_ref[...] if h < group else kg_ref[...]
            turned = turn(part * inv * gain, at)
            if h < group:
                queries[at, h * head:(h + 1) * head] = (turned * (scale * log2e)).astype(bf16)
            else:
                low_keys = turned.astype(bf16)
                keys[at] = low_keys
                keys_t[:, at] = low_keys.T
        return carry

    lax.fori_loop(0, n // 4, project, 0)
    weight_hop(1, 1)
    lax.fori_loop(n // 4, n // 2, project, 0)
    weight_hop(1, 2)
    gather_finish(dy_all, 1)

    def stack(ref, at):
        return jnp.concatenate([ref[at, h * head:(h + 1) * head] for h in range(group)], 0)

    def attend(place, h):
        at = rows(place, 2 * block)
        columns = slice(h * head, (h + 1) * head)
        tokens = slice(2 * h * block, 2 * (h + 1) * block)
        scores = dot_nt(keys[...], queries[at, columns])
        weight = jnp.concatenate(
            [jnp.exp2(jnp.where(
                positions[...] <= pos_row[:, rows(2 * place + k, block)].astype(f32),
                scores[:, k * block:(k + 1) * block], masked_score)) for k in range(2)], 1)
        inv = 1.0 / jnp.sum(weight, 0, keepdims=True)
        low_weight = weight.astype(bf16)
        probs[place, :, tokens] = low_weight
        sums[place, :, tokens] = inv
        result = dot(values_t[...], low_weight) * inv
        mixed_t[place, :, tokens] = result
        low_result = result.astype(bf16)
        mixed_low_t[columns, at] = low_result
        mixed_low[at, columns] = low_result.T

    def output_ready():
        weight_hop(1, 3)
        weight_start(4)
        weight_start(5)
        hand_arrive(1)
        drain(in_plane)

    def hop_third(t, d):
        weight_hop(2 + 2 * t, d)
        weight_hop(3 + 2 * t, d)

    sum_start(
        0, mixed_low, lambda left: dot(left, w_out[...]),
        [lambda place, h=h: attend(place, h) for h in range(group)], output_ready,
        (lambda: hop_third(0, 1), lambda: hop_third(0, 2), lambda: hop_third(1, 1)))
    weight_start(6)
    weight_start(7)
    mid = x_ref[...].astype(f32) + sum_finish(0)
    middle[...] = mid
    mid_scale = lax.rsqrt(jnp.mean(mid * mid, -1, keepdims=True) + epsilon)
    second[rows(c, block)] = (mid * mid_scale * fg_ref[...]).astype(bf16)
    gather_start(second, 2)
    hop_third(1, 2)
    turn_over(dy_all, dy_t)
    hop_third(0, 3)

    def feed(t, at):
        units, pair = slice(t * pw, (t + 1) * pw), 2 * pw * t
        both = dot(second[at], w_gu[:, pair:pair + 2 * pw])
        back = dot_nt(dy_all[at], w_down[units])
        gate, up = both[:, :pw], both[:, pw:]
        sig = 0.5 + 0.5 * jnp.tanh(0.5 * gate)
        silu = gate * sig
        hidden[at, units] = (silu * up).astype(bf16)
        d_gu[at, pair:pair + pw] = (back * up * sig * (1.0 + gate * (1.0 - sig))).astype(bf16)
        d_gu[at, pair + pw:pair + 2 * pw] = (back * silu).astype(bf16)

    def feed_arriving(slot, carry):
        gather_step(second, 2, slot)
        at = rows(chip(slot), 2 * block)
        feed(0, at)
        second_t[:, at] = second[at].T
        pl.when(slot == 1)(lambda: hop_third(2, 1))
        pl.when(slot == 3)(lambda: hop_third(2, 2))
        return carry

    def third_grad(t):
        weight_grad(t, [
            (second_t, lambda: d_gu[:, 2 * pw * t:2 * pw * (t + 1)]),
            (dy_t, lambda: hidden[:, t * pw:(t + 1) * pw]),
        ])

    def feed_third(t):
        def body(i, carry):
            feed(t, rows(i, 4 * block))
            return carry

        lax.fori_loop(0, n // 4, body, 0)

    lax.fori_loop(0, n // 2, feed_arriving, 0)
    gather_sent(second, 2)
    hop_third(1, 3)
    third_grad(0)
    feed_third(1)
    hop_third(2, 3)
    sum_start(
        1, d_gu, lambda left: dot_nt(left, w_gu[...]),
        [lambda place: feed(thirds - 1, rows(place, 2 * block))])
    third_grad(1)
    third_grad(2)
    d_second = sum_finish(1)

    def norm_back(value, gain, grad):
        inv = lax.rsqrt(jnp.mean(value * value, -1, keepdims=True) + epsilon)
        weighted = grad * gain
        inner = jnp.mean(weighted * value, -1, keepdims=True)
        result = inv * weighted - value * (inv * inv * inv * inner)
        return result, jnp.sum(grad * value * inv, 0, keepdims=True)

    gain_own[...] = jnp.zeros_like(gain_own)
    part, gain_own[1:2, :] = norm_back(middle[...], fg_ref[...], d_second)
    d_mid = dy_ref[...].astype(f32) + part
    d_middle[...] = d_mid
    dmid[rows(c, block)] = d_mid.astype(bf16)
    before = list(in_plane)
    in_plane.clear()
    gather_start(dmid, 3)
    drain(before)
    sum_start(2, hidden, lambda left: dot(left, w_down[...]))
    grad_near(0)

    dk_acc[...] = jnp.zeros_like(dk_acc)
    dv_acc[...] = jnp.zeros_like(dv_acc)

    def output_grad():
        def body(i, carry):
            grad = dot(mixed_low_t[...], dmid[:, rows(i, 2 * block)]).astype(bf16).T
            for k in range(2):
                for t in range(planes):
                    start = k * block + t * per
                    stage_out[t, 2 * i + k] = grad[start:start + per]
            return carry

        lax.fori_loop(0, n // 2, body, 0)
        grad_send(3)

    def attend_back(slot, q_sum):
        gather_step(dmid, 3, slot)
        place = chip(slot)
        at = rows(place, 2 * block)
        d_mix = dot_nt(w_out[...], dmid[at])
        pl.when(slot == 3)(output_grad)
        d_mix_t = jnp.concatenate([d_mix[h * head:(h + 1) * head] for h in range(group)], 1)
        d_mix_t = (d_mix_t.astype(bf16).astype(f32) * sums[place]).astype(bf16)
        delta = jnp.sum(d_mix_t.astype(f32) * mixed_t[place], 0, keepdims=True)
        weight = probs[place]
        d_prob = dot(values[...], d_mix_t)
        d_score = (weight.astype(f32) * (d_prob - delta)).astype(bf16)
        d_query = dot(keys_t[...], d_score) * scale
        for h in range(group):
            grad = turn_back(d_query[:, 2 * h * block:2 * (h + 1) * block].T, at)
            part, gain_part = norm_back(raw[at, h * head:(h + 1) * head], qg_ref[...], grad)
            d_qkv[at, h * head:(h + 1) * head] = part.astype(bf16)
            q_sum = q_sum + gain_part
        pl.when(slot == 2)(lambda: grad_near(1))
        dv_acc[...] += dot(weight, d_mix_t.T)
        dk_acc[...] += dot(d_score, stack(queries, at))
        return q_sum

    zero = jnp.zeros((1, head), f32)
    gain_own[2:3, 0:head] = lax.fori_loop(0, n // 2, attend_back, zero)
    gather_sent(dmid, 3)
    weight_grad(4, [(first_t, lambda: d_qkv[:, :qw])])
    grad_far(0)

    def project_back(i, k_sum):
        at = rows(i, 2 * block)
        grad = turn_back(dk_acc[at] * (1.0 / log2e), at)
        part, gain_part = norm_back(raw[at, qw:qw + kw], kg_ref[...], grad)
        d_qkv[at, qw:qw + kw] = part.astype(bf16)
        d_qkv[at, qw + kw:] = dv_acc[at].astype(bf16)
        return k_sum + gain_part

    gain_own[3:4, 0:head] = lax.fori_loop(0, n // 2, project_back, zero)

    weight_grad(5, [(first_t, lambda: d_qkv[:, qw:])])
    grad_far(1)
    grad_near(2)
    own_sum(0)
    drain(in_plane)
    sum_start(3, d_qkv, lambda left: dot_nt(left, w_qkv[...]))
    grad_far(2)
    grad_near(3)
    own_sum(1)
    hand_out(0)
    grad_far(3)
    grad_near(4)
    out_ref[...] = (middle[...] + sum_finish(2)).astype(bf16)
    grad_far(4)
    grad_near_far(5)
    own_sum(2)
    grad_near_inner(5)
    grad_far(5)
    x_part, gain_own[0:1, :] = norm_back(x_ref[...].astype(f32), ag_ref[...], sum_finish(3))
    dx_ref[...] = d_middle[...] + x_part

    def gain_plane_copy(j):
        return remote(gain_own, gain_plane.at[c], gp_send.at[j], gp_recv.at[j], partner(j), z)

    def gain_copy(d):
        return remote(gain_all.at[z], gain_all.at[z], gz_send.at[d], gz_recv.at[d], c, lax.rem(z + d, planes))

    for j in range(1, n):
        launch(in_plane, lambda j=j: gain_plane_copy(j))
    gain_plane[c] = gain_own[...]
    own_sum(3)
    hand_out(1)
    for j in range(1, n):
        gain_plane_copy(j).wait_recv()
    total = gain_plane[0]
    for i in range(1, n):
        total = total + gain_plane[i]
    gain_all[z] = total
    for d in range(1, planes):
        launch(along, lambda d=d: gain_copy(d))
    own_sum(4)
    for d in range(1, planes):
        origin = gain_all.at[lax.rem(z + planes - d, planes)]
        remote(origin, origin, gz_send.at[d], gz_recv.at[d], c, z).wait_recv()
    total = gain_all[0]
    for i in range(1, planes):
        total = total + gain_all[i]
    gains_ref[...] = total

    hand_receive(0)
    own_sum(5)
    hand_out(2)
    drain(weight_sends)
    drain(along)
    hand_receive(1)
    hand_receive(2)
    drain(in_plane)


def finish_kernel(
    n, head, out_in, dx_in, gains_in, got_ab, got_co, got_qkv,
    out_ref, dx_ref, ag_ref, q_ref, k_ref, v_ref, qg_ref, kg_ref, o_ref, fg_ref, g_ref, u_ref, d_ref,
):
    out_ref[...] = out_in[...]
    dx_ref[...] = dx_in[...]
    ag_ref[...] = gains_in[0:1, :]
    fg_ref[...] = gains_in[1:2, :]
    qg_ref[...] = gains_in[2:3, 0:head]
    kg_ref[...] = gains_in[3:4, 0:head]
    qw, kw = q_ref.shape[1] // n, k_ref.shape[1] // n
    fw = g_ref.shape[1] // n
    pw = fw // 3
    thirds = ((got_ab, 0), (got_ab, fw), (got_co, 0))
    for i in range(n):
        q_ref[:, i * qw:(i + 1) * qw] = got_qkv[i, :, 0:qw].astype(f32)
        k_ref[:, i * kw:(i + 1) * kw] = got_qkv[i, :, qw:qw + kw].astype(f32)
        v_ref[:, i * kw:(i + 1) * kw] = got_qkv[i, :, qw + kw:].astype(f32)
        o_ref[:, i * qw:(i + 1) * qw] = got_co[i, :, fw:].astype(f32)
        for t, (got, start) in enumerate(thirds):
            plane, unit = hidden_block(i, t)
            at = plane * (g_ref.shape[1] // 4) + unit * pw
            g_ref[:, at:at + pw] = got[i, :, start:start + pw].astype(f32)
            u_ref[:, at:at + pw] = got[i, :, start + pw:start + 2 * pw].astype(f32)
            d_ref[:, at:at + pw] = got[i, :, start + 2 * pw:start + 3 * pw].astype(f32)


def plane_device(
    layer_input,
    token_positions,
    attention_gain,
    query_weight,
    key_matrix,
    value_matrix,
    query_gain,
    key_norm_gain,
    output_weight,
    feedforward_gain,
    gate_weight,
    up_weight,
    down_weight,
    out_cotangent,
):
    n = lax.axis_size("ctx")
    planes = lax.axis_size("fsdp")
    block, width = layer_input.shape[1:]
    length = token_positions.shape[1]
    head = query_gain.shape[0]
    qw = query_weight.shape[1] // n
    kw = key_matrix.shape[1] // n
    fw = gate_weight.shape[1] // n
    group = qw // head
    per = block // planes
    half = head // 2
    inverse = np.power(rope_base, -np.arange(half) * 2.0 / head).astype(np.float32)
    inverse = np.concatenate([inverse, inverse])[None]
    steps = np.arange(block // 2)[:, None] * inverse.astype(np.float64)
    step_cos, step_sin = (jnp.asarray(f(steps).astype(np.float32)) for f in (np.cos, np.sin))
    inverse = jnp.asarray(inverse)
    vmem = pl.BlockSpec(memory_space=pltpu.VMEM)
    hbm = pl.BlockSpec(memory_space=pl.ANY)
    dma = pltpu.SemaphoreType.DMA
    sizes = (fw, fw, fw, qw, qw, 2 * kw)
    low = lambda *shape: pltpu.VMEM(shape, bf16)
    wide = lambda *shape: pltpu.VMEM(shape, f32)
    scratch = [
        low(width, qw + 2 * kw), low(width, 2 * fw), low(qw, width), low(fw, width),
        low(planes * (output_weight.shape[0] // n), width),
        low(length, width), low(length, width), low(length, width),
        low(width, length), low(width, length), low(width, length),
        wide(length, head), wide(length, head), wide(length, head),
        wide(length, qw + kw), low(length, qw), low(length, kw), low(length, kw),
        low(kw, length), low(kw, length), low(n // 2, length, 2 * group * block), wide(n // 2, 1, 2 * group * block),
        wide(n // 2, head, 2 * group * block), low(length, qw), low(qw, length),
        low(length, fw), low(length, 2 * fw), low(length, qw + 2 * kw),
        wide(length, kw), wide(length, kw),
    ]
    scratch += [low(planes, n, per, size) for size in sizes]
    scratch += [low(planes + 1, n, per, size) for size in sizes]
    scratch += [low(n, per, sizes[m] + sizes[m + 1]) for m in (0, 2, 4)]
    scratch += [low(2, 4, block, width)] * 2 + [low(2, 3, block, width)] * 2 + [wide(2, block, width)]
    scratch += [
        wide(block, width), wide(block, width), wide(8, width), wide(n, 8, width), wide(planes, 8, width),
        dma((13,)), dma((8, 6)), dma((8, planes)), dma((1, 7)), dma((1, 4)),
        dma((4, n)), dma((4, n)), dma((4, 4)), dma((4, 4)), dma((4, 4)), dma((4, 4)),
        dma((6, planes)), dma((6, planes + 1)), dma((3, n)), dma((3, n)), dma((n,)), dma((n,)),
        dma((planes,)), dma((planes,)),
    ]
    shapes = [
        jax.ShapeDtypeStruct((block, width), bf16),
        jax.ShapeDtypeStruct((block, width), f32),
        jax.ShapeDtypeStruct((8, width), f32),
    ] + [jax.ShapeDtypeStruct((n, per, sizes[m] + sizes[m + 1]), bf16) for m in (0, 2, 4)]
    results = pl.pallas_call(
        functools.partial(layer_kernel, n, planes, block, head, group, fw),
        out_shape=shapes,
        in_specs=[vmem] * 10 + [hbm] * 7,
        out_specs=[vmem] * len(shapes),
        scratch_shapes=scratch,
        compiler_params=pltpu.CompilerParams(
            collective_id=0, has_side_effects=True, vmem_limit_bytes=60 * 1024 * 1024),
    )(
        layer_input[0], out_cotangent[0], token_positions, inverse, step_cos, step_sin,
        attention_gain[None], feedforward_gain[None], query_gain[None], key_norm_gain[None],
        query_weight, key_matrix, value_matrix, output_weight, gate_weight, up_weight, down_weight,
    )
    plain = lambda rows, columns, kind=f32: jax.ShapeDtypeStruct((rows, columns), kind)
    finals = [
        plain(block, width, bf16), plain(block, width), plain(1, width),
        plain(per, n * qw), plain(per, n * kw), plain(per, n * kw), plain(1, head), plain(1, head),
        plain(per, n * qw), plain(1, width), plain(per, n * fw), plain(per, n * fw), plain(per, n * fw),
    ]
    done = pl.pallas_call(
        functools.partial(finish_kernel, n, head),
        out_shape=finals,
        in_specs=[vmem] * len(shapes),
        out_specs=[vmem] * len(finals),
    )(*results)
    out, dx, ag, q, k, v, qg, kg, o, fg, g, u, d = done
    return out[None], dx[None], ag[0], q, k, v, qg[0], kg[0], o.T, fg[0], g, u, d.T


def solution(mesh):
    in_specs = (
        P("fsdp", "ctx", None),
        P("fsdp", None),
        P(),
        P("fsdp", None),
        P("fsdp", None),
        P("fsdp", None),
        P(),
        P(),
        P("fsdp", None),
        P(),
        P("fsdp", None),
        P("fsdp", None),
        P("fsdp", None),
        P("fsdp", "ctx", None),
    )
    out_specs = (
        P("fsdp", "ctx", None),
        P("fsdp", "ctx", None),
        P(),
        P(("ctx", "fsdp"), None),
        P(("ctx", "fsdp"), None),
        P(("ctx", "fsdp"), None),
        P(),
        P(),
        P(None, ("ctx", "fsdp")),
        P(),
        P(("ctx", "fsdp"), None),
        P(("ctx", "fsdp"), None),
        P(None, ("ctx", "fsdp")),
    )

    def run(*arguments):
        n, planes = mesh.shape["ctx"], mesh.shape["fsdp"]
        key_heads = arguments[4].shape[1] // arguments[6].shape[0]
        whole_heads = n == 8 and planes == 4 and key_heads == n
        return jax.shard_map(
            plane_device if whole_heads else on_device,
            mesh=mesh, in_specs=in_specs, out_specs=out_specs, check_vma=False,
        )(*arguments)

    return run
```

```python
import functools

import jax
import jax.numpy as jnp
import numpy as np
from jax import lax
from jax.experimental import pallas as pl
from jax.experimental.pallas import tpu as pltpu
from jax.sharding import PartitionSpec as P

epsilon = 1e-06
rope_base = 1000000.0
masked_score = -1e30


def from_behind(block, axis, distance):
    devices = range(lax.axis_size(axis))
    route = [((i - distance) % len(devices), i) for i in devices]
    return lax.ppermute(block, axis, route)


def rotate(value_rows):
    half = value_rows.shape[-1] // 2
    return jnp.concatenate([-value_rows[..., half:], value_rows[..., :half]], -1)


def rotate_back(value_rows):
    half = value_rows.shape[-1] // 2
    return jnp.concatenate([value_rows[..., half:], -value_rows[..., :half]], -1)


def rope_tables(token_offsets, head_size):
    half = head_size // 2
    inverse = rope_base ** (-(jnp.arange(half).astype(jnp.float32) * 2.0) / head_size)
    angles = token_offsets.astype(jnp.float32)[:, None] * inverse[None, :]
    cosine = jnp.cos(angles)
    sine = jnp.sin(angles)
    return (jnp.concatenate([cosine, cosine], -1), jnp.concatenate([sine, sine], -1))


def norm_scale(value_rows):
    return lax.rsqrt(jnp.mean(value_rows * value_rows, -1, keepdims=True) + epsilon)


def norm_back(value_rows, scale, gain, grad):
    weighted = grad * gain
    inner = jnp.mean(weighted * value_rows, -1, keepdims=True)
    result = scale * weighted - value_rows * scale * scale * scale * inner
    gain_part = jnp.sum((grad * value_rows * scale).reshape(-1, gain.shape[0]), 0)
    return (result, gain_part)


def row_products(left, pieces):
    return tuple((jnp.dot(left, piece, preferred_element_type=jnp.float32) for piece in pieces))


def column_products(rights, pieces):
    total = jnp.einsum("tc,rc->tr", rights[0], pieces[0], preferred_element_type=jnp.float32)
    for right, piece in zip(rights[1:], pieces[1:]):
        total = total + jnp.einsum("tc,rc->tr", right, piece, preferred_element_type=jnp.float32)
    return total


def on_device(
    layer_input,
    token_positions,
    attention_gain,
    query_weight,
    key_matrix,
    value_matrix,
    query_gain,
    key_norm_gain,
    output_weight,
    feedforward_gain,
    gate_weight,
    up_weight,
    down_weight,
    out_cotangent,
):
    hidden_in = layer_input[0].astype(jnp.float32)
    count = hidden_in.shape[0]
    head_size = query_gain.shape[0]
    query_width = query_weight.shape[1]
    key_width = key_matrix.shape[1]
    inner_width = gate_weight.shape[1]
    heads = query_width // head_size
    key_heads = key_width // head_size
    group = heads // key_heads
    scale = head_size ** (-0.5)
    cycles = lax.axis_size("ctx")
    own_index = lax.axis_index("ctx")
    sequence_pos = token_positions[0]
    token_offsets = lax.dynamic_slice_in_dim(sequence_pos, own_index * count, count)
    cosine, sine = rope_tables(token_offsets, head_size)
    cosine = cosine[:, None, :]
    sine = sine[:, None, :]
    first_scale = norm_scale(hidden_in)
    first = (hidden_in * first_scale * attention_gain).astype(jnp.bfloat16)
    query_raw, key_unnormed, value_unnormed = row_products(
        first,
        (
            lax.all_gather(query_weight, "fsdp", axis=0, tiled=True),
            lax.all_gather(key_matrix, "fsdp", axis=0, tiled=True),
            lax.all_gather(value_matrix, "fsdp", axis=0, tiled=True),
        ),
    )
    query_heads = query_raw.reshape(count, heads, head_size)
    query_scale = norm_scale(query_heads)
    query_normed = query_heads * query_scale * query_gain
    query_rot = query_normed * cosine + rotate(query_normed) * sine
    query_grouped = (
        query_rot.reshape(count, key_heads, group, head_size)
        .transpose(1, 2, 0, 3)
        .astype(jnp.bfloat16)
    )
    key_heads_raw = key_unnormed.reshape(count, key_heads, head_size)
    key_scale = norm_scale(key_heads_raw)
    key_normed = key_heads_raw * key_scale * key_norm_gain
    key_low = (
        (key_normed * cosine + rotate(key_normed) * sine)
        .reshape(count, key_width)
        .astype(jnp.bfloat16)
    )
    value_low = value_unnormed.astype(jnp.bfloat16)
    rowmax = jnp.full((key_heads, group, count), masked_score, jnp.float32)
    keys_piece = lax.all_gather(key_low, "ctx", axis=0, tiled=True).reshape(
        -1, key_heads, head_size
    )
    values_piece = lax.all_gather(value_low, "ctx", axis=0, tiled=True).reshape(
        -1, key_heads, head_size
    )
    key_pos = sequence_pos
    allowed = token_offsets[:, None] >= key_pos[None, :]
    scores = (
        jnp.einsum("kgtd,skd->kgts", query_grouped, keys_piece, preferred_element_type=jnp.float32)
        * scale
    )
    scores = jnp.where(allowed, scores, masked_score)
    newmax = jnp.maximum(rowmax, jnp.max(scores, -1))
    weights = jnp.where(allowed, jnp.exp(scores - newmax[..., None]), 0.0)
    accum = jnp.einsum(
        "kgts,skd->kgtd",
        weights.astype(jnp.bfloat16),
        values_piece,
        preferred_element_type=jnp.float32,
    )
    rowsum = jnp.sum(weights, -1)
    accum, rowmax, rowsum = (accum, newmax, rowsum)
    normalized = accum / rowsum[..., None]
    logsum = rowmax + jnp.log(rowsum)
    attention_low = (
        normalized.transpose(2, 0, 1, 3).reshape(count, query_width).astype(jnp.bfloat16)
    )
    output_whole = lax.all_gather(output_weight, "fsdp", axis=0, tiled=True)
    branch_out = jnp.dot(attention_low, output_whole, preferred_element_type=jnp.float32)
    middle = hidden_in + branch_out
    second_scale = norm_scale(middle)
    second = (middle * second_scale * feedforward_gain).astype(jnp.bfloat16)
    gate, up = row_products(
        second,
        (
            lax.all_gather(gate_weight, "fsdp", axis=0, tiled=True),
            lax.all_gather(up_weight, "fsdp", axis=0, tiled=True),
        ),
    )
    sigmoid_gate = jax.nn.sigmoid(gate)
    silu_gate = gate * sigmoid_gate
    hidden_low = (silu_gate * up).astype(jnp.bfloat16)
    (down_out,) = row_products(
        hidden_low, (lax.all_gather(down_weight, "fsdp", axis=0, tiled=True),)
    )
    layer_output = (middle + down_out).astype(jnp.bfloat16)[None]
    cotangent = out_cotangent[0]
    hidden_grad = column_products(
        (cotangent,), lax.all_gather((down_weight,), "fsdp", axis=0, tiled=True)
    )
    up_low = (hidden_grad * silu_gate).astype(jnp.bfloat16)
    gate_low = (hidden_grad * up * sigmoid_gate * (1.0 + gate * (1.0 - sigmoid_gate))).astype(
        jnp.bfloat16
    )
    second_grad = column_products(
        (gate_low, up_low), lax.all_gather((gate_weight, up_weight), "fsdp", axis=0, tiled=True)
    )
    middle_part, feedforward_part = norm_back(middle, second_scale, feedforward_gain, second_grad)
    middle_grad = cotangent.astype(jnp.float32) + middle_part
    middle_low = middle_grad.astype(jnp.bfloat16)
    attention_grad = jnp.einsum(
        "tc,rc->tr", middle_low, output_whole, preferred_element_type=jnp.float32
    )
    attention_grad_low = attention_grad.astype(jnp.bfloat16)
    mixed_grad = attention_grad_low.reshape(count, key_heads, group, head_size).transpose(
        1, 2, 0, 3
    )
    delta = jnp.sum(mixed_grad.astype(jnp.float32) * normalized, -1)

    def cycle_step(index, carry):
        keys_held, values_held, key_acc, value_acc, query_acc = carry
        anchor = (own_index - index) % cycles
        key_pos = lax.dynamic_slice_in_dim(sequence_pos, anchor * count, count)
        keys_piece = keys_held.astype(jnp.bfloat16).reshape(count, key_heads, head_size)
        values_piece = values_held.astype(jnp.bfloat16).reshape(count, key_heads, head_size)
        allowed = token_offsets[:, None] >= key_pos[None, :]
        scores = (
            jnp.einsum(
                "kgtd,skd->kgts", query_grouped, keys_piece, preferred_element_type=jnp.float32
            )
            * scale
        )
        probs = jnp.where(allowed, jnp.exp(scores - logsum[..., None]), 0.0)
        value_acc = value_acc + jnp.einsum(
            "kgts,kgtd->skd",
            probs.astype(jnp.bfloat16),
            mixed_grad,
            preferred_element_type=jnp.float32,
        ).reshape(count, key_width)
        prob_grad = jnp.einsum(
            "kgtd,skd->kgts", mixed_grad, values_piece, preferred_element_type=jnp.float32
        )
        score_grad = (probs * (prob_grad - delta[..., None])).astype(jnp.bfloat16)
        query_acc = (
            query_acc
            + jnp.einsum(
                "kgts,skd->kgtd", score_grad, keys_piece, preferred_element_type=jnp.float32
            )
            * scale
        )
        key_acc = (
            key_acc
            + jnp.einsum(
                "kgts,kgtd->skd", score_grad, query_grouped, preferred_element_type=jnp.float32
            ).reshape(count, key_width)
            * scale
        )
        moved = (
            from_behind(keys_held.astype(jnp.bfloat16), "ctx", 1).astype(keys_held.dtype),
            from_behind(values_held.astype(jnp.bfloat16), "ctx", 1).astype(values_held.dtype),
            from_behind(key_acc.astype(jnp.bfloat16), "ctx", 1).astype(key_acc.dtype),
            from_behind(value_acc.astype(jnp.bfloat16), "ctx", 1).astype(value_acc.dtype),
        )
        return (moved[0], moved[1], moved[2], moved[3], query_acc)

    start_cycle = (
        key_low.astype(jnp.float32),
        value_low.astype(jnp.float32),
        jnp.zeros((count, key_width), jnp.float32),
        jnp.zeros((count, key_width), jnp.float32),
        jnp.zeros((key_heads, group, count, head_size), jnp.float32),
    )
    cycle_done = lax.fori_loop(0, cycles, cycle_step, start_cycle)
    key_acc = cycle_done[2]
    value_acc = cycle_done[3]
    query_acc = cycle_done[4]
    query_rot_grad = query_acc.transpose(2, 0, 1, 3).reshape(count, heads, head_size)
    query_normed_grad = query_rot_grad * cosine + rotate_back(query_rot_grad * sine)
    query_heads_grad, query_part = norm_back(
        query_heads, query_scale, query_gain, query_normed_grad
    )
    query_low_grad = query_heads_grad.reshape(count, query_width).astype(jnp.bfloat16)
    key_rot_grad = key_acc.reshape(count, key_heads, head_size)
    key_normed_grad = key_rot_grad * cosine + rotate_back(key_rot_grad * sine)
    key_heads_grad, key_part = norm_back(key_heads_raw, key_scale, key_norm_gain, key_normed_grad)
    key_low_grad = key_heads_grad.reshape(count, key_width).astype(jnp.bfloat16)
    value_low_grad = value_acc.astype(jnp.bfloat16)
    first_grad = column_products(
        (query_low_grad, key_low_grad, value_low_grad),
        lax.all_gather((query_weight, key_matrix, value_matrix), "fsdp", axis=0, tiled=True),
    )
    input_part, attention_part = norm_back(hidden_in, first_scale, attention_gain, first_grad)
    input_gradient = (middle_grad + input_part)[None]
    rights_first = jnp.concatenate([query_low_grad, key_low_grad, value_low_grad], 1)
    rights_second = jnp.concatenate([gate_low, up_low], 1)
    pairs = (
        (first, rights_first),
        (second, rights_second),
        (middle_low, attention_low),
        (cotangent, hidden_low),
    )
    parts = []
    for left, right in pairs:
        parts.append(jnp.einsum("tr,tc->rc", left, right, preferred_element_type=jnp.float32))
    sums = lax.psum_scatter(
        jnp.concatenate(parts, 1), ("ctx", "fsdp"), scatter_dimension=0, tiled=True
    )
    edges = [0, query_width, query_width + key_width, query_width + 2 * key_width]
    edges = edges + [edges[3] + inner_width, edges[3] + 2 * inner_width]
    edges = edges + [edges[5] + query_width, edges[5] + query_width + inner_width]
    query_gradient = sums[:, edges[0] : edges[1]]
    key_gradient = sums[:, edges[1] : edges[2]]
    value_gradient = sums[:, edges[2] : edges[3]]
    gate_gradient = sums[:, edges[3] : edges[4]]
    up_gradient = sums[:, edges[4] : edges[5]]
    output_gradient = sums[:, edges[5] : edges[6]].T
    down_gradient = sums[:, edges[6] : edges[7]].T
    attention_total, query_total, key_total, feedforward_total = lax.psum(
        (attention_part, query_part, key_part, feedforward_part), ("ctx", "fsdp")
    )
    return (
        layer_output,
        input_gradient,
        attention_total,
        query_gradient,
        key_gradient,
        value_gradient,
        query_total,
        key_total,
        output_gradient,
        feedforward_total,
        gate_gradient,
        up_gradient,
        down_gradient,
    )


MESH = pl.DeviceIdType.MESH
f32 = jnp.float32
bf16 = jnp.bfloat16


def dot(left, right):
    return jnp.dot(left, right, preferred_element_type=f32)


def dot_nt(left, right):
    return lax.dot_general(left, right, (((1,), (1,)), ((), ())), preferred_element_type=f32)


def dot_tn(left, right):
    return lax.dot_general(left, right, (((0,), (0,)), ((), ())), preferred_element_type=f32)


def hidden_block(device, third):
    def plane(i, t):
        return ((3, 1, 2), (0, 2, 1), (0, 3, 2), (3, 0, 1))[i // 4 * 2 + i % 2][t]

    own = plane(device, third)
    return own, sum(plane(i, t) == own for i in range(device) for t in range(3))


def layer_kernel(
    n, planes, block, head, group, fw,
    x_hbm, dy_hbm, pos_row, inverse_ref, step_cos, step_sin, ag_ref, fg_ref, qg_ref, kg_ref,
    wq, wk, wv, wo, wg, wu, wd,
    out_ref, dx_ref, gains_ref, got_ab, got_co, got_qkv,
    w_qkv, w_gu, w_out, w_down, t_out,
    first, dy_all, second, first_t, dy_t, second_t,
    positions, cosine, sine, x_ref,
    raw, queries, keys, values, keys_t, values_t, probs, sums, mixed_t, mixed_low, mixed_low_t,
    hidden, d_gu, d_qkv, dk_acc, dv_acc,
    stage_a, stage_b, stage_c, stage_out, stage_q, stage_kv,
    land_a, land_b, land_c, land_out, land_q, land_kv,
    own_ab, own_co, own_qkv,
    rs_sa, rs_ra, rs_sb, rs_rb, rs_acc,
    middle, d_middle, gain_own, gain_plane, gain_all,
    local_sem, wz_send, wz_recv, hand_send, hand_recv,
    ag_send, ag_recv, ra_send, ra_recv, rb_send, rb_recv,
    zr_send, zr_recv, aa_send, aa_recv, gp_send, gp_recv, gz_send, gz_recv,
):
    c = lax.axis_index("ctx")
    z = lax.axis_index("fsdp")
    dmid = first
    cy, cx, ck = lax.div(c, 4), lax.rem(lax.div(c, 2), 2), lax.rem(c, 2)
    ci = lax.rem(c, 4)
    sign = 1 - 2 * ck
    qw, kw = group * head, head
    pw = 128
    thirds = fw // pw
    width = x_ref.shape[1]
    scale = head ** (-0.5)
    log2e = 1.4426950408889634
    gots = (got_ab, got_co, got_qkv)
    owns = (own_ab, own_co, own_qkv)
    stages = (stage_a, stage_b, stage_c, stage_out, stage_q, stage_kv)
    lands = (land_a, land_b, land_c, land_out, land_q, land_kv)

    def partner(j):
        y = lax.rem(cy + lax.div(j, 4), 2)
        x = lax.rem(cx + lax.rem(lax.div(j, 2), 2), 2)
        k = lax.rem(ck + lax.rem(j, 2), 2)
        return y * 4 + x * 2 + k

    def chip(slot):
        return lax.rem(cy + lax.div(slot, 2), 2) * 2 + lax.rem(cx + lax.rem(slot, 2), 2)

    def rows(start, size):
        return pl.ds(pl.multiple_of(start * size, size), size)

    def remote(src, dst, send, recv, ctx, plane):
        return pltpu.make_async_remote_copy(
            src_ref=src, dst_ref=dst, send_sem=send, recv_sem=recv,
            device_id={"ctx": ctx, "fsdp": plane}, device_id_type=MESH,
        )

    in_plane, along, weight_sends = [], [], []

    def launch(started, copy, when=None):
        if when is None:
            copy().start()
        else:
            pl.when(when)(lambda: copy().start())
        started.append((copy, when))

    def drain(started):
        for copy, when in started:
            if when is None:
                copy().wait_send()
            else:
                pl.when(when)(lambda copy=copy: copy().wait_send())
        started.clear()

    def pick(values):
        return sum(jnp.where(c == i, value, 0) for i, value in enumerate(values))

    unit_plane = [pick([hidden_block(i, t)[0] for i in range(n)]) for t in range(thirds)]
    unit_block = [pick([hidden_block(i, t)[1] for i in range(n)]) for t in range(thirds)]
    plane_blocks = wd.shape[0] // pw

    own_rows = wq.shape[0]
    out_rows = wo.shape[0] // n

    def own_slices():
        mine = rows(z, own_rows)
        pairs = [
            (wq.at[:, rows(c, qw)], w_qkv.at[mine, 0:qw]),
            (wk.at[:, rows(c, kw)], w_qkv.at[mine, qw:qw + kw]),
            (wv.at[:, rows(c, kw)], w_qkv.at[mine, qw + kw:qw + 2 * kw]),
            (wo.at[rows(c, out_rows)], t_out.at[rows(z, out_rows)]),
        ]
        for t in range(thirds):
            at = 2 * pw * t
            unit = unit_plane[t] * plane_blocks + unit_block[t]
            pairs.append((wg.at[:, rows(unit, pw)], w_gu.at[mine, at:at + pw]))
            pairs.append((wu.at[:, rows(unit, pw)], w_gu.at[mine, at + pw:at + 2 * pw]))
        return pairs

    local = [pltpu.make_async_copy(src, dst, local_sem.at[i]) for i, (src, dst) in enumerate(own_slices())]
    x_in = pltpu.make_async_copy(x_hbm, x_ref, local_sem.at[13])
    dy_in = pltpu.make_async_copy(dy_hbm, dy_all.at[rows(c, block)], local_sem.at[14])
    for copy in [x_in, *local, dy_in]:
        copy.start()

    def own_down(t):
        return pltpu.make_async_copy(
            wd.at[rows(unit_block[t], pw)], w_down.at[t * pw:(t + 1) * pw], local_sem.at[4 + 2 * thirds + t])

    holds = [unit_plane[t] == z for t in range(thirds)]
    for t in range(thirds):
        pl.when(holds[t])(lambda t=t: own_down(t).start())

    for land in lands:
        @pl.when(z == 0)
        def _(land=land):
            land[0] = jnp.zeros(land.shape[1:], bf16)

        @pl.when(z == planes - 1)
        def _(land=land):
            land[planes] = jnp.zeros(land.shape[1:], bf16)

    barrier = pltpu.get_barrier_semaphore()
    for j in range(1, n):
        pl.semaphore_signal(barrier, inc=1, device_id={"ctx": partner(j), "fsdp": z}, device_id_type=MESH)
    for d in range(1, planes):
        pl.semaphore_signal(
            barrier, inc=1, device_id={"ctx": c, "fsdp": lax.rem(z + d, planes)}, device_id_type=MESH)
    x_in.wait()
    x = x_ref[...].astype(f32)
    x_scale = lax.rsqrt(jnp.mean(x * x, -1, keepdims=True) + epsilon)
    first[rows(c, block)] = (x * x_scale * ag_ref[...]).astype(bf16)
    for copy in local[:3]:
        copy.wait()
    pl.semaphore_wait(barrier, n + planes - 2)

    def inside(t):
        return jnp.logical_and(t >= 0, t < planes)

    weights = [
        (lambda o: w_qkv.at[rows(o, own_rows)], None),
        (lambda o: t_out.at[rows(o, out_rows)], 0),
    ]
    for t in range(thirds):
        weights.append((lambda o, t=t: w_gu.at[rows(o, own_rows), 2 * pw * t:2 * pw * (t + 1)], None))
        weights.append((lambda o, t=t: w_down.at[t * pw:(t + 1) * pw], None))

    def weight_copy(w, slot, origin, target):
        part = weights[w][0](origin)
        return remote(part, part, wz_send.at[w, slot], wz_recv.at[w, origin], c, target)

    def from_plane(w, origin):
        return origin == unit_plane[(w - 3) // 2] if w >= 3 and w % 2 else None

    def both(one, other):
        return one if other is None else jnp.logical_and(one, other)

    def hand_split(origin, valid):
        mine = 2 * origin + cy == c
        return jnp.logical_and(valid, jnp.logical_not(mine)), jnp.logical_and(valid, mine)

    def weight_start(w):
        for side in range(2):
            d = sign * (1 - 2 * side)
            launch(
                weight_sends, lambda side=side, d=d: weight_copy(w, side, z, z + d),
                both(inside(z + d), from_plane(w, z)))
        if weights[w][1] is not None:
            hand_over(w, z, 0, *hand_split(z, True))

    def hand_target(h):
        return lambda i: w_out.at[rows(i, out_rows)]

    def hand_copy(w, origin, slot):
        h = weights[w][1]
        return remote(
            weights[w][0](origin), hand_target(h)(ci), hand_send.at[h, slot], hand_recv.at[h, ci], 2 * origin + cy, z)

    def hand_over(w, origin, slot, away, here):
        launch(in_plane, lambda: hand_copy(w, origin, slot), away)

        @pl.when(here)
        def _():
            hand_target(weights[w][1])(ci)[...] = weights[w][0](origin)[...]

    def hand_arrive(w):
        h = weights[w][1]
        for i in range(4):
            @pl.when(4 * ck + i != c)
            def _(i=i):
                part = hand_target(h)(i)
                remote(part, part, hand_send.at[h, 0], hand_recv.at[h, i], c, z).wait_recv()

    hops = {}
    for w in range(len(weights)):
        for d in range(1, planes):
            for side, way in enumerate((1, -1)):
                origin = z - way * d
                valid = both(inside(origin), from_plane(w, origin))
                passed = jnp.logical_and(valid, inside(z + way))
                split = None if weights[w][1] is None else hand_split(origin, valid)
                hops[w, d, side] = origin, z + way, valid, passed, split

    def weight_hop(w, d):
        for side in range(2):
            origin, following, valid, passed, split = hops[w, d, side]
            pl.when(valid)(lambda: weight_copy(w, 0, origin, z).wait_recv())
            if d < planes - 1:
                launch(
                    weight_sends,
                    lambda side=side, origin=origin, following=following: weight_copy(
                        w, 2 * d + side, origin, following),
                    passed)
            if split is not None:
                hand_over(w, origin, 2 * d - 1 + side, *split)

    def gather_copy(buf, g, j, send, origin, target):
        part = buf.at[rows(origin, block)]
        return remote(part, part, ag_send.at[g, send], ag_recv.at[g, j], target, z)

    def gather_start(buf, g):
        for j in (1, 2 + 2 * ck, 4 - 2 * ck):
            launch(in_plane, lambda j=j: gather_copy(buf, g, j, j, c, partner(j)))

    def gather_half(buf, g, j):
        half = block // 2
        part = buf.at[pl.ds(pl.multiple_of(partner(j) * block + (half if j == 2 else 0), half), half)]
        at = 0 if j == 2 else 6
        return remote(part, part, ag_send.at[g, at], ag_recv.at[g, at], partner(6 - j), z)

    def gather_diagonal(buf, g):
        half = block // 2
        for at in (6, 0):
            part = buf.at[pl.ds(pl.multiple_of(partner(6) * block + (0 if at == 6 else half), half), half)]
            remote(part, part, ag_send.at[g, at], ag_recv.at[g, at], c, z).wait_recv()

    def gather_forward(buf, g, j):
        return gather_copy(buf, g, j + 1, j + 1, partner(j), partner(1))

    def gather_take(buf, g, j):
        if j == 6:
            gather_diagonal(buf, g)
        else:
            gather_copy(buf, g, j, j, partner(j), c).wait_recv()
            gather_half(buf, g, j).start()
        gather_forward(buf, g, j).start()

    def gather_sent(buf, g):
        for j in (2, 4, 6):
            in_plane.append((lambda j=j: gather_forward(buf, g, j), None))
            if j < 6:
                in_plane.append((lambda j=j: gather_half(buf, g, j), None))

    def gather_finish(buf, g):
        for j in (2, 4, 6):
            gather_take(buf, g, j)
        gather_sent(buf, g)
        for j in (1, 3, 5, 7):
            gather_copy(buf, g, j, j, partner(j), c).wait_recv()

    def gather_step(buf, g, slot):
        @pl.when(slot == 1)
        def _():
            gather_take(buf, g, 2)
            gather_take(buf, g, 4)

        pl.when(slot == 3)(lambda: gather_take(buf, g, 6))
        gather_copy(buf, g, 2 * slot + 1, 0, partner(2 * slot + 1), c).wait_recv()

    def sum_pair_copy(s, slot):
        return remote(rs_sa.at[s % 2, slot], rs_ra.at[s % 2, slot], ra_send.at[s, slot], ra_recv.at[s, slot], partner(1), z)

    def sum_chip_copy(s, slot):
        return remote(
            rs_sb.at[s % 2, slot - 1], rs_rb.at[s % 2, slot - 1], rb_send.at[s, slot], rb_recv.at[s, slot], partner(2 * slot), z)

    def sum_half_copy(s, slot):
        half = block // 2
        at = pl.ds(pl.multiple_of((slot - 1) * half, half), half)
        return remote(
            rs_sb.at[s % 2, 2, at], rs_rb.at[s % 2, 2, at], rb_send.at[s, 6 - 3 * slot], rb_recv.at[s, 6 - 3 * slot],
            partner(6 - 2 * slot), z)

    def sum_slot(p):
        return jnp.where(p == 0, 3, jnp.where(p == 1, 2 - ck, jnp.where(p == 2, 1 + ck, 0)))

    def sum_start(s, left, partial, prepare=None, ready=None, during=()):
        if prepare is not None:
            for step in prepare:
                step(chip(sum_slot(0)))
        if ready is not None:
            ready()

        def body(p, carry):
            slot = sum_slot(p)
            at = [rows(partner(2 * slot + 1), block), rows(partner(2 * slot), block)]
            both = partial(jnp.concatenate([left[i] for i in at], 0))
            rs_sa[s % 2, slot] = both[:block].astype(bf16)
            sum_pair_copy(s, slot).start()

            @pl.when(p < 3)
            def _():
                rs_sb[s % 2, slot - 1] = both[block:].astype(bf16)

            @pl.when(p == 3)
            def _():
                rs_acc[s % 2] = both[block:]


            def pair_sum(q):
                before = sum_slot(q)
                sum_pair_copy(s, before).wait_recv()
                rs_sb[s % 2, before - 1] = rs_sb[s % 2, before - 1] + rs_ra[s % 2, before]

            def chip_send(q):
                before = sum_slot(q)
                half = block // 2
                at = pl.ds(pl.multiple_of((before - 1) * half, half), half)
                sum_half_copy(s, before).wait_recv()
                rs_sb[s % 2, before - 1, at] = rs_sb[s % 2, before - 1, at] + rs_rb[s % 2, 2, at]
                sum_chip_copy(s, before).start()

            early = prepare is not None and len(prepare) > 1

            @pl.when(p == 1)
            def _():
                pair_sum(0)
                sum_half_copy(s, 1).start()
                sum_half_copy(s, 2).start()

            @pl.when(p == 2 if early else p > 1)
            def _():
                pair_sum(p - 1)
                chip_send(p - 1)

            if prepare is not None:
                @pl.when(p < 3)
                def _():
                    prepare[0](chip(sum_slot(p + 1)))

            if early:
                @pl.when(p == 2)
                def _():
                    pair_sum(2)
                    chip_send(2)

                @pl.when(p < 3)
                def _():
                    for step in prepare[1:]:
                        step(chip(sum_slot(p + 1)))

            for k, poll in enumerate(during):
                pl.when(p == k)(poll)
            return carry

        lax.fori_loop(0, 4, body, 0)
        for slot in range(4):
            in_plane.append((lambda slot=slot: sum_pair_copy(s, slot), None))
        for slot in (1, 2):
            in_plane.append((lambda slot=slot: sum_half_copy(s, slot), None))
            in_plane.append((lambda slot=slot: sum_chip_copy(s, slot), None))
        sum_pair_copy(s, 0).wait_recv()
        rs_acc[s % 2] = rs_acc[s % 2] + rs_ra[s % 2, 0].astype(f32)

    def sum_finish(s):
        total = rs_acc[s % 2]
        for slot in (1, 2):
            sum_chip_copy(s, slot).wait_recv()
            total = total + rs_rb[s % 2, slot - 1].astype(f32)
        return total

    per = block // planes

    at_edge = jnp.logical_or(z == 0, z == planes - 1)
    edge_targets = [jnp.where(z == 0, planes - 1 - k, k) for k in range(planes - 1)]

    def weight_grad(m, parts):
        def body(i, carry):
            at = 0
            for left, right in parts:
                value = right()
                grad = dot(left[rows(i, 4 * block)], value)
                for k in range(4):
                    for t in range(planes):
                        start = k * block + t * per
                        stages[m][t, 4 * i + k, :, at:at + value.shape[1]] = grad[start:start + per].astype(bf16)
                at += value.shape[1]
            return carry

        lax.fori_loop(0, n // 4, body, 0)
        grad_send(m)

    def grad_send(m):
        for t in edge_targets:
            launch(along, lambda t=t: grad_copy(m, t), at_edge)

    def grad_copy(m, t):
        way = jnp.where(z < t, 1, -1)
        last = z + way == t
        slot = jnp.where(jnp.logical_and(last, way < 0), planes, t)
        return remote(
            stages[m].at[t], lands[m].at[slot], zr_send.at[m, t], zr_recv.at[m, slot], c, z + way)

    def grad_arrive(m, slot):
        part = lands[m].at[slot]
        remote(part, part, zr_send.at[m, 0], zr_recv.at[m, slot], c, z).wait_recv()

    def grad_pass(m, t, valid):
        @pl.when(valid)
        def _():
            grad_arrive(m, t)
            stages[m][t] = stages[m][t] + lands[m][t]

        launch(along, lambda: grad_copy(m, t), valid)

    is_low, is_high = z == 1, z == planes - 2

    def grad_near_far(m):
        grad_pass(m, 3, is_low)
        grad_pass(m, 0, is_high)

    def grad_near_inner(m):
        grad_pass(m, 2, is_low)
        grad_pass(m, 1, is_high)

    def grad_near(m):
        grad_near_far(m)
        grad_near_inner(m)

    def grad_far(m):
        grad_pass(m, 3, is_high)
        grad_pass(m, 0, is_low)

    def owner_copy(g, j):
        return remote(owns[g].at[partner(j)], gots[g].at[c], aa_send.at[g, j], aa_recv.at[g, j], partner(j), z)

    def own_sum(m):
        pl.when(z > 0)(lambda: grad_arrive(m, z))
        pl.when(z < planes - 1)(lambda: grad_arrive(m, planes))
        total = stages[m][z].astype(f32) + lands[m][z].astype(f32) + lands[m][planes].astype(f32)
        first_size = stages[m // 2 * 2].shape[3]
        if m % 2:
            owns[m // 2][:, :, first_size:] = total.astype(bf16)
        else:
            owns[m // 2][:, :, :first_size] = total.astype(bf16)

    def hand_out(g):
        for j in (2 + 2 * ck, 3 + 2 * ck, 4 - 2 * ck, 5 - 2 * ck, 6, 7, 1):
            launch(in_plane, lambda j=j: owner_copy(g, j))
        gots[g][c] = owns[g][c]

    def hand_receive(g):
        for j in range(1, n):
            owner_copy(g, j).wait_recv()

    weight_start(0)
    gather_start(first, 0)
    for copy in local[3:]:
        copy.wait()
    for t in range(thirds):
        pl.when(holds[t])(lambda t=t: own_down(t).wait())

    spread = jnp.broadcast_to(pos_row[...].astype(f32), (head, pos_row.shape[1]))
    positions[...] = spread.T
    side = jnp.where(lax.broadcasted_iota(jnp.int32, (1, head), 1) < head // 2, -1.0, 1.0)

    def table(i, carry):
        run = step_cos.shape[0]
        at = rows(i, run)
        start = positions[pl.ds(pl.multiple_of(i * run, run), 1)] * inverse_ref[...]
        start_cos, start_sin = jnp.cos(start), jnp.sin(start)
        cosine[at] = start_cos * step_cos[...] - start_sin * step_sin[...]
        sine[at] = (start_sin * step_cos[...] + start_cos * step_sin[...]) * side
        return carry

    def turn_over(src, dst):
        def body(i, carry):
            at = rows(i, block)
            dst[:, at] = src[at].T
            return carry

        lax.fori_loop(0, n, body, 0)

    lax.fori_loop(0, 2 * n, table, 0)
    weight_hop(0, 1)
    gather_finish(first, 0)
    weight_hop(0, 2)
    weight_start(1)
    dy_in.wait()
    gather_start(dy_all, 1)
    turn_over(first, first_t)
    weight_hop(0, 3)
    weight_start(2)
    weight_start(3)

    def turn(value, at):
        return value * cosine[at] + pltpu.roll(value, head // 2, 1) * sine[at]

    def turn_back(grad, at):
        return grad * cosine[at] - pltpu.roll(grad, head // 2, 1) * sine[at]

    def project(i, carry):
        at = rows(i, 2 * block)
        result = dot(first[at], w_qkv[...])
        raw[at] = result[:, :qw + kw]
        low_values = result[:, qw + kw:].astype(bf16)
        values[at] = low_values
        values_t[:, at] = low_values.T
        for h in range(group + 1):
            part = result[:, h * head:(h + 1) * head]
            inv = lax.rsqrt(jnp.mean(part * part, -1, keepdims=True) + epsilon)
            gain = qg_ref[...] if h < group else kg_ref[...]
            turned = turn(part * inv * gain, at)
            if h < group:
                queries[at, h * head:(h + 1) * head] = (turned * (scale * log2e)).astype(bf16)
            else:
                low_keys = turned.astype(bf16)
                keys[at] = low_keys
                keys_t[:, at] = low_keys.T
        return carry

    lax.fori_loop(0, n // 4, project, 0)
    weight_hop(1, 1)
    lax.fori_loop(n // 4, n // 2, project, 0)
    weight_hop(1, 2)
    gather_finish(dy_all, 1)

    def stack(ref, at):
        return jnp.concatenate([ref[at, h * head:(h + 1) * head] for h in range(group)], 0)

    def attend(place, h):
        at = rows(place, 2 * block)
        columns = slice(h * head, (h + 1) * head)
        tokens = slice(2 * h * block, 2 * (h + 1) * block)
        scores = dot_nt(keys[...], queries[at, columns])
        weight = jnp.concatenate(
            [jnp.exp2(jnp.where(
                positions[...] <= pos_row[:, rows(2 * place + k, block)].astype(f32),
                scores[:, k * block:(k + 1) * block], masked_score)) for k in range(2)], 1)
        inv = 1.0 / jnp.sum(weight, 0, keepdims=True)
        low_weight = weight.astype(bf16)
        probs[place, :, tokens] = low_weight
        sums[place, :, tokens] = inv
        result = dot(values_t[...], low_weight) * inv
        mixed_t[place, :, tokens] = result
        low_result = result.astype(bf16)
        mixed_low_t[columns, at] = low_result
        mixed_low[at, columns] = low_result.T

    def output_ready():
        weight_hop(1, 3)
        weight_start(4)
        weight_start(5)
        hand_arrive(1)
        drain(in_plane)

    def hop_third(t, d):
        weight_hop(2 + 2 * t, d)
        weight_hop(3 + 2 * t, d)

    sum_start(
        0, mixed_low, lambda left: dot(left, w_out[...]),
        [lambda place, h=h: attend(place, h) for h in range(group)], output_ready,
        (lambda: hop_third(0, 1), lambda: hop_third(0, 2), lambda: hop_third(1, 1)))
    weight_start(6)
    weight_start(7)
    mid = x_ref[...].astype(f32) + sum_finish(0)
    middle[...] = mid
    mid_scale = lax.rsqrt(jnp.mean(mid * mid, -1, keepdims=True) + epsilon)
    second[rows(c, block)] = (mid * mid_scale * fg_ref[...]).astype(bf16)
    gather_start(second, 2)
    hop_third(1, 2)
    turn_over(dy_all, dy_t)
    hop_third(0, 3)

    def feed(t, at):
        units, pair = slice(t * pw, (t + 1) * pw), 2 * pw * t
        both = dot(second[at], w_gu[:, pair:pair + 2 * pw])
        back = dot_nt(dy_all[at], w_down[units])
        gate, up = both[:, :pw], both[:, pw:]
        sig = 0.5 + 0.5 * jnp.tanh(0.5 * gate)
        silu = gate * sig
        hidden[at, units] = (silu * up).astype(bf16)
        d_gu[at, pair:pair + pw] = (back * up * sig * (1.0 + gate * (1.0 - sig))).astype(bf16)
        d_gu[at, pair + pw:pair + 2 * pw] = (back * silu).astype(bf16)

    def feed_arriving(slot, carry):
        gather_step(second, 2, slot)
        at = rows(chip(slot), 2 * block)
        feed(0, at)
        second_t[:, at] = second[at].T
        pl.when(slot == 1)(lambda: hop_third(2, 1))
        pl.when(slot == 3)(lambda: hop_third(2, 2))
        return carry

    def third_grad(t):
        weight_grad(t, [
            (second_t, lambda: d_gu[:, 2 * pw * t:2 * pw * (t + 1)]),
            (dy_t, lambda: hidden[:, t * pw:(t + 1) * pw]),
        ])

    def feed_third(t):
        def body(i, carry):
            feed(t, rows(i, 4 * block))
            return carry

        lax.fori_loop(0, n // 4, body, 0)

    lax.fori_loop(0, n // 2, feed_arriving, 0)
    gather_sent(second, 2)
    hop_third(1, 3)
    third_grad(0)
    feed_third(1)
    hop_third(2, 3)
    sum_start(
        1, d_gu, lambda left: dot_nt(left, w_gu[...]),
        [lambda place: feed(thirds - 1, rows(place, 2 * block))])
    third_grad(1)
    third_grad(2)
    d_second = sum_finish(1)

    def norm_back(value, gain, grad):
        inv = lax.rsqrt(jnp.mean(value * value, -1, keepdims=True) + epsilon)
        weighted = grad * gain
        inner = jnp.mean(weighted * value, -1, keepdims=True)
        result = inv * weighted - value * (inv * inv * inv * inner)
        return result, jnp.sum(grad * value * inv, 0, keepdims=True)

    gain_own[...] = jnp.zeros_like(gain_own)
    part, gain_own[1:2, :] = norm_back(middle[...], fg_ref[...], d_second)
    d_mid = dy_all[rows(c, block)].astype(f32) + part
    d_middle[...] = d_mid
    dmid[rows(c, block)] = d_mid.astype(bf16)
    before = list(in_plane)
    in_plane.clear()
    gather_start(dmid, 3)
    drain(before)
    sum_start(2, hidden, lambda left: dot(left, w_down[...]))
    grad_near(0)

    dk_acc[...] = jnp.zeros_like(dk_acc)
    dv_acc[...] = jnp.zeros_like(dv_acc)

    def output_grad():
        def body(i, carry):
            grad = dot(mixed_low_t[...], dmid[:, rows(i, 2 * block)]).astype(bf16).T
            for k in range(2):
                for t in range(planes):
                    start = k * block + t * per
                    stage_out[t, 2 * i + k] = grad[start:start + per]
            return carry

        lax.fori_loop(0, n // 2, body, 0)
        grad_send(3)

    def attend_back(slot, q_sum):
        gather_step(dmid, 3, slot)
        place = chip(slot)
        at = rows(place, 2 * block)
        d_mix = dot_nt(w_out[...], dmid[at])
        pl.when(slot == 3)(output_grad)
        d_mix_t = jnp.concatenate([d_mix[h * head:(h + 1) * head] for h in range(group)], 1)
        d_mix_t = (d_mix_t.astype(bf16).astype(f32) * sums[place]).astype(bf16)
        delta = jnp.sum(d_mix_t.astype(f32) * mixed_t[place], 0, keepdims=True)
        weight = probs[place]
        d_prob = dot(values[...], d_mix_t)
        d_score = (weight.astype(f32) * (d_prob - delta)).astype(bf16)
        d_query = dot(keys_t[...], d_score) * scale
        for h in range(group):
            grad = turn_back(d_query[:, 2 * h * block:2 * (h + 1) * block].T, at)
            part, gain_part = norm_back(raw[at, h * head:(h + 1) * head], qg_ref[...], grad)
            d_qkv[at, h * head:(h + 1) * head] = part.astype(bf16)
            q_sum = q_sum + gain_part
        pl.when(slot == 2)(lambda: grad_near(1))
        dv_acc[...] += dot(weight, d_mix_t.T)
        dk_acc[...] += dot(d_score, stack(queries, at))
        return q_sum

    zero = jnp.zeros((1, head), f32)
    gain_own[2:3, 0:head] = lax.fori_loop(0, n // 2, attend_back, zero)
    gather_sent(dmid, 3)
    weight_grad(4, [(first_t, lambda: d_qkv[:, :qw])])
    grad_far(0)

    def project_back(i, k_sum):
        at = rows(i, 2 * block)
        grad = turn_back(dk_acc[at] * (1.0 / log2e), at)
        part, gain_part = norm_back(raw[at, qw:qw + kw], kg_ref[...], grad)
        d_qkv[at, qw:qw + kw] = part.astype(bf16)
        d_qkv[at, qw + kw:] = dv_acc[at].astype(bf16)
        return k_sum + gain_part

    gain_own[3:4, 0:head] = lax.fori_loop(0, n // 2, project_back, zero)

    weight_grad(5, [(first_t, lambda: d_qkv[:, qw:])])
    grad_far(1)
    grad_near(2)
    own_sum(0)
    drain(in_plane)
    sum_start(3, d_qkv, lambda left: dot_nt(left, w_qkv[...]))
    grad_far(2)
    grad_near(3)
    own_sum(1)
    hand_out(0)
    grad_far(3)
    grad_near(4)
    second[0:block] = (middle[...] + sum_finish(2)).astype(bf16)
    out_copy = pltpu.make_async_copy(second.at[0:block], out_ref, local_sem.at[15])
    out_copy.start()
    grad_far(4)
    grad_near_far(5)
    own_sum(2)
    grad_near_inner(5)
    grad_far(5)
    x_part, gain_own[0:1, :] = norm_back(x_ref[...].astype(f32), ag_ref[...], sum_finish(3))
    d_middle[...] += x_part
    dx_copy = pltpu.make_async_copy(d_middle, dx_ref, local_sem.at[16])
    dx_copy.start()

    def gain_plane_copy(j):
        return remote(gain_own, gain_plane.at[c], gp_send.at[j], gp_recv.at[j], partner(j), z)

    def gain_copy(d):
        return remote(gain_all.at[z], gain_all.at[z], gz_send.at[d], gz_recv.at[d], c, lax.rem(z + d, planes))

    for j in range(1, n):
        launch(in_plane, lambda j=j: gain_plane_copy(j))
    gain_plane[c] = gain_own[...]
    own_sum(3)
    hand_out(1)
    for j in range(1, n):
        gain_plane_copy(j).wait_recv()
    total = gain_plane[0]
    for i in range(1, n):
        total = total + gain_plane[i]
    gain_all[z] = total
    for d in range(1, planes):
        launch(along, lambda d=d: gain_copy(d))
    own_sum(4)
    for d in range(1, planes):
        origin = gain_all.at[lax.rem(z + planes - d, planes)]
        remote(origin, origin, gz_send.at[d], gz_recv.at[d], c, z).wait_recv()
    total = gain_all[0]
    for i in range(1, planes):
        total = total + gain_all[i]
    gains_ref[...] = total

    hand_receive(0)
    own_sum(5)
    hand_out(2)
    drain(weight_sends)
    drain(along)
    out_copy.wait()
    dx_copy.wait()
    hand_receive(1)
    hand_receive(2)
    drain(in_plane)


def finish_kernel(
    n, head, out_in, dx_in, gains_in, got_ab, got_co, got_qkv,
    out_ref, dx_ref, ag_ref, q_out, k_out, v_out, qg_ref, kg_ref, o_out, fg_ref, g_out, u_out, d_out,
    ab, co, qkv, q_ref, k_ref, v_ref, o_ref, g_ref, u_ref, d_ref, sem,
):
    loads = [pltpu.make_async_copy(src, dst, sem.at[i])
             for i, (src, dst) in enumerate(((got_qkv, qkv), (got_co, co), (got_ab, ab)))]
    stores = [pltpu.make_async_copy(src, dst, sem.at[3 + i])
              for i, (src, dst) in enumerate((
                  (dx_in, dx_ref), (out_in, out_ref), (q_ref, q_out), (k_ref, k_out), (v_ref, v_out),
                  (o_ref, o_out), (g_ref, g_out), (u_ref, u_out), (d_ref, d_out)))]
    for copy in loads + stores[:2]:
        copy.start()
    ag_ref[...] = gains_in[0:1, :]
    fg_ref[...] = gains_in[1:2, :]
    qg_ref[...] = gains_in[2:3, 0:head]
    kg_ref[...] = gains_in[3:4, 0:head]
    qw, kw = q_ref.shape[1] // n, k_ref.shape[1] // n
    fw = g_ref.shape[1] // n
    pw = fw // 3
    loads[0].wait()
    for i in range(n):
        q_ref[:, i * qw:(i + 1) * qw] = qkv[i, :, 0:qw].astype(f32)
        k_ref[:, i * kw:(i + 1) * kw] = qkv[i, :, qw:qw + kw].astype(f32)
        v_ref[:, i * kw:(i + 1) * kw] = qkv[i, :, qw + kw:].astype(f32)
    for copy in stores[2:5]:
        copy.start()
    loads[1].wait()
    for i in range(n):
        o_ref[:, i * qw:(i + 1) * qw] = co[i, :, fw:].astype(f32)
    stores[5].start()
    loads[2].wait()
    for part, (whole, store) in enumerate(zip((g_ref, u_ref, d_ref), stores[6:])):
        for i in range(n):
            for t, (got, start) in enumerate(((ab, 0), (ab, fw), (co, 0))):
                plane, unit = hidden_block(i, t)
                at = plane * (whole.shape[1] // 4) + unit * pw
                begin = start + part * pw
                whole[:, at:at + pw] = got[i, :, begin:begin + pw].astype(f32)
        store.start()
    for copy in stores:
        copy.wait()


def plane_device(
    layer_input,
    token_positions,
    attention_gain,
    query_weight,
    key_matrix,
    value_matrix,
    query_gain,
    key_norm_gain,
    output_weight,
    feedforward_gain,
    gate_weight,
    up_weight,
    down_weight,
    out_cotangent,
):
    n = lax.axis_size("ctx")
    planes = lax.axis_size("fsdp")
    block, width = layer_input.shape[1:]
    length = token_positions.shape[1]
    head = query_gain.shape[0]
    qw = query_weight.shape[1] // n
    kw = key_matrix.shape[1] // n
    fw = gate_weight.shape[1] // n
    group = qw // head
    per = block // planes
    half = head // 2
    inverse = np.power(rope_base, -np.arange(half) * 2.0 / head).astype(np.float32)
    inverse = np.concatenate([inverse, inverse])[None]
    steps = np.arange(block // 2)[:, None] * inverse.astype(np.float64)
    step_cos, step_sin = (jnp.asarray(f(steps).astype(np.float32)) for f in (np.cos, np.sin))
    inverse = jnp.asarray(inverse)
    vmem = pl.BlockSpec(memory_space=pltpu.VMEM)
    hbm = pl.BlockSpec(memory_space=pl.ANY)
    dma = pltpu.SemaphoreType.DMA
    sizes = (fw, fw, fw, qw, qw, 2 * kw)
    low = lambda *shape: pltpu.VMEM(shape, bf16)
    wide = lambda *shape: pltpu.VMEM(shape, f32)
    scratch = [
        low(width, qw + 2 * kw), low(width, 2 * fw), low(qw, width), low(fw, width),
        low(planes * (output_weight.shape[0] // n), width),
        low(length, width), low(length, width), low(length, width),
        low(width, length), low(width, length), low(width, length),
        wide(length, head), wide(length, head), wide(length, head), low(block, width),
        wide(length, qw + kw), low(length, qw), low(length, kw), low(length, kw),
        low(kw, length), low(kw, length), low(n // 2, length, 2 * group * block), wide(n // 2, 1, 2 * group * block),
        wide(n // 2, head, 2 * group * block), low(length, qw), low(qw, length),
        low(length, fw), low(length, 2 * fw), low(length, qw + 2 * kw),
        wide(length, kw), wide(length, kw),
    ]
    scratch += [low(planes, n, per, size) for size in sizes]
    scratch += [low(planes + 1, n, per, size) for size in sizes]
    scratch += [low(n, per, sizes[m] + sizes[m + 1]) for m in (0, 2, 4)]
    scratch += [low(2, 4, block, width)] * 2 + [low(2, 3, block, width)] * 2 + [wide(2, block, width)]
    scratch += [
        wide(block, width), wide(block, width), wide(8, width), wide(n, 8, width), wide(planes, 8, width),
        dma((17,)), dma((8, 6)), dma((8, planes)), dma((1, 7)), dma((1, 4)),
        dma((4, n)), dma((4, n)), dma((4, 4)), dma((4, 4)), dma((4, 4)), dma((4, 4)),
        dma((6, planes)), dma((6, planes + 1)), dma((3, n)), dma((3, n)), dma((n,)), dma((n,)),
        dma((planes,)), dma((planes,)),
    ]
    shapes = [
        jax.ShapeDtypeStruct((block, width), bf16),
        jax.ShapeDtypeStruct((block, width), f32),
        jax.ShapeDtypeStruct((8, width), f32),
    ] + [jax.ShapeDtypeStruct((n, per, sizes[m] + sizes[m + 1]), bf16) for m in (0, 2, 4)]
    results = pl.pallas_call(
        functools.partial(layer_kernel, n, planes, block, head, group, fw),
        out_shape=shapes,
        in_specs=[hbm] * 2 + [vmem] * 8 + [hbm] * 7,
        out_specs=[hbm] * 2 + [vmem] * (len(shapes) - 2),
        scratch_shapes=scratch,
        compiler_params=pltpu.CompilerParams(
            collective_id=0, has_side_effects=True, vmem_limit_bytes=60 * 1024 * 1024),
    )(
        layer_input[0], out_cotangent[0], token_positions, inverse, step_cos, step_sin,
        attention_gain[None], feedforward_gain[None], query_gain[None], key_norm_gain[None],
        query_weight, key_matrix, value_matrix, output_weight, gate_weight, up_weight, down_weight,
    )
    plain = lambda rows, columns, kind=f32: jax.ShapeDtypeStruct((rows, columns), kind)
    finals = [
        plain(block, width, bf16), plain(block, width), plain(1, width),
        plain(per, n * qw), plain(per, n * kw), plain(per, n * kw), plain(1, head), plain(1, head),
        plain(per, n * qw), plain(1, width), plain(per, n * fw), plain(per, n * fw), plain(per, n * fw),
    ]
    done = pl.pallas_call(
        functools.partial(finish_kernel, n, head),
        out_shape=finals,
        in_specs=[hbm, hbm, vmem, hbm, hbm, hbm],
        out_specs=[hbm, hbm, vmem, hbm, hbm, hbm, vmem, vmem, hbm, vmem, hbm, hbm, hbm],
        scratch_shapes=[low(*shape.shape) for shape in shapes[3:]]
        + [wide(*finals[i].shape) for i in (3, 4, 5, 8, 10, 11, 12)] + [dma((12,))],
        compiler_params=pltpu.CompilerParams(vmem_limit_bytes=60 * 1024 * 1024),
    )(*results)
    out, dx, ag, q, k, v, qg, kg, o, fg, g, u, d = done
    return out[None], dx[None], ag[0], q, k, v, qg[0], kg[0], o.T, fg[0], g, u, d.T


def solution(mesh):
    in_specs = (
        P("fsdp", "ctx", None),
        P("fsdp", None),
        P(),
        P("fsdp", None),
        P("fsdp", None),
        P("fsdp", None),
        P(),
        P(),
        P("fsdp", None),
        P(),
        P("fsdp", None),
        P("fsdp", None),
        P("fsdp", None),
        P("fsdp", "ctx", None),
    )
    out_specs = (
        P("fsdp", "ctx", None),
        P("fsdp", "ctx", None),
        P(),
        P(("ctx", "fsdp"), None),
        P(("ctx", "fsdp"), None),
        P(("ctx", "fsdp"), None),
        P(),
        P(),
        P(None, ("ctx", "fsdp")),
        P(),
        P(("ctx", "fsdp"), None),
        P(("ctx", "fsdp"), None),
        P(None, ("ctx", "fsdp")),
    )

    def run(*arguments):
        n, planes = mesh.shape["ctx"], mesh.shape["fsdp"]
        key_heads = arguments[4].shape[1] // arguments[6].shape[0]
        whole_heads = n == 8 and planes == 4 and key_heads == n
        return jax.shard_map(
            plane_device if whole_heads else on_device,
            mesh=mesh, in_specs=in_specs, out_specs=out_specs, check_vma=False,
        )(*arguments)

    return run
```
